32 devices in a mesh: dp: 8 (over z, core), space: 4 (over y, x).
Axes of the slice: x: 2, y: 2, z: 4, core: 2. Of those that a mesh axis runs over, the one named last changes fastest.
Arguments:
- encoder_maps_narrow: float32 [64, 64, 256], P('dp', 'space'), may hold values from -6 to 6
- encoder_maps_middle: float32 [32, 256, 256], P('dp', 'space'), may hold values from -6 to 6
- encoder_maps_wide: float32 [128, 1024, 256], P('dp', 'space'), may hold values from -6 to 6
- extreme_noise_narrow: float32 [64, 64, 512], P('dp', 'space'), as said below
- extreme_noise_middle: float32 [32, 256, 512], P('dp', 'space'), as said below
- extreme_noise_wide: float32 [128, 1024, 512], P('dp', 'space'), as said below
- adjoint_narrow: float32 [64, 64, 64], P('dp', 'space'), may hold values from -6 to 6
- adjoint_middle: float32 [32, 256, 64], P('dp', 'space'), may hold values from -6 to 6
- adjoint_wide: float32 [128, 1024, 64], P('dp', 'space'), may hold values from -6 to 6
- position_pictures_narrow: int32 [8, 8], P('dp'), may hold values from 0 to 7, each once within a row
- position_pictures_middle: int32 [8, 4], P('dp'), may hold values from 0 to 3, each once within a row
- position_pictures_wide: int32 [8, 16], P('dp'), may hold values from 0 to 15, each once within a row
- pointwise_kernel: float32 [256, 64], replicated, may hold values from -0.375 to 0.375
- pointwise_offset: float32 [64], replicated, may hold values from -1.5 to 1.5
- dictionary_vectors: float32 [512, 64], replicated, may hold values from -0.6 to 0.6
- inverse_variance_exponent: float32 [1], replicated, may hold values from -0.5 to -0.2
- relaxation_heat: float32 [1], replicated, may hold values from 1.5 to 2
- kernel_slope_mean: float32 [256, 64], replicated, may hold values from -6 to 6
- offset_slope_mean: float32 [64], replicated, may hold values from -6 to 6
- dictionary_slope_mean: float32 [512, 64], replicated, may hold values from -6 to 6
- inverse_variance_slope_mean: float32 [1], replicated, may hold values from -6 to 6
- entry_occupancy_mean: float32 [512], replicated, may hold values from 0.5 to 2
Outputs:
- codes_small: float32 [64, 64, 512], P(('dp', 'space'))
- codes_mid: float32 [32, 256, 512], P(('dp', 'space'))
- codes_big: float32 [128, 1024, 512], P(('dp', 'space'))
- grad_small: float32 [64, 64, 256], P('dp', 'space')
- grad_mid: float32 [32, 256, 256], P('dp', 'space')
- grad_big: float32 [128, 1024, 256], P('dp', 'space')
- weight_new: float32 [256, 64], replicated
- bias_new: float32 [64], replicated
- codebook_new: float32 [512, 64], replicated
- precision_new: float32 [1], replicated
- usage_new: float32 [512], replicated
The draws below stay inside these ranges and needn't reach their ends.
Inputs may be any that keep to these rules, and one draw needn't show every extreme that they name: `extreme_noise_narrow`: gumbel noise -log(-log u) with u uniform, independent for every pixel and code. `extreme_noise_middle`: gumbel noise -log(-log u) with u uniform, independent for every pixel and code. `extreme_noise_wide`: gumbel noise -log(-log u) with u uniform, independent for every pixel and code. `position_pictures_narrow`: each row is a permutation of the group's 8 images. `position_pictures_middle`: each row is a permutation of the group's 4 images. `position_pictures_wide`: each row is a permutation of the group's 16 images.
All inputs are finite; a program needn't handle non-finite values.
Results may differ from the reference program's by a relative error of at most 0.0003.
Values sent between devices are 32-bit elements; how exact they have to be, the bound alone decides.
No kernel may reach another device: no remote copies, remote signals or barrier semaphores. Data moves between devices by JAX's collectives and lax.ppermute only.
A program may use at most 128 MiB of HBM per device.

```python
import jax
import jax.numpy as jnp
from jax import lax

FEAT = 256
CODE_DIM = 64
CODES = 512
SMALL_PIX = 64
MID_PIX = 256
BIG_PIX = 1024
GROUPS = 8
SMALL_GROUP = 8
MID_GROUP = 4
BIG_GROUP = 16
SMALL_IMGS = 64
MID_IMGS = 32
BIG_IMGS = 128
PIXELS = 143360


def gumbel_field(key, shape):
    uniform_draw = jax.random.uniform(key, shape, jnp.float32, 1e-06, 1.0 - 1e-06)
    return -jnp.log(-jnp.log(uniform_draw))


def draw_extreme_noise_narrow(key, part):
    key = jax.random.fold_in(key, 11)
    return gumbel_field(key, (SMALL_IMGS, SMALL_PIX, CODES))


def draw_extreme_noise_middle(key, part):
    key = jax.random.fold_in(key, 12)
    return gumbel_field(key, (MID_IMGS, MID_PIX, CODES))


def draw_extreme_noise_wide(key, part):
    key = jax.random.fold_in(key, 13)
    return gumbel_field(key, (BIG_IMGS, BIG_PIX, CODES))


def block_levels(own_key, shape, cuts, smallest, top_value):
    def one(axis_at, parts):
        heights = jax.random.uniform(jax.random.fold_in(jax.random.fold_in(own_key, 6), axis_at), (parts,), jnp.float32, smallest / len(cuts), top_value / len(cuts))
        return jnp.repeat(jnp.exp(heights), shape[axis_at] // parts).reshape((-1,) + (1,) * (len(shape) - axis_at - 1))

    factor_of = one(*cuts[0])
    for cut in cuts[1:]:
        factor_of = factor_of * one(*cut)
    return factor_of


def centred(rng, extent, spread, bound, cuts=(), kind=jnp.bfloat16):
    values = jax.random.normal(rng, extent, jnp.float32) * spread
    if len(cuts) > 0:
        values = block_levels(rng, extent, cuts, -0.22, 0.18) * values
    return jnp.clip(values, min=-bound, max=bound).astype(kind)


def setup_inputs(seed: int = 0) -> dict:
    keys = jax.random.split(jax.random.key(seed), 23)
    return {
        "encoder_maps_narrow": centred(keys[0], (SMALL_IMGS, SMALL_PIX, FEAT), 1.0, 6.0, ((0, 8), (1, 4)), jnp.float32),
        "encoder_maps_middle": centred(keys[1], (MID_IMGS, MID_PIX, FEAT), 1.0, 6.0, ((0, 8), (1, 4)), jnp.float32),
        "encoder_maps_wide": centred(keys[2], (BIG_IMGS, BIG_PIX, FEAT), 1.0, 6.0, ((0, 8), (1, 4)), jnp.float32),
        "extreme_noise_narrow": draw_extreme_noise_narrow(jax.random.fold_in(keys[22], 71), 0),
        "extreme_noise_middle": draw_extreme_noise_middle(jax.random.fold_in(keys[22], 71), 0),
        "extreme_noise_wide": draw_extreme_noise_wide(jax.random.fold_in(keys[22], 71), 0),
        "adjoint_narrow": centred(keys[6], (SMALL_IMGS, SMALL_PIX, CODE_DIM), 1.0, 6.0, ((0, 8), (1, 4)), jnp.float32),
        "adjoint_middle": centred(keys[7], (MID_IMGS, MID_PIX, CODE_DIM), 1.0, 6.0, ((0, 8), (1, 4)), jnp.float32),
        "adjoint_wide": centred(keys[8], (BIG_IMGS, BIG_PIX, CODE_DIM), 1.0, 6.0, ((0, 8), (1, 4)), jnp.float32),
        "position_pictures_narrow": jax.vmap(lambda own: jax.random.permutation(own, SMALL_GROUP))(jax.random.split(keys[9], GROUPS)).reshape((GROUPS, SMALL_GROUP)).astype(jnp.int32),
        "position_pictures_middle": jax.vmap(lambda own: jax.random.permutation(own, MID_GROUP))(jax.random.split(keys[10], GROUPS)).reshape((GROUPS, MID_GROUP)).astype(jnp.int32),
        "position_pictures_wide": jax.vmap(lambda own: jax.random.permutation(own, BIG_GROUP))(jax.random.split(keys[11], GROUPS)).reshape((GROUPS, BIG_GROUP)).astype(jnp.int32),
        "pointwise_kernel": centred(keys[12], (FEAT, CODE_DIM), FEAT ** -0.5, 0.375, (), jnp.float32),
        "pointwise_offset": centred(keys[13], (CODE_DIM,), 0.3, 1.5, (), jnp.float32),
        "dictionary_vectors": centred(keys[14], (CODES, CODE_DIM), 0.1, 0.6, (), jnp.float32),
        "inverse_variance_exponent": jnp.clip(jax.random.uniform(keys[15], (1,), jnp.float32, -0.5, -0.2), -0.5, -0.2),
        "relaxation_heat": jnp.clip(jax.random.uniform(keys[16], (1,), jnp.float32, 1.5, 2.0), 1.5, 2.0),
        "kernel_slope_mean": centred(keys[17], (FEAT, CODE_DIM), 1.0, 6.0, (), jnp.float32),
        "offset_slope_mean": centred(keys[18], (CODE_DIM,), 1.0, 6.0, (), jnp.float32),
        "dictionary_slope_mean": centred(keys[19], (CODES, CODE_DIM), 1.0, 6.0, (), jnp.float32),
        "inverse_variance_slope_mean": centred(keys[20], (1,), 1.0, 6.0, (), jnp.float32),
        "entry_occupancy_mean": jnp.clip(jax.random.uniform(keys[21], (CODES,), jnp.float32, 0.5, 2.0), 0.5, 2.0),
    }


HIGH = lax.Precision.HIGHEST

def discretize_pass(encoder_arguments, pointwise_kernel, pointwise_offset, dictionary_vectors, inverse_variance_exponent, extreme_noise_arguments, relaxation_heat):
    precision = jnp.exp(inverse_variance_exponent[0])
    relaxation_coldness = relaxation_heat[0]
    code_sq = lax.optimization_barrier(jnp.sum(dictionary_vectors * dictionary_vectors, axis=1))
    quants = []
    codes = []
    usage = jnp.zeros((CODES,), jnp.float32)
    for feat, random_perturbation in zip(encoder_arguments, extreme_noise_arguments):
        latent = jnp.einsum('ipf,fc->ipc', feat, pointwise_kernel, precision=HIGH) + pointwise_offset
        cross = jnp.einsum('ipc,kc->ipk', latent, dictionary_vectors, precision=HIGH)
        dist = lax.optimization_barrier(jnp.sum(latent * latent, axis=2, keepdims=True)) - 2.0 * cross + code_sq
        unnormalized_scores = -0.5 * precision * dist
        probs = jax.nn.softmax(unnormalized_scores, axis=2)
        entry_matrix = jax.nn.softmax((unnormalized_scores + random_perturbation) / relaxation_coldness, axis=2)
        quants.append(jnp.einsum('ipk,kc->ipc', entry_matrix, dictionary_vectors, precision=HIGH))
        codes.append(entry_matrix)
        usage = usage + lax.optimization_barrier(jnp.sum(probs, axis=(0, 1)))
    return (tuple(quants), (tuple(codes), usage))

def place_slots(values, order):
    group = order.shape[1]
    index = (jnp.arange(order.shape[0], dtype=jnp.int32)[:, None] * group + order.astype(jnp.int32)).reshape(-1)
    return values[index]

def reference(encoder_maps_narrow, encoder_maps_middle, encoder_maps_wide, extreme_noise_narrow, extreme_noise_middle, extreme_noise_wide, adjoint_narrow, adjoint_middle, adjoint_wide, position_pictures_narrow, position_pictures_middle, position_pictures_wide, pointwise_kernel, pointwise_offset, dictionary_vectors, inverse_variance_exponent, relaxation_heat, kernel_slope_mean, offset_slope_mean, dictionary_slope_mean, inverse_variance_slope_mean, entry_occupancy_mean):
    extreme_noise_arguments = (extreme_noise_narrow, extreme_noise_middle, extreme_noise_wide)

    def apply(encoder_arguments, kernel_received, offset_received, dictionary_received, inverse_variance_received):
        return discretize_pass(encoder_arguments, kernel_received, offset_received, dictionary_received, inverse_variance_received, extreme_noise_arguments, relaxation_heat)
    quants, back_fn, aux = jax.vjp(apply, (encoder_maps_narrow, encoder_maps_middle, encoder_maps_wide), pointwise_kernel, pointwise_offset, dictionary_vectors, inverse_variance_exponent, has_aux=True)
    codes, usage = aux
    g_feats, g_weight, g_bias, g_code, g_log = back_fn((adjoint_narrow, adjoint_middle, adjoint_wide))
    scale = lax.rsqrt(jnp.asarray(PIXELS, jnp.float32))
    codes_small = place_slots(codes[0], position_pictures_narrow)
    codes_mid = place_slots(codes[1], position_pictures_middle)
    codes_big = place_slots(codes[2], position_pictures_wide)
    weight_new = 0.5 * kernel_slope_mean + 0.5 * scale * g_weight
    bias_new = 0.5 * offset_slope_mean + 0.5 * scale * g_bias
    codebook_new = 0.5 * dictionary_slope_mean + 0.5 * scale * g_code
    precision_new = 0.5 * inverse_variance_slope_mean + 0.5 * scale * g_log
    usage_new = 0.5 * entry_occupancy_mean + 0.5 * (CODES / PIXELS) * usage
    return (codes_small, codes_mid, codes_big, g_feats[0], g_feats[1], g_feats[2], weight_new, bias_new, codebook_new, precision_new, usage_new)
```

```python
import functools

import jax
import jax.numpy as jnp
from jax import lax
from jax.experimental import pallas as pl
from jax.experimental.pallas import tpu as pltpu
from jax.sharding import PartitionSpec as P

F32 = jnp.float32
BF16 = jnp.bfloat16
VMEM_LIMIT = 40 * 1024 * 1024
ACC_ROWS = 64 + 64 + 8 + 8 + 64 + 8
LANES = 1024


def partner(index, step, count):
    if count & (count - 1) == 0:
        return index ^ step
    return lax.rem(index + step, count)


def route(step, count):
    if count & (count - 1) == 0:
        return [(i, i ^ step) for i in range(count)]
    return [(i, (i + step) % count) for i in range(count)]


def source(index, step, count):
    if count & (count - 1) == 0:
        return index ^ step
    return lax.rem(index + (count - step), count)


def halves(x):
    high = x.astype(BF16)
    return high, (x - high.astype(F32)).astype(BF16)


def dot(left, right, left_dim=1, right_dim=0):
    return lax.dot_general(
        left, right, (((left_dim,), (right_dim,)), ((), ())), preferred_element_type=F32
    )


def scalars(log_ref, heat_ref):
    precision = jnp.exp(jnp.full((8, 128), log_ref[0], F32))[0:1, 0:1]
    heat = jnp.full((8, 128), heat_ref[0], F32)[0:1, 0:1]
    return precision, 1.0 / heat, -0.5 * precision / heat


def prepare(refs, book_scr, books_scr, weight_scr):
    weight_ref, bias_ref, book_ref, log_ref, heat_ref = refs
    dim, codes = book_ref.shape
    precision, _, _ = scalars(log_ref, heat_ref)
    book = book_ref[...]
    high, low = halves(book)
    norm = -0.5 * precision * jnp.sum(book * book, axis=0, keepdims=True)
    n0 = norm.astype(BF16).astype(F32)
    n1 = (norm - n0).astype(BF16).astype(F32)
    n2 = norm - n0 - n1
    row = lax.broadcasted_iota(jnp.int32, (16, codes), 0)
    extra = jnp.where(
        row < 3,
        1.0,
        jnp.where(row == 3, n0, jnp.where(row == 4, n1, jnp.where(row == 5, n2, 0.0))),
    ).astype(BF16)
    book_scr[0:dim] = high
    book_scr[dim : 2 * dim] = low
    book_scr[2 * dim : 3 * dim] = high
    book_scr[3 * dim : 3 * dim + 16] = extra
    books_scr[0:dim] = high
    books_scr[dim : 2 * dim] = low
    books_scr[2 * dim : 2 * dim + 16] = jnp.ones((16, codes), BF16)
    high, low = halves(weight_ref[...])
    weight_scr[0:dim] = high
    weight_scr[dim : 2 * dim] = low
    weight_scr[2 * dim : 3 * dim] = high


def tile(refs, scr, feat, cot, noise_ref, code_ref, acc_ref):
    weight_ref, bias_ref, book_ref, log_ref, heat_ref = refs
    book_scr, books_scr, weight_scr, l_scr, g_scr, wh_scr, wl_scr, gh_scr, gl_scr = scr
    rows = feat.shape[0]
    dim, codes = book_ref.shape
    precision, cold, factor = scalars(log_ref, heat_ref)
    eye = lax.broadcasted_iota(jnp.int32, (dim, dim), 0) == lax.broadcasted_iota(
        jnp.int32, (dim, dim), 1
    )
    bias = jnp.sum(jnp.where(eye, bias_ref[...], 0.0), axis=1, keepdims=True)
    fh, fl = halves(feat)
    both = weight_scr[0 : 2 * dim]
    z2 = dot(both, fh, 1, 1) + dot(both, fl, 1, 1)
    z = z2[0:dim] + z2[dim : 2 * dim] + bias
    square = -0.5 * precision * jnp.sum(z * z, axis=0, keepdims=True)
    s0 = square.astype(BF16).astype(F32)
    s1 = (square - s0).astype(BF16).astype(F32)
    s2 = square - s0 - s1
    row = lax.broadcasted_iota(jnp.int32, (16, rows), 0)
    extra = jnp.where(
        row == 0,
        s0,
        jnp.where(row == 1, s1, jnp.where(row == 2, s2, jnp.where(row < 6, 1.0, 0.0))),
    ).astype(BF16)
    zh, zl = halves(precision * z)
    ch, cl = halves(factor * cot)
    left = jnp.concatenate([zh, zh, zl, extra], axis=0)
    l_scr[0:rows] = dot(left, book_scr[...], 0, 0)
    left = jnp.concatenate([ch, ch, cl, jnp.zeros((16, rows), BF16)], axis=0)
    g_scr[0:rows] = dot(left, book_scr[...], 0, 0)

    step = 32 if rows % 32 == 0 else 16

    def softmaxes(i, usage):
        at = pl.ds(pl.multiple_of(i * step, step), step)
        logits = l_scr[at]
        top = jnp.max(logits, axis=1, keepdims=True)
        e = jnp.exp(logits - top)
        e = e * (1.0 / jnp.sum(e, axis=1, keepdims=True))
        usage = usage + jnp.sum(e.reshape(step // 8, 8, codes), axis=0)
        s = (logits + noise_ref[at]) * cold
        top = jnp.max(s, axis=1, keepdims=True)
        e = jnp.exp(s - top)
        gw = g_scr[at]
        scale = 1.0 / jnp.sum(e, axis=1, keepdims=True)
        inner = jnp.sum(e * gw, axis=1, keepdims=True) * scale
        w = e * scale
        code_ref[at] = w
        gd = w * (gw - inner)
        wh_scr[at], wl_scr[at] = halves(w)
        gh_scr[at], gl_scr[at] = halves(gd)
        return usage

    usage = lax.fori_loop(0, rows // step, softmaxes, jnp.zeros((8, codes), F32))

    wh, wl = wh_scr[0:rows], wl_scr[0:rows]
    gh, gl = gh_scr[0:rows], gl_scr[0:rows]
    p = dot(jnp.concatenate([ch, cl], axis=0), wh)
    acc_ref[0:64] += p[0:dim] + p[dim : 2 * dim] + dot(ch, wl)
    left = jnp.concatenate([zh, zl, jnp.ones((16, rows), BF16)], axis=0)
    p = dot(left, gh) + dot(left, gl)
    acc_ref[64:128] += p[0:dim] + p[dim : 2 * dim]
    acc_ref[128:136] += p[2 * dim : 2 * dim + 8]
    acc_ref[136:144] += usage
    p = dot(books_scr[...], gh, 1, 1) + dot(books_scr[...], gl, 1, 1)
    row_d = p[2 * dim : 2 * dim + 1]
    gz = 2.0 * (row_d * z - (p[0:dim] + p[dim : 2 * dim]))
    zh, zl = halves(gz)
    p = dot(jnp.concatenate([zh, zl], axis=0), fh)
    feats = feat.shape[1]
    acc_ref[144:208, 0:feats] += p[0:dim] + p[dim : 2 * dim] + dot(zh, fl)
    acc_ref[144:208, feats : feats + 128] += jnp.broadcast_to(
        jnp.sum(gz, axis=1, keepdims=True), (dim, 128)
    )
    total = jnp.sum(square * row_d, axis=1, keepdims=True)
    acc_ref[208:216] += jnp.broadcast_to(total, (8, codes))
    return dot(jnp.concatenate([zh, zh, zl], axis=0), weight_scr[...], 0, 0)


def tile_scratch(rows, dim, codes, feats):
    return [
        pltpu.VMEM((3 * dim + 16, codes), BF16),
        pltpu.VMEM((2 * dim + 16, codes), BF16),
        pltpu.VMEM((3 * dim, feats), BF16),
        pltpu.VMEM((rows, codes), F32),
        pltpu.VMEM((rows, codes), F32),
        pltpu.VMEM((rows, codes), BF16),
        pltpu.VMEM((rows, codes), BF16),
        pltpu.VMEM((rows, codes), BF16),
        pltpu.VMEM((rows, codes), BF16),
    ]


def cost(rows, feats, dim, codes):
    return pl.CostEstimate(
        flops=rows * 6 * (5 * dim * codes + 3 * dim * feats),
        bytes_accessed=4 * rows * (2 * feats + 2 * codes + dim),
        transcendentals=2 * rows * codes,
    )


def small_kernel(count, groups, *refs):
    orders = refs[0:2]
    big_order = refs[2]
    feats = refs[3:5]
    noises = refs[5:7]
    cots = refs[7:9]
    params = refs[9:14]
    outs = refs[14:]
    sends = outs[0:count]
    grads = outs[count : count + 2]
    acc_ref, table_ref = outs[count + 2 : count + 4]
    feat_scr, noise_scr, cot_scr, code_scr = outs[count + 4 : count + 8]
    scr = outs[count + 8 :]
    me = lax.axis_index("space")
    share = big_order.shape[1] // count
    for step in range(count):
        there = partner(me, step, count)
        for j in range(share):
            table_ref[0, step * share + j] = big_order[0, there * share + j]
    table_ref[0, count * share] = me
    places = []
    base = 0
    for step in range(count):
        there = partner(me, step, count)
        for size in range(2):
            strip = feats[size].shape[1]
            for j in range(groups[size]):
                image = orders[size][0, there * groups[size] + j]
                places.append((size, image, base, strip))
                base += strip
    for size, image, at, strip in places:
        feat_scr[at : at + strip] = feats[size][image]
        noise_scr[at : at + strip] = noises[size][image]
        cot_scr[at : at + strip] = cots[size][image]
    prepare(params, *scr[0:3])
    acc_ref[...] = jnp.zeros(acc_ref.shape, F32)
    feat_scr[...] = tile(
        params, scr, feat_scr[...], cot_scr[...].T, noise_scr, code_scr, acc_ref
    )
    part = base // count
    for step in range(count):
        sends[step][...] = code_scr[step * part : (step + 1) * part]
    for size, image, at, strip in places:
        grads[size][image] = feat_scr[at : at + strip]


def run_small(count, orders, feats, noises, cots, params):
    dim, codes = params[2].shape
    width = feats[0].shape[2]
    groups = tuple(f.shape[0] // count for f in feats)
    part = sum(g * f.shape[1] for g, f in zip(groups, feats))
    rows = part * count
    smem = pl.BlockSpec(memory_space=pltpu.SMEM)
    vmem = pl.BlockSpec(memory_space=pltpu.VMEM)
    return pl.pallas_call(
        functools.partial(small_kernel, count, groups),
        out_shape=[jax.ShapeDtypeStruct((part, codes), F32)] * count
        + [jax.ShapeDtypeStruct(f.shape, F32) for f in feats]
        + [
            jax.ShapeDtypeStruct((ACC_ROWS, codes), F32),
            jax.ShapeDtypeStruct((1, orders[2].shape[1] + 1), jnp.int32),
        ],
        in_specs=[smem] * 3 + [vmem] * 9 + [smem] * 2,
        out_specs=[vmem] * (count + 3) + [smem],
        scratch_shapes=[
            pltpu.VMEM((rows, width), F32),
            pltpu.VMEM((rows, codes), F32),
            pltpu.VMEM((rows, dim), F32),
            pltpu.VMEM((rows, codes), F32),
        ]
        + tile_scratch(rows, dim, codes, width),
        compiler_params=pltpu.CompilerParams(vmem_limit_bytes=VMEM_LIMIT),
        cost_estimate=cost(rows, width, dim, codes),
        name="small_images",
    )(*orders, *feats, *noises, *cots, *params)


def wide_kernel(count, grown, *refs):
    table_ref, feat_ref, noise_ref, cot_ref = refs[0:4]
    params = refs[4:9]
    acc_in = refs[9]
    outs = refs[11:] if grown else refs[10:]
    sends = outs[0 : count - 1]
    grad_ref, acc_ref = outs[count - 1 : count + 1]
    code_scr = outs[count + 1]
    scr = outs[count + 2 :]
    step = pl.program_id(0)

    @pl.when(step == 0)
    def _():
        prepare(params, *scr[0:3])
        acc_ref[...] = acc_in[...]

    grad_ref[...] = tile(
        params, scr, feat_ref[...], cot_ref[...], noise_ref, code_scr, acc_ref
    )
    for i in range(count - 1):

        @pl.when(step == i)
        def _(i=i):
            sends[i][...] = code_scr[...]


def run_wide(count, slot, table, feat, noise, cot, params, acc, grad):
    dim, codes = params[2].shape
    images, strip, width = feat.shape
    share = images // count
    smem = pl.BlockSpec(memory_space=pltpu.SMEM)

    def image(i, table_ref):
        return (table_ref[0, (i + 1) * share + slot], 0, 0)

    def fixed(shape):
        return pl.BlockSpec(shape, lambda i, table_ref: (0,) * len(shape))

    grown = grad is not None
    acc_shape = jax.ShapeDtypeStruct(acc.shape, F32)
    return pl.pallas_call(
        functools.partial(wide_kernel, count, grown),
        grid_spec=pltpu.PrefetchScalarGridSpec(
            num_scalar_prefetch=1,
            grid=(count - 1,),
            in_specs=[
                pl.BlockSpec((None, strip, width), image),
                pl.BlockSpec((None, strip, codes), image),
                pl.BlockSpec((None, dim, strip), image),
                fixed(params[0].shape),
                fixed(params[1].shape),
                fixed(params[2].shape),
                smem,
                smem,
                fixed(acc.shape),
            ]
            + ([pl.BlockSpec(memory_space=pl.ANY)] if grown else []),
            out_specs=[fixed((strip, codes))] * (count - 1)
            + [pl.BlockSpec((None, strip, width), image), fixed(acc.shape)],
            scratch_shapes=[pltpu.VMEM((strip, codes), F32)]
            + tile_scratch(strip, dim, codes, width),
        ),
        out_shape=[jax.ShapeDtypeStruct((strip, codes), F32)] * (count - 1)
        + [jax.ShapeDtypeStruct(feat.shape, F32), acc_shape],
        input_output_aliases={10: count - 1, 9: count} if grown else {9: count - 0},
        compiler_params=pltpu.CompilerParams(vmem_limit_bytes=VMEM_LIMIT),
        cost_estimate=cost((count - 1) * strip, width, dim, codes),
        name="wide_images",
    )(table, feat, noise, cot, *params, acc, *([grad] if grown else []))


def shard_shape(devices):
    down = min(8, devices)
    across = devices // down
    return down, across, 64 // down, LANES // across


def shard_at(index, devices):
    down, across, height, width = shard_shape(devices)
    if across == 1:
        return pl.ds(pl.multiple_of(index * height, height), height), slice(None)
    row = lax.rem(index, down)
    column = lax.div(index, down)
    return (
        pl.ds(pl.multiple_of(row * height, height), height),
        pl.ds(pl.multiple_of(column * width, width), width),
    )


def own_kernel(devices, *refs):
    table_ref, feat_ref, noise_ref, cot_ref = refs[0:4]
    params = refs[4:9]
    acc_in = refs[9]
    code_ref, grad_ref = refs[11:13]
    shards = refs[13 : 13 + devices]
    acc_ref, sum_scr = refs[13 + devices : 15 + devices]
    scr = refs[15 + devices :]
    weight_ref, bias_ref, book_ref, log_ref, heat_ref = params
    dim, codes = book_ref.shape
    width = weight_ref.shape[1]
    step = pl.program_id(0)
    me = lax.axis_index("dp")

    @pl.when(step == 0)
    def _():
        prepare(params, *scr[0:3])
        acc_ref[...] = acc_in[...]

    grad_ref[...] = tile(
        params, scr, feat_ref[...], cot_ref[...], noise_ref, code_ref, acc_ref
    )

    @pl.when(step == pl.num_programs(0) - 1)
    def _():
        precision, _, factor = scalars(log_ref, heat_ref)
        book = book_ref[...]
        column = acc_ref[128:129]
        moment = acc_ref[64:128] * (1.0 / precision)
        book_sum = acc_ref[0:64] * (1.0 / factor) + 2.0 * (column * book - moment)
        slope = jnp.sum(
            jnp.sum(book * book, axis=0, keepdims=True) * column, axis=1, keepdims=True
        ) - 2.0 * jnp.sum(
            jnp.sum(book * moment, axis=0, keepdims=True), axis=1, keepdims=True
        )
        slope = slope + acc_ref[208:209, 0:1] / (-0.5 * precision)
        usage = jnp.sum(acc_ref[136:144], axis=0, keepdims=True)
        sum_scr[:, 0:codes] = book_sum
        sum_scr[:, codes : codes + width + 128] = acc_ref[144:208, 0 : width + 128]
        rows = codes // 128
        for i in range(rows):
            sum_scr[i : i + 1, LANES - 128 : LANES] = usage[:, i * 128 : (i + 1) * 128]
        sum_scr[rows:64, LANES - 128 : LANES] = jnp.broadcast_to(slope, (64 - rows, 128))
        for i in range(devices):
            shards[i][...] = sum_scr[shard_at(partner(me, i, devices), devices)]


def run_own(count, devices, table, feat, noise, cot, params, acc, grad):
    dim, codes = params[2].shape
    images, strip, width = feat.shape
    share = images // count
    smem = pl.BlockSpec(memory_space=pltpu.SMEM)

    def image(i, table_ref):
        return (table_ref[0, i], 0, 0)

    def fixed(shape):
        return pl.BlockSpec(shape, lambda i, table_ref: (0,) * len(shape))

    _, _, height, lanes = shard_shape(devices)
    return pl.pallas_call(
        functools.partial(own_kernel, devices),
        grid_spec=pltpu.PrefetchScalarGridSpec(
            num_scalar_prefetch=1,
            grid=(share,),
            in_specs=[
                pl.BlockSpec((None, strip, width), image),
                pl.BlockSpec((None, strip, codes), image),
                pl.BlockSpec((None, dim, strip), image),
                fixed(params[0].shape),
                fixed(params[1].shape),
                fixed(params[2].shape),
                smem,
                smem,
                fixed(acc.shape),
                pl.BlockSpec(memory_space=pl.ANY),
            ],
            out_specs=[
                pl.BlockSpec(
                    (None, strip, codes),
                    lambda i, table_ref: (i, table_ref[0, count * share], 0),
                ),
                pl.BlockSpec((None, strip, width), image),
            ]
            + [fixed((height, lanes))] * devices,
            scratch_shapes=[
                pltpu.VMEM(acc.shape, F32),
                pltpu.VMEM((64, LANES), F32),
            ]
            + tile_scratch(strip, dim, codes, width),
        ),
        out_shape=[
            jax.ShapeDtypeStruct((share, strip * count, codes), F32),
            jax.ShapeDtypeStruct(feat.shape, F32),
        ]
        + [jax.ShapeDtypeStruct((height, lanes), F32)] * devices,
        input_output_aliases={10: 1},
        compiler_params=pltpu.CompilerParams(vmem_limit_bytes=VMEM_LIMIT),
        cost_estimate=cost(share * strip, width, dim, codes),
        name="own_images",
    )(table, feat, noise, cot, *params, acc, grad)


def place_kernel(count, slot, table_ref, *refs):
    parts = refs[0 : count - 1]
    out_ref, sems = refs[count], refs[count + 1]
    strip = parts[0].shape[0]
    me = lax.axis_index("space")
    copies = []
    for step in range(1, count):
        row = pl.multiple_of(source(me, step, count) * strip, strip)
        copies.append(
            pltpu.make_async_copy(
                parts[step - 1], out_ref.at[slot, pl.ds(row, strip)], sems.at[step - 1]
            )
        )
    for copy in copies:
        copy.start()
    for copy in copies:
        copy.wait()


def place_wide(count, slot, table, parts, whole):
    hbm = pl.BlockSpec(memory_space=pl.ANY)
    return pl.pallas_call(
        functools.partial(place_kernel, count, slot),
        out_shape=jax.ShapeDtypeStruct(whole.shape, F32),
        in_specs=[pl.BlockSpec(memory_space=pltpu.SMEM)] + [hbm] * count,
        out_specs=hbm,
        scratch_shapes=[pltpu.SemaphoreType.DMA((count - 1,))],
        input_output_aliases={count: 0},
        cost_estimate=pl.CostEstimate(
            flops=0, bytes_accessed=2 * sum(p.size * 4 for p in parts), transcendentals=0
        ),
        name="place_wide",
    )(table, *parts, whole)


def join_kernel(count, *refs):
    parts = refs[0:count]
    outs = refs[count:]
    me = lax.axis_index("space")
    for step in range(count):
        here = source(me, step, count)
        base = 0
        for out in outs:
            for j in range(out.shape[0]):
                strip = out.shape[2]
                out[j, here] = parts[step][base : base + strip]
                base += strip


def join_small(count, parts, shapes):
    codes = parts[0].shape[1]
    return pl.pallas_call(
        functools.partial(join_kernel, count),
        out_shape=[
            jax.ShapeDtypeStruct((images // count, count, strip, codes), F32)
            for images, strip, _ in shapes
        ],
        compiler_params=pltpu.CompilerParams(vmem_limit_bytes=VMEM_LIMIT),
        name="join_small",
    )(*parts)


def tree(values):
    while len(values) > 1:
        values = [
            values[i] + values[i + 1] if i + 1 < len(values) else values[i]
            for i in range(0, len(values), 2)
        ]
    return values[0]


def sum_kernel(*refs):
    refs[-1][...] = tree([ref[...] for ref in refs[:-1]])


def add_all(parts):
    return pl.pallas_call(
        sum_kernel,
        out_shape=jax.ShapeDtypeStruct(parts[0].shape, F32),
        name="add_parts",
    )(*parts)


def final_kernel(devices, pixels, *refs):
    shards = refs[0:devices]
    weight_ref, bias_ref, book_ref, log_ref, usage_ref = refs[devices : devices + 5]
    weight_out, bias_out, book_out, log_out, usage_out = refs[devices + 5 : devices + 10]
    sum_scr = refs[devices + 10]
    me = lax.axis_index("dp")
    for i in range(devices):
        sum_scr[shard_at(source(me, i, devices), devices)] = shards[i][...]
    dim, codes = book_ref.shape
    width = weight_ref.shape[1]
    scale = 0.5 * lax.rsqrt(jnp.full((8, 128), pixels, F32))[0:1, 0:1]
    book_out[...] = 0.5 * book_ref[...] + scale * sum_scr[:, 0:codes]
    weight_out[...] = 0.5 * weight_ref[...] + scale * sum_scr[:, codes : codes + width]
    eye = lax.broadcasted_iota(jnp.int32, (dim, dim), 0) == lax.broadcasted_iota(
        jnp.int32, (dim, dim), 1
    )
    bias = sum_scr[:, codes + width : codes + width + dim]
    bias = jnp.sum(jnp.where(eye, bias, 0.0), axis=0, keepdims=True)
    bias_out[...] = 0.5 * bias_ref[...] + scale * bias
    rows = codes // 128
    usage = jnp.concatenate(
        [sum_scr[i : i + 1, LANES - 128 : LANES] for i in range(rows)], axis=1
    )
    usage_out[...] = 0.5 * usage_ref[...] + 0.5 * (codes / pixels) * usage
    log_out[...] = 0.5 * log_ref[...] + scale * sum_scr[rows : rows + 1, LANES - 128 : LANES - 127]


def finish(devices, pixels, shards, weight, bias, book, log, usage):
    outs = (weight.T, bias.reshape(1, -1), book.T, log.reshape(1, 1), usage.reshape(1, -1))
    outs = pl.pallas_call(
        functools.partial(final_kernel, devices, pixels),
        out_shape=[jax.ShapeDtypeStruct(out.shape, F32) for out in outs],
        scratch_shapes=[pltpu.VMEM((64, LANES), F32)],
        name="new_averages",
    )(*shards, *outs)
    return outs[0].T, outs[1].reshape(-1), outs[2].T, outs[3].reshape(-1), outs[4].reshape(-1)


def per_device(
    feat_small,
    feat_mid,
    feat_wide,
    noise_small,
    noise_mid,
    noise_wide,
    cot_small,
    cot_mid,
    cot_wide,
    order_small,
    order_mid,
    order_wide,
    weight,
    bias,
    book,
    log,
    heat,
    weight_mean,
    bias_mean,
    book_mean,
    log_mean,
    usage_mean,
):
    count = lax.axis_size("space")
    devices = lax.axis_size("dp")
    params = (weight.T, bias.reshape(1, -1), book.T, log, heat)
    feats = (feat_small, feat_mid, feat_wide)
    pixels = sum(f.shape[0] * f.shape[1] for f in feats) * count * devices
    share = feat_wide.shape[0] // count
    cot_wide = jnp.swapaxes(cot_wide, 1, 2)

    def send(values, axis, size):
        return [lax.ppermute(v, axis, route(i + 1, size)) for i, v in enumerate(values)]

    *small, grad_small, grad_mid, acc, table = run_small(
        count,
        (order_small, order_mid, order_wide),
        feats[0:2],
        (noise_small, noise_mid),
        (cot_small, cot_mid),
        params,
    )
    arrived = [send(small[1:], "space", count)]
    grad = None
    for slot in range(share):
        *codes, grad, acc = run_wide(
            count, slot, table, feat_wide, noise_wide, cot_wide, params, acc, grad
        )
        arrived.append(send(codes, "space", count))
    whole, grad, *shards = run_own(
        count, devices, table, feat_wide, noise_wide, cot_wide, params, acc, grad
    )
    mine = add_all([shards[0]] + send(shards[1:], "dp", devices))
    mine = add_all([mine] + send([mine] * (count - 1), "space", count))
    shards = [mine] + send([mine] * (devices - 1), "dp", devices)
    updated = finish(
        devices, pixels, shards, weight_mean, bias_mean, book_mean, log_mean, usage_mean
    )
    codes_small, codes_mid = join_small(
        count, [small[0]] + arrived[0], [f.shape for f in feats[0:2]]
    )
    for slot in range(share):
        whole = place_wide(count, slot, table, arrived[1 + slot], whole)
    codes = whole.shape[2]
    return (
        codes_small.reshape(codes_small.shape[0], -1, codes),
        codes_mid.reshape(codes_mid.shape[0], -1, codes),
        whole,
        grad_small,
        grad_mid,
        grad,
        *updated,
    )


def solution(mesh):
    strips = P("dp", "space", None)
    placed = (strips,) * 9 + (P("dp", None),) * 3 + (P(),) * 10
    return jax.shard_map(
        per_device,
        mesh=mesh,
        in_specs=placed,
        out_specs=(P(("dp", "space"), None, None),) * 3 + (strips,) * 3 + (P(),) * 5,
        check_vma=False,
    )
```

```python
import functools

import jax
import jax.numpy as jnp
from jax import lax
from jax.experimental import pallas as pl
from jax.experimental.pallas import tpu as pltpu
from jax.sharding import PartitionSpec as P

F32 = jnp.float32
BF16 = jnp.bfloat16
VMEM_LIMIT = 60 * 1024 * 1024
ACC_ROWS = 64 + 64 + 8 + 8 + 64 + 8
LANES = 1024


def partner(index, step, count):
    if count & (count - 1) == 0:
        return index ^ step
    return lax.rem(index + step, count)


def route(step, count):
    if count & (count - 1) == 0:
        return [(i, i ^ step) for i in range(count)]
    return [(i, (i + step) % count) for i in range(count)]


def source(index, step, count):
    if count & (count - 1) == 0:
        return index ^ step
    return lax.rem(index + (count - step), count)


def halves(x):
    high = x.astype(BF16)
    return high, (x - high.astype(F32)).astype(BF16)


def dot(left, right, left_dim=1, right_dim=0):
    return lax.dot_general(
        left, right, (((left_dim,), (right_dim,)), ((), ())), preferred_element_type=F32
    )


def scalars(log_ref, heat_ref):
    precision = jnp.exp(jnp.full((8, 128), log_ref[0], F32))[0:1, 0:1]
    heat = jnp.full((8, 128), heat_ref[0], F32)[0:1, 0:1]
    return precision, 1.0 / heat, -0.5 * precision / heat


def prepare(refs, book_scr, books_scr, weight_scr):
    weight_ref, bias_ref, book_ref, log_ref, heat_ref = refs
    dim, codes = book_ref.shape
    precision, _, _ = scalars(log_ref, heat_ref)
    book = book_ref[...]
    high, low = halves(book)
    norm = -0.5 * precision * jnp.sum(book * book, axis=0, keepdims=True)
    n0 = norm.astype(BF16).astype(F32)
    n1 = (norm - n0).astype(BF16).astype(F32)
    n2 = norm - n0 - n1
    row = lax.broadcasted_iota(jnp.int32, (16, codes), 0)
    extra = jnp.where(
        row < 3,
        1.0,
        jnp.where(row == 3, n0, jnp.where(row == 4, n1, jnp.where(row == 5, n2, 0.0))),
    ).astype(BF16)
    book_scr[0:dim] = high
    book_scr[dim : 2 * dim] = low
    book_scr[2 * dim : 3 * dim] = high
    book_scr[3 * dim : 3 * dim + 16] = extra
    books_scr[0:dim] = high
    books_scr[dim : 2 * dim] = low
    books_scr[2 * dim : 2 * dim + 16] = jnp.ones((16, codes), BF16)
    high, low = halves(weight_ref[...])
    weight_scr[0:dim] = high
    weight_scr[dim : 2 * dim] = low
    weight_scr[2 * dim : 3 * dim] = high


def tile(refs, scr, feat, cot, noise_ref, code_ref, acc_ref):
    weight_ref, bias_ref, book_ref, log_ref, heat_ref = refs
    book_scr, books_scr, weight_scr, l_scr, g_scr, wh_scr, wl_scr, gh_scr, gl_scr = scr
    rows = feat.shape[0]
    dim, codes = book_ref.shape
    precision, cold, factor = scalars(log_ref, heat_ref)
    eye = lax.broadcasted_iota(jnp.int32, (dim, dim), 0) == lax.broadcasted_iota(
        jnp.int32, (dim, dim), 1
    )
    bias = jnp.sum(jnp.where(eye, bias_ref[...], 0.0), axis=1, keepdims=True)
    fh, fl = halves(feat)
    both = weight_scr[0 : 2 * dim]
    z2 = dot(both, fh, 1, 1) + dot(both, fl, 1, 1)
    z = z2[0:dim] + z2[dim : 2 * dim] + bias
    square = -0.5 * precision * jnp.sum(z * z, axis=0, keepdims=True)
    s0 = square.astype(BF16).astype(F32)
    s1 = (square - s0).astype(BF16).astype(F32)
    s2 = square - s0 - s1
    row = lax.broadcasted_iota(jnp.int32, (16, rows), 0)
    extra = jnp.where(
        row == 0,
        s0,
        jnp.where(row == 1, s1, jnp.where(row == 2, s2, jnp.where(row < 6, 1.0, 0.0))),
    ).astype(BF16)
    zh, zl = halves(precision * z)
    ch, cl = halves(factor * cot)
    left = jnp.concatenate([zh, zh, zl, extra], axis=0)
    l_scr[0:rows] = dot(left, book_scr[...], 0, 0)
    left = jnp.concatenate([ch, ch, cl, jnp.zeros((16, rows), BF16)], axis=0)
    g_scr[0:rows] = dot(left, book_scr[...], 0, 0)

    step = 32 if rows % 32 == 0 else 16

    def softmaxes(i, usage):
        at = pl.ds(pl.multiple_of(i * step, step), step)
        logits = l_scr[at]
        top = jnp.max(logits, axis=1, keepdims=True)
        e = jnp.exp(logits - top)
        e = e * (1.0 / jnp.sum(e, axis=1, keepdims=True))
        usage = usage + jnp.sum(e.reshape(step // 8, 8, codes), axis=0)
        s = (logits + noise_ref[at]) * cold
        top = jnp.max(s, axis=1, keepdims=True)
        e = jnp.exp(s - top)
        gw = g_scr[at]
        scale = 1.0 / jnp.sum(e, axis=1, keepdims=True)
        inner = jnp.sum(e * gw, axis=1, keepdims=True) * scale
        w = e * scale
        code_ref[at] = w
        gd = w * (gw - inner)
        wh_scr[at], wl_scr[at] = halves(w)
        gh_scr[at], gl_scr[at] = halves(gd)
        return usage

    usage = lax.fori_loop(
        0, rows // step, softmaxes, jnp.zeros((8, codes), F32), unroll=True
    )

    wh, wl = wh_scr[0:rows], wl_scr[0:rows]
    gh, gl = gh_scr[0:rows], gl_scr[0:rows]
    p = dot(jnp.concatenate([ch, cl], axis=0), wh)
    acc_ref[0:64] += p[0:dim] + p[dim : 2 * dim] + dot(ch, wl)
    left = jnp.concatenate([zh, zl, jnp.ones((16, rows), BF16)], axis=0)
    p = dot(left, gh) + dot(left, gl)
    acc_ref[64:128] += p[0:dim] + p[dim : 2 * dim]
    acc_ref[128:136] += p[2 * dim : 2 * dim + 8]
    acc_ref[136:144] += usage
    p = dot(books_scr[...], gh, 1, 1) + dot(books_scr[...], gl, 1, 1)
    row_d = p[2 * dim : 2 * dim + 1]
    gz = 2.0 * (row_d * z - (p[0:dim] + p[dim : 2 * dim]))
    zh, zl = halves(gz)
    p = dot(jnp.concatenate([zh, zl], axis=0), fh)
    feats = feat.shape[1]
    acc_ref[144:208, 0:feats] += p[0:dim] + p[dim : 2 * dim] + dot(zh, fl)
    acc_ref[144:208, feats : feats + 128] += jnp.broadcast_to(
        jnp.sum(gz, axis=1, keepdims=True), (dim, 128)
    )
    total = jnp.sum(square * row_d, axis=1, keepdims=True)
    acc_ref[208:216] += jnp.broadcast_to(total, (8, codes))
    return dot(jnp.concatenate([zh, zh, zl], axis=0), weight_scr[...], 0, 0)


def tile_scratch(rows, dim, codes, feats):
    return [
        pltpu.VMEM((3 * dim + 16, codes), BF16),
        pltpu.VMEM((2 * dim + 16, codes), BF16),
        pltpu.VMEM((3 * dim, feats), BF16),
        pltpu.VMEM((rows, codes), F32),
        pltpu.VMEM((rows, codes), F32),
        pltpu.VMEM((rows, codes), BF16),
        pltpu.VMEM((rows, codes), BF16),
        pltpu.VMEM((rows, codes), BF16),
        pltpu.VMEM((rows, codes), BF16),
    ]


def cost(rows, feats, dim, codes):
    return pl.CostEstimate(
        flops=rows * 6 * (5 * dim * codes + 3 * dim * feats),
        bytes_accessed=4 * rows * (2 * feats + 2 * codes + dim),
        transcendentals=2 * rows * codes,
    )


def small_kernel(count, groups, *refs):
    orders = refs[0:2]
    big_order = refs[2]
    feats = refs[3:5]
    noises = refs[5:7]
    cots = refs[7:9]
    params = refs[9:14]
    outs = refs[14:]
    sends = outs[0:count]
    grads = outs[count : count + 2]
    acc_ref, table_ref = outs[count + 2 : count + 4]
    feat_scr, noise_scr, cot_scr, code_scr = outs[count + 4 : count + 8]
    scr = outs[count + 8 :]
    me = lax.axis_index("space")
    share = big_order.shape[1] // count
    for step in range(count):
        there = partner(me, step, count)
        for j in range(share):
            table_ref[0, step * share + j] = big_order[0, there * share + j]
    table_ref[0, count * share] = me
    places = []
    base = 0
    for step in range(count):
        there = partner(me, step, count)
        for size in range(2):
            strip = feats[size].shape[1]
            for j in range(groups[size]):
                image = orders[size][0, there * groups[size] + j]
                places.append((size, image, base, strip))
                base += strip
    for size, image, at, strip in places:
        feat_scr[at : at + strip] = feats[size][image]
        noise_scr[at : at + strip] = noises[size][image]
        cot_scr[at : at + strip] = cots[size][image]
    prepare(params, *scr[0:3])
    acc_ref[...] = jnp.zeros(acc_ref.shape, F32)
    feat_scr[...] = tile(
        params, scr, feat_scr[...], cot_scr[...].T, noise_scr, code_scr, acc_ref
    )
    part = base // count
    for step in range(count):
        sends[step][...] = code_scr[step * part : (step + 1) * part]
    for size, image, at, strip in places:
        grads[size][image] = feat_scr[at : at + strip]


def run_small(count, orders, feats, noises, cots, params):
    dim, codes = params[2].shape
    width = feats[0].shape[2]
    groups = tuple(f.shape[0] // count for f in feats)
    part = sum(g * f.shape[1] for g, f in zip(groups, feats))
    rows = part * count
    smem = pl.BlockSpec(memory_space=pltpu.SMEM)
    vmem = pl.BlockSpec(memory_space=pltpu.VMEM)
    return pl.pallas_call(
        functools.partial(small_kernel, count, groups),
        out_shape=[jax.ShapeDtypeStruct((part, codes), F32)] * count
        + [jax.ShapeDtypeStruct(f.shape, F32) for f in feats]
        + [
            jax.ShapeDtypeStruct((ACC_ROWS, codes), F32),
            jax.ShapeDtypeStruct((1, orders[2].shape[1] + 1), jnp.int32),
        ],
        in_specs=[smem] * 3 + [vmem] * 9 + [smem] * 2,
        out_specs=[vmem] * (count + 3) + [smem],
        scratch_shapes=[
            pltpu.VMEM((rows, width), F32),
            pltpu.VMEM((rows, codes), F32),
            pltpu.VMEM((rows, dim), F32),
            pltpu.VMEM((rows, codes), F32),
        ]
        + tile_scratch(rows, dim, codes, width),
        compiler_params=pltpu.CompilerParams(vmem_limit_bytes=VMEM_LIMIT),
        cost_estimate=cost(rows, width, dim, codes),
        name="small_images",
    )(*orders, *feats, *noises, *cots, *params)


def wide_kernel(count, slots, grown, *refs):
    table_ref, feat_ref, noise_ref, cot_ref = refs[0:4]
    params = refs[4:9]
    acc_in = refs[9]
    outs = refs[11:] if grown else refs[10:]
    sends = outs[0 : count - 1]
    grad_ref, acc_ref = outs[count - 1 : count + 1]
    code_scr = outs[count + 1]
    scr = outs[count + 2 :]
    step = pl.program_id(0)

    @pl.when(step == 0)
    def _():
        prepare(params, *scr[0:3])
        acc_ref[...] = acc_in[...]

    grad_ref[...] = tile(
        params, scr, feat_ref[...], cot_ref[...], noise_ref, code_scr, acc_ref
    )
    for i in range(count - 1):

        @pl.when(lax.div(step, slots) == i)
        def _(i=i):
            sends[i][...] = code_scr[...]


def run_wide(count, first, slots, table, feat, noise, cot, params, acc, grad):
    dim, codes = params[2].shape
    images, strip, width = feat.shape
    share = images // count
    smem = pl.BlockSpec(memory_space=pltpu.SMEM)

    def image(i, table_ref):
        peer = lax.div(i, slots) + 1
        return (table_ref[0, peer * share + first + lax.rem(i, slots)], 0, 0)

    def fixed(shape):
        return pl.BlockSpec(shape, lambda i, table_ref: (0,) * len(shape))

    def send(peer):
        return pl.BlockSpec(
            (strip, codes),
            lambda i, table_ref: (jnp.clip(i - peer * slots, 0, slots - 1), 0),
        )

    grown = grad is not None
    return pl.pallas_call(
        functools.partial(wide_kernel, count, slots, grown),
        grid_spec=pltpu.PrefetchScalarGridSpec(
            num_scalar_prefetch=1,
            grid=((count - 1) * slots,),
            in_specs=[
                pl.BlockSpec((None, strip, width), image),
                pl.BlockSpec((None, strip, codes), image),
                pl.BlockSpec((None, dim, strip), image),
                fixed(params[0].shape),
                fixed(params[1].shape),
                fixed(params[2].shape),
                smem,
                smem,
                fixed(acc.shape),
            ]
            + ([pl.BlockSpec(memory_space=pl.ANY)] if grown else []),
            out_specs=[send(peer) for peer in range(count - 1)]
            + [pl.BlockSpec((None, strip, width), image), fixed(acc.shape)],
            scratch_shapes=[pltpu.VMEM((strip, codes), F32)]
            + tile_scratch(strip, dim, codes, width),
        ),
        out_shape=[jax.ShapeDtypeStruct((strip * slots, codes), F32)] * (count - 1)
        + [
            jax.ShapeDtypeStruct(feat.shape, F32),
            jax.ShapeDtypeStruct(acc.shape, F32),
        ],
        input_output_aliases={10: count - 1, 9: count} if grown else {9: count},
        compiler_params=pltpu.CompilerParams(vmem_limit_bytes=VMEM_LIMIT),
        cost_estimate=cost((count - 1) * slots * strip, width, dim, codes),
        name="wide_images",
    )(table, feat, noise, cot, *params, acc, *([grad] if grown else []))


def shard_at(index, parts):
    height = 64 // parts
    return pl.ds(pl.multiple_of(index * height, height), height)


def own_kernel(devices, *refs):
    table_ref, feat_ref, noise_ref, cot_ref = refs[0:4]
    params = refs[4:9]
    acc_in = refs[9]
    code_ref, grad_ref = refs[11:13]
    shards = refs[13 : 13 + devices]
    acc_ref, sum_scr = refs[13 + devices : 15 + devices]
    scr = refs[15 + devices :]
    weight_ref, bias_ref, book_ref, log_ref, heat_ref = params
    dim, codes = book_ref.shape
    width = weight_ref.shape[1]
    step = pl.program_id(0)
    me = lax.rem(lax.axis_index("dp"), devices)

    @pl.when(step == 0)
    def _():
        prepare(params, *scr[0:3])
        acc_ref[...] = acc_in[...]

    grad_ref[...] = tile(
        params, scr, feat_ref[...], cot_ref[...], noise_ref, code_ref, acc_ref
    )

    @pl.when(step == pl.num_programs(0) - 1)
    def _():
        precision, _, factor = scalars(log_ref, heat_ref)
        book = book_ref[...]
        column = acc_ref[128:129]
        moment = acc_ref[64:128] * (1.0 / precision)
        book_sum = acc_ref[0:64] * (1.0 / factor) + 2.0 * (column * book - moment)
        slope = jnp.sum(
            jnp.sum(book * book, axis=0, keepdims=True) * column, axis=1, keepdims=True
        ) - 2.0 * jnp.sum(
            jnp.sum(book * moment, axis=0, keepdims=True), axis=1, keepdims=True
        )
        slope = slope + acc_ref[208:209, 0:1] / (-0.5 * precision)
        usage = jnp.sum(acc_ref[136:144], axis=0, keepdims=True)
        sum_scr[:, 0:codes] = book_sum
        sum_scr[:, codes : codes + width + 128] = acc_ref[144:208, 0 : width + 128]
        rows = codes // 128
        for i in range(rows):
            sum_scr[i : i + 1, LANES - 128 : LANES] = usage[:, i * 128 : (i + 1) * 128]
        sum_scr[rows:64, LANES - 128 : LANES] = jnp.broadcast_to(slope, (64 - rows, 128))
        for i in range(devices):
            shards[i][...] = sum_scr[shard_at(partner(me, i, devices), devices)]


def run_own(count, devices, table, feat, noise, cot, params, acc, grad):
    dim, codes = params[2].shape
    images, strip, width = feat.shape
    share = images // count
    smem = pl.BlockSpec(memory_space=pltpu.SMEM)

    def image(i, table_ref):
        return (table_ref[0, i], 0, 0)

    def fixed(shape):
        return pl.BlockSpec(shape, lambda i, table_ref: (0,) * len(shape))

    height = 64 // devices
    return pl.pallas_call(
        functools.partial(own_kernel, devices),
        grid_spec=pltpu.PrefetchScalarGridSpec(
            num_scalar_prefetch=1,
            grid=(share,),
            in_specs=[
                pl.BlockSpec((None, strip, width), image),
                pl.BlockSpec((None, strip, codes), image),
                pl.BlockSpec((None, dim, strip), image),
                fixed(params[0].shape),
                fixed(params[1].shape),
                fixed(params[2].shape),
                smem,
                smem,
                fixed(acc.shape),
                pl.BlockSpec(memory_space=pl.ANY),
            ],
            out_specs=[
                pl.BlockSpec(
                    (None, strip, codes),
                    lambda i, table_ref: (i, table_ref[0, count * share], 0),
                ),
                pl.BlockSpec((None, strip, width), image),
            ]
            + [fixed((height, LANES))] * devices,
            scratch_shapes=[
                pltpu.VMEM(acc.shape, F32),
                pltpu.VMEM((64, LANES), F32),
            ]
            + tile_scratch(strip, dim, codes, width),
        ),
        out_shape=[
            jax.ShapeDtypeStruct((share, strip * count, codes), F32),
            jax.ShapeDtypeStruct(feat.shape, F32),
        ]
        + [jax.ShapeDtypeStruct((height, LANES), F32)] * devices,
        input_output_aliases={10: 1},
        compiler_params=pltpu.CompilerParams(vmem_limit_bytes=VMEM_LIMIT),
        cost_estimate=cost(share * strip, width, dim, codes),
        name="own_images",
    )(table, feat, noise, cot, *params, acc, grad)


def place_kernel(count, slots, table_ref, *refs):
    parts = refs[0 : count - 1]
    out_ref = refs[count]
    step = pl.program_id(0)
    for i in range(count - 1):

        @pl.when(lax.div(step, slots) == i)
        def _(i=i):
            out_ref[...] = parts[i][...]


def place_wide(count, first, slots, table, parts, whole):
    codes = whole.shape[2]
    strip = whole.shape[1] // count

    def part(peer):
        return pl.BlockSpec(
            (strip, codes),
            lambda i, table_ref: (jnp.clip(i - peer * slots, 0, slots - 1), 0),
        )

    def out(i, table_ref):
        me = table_ref[0, table_ref.shape[1] - 1]
        return (
            first + lax.rem(i, slots),
            source(me, lax.div(i, slots) + 1, count),
            0,
        )

    return pl.pallas_call(
        functools.partial(place_kernel, count, slots),
        grid_spec=pltpu.PrefetchScalarGridSpec(
            num_scalar_prefetch=1,
            grid=((count - 1) * slots,),
            in_specs=[part(peer) for peer in range(count - 1)]
            + [pl.BlockSpec(memory_space=pl.ANY)],
            out_specs=pl.BlockSpec((None, strip, codes), out),
        ),
        out_shape=jax.ShapeDtypeStruct(whole.shape, F32),
        input_output_aliases={count: 0},
        compiler_params=pltpu.CompilerParams(vmem_limit_bytes=VMEM_LIMIT),
        cost_estimate=pl.CostEstimate(
            flops=0, bytes_accessed=2 * sum(p.size * 4 for p in parts), transcendentals=0
        ),
        name="place_wide",
    )(table, *parts, whole)


def join_kernel(count, *refs):
    parts = refs[0:count]
    outs = refs[count:]
    me = lax.axis_index("space")
    for step in range(count):
        here = source(me, step, count)
        base = 0
        for out in outs:
            for j in range(out.shape[0]):
                strip = out.shape[2]
                out[j, here] = parts[step][base : base + strip]
                base += strip


def join_small(count, parts, shapes):
    codes = parts[0].shape[1]
    return pl.pallas_call(
        functools.partial(join_kernel, count),
        out_shape=[
            jax.ShapeDtypeStruct((images // count, count, strip, codes), F32)
            for images, strip, _ in shapes
        ],
        compiler_params=pltpu.CompilerParams(vmem_limit_bytes=VMEM_LIMIT),
        name="join_small",
    )(*parts)


def tree(values):
    while len(values) > 1:
        values = [
            values[i] + values[i + 1] if i + 1 < len(values) else values[i]
            for i in range(0, len(values), 2)
        ]
    return values[0]


def sum_kernel(*refs):
    refs[-1][...] = tree([ref[...] for ref in refs[:-1]])


def add_all(parts):
    return pl.pallas_call(
        sum_kernel,
        out_shape=jax.ShapeDtypeStruct(parts[0].shape, F32),
        name="add_parts",
    )(*parts)


def final_kernel(devices, pixels, *refs):
    shards = refs[0:devices]
    weight_ref, bias_ref, book_ref, log_ref, usage_ref = refs[devices : devices + 5]
    weight_out, bias_out, book_out, log_out, usage_out = refs[devices + 5 : devices + 10]
    sum_scr = refs[devices + 10]
    me = lax.rem(lax.axis_index("dp"), devices)
    for i in range(devices):
        sum_scr[shard_at(source(me, i, devices), devices)] = shards[i][...]
    dim, codes = book_ref.shape
    width = weight_ref.shape[1]
    scale = 0.5 * lax.rsqrt(jnp.full((8, 128), pixels, F32))[0:1, 0:1]
    book_out[...] = 0.5 * book_ref[...] + scale * sum_scr[:, 0:codes]
    weight_out[...] = 0.5 * weight_ref[...] + scale * sum_scr[:, codes : codes + width]
    eye = lax.broadcasted_iota(jnp.int32, (dim, dim), 0) == lax.broadcasted_iota(
        jnp.int32, (dim, dim), 1
    )
    bias = sum_scr[:, codes + width : codes + width + dim]
    bias = jnp.sum(jnp.where(eye, bias, 0.0), axis=0, keepdims=True)
    bias_out[...] = 0.5 * bias_ref[...] + scale * bias
    rows = codes // 128
    usage = jnp.concatenate(
        [sum_scr[i : i + 1, LANES - 128 : LANES] for i in range(rows)], axis=1
    )
    usage_out[...] = 0.5 * usage_ref[...] + 0.5 * (codes / pixels) * usage
    log_out[...] = 0.5 * log_ref[...] + scale * sum_scr[rows : rows + 1, LANES - 128 : LANES - 127]


def finish(devices, pixels, shards, weight, bias, book, log, usage):
    outs = (weight.T, bias.reshape(1, -1), book.T, log.reshape(1, 1), usage.reshape(1, -1))
    outs = pl.pallas_call(
        functools.partial(final_kernel, devices, pixels),
        out_shape=[jax.ShapeDtypeStruct(out.shape, F32) for out in outs],
        scratch_shapes=[pltpu.VMEM((64, LANES), F32)],
        name="new_averages",
    )(*shards, *outs)
    return outs[0].T, outs[1].reshape(-1), outs[2].T, outs[3].reshape(-1), outs[4].reshape(-1)


def spans(share):
    if share < 4:
        return [(0, share)]
    return [(0, 1), (1, share - 1)]


def per_device(
    feat_small,
    feat_mid,
    feat_wide,
    noise_small,
    noise_mid,
    noise_wide,
    cot_small,
    cot_mid,
    cot_wide,
    order_small,
    order_mid,
    order_wide,
    weight,
    bias,
    book,
    log,
    heat,
    weight_mean,
    bias_mean,
    book_mean,
    log_mean,
    usage_mean,
):
    count = lax.axis_size("space")
    devices = lax.axis_size("dp")
    params = (weight.T, bias.reshape(1, -1), book.T, log, heat)
    feats = (feat_small, feat_mid, feat_wide)
    pixels = sum(f.shape[0] * f.shape[1] for f in feats) * count * devices
    share = feat_wide.shape[0] // count
    cot_wide = jnp.swapaxes(cot_wide, 1, 2)

    def send(values, axis, size):
        return [lax.ppermute(v, axis, route(i + 1, size)) for i, v in enumerate(values)]

    *small, grad_small, grad_mid, acc, table = run_small(
        count,
        (order_small, order_mid, order_wide),
        feats[0:2],
        (noise_small, noise_mid),
        (cot_small, cot_mid),
        params,
    )
    arrived = [send(small[1:], "space", count)]
    grad = None
    for first, slots in spans(share):
        *codes, grad, acc = run_wide(
            count, first, slots, table, feat_wide, noise_wide, cot_wide, params, acc, grad
        )
        for i in range(count - 1):
            arrived[-1][i], codes[i] = lax.optimization_barrier((arrived[-1][i], codes[i]))
        arrived.append(send(codes, "space", count))
    arrived[-2], acc = lax.optimization_barrier((arrived[-2], acc))
    near = min(4, devices)
    whole, grad, *shards = run_own(
        count, near, table, feat_wide, noise_wide, cot_wide, params, acc, grad
    )
    group = [
        [(i, i - i % near + partner(i % near, step, near)) for i in range(devices)]
        for step in range(near)
    ]
    parts = [lax.ppermute(shards[i], "dp", group[i]) for i in range(1, near)]
    mine = add_all([shards[0]] + parts)
    for axis, size, bit in [("dp", devices, near), ("space", count, 1)]:
        while bit < size:
            mine = mine + lax.ppermute(mine, axis, [(i, i ^ bit) for i in range(size)])
            bit = 2 * bit
    shards = [mine] + [lax.ppermute(mine, "dp", group[i]) for i in range(1, near)]
    updated = finish(
        near, pixels, shards, weight_mean, bias_mean, book_mean, log_mean, usage_mean
    )
    codes_small, codes_mid = join_small(
        count, [small[0]] + arrived[0], [f.shape for f in feats[0:2]]
    )
    for (first, slots), parts in zip(spans(share), arrived[1:]):
        whole = place_wide(count, first, slots, table, parts, whole)
    codes = whole.shape[2]
    return (
        codes_small.reshape(codes_small.shape[0], -1, codes),
        codes_mid.reshape(codes_mid.shape[0], -1, codes),
        whole,
        grad_small,
        grad_mid,
        grad,
        *updated,
    )


def solution(mesh):
    strips = P("dp", "space", None)
    placed = (strips,) * 9 + (P("dp", None),) * 3 + (P(),) * 10
    return jax.shard_map(
        per_device,
        mesh=mesh,
        in_specs=placed,
        out_specs=(P(("dp", "space"), None, None),) * 3 + (strips,) * 3 + (P(),) * 5,
        check_vma=False,
    )
```

```python
import functools

import jax
import jax.numpy as jnp
from jax import lax
from jax.experimental import pallas as pl
from jax.experimental.pallas import tpu as pltpu
from jax.sharding import PartitionSpec as P

F32 = jnp.float32
BF16 = jnp.bfloat16
VMEM_LIMIT = 28 * 1024 * 1024
ACC_ROWS = 64 + 64 + 8 + 8 + 64 + 8
LANES = 1024


def partner(index, step, count):
    if count & (count - 1) == 0:
        return index ^ step
    return lax.rem(index + step, count)


def route(step, count):
    if count & (count - 1) == 0:
        return [(i, i ^ step) for i in range(count)]
    return [(i, (i + step) % count) for i in range(count)]


def source(index, step, count):
    if count & (count - 1) == 0:
        return index ^ step
    return lax.rem(index + (count - step), count)


def in_hbm(arrays):
    return [pltpu.with_memory_space_constraint(a, pltpu.HBM) for a in arrays]


def halves(x):
    high = x.astype(BF16)
    return high, (x - high.astype(F32)).astype(BF16)


def dot(left, right, left_dim=1, right_dim=0):
    return lax.dot_general(
        left, right, (((left_dim,), (right_dim,)), ((), ())), preferred_element_type=F32
    )


def scalars(log_ref, heat_ref):
    precision = jnp.exp(jnp.full((8, 128), log_ref[0], F32))[0:1, 0:1]
    heat = jnp.full((8, 128), heat_ref[0], F32)[0:1, 0:1]
    return precision, 1.0 / heat, -0.5 * precision / heat


def prepare(refs, book_scr, books_scr, weight_scr):
    weight_ref, bias_ref, book_ref, log_ref, heat_ref = refs
    dim, codes = book_ref.shape
    precision, _, _ = scalars(log_ref, heat_ref)
    book = book_ref[...]
    high, low = halves(book)
    norm = -0.5 * precision * jnp.sum(book * book, axis=0, keepdims=True)
    n0 = norm.astype(BF16).astype(F32)
    n1 = (norm - n0).astype(BF16).astype(F32)
    n2 = norm - n0 - n1
    row = lax.broadcasted_iota(jnp.int32, (16, codes), 0)
    extra = jnp.where(
        row < 3,
        1.0,
        jnp.where(row == 3, n0, jnp.where(row == 4, n1, jnp.where(row == 5, n2, 0.0))),
    ).astype(BF16)
    book_scr[0:dim] = high
    book_scr[dim : 2 * dim] = low
    book_scr[2 * dim : 3 * dim] = high
    book_scr[3 * dim : 3 * dim + 16] = extra
    books_scr[0:dim] = high
    books_scr[dim : 2 * dim] = low
    books_scr[2 * dim : 2 * dim + 16] = jnp.ones((16, codes), BF16)
    high, low = halves(weight_ref[...])
    weight_scr[0:dim] = high
    weight_scr[dim : 2 * dim] = low
    weight_scr[2 * dim : 3 * dim] = high


def tile(refs, scr, feat, cot, noise_ref, code_ref, acc_ref):
    weight_ref, bias_ref, book_ref, log_ref, heat_ref = refs
    book_scr, books_scr, weight_scr, l_scr, g_scr, wh_scr, wl_scr, gh_scr, gl_scr = scr
    rows = feat.shape[0]
    dim, codes = book_ref.shape
    precision, cold, factor = scalars(log_ref, heat_ref)
    eye = lax.broadcasted_iota(jnp.int32, (dim, dim), 0) == lax.broadcasted_iota(
        jnp.int32, (dim, dim), 1
    )
    bias = jnp.sum(jnp.where(eye, bias_ref[...], 0.0), axis=1, keepdims=True)
    fh, fl = halves(feat)
    both = weight_scr[0 : 2 * dim]
    z2 = dot(both, fh, 1, 1) + dot(both, fl, 1, 1)
    z = z2[0:dim] + z2[dim : 2 * dim] + bias
    square = -0.5 * precision * jnp.sum(z * z, axis=0, keepdims=True)
    s0 = square.astype(BF16).astype(F32)
    s1 = (square - s0).astype(BF16).astype(F32)
    s2 = square - s0 - s1
    row = lax.broadcasted_iota(jnp.int32, (16, rows), 0)
    extra = jnp.where(
        row == 0,
        s0,
        jnp.where(row == 1, s1, jnp.where(row == 2, s2, jnp.where(row < 6, 1.0, 0.0))),
    ).astype(BF16)
    zh, zl = halves(precision * z)
    ch, cl = halves(factor * cot)
    left = jnp.concatenate([zh, zh, zl, extra], axis=0)
    l_scr[0:rows] = dot(left, book_scr[...], 0, 0)
    left = jnp.concatenate([ch, ch, cl, jnp.zeros((16, rows), BF16)], axis=0)
    g_scr[0:rows] = dot(left, book_scr[...], 0, 0)

    step = 32 if rows % 32 == 0 else 16

    def softmaxes(i, usage):
        at = pl.ds(pl.multiple_of(i * step, step), step)
        logits = l_scr[at]
        top = jnp.max(logits, axis=1, keepdims=True)
        e = jnp.exp(logits - top)
        e = e * (1.0 / jnp.sum(e, axis=1, keepdims=True))
        usage = usage + jnp.sum(e.reshape(step // 8, 8, codes), axis=0)
        s = (logits + noise_ref[at]) * cold
        top = jnp.max(s, axis=1, keepdims=True)
        e = jnp.exp(s - top)
        gw = g_scr[at]
        scale = 1.0 / jnp.sum(e, axis=1, keepdims=True)
        inner = jnp.sum(e * gw, axis=1, keepdims=True) * scale
        w = e * scale
        code_ref[at] = w
        gd = w * (gw - inner)
        wh_scr[at], wl_scr[at] = halves(w)
        gh_scr[at], gl_scr[at] = halves(gd)
        return usage

    usage = lax.fori_loop(
        0, rows // step, softmaxes, jnp.zeros((8, codes), F32), unroll=True
    )

    wh, wl = wh_scr[0:rows], wl_scr[0:rows]
    gh, gl = gh_scr[0:rows], gl_scr[0:rows]
    p = dot(jnp.concatenate([ch, cl], axis=0), wh)
    acc_ref[0:64] += p[0:dim] + p[dim : 2 * dim] + dot(ch, wl)
    left = jnp.concatenate([zh, zl, jnp.ones((16, rows), BF16)], axis=0)
    p = dot(left, gh) + dot(left, gl)
    acc_ref[64:128] += p[0:dim] + p[dim : 2 * dim]
    acc_ref[128:136] += p[2 * dim : 2 * dim + 8]
    acc_ref[136:144] += usage
    p = dot(books_scr[...], gh, 1, 1) + dot(books_scr[...], gl, 1, 1)
    row_d = p[2 * dim : 2 * dim + 1]
    gz = 2.0 * (row_d * z - (p[0:dim] + p[dim : 2 * dim]))
    zh, zl = halves(gz)
    p = dot(jnp.concatenate([zh, zl], axis=0), fh)
    feats = feat.shape[1]
    acc_ref[144:208, 0:feats] += p[0:dim] + p[dim : 2 * dim] + dot(zh, fl)
    acc_ref[144:208, feats : feats + 128] += jnp.broadcast_to(
        jnp.sum(gz, axis=1, keepdims=True), (dim, 128)
    )
    total = jnp.sum(square * row_d, axis=1, keepdims=True)
    acc_ref[208:216] += jnp.broadcast_to(total, (8, codes))
    return dot(jnp.concatenate([zh, zh, zl], axis=0), weight_scr[...], 0, 0)


def tile_scratch(rows, dim, codes, feats):
    return [
        pltpu.VMEM((3 * dim + 16, codes), BF16),
        pltpu.VMEM((2 * dim + 16, codes), BF16),
        pltpu.VMEM((3 * dim, feats), BF16),
        pltpu.VMEM((rows, codes), F32),
        pltpu.VMEM((rows, codes), F32),
        pltpu.VMEM((rows, codes), BF16),
        pltpu.VMEM((rows, codes), BF16),
        pltpu.VMEM((rows, codes), BF16),
        pltpu.VMEM((rows, codes), BF16),
    ]


def cost(rows, feats, dim, codes):
    return pl.CostEstimate(
        flops=rows * 6 * (5 * dim * codes + 3 * dim * feats),
        bytes_accessed=4 * rows * (2 * feats + 2 * codes + dim),
        transcendentals=2 * rows * codes,
    )


def small_kernel(count, groups, *refs):
    orders = refs[0:2]
    big_order = refs[2]
    feats = refs[3:5]
    noises = refs[5:7]
    cots = refs[7:9]
    params = refs[9:14]
    outs = refs[14:]
    sends = outs[0:count]
    grads = outs[count : count + 2]
    acc_ref, table_ref = outs[count + 2 : count + 4]
    feat_scr, noise_scr, cot_scr, code_scr = outs[count + 4 : count + 8]
    scr = outs[count + 8 :]
    me = lax.axis_index("space")
    share = big_order.shape[1] // count
    for step in range(count):
        there = partner(me, step, count)
        for j in range(share):
            table_ref[0, step * share + j] = big_order[0, there * share + j]
    table_ref[0, count * share] = me
    places = []
    base = 0
    for step in range(count):
        there = partner(me, step, count)
        for size in range(2):
            strip = feats[size].shape[1]
            for j in range(groups[size]):
                image = orders[size][0, there * groups[size] + j]
                places.append((size, image, base, strip))
                base += strip
    for size, image, at, strip in places:
        feat_scr[at : at + strip] = feats[size][image]
        noise_scr[at : at + strip] = noises[size][image]
        cot_scr[at : at + strip] = cots[size][image]
    prepare(params, *scr[0:3])
    acc_ref[...] = jnp.zeros(acc_ref.shape, F32)
    feat_scr[...] = tile(
        params, scr, feat_scr[...], cot_scr[...].T, noise_scr, code_scr, acc_ref
    )
    part = base // count
    for step in range(count):
        sends[step][...] = code_scr[step * part : (step + 1) * part]
    for size, image, at, strip in places:
        grads[size][image] = feat_scr[at : at + strip]


def run_small(count, orders, feats, noises, cots, params):
    dim, codes = params[2].shape
    width = feats[0].shape[2]
    groups = tuple(f.shape[0] // count for f in feats)
    part = sum(g * f.shape[1] for g, f in zip(groups, feats))
    rows = part * count
    smem = pl.BlockSpec(memory_space=pltpu.SMEM)
    vmem = pl.BlockSpec(memory_space=pltpu.VMEM)
    return pl.pallas_call(
        functools.partial(small_kernel, count, groups),
        out_shape=[jax.ShapeDtypeStruct((part, codes), F32)] * count
        + [pltpu.HBM(f.shape, F32) for f in feats]
        + [
            pltpu.HBM((ACC_ROWS, codes), F32),
            jax.ShapeDtypeStruct((1, orders[2].shape[1] + 1), jnp.int32),
        ],
        in_specs=[smem] * 3 + [vmem] * 9 + [smem] * 2,
        out_specs=[vmem] * (count + 3) + [smem],
        scratch_shapes=[
            pltpu.VMEM((rows, width), F32),
            pltpu.VMEM((rows, codes), F32),
            pltpu.VMEM((rows, dim), F32),
            pltpu.VMEM((rows, codes), F32),
        ]
        + tile_scratch(rows, dim, codes, width),
        compiler_params=pltpu.CompilerParams(vmem_limit_bytes=VMEM_LIMIT),
        cost_estimate=cost(rows, width, dim, codes),
        name="small_images",
    )(*orders, *in_hbm([*feats, *noises, *cots, *params[0:3]]), *params[3:5])


def wide_kernel(count, slots, grown, *refs):
    table_ref, feat_ref, noise_ref, cot_ref = refs[0:4]
    params = refs[4:9]
    acc_in = refs[9]
    outs = refs[11:] if grown else refs[10:]
    sends = outs[0 : count - 1]
    grad_ref, acc_ref = outs[count - 1 : count + 1]
    code_scr = outs[count + 1]
    scr = outs[count + 2 :]
    step = pl.program_id(0)

    @pl.when(step == 0)
    def _():
        prepare(params, *scr[0:3])
        acc_ref[...] = acc_in[...]

    grad_ref[...] = tile(
        params, scr, feat_ref[...], cot_ref[...], noise_ref, code_scr, acc_ref
    )
    for i in range(count - 1):

        @pl.when(lax.div(step, slots) == i)
        def _(i=i):
            sends[i][...] = code_scr[...]


def run_wide(count, first, slots, table, feat, noise, cot, params, acc, grad):
    dim, codes = params[2].shape
    images, strip, width = feat.shape
    share = images // count
    smem = pl.BlockSpec(memory_space=pltpu.SMEM)

    def image(i, table_ref):
        peer = lax.div(i, slots) + 1
        return (table_ref[0, peer * share + first + lax.rem(i, slots)], 0, 0)

    def fixed(shape):
        return pl.BlockSpec(shape, lambda i, table_ref: (0,) * len(shape))

    def send(peer):
        return pl.BlockSpec(
            (strip, codes),
            lambda i, table_ref: (jnp.clip(i - peer * slots, 0, slots - 1), 0),
        )

    grown = grad is not None
    return pl.pallas_call(
        functools.partial(wide_kernel, count, slots, grown),
        grid_spec=pltpu.PrefetchScalarGridSpec(
            num_scalar_prefetch=1,
            grid=((count - 1) * slots,),
            in_specs=[
                pl.BlockSpec((None, strip, width), image),
                pl.BlockSpec((None, strip, codes), image),
                pl.BlockSpec((None, dim, strip), image),
                fixed(params[0].shape),
                fixed(params[1].shape),
                fixed(params[2].shape),
                smem,
                smem,
                fixed(acc.shape),
            ]
            + ([pl.BlockSpec(memory_space=pl.ANY)] if grown else []),
            out_specs=[send(peer) for peer in range(count - 1)]
            + [pl.BlockSpec((None, strip, width), image), fixed(acc.shape)],
            scratch_shapes=[pltpu.VMEM((strip, codes), F32)]
            + tile_scratch(strip, dim, codes, width),
        ),
        out_shape=[jax.ShapeDtypeStruct((strip * slots, codes), F32)] * (count - 1)
        + [pltpu.HBM(feat.shape, F32), pltpu.HBM(acc.shape, F32)],
        input_output_aliases={10: count - 1, 9: count} if grown else {9: count},
        compiler_params=pltpu.CompilerParams(vmem_limit_bytes=VMEM_LIMIT),
        cost_estimate=cost((count - 1) * slots * strip, width, dim, codes),
        name="wide_images",
    )(
        table,
        *in_hbm([feat, noise, cot, *params[0:3]]),
        *params[3:5],
        *in_hbm([acc] + ([grad] if grown else [])),
    )


def shard_at(index, parts):
    height = 64 // parts
    return pl.ds(pl.multiple_of(index * height, height), height)


def own_kernel(devices, *refs):
    table_ref, feat_ref, noise_ref, cot_ref = refs[0:4]
    params = refs[4:9]
    acc_in = refs[9]
    code_ref, grad_ref = refs[11:13]
    shards = refs[13 : 13 + devices]
    acc_ref, sum_scr = refs[13 + devices : 15 + devices]
    scr = refs[15 + devices :]
    weight_ref, bias_ref, book_ref, log_ref, heat_ref = params
    dim, codes = book_ref.shape
    width = weight_ref.shape[1]
    step = pl.program_id(0)
    me = lax.rem(lax.axis_index("dp"), devices)

    @pl.when(step == 0)
    def _():
        prepare(params, *scr[0:3])
        acc_ref[...] = acc_in[...]

    grad_ref[...] = tile(
        params, scr, feat_ref[...], cot_ref[...], noise_ref, code_ref, acc_ref
    )

    @pl.when(step == pl.num_programs(0) - 1)
    def _():
        precision, _, factor = scalars(log_ref, heat_ref)
        book = book_ref[...]
        column = acc_ref[128:129]
        moment = acc_ref[64:128] * (1.0 / precision)
        book_sum = acc_ref[0:64] * (1.0 / factor) + 2.0 * (column * book - moment)
        slope = jnp.sum(
            jnp.sum(book * book, axis=0, keepdims=True) * column, axis=1, keepdims=True
        ) - 2.0 * jnp.sum(
            jnp.sum(book * moment, axis=0, keepdims=True), axis=1, keepdims=True
        )
        slope = slope + acc_ref[208:209, 0:1] / (-0.5 * precision)
        usage = jnp.sum(acc_ref[136:144], axis=0, keepdims=True)
        sum_scr[:, 0:codes] = book_sum
        sum_scr[:, codes : codes + width + 128] = acc_ref[144:208, 0 : width + 128]
        rows = codes // 128
        for i in range(rows):
            sum_scr[i : i + 1, LANES - 128 : LANES] = usage[:, i * 128 : (i + 1) * 128]
        sum_scr[rows:64, LANES - 128 : LANES] = jnp.broadcast_to(slope, (64 - rows, 128))
        for i in range(devices):
            shards[i][...] = sum_scr[shard_at(partner(me, i, devices), devices)]


def run_own(count, devices, table, feat, noise, cot, params, acc, grad):
    dim, codes = params[2].shape
    images, strip, width = feat.shape
    share = images // count
    smem = pl.BlockSpec(memory_space=pltpu.SMEM)

    def image(i, table_ref):
        return (table_ref[0, i], 0, 0)

    def fixed(shape):
        return pl.BlockSpec(shape, lambda i, table_ref: (0,) * len(shape))

    height = 64 // devices
    return pl.pallas_call(
        functools.partial(own_kernel, devices),
        grid_spec=pltpu.PrefetchScalarGridSpec(
            num_scalar_prefetch=1,
            grid=(share,),
            in_specs=[
                pl.BlockSpec((None, strip, width), image),
                pl.BlockSpec((None, strip, codes), image),
                pl.BlockSpec((None, dim, strip), image),
                fixed(params[0].shape),
                fixed(params[1].shape),
                fixed(params[2].shape),
                smem,
                smem,
                fixed(acc.shape),
                pl.BlockSpec(memory_space=pl.ANY),
            ],
            out_specs=[
                pl.BlockSpec(
                    (None, strip, codes),
                    lambda i, table_ref: (i, table_ref[0, count * share], 0),
                ),
                pl.BlockSpec((None, strip, width), image),
            ]
            + [fixed((height, LANES))] * devices,
            scratch_shapes=[
                pltpu.VMEM(acc.shape, F32),
                pltpu.VMEM((64, LANES), F32),
            ]
            + tile_scratch(strip, dim, codes, width),
        ),
        out_shape=[
            pltpu.HBM((share, strip * count, codes), F32),
            pltpu.HBM(feat.shape, F32),
        ]
        + [jax.ShapeDtypeStruct((height, LANES), F32)] * devices,
        input_output_aliases={10: 1},
        compiler_params=pltpu.CompilerParams(vmem_limit_bytes=VMEM_LIMIT),
        cost_estimate=cost(share * strip, width, dim, codes),
        name="own_images",
    )(
        table,
        *in_hbm([feat, noise, cot, *params[0:3]]),
        *params[3:5],
        *in_hbm([acc, grad]),
    )


def place_kernel(count, first, slots, *refs):
    parts = refs[0 : count - 1]
    out_ref, sem = refs[count], refs[count + 1]
    strip = parts[0].shape[0] // slots
    me = lax.axis_index("space")
    copies = []
    for step in range(1, count):
        row = pl.multiple_of(source(me, step, count) * strip, strip)
        for j in range(slots):
            copies.append(
                pltpu.make_async_copy(
                    parts[step - 1].at[pl.ds(j * strip, strip)],
                    out_ref.at[first + j, pl.ds(row, strip)],
                    sem.at[(step - 1) * slots + j],
                )
            )
    for copy in copies:
        copy.start()
    for copy in copies:
        copy.wait()


def place_wide(count, first, slots, parts, whole):
    return pl.pallas_call(
        functools.partial(place_kernel, count, first, slots),
        out_shape=pltpu.HBM(whole.shape, F32),
        in_specs=[pl.BlockSpec(memory_space=pltpu.VMEM)] * (count - 1)
        + [pl.BlockSpec(memory_space=pltpu.HBM)],
        out_specs=pl.BlockSpec(memory_space=pltpu.HBM),
        scratch_shapes=[pltpu.SemaphoreType.DMA(((count - 1) * slots,))],
        input_output_aliases={count - 1: 0},
        compiler_params=pltpu.CompilerParams(vmem_limit_bytes=VMEM_LIMIT),
        cost_estimate=pl.CostEstimate(
            flops=0, bytes_accessed=2 * sum(p.size * 4 for p in parts), transcendentals=0
        ),
        name="place_wide",
    )(*parts, *in_hbm([whole]))


def join_kernel(count, *refs):
    parts = refs[0:count]
    outs = refs[count:]
    me = lax.axis_index("space")
    for step in range(count):
        here = source(me, step, count)
        base = 0
        for out in outs:
            for j in range(out.shape[0]):
                strip = out.shape[2]
                out[j, here] = parts[step][base : base + strip]
                base += strip


def join_small(count, parts, shapes):
    codes = parts[0].shape[1]
    return pl.pallas_call(
        functools.partial(join_kernel, count),
        out_shape=[
            jax.ShapeDtypeStruct((images // count, count, strip, codes), F32)
            for images, strip, _ in shapes
        ],
        compiler_params=pltpu.CompilerParams(vmem_limit_bytes=VMEM_LIMIT),
        name="join_small",
    )(*parts)


def tree(values):
    while len(values) > 1:
        values = [
            values[i] + values[i + 1] if i + 1 < len(values) else values[i]
            for i in range(0, len(values), 2)
        ]
    return values[0]


def sum_kernel(*refs):
    refs[-1][...] = tree([ref[...] for ref in refs[:-1]])


def add_all(parts):
    return pl.pallas_call(
        sum_kernel,
        out_shape=jax.ShapeDtypeStruct(parts[0].shape, F32),
        name="add_parts",
    )(*parts)


def final_kernel(devices, pixels, *refs):
    shards = refs[0:devices]
    weight_ref, bias_ref, book_ref, log_ref, usage_ref = refs[devices : devices + 5]
    weight_out, bias_out, book_out, log_out, usage_out = refs[devices + 5 : devices + 10]
    sum_scr = refs[devices + 10]
    me = lax.rem(lax.axis_index("dp"), devices)
    for i in range(devices):
        sum_scr[shard_at(source(me, i, devices), devices)] = shards[i][...]
    dim, codes = book_ref.shape
    width = weight_ref.shape[1]
    scale = 0.5 * lax.rsqrt(jnp.full((8, 128), pixels, F32))[0:1, 0:1]
    book_out[...] = 0.5 * book_ref[...] + scale * sum_scr[:, 0:codes]
    weight_out[...] = 0.5 * weight_ref[...] + scale * sum_scr[:, codes : codes + width]
    eye = lax.broadcasted_iota(jnp.int32, (dim, dim), 0) == lax.broadcasted_iota(
        jnp.int32, (dim, dim), 1
    )
    bias = sum_scr[:, codes + width : codes + width + dim]
    bias = jnp.sum(jnp.where(eye, bias, 0.0), axis=0, keepdims=True)
    bias_out[...] = 0.5 * bias_ref[...] + scale * bias
    rows = codes // 128
    usage = jnp.concatenate(
        [sum_scr[i : i + 1, LANES - 128 : LANES] for i in range(rows)], axis=1
    )
    usage_out[...] = 0.5 * usage_ref[...] + 0.5 * (codes / pixels) * usage
    log_out[...] = 0.5 * log_ref[...] + scale * sum_scr[rows : rows + 1, LANES - 128 : LANES - 127]


def finish(devices, pixels, shards, weight, bias, book, log, usage):
    outs = (weight.T, bias.reshape(1, -1), book.T, log.reshape(1, 1), usage.reshape(1, -1))
    outs = pl.pallas_call(
        functools.partial(final_kernel, devices, pixels),
        out_shape=[jax.ShapeDtypeStruct(out.shape, F32) for out in outs],
        scratch_shapes=[pltpu.VMEM((64, LANES), F32)],
        name="new_averages",
    )(*shards, *outs)
    return outs[0].T, outs[1].reshape(-1), outs[2].T, outs[3].reshape(-1), outs[4].reshape(-1)


def exchange(value, axis, bit, size):
    parts = [value]
    while bit < size:
        ways = min(4, size // bit)
        parts = [value]
        for way in range(1, ways):
            pairs = [(i, i ^ (way * bit)) for i in range(size)]
            parts.append(lax.ppermute(value, axis, pairs))
        value = tree(parts)
        bit = bit * ways
    return value, parts[1:]


def spans(share):
    if share < 4:
        return [(0, share)]
    return [(0, 1), (1, share - 2), (share - 1, 1)]


def per_device(
    feat_small,
    feat_mid,
    feat_wide,
    noise_small,
    noise_mid,
    noise_wide,
    cot_small,
    cot_mid,
    cot_wide,
    order_small,
    order_mid,
    order_wide,
    weight,
    bias,
    book,
    log,
    heat,
    weight_mean,
    bias_mean,
    book_mean,
    log_mean,
    usage_mean,
):
    count = lax.axis_size("space")
    devices = lax.axis_size("dp")
    params = (weight.T, bias.reshape(1, -1), book.T, log, heat)
    feats = (feat_small, feat_mid, feat_wide)
    pixels = sum(f.shape[0] * f.shape[1] for f in feats) * count * devices
    share = feat_wide.shape[0] // count
    cot_wide = jnp.swapaxes(cot_wide, 1, 2)

    def send(values, axis, size):
        return [lax.ppermute(v, axis, route(i + 1, size)) for i, v in enumerate(values)]

    *small, grad_small, grad_mid, acc, table = run_small(
        count,
        (order_small, order_mid, order_wide),
        feats[0:2],
        (noise_small, noise_mid),
        (cot_small, cot_mid),
        params,
    )
    arrived = [send(small[1:], "space", count)]
    grad = None
    *early, last = spans(share)

    def pass_on(codes):
        for i in range(count - 1):
            arrived[-1][i], codes[i] = lax.optimization_barrier((arrived[-1][i], codes[i]))
        arrived.append(send(codes, "space", count))

    for first, slots in early:
        *codes, grad, acc = run_wide(
            count, first, slots, table, feat_wide, noise_wide, cot_wide, params, acc, grad
        )
        pass_on(codes)
    *codes, grad, acc = run_wide(
        count, *last, table, feat_wide, noise_wide, cot_wide, params, acc, grad
    )
    near = min(4, devices)
    whole, grad, *shards = run_own(
        count, near, table, feat_wide, noise_wide, cot_wide, params, acc, grad
    )
    group = [
        [(i, i - i % near + partner(i % near, step, near)) for i in range(devices)]
        for step in range(near)
    ]
    parts = [lax.ppermute(shards[i], "dp", group[i]) for i in range(1, near)]
    mine = add_all([shards[0]] + parts)
    mine, _ = exchange(mine, "dp", near, devices)
    mine, crossed = exchange(mine, "space", 1, count)
    for i in range(count - 1):
        j = min(i, len(crossed) - 1)
        crossed[j], codes[i] = lax.optimization_barrier((crossed[j], codes[i]))
    pass_on(codes)
    shards = [mine] + [lax.ppermute(mine, "dp", group[i]) for i in range(1, near)]
    updated = finish(
        near, pixels, shards, weight_mean, bias_mean, book_mean, log_mean, usage_mean
    )
    codes_small, codes_mid = join_small(
        count, [small[0]] + arrived[0], [f.shape for f in feats[0:2]]
    )
    for (first, slots), parts in zip(spans(share), arrived[1:]):
        whole = place_wide(count, first, slots, parts, whole)
    codes = whole.shape[2]
    return (
        codes_small.reshape(codes_small.shape[0], -1, codes),
        codes_mid.reshape(codes_mid.shape[0], -1, codes),
        whole,
        grad_small,
        grad_mid,
        grad,
        *updated,
    )


def solution(mesh):
    strips = P("dp", "space", None)
    placed = (strips,) * 9 + (P("dp", None),) * 3 + (P(),) * 10
    return jax.shard_map(
        per_device,
        mesh=mesh,
        in_specs=placed,
        out_specs=(P(("dp", "space"), None, None),) * 3 + (strips,) * 3 + (P(),) * 5,
        check_vma=False,
    )
```

```python
import functools

import jax
import jax.numpy as jnp
from jax import lax
from jax.experimental import pallas as pl
from jax.experimental.pallas import tpu as pltpu
from jax.sharding import PartitionSpec as P

F32 = jnp.float32
BF16 = jnp.bfloat16
VMEM_LIMIT = 28 * 1024 * 1024
ACC_ROWS = 64 + 64 + 8 + 8 + 64 + 8
LANES = 1024
FORMS = [(16, False), (32, True), (32, True), (64, False)]


def partner(index, step, count):
    if count & (count - 1) == 0:
        return index ^ step
    return lax.rem(index + step, count)


def route(step, count):
    if count & (count - 1) == 0:
        return [(i, i ^ step) for i in range(count)]
    return [(i, (i + step) % count) for i in range(count)]


def source(index, step, count):
    if count & (count - 1) == 0:
        return index ^ step
    return lax.rem(index + (count - step), count)


def in_hbm(arrays):
    return [pltpu.with_memory_space_constraint(a, pltpu.HBM) for a in arrays]


def halves(x):
    high = x.astype(BF16)
    return high, (x - high.astype(F32)).astype(BF16)


def dot(left, right, left_dim=1, right_dim=0):
    return lax.dot_general(
        left, right, (((left_dim,), (right_dim,)), ((), ())), preferred_element_type=F32
    )


def scalars(log_ref, heat_ref):
    precision = jnp.exp(jnp.full((8, 128), log_ref[0], F32))[0:1, 0:1]
    heat = jnp.full((8, 128), heat_ref[0], F32)[0:1, 0:1]
    return precision, 1.0 / heat, -0.5 * precision / heat


def prepare(refs, book_scr, books_scr, weight_scr):
    weight_ref, bias_ref, book_ref, log_ref, heat_ref = refs
    dim, codes = book_ref.shape
    precision, _, _ = scalars(log_ref, heat_ref)
    book = book_ref[...]
    high, low = halves(book)
    norm = -0.5 * precision * jnp.sum(book * book, axis=0, keepdims=True)
    n0 = norm.astype(BF16).astype(F32)
    n1 = (norm - n0).astype(BF16).astype(F32)
    n2 = norm - n0 - n1
    row = lax.broadcasted_iota(jnp.int32, (16, codes), 0)
    extra = jnp.where(
        row < 3,
        1.0,
        jnp.where(row == 3, n0, jnp.where(row == 4, n1, jnp.where(row == 5, n2, 0.0))),
    ).astype(BF16)
    book_scr[0:dim] = high
    book_scr[dim : 2 * dim] = low
    book_scr[2 * dim : 3 * dim] = high
    book_scr[3 * dim : 3 * dim + 16] = extra
    books_scr[0:dim] = high
    books_scr[dim : 2 * dim] = low
    books_scr[2 * dim : 2 * dim + 16] = jnp.ones((16, codes), BF16)
    high, low = halves(weight_ref[...])
    weight_scr[0:dim] = high
    weight_scr[dim : 2 * dim] = low
    weight_scr[2 * dim : 3 * dim] = high


def tile(refs, scr, feat, cot, noise_ref, code_ref, acc_ref, step=32, joint=False):
    weight_ref, bias_ref, book_ref, log_ref, heat_ref = refs
    book_scr, books_scr, weight_scr, l_scr, g_scr, wh_scr, wl_scr, gh_scr, gl_scr = scr
    rows = feat.shape[0]
    dim, codes = book_ref.shape
    precision, cold, factor = scalars(log_ref, heat_ref)
    eye = lax.broadcasted_iota(jnp.int32, (dim, dim), 0) == lax.broadcasted_iota(
        jnp.int32, (dim, dim), 1
    )
    bias = jnp.sum(jnp.where(eye, bias_ref[...], 0.0), axis=1, keepdims=True)
    fh, fl = halves(feat)
    both = weight_scr[0 : 2 * dim]
    z2 = dot(both, fh, 1, 1) + dot(both, fl, 1, 1)
    z = z2[0:dim] + z2[dim : 2 * dim] + bias
    square = -0.5 * precision * jnp.sum(z * z, axis=0, keepdims=True)
    s0 = square.astype(BF16).astype(F32)
    s1 = (square - s0).astype(BF16).astype(F32)
    s2 = square - s0 - s1
    row = lax.broadcasted_iota(jnp.int32, (16, rows), 0)
    extra = jnp.where(
        row == 0,
        s0,
        jnp.where(row == 1, s1, jnp.where(row == 2, s2, jnp.where(row < 6, 1.0, 0.0))),
    ).astype(BF16)
    zh, zl = halves(precision * z)
    ch, cl = halves(factor * cot)
    left = jnp.concatenate([zh, zh, zl, extra], axis=0)
    other = jnp.concatenate([ch, ch, cl, jnp.zeros((16, rows), BF16)], axis=0)
    if joint:
        p = dot(jnp.concatenate([left, other], axis=1), book_scr[...], 0, 0)
        l_scr[0:rows] = p[0:rows]
        g_scr[0:rows] = p[rows : 2 * rows]
    else:
        l_scr[0:rows] = dot(left, book_scr[...], 0, 0)
        g_scr[0:rows] = dot(other, book_scr[...], 0, 0)

    step = step if rows % step == 0 else 16

    def softmaxes(i, usage):
        at = pl.ds(pl.multiple_of(i * step, step), step)
        logits = l_scr[at]
        top = jnp.max(logits, axis=1, keepdims=True)
        e = jnp.exp(logits - top)
        e = e * (1.0 / jnp.sum(e, axis=1, keepdims=True))
        usage = usage + jnp.sum(e.reshape(step // 8, 8, codes), axis=0)
        s = (logits + noise_ref[at]) * cold
        top = jnp.max(s, axis=1, keepdims=True)
        e = jnp.exp(s - top)
        gw = g_scr[at]
        scale = 1.0 / jnp.sum(e, axis=1, keepdims=True)
        inner = jnp.sum(e * gw, axis=1, keepdims=True) * scale
        w = e * scale
        code_ref[at] = w
        gd = w * (gw - inner)
        wh_scr[at], wl_scr[at] = halves(w)
        gh_scr[at], gl_scr[at] = halves(gd)
        return usage

    usage = lax.fori_loop(
        0, rows // step, softmaxes, jnp.zeros((8, codes), F32), unroll=True
    )

    wh, wl = wh_scr[0:rows], wl_scr[0:rows]
    gh, gl = gh_scr[0:rows], gl_scr[0:rows]
    p = dot(jnp.concatenate([ch, cl], axis=0), wh)
    acc_ref[0:64] += p[0:dim] + p[dim : 2 * dim] + dot(ch, wl)
    left = jnp.concatenate([zh, zl, jnp.ones((16, rows), BF16)], axis=0)
    p = dot(left, gh) + dot(left, gl)
    acc_ref[64:128] += p[0:dim] + p[dim : 2 * dim]
    acc_ref[128:136] += p[2 * dim : 2 * dim + 8]
    acc_ref[136:144] += usage
    p = dot(books_scr[...], gh, 1, 1) + dot(books_scr[...], gl, 1, 1)
    row_d = p[2 * dim : 2 * dim + 1]
    gz = 2.0 * (row_d * z - (p[0:dim] + p[dim : 2 * dim]))
    zh, zl = halves(gz)
    p = dot(jnp.concatenate([zh, zl], axis=0), fh)
    feats = feat.shape[1]
    acc_ref[144:208, 0:feats] += p[0:dim] + p[dim : 2 * dim] + dot(zh, fl)
    acc_ref[144:208, feats : feats + 128] += jnp.broadcast_to(
        jnp.sum(gz, axis=1, keepdims=True), (dim, 128)
    )
    total = jnp.sum(square * row_d, axis=1, keepdims=True)
    acc_ref[208:216] += jnp.broadcast_to(total, (8, codes))
    return dot(jnp.concatenate([zh, zh, zl], axis=0), weight_scr[...], 0, 0)


def tile_scratch(rows, dim, codes, feats):
    return [
        pltpu.VMEM((3 * dim + 16, codes), BF16),
        pltpu.VMEM((2 * dim + 16, codes), BF16),
        pltpu.VMEM((3 * dim, feats), BF16),
        pltpu.VMEM((rows, codes), F32),
        pltpu.VMEM((rows, codes), F32),
        pltpu.VMEM((rows, codes), BF16),
        pltpu.VMEM((rows, codes), BF16),
        pltpu.VMEM((rows, codes), BF16),
        pltpu.VMEM((rows, codes), BF16),
    ]


def cost(rows, feats, dim, codes):
    return pl.CostEstimate(
        flops=rows * 6 * (5 * dim * codes + 3 * dim * feats),
        bytes_accessed=4 * rows * (2 * feats + 2 * codes + dim),
        transcendentals=2 * rows * codes,
    )


def small_kernel(count, groups, *refs):
    orders = refs[0:2]
    big_order = refs[2]
    feats = refs[3:5]
    noises = refs[5:7]
    cots = refs[7:9]
    params = refs[9:14]
    outs = refs[14:]
    sends = outs[0:count]
    grads = outs[count : count + 2]
    acc_ref, table_ref = outs[count + 2 : count + 4]
    feat_scr, noise_scr, cot_scr, code_scr = outs[count + 4 : count + 8]
    scr = outs[count + 8 :]
    me = lax.axis_index("space")
    share = big_order.shape[1] // count
    for step in range(count):
        there = partner(me, step, count)
        for j in range(share):
            table_ref[0, step * share + j] = big_order[0, there * share + j]
    table_ref[0, count * share] = me
    places = []
    base = 0
    for step in range(count):
        there = partner(me, step, count)
        for size in range(2):
            strip = feats[size].shape[1]
            for j in range(groups[size]):
                image = orders[size][0, there * groups[size] + j]
                places.append((size, image, base, strip))
                base += strip
    for size, image, at, strip in places:
        feat_scr[at : at + strip] = feats[size][image]
        noise_scr[at : at + strip] = noises[size][image]
        cot_scr[at : at + strip] = cots[size][image]
    prepare(params, *scr[0:3])
    acc_ref[...] = jnp.zeros(acc_ref.shape, F32)
    feat_scr[...] = tile(
        params, scr, feat_scr[...], cot_scr[...].T, noise_scr, code_scr, acc_ref
    )
    part = base // count
    for step in range(count):
        sends[step][...] = code_scr[step * part : (step + 1) * part]
    for size, image, at, strip in places:
        grads[size][image] = feat_scr[at : at + strip]


def run_small(count, orders, feats, noises, cots, params):
    dim, codes = params[2].shape
    width = feats[0].shape[2]
    groups = tuple(f.shape[0] // count for f in feats)
    part = sum(g * f.shape[1] for g, f in zip(groups, feats))
    rows = part * count
    smem = pl.BlockSpec(memory_space=pltpu.SMEM)
    vmem = pl.BlockSpec(memory_space=pltpu.VMEM)
    return pl.pallas_call(
        functools.partial(small_kernel, count, groups),
        out_shape=[jax.ShapeDtypeStruct((part, codes), F32)] * count
        + [pltpu.HBM(f.shape, F32) for f in feats]
        + [
            pltpu.HBM((ACC_ROWS, codes), F32),
            jax.ShapeDtypeStruct((1, orders[2].shape[1] + 1), jnp.int32),
        ],
        in_specs=[smem] * 3 + [vmem] * 9 + [smem] * 2,
        out_specs=[vmem] * (count + 3) + [smem],
        scratch_shapes=[
            pltpu.VMEM((rows, width), F32),
            pltpu.VMEM((rows, codes), F32),
            pltpu.VMEM((rows, dim), F32),
            pltpu.VMEM((rows, codes), F32),
        ]
        + tile_scratch(rows, dim, codes, width),
        compiler_params=pltpu.CompilerParams(vmem_limit_bytes=VMEM_LIMIT),
        cost_estimate=cost(rows, width, dim, codes),
        name="small_images",
    )(*orders, *in_hbm([*feats, *noises, *cots, *params[0:3]]), *params[3:5])


def wide_kernel(count, slots, grown, form, *refs):
    table_ref, feat_ref, noise_ref, cot_ref = refs[0:4]
    params = refs[4:9]
    acc_in = refs[9]
    outs = refs[11:] if grown else refs[10:]
    sends = outs[0 : count - 1]
    grad_ref, acc_ref = outs[count - 1 : count + 1]
    code_scr = outs[count + 1]
    scr = outs[count + 2 :]
    step = pl.program_id(0)

    @pl.when(step == 0)
    def _():
        prepare(params, *scr[0:3])
        acc_ref[...] = acc_in[...]

    grad_ref[...] = tile(
        params, scr, feat_ref[...], cot_ref[...], noise_ref, code_scr, acc_ref, *form
    )
    for i in range(count - 1):

        @pl.when(lax.div(step, slots) == i)
        def _(i=i):
            sends[i][...] = code_scr[...]


def run_wide(count, first, slots, table, feat, noise, cot, params, acc, grad):
    dim, codes = params[2].shape
    images, strip, width = feat.shape
    share = images // count
    smem = pl.BlockSpec(memory_space=pltpu.SMEM)

    def image(i, table_ref):
        peer = lax.div(i, slots) + 1
        return (table_ref[0, peer * share + first + lax.rem(i, slots)], 0, 0)

    def fixed(shape):
        return pl.BlockSpec(shape, lambda i, table_ref: (0,) * len(shape))

    def send(peer):
        return pl.BlockSpec(
            (strip, codes),
            lambda i, table_ref: (jnp.clip(i - peer * slots, 0, slots - 1), 0),
        )

    grown = grad is not None
    return pl.pallas_call(
        functools.partial(wide_kernel, count, slots, grown, FORMS[min(first, 2)]),
        grid_spec=pltpu.PrefetchScalarGridSpec(
            num_scalar_prefetch=1,
            grid=((count - 1) * slots,),
            in_specs=[
                pl.BlockSpec((None, strip, width), image),
                pl.BlockSpec((None, strip, codes), image),
                pl.BlockSpec((None, dim, strip), image),
                fixed(params[0].shape),
                fixed(params[1].shape),
                fixed(params[2].shape),
                smem,
                smem,
                fixed(acc.shape),
            ]
            + ([pl.BlockSpec(memory_space=pl.ANY)] if grown else []),
            out_specs=[send(peer) for peer in range(count - 1)]
            + [pl.BlockSpec((None, strip, width), image), fixed(acc.shape)],
            scratch_shapes=[pltpu.VMEM((strip, codes), F32)]
            + tile_scratch(strip, dim, codes, width),
        ),
        out_shape=[jax.ShapeDtypeStruct((strip * slots, codes), F32)] * (count - 1)
        + [pltpu.HBM(feat.shape, F32), pltpu.HBM(acc.shape, F32)],
        input_output_aliases={10: count - 1, 9: count} if grown else {9: count},
        compiler_params=pltpu.CompilerParams(vmem_limit_bytes=VMEM_LIMIT),
        cost_estimate=cost((count - 1) * slots * strip, width, dim, codes),
        name="wide_images",
    )(
        table,
        *in_hbm([feat, noise, cot, *params[0:3]]),
        *params[3:5],
        *in_hbm([acc] + ([grad] if grown else [])),
    )


def shard_at(index, parts):
    height = 64 // parts
    return pl.ds(pl.multiple_of(index * height, height), height)


def own_kernel(devices, *refs):
    table_ref, feat_ref, noise_ref, cot_ref = refs[0:4]
    params = refs[4:9]
    acc_in = refs[9]
    code_ref, grad_ref = refs[11:13]
    shards = refs[13 : 13 + devices]
    acc_ref, sum_scr = refs[13 + devices : 15 + devices]
    scr = refs[15 + devices :]
    weight_ref, bias_ref, book_ref, log_ref, heat_ref = params
    dim, codes = book_ref.shape
    width = weight_ref.shape[1]
    step = pl.program_id(0)
    me = lax.rem(lax.axis_index("dp"), devices)

    @pl.when(step == 0)
    def _():
        prepare(params, *scr[0:3])
        acc_ref[...] = acc_in[...]

    grad_ref[...] = tile(
        params, scr, feat_ref[...], cot_ref[...], noise_ref, code_ref, acc_ref, *FORMS[3]
    )

    @pl.when(step == pl.num_programs(0) - 1)
    def _():
        precision, _, factor = scalars(log_ref, heat_ref)
        book = book_ref[...]
        column = acc_ref[128:129]
        moment = acc_ref[64:128] * (1.0 / precision)
        book_sum = acc_ref[0:64] * (1.0 / factor) + 2.0 * (column * book - moment)
        slope = jnp.sum(
            jnp.sum(book * book, axis=0, keepdims=True) * column, axis=1, keepdims=True
        ) - 2.0 * jnp.sum(
            jnp.sum(book * moment, axis=0, keepdims=True), axis=1, keepdims=True
        )
        slope = slope + acc_ref[208:209, 0:1] / (-0.5 * precision)
        usage = jnp.sum(acc_ref[136:144], axis=0, keepdims=True)
        sum_scr[:, 0:codes] = book_sum
        sum_scr[:, codes : codes + width + 128] = acc_ref[144:208, 0 : width + 128]
        rows = codes // 128
        for i in range(rows):
            sum_scr[i : i + 1, LANES - 128 : LANES] = usage[:, i * 128 : (i + 1) * 128]
        sum_scr[rows:64, LANES - 128 : LANES] = jnp.broadcast_to(slope, (64 - rows, 128))
        for i in range(devices):
            shards[i][...] = sum_scr[shard_at(partner(me, i, devices), devices)]


def run_own(count, devices, table, feat, noise, cot, params, acc, grad):
    dim, codes = params[2].shape
    images, strip, width = feat.shape
    share = images // count
    smem = pl.BlockSpec(memory_space=pltpu.SMEM)

    def image(i, table_ref):
        return (table_ref[0, i], 0, 0)

    def fixed(shape):
        return pl.BlockSpec(shape, lambda i, table_ref: (0,) * len(shape))

    height = 64 // devices
    return pl.pallas_call(
        functools.partial(own_kernel, devices),
        grid_spec=pltpu.PrefetchScalarGridSpec(
            num_scalar_prefetch=1,
            grid=(share,),
            in_specs=[
                pl.BlockSpec((None, strip, width), image),
                pl.BlockSpec((None, strip, codes), image),
                pl.BlockSpec((None, dim, strip), image),
                fixed(params[0].shape),
                fixed(params[1].shape),
                fixed(params[2].shape),
                smem,
                smem,
                fixed(acc.shape),
                pl.BlockSpec(memory_space=pl.ANY),
            ],
            out_specs=[
                pl.BlockSpec(
                    (None, strip, codes),
                    lambda i, table_ref: (i, table_ref[0, count * share], 0),
                ),
                pl.BlockSpec((None, strip, width), image),
            ]
            + [fixed((height, LANES))] * devices,
            scratch_shapes=[
                pltpu.VMEM(acc.shape, F32),
                pltpu.VMEM((64, LANES), F32),
            ]
            + tile_scratch(strip, dim, codes, width),
        ),
        out_shape=[
            pltpu.HBM((share, strip * count, codes), F32),
            pltpu.HBM(feat.shape, F32),
        ]
        + [jax.ShapeDtypeStruct((height, LANES), F32)] * devices,
        input_output_aliases={10: 1},
        compiler_params=pltpu.CompilerParams(vmem_limit_bytes=VMEM_LIMIT),
        cost_estimate=cost(share * strip, width, dim, codes),
        name="own_images",
    )(
        table,
        *in_hbm([feat, noise, cot, *params[0:3]]),
        *params[3:5],
        *in_hbm([acc, grad]),
    )


def place_kernel(count, first, slots, *refs):
    parts = refs[0 : count - 1]
    out_ref, sem = refs[count], refs[count + 1]
    strip = parts[0].shape[0] // slots
    me = lax.axis_index("space")
    copies = []
    for step in range(1, count):
        row = pl.multiple_of(source(me, step, count) * strip, strip)
        for j in range(slots):
            copies.append(
                pltpu.make_async_copy(
                    parts[step - 1].at[pl.ds(j * strip, strip)],
                    out_ref.at[first + j, pl.ds(row, strip)],
                    sem.at[(step - 1) * slots + j],
                )
            )
    for copy in copies:
        copy.start()
    for copy in copies:
        copy.wait()


def place_wide(count, first, slots, parts, whole):
    return pl.pallas_call(
        functools.partial(place_kernel, count, first, slots),
        out_shape=pltpu.HBM(whole.shape, F32),
        in_specs=[pl.BlockSpec(memory_space=pltpu.VMEM)] * (count - 1)
        + [pl.BlockSpec(memory_space=pltpu.HBM)],
        out_specs=pl.BlockSpec(memory_space=pltpu.HBM),
        scratch_shapes=[pltpu.SemaphoreType.DMA(((count - 1) * slots,))],
        input_output_aliases={count - 1: 0},
        compiler_params=pltpu.CompilerParams(vmem_limit_bytes=VMEM_LIMIT),
        cost_estimate=pl.CostEstimate(
            flops=0, bytes_accessed=2 * sum(p.size * 4 for p in parts), transcendentals=0
        ),
        name="place_wide",
    )(*parts, *in_hbm([whole]))


def join_kernel(count, *refs):
    parts = refs[0:count]
    outs = refs[count:]
    me = lax.axis_index("space")
    for step in range(count):
        here = source(me, step, count)
        base = 0
        for out in outs:
            for j in range(out.shape[0]):
                strip = out.shape[2]
                out[j, here] = parts[step][base : base + strip]
                base += strip


def join_small(count, parts, shapes):
    codes = parts[0].shape[1]
    return pl.pallas_call(
        functools.partial(join_kernel, count),
        out_shape=[
            jax.ShapeDtypeStruct((images // count, count, strip, codes), F32)
            for images, strip, _ in shapes
        ],
        compiler_params=pltpu.CompilerParams(vmem_limit_bytes=VMEM_LIMIT),
        name="join_small",
    )(*parts)


def tree(values):
    while len(values) > 1:
        values = [
            values[i] + values[i + 1] if i + 1 < len(values) else values[i]
            for i in range(0, len(values), 2)
        ]
    return values[0]


def sum_kernel(*refs):
    refs[-1][...] = tree([ref[...] for ref in refs[:-1]])


def add_all(parts):
    return pl.pallas_call(
        sum_kernel,
        out_shape=jax.ShapeDtypeStruct(parts[0].shape, F32),
        name="add_parts",
    )(*parts)


def final_kernel(devices, pixels, *refs):
    shards = refs[0:devices]
    weight_ref, bias_ref, book_ref, log_ref, usage_ref = refs[devices : devices + 5]
    weight_out, bias_out, book_out, log_out, usage_out = refs[devices + 5 : devices + 10]
    sum_scr = refs[devices + 10]
    me = lax.rem(lax.axis_index("dp"), devices)
    for i in range(devices):
        sum_scr[shard_at(source(me, i, devices), devices)] = shards[i][...]
    dim, codes = book_ref.shape
    width = weight_ref.shape[1]
    scale = 0.5 * lax.rsqrt(jnp.full((8, 128), pixels, F32))[0:1, 0:1]
    book_out[...] = 0.5 * book_ref[...] + scale * sum_scr[:, 0:codes]
    weight_out[...] = 0.5 * weight_ref[...] + scale * sum_scr[:, codes : codes + width]
    eye = lax.broadcasted_iota(jnp.int32, (dim, dim), 0) == lax.broadcasted_iota(
        jnp.int32, (dim, dim), 1
    )
    bias = sum_scr[:, codes + width : codes + width + dim]
    bias = jnp.sum(jnp.where(eye, bias, 0.0), axis=0, keepdims=True)
    bias_out[...] = 0.5 * bias_ref[...] + scale * bias
    rows = codes // 128
    usage = jnp.concatenate(
        [sum_scr[i : i + 1, LANES - 128 : LANES] for i in range(rows)], axis=1
    )
    usage_out[...] = 0.5 * usage_ref[...] + 0.5 * (codes / pixels) * usage
    log_out[...] = 0.5 * log_ref[...] + scale * sum_scr[rows : rows + 1, LANES - 128 : LANES - 127]


def finish(devices, pixels, shards, weight, bias, book, log, usage):
    outs = (weight.T, bias.reshape(1, -1), book.T, log.reshape(1, 1), usage.reshape(1, -1))
    outs = pl.pallas_call(
        functools.partial(final_kernel, devices, pixels),
        out_shape=[jax.ShapeDtypeStruct(out.shape, F32) for out in outs],
        scratch_shapes=[pltpu.VMEM((64, LANES), F32)],
        name="new_averages",
    )(*shards, *outs)
    return outs[0].T, outs[1].reshape(-1), outs[2].T, outs[3].reshape(-1), outs[4].reshape(-1)


def exchange(value, bit, size, pairs):
    while bit < size:
        ways = min(4, size // bit)
        value = tree([value] + [pairs(value, way * bit) for way in range(1, ways)])
        bit = bit * ways
    return value


def spans(share):
    if share < 4:
        return [(0, share)]
    return [(0, 1), (1, share - 1)]


def per_device(
    feat_small,
    feat_mid,
    feat_wide,
    noise_small,
    noise_mid,
    noise_wide,
    cot_small,
    cot_mid,
    cot_wide,
    order_small,
    order_mid,
    order_wide,
    weight,
    bias,
    book,
    log,
    heat,
    weight_mean,
    bias_mean,
    book_mean,
    log_mean,
    usage_mean,
):
    count = lax.axis_size("space")
    devices = lax.axis_size("dp")
    params = (weight.T, bias.reshape(1, -1), book.T, log, heat)
    feats = (feat_small, feat_mid, feat_wide)
    pixels = sum(f.shape[0] * f.shape[1] for f in feats) * count * devices
    share = feat_wide.shape[0] // count
    cot_wide = jnp.swapaxes(cot_wide, 1, 2)

    def send(values, axis, size):
        return [lax.ppermute(v, axis, route(i + 1, size)) for i, v in enumerate(values)]

    *small, grad_small, grad_mid, acc, table = run_small(
        count,
        (order_small, order_mid, order_wide),
        feats[0:2],
        (noise_small, noise_mid),
        (cot_small, cot_mid),
        params,
    )
    arrived = [send(small[1:], "space", count)]
    grad = None
    for first, slots in spans(share):
        *codes, grad, acc = run_wide(
            count, first, slots, table, feat_wide, noise_wide, cot_wide, params, acc, grad
        )
        for i in range(count - 1):
            arrived[-1][i], codes[i] = lax.optimization_barrier((arrived[-1][i], codes[i]))
        arrived.append(send(codes, "space", count))
    arrived[-2], acc = lax.optimization_barrier((arrived[-2], acc))
    near = min(4, devices)
    whole, grad, *shards = run_own(
        count, near, table, feat_wide, noise_wide, cot_wide, params, acc, grad
    )
    group = [
        [(i, i - i % near + partner(i % near, step, near)) for i in range(devices)]
        for step in range(near)
    ]
    parts = [lax.ppermute(shards[i], "dp", group[i]) for i in range(1, near)]
    mine = add_all([shards[0]] + parts)

    def along(value, offset):
        return lax.ppermute(value, "dp", [(i, i ^ offset) for i in range(devices)])

    def across(value, offset):
        turn = near if devices > near else 0
        pairs = [
            (i * count + j, (i ^ turn) * count + (j ^ offset))
            for i in range(devices)
            for j in range(count)
        ]
        return lax.ppermute(value, ("dp", "space"), pairs)

    mine = exchange(mine, near, devices, along)
    mine = exchange(mine, 1, count, across)
    shards = [mine] + [lax.ppermute(mine, "dp", group[i]) for i in range(1, near)]
    updated = finish(
        near, pixels, shards, weight_mean, bias_mean, book_mean, log_mean, usage_mean
    )
    codes_small, codes_mid = join_small(
        count, [small[0]] + arrived[0], [f.shape for f in feats[0:2]]
    )
    for (first, slots), parts in zip(spans(share), arrived[1:]):
        whole = place_wide(count, first, slots, parts, whole)
    codes = whole.shape[2]
    return (
        codes_small.reshape(codes_small.shape[0], -1, codes),
        codes_mid.reshape(codes_mid.shape[0], -1, codes),
        whole,
        grad_small,
        grad_mid,
        grad,
        *updated,
    )


def solution(mesh):
    strips = P("dp", "space", None)
    placed = (strips,) * 9 + (P("dp", None),) * 3 + (P(),) * 10
    return jax.shard_map(
        per_device,
        mesh=mesh,
        in_specs=placed,
        out_specs=(P(("dp", "space"), None, None),) * 3 + (strips,) * 3 + (P(),) * 5,
        check_vma=False,
    )
```

```python
import functools

import jax
import jax.numpy as jnp
from jax import lax
from jax.experimental import pallas as pl
from jax.experimental.pallas import tpu as pltpu
from jax.sharding import PartitionSpec as P

F32 = jnp.float32
BF16 = jnp.bfloat16
VMEM_LIMIT = 24 * 1024 * 1024
ACC_ROWS = 64 + 64 + 8 + 8 + 64 + 8
LANES = 1024


def partner(index, step, count):
    if count & (count - 1) == 0:
        return index ^ step
    return lax.rem(index + step, count)


def route(step, count):
    if count & (count - 1) == 0:
        return [(i, i ^ step) for i in range(count)]
    return [(i, (i + step) % count) for i in range(count)]


def source(index, step, count):
    if count & (count - 1) == 0:
        return index ^ step
    return lax.rem(index + (count - step), count)


def in_hbm(arrays):
    return [pltpu.with_memory_space_constraint(a, pltpu.HBM) for a in arrays]


def halves(x):
    high = x.astype(BF16)
    return high, (x - high.astype(F32)).astype(BF16)


def dot(left, right, left_dim=1, right_dim=0):
    return lax.dot_general(
        left, right, (((left_dim,), (right_dim,)), ((), ())), preferred_element_type=F32
    )


def set_scalars(log_ref, heat_ref, out_ref):
    precision = jnp.exp(jnp.full((8, 128), log_ref[0], F32))
    heat = jnp.full((8, 128), heat_ref[0], F32)
    row = lax.broadcasted_iota(jnp.int32, (8, 128), 0)
    factor = -0.5 * precision / heat
    out_ref[...] = jnp.where(row == 0, precision, jnp.where(row == 1, 1.0 / heat, factor))


def scalars(ref):
    return ref[0:1, 0:1], ref[1:2, 0:1], ref[2:3, 0:1]


def prepare(refs, book_scr, books_scr, weight_scr):
    weight_ref, bias_ref, book_ref, scalar_ref = refs
    dim, codes = book_ref.shape
    precision, _, _ = scalars(scalar_ref)
    book = book_ref[...]
    high, low = halves(book)
    norm = -0.5 * precision * jnp.sum(book * book, axis=0, keepdims=True)
    n0 = norm.astype(BF16).astype(F32)
    n1 = (norm - n0).astype(BF16).astype(F32)
    n2 = norm - n0 - n1
    row = lax.broadcasted_iota(jnp.int32, (16, codes), 0)
    extra = jnp.where(
        row < 3,
        1.0,
        jnp.where(row == 3, n0, jnp.where(row == 4, n1, jnp.where(row == 5, n2, 0.0))),
    ).astype(BF16)
    book_scr[0:dim] = high
    book_scr[dim : 2 * dim] = low
    book_scr[2 * dim : 3 * dim] = high
    book_scr[3 * dim : 3 * dim + 16] = extra
    books_scr[0:dim] = high
    books_scr[dim : 2 * dim] = low
    books_scr[2 * dim : 2 * dim + 16] = jnp.ones((16, codes), BF16)
    high, low = halves(weight_ref[...])
    weight_scr[0:dim] = high
    weight_scr[dim : 2 * dim] = low
    weight_scr[2 * dim : 3 * dim] = high


def latents(refs, scr, feat):
    weight_ref, bias_ref, book_ref, scalar_ref = refs
    weight_scr = scr[2]
    dim = book_ref.shape[0]
    precision, _, _ = scalars(scalar_ref)
    eye = lax.broadcasted_iota(jnp.int32, (dim, dim), 0) == lax.broadcasted_iota(
        jnp.int32, (dim, dim), 1
    )
    bias = jnp.sum(jnp.where(eye, bias_ref[...], 0.0), axis=1, keepdims=True)
    fh, fl = halves(feat)
    both = weight_scr[0 : 2 * dim]
    z2 = dot(both, fh, 1, 1) + dot(both, fl, 1, 1)
    z = z2[0:dim] + z2[dim : 2 * dim] + bias
    square = -0.5 * precision * jnp.sum(z * z, axis=0, keepdims=True)
    return fh, fl, z, square


def logit_rows(zh, zl, square):
    rows = zh.shape[1]
    s0 = square.astype(BF16).astype(F32)
    s1 = (square - s0).astype(BF16).astype(F32)
    s2 = square - s0 - s1
    row = lax.broadcasted_iota(jnp.int32, (16, rows), 0)
    extra = jnp.where(
        row == 0,
        s0,
        jnp.where(row == 1, s1, jnp.where(row == 2, s2, jnp.where(row < 6, 1.0, 0.0))),
    ).astype(BF16)
    return jnp.concatenate([zh, zh, zl, extra], axis=0)


def cot_rows(ch, cl):
    return jnp.concatenate([ch, ch, cl, jnp.zeros((16, ch.shape[1]), BF16)], axis=0)


def over_rows(rows, body, carry):
    step = 32 if rows % 32 == 0 else 16

    def at(i, carry):
        return body(pl.ds(pl.multiple_of(i * step, step), step), carry)

    return lax.fori_loop(0, rows // step, at, carry, unroll=True)


def folded(x):
    return jnp.sum(x.reshape(x.shape[0] // 8, 8, x.shape[1]), axis=0)


def probabilities(logits):
    top = jnp.max(logits, axis=1, keepdims=True)
    e = jnp.exp(logits - top)
    return e * (1.0 / jnp.sum(e, axis=1, keepdims=True))


def forward(refs, scr, feat, noise_ref, code_ref, usage_ref):
    weight_ref, bias_ref, book_ref, scalar_ref = refs
    book_scr, l_scr = scr[0], scr[3]
    rows = feat.shape[0]
    precision, cold, _ = scalars(scalar_ref)
    _, _, z, square = latents(refs, scr, feat)
    zh, zl = halves(precision * z)
    l_scr[0:rows] = dot(logit_rows(zh, zl, square), book_scr[...], 0, 0)

    def body(at, usage):
        logits = l_scr[at]
        code_ref[at] = probabilities((logits + noise_ref[at]) * cold)
        return usage + folded(probabilities(logits))

    usage_ref[...] = over_rows(rows, body, usage_ref[...])


def gradients(refs, scr, fh, fl, z, square, zh, zl, ch, cl, acc_ref):
    books_scr, weight_scr = scr[1:3]
    wh_scr, wl_scr, gh_scr, gl_scr = scr[5:9]
    rows, feats = fh.shape
    dim, codes = refs[2].shape
    wh, wl = wh_scr[0:rows], wl_scr[0:rows]
    gh, gl = gh_scr[0:rows], gl_scr[0:rows]
    p = dot(jnp.concatenate([ch, cl], axis=0), wh)
    acc_ref[0:64] += p[0:dim] + p[dim : 2 * dim] + dot(ch, wl)
    left = jnp.concatenate([zh, zl, jnp.ones((16, rows), BF16)], axis=0)
    p = dot(left, gh) + dot(left, gl)
    acc_ref[64:128] += p[0:dim] + p[dim : 2 * dim]
    acc_ref[128:136] += p[2 * dim : 2 * dim + 8]
    p = dot(books_scr[...], gh, 1, 1) + dot(books_scr[...], gl, 1, 1)
    row_d = p[2 * dim : 2 * dim + 1]
    gz = 2.0 * (row_d * z - (p[0:dim] + p[dim : 2 * dim]))
    zh, zl = halves(gz)
    p = dot(jnp.concatenate([zh, zl], axis=0), fh)
    acc_ref[144:208, 0:feats] += p[0:dim] + p[dim : 2 * dim] + dot(zh, fl)
    acc_ref[144:208, feats : feats + 128] += jnp.broadcast_to(
        jnp.sum(gz, axis=1, keepdims=True), (dim, 128)
    )
    total = jnp.sum(square * row_d, axis=1, keepdims=True)
    acc_ref[208:216] += jnp.broadcast_to(total, (8, codes))
    return dot(jnp.concatenate([zh, zh, zl], axis=0), weight_scr[...], 0, 0)


def backward(refs, scr, feat, cot, code_ref, acc_ref):
    weight_ref, bias_ref, book_ref, scalar_ref = refs
    book_scr, _, _, _, g_scr, wh_scr, wl_scr, gh_scr, gl_scr = scr
    rows = feat.shape[0]
    precision, _, factor = scalars(scalar_ref)
    fh, fl, z, square = latents(refs, scr, feat)
    zh, zl = halves(precision * z)
    ch, cl = halves(factor * cot)
    g_scr[0:rows] = dot(cot_rows(ch, cl), book_scr[...], 0, 0)

    def body(at, carry):
        w = code_ref[at]
        gw = g_scr[at]
        gd = w * (gw - jnp.sum(w * gw, axis=1, keepdims=True))
        wh_scr[at], wl_scr[at] = halves(w)
        gh_scr[at], gl_scr[at] = halves(gd)
        return carry

    over_rows(rows, body, 0)
    return gradients(refs, scr, fh, fl, z, square, zh, zl, ch, cl, acc_ref)


def both_ways(refs, scr, feat, cot, noise_ref, code_ref, acc_ref):
    weight_ref, bias_ref, book_ref, scalar_ref = refs
    book_scr, _, _, l_scr, g_scr, wh_scr, wl_scr, gh_scr, gl_scr = scr
    rows = feat.shape[0]
    precision, cold, factor = scalars(scalar_ref)
    fh, fl, z, square = latents(refs, scr, feat)
    zh, zl = halves(precision * z)
    ch, cl = halves(factor * cot)
    left = jnp.concatenate([logit_rows(zh, zl, square), cot_rows(ch, cl)], axis=1)
    p = dot(left, book_scr[...], 0, 0)
    l_scr[0:rows] = p[0:rows]
    g_scr[0:rows] = p[rows : 2 * rows]

    def body(at, usage):
        logits = l_scr[at]
        s = (logits + noise_ref[at]) * cold
        e = jnp.exp(s - jnp.max(s, axis=1, keepdims=True))
        gw = g_scr[at]
        scale = 1.0 / jnp.sum(e, axis=1, keepdims=True)
        inner = jnp.sum(e * gw, axis=1, keepdims=True) * scale
        w = e * scale
        code_ref[at] = w
        gd = w * (gw - inner)
        wh_scr[at], wl_scr[at] = halves(w)
        gh_scr[at], gl_scr[at] = halves(gd)
        return usage + folded(probabilities(logits))

    acc_ref[136:144] = over_rows(rows, body, acc_ref[136:144])
    return gradients(refs, scr, fh, fl, z, square, zh, zl, ch, cl, acc_ref)


def tile_scratch(rows, dim, codes, feats):
    return [
        pltpu.VMEM((3 * dim + 16, codes), BF16),
        pltpu.VMEM((2 * dim + 16, codes), BF16),
        pltpu.VMEM((3 * dim, feats), BF16),
        pltpu.VMEM((rows, codes), F32),
        pltpu.VMEM((rows, codes), F32),
        pltpu.VMEM((rows, codes), BF16),
        pltpu.VMEM((rows, codes), BF16),
        pltpu.VMEM((rows, codes), BF16),
        pltpu.VMEM((rows, codes), BF16),
    ]


def settings():
    return pltpu.CompilerParams(vmem_limit_bytes=VMEM_LIMIT)


def cost(rows, feats, dim, codes, tenths):
    return pl.CostEstimate(
        flops=rows * 24 * tenths * (5 * dim * codes + 3 * dim * feats) // 10,
        bytes_accessed=4 * rows * (2 * feats + 2 * codes + dim),
        transcendentals=2 * rows * codes,
    )


SMEM = pl.BlockSpec(memory_space=pltpu.SMEM)
VMEM = pl.BlockSpec(memory_space=pltpu.VMEM)
HBM = pl.BlockSpec(memory_space=pltpu.HBM)


def fixed(shape):
    return pl.BlockSpec(shape, lambda *_: (0,) * len(shape))


def part_rows(peer, slots, shape):
    return pl.BlockSpec(shape, lambda i, _: (jnp.clip(i - peer * slots, 0, slots - 1), 0))


def places_of(table_ref, wide, shapes, groups, count):
    places = []
    base = 0
    entry = wide + 1
    for _ in range(count):
        for size in range(2):
            strip = shapes[size][1]
            for _ in range(groups[size]):
                places.append((size, table_ref[0, entry], base, strip))
                base += strip
                entry += 1
    return places, base


def small_forward_kernel(count, groups, *refs):
    sources = refs[0:10]
    log_ref, heat_ref = refs[10:12]
    sends = refs[12 : 12 + count]
    table_ref, usage_ref, scalar_ref = refs[12 + count : 15 + count]
    held = refs[15 + count : 25 + count]
    sems, feat_scr, noise_scr, code_scr = refs[25 + count : 29 + count]
    scr = refs[29 + count :]
    copies = [
        pltpu.make_async_copy(there, here, sems.at[i])
        for i, (there, here) in enumerate(zip(sources, held))
    ]
    for copy in copies:
        copy.start()
    orders, feats, noises, params = held[0:3], held[3:5], held[5:7], (*held[7:10], scalar_ref)
    me = lax.axis_index("space")
    set_scalars(log_ref, heat_ref, scalar_ref)
    for copy in copies[7:10]:
        copy.wait()
    prepare(params, *scr[0:3])
    for copy in copies[0:5]:
        copy.wait()
    wide = orders[2].shape[1]
    share = wide // count
    entry = wide + 1
    table_ref[0, wide] = me
    for step in range(count):
        there = partner(me, step, count)
        for j in range(share):
            table_ref[0, step * share + j] = orders[2][0, there * share + j]
        for size in range(2):
            for j in range(groups[size]):
                table_ref[0, entry] = orders[size][0, there * groups[size] + j]
                entry += 1
    places, base = places_of(table_ref, wide, [f.shape for f in feats], groups, count)
    for size, image, at, strip in places:
        feat_scr[at : at + strip] = feats[size][image]
    for copy in copies[5:7]:
        copy.wait()
    for size, image, at, strip in places:
        noise_scr[at : at + strip] = noises[size][image]
    usage_ref[...] = jnp.zeros(usage_ref.shape, F32)
    forward(params, scr, feat_scr[...], noise_scr, code_scr, usage_ref)
    part = base // count
    for step in range(count):
        sends[step][...] = code_scr[step * part : (step + 1) * part]


def small_forward(count, orders, feats, noises, params):
    dim, codes = params[2].shape
    width = feats[0].shape[2]
    groups = tuple(f.shape[0] // count for f in feats)
    part = sum(g * f.shape[1] for g, f in zip(groups, feats))
    rows = part * count
    arrays = [*orders, *feats, *noises, *params[0:3]]
    return pl.pallas_call(
        functools.partial(small_forward_kernel, count, groups),
        out_shape=[jax.ShapeDtypeStruct((part, codes), F32)] * count
        + [
            jax.ShapeDtypeStruct((1, sum(o.shape[1] for o in orders) + 1), jnp.int32),
            pltpu.HBM((8, codes), F32),
            pltpu.HBM((8, 128), F32),
        ],
        in_specs=[HBM] * 10 + [SMEM] * 2,
        out_specs=[VMEM] * count + [SMEM, VMEM, VMEM],
        scratch_shapes=[
            (pltpu.SMEM if i < 3 else pltpu.VMEM)(a.shape, a.dtype)
            for i, a in enumerate(arrays)
        ]
        + [
            pltpu.SemaphoreType.DMA((10,)),
            pltpu.VMEM((rows, width), F32),
            pltpu.VMEM((rows, codes), F32),
            pltpu.VMEM((rows, codes), F32),
        ]
        + tile_scratch(rows, dim, codes, width),
        compiler_params=settings(),
        cost_estimate=cost(rows, width, dim, codes, 4),
        name="small_forward",
    )(*in_hbm(arrays), *params[3:5])


def small_backward_kernel(count, wide, groups, *refs):
    table_ref = refs[0]
    feats, cots = refs[1:3], refs[3:5]
    parts = refs[5 : 5 + count]
    params = refs[5 + count : 9 + count]
    acc_in = refs[9 + count]
    grads = refs[10 + count : 12 + count]
    acc_ref = refs[12 + count]
    feat_scr, cot_scr, code_scr = refs[13 + count : 16 + count]
    scr = refs[16 + count :]
    places, base = places_of(table_ref, wide, [f.shape for f in feats], groups, count)
    for size, image, at, strip in places:
        feat_scr[at : at + strip] = feats[size][image]
        cot_scr[at : at + strip] = cots[size][image]
    part = base // count
    for step in range(count):
        code_scr[step * part : (step + 1) * part] = parts[step][...]
    prepare(params, *scr[0:3])
    acc_ref[...] = acc_in[...]
    feat_scr[...] = backward(params, scr, feat_scr[...], cot_scr[...].T, code_scr, acc_ref)
    for size, image, at, strip in places:
        grads[size][image] = feat_scr[at : at + strip]


def small_backward(count, wide, table, feats, cots, parts, params, acc):
    dim, codes = params[2].shape
    width = feats[0].shape[2]
    groups = tuple(f.shape[0] // count for f in feats)
    rows = parts[0].shape[0] * count
    return pl.pallas_call(
        functools.partial(small_backward_kernel, count, wide, groups),
        out_shape=[pltpu.HBM(f.shape, F32) for f in feats] + [pltpu.HBM(acc.shape, F32)],
        in_specs=[SMEM] + [VMEM] * (9 + count),
        out_specs=[VMEM] * 3,
        scratch_shapes=[
            pltpu.VMEM((rows, width), F32),
            pltpu.VMEM((rows, dim), F32),
            pltpu.VMEM((rows, codes), F32),
        ]
        + tile_scratch(rows, dim, codes, width),
        compiler_params=settings(),
        cost_estimate=cost(rows, width, dim, codes, 6),
        name="small_backward",
    )(
        table,
        *in_hbm([*feats, *cots]),
        *parts,
        *in_hbm([*params, acc]),
    )


def wide_forward_kernel(count, slots, *refs):
    feat_ref, noise_ref = refs[1:3]
    params = refs[3:7]
    usage_in = refs[7]
    sends = refs[8 : 7 + count]
    usage_ref = refs[7 + count]
    code_scr = refs[8 + count]
    scr = refs[9 + count :]
    step = pl.program_id(0)

    @pl.when(step == 0)
    def _():
        prepare(params, *scr[0:3])
        usage_ref[...] = usage_in[...]

    forward(params, scr, feat_ref[...], noise_ref, code_scr, usage_ref)
    for i in range(count - 1):

        @pl.when(lax.div(step, slots) == i)
        def _(i=i):
            sends[i][...] = code_scr[...]


def peer_image(count, share, first, slots):
    def image(i, table_ref):
        peer = lax.div(i, slots) + 1
        return (table_ref[0, peer * share + first + lax.rem(i, slots)], 0, 0)

    return image


def wide_forward(count, first, slots, table, feat, noise, params, usage):
    dim, codes = params[2].shape
    images, strip, width = feat.shape
    image = peer_image(count, images // count, first, slots)
    return pl.pallas_call(
        functools.partial(wide_forward_kernel, count, slots),
        grid_spec=pltpu.PrefetchScalarGridSpec(
            num_scalar_prefetch=1,
            grid=((count - 1) * slots,),
            in_specs=[
                pl.BlockSpec((None, strip, width), image),
                pl.BlockSpec((None, strip, codes), image),
                fixed(params[0].shape),
                fixed(params[1].shape),
                fixed(params[2].shape),
                fixed(params[3].shape),
                fixed(usage.shape),
            ],
            out_specs=[part_rows(i, slots, (strip, codes)) for i in range(count - 1)]
            + [fixed(usage.shape)],
            scratch_shapes=[pltpu.VMEM((strip, codes), F32)]
            + tile_scratch(strip, dim, codes, width),
        ),
        out_shape=[jax.ShapeDtypeStruct((strip * slots, codes), F32)] * (count - 1)
        + [pltpu.HBM(usage.shape, F32)],
        input_output_aliases={7: count - 1},
        compiler_params=settings(),
        cost_estimate=cost((count - 1) * slots * strip, width, dim, codes, 4),
        name="wide_forward",
    )(table, *in_hbm([feat, noise, *params, usage]))


def wide_backward_kernel(count, slots, new, devices, *refs):
    feat_ref, cot_ref = refs[1:3]
    parts = refs[3 : 2 + count]
    params = refs[2 + count : 6 + count]
    rest = refs[6 + count :]
    if not new:
        acc_in, rest = rest[0], rest[2:]
    if devices:
        usage_ref, rest = rest[0], rest[1:]
        grad_ref, shards, rest = rest[0], rest[1 : 1 + devices], rest[1 + devices :]
        acc_ref, sum_scr, rest = rest[0], rest[1], rest[2:]
    else:
        grad_ref, acc_ref, rest = rest[0], rest[1], rest[2:]
    code_scr, scr = rest[0], rest[1:]
    step = pl.program_id(0)

    @pl.when(step == 0)
    def _():
        prepare(params, *scr[0:3])
        acc_ref[...] = jnp.zeros(acc_ref.shape, F32) if new else acc_in[...]

    for i in range(count - 1):

        @pl.when(lax.div(step, slots) == i)
        def _(i=i):
            code_scr[...] = parts[i][...]

    grad_ref[...] = backward(params, scr, feat_ref[...], cot_ref[...], code_scr, acc_ref)
    if devices:

        @pl.when(step == pl.num_programs(0) - 1)
        def _():
            lay_out(params, acc_ref, usage_ref, sum_scr, shards)


def wide_backward(count, first, slots, table, feat, cot, parts, params, acc, grad, usage, devices):
    dim, codes = params[2].shape
    images, strip, width = feat.shape
    image = peer_image(count, images // count, first, slots)
    new = acc is None
    acc_shape = (ACC_ROWS, codes)
    last = usage is not None
    height = 64 // devices
    return pl.pallas_call(
        functools.partial(wide_backward_kernel, count, slots, new, devices if last else 0),
        grid_spec=pltpu.PrefetchScalarGridSpec(
            num_scalar_prefetch=1,
            grid=((count - 1) * slots,),
            in_specs=[
                pl.BlockSpec((None, strip, width), image),
                pl.BlockSpec((None, dim, strip), image),
            ]
            + [part_rows(i, slots, (strip, codes)) for i in range(count - 1)]
            + [
                fixed(params[0].shape),
                fixed(params[1].shape),
                fixed(params[2].shape),
                fixed(params[3].shape),
            ]
            + ([] if new else [fixed(acc_shape), HBM])
            + ([fixed(usage.shape)] if last else []),
            out_specs=[pl.BlockSpec((None, strip, width), image)]
            + ([fixed((height, LANES))] * devices if last else [fixed(acc_shape)]),
            scratch_shapes=(
                [pltpu.VMEM(acc_shape, F32), pltpu.VMEM((64, LANES), F32)] if last else []
            )
            + [pltpu.VMEM((strip, codes), F32)]
            + tile_scratch(strip, dim, codes, width),
        ),
        out_shape=[pltpu.HBM(feat.shape, F32)]
        + (
            [jax.ShapeDtypeStruct((height, LANES), F32)] * devices
            if last
            else [pltpu.HBM(acc_shape, F32)]
        ),
        input_output_aliases={} if new else {7 + count: 0},
        compiler_params=settings(),
        cost_estimate=cost((count - 1) * slots * strip, width, dim, codes, 6),
        name="wide_backward",
    )(
        table,
        *in_hbm([feat, cot]),
        *parts,
        *in_hbm(params),
        *in_hbm([] if new else [acc, grad]),
        *in_hbm([usage] if last else []),
    )


def shard_at(index, parts):
    height = 64 // parts
    return pl.ds(pl.multiple_of(index * height, height), height)


def lay_out(params, acc_ref, usage_ref, sum_scr, shards):
    weight_ref, bias_ref, book_ref, scalar_ref = params
    codes = book_ref.shape[1]
    width = weight_ref.shape[1]
    devices = len(shards)
    me = lax.rem(lax.axis_index("dp"), devices)
    precision, _, factor = scalars(scalar_ref)
    book = book_ref[...]
    column = acc_ref[128:129]
    moment = acc_ref[64:128] * (1.0 / precision)
    book_sum = acc_ref[0:64] * (1.0 / factor) + 2.0 * (column * book - moment)
    slope = jnp.sum(
        jnp.sum(book * book, axis=0, keepdims=True) * column, axis=1, keepdims=True
    ) - 2.0 * jnp.sum(jnp.sum(book * moment, axis=0, keepdims=True), axis=1, keepdims=True)
    slope = slope + acc_ref[208:209, 0:1] / (-0.5 * precision)
    usage = jnp.sum(acc_ref[136:144] + usage_ref[...], axis=0, keepdims=True)
    sum_scr[:, 0:codes] = book_sum
    sum_scr[:, codes : codes + width + 128] = acc_ref[144:208, 0 : width + 128]
    rows = codes // 128
    for i in range(rows):
        sum_scr[i : i + 1, LANES - 128 : LANES] = usage[:, i * 128 : (i + 1) * 128]
    sum_scr[rows:64, LANES - 128 : LANES] = jnp.broadcast_to(slope, (64 - rows, 128))
    for i in range(devices):
        shards[i][...] = sum_scr[shard_at(partner(me, i, devices), devices)]


def own_kernel(*refs):
    feat_ref, noise_ref, cot_ref = refs[1:4]
    params = refs[4:8]
    acc_in = refs[8]
    code_ref, grad_ref, acc_ref = refs[10:13]
    scr = refs[13:]

    @pl.when(pl.program_id(0) == 0)
    def _():
        prepare(params, *scr[0:3])
        acc_ref[...] = acc_in[...]

    grad_ref[...] = both_ways(
        params, scr, feat_ref[...], cot_ref[...], noise_ref, code_ref, acc_ref
    )


def run_own(count, table, feat, noise, cot, params, acc, grad):
    dim, codes = params[2].shape
    images, strip, width = feat.shape
    share = images // count

    def image(i, table_ref):
        return (table_ref[0, i], 0, 0)

    return pl.pallas_call(
        own_kernel,
        grid_spec=pltpu.PrefetchScalarGridSpec(
            num_scalar_prefetch=1,
            grid=(share,),
            in_specs=[
                pl.BlockSpec((None, strip, width), image),
                pl.BlockSpec((None, strip, codes), image),
                pl.BlockSpec((None, dim, strip), image),
                fixed(params[0].shape),
                fixed(params[1].shape),
                fixed(params[2].shape),
                fixed(params[3].shape),
                fixed(acc.shape),
                HBM,
            ],
            out_specs=[
                pl.BlockSpec(
                    (None, strip, codes),
                    lambda i, table_ref: (i, table_ref[0, count * share], 0),
                ),
                pl.BlockSpec((None, strip, width), image),
                fixed(acc.shape),
            ],
            scratch_shapes=tile_scratch(strip, dim, codes, width),
        ),
        out_shape=[
            pltpu.HBM((share, strip * count, codes), F32),
            pltpu.HBM(feat.shape, F32),
            pltpu.HBM(acc.shape, F32),
        ],
        input_output_aliases={8: 2, 9: 1},
        compiler_params=settings(),
        cost_estimate=cost(share * strip, width, dim, codes, 10),
        name="own_images",
    )(table, *in_hbm([feat, noise, cot, *params, acc, grad]))


def place_kernel(count, first, slots, *refs):
    parts = refs[0 : count - 1]
    out_ref, sem = refs[count], refs[count + 1]
    strip = parts[0].shape[0] // slots
    me = lax.axis_index("space")
    copies = []
    for step in range(1, count):
        row = pl.multiple_of(source(me, step, count) * strip, strip)
        for j in range(slots):
            copies.append(
                pltpu.make_async_copy(
                    parts[step - 1].at[pl.ds(j * strip, strip)],
                    out_ref.at[first + j, pl.ds(row, strip)],
                    sem.at[(step - 1) * slots + j],
                )
            )
    for copy in copies:
        copy.start()
    for copy in copies:
        copy.wait()


def place_wide(count, first, slots, parts, whole):
    return pl.pallas_call(
        functools.partial(place_kernel, count, first, slots),
        out_shape=pltpu.HBM(whole.shape, F32),
        in_specs=[pl.BlockSpec(memory_space=pltpu.VMEM)] * (count - 1)
        + [pl.BlockSpec(memory_space=pltpu.HBM)],
        out_specs=pl.BlockSpec(memory_space=pltpu.HBM),
        scratch_shapes=[pltpu.SemaphoreType.DMA(((count - 1) * slots,))],
        input_output_aliases={count - 1: 0},
        compiler_params=settings(),
        cost_estimate=pl.CostEstimate(
            flops=0, bytes_accessed=2 * sum(p.size * 4 for p in parts), transcendentals=0
        ),
        name="place_wide",
    )(*[pltpu.with_memory_space_constraint(p, pltpu.VMEM) for p in parts], *in_hbm([whole]))


def join_kernel(count, *refs):
    parts = refs[0:count]
    outs = refs[count:]
    me = lax.axis_index("space")
    for step in range(count):
        here = source(me, step, count)
        base = 0
        for out in outs:
            for j in range(out.shape[0]):
                strip = out.shape[2]
                out[j, here] = parts[step][base : base + strip]
                base += strip


def join_small(count, parts, shapes):
    codes = parts[0].shape[1]
    return pl.pallas_call(
        functools.partial(join_kernel, count),
        out_shape=[
            jax.ShapeDtypeStruct((images // count, count, strip, codes), F32)
            for images, strip, _ in shapes
        ],
        compiler_params=settings(),
        name="join_small",
    )(*parts)


def tree(values):
    while len(values) > 1:
        values = [
            values[i] + values[i + 1] if i + 1 < len(values) else values[i]
            for i in range(0, len(values), 2)
        ]
    return values[0]


def sum_kernel(*refs):
    refs[-1][...] = tree([ref[...] for ref in refs[:-1]])


def add_all(parts):
    return pl.pallas_call(
        sum_kernel,
        out_shape=jax.ShapeDtypeStruct(parts[0].shape, F32),
        name="add_parts",
    )(*parts)


def final_kernel(devices, pixels, *refs):
    shards = refs[0:devices]
    weight_ref, bias_ref, book_ref, log_ref, usage_ref = refs[devices : devices + 5]
    weight_out, bias_out, book_out, log_out, usage_out = refs[devices + 5 : devices + 10]
    sum_scr = refs[devices + 10]
    me = lax.rem(lax.axis_index("dp"), devices)
    for i in range(devices):
        sum_scr[shard_at(source(me, i, devices), devices)] = shards[i][...]
    dim, codes = book_ref.shape
    width = weight_ref.shape[1]
    scale = 0.5 * lax.rsqrt(jnp.full((8, 128), pixels, F32))[0:1, 0:1]
    book_out[...] = 0.5 * book_ref[...] + scale * sum_scr[:, 0:codes]
    weight_out[...] = 0.5 * weight_ref[...] + scale * sum_scr[:, codes : codes + width]
    eye = lax.broadcasted_iota(jnp.int32, (dim, dim), 0) == lax.broadcasted_iota(
        jnp.int32, (dim, dim), 1
    )
    bias = sum_scr[:, codes + width : codes + width + dim]
    bias = jnp.sum(jnp.where(eye, bias, 0.0), axis=0, keepdims=True)
    bias_out[...] = 0.5 * bias_ref[...] + scale * bias
    rows = codes // 128
    usage = jnp.concatenate(
        [sum_scr[i : i + 1, LANES - 128 : LANES] for i in range(rows)], axis=1
    )
    usage_out[...] = 0.5 * usage_ref[...] + 0.5 * (codes / pixels) * usage
    log_out[...] = 0.5 * log_ref[...] + scale * sum_scr[rows : rows + 1, LANES - 128 : LANES - 127]


def finish(devices, pixels, shards, weight, bias, book, log, usage):
    outs = (weight.T, bias.reshape(1, -1), book.T, log.reshape(1, 1), usage.reshape(1, -1))
    outs = pl.pallas_call(
        functools.partial(final_kernel, devices, pixels),
        out_shape=[jax.ShapeDtypeStruct(out.shape, F32) for out in outs],
        scratch_shapes=[pltpu.VMEM((64, LANES), F32)],
        name="new_averages",
    )(*shards, *outs)
    return outs[0].T, outs[1].reshape(-1), outs[2].T, outs[3].reshape(-1), outs[4].reshape(-1)


def exchange(value, bit, size, pairs):
    while bit < size:
        ways = min(4, size // bit)
        value = tree([value] + [pairs(value, way * bit) for way in range(1, ways)])
        bit = bit * ways
    return value


def spans(share):
    return [(0, 1), (1, share - 1)]


def per_device(
    feat_small,
    feat_mid,
    feat_wide,
    noise_small,
    noise_mid,
    noise_wide,
    cot_small,
    cot_mid,
    cot_wide,
    order_small,
    order_mid,
    order_wide,
    weight,
    bias,
    book,
    log,
    heat,
    weight_mean,
    bias_mean,
    book_mean,
    log_mean,
    usage_mean,
):
    count = lax.axis_size("space")
    devices = lax.axis_size("dp")
    params = (weight.T, bias.reshape(1, -1), book.T, log, heat)
    feats = (feat_small, feat_mid, feat_wide)
    pixels = sum(f.shape[0] * f.shape[1] for f in feats) * count * devices
    share = feat_wide.shape[0] // count
    cot_wide = jnp.swapaxes(cot_wide, 1, 2)

    def send(values):
        return [lax.ppermute(v, "space", route(i + 1, count)) for i, v in enumerate(values)]

    def follow(codes, before):
        before[0], codes[-1] = lax.optimization_barrier((before[0], codes[-1]))
        return send(codes)

    orders = (order_small, order_mid, order_wide)
    *small, table, usage, scalar = small_forward(
        count, orders, feats[0:2], (noise_small, noise_mid), params
    )
    params = (*params[0:3], scalar)
    arrived = [send(small[1:])]
    codes = []
    for first, slots in spans(share):
        *part, usage = wide_forward(
            count, first, slots, table, feat_wide, noise_wide, params, usage
        )
        codes.append(part)
        arrived.append(follow(list(part), arrived[-1]))
    near = min(4, devices)
    grad, acc = wide_backward(
        count, *spans(share)[0], table, feat_wide, cot_wide, codes[0], params, None, None, None, near
    )
    codes_small, codes_mid = join_small(
        count, [small[0]] + arrived[0], [f.shape for f in feats[0:2]]
    )
    codes_small, codes_mid, acc = lax.optimization_barrier((codes_small, codes_mid, acc))
    whole, grad, acc = run_own(
        count, table, feat_wide, noise_wide, cot_wide, params, acc, grad
    )
    whole = place_wide(count, *spans(share)[0], arrived[1], whole)
    whole, acc = lax.optimization_barrier((whole, acc))
    grad_small, grad_mid, acc = small_backward(
        count, feat_wide.shape[0], table, feats[0:2], (cot_small, cot_mid), small, params, acc
    )
    grad, *shards = wide_backward(
        count, *spans(share)[1], table, feat_wide, cot_wide, codes[1], params, acc, grad, usage, near
    )
    group = [
        [(i, i - i % near + partner(i % near, step, near)) for i in range(devices)]
        for step in range(near)
    ]
    parts = [lax.ppermute(shards[i], "dp", group[i]) for i in range(1, near)]
    mine = add_all([shards[0]] + parts)

    def along(value, offset):
        return lax.ppermute(value, "dp", [(i, i ^ offset) for i in range(devices)])

    def across(value, offset):
        turn = near if devices > near else 0
        pairs = [
            (i * count + j, (i ^ turn) * count + (j ^ offset))
            for i in range(devices)
            for j in range(count)
        ]
        return lax.ppermute(value, ("dp", "space"), pairs)

    mine = exchange(mine, near, devices, along)
    mine = exchange(mine, 1, count, across)
    shards = [mine] + [lax.ppermute(mine, "dp", group[i]) for i in range(1, near)]
    updated = finish(
        near, pixels, shards, weight_mean, bias_mean, book_mean, log_mean, usage_mean
    )
    whole = place_wide(count, *spans(share)[1], arrived[2], whole)
    codes = whole.shape[2]
    return (
        codes_small.reshape(codes_small.shape[0], -1, codes),
        codes_mid.reshape(codes_mid.shape[0], -1, codes),
        whole,
        grad_small,
        grad_mid,
        grad,
        *updated,
    )


def solution(mesh):
    strips = P("dp", "space", None)
    placed = (strips,) * 9 + (P("dp", None),) * 3 + (P(),) * 10
    return jax.shard_map(
        per_device,
        mesh=mesh,
        in_specs=placed,
        out_specs=(P(("dp", "space"), None, None),) * 3 + (strips,) * 3 + (P(),) * 5,
        check_vma=False,
    )
```

```python
import functools

import jax
import jax.numpy as jnp
from jax import lax
from jax.experimental import pallas as pl
from jax.experimental.pallas import tpu as pltpu
from jax.sharding import PartitionSpec as P

F32 = jnp.float32
BF16 = jnp.bfloat16
VMEM_LIMIT = 24 * 1024 * 1024
ACC_ROWS = 64 + 64 + 8 + 8 + 64 + 8
LANES = 1024


def partner(index, step, count):
    if count & (count - 1) == 0:
        return index ^ step
    return lax.rem(index + step, count)


def route(step, count):
    if count & (count - 1) == 0:
        return [(i, i ^ step) for i in range(count)]
    return [(i, (i + step) % count) for i in range(count)]


def source(index, step, count):
    if count & (count - 1) == 0:
        return index ^ step
    return lax.rem(index + (count - step), count)


def in_hbm(arrays):
    return [pltpu.with_memory_space_constraint(a, pltpu.HBM) for a in arrays]


def halves(x):
    high = x.astype(BF16)
    return high, (x - high.astype(F32)).astype(BF16)


def dot(left, right, left_dim=1, right_dim=0):
    return lax.dot_general(
        left, right, (((left_dim,), (right_dim,)), ((), ())), preferred_element_type=F32
    )


def set_scalars(log_ref, heat_ref, out_ref):
    precision = jnp.exp(jnp.full((8, 128), log_ref[0], F32))
    heat = jnp.full((8, 128), heat_ref[0], F32)
    row = lax.broadcasted_iota(jnp.int32, (8, 128), 0)
    factor = -0.5 * precision / heat
    out_ref[...] = jnp.where(row == 0, precision, jnp.where(row == 1, 1.0 / heat, factor))


def scalars(ref):
    return ref[0:1, 0:1], ref[1:2, 0:1], ref[2:3, 0:1]


def prepare(refs, book_scr, books_scr, weight_scr):
    weight_ref, bias_ref, book_ref, scalar_ref = refs
    dim, codes = book_ref.shape
    precision, _, _ = scalars(scalar_ref)
    book = book_ref[...]
    high, low = halves(book)
    norm = -0.5 * precision * jnp.sum(book * book, axis=0, keepdims=True)
    n0 = norm.astype(BF16).astype(F32)
    n1 = (norm - n0).astype(BF16).astype(F32)
    n2 = norm - n0 - n1
    row = lax.broadcasted_iota(jnp.int32, (16, codes), 0)
    extra = jnp.where(
        row < 3,
        1.0,
        jnp.where(row == 3, n0, jnp.where(row == 4, n1, jnp.where(row == 5, n2, 0.0))),
    ).astype(BF16)
    book_scr[0:dim] = high
    book_scr[dim : 2 * dim] = low
    book_scr[2 * dim : 3 * dim] = high
    book_scr[3 * dim : 3 * dim + 16] = extra
    books_scr[0:dim] = high
    books_scr[dim : 2 * dim] = low
    books_scr[2 * dim : 2 * dim + 16] = jnp.ones((16, codes), BF16)
    high, low = halves(weight_ref[...])
    weight_scr[0:dim] = high
    weight_scr[dim : 2 * dim] = low
    weight_scr[2 * dim : 3 * dim] = high


def latents(refs, scr, feat):
    weight_ref, bias_ref, book_ref, scalar_ref = refs
    weight_scr = scr[2]
    dim = book_ref.shape[0]
    precision, _, _ = scalars(scalar_ref)
    eye = lax.broadcasted_iota(jnp.int32, (dim, dim), 0) == lax.broadcasted_iota(
        jnp.int32, (dim, dim), 1
    )
    bias = jnp.sum(jnp.where(eye, bias_ref[...], 0.0), axis=1, keepdims=True)
    fh, fl = halves(feat)
    both = weight_scr[0 : 2 * dim]
    z2 = dot(both, fh, 1, 1) + dot(both, fl, 1, 1)
    z = z2[0:dim] + z2[dim : 2 * dim] + bias
    square = -0.5 * precision * jnp.sum(z * z, axis=0, keepdims=True)
    return fh, fl, z, square


def logit_rows(zh, zl, square):
    rows = zh.shape[1]
    s0 = square.astype(BF16).astype(F32)
    s1 = (square - s0).astype(BF16).astype(F32)
    s2 = square - s0 - s1
    row = lax.broadcasted_iota(jnp.int32, (16, rows), 0)
    extra = jnp.where(
        row == 0,
        s0,
        jnp.where(row == 1, s1, jnp.where(row == 2, s2, jnp.where(row < 6, 1.0, 0.0))),
    ).astype(BF16)
    return jnp.concatenate([zh, zh, zl, extra], axis=0)


def cot_rows(ch, cl):
    return jnp.concatenate([ch, ch, cl, jnp.zeros((16, ch.shape[1]), BF16)], axis=0)


def over_rows(rows, body, carry):
    step = 32 if rows % 32 == 0 else 16

    def at(i, carry):
        return body(pl.ds(pl.multiple_of(i * step, step), step), carry)

    return lax.fori_loop(0, rows // step, at, carry, unroll=True)


def folded(x):
    return jnp.sum(x.reshape(x.shape[0] // 8, 8, x.shape[1]), axis=0)


def probabilities(logits):
    top = jnp.max(logits, axis=1, keepdims=True)
    e = jnp.exp(logits - top)
    return e * (1.0 / jnp.sum(e, axis=1, keepdims=True))


def forward(refs, scr, feat, noise_ref, code_ref, usage_ref):
    weight_ref, bias_ref, book_ref, scalar_ref = refs
    book_scr, l_scr = scr[0], scr[3]
    rows = feat.shape[0]
    precision, cold, _ = scalars(scalar_ref)
    _, _, z, square = latents(refs, scr, feat)
    zh, zl = halves(precision * z)
    l_scr[0:rows] = dot(logit_rows(zh, zl, square), book_scr[...], 0, 0)

    def body(at, usage):
        logits = l_scr[at]
        code_ref[at] = probabilities((logits + noise_ref[at]) * cold)
        return usage + folded(probabilities(logits))

    usage_ref[...] = over_rows(rows, body, usage_ref[...])


def gradients(refs, scr, fh, fl, z, square, zh, zl, ch, cl, acc_ref):
    books_scr, weight_scr = scr[1:3]
    wh_scr, wl_scr, gh_scr, gl_scr = scr[5:9]
    rows, feats = fh.shape
    dim, codes = refs[2].shape
    wh, wl = wh_scr[0:rows], wl_scr[0:rows]
    gh, gl = gh_scr[0:rows], gl_scr[0:rows]
    p = dot(jnp.concatenate([ch, cl], axis=0), wh)
    acc_ref[0:64] += p[0:dim] + p[dim : 2 * dim] + dot(ch, wl)
    left = jnp.concatenate([zh, zl, jnp.ones((16, rows), BF16)], axis=0)
    p = dot(left, gh) + dot(left, gl)
    acc_ref[64:128] += p[0:dim] + p[dim : 2 * dim]
    acc_ref[128:136] += p[2 * dim : 2 * dim + 8]
    p = dot(books_scr[...], gh, 1, 1) + dot(books_scr[...], gl, 1, 1)
    row_d = p[2 * dim : 2 * dim + 1]
    gz = 2.0 * (row_d * z - (p[0:dim] + p[dim : 2 * dim]))
    zh, zl = halves(gz)
    p = dot(jnp.concatenate([zh, zl], axis=0), fh)
    acc_ref[144:208, 0:feats] += p[0:dim] + p[dim : 2 * dim] + dot(zh, fl)
    acc_ref[144:208, feats : feats + 128] += jnp.broadcast_to(
        jnp.sum(gz, axis=1, keepdims=True), (dim, 128)
    )
    total = jnp.sum(square * row_d, axis=1, keepdims=True)
    acc_ref[208:216] += jnp.broadcast_to(total, (8, codes))
    return dot(jnp.concatenate([zh, zh, zl], axis=0), weight_scr[...], 0, 0)


def backward(refs, scr, feat, cot, code_ref, acc_ref):
    weight_ref, bias_ref, book_ref, scalar_ref = refs
    book_scr, _, _, _, g_scr, wh_scr, wl_scr, gh_scr, gl_scr = scr
    rows = feat.shape[0]
    precision, _, factor = scalars(scalar_ref)
    fh, fl, z, square = latents(refs, scr, feat)
    zh, zl = halves(precision * z)
    ch, cl = halves(factor * cot)
    g_scr[0:rows] = dot(cot_rows(ch, cl), book_scr[...], 0, 0)

    def body(at, carry):
        w = code_ref[at]
        gw = g_scr[at]
        gd = w * (gw - jnp.sum(w * gw, axis=1, keepdims=True))
        wh_scr[at], wl_scr[at] = halves(w)
        gh_scr[at], gl_scr[at] = halves(gd)
        return carry

    over_rows(rows, body, 0)
    return gradients(refs, scr, fh, fl, z, square, zh, zl, ch, cl, acc_ref)


def both_ways(refs, scr, feat, cot, noise_ref, code_ref, acc_ref):
    weight_ref, bias_ref, book_ref, scalar_ref = refs
    book_scr, _, _, l_scr, g_scr, wh_scr, wl_scr, gh_scr, gl_scr = scr
    rows = feat.shape[0]
    precision, cold, factor = scalars(scalar_ref)
    fh, fl, z, square = latents(refs, scr, feat)
    zh, zl = halves(precision * z)
    ch, cl = halves(factor * cot)
    left = jnp.concatenate([logit_rows(zh, zl, square), cot_rows(ch, cl)], axis=1)
    p = dot(left, book_scr[...], 0, 0)
    l_scr[0:rows] = p[0:rows]
    g_scr[0:rows] = p[rows : 2 * rows]

    def body(at, usage):
        logits = l_scr[at]
        s = (logits + noise_ref[at]) * cold
        e = jnp.exp(s - jnp.max(s, axis=1, keepdims=True))
        gw = g_scr[at]
        scale = 1.0 / jnp.sum(e, axis=1, keepdims=True)
        inner = jnp.sum(e * gw, axis=1, keepdims=True) * scale
        w = e * scale
        code_ref[at] = w
        gd = w * (gw - inner)
        wh_scr[at], wl_scr[at] = halves(w)
        gh_scr[at], gl_scr[at] = halves(gd)
        return usage + folded(probabilities(logits))

    acc_ref[136:144] = over_rows(rows, body, acc_ref[136:144])
    return gradients(refs, scr, fh, fl, z, square, zh, zl, ch, cl, acc_ref)


def tile_scratch(rows, dim, codes, feats):
    return [
        pltpu.VMEM((3 * dim + 16, codes), BF16),
        pltpu.VMEM((2 * dim + 16, codes), BF16),
        pltpu.VMEM((3 * dim, feats), BF16),
        pltpu.VMEM((rows, codes), F32),
        pltpu.VMEM((rows, codes), F32),
        pltpu.VMEM((rows, codes), BF16),
        pltpu.VMEM((rows, codes), BF16),
        pltpu.VMEM((rows, codes), BF16),
        pltpu.VMEM((rows, codes), BF16),
    ]


def settings():
    return pltpu.CompilerParams(vmem_limit_bytes=VMEM_LIMIT)


def cost(rows, feats, dim, codes, tenths):
    return pl.CostEstimate(
        flops=rows * 24 * tenths * (5 * dim * codes + 3 * dim * feats) // 10,
        bytes_accessed=4 * rows * (2 * feats + 2 * codes + dim),
        transcendentals=2 * rows * codes,
    )


SMEM = pl.BlockSpec(memory_space=pltpu.SMEM)
VMEM = pl.BlockSpec(memory_space=pltpu.VMEM)
HBM = pl.BlockSpec(memory_space=pltpu.HBM)


def fixed(shape):
    return pl.BlockSpec(shape, lambda *_: (0,) * len(shape))


def part_rows(peer, slots, shape):
    return pl.BlockSpec(shape, lambda i, _: (jnp.clip(i - peer * slots, 0, slots - 1), 0))


def places_of(table_ref, wide, shapes, groups, count):
    places = []
    base = 0
    entry = wide + 1
    for _ in range(count):
        for size in range(2):
            strip = shapes[size][1]
            for _ in range(groups[size]):
                places.append((size, table_ref[0, entry], base, strip))
                base += strip
                entry += 1
    return places, base


def small_forward_kernel(count, groups, *refs):
    sources = refs[0:10]
    log_ref, heat_ref = refs[10:12]
    sends = refs[12 : 12 + count]
    table_ref, usage_ref, scalar_ref = refs[12 + count : 15 + count]
    held = refs[15 + count : 25 + count]
    sems, feat_scr, noise_scr, code_scr = refs[25 + count : 29 + count]
    scr = refs[29 + count :]
    copies = [
        pltpu.make_async_copy(there, here, sems.at[i])
        for i, (there, here) in enumerate(zip(sources, held))
    ]
    for copy in copies:
        copy.start()
    orders, feats, noises, params = held[0:3], held[3:5], held[5:7], (*held[7:10], scalar_ref)
    me = lax.axis_index("space")
    set_scalars(log_ref, heat_ref, scalar_ref)
    for copy in copies[7:10]:
        copy.wait()
    prepare(params, *scr[0:3])
    for copy in copies[0:5]:
        copy.wait()
    wide = orders[2].shape[1]
    share = wide // count
    entry = wide + 1
    table_ref[0, wide] = me
    for step in range(count):
        there = partner(me, step, count)
        for j in range(share):
            table_ref[0, step * share + j] = orders[2][0, there * share + j]
        for size in range(2):
            for j in range(groups[size]):
                table_ref[0, entry] = orders[size][0, there * groups[size] + j]
                entry += 1
    places, base = places_of(table_ref, wide, [f.shape for f in feats], groups, count)
    for size, image, at, strip in places:
        feat_scr[at : at + strip] = feats[size][image]
    for copy in copies[5:7]:
        copy.wait()
    for size, image, at, strip in places:
        noise_scr[at : at + strip] = noises[size][image]
    usage_ref[...] = jnp.zeros(usage_ref.shape, F32)
    forward(params, scr, feat_scr[...], noise_scr, code_scr, usage_ref)
    part = base // count
    for step in range(count):
        sends[step][...] = code_scr[step * part : (step + 1) * part]


def small_forward(count, orders, feats, noises, params):
    dim, codes = params[2].shape
    width = feats[0].shape[2]
    groups = tuple(f.shape[0] // count for f in feats)
    part = sum(g * f.shape[1] for g, f in zip(groups, feats))
    rows = part * count
    arrays = [*orders, *feats, *noises, *params[0:3]]
    return pl.pallas_call(
        functools.partial(small_forward_kernel, count, groups),
        out_shape=[jax.ShapeDtypeStruct((part, codes), F32)] * count
        + [
            jax.ShapeDtypeStruct((1, sum(o.shape[1] for o in orders) + 1), jnp.int32),
            pltpu.HBM((8, codes), F32),
            pltpu.HBM((8, 128), F32),
        ],
        in_specs=[HBM] * 10 + [SMEM] * 2,
        out_specs=[VMEM] * count + [SMEM, VMEM, VMEM],
        scratch_shapes=[
            (pltpu.SMEM if i < 3 else pltpu.VMEM)(a.shape, a.dtype)
            for i, a in enumerate(arrays)
        ]
        + [
            pltpu.SemaphoreType.DMA((10,)),
            pltpu.VMEM((rows, width), F32),
            pltpu.VMEM((rows, codes), F32),
            pltpu.VMEM((rows, codes), F32),
        ]
        + tile_scratch(rows, dim, codes, width),
        compiler_params=settings(),
        cost_estimate=cost(rows, width, dim, codes, 4),
        name="small_forward",
    )(*in_hbm(arrays), *params[3:5])


def small_backward_kernel(count, devices, wide, groups, *refs):
    table_ref = refs[0]
    feats, cots = refs[1:3], refs[3:5]
    parts = refs[5 : 5 + count]
    params = refs[5 + count : 9 + count]
    acc_in, usage_ref = refs[9 + count : 11 + count]
    grads = refs[11 + count : 13 + count]
    shards = refs[13 + count : 13 + count + devices]
    rest = refs[13 + count + devices :]
    acc_ref, sum_scr, feat_scr, cot_scr, code_scr = rest[0:5]
    scr = rest[5:]
    places, base = places_of(table_ref, wide, [f.shape for f in feats], groups, count)
    for size, image, at, strip in places:
        feat_scr[at : at + strip] = feats[size][image]
        cot_scr[at : at + strip] = cots[size][image]
    part = base // count
    for step in range(count):
        code_scr[step * part : (step + 1) * part] = parts[step][...]
    prepare(params, *scr[0:3])
    acc_ref[...] = acc_in[...]
    feat_scr[...] = backward(params, scr, feat_scr[...], cot_scr[...].T, code_scr, acc_ref)
    lay_out(params, acc_ref, usage_ref, sum_scr, shards)
    for size, image, at, strip in places:
        grads[size][image] = feat_scr[at : at + strip]


def small_backward(count, devices, wide, table, feats, cots, parts, params, acc, usage):
    dim, codes = params[2].shape
    width = feats[0].shape[2]
    groups = tuple(f.shape[0] // count for f in feats)
    rows = parts[0].shape[0] * count
    return pl.pallas_call(
        functools.partial(small_backward_kernel, count, devices, wide, groups),
        out_shape=[pltpu.HBM(f.shape, F32) for f in feats]
        + [jax.ShapeDtypeStruct((64 // devices, LANES), F32)] * devices,
        in_specs=[SMEM] + [VMEM] * (10 + count),
        out_specs=[VMEM] * (2 + devices),
        scratch_shapes=[
            pltpu.VMEM(acc.shape, F32),
            pltpu.VMEM((64, LANES), F32),
            pltpu.VMEM((rows, width), F32),
            pltpu.VMEM((rows, dim), F32),
            pltpu.VMEM((rows, codes), F32),
        ]
        + tile_scratch(rows, dim, codes, width),
        compiler_params=settings(),
        cost_estimate=cost(rows, width, dim, codes, 6),
        name="small_backward",
    )(
        table,
        *in_hbm([*feats, *cots]),
        *parts,
        *in_hbm([*params, acc, usage]),
    )


def wide_forward_kernel(count, slots, *refs):
    feat_ref, noise_ref = refs[1:3]
    params = refs[3:7]
    usage_in = refs[7]
    sends = refs[8 : 7 + count]
    usage_ref = refs[7 + count]
    code_scr = refs[8 + count]
    scr = refs[9 + count :]
    step = pl.program_id(0)

    @pl.when(step == 0)
    def _():
        prepare(params, *scr[0:3])
        usage_ref[...] = usage_in[...]

    forward(params, scr, feat_ref[...], noise_ref, code_scr, usage_ref)
    for i in range(count - 1):

        @pl.when(lax.div(step, slots) == i)
        def _(i=i):
            sends[i][...] = code_scr[...]


def peer_image(count, share, first, slots):
    def image(i, table_ref):
        peer = lax.div(i, slots) + 1
        return (table_ref[0, peer * share + first + lax.rem(i, slots)], 0, 0)

    return image


def wide_forward(count, first, slots, table, feat, noise, params, usage):
    dim, codes = params[2].shape
    images, strip, width = feat.shape
    image = peer_image(count, images // count, first, slots)
    return pl.pallas_call(
        functools.partial(wide_forward_kernel, count, slots),
        grid_spec=pltpu.PrefetchScalarGridSpec(
            num_scalar_prefetch=1,
            grid=((count - 1) * slots,),
            in_specs=[
                pl.BlockSpec((None, strip, width), image),
                pl.BlockSpec((None, strip, codes), image),
                fixed(params[0].shape),
                fixed(params[1].shape),
                fixed(params[2].shape),
                fixed(params[3].shape),
                fixed(usage.shape),
            ],
            out_specs=[part_rows(i, slots, (strip, codes)) for i in range(count - 1)]
            + [fixed(usage.shape)],
            scratch_shapes=[pltpu.VMEM((strip, codes), F32)]
            + tile_scratch(strip, dim, codes, width),
        ),
        out_shape=[jax.ShapeDtypeStruct((strip * slots, codes), F32)] * (count - 1)
        + [pltpu.HBM(usage.shape, F32)],
        input_output_aliases={7: count - 1},
        compiler_params=settings(),
        cost_estimate=cost((count - 1) * slots * strip, width, dim, codes, 4),
        name="wide_forward",
    )(table, *in_hbm([feat, noise, *params, usage]))


def wide_both_kernel(count, slots, *refs):
    feat_ref, noise_ref, cot_ref = refs[1:4]
    params = refs[4:8]
    sends = refs[8 : 7 + count]
    grad_ref, acc_ref, code_scr = refs[7 + count : 10 + count]
    scr = refs[10 + count :]
    step = pl.program_id(0)

    @pl.when(step == 0)
    def _():
        prepare(params, *scr[0:3])
        acc_ref[...] = jnp.zeros(acc_ref.shape, F32)

    grad_ref[...] = both_ways(
        params, scr, feat_ref[...], cot_ref[...], noise_ref, code_scr, acc_ref
    )
    for i in range(count - 1):

        @pl.when(lax.div(step, slots) == i)
        def _(i=i):
            sends[i][...] = code_scr[...]


def wide_both(count, first, slots, table, feat, noise, cot, params):
    dim, codes = params[2].shape
    images, strip, width = feat.shape
    image = peer_image(count, images // count, first, slots)
    acc_shape = (ACC_ROWS, codes)
    return pl.pallas_call(
        functools.partial(wide_both_kernel, count, slots),
        grid_spec=pltpu.PrefetchScalarGridSpec(
            num_scalar_prefetch=1,
            grid=((count - 1) * slots,),
            in_specs=[
                pl.BlockSpec((None, strip, width), image),
                pl.BlockSpec((None, strip, codes), image),
                pl.BlockSpec((None, dim, strip), image),
            ]
            + [fixed(p.shape) for p in params],
            out_specs=[part_rows(i, slots, (strip, codes)) for i in range(count - 1)]
            + [pl.BlockSpec((None, strip, width), image), fixed(acc_shape)],
            scratch_shapes=[pltpu.VMEM((strip, codes), F32)]
            + tile_scratch(strip, dim, codes, width),
        ),
        out_shape=[jax.ShapeDtypeStruct((strip * slots, codes), F32)] * (count - 1)
        + [pltpu.HBM(feat.shape, F32), pltpu.HBM(acc_shape, F32)],
        compiler_params=settings(),
        cost_estimate=cost((count - 1) * slots * strip, width, dim, codes, 10),
        name="wide_both",
    )(table, *in_hbm([feat, noise, cot, *params]))


def wide_backward_kernel(count, slots, *refs):
    feat_ref, cot_ref = refs[1:3]
    parts = refs[3 : 2 + count]
    params = refs[2 + count : 6 + count]
    acc_in = refs[6 + count]
    grad_ref, acc_ref, code_scr = refs[8 + count : 11 + count]
    scr = refs[11 + count :]
    step = pl.program_id(0)

    @pl.when(step == 0)
    def _():
        prepare(params, *scr[0:3])
        acc_ref[...] = acc_in[...]

    for i in range(count - 1):

        @pl.when(lax.div(step, slots) == i)
        def _(i=i):
            code_scr[...] = parts[i][...]

    grad_ref[...] = backward(params, scr, feat_ref[...], cot_ref[...], code_scr, acc_ref)


def wide_backward(count, first, slots, table, feat, cot, parts, params, acc, grad):
    dim, codes = params[2].shape
    images, strip, width = feat.shape
    image = peer_image(count, images // count, first, slots)
    return pl.pallas_call(
        functools.partial(wide_backward_kernel, count, slots),
        grid_spec=pltpu.PrefetchScalarGridSpec(
            num_scalar_prefetch=1,
            grid=((count - 1) * slots,),
            in_specs=[
                pl.BlockSpec((None, strip, width), image),
                pl.BlockSpec((None, dim, strip), image),
            ]
            + [part_rows(i, slots, (strip, codes)) for i in range(count - 1)]
            + [fixed(p.shape) for p in params]
            + [fixed(acc.shape), HBM],
            out_specs=[pl.BlockSpec((None, strip, width), image), fixed(acc.shape)],
            scratch_shapes=[pltpu.VMEM((strip, codes), F32)]
            + tile_scratch(strip, dim, codes, width),
        ),
        out_shape=[pltpu.HBM(feat.shape, F32), pltpu.HBM(acc.shape, F32)],
        input_output_aliases={6 + count: 1, 7 + count: 0},
        compiler_params=settings(),
        cost_estimate=cost((count - 1) * slots * strip, width, dim, codes, 6),
        name="wide_backward",
    )(table, *in_hbm([feat, cot]), *parts, *in_hbm([*params, acc, grad]))


def shard_at(index, parts):
    height = 64 // parts
    return pl.ds(pl.multiple_of(index * height, height), height)


def lay_out(params, acc_ref, usage_ref, sum_scr, shards):
    weight_ref, bias_ref, book_ref, scalar_ref = params
    codes = book_ref.shape[1]
    width = weight_ref.shape[1]
    devices = len(shards)
    me = lax.rem(lax.axis_index("dp"), devices)
    precision, _, factor = scalars(scalar_ref)
    book = book_ref[...]
    column = acc_ref[128:129]
    moment = acc_ref[64:128] * (1.0 / precision)
    book_sum = acc_ref[0:64] * (1.0 / factor) + 2.0 * (column * book - moment)
    slope = jnp.sum(
        jnp.sum(book * book, axis=0, keepdims=True) * column, axis=1, keepdims=True
    ) - 2.0 * jnp.sum(jnp.sum(book * moment, axis=0, keepdims=True), axis=1, keepdims=True)
    slope = slope + acc_ref[208:209, 0:1] / (-0.5 * precision)
    usage = jnp.sum(acc_ref[136:144] + usage_ref[...], axis=0, keepdims=True)
    sum_scr[:, 0:codes] = book_sum
    sum_scr[:, codes : codes + width + 128] = acc_ref[144:208, 0 : width + 128]
    rows = codes // 128
    for i in range(rows):
        sum_scr[i : i + 1, LANES - 128 : LANES] = usage[:, i * 128 : (i + 1) * 128]
    sum_scr[rows:64, LANES - 128 : LANES] = jnp.broadcast_to(slope, (64 - rows, 128))
    for i in range(devices):
        shards[i][...] = sum_scr[shard_at(partner(me, i, devices), devices)]


def own_kernel(*refs):
    feat_ref, noise_ref, cot_ref = refs[1:4]
    params = refs[4:8]
    acc_in = refs[8]
    code_ref, grad_ref, acc_ref = refs[10:13]
    scr = refs[13:]

    @pl.when(pl.program_id(0) == 0)
    def _():
        prepare(params, *scr[0:3])
        acc_ref[...] = acc_in[...]

    grad_ref[...] = both_ways(
        params, scr, feat_ref[...], cot_ref[...], noise_ref, code_ref, acc_ref
    )


def run_own(count, table, feat, noise, cot, params, acc, grad):
    dim, codes = params[2].shape
    images, strip, width = feat.shape
    share = images // count

    def image(i, table_ref):
        return (table_ref[0, i], 0, 0)

    return pl.pallas_call(
        own_kernel,
        grid_spec=pltpu.PrefetchScalarGridSpec(
            num_scalar_prefetch=1,
            grid=(share,),
            in_specs=[
                pl.BlockSpec((None, strip, width), image),
                pl.BlockSpec((None, strip, codes), image),
                pl.BlockSpec((None, dim, strip), image),
                fixed(params[0].shape),
                fixed(params[1].shape),
                fixed(params[2].shape),
                fixed(params[3].shape),
                fixed(acc.shape),
                HBM,
            ],
            out_specs=[
                pl.BlockSpec(
                    (None, strip, codes),
                    lambda i, table_ref: (i, table_ref[0, count * share], 0),
                ),
                pl.BlockSpec((None, strip, width), image),
                fixed(acc.shape),
            ],
            scratch_shapes=tile_scratch(strip, dim, codes, width),
        ),
        out_shape=[
            pltpu.HBM((share, strip * count, codes), F32),
            pltpu.HBM(feat.shape, F32),
            pltpu.HBM(acc.shape, F32),
        ],
        input_output_aliases={8: 2, 9: 1},
        compiler_params=settings(),
        cost_estimate=cost(share * strip, width, dim, codes, 10),
        name="own_images",
    )(table, *in_hbm([feat, noise, cot, *params, acc, grad]))


def place_kernel(count, first, slots, steps, *refs):
    parts = refs[0 : len(steps)]
    out_ref, sem = refs[len(steps) + 1 : len(steps) + 3]
    strip = parts[0].shape[0] // slots
    me = lax.axis_index("space")
    copies = []
    for part, step in zip(parts, steps):
        row = pl.multiple_of(source(me, step, count) * strip, strip)
        for j in range(slots):
            copies.append(
                pltpu.make_async_copy(
                    part.at[pl.ds(j * strip, strip)],
                    out_ref.at[first + j, pl.ds(row, strip)],
                    sem.at[len(copies)],
                )
            )
    for copy in copies:
        copy.start()
    for copy in copies:
        copy.wait()


def place_wide(count, first, slots, steps, parts, whole):
    steps = list(steps)
    return pl.pallas_call(
        functools.partial(place_kernel, count, first, slots, steps),
        out_shape=pltpu.HBM(whole.shape, F32),
        in_specs=[VMEM] * len(steps) + [HBM],
        out_specs=HBM,
        scratch_shapes=[pltpu.SemaphoreType.DMA((len(steps) * slots,))],
        input_output_aliases={len(steps): 0},
        compiler_params=settings(),
        cost_estimate=pl.CostEstimate(
            flops=0, bytes_accessed=2 * sum(p.size * 4 for p in parts), transcendentals=0
        ),
        name="place_wide",
    )(*[pltpu.with_memory_space_constraint(p, pltpu.VMEM) for p in parts], *in_hbm([whole]))


def join_kernel(count, *refs):
    parts = refs[0:count]
    outs = refs[count:]
    me = lax.axis_index("space")
    for step in range(count):
        here = source(me, step, count)
        base = 0
        for out in outs:
            for j in range(out.shape[0]):
                strip = out.shape[2]
                out[j, here] = parts[step][base : base + strip]
                base += strip


def join_small(count, parts, shapes):
    codes = parts[0].shape[1]
    return pl.pallas_call(
        functools.partial(join_kernel, count),
        out_shape=[
            jax.ShapeDtypeStruct((images // count, count, strip, codes), F32)
            for images, strip, _ in shapes
        ],
        compiler_params=settings(),
        name="join_small",
    )(*parts)


def tree(values):
    while len(values) > 1:
        values = [
            values[i] + values[i + 1] if i + 1 < len(values) else values[i]
            for i in range(0, len(values), 2)
        ]
    return values[0]


def sum_kernel(*refs):
    refs[-1][...] = tree([ref[...] for ref in refs[:-1]])


def add_all(parts):
    return pl.pallas_call(
        sum_kernel,
        out_shape=jax.ShapeDtypeStruct(parts[0].shape, F32),
        name="add_parts",
    )(*parts)


def final_kernel(devices, pixels, *refs):
    shards = refs[0:devices]
    weight_ref, bias_ref, book_ref, log_ref, usage_ref = refs[devices : devices + 5]
    weight_out, bias_out, book_out, log_out, usage_out = refs[devices + 5 : devices + 10]
    sum_scr = refs[devices + 10]
    me = lax.rem(lax.axis_index("dp"), devices)
    for i in range(devices):
        sum_scr[shard_at(source(me, i, devices), devices)] = shards[i][...]
    dim, codes = book_ref.shape
    width = weight_ref.shape[1]
    scale = 0.5 * lax.rsqrt(jnp.full((8, 128), pixels, F32))[0:1, 0:1]
    book_out[...] = 0.5 * book_ref[...] + scale * sum_scr[:, 0:codes]
    weight_out[...] = 0.5 * weight_ref[...] + scale * sum_scr[:, codes : codes + width]
    eye = lax.broadcasted_iota(jnp.int32, (dim, dim), 0) == lax.broadcasted_iota(
        jnp.int32, (dim, dim), 1
    )
    bias = sum_scr[:, codes + width : codes + width + dim]
    bias = jnp.sum(jnp.where(eye, bias, 0.0), axis=0, keepdims=True)
    bias_out[...] = 0.5 * bias_ref[...] + scale * bias
    rows = codes // 128
    usage = jnp.concatenate(
        [sum_scr[i : i + 1, LANES - 128 : LANES] for i in range(rows)], axis=1
    )
    usage_out[...] = 0.5 * usage_ref[...] + 0.5 * (codes / pixels) * usage
    log_out[...] = 0.5 * log_ref[...] + scale * sum_scr[rows : rows + 1, LANES - 128 : LANES - 127]


def finish(devices, pixels, shards, weight, bias, book, log, usage):
    outs = (weight.T, bias.reshape(1, -1), book.T, log.reshape(1, 1), usage.reshape(1, -1))
    outs = pl.pallas_call(
        functools.partial(final_kernel, devices, pixels),
        out_shape=[jax.ShapeDtypeStruct(out.shape, F32) for out in outs],
        scratch_shapes=[pltpu.VMEM((64, LANES), F32)],
        name="new_averages",
    )(*shards, *outs)
    return outs[0].T, outs[1].reshape(-1), outs[2].T, outs[3].reshape(-1), outs[4].reshape(-1)


def exchange(value, bit, size, pairs):
    while bit < size:
        ways = min(4, size // bit)
        value = tree([value] + [pairs(value, way * bit) for way in range(1, ways)])
        bit = bit * ways
    return value


def spans(share):
    return [(0, 1), (1, share - 1)]


def per_device(
    feat_small,
    feat_mid,
    feat_wide,
    noise_small,
    noise_mid,
    noise_wide,
    cot_small,
    cot_mid,
    cot_wide,
    order_small,
    order_mid,
    order_wide,
    weight,
    bias,
    book,
    log,
    heat,
    weight_mean,
    bias_mean,
    book_mean,
    log_mean,
    usage_mean,
):
    count = lax.axis_size("space")
    devices = lax.axis_size("dp")
    params = (weight.T, bias.reshape(1, -1), book.T, log, heat)
    feats = (feat_small, feat_mid, feat_wide)
    pixels = sum(f.shape[0] * f.shape[1] for f in feats) * count * devices
    share = feat_wide.shape[0] // count
    cot_wide = jnp.swapaxes(cot_wide, 1, 2)

    def send(values):
        return [lax.ppermute(v, "space", route(i + 1, count)) for i, v in enumerate(values)]

    def follow(codes, before):
        before[0], codes[-1] = lax.optimization_barrier((before[0], codes[-1]))
        return send(codes)

    orders = (order_small, order_mid, order_wide)
    *small, table, usage, scalar = small_forward(
        count, orders, feats[0:2], (noise_small, noise_mid), params
    )
    params = (*params[0:3], scalar)
    arrived = [send(small[1:])]
    near = min(4, devices)
    early, late = spans(share)
    *early_codes, usage = wide_forward(
        count, *early, table, feat_wide, noise_wide, params, usage
    )
    arrived.append(follow(list(early_codes), arrived[0]))
    codes_small, codes_mid = join_small(
        count, [small[0]] + arrived[0], [f.shape for f in feats[0:2]]
    )
    codes_small, codes_mid, scalar = lax.optimization_barrier(
        (codes_small, codes_mid, scalar)
    )
    params = (*params[0:3], scalar)
    *codes, grad, acc = wide_both(
        count, *late, table, feat_wide, noise_wide, cot_wide, params
    )
    arrived.append(follow(codes, arrived[1]))
    arrived[1], acc = lax.optimization_barrier((arrived[1], acc))
    whole, grad, acc = run_own(
        count, table, feat_wide, noise_wide, cot_wide, params, acc, grad
    )
    whole = place_wide(count, *early, range(1, count), arrived[1], whole)
    whole, acc = lax.optimization_barrier((whole, acc))
    grad, acc = wide_backward(
        count, *early, table, feat_wide, cot_wide, early_codes, params, acc, grad
    )
    grad_small, grad_mid, *shards = small_backward(
        count,
        near,
        feat_wide.shape[0],
        table,
        feats[0:2],
        (cot_small, cot_mid),
        small,
        params,
        acc,
        usage,
    )
    group = [
        [(i, i - i % near + partner(i % near, step, near)) for i in range(devices)]
        for step in range(near)
    ]
    parts = [lax.ppermute(shards[i], "dp", group[i]) for i in range(1, near)]
    mine = add_all([shards[0]] + parts)

    def along(value, offset):
        return lax.ppermute(value, "dp", [(i, i ^ offset) for i in range(devices)])

    def across(value, offset):
        turn = near if devices > near else 0
        pairs = [
            (i * count + j, (i ^ turn) * count + (j ^ offset))
            for i in range(devices)
            for j in range(count)
        ]
        return lax.ppermute(value, ("dp", "space"), pairs)

    mine = exchange(mine, near, devices, along)
    mine = exchange(mine, 1, count, across)
    shards = [mine] + [lax.ppermute(mine, "dp", group[i]) for i in range(1, near)]
    updated = finish(
        near, pixels, shards, weight_mean, bias_mean, book_mean, log_mean, usage_mean
    )
    for step in range(1, count):
        whole = place_wide(count, *late, [step], [arrived[2][step - 1]], whole)
    codes = whole.shape[2]
    return (
        codes_small.reshape(codes_small.shape[0], -1, codes),
        codes_mid.reshape(codes_mid.shape[0], -1, codes),
        whole,
        grad_small,
        grad_mid,
        grad,
        *updated,
    )


def solution(mesh):
    strips = P("dp", "space", None)
    placed = (strips,) * 9 + (P("dp", None),) * 3 + (P(),) * 10
    return jax.shard_map(
        per_device,
        mesh=mesh,
        in_specs=placed,
        out_specs=(P(("dp", "space"), None, None),) * 3 + (strips,) * 3 + (P(),) * 5,
        check_vma=False,
    )
```

```python
import functools

import jax
import jax.numpy as jnp
from jax import lax
from jax.experimental import pallas as pl
from jax.experimental.pallas import tpu as pltpu
from jax.sharding import PartitionSpec as P

F32 = jnp.float32
BF16 = jnp.bfloat16
VMEM_LIMIT = 24 * 1024 * 1024
ACC_ROWS = 64 + 64 + 8 + 8 + 64 + 8
LANES = 896


def partner(index, step, count):
    if count & (count - 1) == 0:
        return index ^ step
    return lax.rem(index + step, count)


def route(step, count):
    if count & (count - 1) == 0:
        return [(i, i ^ step) for i in range(count)]
    return [(i, (i + step) % count) for i in range(count)]


def source(index, step, count):
    if count & (count - 1) == 0:
        return index ^ step
    return lax.rem(index + (count - step), count)


def in_hbm(arrays):
    return [pltpu.with_memory_space_constraint(a, pltpu.HBM) for a in arrays]


def halves(x):
    high = x.astype(BF16)
    return high, (x - high.astype(F32)).astype(BF16)


def dot(left, right, left_dim=1, right_dim=0):
    return lax.dot_general(
        left, right, (((left_dim,), (right_dim,)), ((), ())), preferred_element_type=F32
    )


def set_scalars(log_ref, heat_ref, out_ref):
    precision = jnp.exp(jnp.full((8, 128), log_ref[0], F32))
    heat = jnp.full((8, 128), heat_ref[0], F32)
    row = lax.broadcasted_iota(jnp.int32, (8, 128), 0)
    factor = -0.5 * precision / heat
    out_ref[...] = jnp.where(row == 0, precision, jnp.where(row == 1, 1.0 / heat, factor))


def scalars(ref):
    return ref[0:1, 0:1], ref[1:2, 0:1], ref[2:3, 0:1]


def prepare(refs, book_scr, books_scr, weight_scr):
    weight_ref, bias_ref, book_ref, scalar_ref = refs
    dim, codes = book_ref.shape
    precision, _, _ = scalars(scalar_ref)
    book = book_ref[...]
    high, low = halves(book)
    norm = -0.5 * precision * jnp.sum(book * book, axis=0, keepdims=True)
    n0 = norm.astype(BF16).astype(F32)
    n1 = (norm - n0).astype(BF16).astype(F32)
    n2 = norm - n0 - n1
    row = lax.broadcasted_iota(jnp.int32, (16, codes), 0)
    extra = jnp.where(
        row < 3,
        1.0,
        jnp.where(row == 3, n0, jnp.where(row == 4, n1, jnp.where(row == 5, n2, 0.0))),
    ).astype(BF16)
    book_scr[0:dim] = high
    book_scr[dim : 2 * dim] = low
    book_scr[2 * dim : 3 * dim] = high
    book_scr[3 * dim : 3 * dim + 16] = extra
    books_scr[0:dim] = high
    books_scr[dim : 2 * dim] = low
    books_scr[2 * dim : 2 * dim + 16] = jnp.ones((16, codes), BF16)
    high, low = halves(weight_ref[...])
    weight_scr[0:dim] = high
    weight_scr[dim : 2 * dim] = low
    weight_scr[2 * dim : 3 * dim] = high


def latents(refs, scr, feat):
    weight_ref, bias_ref, book_ref, scalar_ref = refs
    weight_scr = scr[2]
    dim = book_ref.shape[0]
    precision, _, _ = scalars(scalar_ref)
    eye = lax.broadcasted_iota(jnp.int32, (dim, dim), 0) == lax.broadcasted_iota(
        jnp.int32, (dim, dim), 1
    )
    bias = jnp.sum(jnp.where(eye, bias_ref[...], 0.0), axis=1, keepdims=True)
    fh, fl = halves(feat)
    both = weight_scr[0 : 2 * dim]
    z2 = dot(both, fh, 1, 1) + dot(both, fl, 1, 1)
    z = z2[0:dim] + z2[dim : 2 * dim] + bias
    square = -0.5 * precision * jnp.sum(z * z, axis=0, keepdims=True)
    return fh, fl, z, square


def logit_rows(zh, zl, square):
    rows = zh.shape[1]
    s0 = square.astype(BF16).astype(F32)
    s1 = (square - s0).astype(BF16).astype(F32)
    s2 = square - s0 - s1
    row = lax.broadcasted_iota(jnp.int32, (16, rows), 0)
    extra = jnp.where(
        row == 0,
        s0,
        jnp.where(row == 1, s1, jnp.where(row == 2, s2, jnp.where(row < 6, 1.0, 0.0))),
    ).astype(BF16)
    return jnp.concatenate([zh, zh, zl, extra], axis=0)


def cot_rows(ch, cl):
    return jnp.concatenate([ch, ch, cl, jnp.zeros((16, ch.shape[1]), BF16)], axis=0)


def over_rows(rows, body, carry):
    step = next(s for s in (32, 16, 8) if rows % s == 0)

    def at(i, carry):
        return body(pl.ds(pl.multiple_of(i * step, step), step), carry)

    return lax.fori_loop(0, rows // step, at, carry, unroll=True)


def folded(x):
    return jnp.sum(x.reshape(x.shape[0] // 8, 8, x.shape[1]), axis=0)


def probabilities(logits):
    top = jnp.max(logits, axis=1, keepdims=True)
    e = jnp.exp(logits - top)
    return e * (1.0 / jnp.sum(e, axis=1, keepdims=True))


def forward(refs, scr, feat, noise_ref, code_refs, usage_ref):
    weight_ref, bias_ref, book_ref, scalar_ref = refs
    book_scr, l_scr = scr[0], scr[3]
    rows = feat.shape[0]
    precision, cold, _ = scalars(scalar_ref)
    _, _, z, square = latents(refs, scr, feat)
    zh, zl = halves(precision * z)
    l_scr[0:rows] = dot(logit_rows(zh, zl, square), book_scr[...], 0, 0)

    usage = usage_ref[...]
    part = rows // len(code_refs)
    for i, code_ref in enumerate(code_refs):
        logit_part = l_scr.at[pl.ds(i * part, part)]
        noise_part = noise_ref.at[pl.ds(i * part, part)]

        def body(at, usage, code_ref=code_ref, logit_part=logit_part, noise_part=noise_part):
            logits = logit_part[at]
            code_ref[at] = probabilities((logits + noise_part[at]) * cold)
            return usage + folded(probabilities(logits))

        usage = over_rows(part, body, usage)
    usage_ref[...] = usage


def gradients(refs, scr, fh, fl, z, square, zh, zl, ch, cl, acc_ref):
    books_scr, weight_scr = scr[1:3]
    wh_scr, wl_scr, gh_scr, gl_scr = scr[5:9]
    rows, feats = fh.shape
    dim, codes = refs[2].shape
    wh, wl = wh_scr[0:rows], wl_scr[0:rows]
    gh, gl = gh_scr[0:rows], gl_scr[0:rows]
    p = dot(jnp.concatenate([ch, cl], axis=0), wh)
    acc_ref[0:64] += p[0:dim] + p[dim : 2 * dim] + dot(ch, wl)
    left = jnp.concatenate([zh, zl, jnp.ones((16, rows), BF16)], axis=0)
    p = dot(left, gh) + dot(left, gl)
    acc_ref[64:128] += p[0:dim] + p[dim : 2 * dim]
    acc_ref[128:136] += p[2 * dim : 2 * dim + 8]
    p = dot(books_scr[...], gh, 1, 1) + dot(books_scr[...], gl, 1, 1)
    row_d = p[2 * dim : 2 * dim + 1]
    gz = 2.0 * (row_d * z - (p[0:dim] + p[dim : 2 * dim]))
    zh, zl = halves(gz)
    p = dot(jnp.concatenate([zh, zl], axis=0), fh)
    acc_ref[144:208, 0:feats] += p[0:dim] + p[dim : 2 * dim] + dot(zh, fl)
    acc_ref[144:208, feats : feats + 128] += jnp.broadcast_to(
        jnp.sum(gz, axis=1, keepdims=True), (dim, 128)
    )
    total = jnp.sum(square * row_d, axis=1, keepdims=True)
    acc_ref[208:216] += jnp.broadcast_to(total, (8, codes))
    return dot(jnp.concatenate([zh, zh, zl], axis=0), weight_scr[...], 0, 0)


def backward(refs, scr, feat, cot, code_ref, acc_ref):
    weight_ref, bias_ref, book_ref, scalar_ref = refs
    book_scr, _, _, _, g_scr, wh_scr, wl_scr, gh_scr, gl_scr = scr
    rows = feat.shape[0]
    precision, _, factor = scalars(scalar_ref)
    fh, fl, z, square = latents(refs, scr, feat)
    zh, zl = halves(precision * z)
    ch, cl = halves(factor * cot)
    g_scr[0:rows] = dot(cot_rows(ch, cl), book_scr[...], 0, 0)

    def body(at, carry):
        w = code_ref[at]
        gw = g_scr[at]
        gd = w * (gw - jnp.sum(w * gw, axis=1, keepdims=True))
        wh_scr[at], wl_scr[at] = halves(w)
        gh_scr[at], gl_scr[at] = halves(gd)
        return carry

    over_rows(rows, body, 0)
    return gradients(refs, scr, fh, fl, z, square, zh, zl, ch, cl, acc_ref)


def both_ways(refs, scr, feat, cot, noise_ref, code_ref, acc_ref):
    weight_ref, bias_ref, book_ref, scalar_ref = refs
    book_scr, _, _, l_scr, g_scr, wh_scr, wl_scr, gh_scr, gl_scr = scr
    rows = feat.shape[0]
    precision, cold, factor = scalars(scalar_ref)
    fh, fl, z, square = latents(refs, scr, feat)
    zh, zl = halves(precision * z)
    ch, cl = halves(factor * cot)
    left = jnp.concatenate([logit_rows(zh, zl, square), cot_rows(ch, cl)], axis=1)
    p = dot(left, book_scr[...], 0, 0)
    l_scr[0:rows] = p[0:rows]
    g_scr[0:rows] = p[rows : 2 * rows]

    def body(at, usage):
        logits = l_scr[at]
        s = (logits + noise_ref[at]) * cold
        e = jnp.exp(s - jnp.max(s, axis=1, keepdims=True))
        gw = g_scr[at]
        scale = 1.0 / jnp.sum(e, axis=1, keepdims=True)
        inner = jnp.sum(e * gw, axis=1, keepdims=True) * scale
        w = e * scale
        code_ref[at] = w
        gd = w * (gw - inner)
        wh_scr[at], wl_scr[at] = halves(w)
        gh_scr[at], gl_scr[at] = halves(gd)
        return usage + folded(probabilities(logits))

    acc_ref[136:144] = over_rows(rows, body, acc_ref[136:144])
    return gradients(refs, scr, fh, fl, z, square, zh, zl, ch, cl, acc_ref)


def tile_scratch(rows, dim, codes, feats):
    return [
        pltpu.VMEM((3 * dim + 16, codes), BF16),
        pltpu.VMEM((2 * dim + 16, codes), BF16),
        pltpu.VMEM((3 * dim, feats), BF16),
        pltpu.VMEM((rows, codes), F32),
        pltpu.VMEM((rows, codes), F32),
        pltpu.VMEM((rows, codes), BF16),
        pltpu.VMEM((rows, codes), BF16),
        pltpu.VMEM((rows, codes), BF16),
        pltpu.VMEM((rows, codes), BF16),
    ]


def settings():
    return pltpu.CompilerParams(vmem_limit_bytes=VMEM_LIMIT)


def cost(rows, feats, dim, codes, tenths):
    return pl.CostEstimate(
        flops=rows * 24 * tenths * (5 * dim * codes + 3 * dim * feats) // 10,
        bytes_accessed=4 * rows * (2 * feats + 2 * codes + dim),
        transcendentals=2 * rows * codes,
    )


SMEM = pl.BlockSpec(memory_space=pltpu.SMEM)
VMEM = pl.BlockSpec(memory_space=pltpu.VMEM)
HBM = pl.BlockSpec(memory_space=pltpu.HBM)


def fixed(shape):
    return pl.BlockSpec(shape, lambda *_: (0,) * len(shape))


def part_rows(peer, slots, shape):
    return pl.BlockSpec(shape, lambda i, _: (jnp.clip(i - peer * slots, 0, slots - 1), 0))


def places_of(table_ref, wide, shapes, groups, count):
    places = []
    base = 0
    entry = wide + 1
    for _ in range(count):
        for size in range(2):
            strip = shapes[size][1]
            for _ in range(groups[size]):
                places.append((size, table_ref[0, entry], base, strip))
                base += strip
                entry += 1
    return places, base


def small_forward_kernel(count, groups, *refs):
    sources = refs[0:10]
    log_ref, heat_ref = refs[10:12]
    sends = refs[12 : 12 + count]
    table_ref, usage_ref, scalar_ref = refs[12 + count : 15 + count]
    held = refs[15 + count : 25 + count]
    sems, feat_scr, noise_scr = refs[25 + count : 28 + count]
    scr = refs[28 + count :]
    copies = [
        pltpu.make_async_copy(there, here, sems.at[i])
        for i, (there, here) in enumerate(zip(sources, held))
    ]
    for copy in copies:
        copy.start()
    orders, feats, noises, params = held[0:3], held[3:5], held[5:7], (*held[7:10], scalar_ref)
    me = lax.axis_index("space")
    set_scalars(log_ref, heat_ref, scalar_ref)
    for copy in copies[7:10]:
        copy.wait()
    prepare(params, *scr[0:3])
    for copy in copies[0:5]:
        copy.wait()
    wide = orders[2].shape[1]
    share = wide // count
    entry = wide + 1
    table_ref[0, wide] = me
    for step in range(count):
        there = partner(me, step, count)
        for j in range(share):
            table_ref[0, step * share + j] = orders[2][0, there * share + j]
        for size in range(2):
            for j in range(groups[size]):
                table_ref[0, entry] = orders[size][0, there * groups[size] + j]
                entry += 1
    places, _ = places_of(table_ref, wide, [f.shape for f in feats], groups, count)
    for size, image, at, strip in places:
        feat_scr[at : at + strip] = feats[size][image]
    for copy in copies[5:7]:
        copy.wait()
    for size, image, at, strip in places:
        noise_scr[at : at + strip] = noises[size][image]
    usage_ref[...] = jnp.zeros(usage_ref.shape, F32)
    forward(params, scr, feat_scr[...], noise_scr, sends, usage_ref)


def small_forward(count, orders, feats, noises, params):
    dim, codes = params[2].shape
    width = feats[0].shape[2]
    groups = tuple(f.shape[0] // count for f in feats)
    part = sum(g * f.shape[1] for g, f in zip(groups, feats))
    rows = part * count
    arrays = [*orders, *feats, *noises, *params[0:3]]
    return pl.pallas_call(
        functools.partial(small_forward_kernel, count, groups),
        out_shape=[jax.ShapeDtypeStruct((part, codes), F32)] * count
        + [
            jax.ShapeDtypeStruct((1, sum(o.shape[1] for o in orders) + 1), jnp.int32),
            pltpu.HBM((8, codes), F32),
            pltpu.HBM((8, 128), F32),
        ],
        in_specs=[HBM] * 10 + [SMEM] * 2,
        out_specs=[VMEM] * count + [SMEM, VMEM, VMEM],
        scratch_shapes=[
            (pltpu.SMEM if i < 3 else pltpu.VMEM)(a.shape, a.dtype)
            for i, a in enumerate(arrays)
        ]
        + [
            pltpu.SemaphoreType.DMA((10,)),
            pltpu.VMEM((rows, width), F32),
            pltpu.VMEM((rows, codes), F32),
        ]
        + tile_scratch(rows, dim, codes, width),
        compiler_params=settings(),
        cost_estimate=cost(rows, width, dim, codes, 4),
        name="small_forward",
    )(*in_hbm(arrays), *params[3:5])


def small_backward_kernel(count, devices, wide, groups, *refs):
    table_ref = refs[0]
    feats, cots = refs[1:3], refs[3:5]
    parts = refs[5 : 5 + count]
    params = refs[5 + count : 9 + count]
    acc_in, usage_ref = refs[9 + count : 11 + count]
    grads = refs[11 + count : 13 + count]
    shards = refs[13 + count : 13 + count + devices]
    rest = refs[13 + count + devices :]
    acc_ref, sum_scr, feat_scr, cot_scr, code_scr = rest[0:5]
    scr = rest[5:]
    places, base = places_of(table_ref, wide, [f.shape for f in feats], groups, count)
    for size, image, at, strip in places:
        feat_scr[at : at + strip] = feats[size][image]
        cot_scr[at : at + strip] = cots[size][image]
    part = base // count
    for step in range(count):
        code_scr[step * part : (step + 1) * part] = parts[step][...]
    prepare(params, *scr[0:3])
    acc_ref[...] = acc_in[...]
    feat_scr[...] = backward(params, scr, feat_scr[...], cot_scr[...].T, code_scr, acc_ref)
    lay_out(params, acc_ref, usage_ref, sum_scr, shards)
    for size, image, at, strip in places:
        grads[size][image] = feat_scr[at : at + strip]


def small_backward(count, devices, wide, table, feats, cots, parts, params, acc, usage):
    dim, codes = params[2].shape
    width = feats[0].shape[2]
    groups = tuple(f.shape[0] // count for f in feats)
    rows = parts[0].shape[0] * count
    return pl.pallas_call(
        functools.partial(small_backward_kernel, count, devices, wide, groups),
        out_shape=[pltpu.HBM(f.shape, F32) for f in feats]
        + [jax.ShapeDtypeStruct((64 // devices, LANES), F32)] * devices,
        in_specs=[SMEM] + [VMEM] * (10 + count),
        out_specs=[VMEM] * (2 + devices),
        scratch_shapes=[
            pltpu.VMEM(acc.shape, F32),
            pltpu.VMEM((64, LANES), F32),
            pltpu.VMEM((rows, width), F32),
            pltpu.VMEM((rows, dim), F32),
            pltpu.VMEM((rows, codes), F32),
        ]
        + tile_scratch(rows, dim, codes, width),
        compiler_params=settings(),
        cost_estimate=cost(rows, width, dim, codes, 6),
        name="small_backward",
    )(
        table,
        *in_hbm([*feats, *cots]),
        *parts,
        *in_hbm([*params, acc, usage]),
    )


def wide_forward_kernel(count, slots, *refs):
    feat_ref, noise_ref = refs[1:3]
    params = refs[3:7]
    usage_in = refs[7]
    sends = refs[8 : 7 + count]
    usage_ref = refs[7 + count]
    code_scr = refs[8 + count]
    scr = refs[9 + count :]
    step = pl.program_id(0)

    @pl.when(step == 0)
    def _():
        prepare(params, *scr[0:3])
        usage_ref[...] = usage_in[...]

    forward(params, scr, feat_ref[...], noise_ref, [code_scr], usage_ref)
    for i in range(count - 1):

        @pl.when(lax.div(step, slots) == i)
        def _(i=i):
            sends[i][...] = code_scr[...]


def peer_image(start, share, first, slots):
    def image(i, table_ref):
        peer = lax.div(i, slots) + start
        return (table_ref[0, peer * share + first + lax.rem(i, slots)], 0, 0)

    return image


def wide_forward(count, first, slots, table, feat, noise, params, usage):
    dim, codes = params[2].shape
    images, strip, width = feat.shape
    image = peer_image(1, images // count, first, slots)
    return pl.pallas_call(
        functools.partial(wide_forward_kernel, count, slots),
        grid_spec=pltpu.PrefetchScalarGridSpec(
            num_scalar_prefetch=1,
            grid=((count - 1) * slots,),
            in_specs=[
                pl.BlockSpec((None, strip, width), image),
                pl.BlockSpec((None, strip, codes), image),
                fixed(params[0].shape),
                fixed(params[1].shape),
                fixed(params[2].shape),
                fixed(params[3].shape),
                fixed(usage.shape),
            ],
            out_specs=[part_rows(i, slots, (strip, codes)) for i in range(count - 1)]
            + [fixed(usage.shape)],
            scratch_shapes=[pltpu.VMEM((strip, codes), F32)]
            + tile_scratch(strip, dim, codes, width),
        ),
        out_shape=[jax.ShapeDtypeStruct((strip * slots, codes), F32)] * (count - 1)
        + [pltpu.HBM(usage.shape, F32)],
        input_output_aliases={7: count - 1},
        compiler_params=settings(),
        cost_estimate=cost((count - 1) * slots * strip, width, dim, codes, 4),
        name="wide_forward",
    )(table, *in_hbm([feat, noise, *params, usage]))


def wide_both_kernel(peers, slots, new, *refs):
    feat_ref, noise_ref, cot_ref = refs[1:4]
    params = refs[4:8]
    rest = refs[8:]
    if not new:
        acc_in, rest = rest[0], rest[2:]
    sends = rest[0:peers]
    grad_ref, acc_ref, code_scr = rest[peers : 3 + peers]
    scr = rest[3 + peers :]
    step = pl.program_id(0)

    @pl.when(step == 0)
    def _():
        prepare(params, *scr[0:3])
        acc_ref[...] = jnp.zeros(acc_ref.shape, F32) if new else acc_in[...]

    grad_ref[...] = both_ways(
        params, scr, feat_ref[...], cot_ref[...], noise_ref, code_scr, acc_ref
    )
    for i in range(peers):

        @pl.when(lax.div(step, slots) == i)
        def _(i=i):
            sends[i][...] = code_scr[...]


def wide_both(count, steps, first, slots, table, feat, noise, cot, params, acc, grad):
    dim, codes = params[2].shape
    images, strip, width = feat.shape
    image = peer_image(steps[0], images // count, first, slots)
    acc_shape = (ACC_ROWS, codes)
    peers = len(steps)
    new = acc is None
    return pl.pallas_call(
        functools.partial(wide_both_kernel, peers, slots, new),
        grid_spec=pltpu.PrefetchScalarGridSpec(
            num_scalar_prefetch=1,
            grid=(peers * slots,),
            in_specs=[
                pl.BlockSpec((None, strip, width), image),
                pl.BlockSpec((None, strip, codes), image),
                pl.BlockSpec((None, dim, strip), image),
            ]
            + [fixed(p.shape) for p in params]
            + ([] if new else [fixed(acc_shape), HBM]),
            out_specs=[part_rows(i, slots, (strip, codes)) for i in range(peers)]
            + [pl.BlockSpec((None, strip, width), image), fixed(acc_shape)],
            scratch_shapes=[pltpu.VMEM((strip, codes), F32)]
            + tile_scratch(strip, dim, codes, width),
        ),
        out_shape=[jax.ShapeDtypeStruct((strip * slots, codes), F32)] * peers
        + [pltpu.HBM(feat.shape, F32), pltpu.HBM(acc_shape, F32)],
        input_output_aliases={} if new else {8: peers + 1, 9: peers},
        compiler_params=settings(),
        cost_estimate=cost(peers * slots * strip, width, dim, codes, 10 if new else 3),
        name="wide_both",
    )(table, *in_hbm([feat, noise, cot, *params] + ([] if new else [acc, grad])))


def wide_backward_kernel(count, slots, *refs):
    feat_ref, cot_ref = refs[1:3]
    parts = refs[3 : 2 + count]
    params = refs[2 + count : 6 + count]
    acc_in = refs[6 + count]
    grad_ref, acc_ref, code_scr = refs[8 + count : 11 + count]
    scr = refs[11 + count :]
    step = pl.program_id(0)

    @pl.when(step == 0)
    def _():
        prepare(params, *scr[0:3])
        acc_ref[...] = acc_in[...]

    for i in range(count - 1):

        @pl.when(lax.div(step, slots) == i)
        def _(i=i):
            code_scr[...] = parts[i][...]

    grad_ref[...] = backward(params, scr, feat_ref[...], cot_ref[...], code_scr, acc_ref)


def wide_backward(count, first, slots, table, feat, cot, parts, params, acc, grad):
    dim, codes = params[2].shape
    images, strip, width = feat.shape
    image = peer_image(1, images // count, first, slots)
    return pl.pallas_call(
        functools.partial(wide_backward_kernel, count, slots),
        grid_spec=pltpu.PrefetchScalarGridSpec(
            num_scalar_prefetch=1,
            grid=((count - 1) * slots,),
            in_specs=[
                pl.BlockSpec((None, strip, width), image),
                pl.BlockSpec((None, dim, strip), image),
            ]
            + [part_rows(i, slots, (strip, codes)) for i in range(count - 1)]
            + [fixed(p.shape) for p in params]
            + [fixed(acc.shape), HBM],
            out_specs=[pl.BlockSpec((None, strip, width), image), fixed(acc.shape)],
            scratch_shapes=[pltpu.VMEM((strip, codes), F32)]
            + tile_scratch(strip, dim, codes, width),
        ),
        out_shape=[pltpu.HBM(feat.shape, F32), pltpu.HBM(acc.shape, F32)],
        input_output_aliases={6 + count: 1, 7 + count: 0},
        compiler_params=settings(),
        cost_estimate=cost((count - 1) * slots * strip, width, dim, codes, 6),
        name="wide_backward",
    )(table, *in_hbm([feat, cot]), *parts, *in_hbm([*params, acc, grad]))


def shard_at(index, parts):
    height = 64 // parts
    return pl.ds(pl.multiple_of(index * height, height), height)


def lay_out(params, acc_ref, usage_ref, sum_scr, shards):
    weight_ref, bias_ref, book_ref, scalar_ref = params
    codes = book_ref.shape[1]
    width = weight_ref.shape[1]
    devices = len(shards)
    me = lax.rem(lax.axis_index("dp"), devices)
    precision, _, factor = scalars(scalar_ref)
    book = book_ref[...]
    column = acc_ref[128:129]
    moment = acc_ref[64:128] * (1.0 / precision)
    book_sum = acc_ref[0:64] * (1.0 / factor) + 2.0 * (column * book - moment)
    slope = jnp.sum(
        jnp.sum(book * book, axis=0, keepdims=True) * column, axis=1, keepdims=True
    ) - 2.0 * jnp.sum(jnp.sum(book * moment, axis=0, keepdims=True), axis=1, keepdims=True)
    slope = slope + acc_ref[208:209, 0:1] / (-0.5 * precision)
    usage = jnp.sum(acc_ref[136:144] + usage_ref[...], axis=0, keepdims=True)
    dim = book_ref.shape[0]
    eye = lax.broadcasted_iota(jnp.int32, (dim, dim), 0) == lax.broadcasted_iota(
        jnp.int32, (dim, dim), 1
    )
    bias = acc_ref[144:208, width : width + dim]
    bias = jnp.sum(jnp.where(eye, bias, 0.0), axis=0, keepdims=True)
    rest = codes + width
    sum_scr[:, 0:codes] = book_sum
    sum_scr[:, codes:rest] = acc_ref[144:208, 0:width]
    sum_scr[:, rest : rest + 128] = jnp.broadcast_to(slope, (64, 128))
    rows = codes // 128
    for i in range(rows):
        sum_scr[i : i + 1, rest : rest + 128] = usage[:, i * 128 : (i + 1) * 128]
    sum_scr[rows : rows + 1, rest : rest + dim] = bias
    for i in range(devices):
        shards[i][...] = sum_scr[shard_at(partner(me, i, devices), devices)]


def own_kernel(*refs):
    feat_ref, noise_ref, cot_ref = refs[1:4]
    params = refs[4:8]
    acc_in = refs[8]
    code_ref, grad_ref, acc_ref = refs[10:13]
    scr = refs[13:]

    @pl.when(pl.program_id(0) == 0)
    def _():
        prepare(params, *scr[0:3])
        acc_ref[...] = acc_in[...]

    grad_ref[...] = both_ways(
        params, scr, feat_ref[...], cot_ref[...], noise_ref, code_ref, acc_ref
    )


def run_own(count, table, feat, noise, cot, params, acc, grad):
    dim, codes = params[2].shape
    images, strip, width = feat.shape
    share = images // count

    def image(i, table_ref):
        return (table_ref[0, i], 0, 0)

    return pl.pallas_call(
        own_kernel,
        grid_spec=pltpu.PrefetchScalarGridSpec(
            num_scalar_prefetch=1,
            grid=(share,),
            in_specs=[
                pl.BlockSpec((None, strip, width), image),
                pl.BlockSpec((None, strip, codes), image),
                pl.BlockSpec((None, dim, strip), image),
                fixed(params[0].shape),
                fixed(params[1].shape),
                fixed(params[2].shape),
                fixed(params[3].shape),
                fixed(acc.shape),
                HBM,
            ],
            out_specs=[
                pl.BlockSpec(
                    (None, strip, codes),
                    lambda i, table_ref: (i, table_ref[0, count * share], 0),
                ),
                pl.BlockSpec((None, strip, width), image),
                fixed(acc.shape),
            ],
            scratch_shapes=tile_scratch(strip, dim, codes, width),
        ),
        out_shape=[
            pltpu.HBM((share, strip * count, codes), F32),
            pltpu.HBM(feat.shape, F32),
            pltpu.HBM(acc.shape, F32),
        ],
        input_output_aliases={8: 2, 9: 1},
        compiler_params=settings(),
        cost_estimate=cost(share * strip, width, dim, codes, 10),
        name="own_images",
    )(table, *in_hbm([feat, noise, cot, *params, acc, grad]))


def place_kernel(count, first, slots, steps, *refs):
    parts = refs[0 : len(steps)]
    out_ref, sem = refs[len(steps) + 1 : len(steps) + 3]
    strip = parts[0].shape[0] // slots
    me = lax.axis_index("space")
    copies = []
    for part, step in zip(parts, steps):
        row = pl.multiple_of(source(me, step, count) * strip, strip)
        for j in range(slots):
            copies.append(
                pltpu.make_async_copy(
                    part.at[pl.ds(j * strip, strip)],
                    out_ref.at[first + j, pl.ds(row, strip)],
                    sem.at[len(copies)],
                )
            )
    for copy in copies:
        copy.start()
    for copy in copies:
        copy.wait()


def place_wide(count, first, slots, steps, parts, whole):
    steps = list(steps)
    return pl.pallas_call(
        functools.partial(place_kernel, count, first, slots, steps),
        out_shape=pltpu.HBM(whole.shape, F32),
        in_specs=[VMEM] * len(steps) + [HBM],
        out_specs=HBM,
        scratch_shapes=[pltpu.SemaphoreType.DMA((len(steps) * slots,))],
        input_output_aliases={len(steps): 0},
        compiler_params=settings(),
        cost_estimate=pl.CostEstimate(
            flops=0, bytes_accessed=2 * sum(p.size * 4 for p in parts), transcendentals=0
        ),
        name="place_wide",
    )(*[pltpu.with_memory_space_constraint(p, pltpu.VMEM) for p in parts], *in_hbm([whole]))


def join_kernel(count, *refs):
    parts = refs[0:count]
    outs = refs[count:]
    me = lax.axis_index("space")
    for step in range(count):
        here = source(me, step, count)
        base = 0
        for out in outs:
            for j in range(out.shape[0]):
                strip = out.shape[2]
                out[j, here] = parts[step][base : base + strip]
                base += strip


def join_small(count, parts, shapes):
    codes = parts[0].shape[1]
    return pl.pallas_call(
        functools.partial(join_kernel, count),
        out_shape=[
            jax.ShapeDtypeStruct((images // count, count, strip, codes), F32)
            for images, strip, _ in shapes
        ],
        compiler_params=settings(),
        name="join_small",
    )(*parts)


def tree(values):
    while len(values) > 1:
        values = [
            values[i] + values[i + 1] if i + 1 < len(values) else values[i]
            for i in range(0, len(values), 2)
        ]
    return values[0]


def sum_kernel(*refs):
    refs[-1][...] = tree([ref[...] for ref in refs[:-1]])


def add_all(parts):
    return pl.pallas_call(
        sum_kernel,
        out_shape=jax.ShapeDtypeStruct(parts[0].shape, F32),
        name="add_parts",
    )(*parts)


def final_kernel(devices, pixels, *refs):
    shards = refs[0:devices]
    weight_ref, bias_ref, book_ref, log_ref, usage_ref = refs[devices : devices + 5]
    weight_out, bias_out, book_out, log_out, usage_out = refs[devices + 5 : devices + 10]
    sum_scr = refs[devices + 10]
    me = lax.rem(lax.axis_index("dp"), devices)
    for i in range(devices):
        sum_scr[shard_at(source(me, i, devices), devices)] = shards[i][...]
    dim, codes = book_ref.shape
    width = weight_ref.shape[1]
    scale = 0.5 * lax.rsqrt(jnp.full((8, 128), pixels, F32))[0:1, 0:1]
    book_out[...] = 0.5 * book_ref[...] + scale * sum_scr[:, 0:codes]
    rest = codes + width
    weight_out[...] = 0.5 * weight_ref[...] + scale * sum_scr[:, codes:rest]
    rows = codes // 128
    bias_out[...] = 0.5 * bias_ref[...] + scale * sum_scr[rows : rows + 1, rest : rest + dim]
    usage = jnp.concatenate(
        [sum_scr[i : i + 1, rest : rest + 128] for i in range(rows)], axis=1
    )
    usage_out[...] = 0.5 * usage_ref[...] + 0.5 * (codes / pixels) * usage
    log_out[...] = 0.5 * log_ref[...] + scale * sum_scr[rows + 1 : rows + 2, rest : rest + 1]


def finish(devices, pixels, shards, weight, bias, book, log, usage):
    outs = (weight.T, bias.reshape(1, -1), book.T, log.reshape(1, 1), usage.reshape(1, -1))
    outs = pl.pallas_call(
        functools.partial(final_kernel, devices, pixels),
        out_shape=[jax.ShapeDtypeStruct(out.shape, F32) for out in outs],
        scratch_shapes=[pltpu.VMEM((64, LANES), F32)],
        name="new_averages",
    )(*shards, *outs)
    return outs[0].T, outs[1].reshape(-1), outs[2].T, outs[3].reshape(-1), outs[4].reshape(-1)


def exchange(value, bit, size, pairs):
    while bit < size:
        value = value + pairs(value, bit)
        bit = 2 * bit
    return value


def spans(share):
    return [(0, 1), (1, share - 1)]


def per_device(
    feat_small,
    feat_mid,
    feat_wide,
    noise_small,
    noise_mid,
    noise_wide,
    cot_small,
    cot_mid,
    cot_wide,
    order_small,
    order_mid,
    order_wide,
    weight,
    bias,
    book,
    log,
    heat,
    weight_mean,
    bias_mean,
    book_mean,
    log_mean,
    usage_mean,
):
    count = lax.axis_size("space")
    devices = lax.axis_size("dp")
    params = (weight.T, bias.reshape(1, -1), book.T, log, heat)
    feats = (feat_small, feat_mid, feat_wide)
    pixels = sum(f.shape[0] * f.shape[1] for f in feats) * count * devices
    share = feat_wide.shape[0] // count
    cot_wide = jnp.swapaxes(cot_wide, 1, 2)

    def send(values):
        return [lax.ppermute(v, "space", route(i + 1, count)) for i, v in enumerate(values)]

    def follow(codes, before):
        before[0], codes[-1] = lax.optimization_barrier((before[0], codes[-1]))
        return send(codes)

    orders = (order_small, order_mid, order_wide)
    *small, table, usage, scalar = small_forward(
        count, orders, feats[0:2], (noise_small, noise_mid), params
    )
    params = (*params[0:3], scalar)
    arrived = [send(small[1:])]
    near = min(4, devices)
    early, late = spans(share)
    *early_codes, usage = wide_forward(
        count, *early, table, feat_wide, noise_wide, params, usage
    )
    arrived.append(follow(list(early_codes), arrived[0]))
    codes_small, codes_mid = join_small(
        count, [small[0]] + arrived[0], [f.shape for f in feats[0:2]]
    )
    codes_small, codes_mid, scalar = lax.optimization_barrier(
        (codes_small, codes_mid, scalar)
    )
    params = (*params[0:3], scalar)
    codes = []
    grad = acc = None
    for steps in (range(1, count - 1), range(count - 1, count)):
        *part, grad, acc = wide_both(
            count, steps, *late, table, feat_wide, noise_wide, cot_wide, params, acc, grad
        )
        codes.extend(part)
    arrived.append(follow(codes, arrived[1]))
    arrived[1], acc = lax.optimization_barrier((arrived[1], acc))
    whole, grad, acc = run_own(
        count, table, feat_wide, noise_wide, cot_wide, params, acc, grad
    )
    whole = place_wide(count, *early, range(1, count), arrived[1], whole)
    whole, acc = lax.optimization_barrier((whole, acc))
    grad, acc = wide_backward(
        count, *early, table, feat_wide, cot_wide, early_codes, params, acc, grad
    )
    grad_small, grad_mid, *shards = small_backward(
        count,
        near,
        feat_wide.shape[0],
        table,
        feats[0:2],
        (cot_small, cot_mid),
        small,
        params,
        acc,
        usage,
    )
    group = [
        [(i, i - i % near + partner(i % near, step, near)) for i in range(devices)]
        for step in range(near)
    ]
    parts = [lax.ppermute(shards[i], "dp", group[i]) for i in range(1, near)]
    mine = add_all([shards[0]] + parts)

    def along(value, offset):
        return lax.ppermute(value, "dp", [(i, i ^ offset) for i in range(devices)])

    def across(value, offset):
        turn = near if devices > near else 0
        pairs = [
            (i * count + j, (i ^ turn) * count + (j ^ offset))
            for i in range(devices)
            for j in range(count)
        ]
        return lax.ppermute(value, ("dp", "space"), pairs)

    mine = exchange(mine, near, devices, along)
    mine = exchange(mine, 1, count, across)
    shards = [mine] + [lax.ppermute(mine, "dp", group[i]) for i in range(1, near)]
    updated = finish(
        near, pixels, shards, weight_mean, bias_mean, book_mean, log_mean, usage_mean
    )
    for step in range(1, count):
        whole = place_wide(count, *late, [step], [arrived[2][step - 1]], whole)
    codes = whole.shape[2]
    return (
        codes_small.reshape(codes_small.shape[0], -1, codes),
        codes_mid.reshape(codes_mid.shape[0], -1, codes),
        whole,
        grad_small,
        grad_mid,
        grad,
        *updated,
    )


def solution(mesh):
    strips = P("dp", "space", None)
    placed = (strips,) * 9 + (P("dp", None),) * 3 + (P(),) * 10
    return jax.shard_map(
        per_device,
        mesh=mesh,
        in_specs=placed,
        out_specs=(P(("dp", "space"), None, None),) * 3 + (strips,) * 3 + (P(),) * 5,
        check_vma=False,
    )
```

```python
import functools

import jax
import jax.numpy as jnp
from jax import lax
from jax.experimental import pallas as pl
from jax.experimental.pallas import tpu as pltpu
from jax.sharding import PartitionSpec as P

F32 = jnp.float32
BF16 = jnp.bfloat16
VMEM_LIMIT = 16 * 1024 * 1024
ACC_ROWS = 64 + 64 + 8 + 8 + 64 + 8
LANES = 896


def partner(index, step, count):
    if count & (count - 1) == 0:
        return index ^ step
    return lax.rem(index + step, count)


def route(step, count):
    if count & (count - 1) == 0:
        return [(i, i ^ step) for i in range(count)]
    return [(i, (i + step) % count) for i in range(count)]


def source(index, step, count):
    if count & (count - 1) == 0:
        return index ^ step
    return lax.rem(index + (count - step), count)


def in_hbm(arrays):
    return [pltpu.with_memory_space_constraint(a, pltpu.HBM) for a in arrays]


def halves(x):
    high = x.astype(BF16)
    return high, (x - high.astype(F32)).astype(BF16)


def dot(left, right, left_dim=1, right_dim=0):
    return lax.dot_general(
        left, right, (((left_dim,), (right_dim,)), ((), ())), preferred_element_type=F32
    )


def set_scalars(log_ref, heat_ref, out_ref):
    precision = jnp.exp(jnp.full((8, 128), log_ref[0], F32))
    heat = jnp.full((8, 128), heat_ref[0], F32)
    row = lax.broadcasted_iota(jnp.int32, (8, 128), 0)
    factor = -0.5 * precision / heat
    out_ref[...] = jnp.where(row == 0, precision, jnp.where(row == 1, 1.0 / heat, factor))


def scalars(ref):
    return ref[0:1, 0:1], ref[1:2, 0:1], ref[2:3, 0:1]


def prepare(refs, book_scr, books_scr, weight_scr):
    weight_ref, bias_ref, book_ref, scalar_ref = refs
    dim, codes = book_ref.shape
    precision, _, _ = scalars(scalar_ref)
    book = book_ref[...]
    high, low = halves(book)
    norm = -0.5 * precision * jnp.sum(book * book, axis=0, keepdims=True)
    n0 = norm.astype(BF16).astype(F32)
    n1 = (norm - n0).astype(BF16).astype(F32)
    n2 = norm - n0 - n1
    row = lax.broadcasted_iota(jnp.int32, (16, codes), 0)
    extra = jnp.where(
        row < 3,
        1.0,
        jnp.where(row == 3, n0, jnp.where(row == 4, n1, jnp.where(row == 5, n2, 0.0))),
    ).astype(BF16)
    book_scr[0:dim] = high
    book_scr[dim : 2 * dim] = low
    book_scr[2 * dim : 3 * dim] = high
    book_scr[3 * dim : 3 * dim + 16] = extra
    books_scr[0:dim] = high
    books_scr[dim : 2 * dim] = low
    books_scr[2 * dim : 2 * dim + 16] = jnp.ones((16, codes), BF16)
    high, low = halves(weight_ref[...])
    weight_scr[0:dim] = high
    weight_scr[dim : 2 * dim] = low
    weight_scr[2 * dim : 3 * dim] = high


def latents(refs, scr, feat):
    weight_ref, bias_ref, book_ref, scalar_ref = refs
    weight_scr = scr[2]
    dim = book_ref.shape[0]
    precision, _, _ = scalars(scalar_ref)
    eye = lax.broadcasted_iota(jnp.int32, (dim, dim), 0) == lax.broadcasted_iota(
        jnp.int32, (dim, dim), 1
    )
    bias = jnp.sum(jnp.where(eye, bias_ref[...], 0.0), axis=1, keepdims=True)
    fh, fl = halves(feat)
    both = weight_scr[0 : 2 * dim]
    z2 = dot(both, fh, 1, 1) + dot(both, fl, 1, 1)
    z = z2[0:dim] + z2[dim : 2 * dim] + bias
    square = -0.5 * precision * jnp.sum(z * z, axis=0, keepdims=True)
    return fh, fl, z, square


def logit_rows(zh, zl, square):
    rows = zh.shape[1]
    s0 = square.astype(BF16).astype(F32)
    s1 = (square - s0).astype(BF16).astype(F32)
    s2 = square - s0 - s1
    row = lax.broadcasted_iota(jnp.int32, (16, rows), 0)
    extra = jnp.where(
        row == 0,
        s0,
        jnp.where(row == 1, s1, jnp.where(row == 2, s2, jnp.where(row < 6, 1.0, 0.0))),
    ).astype(BF16)
    return jnp.concatenate([zh, zh, zl, extra], axis=0)


def cot_rows(ch, cl):
    return jnp.concatenate([ch, ch, cl, jnp.zeros((16, ch.shape[1]), BF16)], axis=0)


def over_rows(rows, body, carry):
    step = next(s for s in (32, 16, 8) if rows % s == 0)

    def at(i, carry):
        return body(pl.ds(pl.multiple_of(i * step, step), step), carry)

    return lax.fori_loop(0, rows // step, at, carry, unroll=True)


def folded(x):
    return jnp.sum(x.reshape(x.shape[0] // 8, 8, x.shape[1]), axis=0)


def probabilities(logits):
    top = jnp.max(logits, axis=1, keepdims=True)
    e = jnp.exp(logits - top)
    return e * (1.0 / jnp.sum(e, axis=1, keepdims=True))


def forward(refs, scr, feat, noise_ref, code_refs, usage_ref):
    weight_ref, bias_ref, book_ref, scalar_ref = refs
    book_scr, l_scr = scr[0], scr[3]
    rows = feat.shape[0]
    precision, cold, _ = scalars(scalar_ref)
    _, _, z, square = latents(refs, scr, feat)
    zh, zl = halves(precision * z)
    l_scr[0:rows] = dot(logit_rows(zh, zl, square), book_scr[...], 0, 0)

    usage = usage_ref[...]
    part = rows // len(code_refs)
    for i, code_ref in enumerate(code_refs):
        logit_part = l_scr.at[pl.ds(i * part, part)]
        noise_part = noise_ref.at[pl.ds(i * part, part)]

        def body(at, usage, code_ref=code_ref, logit_part=logit_part, noise_part=noise_part):
            logits = logit_part[at]
            code_ref[at] = probabilities((logits + noise_part[at]) * cold)
            return usage + folded(probabilities(logits))

        usage = over_rows(part, body, usage)
    usage_ref[...] = usage


def gradients(refs, scr, fh, fl, z, square, zh, zl, ch, cl, acc_ref):
    books_scr, weight_scr = scr[1:3]
    wh_scr, wl_scr, gh_scr, gl_scr = scr[5:9]
    rows, feats = fh.shape
    dim, codes = refs[2].shape
    wh, wl = wh_scr[0:rows], wl_scr[0:rows]
    gh, gl = gh_scr[0:rows], gl_scr[0:rows]
    p = dot(jnp.concatenate([ch, cl], axis=0), wh)
    acc_ref[0:64] += p[0:dim] + p[dim : 2 * dim] + dot(ch, wl)
    left = jnp.concatenate([zh, zl, jnp.ones((16, rows), BF16)], axis=0)
    p = dot(left, gh) + dot(left, gl)
    acc_ref[64:128] += p[0:dim] + p[dim : 2 * dim]
    acc_ref[128:136] += p[2 * dim : 2 * dim + 8]
    p = dot(books_scr[...], gh, 1, 1) + dot(books_scr[...], gl, 1, 1)
    row_d = p[2 * dim : 2 * dim + 1]
    gz = 2.0 * (row_d * z - (p[0:dim] + p[dim : 2 * dim]))
    zh, zl = halves(gz)
    p = dot(jnp.concatenate([zh, zl], axis=0), fh)
    acc_ref[144:208, 0:feats] += p[0:dim] + p[dim : 2 * dim] + dot(zh, fl)
    acc_ref[144:208, feats : feats + 128] += jnp.broadcast_to(
        jnp.sum(gz, axis=1, keepdims=True), (dim, 128)
    )
    total = jnp.sum(square * row_d, axis=1, keepdims=True)
    acc_ref[208:216] += jnp.broadcast_to(total, (8, codes))
    return dot(jnp.concatenate([zh, zh, zl], axis=0), weight_scr[...], 0, 0)


def backward(refs, scr, feat, cot, code_ref, acc_ref):
    weight_ref, bias_ref, book_ref, scalar_ref = refs
    book_scr, _, _, _, g_scr, wh_scr, wl_scr, gh_scr, gl_scr = scr
    rows = feat.shape[0]
    precision, _, factor = scalars(scalar_ref)
    fh, fl, z, square = latents(refs, scr, feat)
    zh, zl = halves(precision * z)
    ch, cl = halves(factor * cot)
    g_scr[0:rows] = dot(cot_rows(ch, cl), book_scr[...], 0, 0)

    def body(at, carry):
        w = code_ref[at]
        gw = g_scr[at]
        gd = w * (gw - jnp.sum(w * gw, axis=1, keepdims=True))
        wh_scr[at], wl_scr[at] = halves(w)
        gh_scr[at], gl_scr[at] = halves(gd)
        return carry

    over_rows(rows, body, 0)
    return gradients(refs, scr, fh, fl, z, square, zh, zl, ch, cl, acc_ref)


def both_ways(refs, scr, feat, cot, noise_ref, code_ref, acc_ref):
    weight_ref, bias_ref, book_ref, scalar_ref = refs
    book_scr, _, _, l_scr, g_scr, wh_scr, wl_scr, gh_scr, gl_scr = scr
    rows = feat.shape[0]
    precision, cold, factor = scalars(scalar_ref)
    fh, fl, z, square = latents(refs, scr, feat)
    zh, zl = halves(precision * z)
    ch, cl = halves(factor * cot)
    left = jnp.concatenate([logit_rows(zh, zl, square), cot_rows(ch, cl)], axis=1)
    p = dot(left, book_scr[...], 0, 0)
    l_scr[0:rows] = p[0:rows]
    g_scr[0:rows] = p[rows : 2 * rows]

    def body(at, usage):
        logits = l_scr[at]
        s = (logits + noise_ref[at]) * cold
        e = jnp.exp(s - jnp.max(s, axis=1, keepdims=True))
        gw = g_scr[at]
        scale = 1.0 / jnp.sum(e, axis=1, keepdims=True)
        inner = jnp.sum(e * gw, axis=1, keepdims=True) * scale
        w = e * scale
        code_ref[at] = w
        gd = w * (gw - inner)
        wh_scr[at], wl_scr[at] = halves(w)
        gh_scr[at], gl_scr[at] = halves(gd)
        return usage + folded(probabilities(logits))

    acc_ref[136:144] = over_rows(rows, body, acc_ref[136:144])
    return gradients(refs, scr, fh, fl, z, square, zh, zl, ch, cl, acc_ref)


def tile_scratch(rows, dim, codes, feats):
    return [
        pltpu.VMEM((3 * dim + 16, codes), BF16),
        pltpu.VMEM((2 * dim + 16, codes), BF16),
        pltpu.VMEM((3 * dim, feats), BF16),
        pltpu.VMEM((rows, codes), F32),
        pltpu.VMEM((rows, codes), F32),
        pltpu.VMEM((rows, codes), BF16),
        pltpu.VMEM((rows, codes), BF16),
        pltpu.VMEM((rows, codes), BF16),
        pltpu.VMEM((rows, codes), BF16),
    ]


def settings(limit=VMEM_LIMIT):
    return pltpu.CompilerParams(vmem_limit_bytes=limit)


def cost(rows, feats, dim, codes, tenths):
    return pl.CostEstimate(
        flops=rows * 24 * tenths * (5 * dim * codes + 3 * dim * feats) // 10,
        bytes_accessed=4 * rows * (2 * feats + 2 * codes + dim),
        transcendentals=2 * rows * codes,
    )


SMEM = pl.BlockSpec(memory_space=pltpu.SMEM)
VMEM = pl.BlockSpec(memory_space=pltpu.VMEM)
HBM = pl.BlockSpec(memory_space=pltpu.HBM)


def fixed(shape):
    return pl.BlockSpec(shape, lambda *_: (0,) * len(shape))


def part_rows(peer, slots, shape):
    return pl.BlockSpec(shape, lambda i, _: (jnp.clip(i - peer * slots, 0, slots - 1), 0))


def places_of(table_ref, wide, shapes, groups, count):
    places = []
    base = 0
    entry = wide + 1
    for _ in range(count):
        for size in range(2):
            strip = shapes[size][1]
            for _ in range(groups[size]):
                places.append((size, table_ref[0, entry], base, strip))
                base += strip
                entry += 1
    return places, base


def small_forward_kernel(count, groups, *refs):
    sources = refs[0:10]
    log_ref, heat_ref = refs[10:12]
    sends = refs[12 : 12 + count]
    table_ref, usage_ref, scalar_ref = refs[12 + count : 15 + count]
    held = refs[15 + count : 25 + count]
    sems, feat_scr, noise_scr = refs[25 + count : 28 + count]
    scr = refs[28 + count :]
    copies = [
        pltpu.make_async_copy(there, here, sems.at[i])
        for i, (there, here) in enumerate(zip(sources, held))
    ]
    for copy in copies:
        copy.start()
    orders, feats, noises, params = held[0:3], held[3:5], held[5:7], (*held[7:10], scalar_ref)
    me = lax.axis_index("space")
    set_scalars(log_ref, heat_ref, scalar_ref)
    for copy in copies[7:10]:
        copy.wait()
    prepare(params, *scr[0:3])
    for copy in copies[0:5]:
        copy.wait()
    wide = orders[2].shape[1]
    share = wide // count
    entry = wide + 1
    table_ref[0, wide] = me
    for step in range(count):
        there = partner(me, step, count)
        for j in range(share):
            table_ref[0, step * share + j] = orders[2][0, there * share + j]
        for size in range(2):
            for j in range(groups[size]):
                table_ref[0, entry] = orders[size][0, there * groups[size] + j]
                entry += 1
    places, _ = places_of(table_ref, wide, [f.shape for f in feats], groups, count)
    for size, image, at, strip in places:
        feat_scr[at : at + strip] = feats[size][image]
    for copy in copies[5:7]:
        copy.wait()
    for size, image, at, strip in places:
        noise_scr[at : at + strip] = noises[size][image]
    usage_ref[...] = jnp.zeros(usage_ref.shape, F32)
    forward(params, scr, feat_scr[...], noise_scr, sends, usage_ref)


def small_forward(count, orders, feats, noises, params):
    dim, codes = params[2].shape
    width = feats[0].shape[2]
    groups = tuple(f.shape[0] // count for f in feats)
    part = sum(g * f.shape[1] for g, f in zip(groups, feats))
    rows = part * count
    arrays = [*orders, *feats, *noises, *params[0:3]]
    return pl.pallas_call(
        functools.partial(small_forward_kernel, count, groups),
        out_shape=[jax.ShapeDtypeStruct((part, codes), F32)] * count
        + [
            jax.ShapeDtypeStruct((1, sum(o.shape[1] for o in orders) + 1), jnp.int32),
            pltpu.HBM((8, codes), F32),
            pltpu.HBM((8, 128), F32),
        ],
        in_specs=[HBM] * 10 + [SMEM] * 2,
        out_specs=[VMEM] * count + [SMEM, VMEM, VMEM],
        scratch_shapes=[
            (pltpu.SMEM if i < 3 else pltpu.VMEM)(a.shape, a.dtype)
            for i, a in enumerate(arrays)
        ]
        + [
            pltpu.SemaphoreType.DMA((10,)),
            pltpu.VMEM((rows, width), F32),
            pltpu.VMEM((rows, codes), F32),
        ]
        + tile_scratch(rows, dim, codes, width),
        compiler_params=settings(),
        cost_estimate=cost(rows, width, dim, codes, 4),
        name="small_forward",
    )(*in_hbm(arrays), *params[3:5])


def small_backward_kernel(count, devices, wide, groups, *refs):
    table_ref = refs[0]
    feats, cots = refs[1:3], refs[3:5]
    parts = refs[5 : 5 + count]
    params = refs[5 + count : 9 + count]
    acc_in, usage_ref = refs[9 + count : 11 + count]
    grads = refs[11 + count : 13 + count]
    shards = refs[13 + count : 13 + count + devices]
    rest = refs[13 + count + devices :]
    acc_ref, sum_scr, feat_scr, cot_scr, code_scr = rest[0:5]
    scr = rest[5:]
    places, base = places_of(table_ref, wide, [f.shape for f in feats], groups, count)
    for size, image, at, strip in places:
        feat_scr[at : at + strip] = feats[size][image]
        cot_scr[at : at + strip] = cots[size][image]
    part = base // count
    for step in range(count):
        code_scr[step * part : (step + 1) * part] = parts[step][...]
    prepare(params, *scr[0:3])
    acc_ref[...] = acc_in[...]
    feat_scr[...] = backward(params, scr, feat_scr[...], cot_scr[...].T, code_scr, acc_ref)
    lay_out(params, acc_ref, usage_ref, sum_scr, shards)
    for size, image, at, strip in places:
        grads[size][image] = feat_scr[at : at + strip]


def small_backward(count, devices, wide, table, feats, cots, parts, params, acc, usage):
    dim, codes = params[2].shape
    width = feats[0].shape[2]
    groups = tuple(f.shape[0] // count for f in feats)
    rows = parts[0].shape[0] * count
    return pl.pallas_call(
        functools.partial(small_backward_kernel, count, devices, wide, groups),
        out_shape=[pltpu.HBM(f.shape, F32) for f in feats]
        + [jax.ShapeDtypeStruct((64 // devices, LANES), F32)] * devices,
        in_specs=[SMEM] + [VMEM] * (10 + count),
        out_specs=[VMEM] * (2 + devices),
        scratch_shapes=[
            pltpu.VMEM(acc.shape, F32),
            pltpu.VMEM((64, LANES), F32),
            pltpu.VMEM((rows, width), F32),
            pltpu.VMEM((rows, dim), F32),
            pltpu.VMEM((rows, codes), F32),
        ]
        + tile_scratch(rows, dim, codes, width),
        compiler_params=settings(),
        cost_estimate=cost(rows, width, dim, codes, 6),
        name="small_backward",
    )(
        table,
        *in_hbm([*feats, *cots]),
        *parts,
        *in_hbm([*params, acc, usage]),
    )


def wide_forward_kernel(count, slots, *refs):
    feat_ref, noise_ref = refs[1:3]
    params = refs[3:7]
    usage_in = refs[7]
    sends = refs[8 : 7 + count]
    usage_ref = refs[7 + count]
    code_scr = refs[8 + count]
    scr = refs[9 + count :]
    step = pl.program_id(0)

    @pl.when(step == 0)
    def _():
        prepare(params, *scr[0:3])
        usage_ref[...] = usage_in[...]

    forward(params, scr, feat_ref[...], noise_ref, [code_scr], usage_ref)
    for i in range(count - 1):

        @pl.when(lax.div(step, slots) == i)
        def _(i=i):
            sends[i][...] = code_scr[...]


def peer_image(start, share, first, slots):
    def image(i, table_ref):
        peer = lax.div(i, slots) + start
        return (table_ref[0, peer * share + first + lax.rem(i, slots)], 0, 0)

    return image


def wide_forward(count, first, slots, table, feat, noise, params, usage):
    dim, codes = params[2].shape
    images, strip, width = feat.shape
    image = peer_image(1, images // count, first, slots)
    return pl.pallas_call(
        functools.partial(wide_forward_kernel, count, slots),
        grid_spec=pltpu.PrefetchScalarGridSpec(
            num_scalar_prefetch=1,
            grid=((count - 1) * slots,),
            in_specs=[
                pl.BlockSpec((None, strip, width), image),
                pl.BlockSpec((None, strip, codes), image),
                fixed(params[0].shape),
                fixed(params[1].shape),
                fixed(params[2].shape),
                fixed(params[3].shape),
                fixed(usage.shape),
            ],
            out_specs=[part_rows(i, slots, (strip, codes)) for i in range(count - 1)]
            + [fixed(usage.shape)],
            scratch_shapes=[pltpu.VMEM((strip, codes), F32)]
            + tile_scratch(strip, dim, codes, width),
        ),
        out_shape=[jax.ShapeDtypeStruct((strip * slots, codes), F32)] * (count - 1)
        + [pltpu.HBM(usage.shape, F32)],
        input_output_aliases={7: count - 1},
        compiler_params=settings(),
        cost_estimate=cost((count - 1) * slots * strip, width, dim, codes, 4),
        name="wide_forward",
    )(table, *in_hbm([feat, noise, *params, usage]))


def wide_both_kernel(peers, slots, new, *refs):
    feat_ref, noise_ref, cot_ref = refs[1:4]
    params = refs[4:8]
    rest = refs[8:]
    if not new:
        acc_in, rest = rest[0], rest[2:]
    sends = rest[0:peers]
    grad_ref, acc_ref, code_scr = rest[peers : 3 + peers]
    scr = rest[3 + peers :]
    step = pl.program_id(0)

    @pl.when(step == 0)
    def _():
        prepare(params, *scr[0:3])
        acc_ref[...] = jnp.zeros(acc_ref.shape, F32) if new else acc_in[...]

    grad_ref[...] = both_ways(
        params, scr, feat_ref[...], cot_ref[...], noise_ref, code_scr, acc_ref
    )
    for i in range(peers):

        @pl.when(lax.div(step, slots) == i)
        def _(i=i):
            sends[i][...] = code_scr[...]


def wide_both(count, steps, first, slots, table, feat, noise, cot, params, acc, grad):
    dim, codes = params[2].shape
    images, strip, width = feat.shape
    image = peer_image(steps[0], images // count, first, slots)
    acc_shape = (ACC_ROWS, codes)
    peers = len(steps)
    new = acc is None
    return pl.pallas_call(
        functools.partial(wide_both_kernel, peers, slots, new),
        grid_spec=pltpu.PrefetchScalarGridSpec(
            num_scalar_prefetch=1,
            grid=(peers * slots,),
            in_specs=[
                pl.BlockSpec((None, strip, width), image),
                pl.BlockSpec((None, strip, codes), image),
                pl.BlockSpec((None, dim, strip), image),
            ]
            + [fixed(p.shape) for p in params]
            + ([] if new else [fixed(acc_shape), HBM]),
            out_specs=[part_rows(i, slots, (strip, codes)) for i in range(peers)]
            + [pl.BlockSpec((None, strip, width), image), fixed(acc_shape)],
            scratch_shapes=[pltpu.VMEM((strip, codes), F32)]
            + tile_scratch(strip, dim, codes, width),
        ),
        out_shape=[jax.ShapeDtypeStruct((strip * slots, codes), F32)] * peers
        + [pltpu.HBM(feat.shape, F32), pltpu.HBM(acc_shape, F32)],
        input_output_aliases={} if new else {8: peers + 1, 9: peers},
        compiler_params=settings(),
        cost_estimate=cost(peers * slots * strip, width, dim, codes, 10 if new else 2),
        name="wide_both",
    )(table, *in_hbm([feat, noise, cot, *params] + ([] if new else [acc, grad])))


def wide_backward_kernel(count, slots, *refs):
    feat_ref, cot_ref = refs[1:3]
    parts = refs[3 : 2 + count]
    params = refs[2 + count : 6 + count]
    acc_in = refs[6 + count]
    grad_ref, acc_ref, code_scr = refs[8 + count : 11 + count]
    scr = refs[11 + count :]
    step = pl.program_id(0)

    @pl.when(step == 0)
    def _():
        prepare(params, *scr[0:3])
        acc_ref[...] = acc_in[...]

    for i in range(count - 1):

        @pl.when(lax.div(step, slots) == i)
        def _(i=i):
            code_scr[...] = parts[i][...]

    grad_ref[...] = backward(params, scr, feat_ref[...], cot_ref[...], code_scr, acc_ref)


def wide_backward(count, first, slots, table, feat, cot, parts, params, acc, grad):
    dim, codes = params[2].shape
    images, strip, width = feat.shape
    image = peer_image(1, images // count, first, slots)
    return pl.pallas_call(
        functools.partial(wide_backward_kernel, count, slots),
        grid_spec=pltpu.PrefetchScalarGridSpec(
            num_scalar_prefetch=1,
            grid=((count - 1) * slots,),
            in_specs=[
                pl.BlockSpec((None, strip, width), image),
                pl.BlockSpec((None, dim, strip), image),
            ]
            + [part_rows(i, slots, (strip, codes)) for i in range(count - 1)]
            + [fixed(p.shape) for p in params]
            + [fixed(acc.shape), HBM],
            out_specs=[pl.BlockSpec((None, strip, width), image), fixed(acc.shape)],
            scratch_shapes=[pltpu.VMEM((strip, codes), F32)]
            + tile_scratch(strip, dim, codes, width),
        ),
        out_shape=[pltpu.HBM(feat.shape, F32), pltpu.HBM(acc.shape, F32)],
        input_output_aliases={6 + count: 1, 7 + count: 0},
        compiler_params=settings(),
        cost_estimate=cost((count - 1) * slots * strip, width, dim, codes, 6),
        name="wide_backward",
    )(table, *in_hbm([feat, cot]), *parts, *in_hbm([*params, acc, grad]))


def shard_at(index, parts):
    height = 64 // parts
    return pl.ds(pl.multiple_of(index * height, height), height)


def lay_out(params, acc_ref, usage_ref, sum_scr, shards):
    weight_ref, bias_ref, book_ref, scalar_ref = params
    codes = book_ref.shape[1]
    width = weight_ref.shape[1]
    devices = len(shards)
    me = lax.rem(lax.axis_index("dp"), devices)
    precision, _, factor = scalars(scalar_ref)
    book = book_ref[...]
    column = acc_ref[128:129]
    moment = acc_ref[64:128] * (1.0 / precision)
    book_sum = acc_ref[0:64] * (1.0 / factor) + 2.0 * (column * book - moment)
    slope = jnp.sum(
        jnp.sum(book * book, axis=0, keepdims=True) * column, axis=1, keepdims=True
    ) - 2.0 * jnp.sum(jnp.sum(book * moment, axis=0, keepdims=True), axis=1, keepdims=True)
    slope = slope + acc_ref[208:209, 0:1] / (-0.5 * precision)
    usage = jnp.sum(acc_ref[136:144] + usage_ref[...], axis=0, keepdims=True)
    dim = book_ref.shape[0]
    eye = lax.broadcasted_iota(jnp.int32, (dim, dim), 0) == lax.broadcasted_iota(
        jnp.int32, (dim, dim), 1
    )
    bias = acc_ref[144:208, width : width + dim]
    bias = jnp.sum(jnp.where(eye, bias, 0.0), axis=0, keepdims=True)
    rest = codes + width
    sum_scr[:, 0:codes] = book_sum
    sum_scr[:, codes:rest] = acc_ref[144:208, 0:width]
    sum_scr[:, rest : rest + 128] = jnp.broadcast_to(slope, (64, 128))
    rows = codes // 128
    for i in range(rows):
        sum_scr[i : i + 1, rest : rest + 128] = usage[:, i * 128 : (i + 1) * 128]
    sum_scr[rows : rows + 1, rest : rest + dim] = bias
    for i in range(devices):
        shards[i][...] = sum_scr[shard_at(partner(me, i, devices), devices)]


def own_kernel(*refs):
    feat_ref, noise_ref, cot_ref = refs[1:4]
    params = refs[4:8]
    acc_in = refs[8]
    code_ref, grad_ref, acc_ref = refs[10:13]
    scr = refs[13:]

    @pl.when(pl.program_id(0) == 0)
    def _():
        prepare(params, *scr[0:3])
        acc_ref[...] = acc_in[...]

    grad_ref[...] = both_ways(
        params, scr, feat_ref[...], cot_ref[...], noise_ref, code_ref, acc_ref
    )


def run_own(count, table, feat, noise, cot, params, acc, grad):
    dim, codes = params[2].shape
    images, strip, width = feat.shape
    share = images // count

    def image(i, table_ref):
        return (table_ref[0, i], 0, 0)

    return pl.pallas_call(
        own_kernel,
        grid_spec=pltpu.PrefetchScalarGridSpec(
            num_scalar_prefetch=1,
            grid=(share,),
            in_specs=[
                pl.BlockSpec((None, strip, width), image),
                pl.BlockSpec((None, strip, codes), image),
                pl.BlockSpec((None, dim, strip), image),
                fixed(params[0].shape),
                fixed(params[1].shape),
                fixed(params[2].shape),
                fixed(params[3].shape),
                fixed(acc.shape),
                HBM,
            ],
            out_specs=[
                pl.BlockSpec(
                    (None, strip, codes),
                    lambda i, table_ref: (i, table_ref[0, count * share], 0),
                ),
                pl.BlockSpec((None, strip, width), image),
                fixed(acc.shape),
            ],
            scratch_shapes=tile_scratch(strip, dim, codes, width),
        ),
        out_shape=[
            pltpu.HBM((share, strip * count, codes), F32),
            pltpu.HBM(feat.shape, F32),
            pltpu.HBM(acc.shape, F32),
        ],
        input_output_aliases={8: 2, 9: 1},
        compiler_params=settings(),
        cost_estimate=cost(share * strip, width, dim, codes, 10),
        name="own_images",
    )(table, *in_hbm([feat, noise, cot, *params, acc, grad]))


def place_kernel(count, first, slots, steps, *refs):
    parts = refs[0 : len(steps)]
    out_ref, sem = refs[len(steps) + 1 : len(steps) + 3]
    strip = parts[0].shape[0] // slots
    me = lax.axis_index("space")
    copies = []
    for part, step in zip(parts, steps):
        row = pl.multiple_of(source(me, step, count) * strip, strip)
        for j in range(slots):
            copies.append(
                pltpu.make_async_copy(
                    part.at[pl.ds(j * strip, strip)],
                    out_ref.at[first + j, pl.ds(row, strip)],
                    sem.at[len(copies)],
                )
            )
    for copy in copies:
        copy.start()
    for copy in copies:
        copy.wait()


def place_wide(count, first, slots, steps, parts, whole):
    steps = list(steps)
    return pl.pallas_call(
        functools.partial(place_kernel, count, first, slots, steps),
        out_shape=pltpu.HBM(whole.shape, F32),
        in_specs=[VMEM] * len(steps) + [HBM],
        out_specs=HBM,
        scratch_shapes=[pltpu.SemaphoreType.DMA((len(steps) * slots,))],
        input_output_aliases={len(steps): 0},
        compiler_params=settings(VMEM_LIMIT // 2),
        cost_estimate=pl.CostEstimate(
            flops=0, bytes_accessed=2 * sum(p.size * 4 for p in parts), transcendentals=0
        ),
        name="place_wide",
    )(*[pltpu.with_memory_space_constraint(p, pltpu.VMEM) for p in parts], *in_hbm([whole]))


def join_kernel(count, *refs):
    parts = refs[0:count]
    outs = refs[count:]
    me = lax.axis_index("space")
    for step in range(count):
        here = source(me, step, count)
        base = 0
        for out in outs:
            for j in range(out.shape[0]):
                strip = out.shape[2]
                out[j, here] = parts[step][base : base + strip]
                base += strip


def join_small(count, parts, shapes):
    codes = parts[0].shape[1]
    return pl.pallas_call(
        functools.partial(join_kernel, count),
        out_shape=[
            jax.ShapeDtypeStruct((images // count, count, strip, codes), F32)
            for images, strip, _ in shapes
        ],
        compiler_params=settings(VMEM_LIMIT // 2),
        name="join_small",
    )(*parts)


def tree(values):
    while len(values) > 1:
        values = [
            values[i] + values[i + 1] if i + 1 < len(values) else values[i]
            for i in range(0, len(values), 2)
        ]
    return values[0]


def sum_kernel(*refs):
    refs[-1][...] = tree([ref[...] for ref in refs[:-1]])


def add_all(parts):
    return pl.pallas_call(
        sum_kernel,
        out_shape=jax.ShapeDtypeStruct(parts[0].shape, F32),
        compiler_params=settings(VMEM_LIMIT // 2),
        name="add_parts",
    )(*parts)


def final_kernel(devices, pixels, *refs):
    shards = refs[0:devices]
    weight_ref, bias_ref, book_ref, log_ref, usage_ref = refs[devices : devices + 5]
    weight_out, bias_out, book_out, log_out, usage_out = refs[devices + 5 : devices + 10]
    sum_scr = refs[devices + 10]
    me = lax.rem(lax.axis_index("dp"), devices)
    for i in range(devices):
        sum_scr[shard_at(source(me, i, devices), devices)] = shards[i][...]
    dim, codes = book_ref.shape
    width = weight_ref.shape[1]
    scale = 0.5 * lax.rsqrt(jnp.full((8, 128), pixels, F32))[0:1, 0:1]
    book_out[...] = 0.5 * book_ref[...] + scale * sum_scr[:, 0:codes]
    rest = codes + width
    weight_out[...] = 0.5 * weight_ref[...] + scale * sum_scr[:, codes:rest]
    rows = codes // 128
    bias_out[...] = 0.5 * bias_ref[...] + scale * sum_scr[rows : rows + 1, rest : rest + dim]
    usage = jnp.concatenate(
        [sum_scr[i : i + 1, rest : rest + 128] for i in range(rows)], axis=1
    )
    usage_out[...] = 0.5 * usage_ref[...] + 0.5 * (codes / pixels) * usage
    log_out[...] = 0.5 * log_ref[...] + scale * sum_scr[rows + 1 : rows + 2, rest : rest + 1]


def finish(devices, pixels, shards, weight, bias, book, log, usage):
    outs = (weight.T, bias.reshape(1, -1), book.T, log.reshape(1, 1), usage.reshape(1, -1))
    outs = pl.pallas_call(
        functools.partial(final_kernel, devices, pixels),
        out_shape=[jax.ShapeDtypeStruct(out.shape, F32) for out in outs],
        scratch_shapes=[pltpu.VMEM((64, LANES), F32)],
        compiler_params=settings(VMEM_LIMIT // 2),
        name="new_averages",
    )(*shards, *outs)
    return outs[0].T, outs[1].reshape(-1), outs[2].T, outs[3].reshape(-1), outs[4].reshape(-1)


def exchange(value, bit, size, pairs):
    while bit < size:
        value = value + pairs(value, bit)
        bit = 2 * bit
    return value


def spans(share):
    return [(0, 1), (1, share - 1)]


def per_device(
    feat_small,
    feat_mid,
    feat_wide,
    noise_small,
    noise_mid,
    noise_wide,
    cot_small,
    cot_mid,
    cot_wide,
    order_small,
    order_mid,
    order_wide,
    weight,
    bias,
    book,
    log,
    heat,
    weight_mean,
    bias_mean,
    book_mean,
    log_mean,
    usage_mean,
):
    count = lax.axis_size("space")
    devices = lax.axis_size("dp")
    params = (weight.T, bias.reshape(1, -1), book.T, log, heat)
    feats = (feat_small, feat_mid, feat_wide)
    pixels = sum(f.shape[0] * f.shape[1] for f in feats) * count * devices
    share = feat_wide.shape[0] // count
    cot_wide = jnp.swapaxes(cot_wide, 1, 2)

    def send(values):
        return [lax.ppermute(v, "space", route(i + 1, count)) for i, v in enumerate(values)]

    def follow(codes, before):
        before[0], codes[-1] = lax.optimization_barrier((before[0], codes[-1]))
        return send(codes)

    orders = (order_small, order_mid, order_wide)
    *small, table, usage, scalar = small_forward(
        count, orders, feats[0:2], (noise_small, noise_mid), params
    )
    params = (*params[0:3], scalar)
    arrived = [send(small[1:])]
    near = min(4, devices)
    early, late = spans(share)
    *early_codes, usage = wide_forward(
        count, *early, table, feat_wide, noise_wide, params, usage
    )
    arrived.append(follow(list(early_codes), arrived[0]))
    codes_small, codes_mid = join_small(
        count, [small[0]] + arrived[0], [f.shape for f in feats[0:2]]
    )
    codes_small, codes_mid, scalar = lax.optimization_barrier(
        (codes_small, codes_mid, scalar)
    )
    params = (*params[0:3], scalar)
    codes = []
    grad = acc = None
    for steps in (range(1, count - 1), range(count - 1, count)):
        *part, grad, acc = wide_both(
            count, steps, *late, table, feat_wide, noise_wide, cot_wide, params, acc, grad
        )
        codes.extend(part)
    arrived.append(follow(codes, arrived[1]))
    arrived[1], acc = lax.optimization_barrier((arrived[1], acc))
    whole, grad, acc = run_own(
        count, table, feat_wide, noise_wide, cot_wide, params, acc, grad
    )
    whole = place_wide(count, *early, range(1, count), arrived[1], whole)
    whole, acc = lax.optimization_barrier((whole, acc))
    grad, acc = wide_backward(
        count, *early, table, feat_wide, cot_wide, early_codes, params, acc, grad
    )
    grad_small, grad_mid, *shards = small_backward(
        count,
        near,
        feat_wide.shape[0],
        table,
        feats[0:2],
        (cot_small, cot_mid),
        small,
        params,
        acc,
        usage,
    )
    group = [
        [(i, i - i % near + partner(i % near, step, near)) for i in range(devices)]
        for step in range(near)
    ]
    parts = [lax.ppermute(shards[i], "dp", group[i]) for i in range(1, near)]
    mine = add_all([shards[0]] + parts)

    def along(value, offset):
        return lax.ppermute(value, "dp", [(i, i ^ offset) for i in range(devices)])

    def across(value, offset):
        turn = near if devices > near else 0
        pairs = [
            (i * count + j, (i ^ turn) * count + (j ^ offset))
            for i in range(devices)
            for j in range(count)
        ]
        return lax.ppermute(value, ("dp", "space"), pairs)

    mine = exchange(mine, near, devices, along)
    mine = exchange(mine, 1, count, across)
    shards = [mine] + [lax.ppermute(mine, "dp", group[i]) for i in range(1, near)]
    updated = finish(
        near, pixels, shards, weight_mean, bias_mean, book_mean, log_mean, usage_mean
    )
    for step in range(1, count):
        whole = place_wide(count, *late, [step], [arrived[2][step - 1]], whole)
    codes = whole.shape[2]
    return (
        codes_small.reshape(codes_small.shape[0], -1, codes),
        codes_mid.reshape(codes_mid.shape[0], -1, codes),
        whole,
        grad_small,
        grad_mid,
        grad,
        *updated,
    )


def solution(mesh):
    strips = P("dp", "space", None)
    placed = (strips,) * 9 + (P("dp", None),) * 3 + (P(),) * 10
    return jax.shard_map(
        per_device,
        mesh=mesh,
        in_specs=placed,
        out_specs=(P(("dp", "space"), None, None),) * 3 + (strips,) * 3 + (P(),) * 5,
        check_vma=False,
    )
```

```python
import functools

import jax
import jax.numpy as jnp
from jax import lax
from jax.experimental import pallas as pl
from jax.experimental.pallas import tpu as pltpu
from jax.sharding import PartitionSpec as P

F32 = jnp.float32
BF16 = jnp.bfloat16
VMEM_LIMIT = 16 * 1024 * 1024
ACC_ROWS = 64 + 64 + 8 + 8 + 64 + 8
LANES = 896


def partner(index, step, count):
    if count & (count - 1) == 0:
        return index ^ step
    return lax.rem(index + step, count)


def route(step, count):
    if count & (count - 1) == 0:
        return [(i, i ^ step) for i in range(count)]
    return [(i, (i + step) % count) for i in range(count)]


def source(index, step, count):
    if count & (count - 1) == 0:
        return index ^ step
    return lax.rem(index + (count - step), count)


def in_hbm(arrays):
    return [pltpu.with_memory_space_constraint(a, pltpu.HBM) for a in arrays]


def halves(x):
    high = x.astype(BF16)
    return high, (x - high.astype(F32)).astype(BF16)


def dot(left, right, left_dim=1, right_dim=0):
    return lax.dot_general(
        left, right, (((left_dim,), (right_dim,)), ((), ())), preferred_element_type=F32
    )


def set_scalars(log_ref, heat_ref, out_ref):
    precision = jnp.exp(jnp.full((8, 128), log_ref[0], F32))
    heat = jnp.full((8, 128), heat_ref[0], F32)
    row = lax.broadcasted_iota(jnp.int32, (8, 128), 0)
    factor = -0.5 * precision / heat
    out_ref[...] = jnp.where(row == 0, precision, jnp.where(row == 1, 1.0 / heat, factor))


def scalars(ref):
    return ref[0:1, 0:1], ref[1:2, 0:1], ref[2:3, 0:1]


def prepare(refs, book_scr, books_scr, weight_scr):
    weight_ref, bias_ref, book_ref, scalar_ref = refs
    dim, codes = book_ref.shape
    precision, _, _ = scalars(scalar_ref)
    book = book_ref[...]
    high, low = halves(book)
    norm = -0.5 * precision * jnp.sum(book * book, axis=0, keepdims=True)
    n0 = norm.astype(BF16).astype(F32)
    n1 = (norm - n0).astype(BF16).astype(F32)
    n2 = norm - n0 - n1
    row = lax.broadcasted_iota(jnp.int32, (16, codes), 0)
    extra = jnp.where(
        row < 3,
        1.0,
        jnp.where(row == 3, n0, jnp.where(row == 4, n1, jnp.where(row == 5, n2, 0.0))),
    ).astype(BF16)
    book_scr[0:dim] = high
    book_scr[dim : 2 * dim] = low
    book_scr[2 * dim : 3 * dim] = high
    book_scr[3 * dim : 3 * dim + 16] = extra
    books_scr[0:dim] = high
    books_scr[dim : 2 * dim] = low
    books_scr[2 * dim : 2 * dim + 16] = jnp.ones((16, codes), BF16)
    high, low = halves(weight_ref[...])
    weight_scr[0:dim] = high
    weight_scr[dim : 2 * dim] = low
    weight_scr[2 * dim : 3 * dim] = high


def latents(refs, scr, feat):
    weight_ref, bias_ref, book_ref, scalar_ref = refs
    weight_scr = scr[2]
    dim = book_ref.shape[0]
    precision, _, _ = scalars(scalar_ref)
    eye = lax.broadcasted_iota(jnp.int32, (dim, dim), 0) == lax.broadcasted_iota(
        jnp.int32, (dim, dim), 1
    )
    bias = jnp.sum(jnp.where(eye, bias_ref[...], 0.0), axis=1, keepdims=True)
    fh, fl = halves(feat)
    both = weight_scr[0 : 2 * dim]
    z2 = dot(both, fh, 1, 1) + dot(both, fl, 1, 1)
    z = z2[0:dim] + z2[dim : 2 * dim] + bias
    square = -0.5 * precision * jnp.sum(z * z, axis=0, keepdims=True)
    return fh, fl, z, square


def logit_rows(zh, zl, square):
    rows = zh.shape[1]
    s0 = square.astype(BF16).astype(F32)
    s1 = (square - s0).astype(BF16).astype(F32)
    s2 = square - s0 - s1
    row = lax.broadcasted_iota(jnp.int32, (16, rows), 0)
    extra = jnp.where(
        row == 0,
        s0,
        jnp.where(row == 1, s1, jnp.where(row == 2, s2, jnp.where(row < 6, 1.0, 0.0))),
    ).astype(BF16)
    return jnp.concatenate([zh, zh, zl, extra], axis=0)


def cot_rows(ch, cl):
    return jnp.concatenate([ch, ch, cl, jnp.zeros((16, ch.shape[1]), BF16)], axis=0)


def over_rows(rows, body, carry):
    step = next(s for s in (32, 16, 8) if rows % s == 0)

    def at(i, carry):
        return body(pl.ds(pl.multiple_of(i * step, step), step), carry)

    return lax.fori_loop(0, rows // step, at, carry, unroll=True)


def folded(x):
    return jnp.sum(x.reshape(x.shape[0] // 8, 8, x.shape[1]), axis=0)


def probabilities(logits):
    top = jnp.max(logits, axis=1, keepdims=True)
    e = jnp.exp(logits - top)
    return e * (1.0 / jnp.sum(e, axis=1, keepdims=True))


def forward(refs, scr, feat, noise_ref, code_refs, usage_ref):
    weight_ref, bias_ref, book_ref, scalar_ref = refs
    book_scr, l_scr = scr[0], scr[3]
    rows = feat.shape[0]
    precision, cold, _ = scalars(scalar_ref)
    _, _, z, square = latents(refs, scr, feat)
    zh, zl = halves(precision * z)
    l_scr[0:rows] = dot(logit_rows(zh, zl, square), book_scr[...], 0, 0)

    usage = usage_ref[...]
    part = rows // len(code_refs)
    for i, code_ref in enumerate(code_refs):
        logit_part = l_scr.at[pl.ds(i * part, part)]
        noise_part = noise_ref.at[pl.ds(i * part, part)]

        def body(at, usage, code_ref=code_ref, logit_part=logit_part, noise_part=noise_part):
            logits = logit_part[at]
            code_ref[at] = probabilities((logits + noise_part[at]) * cold)
            return usage + folded(probabilities(logits))

        usage = over_rows(part, body, usage)
    usage_ref[...] = usage


def gradients(refs, scr, fh, fl, z, square, zh, zl, ch, cl, acc_ref):
    books_scr, weight_scr = scr[1:3]
    wh_scr, wl_scr, gh_scr, gl_scr = scr[5:9]
    rows, feats = fh.shape
    dim, codes = refs[2].shape
    wh, wl = wh_scr[0:rows], wl_scr[0:rows]
    gh, gl = gh_scr[0:rows], gl_scr[0:rows]
    p = dot(jnp.concatenate([ch, cl], axis=0), wh)
    acc_ref[0:64] += p[0:dim] + p[dim : 2 * dim] + dot(ch, wl)
    left = jnp.concatenate([zh, zl, jnp.ones((16, rows), BF16)], axis=0)
    p = dot(left, gh) + dot(left, gl)
    acc_ref[64:128] += p[0:dim] + p[dim : 2 * dim]
    acc_ref[128:136] += p[2 * dim : 2 * dim + 8]
    p = dot(books_scr[...], gh, 1, 1) + dot(books_scr[...], gl, 1, 1)
    row_d = p[2 * dim : 2 * dim + 1]
    gz = 2.0 * (row_d * z - (p[0:dim] + p[dim : 2 * dim]))
    zh, zl = halves(gz)
    p = dot(jnp.concatenate([zh, zl], axis=0), fh)
    acc_ref[144:208, 0:feats] += p[0:dim] + p[dim : 2 * dim] + dot(zh, fl)
    acc_ref[144:208, feats : feats + 128] += jnp.broadcast_to(
        jnp.sum(gz, axis=1, keepdims=True), (dim, 128)
    )
    total = jnp.sum(square * row_d, axis=1, keepdims=True)
    acc_ref[208:216] += jnp.broadcast_to(total, (8, codes))
    return dot(jnp.concatenate([zh, zh, zl], axis=0), weight_scr[...], 0, 0)


def backward(refs, scr, feat, cot, code_ref, acc_ref):
    weight_ref, bias_ref, book_ref, scalar_ref = refs
    book_scr, _, _, _, g_scr, wh_scr, wl_scr, gh_scr, gl_scr = scr
    rows = feat.shape[0]
    precision, _, factor = scalars(scalar_ref)
    fh, fl, z, square = latents(refs, scr, feat)
    zh, zl = halves(precision * z)
    ch, cl = halves(factor * cot)
    g_scr[0:rows] = dot(cot_rows(ch, cl), book_scr[...], 0, 0)

    def body(at, carry):
        w = code_ref[at]
        gw = g_scr[at]
        gd = w * (gw - jnp.sum(w * gw, axis=1, keepdims=True))
        wh_scr[at], wl_scr[at] = halves(w)
        gh_scr[at], gl_scr[at] = halves(gd)
        return carry

    over_rows(rows, body, 0)
    return gradients(refs, scr, fh, fl, z, square, zh, zl, ch, cl, acc_ref)


def both_ways(refs, scr, feat, cot, noise_ref, code_ref, acc_ref):
    weight_ref, bias_ref, book_ref, scalar_ref = refs
    book_scr, _, _, l_scr, g_scr, wh_scr, wl_scr, gh_scr, gl_scr = scr
    rows = feat.shape[0]
    precision, cold, factor = scalars(scalar_ref)
    fh, fl, z, square = latents(refs, scr, feat)
    zh, zl = halves(precision * z)
    ch, cl = halves(factor * cot)
    left = jnp.concatenate([logit_rows(zh, zl, square), cot_rows(ch, cl)], axis=1)
    p = dot(left, book_scr[...], 0, 0)
    l_scr[0:rows] = p[0:rows]
    g_scr[0:rows] = p[rows : 2 * rows]

    def body(at, usage):
        logits = l_scr[at]
        s = (logits + noise_ref[at]) * cold
        e = jnp.exp(s - jnp.max(s, axis=1, keepdims=True))
        gw = g_scr[at]
        scale = 1.0 / jnp.sum(e, axis=1, keepdims=True)
        inner = jnp.sum(e * gw, axis=1, keepdims=True) * scale
        w = e * scale
        code_ref[at] = w
        gd = w * (gw - inner)
        wh_scr[at], wl_scr[at] = halves(w)
        gh_scr[at], gl_scr[at] = halves(gd)
        return usage + folded(probabilities(logits))

    acc_ref[136:144] = over_rows(rows, body, acc_ref[136:144])
    return gradients(refs, scr, fh, fl, z, square, zh, zl, ch, cl, acc_ref)


def tile_scratch(rows, dim, codes, feats):
    return [
        pltpu.VMEM((3 * dim + 16, codes), BF16),
        pltpu.VMEM((2 * dim + 16, codes), BF16),
        pltpu.VMEM((3 * dim, feats), BF16),
        pltpu.VMEM((rows, codes), F32),
        pltpu.VMEM((rows, codes), F32),
        pltpu.VMEM((rows, codes), BF16),
        pltpu.VMEM((rows, codes), BF16),
        pltpu.VMEM((rows, codes), BF16),
        pltpu.VMEM((rows, codes), BF16),
    ]


def settings(limit=VMEM_LIMIT):
    return pltpu.CompilerParams(vmem_limit_bytes=limit)


def cost(rows, feats, dim, codes, tenths):
    return pl.CostEstimate(
        flops=rows * 24 * tenths * (5 * dim * codes + 3 * dim * feats) // 10,
        bytes_accessed=4 * rows * (2 * feats + 2 * codes + dim),
        transcendentals=2 * rows * codes,
    )


SMEM = pl.BlockSpec(memory_space=pltpu.SMEM)
VMEM = pl.BlockSpec(memory_space=pltpu.VMEM)
HBM = pl.BlockSpec(memory_space=pltpu.HBM)


def fixed(shape):
    return pl.BlockSpec(shape, lambda *_: (0,) * len(shape))


def part_rows(peer, slots, shape):
    return pl.BlockSpec(shape, lambda i, _: (jnp.clip(i - peer * slots, 0, slots - 1), 0))


def places_of(table_ref, wide, shapes, groups, count):
    places = []
    base = 0
    entry = wide + 1
    for _ in range(count):
        for size in range(2):
            strip = shapes[size][1]
            for _ in range(groups[size]):
                places.append((size, table_ref[0, entry], base, strip))
                base += strip
                entry += 1
    return places, base


def small_forward_kernel(count, groups, *refs):
    sources = refs[0:10]
    log_ref, heat_ref = refs[10:12]
    sends = refs[12 : 12 + count]
    table_ref, usage_ref, scalar_ref = refs[12 + count : 15 + count]
    held = refs[15 + count : 25 + count]
    sems, feat_scr, noise_scr = refs[25 + count : 28 + count]
    scr = refs[28 + count :]
    copies = [
        pltpu.make_async_copy(there, here, sems.at[i])
        for i, (there, here) in enumerate(zip(sources, held))
    ]
    for copy in copies:
        copy.start()
    orders, feats, noises, params = held[0:3], held[3:5], held[5:7], (*held[7:10], scalar_ref)
    me = lax.axis_index("space")
    set_scalars(log_ref, heat_ref, scalar_ref)
    for copy in copies[7:10]:
        copy.wait()
    prepare(params, *scr[0:3])
    for copy in copies[0:5]:
        copy.wait()
    wide = orders[2].shape[1]
    share = wide // count
    entry = wide + 1
    table_ref[0, wide] = me
    for step in range(count):
        there = partner(me, step, count)
        for j in range(share):
            table_ref[0, step * share + j] = orders[2][0, there * share + j]
        for size in range(2):
            for j in range(groups[size]):
                table_ref[0, entry] = orders[size][0, there * groups[size] + j]
                entry += 1
    places, _ = places_of(table_ref, wide, [f.shape for f in feats], groups, count)
    for size, image, at, strip in places:
        feat_scr[at : at + strip] = feats[size][image]
    for copy in copies[5:7]:
        copy.wait()
    for size, image, at, strip in places:
        noise_scr[at : at + strip] = noises[size][image]
    usage_ref[...] = jnp.zeros(usage_ref.shape, F32)
    forward(params, scr, feat_scr[...], noise_scr, sends, usage_ref)


def small_forward(count, orders, feats, noises, params):
    dim, codes = params[2].shape
    width = feats[0].shape[2]
    groups = tuple(f.shape[0] // count for f in feats)
    part = sum(g * f.shape[1] for g, f in zip(groups, feats))
    rows = part * count
    arrays = [*orders, *feats, *noises, *params[0:3]]
    return pl.pallas_call(
        functools.partial(small_forward_kernel, count, groups),
        out_shape=[jax.ShapeDtypeStruct((part, codes), F32)] * count
        + [
            jax.ShapeDtypeStruct((1, sum(o.shape[1] for o in orders) + 1), jnp.int32),
            pltpu.HBM((8, codes), F32),
            pltpu.HBM((8, 128), F32),
        ],
        in_specs=[HBM] * 10 + [SMEM] * 2,
        out_specs=[VMEM] * count + [SMEM, VMEM, VMEM],
        scratch_shapes=[
            (pltpu.SMEM if i < 3 else pltpu.VMEM)(a.shape, a.dtype)
            for i, a in enumerate(arrays)
        ]
        + [
            pltpu.SemaphoreType.DMA((10,)),
            pltpu.VMEM((rows, width), F32),
            pltpu.VMEM((rows, codes), F32),
        ]
        + tile_scratch(rows, dim, codes, width),
        compiler_params=settings(),
        cost_estimate=cost(rows, width, dim, codes, 4),
        name="small_forward",
    )(*in_hbm(arrays), *params[3:5])


def small_backward_kernel(count, devices, wide, groups, *refs):
    table_ref = refs[0]
    feats, cots = refs[1:3], refs[3:5]
    parts = refs[5 : 5 + count]
    params = refs[5 + count : 9 + count]
    acc_in, usage_ref = refs[9 + count : 11 + count]
    grads = refs[11 + count : 13 + count]
    shards = refs[13 + count : 13 + count + devices]
    rest = refs[13 + count + devices :]
    acc_ref, sum_scr, feat_scr, cot_scr, code_scr = rest[0:5]
    scr = rest[5:]
    places, base = places_of(table_ref, wide, [f.shape for f in feats], groups, count)
    for size, image, at, strip in places:
        feat_scr[at : at + strip] = feats[size][image]
        cot_scr[at : at + strip] = cots[size][image]
    part = base // count
    for step in range(count):
        code_scr[step * part : (step + 1) * part] = parts[step][...]
    prepare(params, *scr[0:3])
    acc_ref[...] = acc_in[...]
    feat_scr[...] = backward(params, scr, feat_scr[...], cot_scr[...].T, code_scr, acc_ref)
    lay_out(params, acc_ref, usage_ref, sum_scr, shards)
    for size, image, at, strip in places:
        grads[size][image] = feat_scr[at : at + strip]


def small_backward(count, devices, wide, table, feats, cots, parts, params, acc, usage):
    dim, codes = params[2].shape
    width = feats[0].shape[2]
    groups = tuple(f.shape[0] // count for f in feats)
    rows = parts[0].shape[0] * count
    return pl.pallas_call(
        functools.partial(small_backward_kernel, count, devices, wide, groups),
        out_shape=[pltpu.HBM(f.shape, F32) for f in feats]
        + [jax.ShapeDtypeStruct((64 // devices, LANES), F32)] * devices,
        in_specs=[SMEM] + [VMEM] * (10 + count),
        out_specs=[VMEM] * (2 + devices),
        scratch_shapes=[
            pltpu.VMEM(acc.shape, F32),
            pltpu.VMEM((64, LANES), F32),
            pltpu.VMEM((rows, width), F32),
            pltpu.VMEM((rows, dim), F32),
            pltpu.VMEM((rows, codes), F32),
        ]
        + tile_scratch(rows, dim, codes, width),
        compiler_params=settings(),
        cost_estimate=cost(rows, width, dim, codes, 6),
        name="small_backward",
    )(
        table,
        *in_hbm([*feats, *cots]),
        *parts,
        *in_hbm([*params, acc, usage]),
    )


def wide_forward_kernel(peers, slots, *refs):
    feat_ref, noise_ref = refs[1:3]
    params = refs[3:7]
    usage_in = refs[7]
    sends = refs[8 : 8 + peers]
    usage_ref, code_scr = refs[8 + peers : 10 + peers]
    scr = refs[10 + peers :]
    step = pl.program_id(0)

    @pl.when(step == 0)
    def _():
        prepare(params, *scr[0:3])
        usage_ref[...] = usage_in[...]

    forward(params, scr, feat_ref[...], noise_ref, [code_scr], usage_ref)
    for i in range(peers):

        @pl.when(lax.div(step, slots) == i)
        def _(i=i):
            sends[i][...] = code_scr[...]


def peer_image(start, share, first, slots):
    def image(i, table_ref):
        peer = lax.div(i, slots) + start
        return (table_ref[0, peer * share + first + lax.rem(i, slots)], 0, 0)

    return image


def wide_forward(count, steps, first, slots, table, feat, noise, params, usage, tenths):
    dim, codes = params[2].shape
    images, strip, width = feat.shape
    image = peer_image(steps[0], images // count, first, slots)
    peers = len(steps)
    return pl.pallas_call(
        functools.partial(wide_forward_kernel, peers, slots),
        grid_spec=pltpu.PrefetchScalarGridSpec(
            num_scalar_prefetch=1,
            grid=(peers * slots,),
            in_specs=[
                pl.BlockSpec((None, strip, width), image),
                pl.BlockSpec((None, strip, codes), image),
            ]
            + [fixed(p.shape) for p in params]
            + [fixed(usage.shape)],
            out_specs=[part_rows(i, slots, (strip, codes)) for i in range(peers)]
            + [fixed(usage.shape)],
            scratch_shapes=[pltpu.VMEM((strip, codes), F32)]
            + tile_scratch(strip, dim, codes, width),
        ),
        out_shape=[jax.ShapeDtypeStruct((strip * slots, codes), F32)] * peers
        + [pltpu.HBM(usage.shape, F32)],
        input_output_aliases={7: peers},
        compiler_params=settings(),
        cost_estimate=cost(peers * slots * strip, width, dim, codes, tenths),
        name="wide_forward",
    )(table, *in_hbm([feat, noise, *params, usage]))


def wide_both_kernel(peers, slots, new, *refs):
    feat_ref, noise_ref, cot_ref = refs[1:4]
    params = refs[4:8]
    rest = refs[8:]
    if not new:
        acc_in, rest = rest[0], rest[2:]
    sends = rest[0:peers]
    grad_ref, acc_ref, code_scr = rest[peers : 3 + peers]
    scr = rest[3 + peers :]
    step = pl.program_id(0)

    @pl.when(step == 0)
    def _():
        prepare(params, *scr[0:3])
        acc_ref[...] = jnp.zeros(acc_ref.shape, F32) if new else acc_in[...]

    grad_ref[...] = both_ways(
        params, scr, feat_ref[...], cot_ref[...], noise_ref, code_scr, acc_ref
    )
    for i in range(peers):

        @pl.when(lax.div(step, slots) == i)
        def _(i=i):
            sends[i][...] = code_scr[...]


def wide_both(count, steps, first, slots, table, feat, noise, cot, params, acc, grad):
    dim, codes = params[2].shape
    images, strip, width = feat.shape
    image = peer_image(steps[0], images // count, first, slots)
    acc_shape = (ACC_ROWS, codes)
    peers = len(steps)
    new = acc is None
    return pl.pallas_call(
        functools.partial(wide_both_kernel, peers, slots, new),
        grid_spec=pltpu.PrefetchScalarGridSpec(
            num_scalar_prefetch=1,
            grid=(peers * slots,),
            in_specs=[
                pl.BlockSpec((None, strip, width), image),
                pl.BlockSpec((None, strip, codes), image),
                pl.BlockSpec((None, dim, strip), image),
            ]
            + [fixed(p.shape) for p in params]
            + ([] if new else [fixed(acc_shape), HBM]),
            out_specs=[part_rows(i, slots, (strip, codes)) for i in range(peers)]
            + [pl.BlockSpec((None, strip, width), image), fixed(acc_shape)],
            scratch_shapes=[pltpu.VMEM((strip, codes), F32)]
            + tile_scratch(strip, dim, codes, width),
        ),
        out_shape=[jax.ShapeDtypeStruct((strip * slots, codes), F32)] * peers
        + [pltpu.HBM(feat.shape, F32), pltpu.HBM(acc_shape, F32)],
        input_output_aliases={} if new else {8: peers + 1, 9: peers},
        compiler_params=settings(),
        cost_estimate=cost(peers * slots * strip, width, dim, codes, 10),
        name="wide_both",
    )(table, *in_hbm([feat, noise, cot, *params] + ([] if new else [acc, grad])))


def wide_backward_kernel(bounds, *refs):
    feat_ref, cot_ref = refs[1:3]
    count = len(bounds) - 1
    parts = refs[3 : 3 + count]
    params = refs[3 + count : 7 + count]
    acc_in = refs[7 + count]
    grad_ref, acc_ref, code_scr = refs[9 + count : 12 + count]
    scr = refs[12 + count :]
    step = pl.program_id(0)

    @pl.when(step == 0)
    def _():
        prepare(params, *scr[0:3])
        acc_ref[...] = acc_in[...]

    for i in range(count):

        @pl.when((step >= bounds[i]) & (step < bounds[i + 1]))
        def _(i=i):
            code_scr[...] = parts[i][...]

    grad_ref[...] = backward(params, scr, feat_ref[...], cot_ref[...], code_scr, acc_ref)


def wide_backward(count, pieces, table, feat, cot, params, acc, grad):
    dim, codes = params[2].shape
    images, strip, width = feat.shape
    share = images // count
    bounds = [0]
    for _, _, _, slots in pieces:
        bounds.append(bounds[-1] + slots)

    def image(i, table_ref):
        entry = 0
        for (_, step, first, _), start in zip(pieces, bounds):
            entry = jnp.where(i >= start, step * share + first + i - start, entry)
        return (table_ref[0, entry], 0, 0)

    def part(k):
        start, slots = bounds[k], pieces[k][3]
        return pl.BlockSpec(
            (strip, codes), lambda i, _: (jnp.clip(i - start, 0, slots - 1), 0)
        )

    n = len(pieces)
    return pl.pallas_call(
        functools.partial(wide_backward_kernel, bounds),
        grid_spec=pltpu.PrefetchScalarGridSpec(
            num_scalar_prefetch=1,
            grid=(bounds[-1],),
            in_specs=[
                pl.BlockSpec((None, strip, width), image),
                pl.BlockSpec((None, dim, strip), image),
            ]
            + [part(k) for k in range(n)]
            + [fixed(p.shape) for p in params]
            + [fixed(acc.shape), HBM],
            out_specs=[pl.BlockSpec((None, strip, width), image), fixed(acc.shape)],
            scratch_shapes=[pltpu.VMEM((strip, codes), F32)]
            + tile_scratch(strip, dim, codes, width),
        ),
        out_shape=[pltpu.HBM(feat.shape, F32), pltpu.HBM(acc.shape, F32)],
        input_output_aliases={7 + n: 1, 8 + n: 0},
        compiler_params=settings(),
        cost_estimate=cost(bounds[-1] * strip, width, dim, codes, 6),
        name="wide_backward",
    )(
        table,
        *in_hbm([feat, cot]),
        *[piece[0] for piece in pieces],
        *in_hbm([*params, acc, grad]),
    )


def shard_at(index, parts):
    height = 64 // parts
    return pl.ds(pl.multiple_of(index * height, height), height)


def lay_out(params, acc_ref, usage_ref, sum_scr, shards):
    weight_ref, bias_ref, book_ref, scalar_ref = params
    codes = book_ref.shape[1]
    width = weight_ref.shape[1]
    devices = len(shards)
    me = lax.rem(lax.axis_index("dp"), devices)
    precision, _, factor = scalars(scalar_ref)
    book = book_ref[...]
    column = acc_ref[128:129]
    moment = acc_ref[64:128] * (1.0 / precision)
    book_sum = acc_ref[0:64] * (1.0 / factor) + 2.0 * (column * book - moment)
    slope = jnp.sum(
        jnp.sum(book * book, axis=0, keepdims=True) * column, axis=1, keepdims=True
    ) - 2.0 * jnp.sum(jnp.sum(book * moment, axis=0, keepdims=True), axis=1, keepdims=True)
    slope = slope + acc_ref[208:209, 0:1] / (-0.5 * precision)
    usage = jnp.sum(acc_ref[136:144] + usage_ref[...], axis=0, keepdims=True)
    dim = book_ref.shape[0]
    eye = lax.broadcasted_iota(jnp.int32, (dim, dim), 0) == lax.broadcasted_iota(
        jnp.int32, (dim, dim), 1
    )
    bias = acc_ref[144:208, width : width + dim]
    bias = jnp.sum(jnp.where(eye, bias, 0.0), axis=0, keepdims=True)
    rest = codes + width
    sum_scr[:, 0:codes] = book_sum
    sum_scr[:, codes:rest] = acc_ref[144:208, 0:width]
    sum_scr[:, rest : rest + 128] = jnp.broadcast_to(slope, (64, 128))
    rows = codes // 128
    for i in range(rows):
        sum_scr[i : i + 1, rest : rest + 128] = usage[:, i * 128 : (i + 1) * 128]
    sum_scr[rows : rows + 1, rest : rest + dim] = bias
    for i in range(devices):
        shards[i][...] = sum_scr[shard_at(partner(me, i, devices), devices)]


def own_kernel(*refs):
    feat_ref, noise_ref, cot_ref = refs[1:4]
    params = refs[4:8]
    acc_in = refs[8]
    code_ref, grad_ref, acc_ref = refs[10:13]
    scr = refs[13:]

    @pl.when(pl.program_id(0) == 0)
    def _():
        prepare(params, *scr[0:3])
        acc_ref[...] = acc_in[...]

    grad_ref[...] = both_ways(
        params, scr, feat_ref[...], cot_ref[...], noise_ref, code_ref, acc_ref
    )


def run_own(count, table, feat, noise, cot, params, acc, grad):
    dim, codes = params[2].shape
    images, strip, width = feat.shape
    share = images // count

    def image(i, table_ref):
        return (table_ref[0, i], 0, 0)

    return pl.pallas_call(
        own_kernel,
        grid_spec=pltpu.PrefetchScalarGridSpec(
            num_scalar_prefetch=1,
            grid=(share,),
            in_specs=[
                pl.BlockSpec((None, strip, width), image),
                pl.BlockSpec((None, strip, codes), image),
                pl.BlockSpec((None, dim, strip), image),
                fixed(params[0].shape),
                fixed(params[1].shape),
                fixed(params[2].shape),
                fixed(params[3].shape),
                fixed(acc.shape),
                HBM,
            ],
            out_specs=[
                pl.BlockSpec(
                    (None, strip, codes),
                    lambda i, table_ref: (i, table_ref[0, count * share], 0),
                ),
                pl.BlockSpec((None, strip, width), image),
                fixed(acc.shape),
            ],
            scratch_shapes=tile_scratch(strip, dim, codes, width),
        ),
        out_shape=[
            pltpu.HBM((share, strip * count, codes), F32),
            pltpu.HBM(feat.shape, F32),
            pltpu.HBM(acc.shape, F32),
        ],
        input_output_aliases={8: 2, 9: 1},
        compiler_params=settings(),
        cost_estimate=cost(share * strip, width, dim, codes, 10),
        name="own_images",
    )(table, *in_hbm([feat, noise, cot, *params, acc, grad]))


def place_kernel(count, first, slots, steps, *refs):
    parts = refs[0 : len(steps)]
    out_ref, sem = refs[len(steps) + 1 : len(steps) + 3]
    strip = parts[0].shape[0] // slots
    me = lax.axis_index("space")
    copies = []
    for part, step in zip(parts, steps):
        row = pl.multiple_of(source(me, step, count) * strip, strip)
        for j in range(slots):
            copies.append(
                pltpu.make_async_copy(
                    part.at[pl.ds(j * strip, strip)],
                    out_ref.at[first + j, pl.ds(row, strip)],
                    sem.at[len(copies)],
                )
            )
    for copy in copies:
        copy.start()
    for copy in copies:
        copy.wait()


def place_wide(count, first, slots, steps, parts, whole):
    steps = list(steps)
    return pl.pallas_call(
        functools.partial(place_kernel, count, first, slots, steps),
        out_shape=pltpu.HBM(whole.shape, F32),
        in_specs=[VMEM] * len(steps) + [HBM],
        out_specs=HBM,
        scratch_shapes=[pltpu.SemaphoreType.DMA((len(steps) * slots,))],
        input_output_aliases={len(steps): 0},
        compiler_params=settings(VMEM_LIMIT // 2),
        cost_estimate=pl.CostEstimate(
            flops=0, bytes_accessed=2 * sum(p.size * 4 for p in parts), transcendentals=0
        ),
        name="place_wide",
    )(*[pltpu.with_memory_space_constraint(p, pltpu.VMEM) for p in parts], *in_hbm([whole]))


def join_kernel(count, *refs):
    parts = refs[0:count]
    outs = refs[count:]
    me = lax.axis_index("space")
    for step in range(count):
        here = source(me, step, count)
        base = 0
        for out in outs:
            for j in range(out.shape[0]):
                strip = out.shape[2]
                out[j, here] = parts[step][base : base + strip]
                base += strip


def join_small(count, parts, shapes):
    codes = parts[0].shape[1]
    return pl.pallas_call(
        functools.partial(join_kernel, count),
        out_shape=[
            jax.ShapeDtypeStruct((images // count, count, strip, codes), F32)
            for images, strip, _ in shapes
        ],
        compiler_params=settings(VMEM_LIMIT // 2),
        name="join_small",
    )(*parts)


def tree(values):
    while len(values) > 1:
        values = [
            values[i] + values[i + 1] if i + 1 < len(values) else values[i]
            for i in range(0, len(values), 2)
        ]
    return values[0]


def sum_kernel(*refs):
    refs[-1][...] = tree([ref[...] for ref in refs[:-1]])


def add_all(parts):
    return pl.pallas_call(
        sum_kernel,
        out_shape=jax.ShapeDtypeStruct(parts[0].shape, F32),
        compiler_params=settings(VMEM_LIMIT // 2),
        name="add_parts",
    )(*parts)


def final_kernel(devices, pixels, *refs):
    shards = refs[0:devices]
    weight_ref, bias_ref, book_ref, log_ref, usage_ref = refs[devices : devices + 5]
    weight_out, bias_out, book_out, log_out, usage_out = refs[devices + 5 : devices + 10]
    sum_scr = refs[devices + 10]
    me = lax.rem(lax.axis_index("dp"), devices)
    for i in range(devices):
        sum_scr[shard_at(source(me, i, devices), devices)] = shards[i][...]
    dim, codes = book_ref.shape
    width = weight_ref.shape[1]
    scale = 0.5 * lax.rsqrt(jnp.full((8, 128), pixels, F32))[0:1, 0:1]
    book_out[...] = 0.5 * book_ref[...] + scale * sum_scr[:, 0:codes]
    rest = codes + width
    weight_out[...] = 0.5 * weight_ref[...] + scale * sum_scr[:, codes:rest]
    rows = codes // 128
    bias_out[...] = 0.5 * bias_ref[...] + scale * sum_scr[rows : rows + 1, rest : rest + dim]
    usage = jnp.concatenate(
        [sum_scr[i : i + 1, rest : rest + 128] for i in range(rows)], axis=1
    )
    usage_out[...] = 0.5 * usage_ref[...] + 0.5 * (codes / pixels) * usage
    log_out[...] = 0.5 * log_ref[...] + scale * sum_scr[rows + 1 : rows + 2, rest : rest + 1]


def finish(devices, pixels, shards, weight, bias, book, log, usage):
    outs = (weight.T, bias.reshape(1, -1), book.T, log.reshape(1, 1), usage.reshape(1, -1))
    outs = pl.pallas_call(
        functools.partial(final_kernel, devices, pixels),
        out_shape=[jax.ShapeDtypeStruct(out.shape, F32) for out in outs],
        scratch_shapes=[pltpu.VMEM((64, LANES), F32)],
        compiler_params=settings(VMEM_LIMIT // 2),
        name="new_averages",
    )(*shards, *outs)
    return outs[0].T, outs[1].reshape(-1), outs[2].T, outs[3].reshape(-1), outs[4].reshape(-1)


def exchange(value, bit, size, pairs):
    while bit < size:
        value = value + pairs(value, bit)
        bit = 2 * bit
    return value


def spans(share):
    return [(0, 1), (1, share - 1)]


def per_device(
    feat_small,
    feat_mid,
    feat_wide,
    noise_small,
    noise_mid,
    noise_wide,
    cot_small,
    cot_mid,
    cot_wide,
    order_small,
    order_mid,
    order_wide,
    weight,
    bias,
    book,
    log,
    heat,
    weight_mean,
    bias_mean,
    book_mean,
    log_mean,
    usage_mean,
):
    count = lax.axis_size("space")
    devices = lax.axis_size("dp")
    params = (weight.T, bias.reshape(1, -1), book.T, log, heat)
    feats = (feat_small, feat_mid, feat_wide)
    pixels = sum(f.shape[0] * f.shape[1] for f in feats) * count * devices
    share = feat_wide.shape[0] // count
    cot_wide = jnp.swapaxes(cot_wide, 1, 2)

    def send(values):
        return [lax.ppermute(v, "space", route(i + 1, count)) for i, v in enumerate(values)]

    def follow(codes, before):
        before[-1], codes[-1] = lax.optimization_barrier((before[-1], codes[-1]))
        return send(codes)

    orders = (order_small, order_mid, order_wide)
    *small, table, usage, scalar = small_forward(
        count, orders, feats[0:2], (noise_small, noise_mid), params
    )
    params = (*params[0:3], scalar)
    arrived = [send(small[1:])]
    near = min(4, devices)
    early, late = spans(share)
    direct, last = range(1, count - 1), range(count - 1, count)
    *early_codes, usage = wide_forward(
        count, range(1, count), *early, table, feat_wide, noise_wide, params, usage, 4
    )
    arrived.append(follow(list(early_codes), arrived[0]))
    *codes, grad, acc = wide_both(
        count, direct, *late, table, feat_wide, noise_wide, cot_wide, params, None, None
    )
    codes_small, codes_mid = join_small(
        count, [small[0]] + arrived[0], [f.shape for f in feats[0:2]]
    )
    codes_small, codes_mid, usage = lax.optimization_barrier(
        (codes_small, codes_mid, usage)
    )
    last_codes, usage = wide_forward(
        count, last, *late, table, feat_wide, noise_wide, params, usage, 1
    )
    arrived.append(follow([*codes, last_codes], arrived[1]))
    arrived[1], acc = lax.optimization_barrier((arrived[1], acc))
    whole, grad, acc = run_own(
        count, table, feat_wide, noise_wide, cot_wide, params, acc, grad
    )
    whole = place_wide(count, *early, range(1, count), arrived[1], whole)
    whole, acc = lax.optimization_barrier((whole, acc))
    pieces = [(part, i + 1, *early) for i, part in enumerate(early_codes)]
    pieces.append((last_codes, count - 1, *late))
    grad, acc = wide_backward(
        count, pieces, table, feat_wide, cot_wide, params, acc, grad
    )
    grad_small, grad_mid, *shards = small_backward(
        count,
        near,
        feat_wide.shape[0],
        table,
        feats[0:2],
        (cot_small, cot_mid),
        small,
        params,
        acc,
        usage,
    )
    group = [
        [(i, i - i % near + partner(i % near, step, near)) for i in range(devices)]
        for step in range(near)
    ]
    parts = [lax.ppermute(shards[i], "dp", group[i]) for i in range(1, near)]
    mine = add_all([shards[0]] + parts)

    def along(value, offset):
        return lax.ppermute(value, "dp", [(i, i ^ offset) for i in range(devices)])

    def across(value, offset):
        turn = near if devices > near else 0
        pairs = [
            (i * count + j, (i ^ turn) * count + (j ^ offset))
            for i in range(devices)
            for j in range(count)
        ]
        return lax.ppermute(value, ("dp", "space"), pairs)

    mine = exchange(mine, near, devices, along)
    mine = exchange(mine, 1, count, across)
    shards = [mine] + [lax.ppermute(mine, "dp", group[i]) for i in range(1, near)]
    updated = finish(
        near, pixels, shards, weight_mean, bias_mean, book_mean, log_mean, usage_mean
    )
    for step in range(1, count):
        whole = place_wide(count, *late, [step], [arrived[2][step - 1]], whole)
    codes = whole.shape[2]
    return (
        codes_small.reshape(codes_small.shape[0], -1, codes),
        codes_mid.reshape(codes_mid.shape[0], -1, codes),
        whole,
        grad_small,
        grad_mid,
        grad,
        *updated,
    )


def solution(mesh):
    strips = P("dp", "space", None)
    placed = (strips,) * 9 + (P("dp", None),) * 3 + (P(),) * 10
    return jax.shard_map(
        per_device,
        mesh=mesh,
        in_specs=placed,
        out_specs=(P(("dp", "space"), None, None),) * 3 + (strips,) * 3 + (P(),) * 5,
        check_vma=False,
    )
```

```python
import functools

import jax
import jax.numpy as jnp
from jax import lax
from jax.experimental import pallas as pl
from jax.experimental.pallas import tpu as pltpu
from jax.sharding import PartitionSpec as P

F32 = jnp.float32
BF16 = jnp.bfloat16
VMEM_LIMIT = 16 * 1024 * 1024
ACC_ROWS = 64 + 64 + 8 + 8 + 64 + 8
LANES = 896


def partner(index, step, count):
    if count & (count - 1) == 0:
        return index ^ step
    return lax.rem(index + step, count)


def route(step, count):
    if count & (count - 1) == 0:
        return [(i, i ^ step) for i in range(count)]
    return [(i, (i + step) % count) for i in range(count)]


def source(index, step, count):
    if count & (count - 1) == 0:
        return index ^ step
    return lax.rem(index + (count - step), count)


def in_hbm(arrays):
    return [pltpu.with_memory_space_constraint(a, pltpu.HBM) for a in arrays]


def halves(x):
    high = x.astype(BF16)
    return high, (x - high.astype(F32)).astype(BF16)


def dot(left, right, left_dim=1, right_dim=0):
    return lax.dot_general(
        left, right, (((left_dim,), (right_dim,)), ((), ())), preferred_element_type=F32
    )


def set_scalars(log_ref, heat_ref, out_ref):
    precision = jnp.exp(jnp.full((8, 128), log_ref[0], F32))
    heat = jnp.full((8, 128), heat_ref[0], F32)
    row = lax.broadcasted_iota(jnp.int32, (8, 128), 0)
    factor = -0.5 * precision / heat
    out_ref[...] = jnp.where(row == 0, precision, jnp.where(row == 1, 1.0 / heat, factor))


def scalars(ref):
    return ref[0:1, 0:1], ref[1:2, 0:1], ref[2:3, 0:1]


def prepare(refs, book_scr, books_scr, weight_scr):
    weight_ref, bias_ref, book_ref, scalar_ref = refs
    dim, codes = book_ref.shape
    precision, _, _ = scalars(scalar_ref)
    book = book_ref[...]
    high, low = halves(book)
    norm = -0.5 * precision * jnp.sum(book * book, axis=0, keepdims=True)
    n0 = norm.astype(BF16).astype(F32)
    n1 = (norm - n0).astype(BF16).astype(F32)
    n2 = norm - n0 - n1
    row = lax.broadcasted_iota(jnp.int32, (16, codes), 0)
    extra = jnp.where(
        row < 3,
        1.0,
        jnp.where(row == 3, n0, jnp.where(row == 4, n1, jnp.where(row == 5, n2, 0.0))),
    ).astype(BF16)
    book_scr[0:dim] = high
    book_scr[dim : 2 * dim] = low
    book_scr[2 * dim : 3 * dim] = high
    book_scr[3 * dim : 3 * dim + 16] = extra
    books_scr[0:dim] = high
    books_scr[dim : 2 * dim] = low
    books_scr[2 * dim : 2 * dim + 16] = jnp.ones((16, codes), BF16)
    high, low = halves(weight_ref[...])
    weight_scr[0:dim] = high
    weight_scr[dim : 2 * dim] = low
    weight_scr[2 * dim : 3 * dim] = high


def latents(refs, scr, feat):
    weight_ref, bias_ref, book_ref, scalar_ref = refs
    weight_scr = scr[2]
    dim = book_ref.shape[0]
    precision, _, _ = scalars(scalar_ref)
    eye = lax.broadcasted_iota(jnp.int32, (dim, dim), 0) == lax.broadcasted_iota(
        jnp.int32, (dim, dim), 1
    )
    bias = jnp.sum(jnp.where(eye, bias_ref[...], 0.0), axis=1, keepdims=True)
    fh, fl = halves(feat)
    both = weight_scr[0 : 2 * dim]
    z2 = dot(both, fh, 1, 1) + dot(both, fl, 1, 1)
    z = z2[0:dim] + z2[dim : 2 * dim] + bias
    square = -0.5 * precision * jnp.sum(z * z, axis=0, keepdims=True)
    return fh, fl, z, square


def logit_rows(zh, zl, square):
    rows = zh.shape[1]
    s0 = square.astype(BF16).astype(F32)
    s1 = (square - s0).astype(BF16).astype(F32)
    s2 = square - s0 - s1
    row = lax.broadcasted_iota(jnp.int32, (16, rows), 0)
    extra = jnp.where(
        row == 0,
        s0,
        jnp.where(row == 1, s1, jnp.where(row == 2, s2, jnp.where(row < 6, 1.0, 0.0))),
    ).astype(BF16)
    return jnp.concatenate([zh, zh, zl, extra], axis=0)


def cot_rows(ch, cl):
    return jnp.concatenate([ch, ch, cl, jnp.zeros((16, ch.shape[1]), BF16)], axis=0)


def over_rows(rows, body, carry):
    step = next(s for s in (32, 16, 8) if rows % s == 0)

    def at(i, carry):
        return body(pl.ds(pl.multiple_of(i * step, step), step), carry)

    return lax.fori_loop(0, rows // step, at, carry, unroll=True)


def folded(x):
    return jnp.sum(x.reshape(x.shape[0] // 8, 8, x.shape[1]), axis=0)


def probabilities(logits):
    top = jnp.max(logits, axis=1, keepdims=True)
    e = jnp.exp(logits - top)
    return e * (1.0 / jnp.sum(e, axis=1, keepdims=True))


def forward(refs, scr, feat, noise_ref, code_refs, usage_ref):
    weight_ref, bias_ref, book_ref, scalar_ref = refs
    book_scr, l_scr = scr[0], scr[3]
    rows = feat.shape[0]
    precision, cold, _ = scalars(scalar_ref)
    _, _, z, square = latents(refs, scr, feat)
    zh, zl = halves(precision * z)
    l_scr[0:rows] = dot(logit_rows(zh, zl, square), book_scr[...], 0, 0)

    usage = usage_ref[...]
    part = rows // len(code_refs)
    for i, code_ref in enumerate(code_refs):
        logit_part = l_scr.at[pl.ds(i * part, part)]
        noise_part = noise_ref.at[pl.ds(i * part, part)]

        def body(at, usage, code_ref=code_ref, logit_part=logit_part, noise_part=noise_part):
            logits = logit_part[at]
            code_ref[at] = probabilities((logits + noise_part[at]) * cold)
            return usage + folded(probabilities(logits))

        usage = over_rows(part, body, usage)
    usage_ref[...] = usage


def gradients(refs, scr, fh, fl, z, square, zh, zl, ch, cl, acc_ref):
    books_scr, weight_scr = scr[1:3]
    wh_scr, wl_scr, gh_scr, gl_scr = scr[5:9]
    rows, feats = fh.shape
    dim, codes = refs[2].shape
    wh, wl = wh_scr[0:rows], wl_scr[0:rows]
    gh, gl = gh_scr[0:rows], gl_scr[0:rows]
    p = dot(jnp.concatenate([ch, cl], axis=0), wh)
    acc_ref[0:64] += p[0:dim] + p[dim : 2 * dim] + dot(ch, wl)
    left = jnp.concatenate([zh, zl, jnp.ones((16, rows), BF16)], axis=0)
    p = dot(left, gh) + dot(left, gl)
    acc_ref[64:128] += p[0:dim] + p[dim : 2 * dim]
    acc_ref[128:136] += p[2 * dim : 2 * dim + 8]
    p = dot(books_scr[...], gh, 1, 1) + dot(books_scr[...], gl, 1, 1)
    row_d = p[2 * dim : 2 * dim + 1]
    gz = 2.0 * (row_d * z - (p[0:dim] + p[dim : 2 * dim]))
    zh, zl = halves(gz)
    p = dot(jnp.concatenate([zh, zl], axis=0), fh)
    acc_ref[144:208, 0:feats] += p[0:dim] + p[dim : 2 * dim] + dot(zh, fl)
    acc_ref[144:208, feats : feats + 128] += jnp.broadcast_to(
        jnp.sum(gz, axis=1, keepdims=True), (dim, 128)
    )
    total = jnp.sum(square * row_d, axis=1, keepdims=True)
    acc_ref[208:216] += jnp.broadcast_to(total, (8, codes))
    return dot(jnp.concatenate([zh, zh, zl], axis=0), weight_scr[...], 0, 0)


def backward(refs, scr, feat, cot, code_ref, acc_ref):
    weight_ref, bias_ref, book_ref, scalar_ref = refs
    book_scr, _, _, _, g_scr, wh_scr, wl_scr, gh_scr, gl_scr = scr
    rows = feat.shape[0]
    precision, _, factor = scalars(scalar_ref)
    fh, fl, z, square = latents(refs, scr, feat)
    zh, zl = halves(precision * z)
    ch, cl = halves(factor * cot)
    g_scr[0:rows] = dot(cot_rows(ch, cl), book_scr[...], 0, 0)

    def body(at, carry):
        w = code_ref[at]
        gw = g_scr[at]
        gd = w * (gw - jnp.sum(w * gw, axis=1, keepdims=True))
        wh_scr[at], wl_scr[at] = halves(w)
        gh_scr[at], gl_scr[at] = halves(gd)
        return carry

    over_rows(rows, body, 0)
    return gradients(refs, scr, fh, fl, z, square, zh, zl, ch, cl, acc_ref)


def both_ways(refs, scr, feat, cot, noise_ref, code_ref, acc_ref):
    weight_ref, bias_ref, book_ref, scalar_ref = refs
    book_scr, _, _, l_scr, g_scr, wh_scr, wl_scr, gh_scr, gl_scr = scr
    rows = feat.shape[0]
    precision, cold, factor = scalars(scalar_ref)
    fh, fl, z, square = latents(refs, scr, feat)
    zh, zl = halves(precision * z)
    ch, cl = halves(factor * cot)
    left = jnp.concatenate([logit_rows(zh, zl, square), cot_rows(ch, cl)], axis=1)
    p = dot(left, book_scr[...], 0, 0)
    l_scr[0:rows] = p[0:rows]
    g_scr[0:rows] = p[rows : 2 * rows]

    def body(at, usage):
        logits = l_scr[at]
        s = (logits + noise_ref[at]) * cold
        e = jnp.exp(s - jnp.max(s, axis=1, keepdims=True))
        gw = g_scr[at]
        scale = 1.0 / jnp.sum(e, axis=1, keepdims=True)
        inner = jnp.sum(e * gw, axis=1, keepdims=True) * scale
        w = e * scale
        code_ref[at] = w
        gd = w * (gw - inner)
        wh_scr[at], wl_scr[at] = halves(w)
        gh_scr[at], gl_scr[at] = halves(gd)
        return usage + folded(probabilities(logits))

    acc_ref[136:144] = over_rows(rows, body, acc_ref[136:144])
    return gradients(refs, scr, fh, fl, z, square, zh, zl, ch, cl, acc_ref)


def tile_scratch(rows, dim, codes, feats):
    return [
        pltpu.VMEM((3 * dim + 16, codes), BF16),
        pltpu.VMEM((2 * dim + 16, codes), BF16),
        pltpu.VMEM((3 * dim, feats), BF16),
        pltpu.VMEM((rows, codes), F32),
        pltpu.VMEM((rows, codes), F32),
        pltpu.VMEM((rows, codes), BF16),
        pltpu.VMEM((rows, codes), BF16),
        pltpu.VMEM((rows, codes), BF16),
        pltpu.VMEM((rows, codes), BF16),
    ]


def settings(limit=VMEM_LIMIT):
    return pltpu.CompilerParams(vmem_limit_bytes=limit)


def cost(rows, feats, dim, codes, tenths):
    return pl.CostEstimate(
        flops=rows * 24 * tenths * (5 * dim * codes + 3 * dim * feats) // 10,
        bytes_accessed=4 * rows * (2 * feats + 2 * codes + dim),
        transcendentals=2 * rows * codes,
    )


SMEM = pl.BlockSpec(memory_space=pltpu.SMEM)
VMEM = pl.BlockSpec(memory_space=pltpu.VMEM)
HBM = pl.BlockSpec(memory_space=pltpu.HBM)


def fixed(shape):
    return pl.BlockSpec(shape, lambda *_: (0,) * len(shape))


class Pieces:
    def __init__(self, runs):
        self.runs = list(runs)
        self.bounds = [0]
        for _, _, slots in self.runs:
            self.bounds.append(self.bounds[-1] + slots)

    def total(self):
        return self.bounds[-1]

    def image(self, share):
        def index(i, table_ref):
            entry = 0
            for (step, first, _), start in zip(self.runs, self.bounds):
                entry = jnp.where(i >= start, step * share + first + i - start, entry)
            return (table_ref[0, entry], 0, 0)

        return index

    def blocks(self, shape):
        return [
            pl.BlockSpec(
                shape,
                lambda i, _, start=start, last=slots - 1: (jnp.clip(i - start, 0, last), 0),
            )
            for (_, _, slots), start in zip(self.runs, self.bounds)
        ]

    def each(self, step, body):
        for i, (low, high) in enumerate(zip(self.bounds, self.bounds[1:])):
            pl.when((step >= low) & (step < high))(functools.partial(body, i))


def places_of(table_ref, wide, shapes, groups, count):
    places = []
    base = 0
    entry = wide + 1
    for _ in range(count):
        for size in range(2):
            strip = shapes[size][1]
            for _ in range(groups[size]):
                places.append((size, table_ref[0, entry], base, strip))
                base += strip
                entry += 1
    return places, base


def small_forward_kernel(count, groups, *refs):
    sources = refs[0:10]
    log_ref, heat_ref = refs[10:12]
    sends = refs[12 : 12 + count]
    table_ref, usage_ref, scalar_ref = refs[12 + count : 15 + count]
    held = refs[15 + count : 25 + count]
    sems, feat_scr, noise_scr = refs[25 + count : 28 + count]
    scr = refs[28 + count :]
    copies = [
        pltpu.make_async_copy(there, here, sems.at[i])
        for i, (there, here) in enumerate(zip(sources, held))
    ]
    for copy in copies:
        copy.start()
    orders, feats, noises, params = held[0:3], held[3:5], held[5:7], (*held[7:10], scalar_ref)
    me = lax.axis_index("space")
    set_scalars(log_ref, heat_ref, scalar_ref)
    for copy in copies[7:10]:
        copy.wait()
    prepare(params, *scr[0:3])
    for copy in copies[0:5]:
        copy.wait()
    wide = orders[2].shape[1]
    share = wide // count
    entry = wide + 1
    table_ref[0, wide] = me
    for step in range(count):
        there = partner(me, step, count)
        for j in range(share):
            table_ref[0, step * share + j] = orders[2][0, there * share + j]
        for size in range(2):
            for j in range(groups[size]):
                table_ref[0, entry] = orders[size][0, there * groups[size] + j]
                entry += 1
    places, _ = places_of(table_ref, wide, [f.shape for f in feats], groups, count)
    for size, image, at, strip in places:
        feat_scr[at : at + strip] = feats[size][image]
    for copy in copies[5:7]:
        copy.wait()
    for size, image, at, strip in places:
        noise_scr[at : at + strip] = noises[size][image]
    usage_ref[...] = jnp.zeros(usage_ref.shape, F32)
    forward(params, scr, feat_scr[...], noise_scr, sends, usage_ref)


def small_forward(count, orders, feats, noises, params):
    dim, codes = params[2].shape
    width = feats[0].shape[2]
    groups = tuple(f.shape[0] // count for f in feats)
    part = sum(g * f.shape[1] for g, f in zip(groups, feats))
    rows = part * count
    arrays = [*orders, *feats, *noises, *params[0:3]]
    return pl.pallas_call(
        functools.partial(small_forward_kernel, count, groups),
        out_shape=[jax.ShapeDtypeStruct((part, codes), F32)] * count
        + [
            jax.ShapeDtypeStruct((1, sum(o.shape[1] for o in orders) + 1), jnp.int32),
            pltpu.HBM((8, codes), F32),
            pltpu.HBM((8, 128), F32),
        ],
        in_specs=[HBM] * 10 + [SMEM] * 2,
        out_specs=[VMEM] * count + [SMEM, VMEM, VMEM],
        scratch_shapes=[
            (pltpu.SMEM if i < 3 else pltpu.VMEM)(a.shape, a.dtype)
            for i, a in enumerate(arrays)
        ]
        + [
            pltpu.SemaphoreType.DMA((10,)),
            pltpu.VMEM((rows, width), F32),
            pltpu.VMEM((rows, codes), F32),
        ]
        + tile_scratch(rows, dim, codes, width),
        compiler_params=settings(),
        cost_estimate=cost(rows, width, dim, codes, 4),
        name="small_forward",
    )(*in_hbm(arrays), *params[3:5])


def small_backward_kernel(count, devices, wide, groups, *refs):
    table_ref = refs[0]
    feats, cots = refs[1:3], refs[3:5]
    parts = refs[5 : 5 + count]
    params = refs[5 + count : 9 + count]
    acc_in, usage_ref = refs[9 + count : 11 + count]
    grads = refs[11 + count : 13 + count]
    shards = refs[13 + count : 13 + count + devices]
    rest = refs[13 + count + devices :]
    acc_ref, sum_scr, feat_scr, cot_scr, code_scr = rest[0:5]
    scr = rest[5:]
    places, base = places_of(table_ref, wide, [f.shape for f in feats], groups, count)
    for size, image, at, strip in places:
        feat_scr[at : at + strip] = feats[size][image]
        cot_scr[at : at + strip] = cots[size][image]
    part = base // count
    for step in range(count):
        code_scr[step * part : (step + 1) * part] = parts[step][...]
    prepare(params, *scr[0:3])
    acc_ref[...] = acc_in[...]
    feat_scr[...] = backward(params, scr, feat_scr[...], cot_scr[...].T, code_scr, acc_ref)
    lay_out(params, acc_ref, usage_ref, sum_scr, shards)
    for size, image, at, strip in places:
        grads[size][image] = feat_scr[at : at + strip]


def small_backward(count, devices, wide, table, feats, cots, parts, params, acc, usage):
    dim, codes = params[2].shape
    width = feats[0].shape[2]
    groups = tuple(f.shape[0] // count for f in feats)
    rows = parts[0].shape[0] * count
    return pl.pallas_call(
        functools.partial(small_backward_kernel, count, devices, wide, groups),
        out_shape=[pltpu.HBM(f.shape, F32) for f in feats]
        + [jax.ShapeDtypeStruct((64 // devices, LANES), F32)] * devices,
        in_specs=[SMEM] + [VMEM] * (10 + count),
        out_specs=[VMEM] * (2 + devices),
        scratch_shapes=[
            pltpu.VMEM(acc.shape, F32),
            pltpu.VMEM((64, LANES), F32),
            pltpu.VMEM((rows, width), F32),
            pltpu.VMEM((rows, dim), F32),
            pltpu.VMEM((rows, codes), F32),
        ]
        + tile_scratch(rows, dim, codes, width),
        compiler_params=settings(),
        cost_estimate=cost(rows, width, dim, codes, 6),
        name="small_backward",
    )(
        table,
        *in_hbm([*feats, *cots]),
        *parts,
        *in_hbm([*params, acc, usage]),
    )


def wide_forward_kernel(pieces, *refs):
    n = len(pieces.runs)
    feat_ref, noise_ref = refs[1:3]
    params = refs[3:7]
    usage_in = refs[7]
    sends = refs[8 : 8 + n]
    usage_ref, code_scr = refs[8 + n : 10 + n]
    scr = refs[10 + n :]
    step = pl.program_id(0)

    @pl.when(step == 0)
    def _():
        prepare(params, *scr[0:3])
        usage_ref[...] = usage_in[...]

    forward(params, scr, feat_ref[...], noise_ref, [code_scr], usage_ref)

    def keep(i):
        sends[i][...] = code_scr[...]

    pieces.each(step, keep)


def wide_forward(count, pieces, table, feat, noise, params, usage, tenths):
    dim, codes = params[2].shape
    images, strip, width = feat.shape
    image = pieces.image(images // count)
    n = len(pieces.runs)
    return pl.pallas_call(
        functools.partial(wide_forward_kernel, pieces),
        grid_spec=pltpu.PrefetchScalarGridSpec(
            num_scalar_prefetch=1,
            grid=(pieces.total(),),
            in_specs=[
                pl.BlockSpec((None, strip, width), image),
                pl.BlockSpec((None, strip, codes), image),
            ]
            + [fixed(p.shape) for p in params]
            + [fixed(usage.shape)],
            out_specs=pieces.blocks((strip, codes)) + [fixed(usage.shape)],
            scratch_shapes=[pltpu.VMEM((strip, codes), F32)]
            + tile_scratch(strip, dim, codes, width),
        ),
        out_shape=[jax.ShapeDtypeStruct((strip * r[2], codes), F32) for r in pieces.runs]
        + [pltpu.HBM(usage.shape, F32)],
        input_output_aliases={7: n},
        compiler_params=settings(),
        cost_estimate=cost(pieces.total() * strip, width, dim, codes, tenths),
        name="wide_forward",
    )(table, *in_hbm([feat, noise, *params, usage]))


def wide_both_kernel(pieces, *refs):
    n = len(pieces.runs)
    feat_ref, noise_ref, cot_ref = refs[1:4]
    params = refs[4:8]
    sends = refs[8 : 8 + n]
    grad_ref, acc_ref, code_scr = refs[8 + n : 11 + n]
    scr = refs[11 + n :]
    step = pl.program_id(0)

    @pl.when(step == 0)
    def _():
        prepare(params, *scr[0:3])
        acc_ref[...] = jnp.zeros(acc_ref.shape, F32)

    grad_ref[...] = both_ways(
        params, scr, feat_ref[...], cot_ref[...], noise_ref, code_scr, acc_ref
    )

    def keep(i):
        sends[i][...] = code_scr[...]

    pieces.each(step, keep)


def wide_both(count, pieces, table, feat, noise, cot, params):
    dim, codes = params[2].shape
    images, strip, width = feat.shape
    image = pieces.image(images // count)
    acc_shape = (ACC_ROWS, codes)
    return pl.pallas_call(
        functools.partial(wide_both_kernel, pieces),
        grid_spec=pltpu.PrefetchScalarGridSpec(
            num_scalar_prefetch=1,
            grid=(pieces.total(),),
            in_specs=[
                pl.BlockSpec((None, strip, width), image),
                pl.BlockSpec((None, strip, codes), image),
                pl.BlockSpec((None, dim, strip), image),
            ]
            + [fixed(p.shape) for p in params],
            out_specs=pieces.blocks((strip, codes))
            + [pl.BlockSpec((None, strip, width), image), fixed(acc_shape)],
            scratch_shapes=[pltpu.VMEM((strip, codes), F32)]
            + tile_scratch(strip, dim, codes, width),
        ),
        out_shape=[jax.ShapeDtypeStruct((strip * r[2], codes), F32) for r in pieces.runs]
        + [pltpu.HBM(feat.shape, F32), pltpu.HBM(acc_shape, F32)],
        compiler_params=settings(),
        cost_estimate=cost(pieces.total() * strip, width, dim, codes, 10),
        name="wide_both",
    )(table, *in_hbm([feat, noise, cot, *params]))


def wide_backward_kernel(pieces, *refs):
    n = len(pieces.runs)
    feat_ref, cot_ref = refs[1:3]
    parts = refs[3 : 3 + n]
    params = refs[3 + n : 7 + n]
    acc_in = refs[7 + n]
    grad_ref, acc_ref, code_scr = refs[9 + n : 12 + n]
    scr = refs[12 + n :]
    step = pl.program_id(0)

    @pl.when(step == 0)
    def _():
        prepare(params, *scr[0:3])
        acc_ref[...] = acc_in[...]

    def fetch(i):
        code_scr[...] = parts[i][...]

    pieces.each(step, fetch)
    grad_ref[...] = backward(params, scr, feat_ref[...], cot_ref[...], code_scr, acc_ref)


def wide_backward(count, pieces, parts, table, feat, cot, params, acc, grad):
    dim, codes = params[2].shape
    images, strip, width = feat.shape
    image = pieces.image(images // count)
    n = len(pieces.runs)
    return pl.pallas_call(
        functools.partial(wide_backward_kernel, pieces),
        grid_spec=pltpu.PrefetchScalarGridSpec(
            num_scalar_prefetch=1,
            grid=(pieces.total(),),
            in_specs=[
                pl.BlockSpec((None, strip, width), image),
                pl.BlockSpec((None, dim, strip), image),
            ]
            + pieces.blocks((strip, codes))
            + [fixed(p.shape) for p in params]
            + [fixed(acc.shape), HBM],
            out_specs=[pl.BlockSpec((None, strip, width), image), fixed(acc.shape)],
            scratch_shapes=[pltpu.VMEM((strip, codes), F32)]
            + tile_scratch(strip, dim, codes, width),
        ),
        out_shape=[pltpu.HBM(feat.shape, F32), pltpu.HBM(acc.shape, F32)],
        input_output_aliases={7 + n: 1, 8 + n: 0},
        compiler_params=settings(),
        cost_estimate=cost(pieces.total() * strip, width, dim, codes, 6),
        name="wide_backward",
    )(table, *in_hbm([feat, cot]), *parts, *in_hbm([*params, acc, grad]))


def shard_at(index, parts):
    height = 64 // parts
    return pl.ds(pl.multiple_of(index * height, height), height)


def lay_out(params, acc_ref, usage_ref, sum_scr, shards):
    weight_ref, bias_ref, book_ref, scalar_ref = params
    codes = book_ref.shape[1]
    width = weight_ref.shape[1]
    devices = len(shards)
    me = lax.rem(lax.axis_index("dp"), devices)
    precision, _, factor = scalars(scalar_ref)
    book = book_ref[...]
    column = acc_ref[128:129]
    moment = acc_ref[64:128] * (1.0 / precision)
    book_sum = acc_ref[0:64] * (1.0 / factor) + 2.0 * (column * book - moment)
    slope = jnp.sum(
        jnp.sum(book * book, axis=0, keepdims=True) * column, axis=1, keepdims=True
    ) - 2.0 * jnp.sum(jnp.sum(book * moment, axis=0, keepdims=True), axis=1, keepdims=True)
    slope = slope + acc_ref[208:209, 0:1] / (-0.5 * precision)
    usage = jnp.sum(acc_ref[136:144] + usage_ref[...], axis=0, keepdims=True)
    dim = book_ref.shape[0]
    eye = lax.broadcasted_iota(jnp.int32, (dim, dim), 0) == lax.broadcasted_iota(
        jnp.int32, (dim, dim), 1
    )
    bias = acc_ref[144:208, width : width + dim]
    bias = jnp.sum(jnp.where(eye, bias, 0.0), axis=0, keepdims=True)
    rest = codes + width
    sum_scr[:, 0:codes] = book_sum
    sum_scr[:, codes:rest] = acc_ref[144:208, 0:width]
    sum_scr[:, rest : rest + 128] = jnp.broadcast_to(slope, (64, 128))
    rows = codes // 128
    for i in range(rows):
        sum_scr[i : i + 1, rest : rest + 128] = usage[:, i * 128 : (i + 1) * 128]
    sum_scr[rows : rows + 1, rest : rest + dim] = bias
    for i in range(devices):
        shards[i][...] = sum_scr[shard_at(partner(me, i, devices), devices)]


def own_kernel(*refs):
    feat_ref, noise_ref, cot_ref = refs[1:4]
    params = refs[4:8]
    acc_in = refs[8]
    code_ref, grad_ref, acc_ref = refs[10:13]
    scr = refs[13:]

    @pl.when(pl.program_id(0) == 0)
    def _():
        prepare(params, *scr[0:3])
        acc_ref[...] = acc_in[...]

    grad_ref[...] = both_ways(
        params, scr, feat_ref[...], cot_ref[...], noise_ref, code_ref, acc_ref
    )


def run_own(count, table, feat, noise, cot, params, acc, grad):
    dim, codes = params[2].shape
    images, strip, width = feat.shape
    share = images // count

    def image(i, table_ref):
        return (table_ref[0, i], 0, 0)

    return pl.pallas_call(
        own_kernel,
        grid_spec=pltpu.PrefetchScalarGridSpec(
            num_scalar_prefetch=1,
            grid=(share,),
            in_specs=[
                pl.BlockSpec((None, strip, width), image),
                pl.BlockSpec((None, strip, codes), image),
                pl.BlockSpec((None, dim, strip), image),
                fixed(params[0].shape),
                fixed(params[1].shape),
                fixed(params[2].shape),
                fixed(params[3].shape),
                fixed(acc.shape),
                HBM,
            ],
            out_specs=[
                pl.BlockSpec(
                    (None, strip, codes),
                    lambda i, table_ref: (i, table_ref[0, count * share], 0),
                ),
                pl.BlockSpec((None, strip, width), image),
                fixed(acc.shape),
            ],
            scratch_shapes=tile_scratch(strip, dim, codes, width),
        ),
        out_shape=[
            pltpu.HBM((share, strip * count, codes), F32),
            pltpu.HBM(feat.shape, F32),
            pltpu.HBM(acc.shape, F32),
        ],
        input_output_aliases={8: 2, 9: 1},
        compiler_params=settings(),
        cost_estimate=cost(share * strip, width, dim, codes, 10),
        name="own_images",
    )(table, *in_hbm([feat, noise, cot, *params, acc, grad]))


def place_kernel(count, runs, *refs):
    parts = refs[0 : len(runs)]
    out_ref, sem = refs[len(runs) + 1 : len(runs) + 3]
    me = lax.axis_index("space")
    copies = []
    for part, (step, first, slots) in zip(parts, runs):
        strip = part.shape[0] // slots
        row = pl.multiple_of(source(me, step, count) * strip, strip)
        for j in range(slots):
            copies.append(
                pltpu.make_async_copy(
                    part.at[pl.ds(j * strip, strip)],
                    out_ref.at[first + j, pl.ds(row, strip)],
                    sem.at[len(copies)],
                )
            )
    for copy in copies:
        copy.start()
    for copy in copies:
        copy.wait()


def place_wide(count, runs, parts, whole):
    return pl.pallas_call(
        functools.partial(place_kernel, count, runs),
        out_shape=pltpu.HBM(whole.shape, F32),
        in_specs=[VMEM] * len(runs) + [HBM],
        out_specs=HBM,
        scratch_shapes=[pltpu.SemaphoreType.DMA((sum(r[2] for r in runs),))],
        input_output_aliases={len(runs): 0},
        compiler_params=settings(VMEM_LIMIT // 2),
        cost_estimate=pl.CostEstimate(
            flops=0, bytes_accessed=2 * sum(p.size * 4 for p in parts), transcendentals=0
        ),
        name="place_wide",
    )(*[pltpu.with_memory_space_constraint(p, pltpu.VMEM) for p in parts], *in_hbm([whole]))


def join_kernel(count, *refs):
    parts = refs[0:count]
    outs = refs[count:]
    me = lax.axis_index("space")
    for step in range(count):
        here = source(me, step, count)
        base = 0
        for out in outs:
            for j in range(out.shape[0]):
                strip = out.shape[2]
                out[j, here] = parts[step][base : base + strip]
                base += strip


def join_small(count, parts, shapes):
    codes = parts[0].shape[1]
    return pl.pallas_call(
        functools.partial(join_kernel, count),
        out_shape=[
            jax.ShapeDtypeStruct((images // count, count, strip, codes), F32)
            for images, strip, _ in shapes
        ],
        compiler_params=settings(VMEM_LIMIT // 2),
        name="join_small",
    )(*parts)


def tree(values):
    while len(values) > 1:
        values = [
            values[i] + values[i + 1] if i + 1 < len(values) else values[i]
            for i in range(0, len(values), 2)
        ]
    return values[0]


def sum_kernel(*refs):
    refs[-1][...] = tree([ref[...] for ref in refs[:-1]])


def add_all(parts):
    return pl.pallas_call(
        sum_kernel,
        out_shape=jax.ShapeDtypeStruct(parts[0].shape, F32),
        compiler_params=settings(VMEM_LIMIT // 2),
        name="add_parts",
    )(*parts)


def final_kernel(devices, pixels, *refs):
    shards = refs[0:devices]
    weight_ref, bias_ref, book_ref, log_ref, usage_ref = refs[devices : devices + 5]
    weight_out, bias_out, book_out, log_out, usage_out = refs[devices + 5 : devices + 10]
    sum_scr = refs[devices + 10]
    me = lax.rem(lax.axis_index("dp"), devices)
    for i in range(devices):
        sum_scr[shard_at(source(me, i, devices), devices)] = shards[i][...]
    dim, codes = book_ref.shape
    width = weight_ref.shape[1]
    scale = 0.5 * lax.rsqrt(jnp.full((8, 128), pixels, F32))[0:1, 0:1]
    book_out[...] = 0.5 * book_ref[...] + scale * sum_scr[:, 0:codes]
    rest = codes + width
    weight_out[...] = 0.5 * weight_ref[...] + scale * sum_scr[:, codes:rest]
    rows = codes // 128
    bias_out[...] = 0.5 * bias_ref[...] + scale * sum_scr[rows : rows + 1, rest : rest + dim]
    usage = jnp.concatenate(
        [sum_scr[i : i + 1, rest : rest + 128] for i in range(rows)], axis=1
    )
    usage_out[...] = 0.5 * usage_ref[...] + 0.5 * (codes / pixels) * usage
    log_out[...] = 0.5 * log_ref[...] + scale * sum_scr[rows + 1 : rows + 2, rest : rest + 1]


def finish(devices, pixels, shards, weight, bias, book, log, usage):
    outs = (weight.T, bias.reshape(1, -1), book.T, log.reshape(1, 1), usage.reshape(1, -1))
    outs = pl.pallas_call(
        functools.partial(final_kernel, devices, pixels),
        out_shape=[jax.ShapeDtypeStruct(out.shape, F32) for out in outs],
        scratch_shapes=[pltpu.VMEM((64, LANES), F32)],
        compiler_params=settings(VMEM_LIMIT // 2),
        name="new_averages",
    )(*shards, *outs)
    return outs[0].T, outs[1].reshape(-1), outs[2].T, outs[3].reshape(-1), outs[4].reshape(-1)


def exchange(value, bit, size, pairs):
    while bit < size:
        value = value + pairs(value, bit)
        bit = 2 * bit
    return value


def per_device(
    feat_small,
    feat_mid,
    feat_wide,
    noise_small,
    noise_mid,
    noise_wide,
    cot_small,
    cot_mid,
    cot_wide,
    order_small,
    order_mid,
    order_wide,
    weight,
    bias,
    book,
    log,
    heat,
    weight_mean,
    bias_mean,
    book_mean,
    log_mean,
    usage_mean,
):
    count = lax.axis_size("space")
    devices = lax.axis_size("dp")
    params = (weight.T, bias.reshape(1, -1), book.T, log, heat)
    feats = (feat_small, feat_mid, feat_wide)
    pixels = sum(f.shape[0] * f.shape[1] for f in feats) * count * devices
    share = feat_wide.shape[0] // count
    cot_wide = jnp.swapaxes(cot_wide, 1, 2)

    def send(values):
        return [lax.ppermute(v, "space", route(i + 1, count)) for i, v in enumerate(values)]

    def after(part, codes):
        return lax.optimization_barrier((part, codes))

    turned = devices % 2 == 0

    def around(codes, step):
        turn = 1 if turned else 0
        pairs = [
            (i * count + j, (i ^ turn) * count + k)
            for i in range(devices)
            for j, k in route(step, count)
        ]
        return lax.ppermute(codes, ("dp", "space"), pairs)

    def back(codes):
        if not turned:
            return codes
        return lax.ppermute(codes, "dp", [(i, i ^ 1) for i in range(devices)])

    orders = (order_small, order_mid, order_wide)
    *small, table, usage, scalar = small_forward(
        count, orders, feats[0:2], (noise_small, noise_mid), params
    )
    params = (*params[0:3], scalar)
    arrived = send(small[1:])
    near = min(4, devices)
    last = count - 1
    early = Pieces([(step, 0, 1) for step in range(1, count)] + [(last, 1, 1)])
    direct = Pieces([(step, 1, share - 1) for step in range(1, last)])
    late = Pieces([(last, 2, share - 2)])
    *early_codes, usage = wide_forward(
        count, early, table, feat_wide, noise_wide, params, usage, 4
    )
    leaving = list(early_codes)
    arrived[-1], leaving[-2] = after(arrived[-1], leaving[-2])
    arrived[:-1], leaving[-1] = after(arrived[:-1], leaving[-1])
    early_arrived = [*send(leaving[:-1]), around(leaving[-1], last)]
    *direct_codes, grad, acc = wide_both(
        count, direct, table, feat_wide, noise_wide, cot_wide, params
    )
    codes_small, codes_mid = join_small(
        count, [small[0]] + arrived, [f.shape for f in feats[0:2]]
    )
    codes_small, codes_mid, usage = lax.optimization_barrier(
        (codes_small, codes_mid, usage)
    )
    late_codes, usage = wide_forward(
        count, late, table, feat_wide, noise_wide, params, usage, 1
    )
    leaving = list(direct_codes)
    late_codes, leaving[-1] = after(late_codes, leaving[-1])
    early_arrived[0], leaving[-1] = after(early_arrived[0], leaving[-1])
    direct_arrived = send(leaving)
    early_arrived[-2], leaving = after(early_arrived[-2], late_codes)
    late_arrived = lax.ppermute(leaving, "space", route(last, count))
    early_arrived, acc = lax.optimization_barrier((early_arrived, acc))
    early_arrived[-1] = back(early_arrived[-1])
    whole, grad, acc = run_own(
        count, table, feat_wide, noise_wide, cot_wide, params, acc, grad
    )
    whole = place_wide(count, early.runs, early_arrived, whole)
    whole, acc = lax.optimization_barrier((whole, acc))
    grad, acc = wide_backward(
        count,
        Pieces(early.runs + late.runs),
        [*early_codes, late_codes],
        table,
        feat_wide,
        cot_wide,
        params,
        acc,
        grad,
    )
    grad_small, grad_mid, *shards = small_backward(
        count,
        near,
        feat_wide.shape[0],
        table,
        feats[0:2],
        (cot_small, cot_mid),
        small,
        params,
        acc,
        usage,
    )
    group = [
        [(i, i - i % near + partner(i % near, step, near)) for i in range(devices)]
        for step in range(near)
    ]
    parts = [lax.ppermute(shards[i], "dp", group[i]) for i in range(1, near)]
    mine = add_all([shards[0]] + parts)

    def along(value, offset):
        return lax.ppermute(value, "dp", [(i, i ^ offset) for i in range(devices)])

    def across(value, offset):
        turn = near if devices > near else 0
        pairs = [
            (i * count + j, (i ^ turn) * count + (j ^ offset))
            for i in range(devices)
            for j in range(count)
        ]
        return lax.ppermute(value, ("dp", "space"), pairs)

    mine = exchange(mine, near, devices, along)
    mine = exchange(mine, 1, count, across)
    shards = [mine] + [lax.ppermute(mine, "dp", group[i]) for i in range(1, near)]
    updated = finish(
        near, pixels, shards, weight_mean, bias_mean, book_mean, log_mean, usage_mean
    )
    whole = place_wide(count, late.runs, [late_arrived], whole)
    for run, part in zip(direct.runs, direct_arrived):
        whole = place_wide(count, [run], [part], whole)
    codes = whole.shape[2]
    return (
        codes_small.reshape(codes_small.shape[0], -1, codes),
        codes_mid.reshape(codes_mid.shape[0], -1, codes),
        whole,
        grad_small,
        grad_mid,
        grad,
        *updated,
    )


def solution(mesh):
    strips = P("dp", "space", None)
    placed = (strips,) * 9 + (P("dp", None),) * 3 + (P(),) * 10
    return jax.shard_map(
        per_device,
        mesh=mesh,
        in_specs=placed,
        out_specs=(P(("dp", "space"), None, None),) * 3 + (strips,) * 3 + (P(),) * 5,
        check_vma=False,
    )
```

```python
import functools

import jax
import jax.numpy as jnp
from jax import lax
from jax.experimental import pallas as pl
from jax.experimental.pallas import tpu as pltpu
from jax.sharding import PartitionSpec as P

F32 = jnp.float32
BF16 = jnp.bfloat16
VMEM_LIMIT = 24 * 1024 * 1024
ACC_ROWS = 64 + 64 + 8 + 8 + 64 + 8
LANES = 896


def partner(index, step, count):
    if count & (count - 1) == 0:
        return index ^ step
    return lax.rem(index + step, count)


def route(step, count):
    if count & (count - 1) == 0:
        return [(i, i ^ step) for i in range(count)]
    return [(i, (i + step) % count) for i in range(count)]


def source(index, step, count):
    if count & (count - 1) == 0:
        return index ^ step
    return lax.rem(index + (count - step), count)


def in_hbm(arrays):
    return [pltpu.with_memory_space_constraint(a, pltpu.HBM) for a in arrays]


def halves(x):
    high = x.astype(BF16)
    return high, (x - high.astype(F32)).astype(BF16)


def dot(left, right, left_dim=1, right_dim=0):
    return lax.dot_general(
        left, right, (((left_dim,), (right_dim,)), ((), ())), preferred_element_type=F32
    )


def set_scalars(log_ref, heat_ref, out_ref):
    precision = jnp.exp(jnp.full((8, 128), log_ref[0], F32))
    heat = jnp.full((8, 128), heat_ref[0], F32)
    row = lax.broadcasted_iota(jnp.int32, (8, 128), 0)
    factor = -0.5 * precision / heat
    out_ref[...] = jnp.where(row == 0, precision, jnp.where(row == 1, 1.0 / heat, factor))


def scalars(ref):
    return ref[0:1, 0:1], ref[1:2, 0:1], ref[2:3, 0:1]


def prepare(refs, book_scr, books_scr, weight_scr):
    weight_ref, bias_ref, book_ref, scalar_ref = refs
    dim, codes = book_ref.shape
    precision, _, _ = scalars(scalar_ref)
    book = book_ref[...]
    high, low = halves(book)
    norm = -0.5 * precision * jnp.sum(book * book, axis=0, keepdims=True)
    n0 = norm.astype(BF16).astype(F32)
    n1 = (norm - n0).astype(BF16).astype(F32)
    n2 = norm - n0 - n1
    row = lax.broadcasted_iota(jnp.int32, (16, codes), 0)
    extra = jnp.where(
        row < 3,
        1.0,
        jnp.where(row == 3, n0, jnp.where(row == 4, n1, jnp.where(row == 5, n2, 0.0))),
    ).astype(BF16)
    book_scr[0:dim] = high
    book_scr[dim : 2 * dim] = low
    book_scr[2 * dim : 3 * dim] = high
    book_scr[3 * dim : 3 * dim + 16] = extra
    books_scr[0:dim] = high
    books_scr[dim : 2 * dim] = low
    books_scr[2 * dim : 2 * dim + 16] = jnp.ones((16, codes), BF16)
    high, low = halves(weight_ref[...])
    weight_scr[0:dim] = high
    weight_scr[dim : 2 * dim] = low
    weight_scr[2 * dim : 3 * dim] = high


def latents(refs, shared, feat):
    weight_ref, bias_ref, book_ref, scalar_ref = refs
    weight_scr = shared[2]
    dim = book_ref.shape[0]
    precision, _, _ = scalars(scalar_ref)
    eye = lax.broadcasted_iota(jnp.int32, (dim, dim), 0) == lax.broadcasted_iota(
        jnp.int32, (dim, dim), 1
    )
    bias = jnp.sum(jnp.where(eye, bias_ref[...], 0.0), axis=1, keepdims=True)
    fh, fl = halves(feat)
    both = weight_scr[0 : 2 * dim]
    z2 = dot(both, fh, 1, 1) + dot(both, fl, 1, 1)
    z = z2[0:dim] + z2[dim : 2 * dim] + bias
    square = -0.5 * precision * jnp.sum(z * z, axis=0, keepdims=True)
    return fh, fl, z, square


def logit_rows(zh, zl, square):
    rows = zh.shape[1]
    s0 = square.astype(BF16).astype(F32)
    s1 = (square - s0).astype(BF16).astype(F32)
    s2 = square - s0 - s1
    row = lax.broadcasted_iota(jnp.int32, (16, rows), 0)
    extra = jnp.where(
        row == 0,
        s0,
        jnp.where(row == 1, s1, jnp.where(row == 2, s2, jnp.where(row < 6, 1.0, 0.0))),
    ).astype(BF16)
    return jnp.concatenate([zh, zh, zl, extra], axis=0)


def cot_rows(ch, cl):
    return jnp.concatenate([ch, ch, cl, jnp.zeros((16, ch.shape[1]), BF16)], axis=0)


def over_rows(rows, body, carry):
    step = next(s for s in (32, 16, 8) if rows % s == 0)

    def at(i, carry):
        return body(pl.ds(pl.multiple_of(i * step, step), step), carry)

    return lax.fori_loop(0, rows // step, at, carry, unroll=True)


def folded(x):
    return jnp.sum(x.reshape(x.shape[0] // 8, 8, x.shape[1]), axis=0)


def probabilities(logits):
    top = jnp.max(logits, axis=1, keepdims=True)
    e = jnp.exp(logits - top)
    return e * (1.0 / jnp.sum(e, axis=1, keepdims=True))


def forward_products(refs, shared, feat, l_scr):
    precision, _, _ = scalars(refs[3])
    _, _, z, square = latents(refs, shared, feat)
    zh, zl = halves(precision * z)
    l_scr[0 : feat.shape[0]] = dot(logit_rows(zh, zl, square), shared[0][...], 0, 0)


def forward_rows(refs, l_scr, noise_ref, code_ref, usage):
    _, cold, _ = scalars(refs[3])

    def body(at, usage):
        logits = l_scr[at]
        code_ref[at] = probabilities((logits + noise_ref[at]) * cold)
        return usage + folded(probabilities(logits))

    return over_rows(code_ref.shape[0], body, usage)


def products(refs, shared, scr, feat, cot, forward):
    l_scr, g_scr = scr[0:2]
    rows = feat.shape[0]
    precision, _, factor = scalars(refs[3])
    fh, fl, z, square = latents(refs, shared, feat)
    zh, zl = halves(precision * z)
    ch, cl = halves(factor * cot)
    if forward:
        left = jnp.concatenate([logit_rows(zh, zl, square), cot_rows(ch, cl)], axis=1)
        p = dot(left, shared[0][...], 0, 0)
        l_scr[0:rows] = p[0:rows]
        g_scr[0:rows] = p[rows : 2 * rows]
    else:
        g_scr[0:rows] = dot(cot_rows(ch, cl), shared[0][...], 0, 0)
    return fh, fl, z, square, zh, zl, ch, cl


def both_rows(refs, scr, noise_ref, code_ref, usage):
    l_scr, g_scr, wh_scr, wl_scr, gh_scr, gl_scr = scr
    _, cold, _ = scalars(refs[3])

    def body(at, usage):
        logits = l_scr[at]
        s = (logits + noise_ref[at]) * cold
        e = jnp.exp(s - jnp.max(s, axis=1, keepdims=True))
        gw = g_scr[at]
        scale = 1.0 / jnp.sum(e, axis=1, keepdims=True)
        inner = jnp.sum(e * gw, axis=1, keepdims=True) * scale
        w = e * scale
        code_ref[at] = w
        gd = w * (gw - inner)
        wh_scr[at], wl_scr[at] = halves(w)
        gh_scr[at], gl_scr[at] = halves(gd)
        return usage + folded(probabilities(logits))

    return over_rows(code_ref.shape[0], body, usage)


def backward_rows(scr, code_ref):
    _, g_scr, wh_scr, wl_scr, gh_scr, gl_scr = scr

    def body(at, carry):
        w = code_ref[at]
        gw = g_scr[at]
        gd = w * (gw - jnp.sum(w * gw, axis=1, keepdims=True))
        wh_scr[at], wl_scr[at] = halves(w)
        gh_scr[at], gl_scr[at] = halves(gd)
        return carry

    over_rows(code_ref.shape[0], body, 0)


def gradients(refs, shared, scr, state, acc_ref):
    _, books_scr, weight_scr = shared
    wh_scr, wl_scr, gh_scr, gl_scr = scr[2:6]
    fh, fl, z, square, zh, zl, ch, cl = state
    rows, feats = fh.shape
    dim, codes = refs[2].shape
    wh, wl = wh_scr[0:rows], wl_scr[0:rows]
    gh, gl = gh_scr[0:rows], gl_scr[0:rows]
    p = dot(jnp.concatenate([ch, cl], axis=0), wh)
    acc_ref[0:64] += p[0:dim] + p[dim : 2 * dim] + dot(ch, wl)
    left = jnp.concatenate([zh, zl, jnp.ones((16, rows), BF16)], axis=0)
    p = dot(left, gh) + dot(left, gl)
    acc_ref[64:128] += p[0:dim] + p[dim : 2 * dim]
    acc_ref[128:136] += p[2 * dim : 2 * dim + 8]
    p = dot(books_scr[...], gh, 1, 1) + dot(books_scr[...], gl, 1, 1)
    row_d = p[2 * dim : 2 * dim + 1]
    gz = 2.0 * (row_d * z - (p[0:dim] + p[dim : 2 * dim]))
    zh, zl = halves(gz)
    p = dot(jnp.concatenate([zh, zl], axis=0), fh)
    acc_ref[144:208, 0:feats] += p[0:dim] + p[dim : 2 * dim] + dot(zh, fl)
    acc_ref[144:208, feats : feats + 128] += jnp.broadcast_to(
        jnp.sum(gz, axis=1, keepdims=True), (dim, 128)
    )
    total = jnp.sum(square * row_d, axis=1, keepdims=True)
    acc_ref[208:216] += jnp.broadcast_to(total, (8, codes))
    return dot(jnp.concatenate([zh, zh, zl], axis=0), weight_scr[...], 0, 0)


def shared_scratch(dim, codes, feats):
    return [
        pltpu.VMEM((3 * dim + 16, codes), BF16),
        pltpu.VMEM((2 * dim + 16, codes), BF16),
        pltpu.VMEM((3 * dim, feats), BF16),
    ]


def tile_scratch(rows, codes):
    return [pltpu.VMEM((rows, codes), F32)] * 2 + [pltpu.VMEM((rows, codes), BF16)] * 4


def settings(limit=VMEM_LIMIT):
    return pltpu.CompilerParams(vmem_limit_bytes=limit)


def cost(rows, feats, dim, codes, tenths):
    return pl.CostEstimate(
        flops=rows * 24 * tenths * (5 * dim * codes + 3 * dim * feats) // 10,
        bytes_accessed=4 * rows * (2 * feats + 2 * codes + dim),
        transcendentals=2 * rows * codes,
    )


SMEM = pl.BlockSpec(memory_space=pltpu.SMEM)
VMEM = pl.BlockSpec(memory_space=pltpu.VMEM)
HBM = pl.BlockSpec(memory_space=pltpu.HBM)


def fixed(shape):
    return pl.BlockSpec(shape, lambda *_: (0,) * len(shape))


class Lane:
    def __init__(self, runs):
        self.runs = list(runs)
        self.bounds = [0]
        for _, _, slots in self.runs:
            self.bounds.append(self.bounds[-1] + slots)

    def total(self):
        return self.bounds[-1]

    def entry(self, i, share):
        entry = 0
        for (step, first, _), start in zip(self.runs, self.bounds):
            here = step * share + first + i - start
            entry = here if start == 0 else jnp.where(i >= start, here, entry)
        return entry

    def image(self, shape, share):
        return pl.BlockSpec(
            (None, *shape), lambda i, table_ref: (table_ref[0, self.entry(i, share)], 0, 0)
        )

    def blocks(self, shape):
        return [
            pl.BlockSpec(
                shape,
                lambda i, _, start=start, last=slots - 1: (jnp.clip(i - start, 0, last), 0),
            )
            for (_, _, slots), start in zip(self.runs, self.bounds)
        ]

    def each(self, step, body):
        for i, (low, high) in enumerate(zip(self.bounds, self.bounds[1:])):
            pl.when((step >= low) & (step < high))(functools.partial(body, i))


def split(runs, ways):
    whole = Lane(runs)
    lanes, current = [], []
    for run in whole.runs:
        current.append(run)
        if Lane(current).total() * ways == whole.total():
            lanes.append(Lane(current))
            current = []
    return lanes if len(lanes) == ways and not current else [whole]


def take(refs, *sizes):
    groups, at = [], 0
    for size in sizes:
        groups.append(refs[at : at + size])
        at += size
    return groups


def by_lane(refs, lanes):
    return take(refs, *[len(lane.runs) for lane in lanes])


def keep_codes(step, lanes, sends, code_scrs):
    for lane, refs, code_scr in zip(lanes, by_lane(sends, lanes), code_scrs):
        if len(lane.runs) > 1:

            def keep(i, refs=refs, code_scr=code_scr):
                refs[i][...] = code_scr[...]

            lane.each(step, keep)


def code_targets(lanes, sends, code_scrs):
    return [
        refs[0] if len(lane.runs) == 1 else code_scr
        for lane, refs, code_scr in zip(lanes, by_lane(sends, lanes), code_scrs)
    ]


class Gradients:
    def __init__(self, out_ref, scr, sems):
        self.out_ref, self.scr, self.sems = out_ref, scr, sems

    def copy(self, lane, slot, image):
        return pltpu.make_async_copy(
            self.scr.at[lane, slot], self.out_ref.at[image], self.sems.at[lane, slot]
        )

    def ready(self, step, lanes):
        @pl.when(step >= 2)
        def _():
            for lane in range(lanes):
                self.copy(lane, lax.rem(step, 2), 0).wait()

    def store(self, step, values, images):
        slot = lax.rem(step, 2)
        for lane, (value, image) in enumerate(zip(values, images)):
            self.scr[lane, slot] = value
            self.copy(lane, slot, image).start()

    def end(self, step, lanes, steps):
        @pl.when(step == steps - 1)
        def _():
            for lane in range(lanes):
                for slot in range(min(2, steps)):
                    self.copy(lane, slot, 0).wait()


def gradient_scratch(lanes, strip, width):
    return [pltpu.VMEM((lanes, 2, strip, width), F32), pltpu.SemaphoreType.DMA((lanes, 2))]


def places_of(table_ref, wide, shapes, groups, count):
    places = []
    base = 0
    entry = wide + 1
    for _ in range(count):
        for size in range(2):
            strip = shapes[size][1]
            for _ in range(groups[size]):
                places.append((size, table_ref[0, entry], base, strip))
                base += strip
                entry += 1
    return places, base


def small_forward_kernel(count, groups, *refs):
    sources = refs[0:10]
    log_ref, heat_ref = refs[10:12]
    sends = refs[12 : 12 + count]
    table_ref, usage_ref, scalar_ref = refs[12 + count : 15 + count]
    held = refs[15 + count : 25 + count]
    sems, feat_scr, noise_scr = refs[25 + count : 28 + count]
    scr = refs[28 + count :]
    copies = [
        pltpu.make_async_copy(there, here, sems.at[i])
        for i, (there, here) in enumerate(zip(sources, held))
    ]
    for copy in copies:
        copy.start()
    orders, feats, noises, params = held[0:3], held[3:5], held[5:7], (*held[7:10], scalar_ref)
    me = lax.axis_index("space")
    set_scalars(log_ref, heat_ref, scalar_ref)
    for copy in copies[7:10]:
        copy.wait()
    shared, tile_scr = take(scr, 3, 6)
    prepare(params, *shared)
    for copy in copies[0:5]:
        copy.wait()
    wide = orders[2].shape[1]
    share = wide // count
    entry = wide + 1
    table_ref[0, wide] = me
    for step in range(count):
        there = partner(me, step, count)
        for j in range(share):
            table_ref[0, step * share + j] = orders[2][0, there * share + j]
        for size in range(2):
            for j in range(groups[size]):
                table_ref[0, entry] = orders[size][0, there * groups[size] + j]
                entry += 1
    places, _ = places_of(table_ref, wide, [f.shape for f in feats], groups, count)
    for size, image, at, strip in places:
        feat_scr[at : at + strip] = feats[size][image]
    for copy in copies[5:7]:
        copy.wait()
    for size, image, at, strip in places:
        noise_scr[at : at + strip] = noises[size][image]
    forward_products(params, shared, feat_scr[...], tile_scr[0])
    usage = jnp.zeros(usage_ref.shape, F32)
    part = sends[0].shape[0]
    for step in range(count):
        rows = pl.ds(step * part, part)
        usage = forward_rows(
            params, tile_scr[0].at[rows], noise_scr.at[rows], sends[step], usage
        )
    usage_ref[...] = usage


def small_forward(count, orders, feats, noises, params):
    dim, codes = params[2].shape
    width = feats[0].shape[2]
    groups = tuple(f.shape[0] // count for f in feats)
    part = sum(g * f.shape[1] for g, f in zip(groups, feats))
    rows = part * count
    arrays = [*orders, *feats, *noises, *params[0:3]]
    return pl.pallas_call(
        functools.partial(small_forward_kernel, count, groups),
        out_shape=[jax.ShapeDtypeStruct((part, codes), F32)] * count
        + [
            jax.ShapeDtypeStruct((1, sum(o.shape[1] for o in orders) + 1), jnp.int32),
            pltpu.HBM((8, codes), F32),
            pltpu.HBM((8, 128), F32),
        ],
        in_specs=[HBM] * 10 + [SMEM] * 2,
        out_specs=[VMEM] * count + [SMEM, VMEM, VMEM],
        scratch_shapes=[
            (pltpu.SMEM if i < 3 else pltpu.VMEM)(a.shape, a.dtype)
            for i, a in enumerate(arrays)
        ]
        + [
            pltpu.SemaphoreType.DMA((10,)),
            pltpu.VMEM((rows, width), F32),
            pltpu.VMEM((rows, codes), F32),
        ]
        + shared_scratch(dim, codes, width)
        + tile_scratch(rows, codes),
        compiler_params=settings(),
        cost_estimate=cost(rows, width, dim, codes, 4),
        name="small_forward",
    )(*in_hbm(arrays), *params[3:5])


def small_backward_kernel(count, devices, wide, groups, *refs):
    table_ref = refs[0]
    feats, cots = refs[1:3], refs[3:5]
    parts = refs[5 : 5 + count]
    params = refs[5 + count : 9 + count]
    acc_in, usage_ref = refs[9 + count : 11 + count]
    grads = refs[11 + count : 13 + count]
    shards = refs[13 + count : 13 + count + devices]
    rest = refs[13 + count + devices :]
    acc_ref, sum_scr, feat_scr, cot_scr, code_scr = rest[0:5]
    scr = rest[5:]
    places, base = places_of(table_ref, wide, [f.shape for f in feats], groups, count)
    for size, image, at, strip in places:
        feat_scr[at : at + strip] = feats[size][image]
        cot_scr[at : at + strip] = cots[size][image]
    part = base // count
    for step in range(count):
        code_scr[step * part : (step + 1) * part] = parts[step][...]
    shared, tile_scr = take(scr, 3, 6)
    prepare(params, *shared)
    acc_ref[...] = acc_in[...]
    state = products(params, shared, tile_scr, feat_scr[...], cot_scr[...].T, False)
    backward_rows(tile_scr, code_scr)
    feat_scr[...] = gradients(params, shared, tile_scr, state, acc_ref)
    lay_out(params, acc_ref, usage_ref, sum_scr, shards)
    for size, image, at, strip in places:
        grads[size][image] = feat_scr[at : at + strip]


def small_backward(count, devices, wide, table, feats, cots, parts, params, acc, usage):
    dim, codes = params[2].shape
    width = feats[0].shape[2]
    groups = tuple(f.shape[0] // count for f in feats)
    rows = parts[0].shape[0] * count
    return pl.pallas_call(
        functools.partial(small_backward_kernel, count, devices, wide, groups),
        out_shape=[pltpu.HBM(f.shape, F32) for f in feats]
        + [jax.ShapeDtypeStruct((64 // devices, LANES), F32)] * devices,
        in_specs=[SMEM] + [VMEM] * (10 + count),
        out_specs=[VMEM] * (2 + devices),
        scratch_shapes=[
            pltpu.VMEM(acc.shape, F32),
            pltpu.VMEM((64, LANES), F32),
            pltpu.VMEM((rows, width), F32),
            pltpu.VMEM((rows, dim), F32),
            pltpu.VMEM((rows, codes), F32),
        ]
        + shared_scratch(dim, codes, width)
        + tile_scratch(rows, codes),
        compiler_params=settings(),
        cost_estimate=cost(rows, width, dim, codes, 6),
        name="small_backward",
    )(
        table,
        *in_hbm([*feats, *cots]),
        *parts,
        *in_hbm([*params, acc, usage]),
    )


def wide_forward_kernel(lanes, joined, *refs):
    n = len(lanes)
    arrays = 1 if joined else sum(len(lane.runs) for lane in lanes)
    _, feats, noises, params, usage_in, sends, rest = take(
        refs, 1, n, n, 4, 1, arrays, len(refs)
    )
    (usage_ref,), code_scrs, shared, l_scrs = take(rest, 1, n, 3, n)
    step = pl.program_id(0)

    @pl.when(step == 0)
    def _():
        prepare(params, *shared)
        usage_ref[...] = usage_in[0][...]

    if joined:
        strip = code_scrs[0].shape[0]
        targets = [sends[0].at[pl.ds(i * strip, strip)] for i in range(n)]
    else:
        targets = code_targets(lanes, sends, code_scrs)
    for feat_ref, l_scr in zip(feats, l_scrs):
        forward_products(params, shared, feat_ref[...], l_scr)
    usage = usage_ref[...]
    for l_scr, noise_ref, target in zip(l_scrs, noises, targets):
        usage = forward_rows(params, l_scr, noise_ref, target, usage)
    usage_ref[...] = usage
    if not joined:
        keep_codes(step, lanes, sends, code_scrs)


def wide_forward(count, lanes, joined, table, feat, noise, params, usage, tenths):
    dim, codes = params[2].shape
    images, strip, width = feat.shape
    share = images // count
    n, steps = len(lanes), lanes[0].total()
    if joined:
        blocks = [fixed((n * strip, codes))]
        sizes = [n]
    else:
        blocks = [block for lane in lanes for block in lane.blocks((strip, codes))]
        sizes = [run[2] for lane in lanes for run in lane.runs]
    return pl.pallas_call(
        functools.partial(wide_forward_kernel, lanes, joined),
        grid_spec=pltpu.PrefetchScalarGridSpec(
            num_scalar_prefetch=1,
            grid=(steps,),
            in_specs=[lane.image((strip, width), share) for lane in lanes]
            + [lane.image((strip, codes), share) for lane in lanes]
            + [fixed(p.shape) for p in params]
            + [fixed(usage.shape)],
            out_specs=blocks + [fixed(usage.shape)],
            scratch_shapes=[pltpu.VMEM((strip, codes), F32)] * n
            + shared_scratch(dim, codes, width)
            + [pltpu.VMEM((strip, codes), F32)] * n,
        ),
        out_shape=[jax.ShapeDtypeStruct((strip * slots, codes), F32) for slots in sizes]
        + [pltpu.HBM(usage.shape, F32)],
        input_output_aliases={5 + 2 * n: len(sizes)},
        compiler_params=settings(),
        cost_estimate=cost(n * steps * strip, width, dim, codes, tenths),
        name="wide_forward",
    )(table, *in_hbm([feat] * n + [noise] * n + [*params, usage]))


def wide_both_kernel(lanes, share, *refs):
    n = len(lanes)
    arrays = sum(len(lane.runs) for lane in lanes)
    table, feats, noises, cots, params, sends, rest = take(
        refs, 1, n, n, n, 4, arrays, len(refs)
    )
    (grad_out, acc_ref), code_scrs, (grad_scr, sems), shared, rest = take(
        rest, 2, n, 2, 3, 6 * n
    )
    scrs = take(rest, *[6] * n)
    grads = Gradients(grad_out, grad_scr, sems)
    step, steps = pl.program_id(0), lanes[0].total()

    @pl.when(step == 0)
    def _():
        prepare(params, *shared)
        acc_ref[...] = jnp.zeros(acc_ref.shape, F32)

    grads.ready(step, n)
    targets = code_targets(lanes, sends, code_scrs)
    states = [
        products(params, shared, scr, feat_ref[...], cot_ref[...], True)
        for scr, feat_ref, cot_ref in zip(scrs, feats, cots)
    ]
    usage = acc_ref[136:144]
    for scr, noise_ref, target in zip(scrs, noises, targets):
        usage = both_rows(params, scr, noise_ref, target, usage)
    acc_ref[136:144] = usage
    values = [
        gradients(params, shared, scr, state, acc_ref) for scr, state in zip(scrs, states)
    ]
    grads.store(step, values, [table[0][0, lane.entry(step, share)] for lane in lanes])
    keep_codes(step, lanes, sends, code_scrs)
    grads.end(step, n, steps)


def wide_both(count, lanes, table, feat, noise, cot, params):
    dim, codes = params[2].shape
    images, strip, width = feat.shape
    share = images // count
    n, steps = len(lanes), lanes[0].total()
    acc_shape = (ACC_ROWS, codes)
    sizes = [run[2] for lane in lanes for run in lane.runs]
    return pl.pallas_call(
        functools.partial(wide_both_kernel, lanes, share),
        grid_spec=pltpu.PrefetchScalarGridSpec(
            num_scalar_prefetch=1,
            grid=(steps,),
            in_specs=[lane.image((strip, width), share) for lane in lanes]
            + [lane.image((strip, codes), share) for lane in lanes]
            + [lane.image((dim, strip), share) for lane in lanes]
            + [fixed(p.shape) for p in params],
            out_specs=[block for lane in lanes for block in lane.blocks((strip, codes))]
            + [HBM, fixed(acc_shape)],
            scratch_shapes=[pltpu.VMEM((strip, codes), F32)] * n
            + gradient_scratch(n, strip, width)
            + shared_scratch(dim, codes, width)
            + tile_scratch(strip, codes) * n,
        ),
        out_shape=[jax.ShapeDtypeStruct((strip * slots, codes), F32) for slots in sizes]
        + [pltpu.HBM(feat.shape, F32), pltpu.HBM(acc_shape, F32)],
        compiler_params=settings(),
        cost_estimate=cost(n * steps * strip, width, dim, codes, 10),
        name="wide_both",
    )(table, *in_hbm([feat] * n + [noise] * n + [cot] * n + [*params]))


def wide_backward_kernel(lanes, share, *refs):
    n = len(lanes)
    arrays = sum(len(lane.runs) for lane in lanes)
    table, feats, cots, parts, params, (acc_in, _), rest = take(
        refs, 1, n, n, arrays, 4, 2, len(refs)
    )
    (grad_out, acc_ref), code_scrs, (grad_scr, sems), shared, rest = take(
        rest, 2, n, 2, 3, 6 * n
    )
    scrs = take(rest, *[6] * n)
    grads = Gradients(grad_out, grad_scr, sems)
    step, steps = pl.program_id(0), lanes[0].total()

    @pl.when(step == 0)
    def _():
        prepare(params, *shared)
        acc_ref[...] = acc_in[...]

    grads.ready(step, n)
    for lane, refs_of, code_scr in zip(lanes, by_lane(parts, lanes), code_scrs):
        if len(lane.runs) > 1:

            def fetch(i, refs_of=refs_of, code_scr=code_scr):
                code_scr[...] = refs_of[i][...]

            lane.each(step, fetch)
    states = [
        products(params, shared, scr, feat_ref[...], cot_ref[...], False)
        for scr, feat_ref, cot_ref in zip(scrs, feats, cots)
    ]
    for scr, code_ref in zip(scrs, code_targets(lanes, parts, code_scrs)):
        backward_rows(scr, code_ref)
    values = [
        gradients(params, shared, scr, state, acc_ref) for scr, state in zip(scrs, states)
    ]
    grads.store(step, values, [table[0][0, lane.entry(step, share)] for lane in lanes])
    grads.end(step, n, steps)


def wide_backward(count, lanes, parts, table, feat, cot, params, acc, grad):
    dim, codes = params[2].shape
    images, strip, width = feat.shape
    share = images // count
    n, steps = len(lanes), lanes[0].total()
    return pl.pallas_call(
        functools.partial(wide_backward_kernel, lanes, share),
        grid_spec=pltpu.PrefetchScalarGridSpec(
            num_scalar_prefetch=1,
            grid=(steps,),
            in_specs=[lane.image((strip, width), share) for lane in lanes]
            + [lane.image((dim, strip), share) for lane in lanes]
            + [block for lane in lanes for block in lane.blocks((strip, codes))]
            + [fixed(p.shape) for p in params]
            + [fixed(acc.shape), HBM],
            out_specs=[HBM, fixed(acc.shape)],
            scratch_shapes=[pltpu.VMEM((strip, codes), F32)] * n
            + gradient_scratch(n, strip, width)
            + shared_scratch(dim, codes, width)
            + tile_scratch(strip, codes) * n,
        ),
        out_shape=[pltpu.HBM(feat.shape, F32), pltpu.HBM(acc.shape, F32)],
        input_output_aliases={5 + 2 * n + len(parts): 1, 6 + 2 * n + len(parts): 0},
        compiler_params=settings(),
        cost_estimate=cost(n * steps * strip, width, dim, codes, 6),
        name="wide_backward",
    )(
        table,
        *in_hbm([feat] * n + [cot] * n),
        *parts,
        *in_hbm([*params, acc, grad]),
    )


def shard_at(index, parts):
    height = 64 // parts
    return pl.ds(pl.multiple_of(index * height, height), height)


def lay_out(params, acc_ref, usage_ref, sum_scr, shards):
    weight_ref, bias_ref, book_ref, scalar_ref = params
    codes = book_ref.shape[1]
    width = weight_ref.shape[1]
    devices = len(shards)
    me = lax.rem(lax.axis_index("dp"), devices)
    precision, _, factor = scalars(scalar_ref)
    book = book_ref[...]
    column = acc_ref[128:129]
    moment = acc_ref[64:128] * (1.0 / precision)
    book_sum = acc_ref[0:64] * (1.0 / factor) + 2.0 * (column * book - moment)
    slope = jnp.sum(
        jnp.sum(book * book, axis=0, keepdims=True) * column, axis=1, keepdims=True
    ) - 2.0 * jnp.sum(jnp.sum(book * moment, axis=0, keepdims=True), axis=1, keepdims=True)
    slope = slope + acc_ref[208:209, 0:1] / (-0.5 * precision)
    usage = jnp.sum(acc_ref[136:144] + usage_ref[...], axis=0, keepdims=True)
    dim = book_ref.shape[0]
    eye = lax.broadcasted_iota(jnp.int32, (dim, dim), 0) == lax.broadcasted_iota(
        jnp.int32, (dim, dim), 1
    )
    bias = acc_ref[144:208, width : width + dim]
    bias = jnp.sum(jnp.where(eye, bias, 0.0), axis=0, keepdims=True)
    rest = codes + width
    sum_scr[:, 0:codes] = book_sum
    sum_scr[:, codes:rest] = acc_ref[144:208, 0:width]
    sum_scr[:, rest : rest + 128] = jnp.broadcast_to(slope, (64, 128))
    rows = codes // 128
    for i in range(rows):
        sum_scr[i : i + 1, rest : rest + 128] = usage[:, i * 128 : (i + 1) * 128]
    sum_scr[rows : rows + 1, rest : rest + dim] = bias
    for i in range(devices):
        shards[i][...] = sum_scr[shard_at(partner(me, i, devices), devices)]


def own_kernel(n, *refs):
    table, feats, noises, cots, params, (acc_in, _), rest = take(
        refs, 1, n, n, n, 4, 2, len(refs)
    )
    (code_ref, grad_out, acc_ref), (grad_scr, sems), shared, rest = take(rest, 3, 2, 3, 6 * n)
    scrs = take(rest, *[6] * n)
    grads = Gradients(grad_out, grad_scr, sems)
    step = pl.program_id(0)

    @pl.when(step == 0)
    def _():
        prepare(params, *shared)
        acc_ref[...] = acc_in[...]

    grads.ready(step, n)
    states = [
        products(params, shared, scr, feat_ref[...], cot_ref[...], True)
        for scr, feat_ref, cot_ref in zip(scrs, feats, cots)
    ]
    usage = acc_ref[136:144]
    for i, (scr, noise_ref) in enumerate(zip(scrs, noises)):
        usage = both_rows(params, scr, noise_ref, code_ref.at[i], usage)
    acc_ref[136:144] = usage
    values = [
        gradients(params, shared, scr, state, acc_ref) for scr, state in zip(scrs, states)
    ]
    grads.store(step, values, [table[0][0, step * n + i] for i in range(n)])
    grads.end(step, n, pl.num_programs(0))


def run_own(count, table, feat, noise, cot, params, acc, grad):
    dim, codes = params[2].shape
    images, strip, width = feat.shape
    share = images // count
    n = 2 if share % 2 == 0 else 1

    def image(lane, shape):
        return pl.BlockSpec(
            (None, *shape), lambda i, table_ref: (table_ref[0, i * n + lane], 0, 0)
        )

    return pl.pallas_call(
        functools.partial(own_kernel, n),
        grid_spec=pltpu.PrefetchScalarGridSpec(
            num_scalar_prefetch=1,
            grid=(share // n,),
            in_specs=[image(lane, (strip, width)) for lane in range(n)]
            + [image(lane, (strip, codes)) for lane in range(n)]
            + [image(lane, (dim, strip)) for lane in range(n)]
            + [fixed(p.shape) for p in params]
            + [fixed(acc.shape), HBM],
            out_specs=[
                pl.BlockSpec(
                    (n, strip, codes),
                    lambda i, table_ref: (i, table_ref[0, count * share], 0),
                ),
                HBM,
                fixed(acc.shape),
            ],
            scratch_shapes=gradient_scratch(n, strip, width)
            + shared_scratch(dim, codes, width)
            + tile_scratch(strip, codes) * n,
        ),
        out_shape=[
            pltpu.HBM((share, strip * count, codes), F32),
            pltpu.HBM(feat.shape, F32),
            pltpu.HBM(acc.shape, F32),
        ],
        input_output_aliases={5 + 3 * n: 2, 6 + 3 * n: 1},
        compiler_params=settings(),
        cost_estimate=cost(share * strip, width, dim, codes, 10),
        name="own_images",
    )(table, *in_hbm([feat] * n + [noise] * n + [cot] * n + [*params, acc, grad]))


def place_kernel(count, runs, *refs):
    parts = refs[0 : len(runs)]
    out_ref, sem = refs[len(runs) + 1 : len(runs) + 3]
    me = lax.axis_index("space")
    copies = []
    for part, (step, first, slots) in zip(parts, runs):
        strip = part.shape[0] // slots
        row = pl.multiple_of(source(me, step, count) * strip, strip)
        for j in range(slots):
            copies.append(
                pltpu.make_async_copy(
                    part.at[pl.ds(j * strip, strip)],
                    out_ref.at[first + j, pl.ds(row, strip)],
                    sem.at[len(copies)],
                )
            )
    for copy in copies:
        copy.start()
    for copy in copies:
        copy.wait()


def place_wide(count, runs, parts, whole):
    return pl.pallas_call(
        functools.partial(place_kernel, count, runs),
        out_shape=pltpu.HBM(whole.shape, F32),
        in_specs=[VMEM] * len(runs) + [HBM],
        out_specs=HBM,
        scratch_shapes=[pltpu.SemaphoreType.DMA((sum(r[2] for r in runs),))],
        input_output_aliases={len(runs): 0},
        compiler_params=settings(VMEM_LIMIT // 2),
        cost_estimate=pl.CostEstimate(
            flops=0, bytes_accessed=2 * sum(p.size * 4 for p in parts), transcendentals=0
        ),
        name="place_wide",
    )(*[pltpu.with_memory_space_constraint(p, pltpu.VMEM) for p in parts], *in_hbm([whole]))


def join_kernel(count, *refs):
    parts = refs[0:count]
    outs = refs[count:]
    me = lax.axis_index("space")
    for step in range(count):
        here = source(me, step, count)
        base = 0
        for out in outs:
            for j in range(out.shape[0]):
                strip = out.shape[2]
                out[j, here] = parts[step][base : base + strip]
                base += strip


def join_small(count, parts, shapes):
    codes = parts[0].shape[1]
    return pl.pallas_call(
        functools.partial(join_kernel, count),
        out_shape=[
            jax.ShapeDtypeStruct((images // count, count, strip, codes), F32)
            for images, strip, _ in shapes
        ],
        compiler_params=settings(VMEM_LIMIT // 2),
        name="join_small",
    )(*parts)


def tree(values):
    while len(values) > 1:
        values = [
            values[i] + values[i + 1] if i + 1 < len(values) else values[i]
            for i in range(0, len(values), 2)
        ]
    return values[0]


def sum_kernel(*refs):
    refs[-1][...] = tree([ref[...] for ref in refs[:-1]])


def add_all(parts):
    return pl.pallas_call(
        sum_kernel,
        out_shape=jax.ShapeDtypeStruct(parts[0].shape, F32),
        compiler_params=settings(VMEM_LIMIT // 2),
        name="add_parts",
    )(*parts)


def final_kernel(devices, pixels, *refs):
    shards = refs[0:devices]
    weight_ref, bias_ref, book_ref, log_ref, usage_ref = refs[devices : devices + 5]
    weight_out, bias_out, book_out, log_out, usage_out = refs[devices + 5 : devices + 10]
    sum_scr = refs[devices + 10]
    me = lax.rem(lax.axis_index("dp"), devices)
    for i in range(devices):
        sum_scr[shard_at(source(me, i, devices), devices)] = shards[i][...]
    dim, codes = book_ref.shape
    width = weight_ref.shape[1]
    scale = 0.5 * lax.rsqrt(jnp.full((8, 128), pixels, F32))[0:1, 0:1]
    book_out[...] = 0.5 * book_ref[...] + scale * sum_scr[:, 0:codes]
    rest = codes + width
    weight_out[...] = 0.5 * weight_ref[...] + scale * sum_scr[:, codes:rest]
    rows = codes // 128
    bias_out[...] = 0.5 * bias_ref[...] + scale * sum_scr[rows : rows + 1, rest : rest + dim]
    usage = jnp.concatenate(
        [sum_scr[i : i + 1, rest : rest + 128] for i in range(rows)], axis=1
    )
    usage_out[...] = 0.5 * usage_ref[...] + 0.5 * (codes / pixels) * usage
    log_out[...] = 0.5 * log_ref[...] + scale * sum_scr[rows + 1 : rows + 2, rest : rest + 1]


def finish(devices, pixels, shards, weight, bias, book, log, usage):
    outs = (weight.T, bias.reshape(1, -1), book.T, log.reshape(1, 1), usage.reshape(1, -1))
    outs = pl.pallas_call(
        functools.partial(final_kernel, devices, pixels),
        out_shape=[jax.ShapeDtypeStruct(out.shape, F32) for out in outs],
        scratch_shapes=[pltpu.VMEM((64, LANES), F32)],
        compiler_params=settings(VMEM_LIMIT // 2),
        name="new_averages",
    )(*shards, *outs)
    return outs[0].T, outs[1].reshape(-1), outs[2].T, outs[3].reshape(-1), outs[4].reshape(-1)


def exchange(value, bit, size, pairs):
    while bit < size:
        value = value + pairs(value, bit)
        bit = 2 * bit
    return value


def per_device(
    feat_small,
    feat_mid,
    feat_wide,
    noise_small,
    noise_mid,
    noise_wide,
    cot_small,
    cot_mid,
    cot_wide,
    order_small,
    order_mid,
    order_wide,
    weight,
    bias,
    book,
    log,
    heat,
    weight_mean,
    bias_mean,
    book_mean,
    log_mean,
    usage_mean,
):
    count = lax.axis_size("space")
    devices = lax.axis_size("dp")
    params = (weight.T, bias.reshape(1, -1), book.T, log, heat)
    feats = (feat_small, feat_mid, feat_wide)
    pixels = sum(f.shape[0] * f.shape[1] for f in feats) * count * devices
    share = feat_wide.shape[0] // count
    cot_wide = jnp.swapaxes(cot_wide, 1, 2)

    def send(values):
        return [lax.ppermute(v, "space", route(i + 1, count)) for i, v in enumerate(values)]

    def follow(codes, before):
        before[-1], codes[-1] = lax.optimization_barrier((before[-1], codes[-1]))
        return send(codes)

    orders = (order_small, order_mid, order_wide)
    *small, table, usage, scalar = small_forward(
        count, orders, feats[0:2], (noise_small, noise_mid), params
    )
    params = (*params[0:3], scalar)
    arrived = [send(small[1:])]
    near = min(4, devices)
    last = count - 1
    early = [(step, 0, 1) for step in range(1, count)]
    direct = [(step, 1, share - 1) for step in range(1, last)]
    late = [(last, 1, share - 1)]
    *early_codes, usage = wide_forward(
        count, split(early, 3), False, table, feat_wide, noise_wide, params, usage, 4
    )
    arrived.append(follow(list(early_codes), arrived[0]))
    *codes, grad, acc = wide_both(
        count, split(direct, 2), table, feat_wide, noise_wide, cot_wide, params
    )
    codes_small, codes_mid = join_small(
        count, [small[0]] + arrived[0], [f.shape for f in feats[0:2]]
    )
    codes_small, codes_mid, usage = lax.optimization_barrier(
        (codes_small, codes_mid, usage)
    )
    late_lanes = [Lane([(last, slot, 1)]) for slot in range(1, share)]
    late_codes, usage = wide_forward(
        count, late_lanes, True, table, feat_wide, noise_wide, params, usage, 1
    )
    arrived.append(follow([*codes, late_codes], arrived[1]))
    arrived[1], acc = lax.optimization_barrier((arrived[1], acc))
    whole, grad, acc = run_own(
        count, table, feat_wide, noise_wide, cot_wide, params, acc, grad
    )
    whole = place_wide(count, early, arrived[1], whole)
    whole, acc = lax.optimization_barrier((whole, acc))
    grad, acc = wide_backward(
        count,
        split(early + late, 2),
        [*early_codes, late_codes],
        table,
        feat_wide,
        cot_wide,
        params,
        acc,
        grad,
    )
    grad_small, grad_mid, *shards = small_backward(
        count,
        near,
        feat_wide.shape[0],
        table,
        feats[0:2],
        (cot_small, cot_mid),
        small,
        params,
        acc,
        usage,
    )
    group = [
        [(i, i - i % near + partner(i % near, step, near)) for i in range(devices)]
        for step in range(near)
    ]
    parts = [lax.ppermute(shards[i], "dp", group[i]) for i in range(1, near)]
    mine = add_all([shards[0]] + parts)

    def along(value, offset):
        return lax.ppermute(value, "dp", [(i, i ^ offset) for i in range(devices)])

    def across(value, offset):
        turn = near if devices > near else 0
        pairs = [
            (i * count + j, (i ^ turn) * count + (j ^ offset))
            for i in range(devices)
            for j in range(count)
        ]
        return lax.ppermute(value, ("dp", "space"), pairs)

    mine = exchange(mine, near, devices, along)
    mine = exchange(mine, 1, count, across)
    shards = [mine] + [lax.ppermute(mine, "dp", group[i]) for i in range(1, near)]
    updated = finish(
        near, pixels, shards, weight_mean, bias_mean, book_mean, log_mean, usage_mean
    )
    for run, part in zip(direct + late, arrived[2]):
        whole = place_wide(count, [run], [part], whole)
    codes = whole.shape[2]
    return (
        codes_small.reshape(codes_small.shape[0], -1, codes),
        codes_mid.reshape(codes_mid.shape[0], -1, codes),
        whole,
        grad_small,
        grad_mid,
        grad,
        *updated,
    )


def solution(mesh):
    strips = P("dp", "space", None)
    placed = (strips,) * 9 + (P("dp", None),) * 3 + (P(),) * 10
    return jax.shard_map(
        per_device,
        mesh=mesh,
        in_specs=placed,
        out_specs=(P(("dp", "space"), None, None),) * 3 + (strips,) * 3 + (P(),) * 5,
        check_vma=False,
    )
```

```python
import functools

import jax
import jax.numpy as jnp
from jax import lax
from jax.experimental import pallas as pl
from jax.experimental.pallas import tpu as pltpu
from jax.sharding import PartitionSpec as P

F32 = jnp.float32
BF16 = jnp.bfloat16
VMEM_LIMIT = 24 * 1024 * 1024
ACC_ROWS = 64 + 64 + 8 + 8 + 64 + 8
LANES = 896


def partner(index, step, count):
    if count & (count - 1) == 0:
        return index ^ step
    return lax.rem(index + step, count)


def route(step, count):
    if count & (count - 1) == 0:
        return [(i, i ^ step) for i in range(count)]
    return [(i, (i + step) % count) for i in range(count)]


def source(index, step, count):
    if count & (count - 1) == 0:
        return index ^ step
    return lax.rem(index + (count - step), count)


def in_hbm(arrays):
    return [pltpu.with_memory_space_constraint(a, pltpu.HBM) for a in arrays]


def halves(x):
    high = x.astype(BF16)
    return high, (x - high.astype(F32)).astype(BF16)


def dot(left, right, left_dim=1, right_dim=0):
    return lax.dot_general(
        left, right, (((left_dim,), (right_dim,)), ((), ())), preferred_element_type=F32
    )


def set_scalars(log_ref, heat_ref, out_ref):
    precision = jnp.exp(jnp.full((8, 128), log_ref[0], F32))
    heat = jnp.full((8, 128), heat_ref[0], F32)
    row = lax.broadcasted_iota(jnp.int32, (8, 128), 0)
    factor = -0.5 * precision / heat
    out_ref[...] = jnp.where(row == 0, precision, jnp.where(row == 1, 1.0 / heat, factor))


def scalars(ref):
    return ref[0:1, 0:1], ref[1:2, 0:1], ref[2:3, 0:1]


def prepare(refs, book_scr, books_scr, weight_scr):
    weight_ref, bias_ref, book_ref, scalar_ref = refs
    dim, codes = book_ref.shape
    precision, _, _ = scalars(scalar_ref)
    book = book_ref[...]
    high, low = halves(book)
    norm = -0.5 * precision * jnp.sum(book * book, axis=0, keepdims=True)
    n0 = norm.astype(BF16).astype(F32)
    n1 = (norm - n0).astype(BF16).astype(F32)
    n2 = norm - n0 - n1
    row = lax.broadcasted_iota(jnp.int32, (16, codes), 0)
    extra = jnp.where(
        row < 3,
        1.0,
        jnp.where(row == 3, n0, jnp.where(row == 4, n1, jnp.where(row == 5, n2, 0.0))),
    ).astype(BF16)
    book_scr[0:dim] = high
    book_scr[dim : 2 * dim] = low
    book_scr[2 * dim : 3 * dim] = high
    book_scr[3 * dim : 3 * dim + 16] = extra
    books_scr[0:dim] = high
    books_scr[dim : 2 * dim] = low
    books_scr[2 * dim : 2 * dim + 16] = jnp.ones((16, codes), BF16)
    high, low = halves(weight_ref[...])
    weight_scr[0:dim] = high
    weight_scr[dim : 2 * dim] = low
    weight_scr[2 * dim : 3 * dim] = high


def latents(refs, shared, feat):
    weight_ref, bias_ref, book_ref, scalar_ref = refs
    weight_scr = shared[2]
    dim = book_ref.shape[0]
    precision, _, _ = scalars(scalar_ref)
    eye = lax.broadcasted_iota(jnp.int32, (dim, dim), 0) == lax.broadcasted_iota(
        jnp.int32, (dim, dim), 1
    )
    bias = jnp.sum(jnp.where(eye, bias_ref[...], 0.0), axis=1, keepdims=True)
    fh, fl = halves(feat)
    both = weight_scr[0 : 2 * dim]
    z2 = dot(both, fh, 1, 1) + dot(both, fl, 1, 1)
    z = z2[0:dim] + z2[dim : 2 * dim] + bias
    square = -0.5 * precision * jnp.sum(z * z, axis=0, keepdims=True)
    return fh, fl, z, square


def logit_rows(zh, zl, square):
    rows = zh.shape[1]
    s0 = square.astype(BF16).astype(F32)
    s1 = (square - s0).astype(BF16).astype(F32)
    s2 = square - s0 - s1
    row = lax.broadcasted_iota(jnp.int32, (16, rows), 0)
    extra = jnp.where(
        row == 0,
        s0,
        jnp.where(row == 1, s1, jnp.where(row == 2, s2, jnp.where(row < 6, 1.0, 0.0))),
    ).astype(BF16)
    return jnp.concatenate([zh, zh, zl, extra], axis=0)


def cot_rows(ch, cl):
    return jnp.concatenate([ch, ch, cl, jnp.zeros((16, ch.shape[1]), BF16)], axis=0)


def over_rows(rows, body, carry):
    step = next(s for s in (32, 16, 8) if rows % s == 0)

    def at(i, carry):
        return body(pl.ds(pl.multiple_of(i * step, step), step), carry)

    return lax.fori_loop(0, rows // step, at, carry, unroll=True)


def folded(x):
    return jnp.sum(x.reshape(x.shape[0] // 8, 8, x.shape[1]), axis=0)


def normal(e):
    return e * (1.0 / jnp.sum(e, axis=1, keepdims=True))


def shifted(logits):
    return logits - jnp.max(logits, axis=1, keepdims=True)


def forward_products(refs, shared, feat, l_scr):
    precision, _, _ = scalars(refs[3])
    _, _, z, square = latents(refs, shared, feat)
    zh, zl = halves(precision * z)
    l_scr[0 : feat.shape[0]] = dot(logit_rows(zh, zl, square), shared[0][...], 0, 0)


def forward_rows(refs, l_scr, noise_ref, code_ref, usage):
    _, cold, _ = scalars(refs[3])

    def body(at, usage):
        logits = shifted(l_scr[at])
        code_ref[at] = normal(jnp.exp((logits + noise_ref[at]) * cold))
        return usage + folded(normal(jnp.exp(logits)))

    return over_rows(code_ref.shape[0], body, usage)


def products(refs, shared, scr, feat, cot, forward):
    l_scr, g_scr = scr[0:2]
    rows = feat.shape[0]
    precision, _, factor = scalars(refs[3])
    fh, fl, z, square = latents(refs, shared, feat)
    zh, zl = halves(precision * z)
    ch, cl = halves(factor * cot)
    if forward:
        left = jnp.concatenate([logit_rows(zh, zl, square), cot_rows(ch, cl)], axis=1)
        p = dot(left, shared[0][...], 0, 0)
        l_scr[0:rows] = p[0:rows]
        g_scr[0:rows] = p[rows : 2 * rows]
    else:
        g_scr[0:rows] = dot(cot_rows(ch, cl), shared[0][...], 0, 0)
    return fh, fl, z, square, zh, zl, ch, cl


def both_rows(refs, scr, noise_ref, code_ref, usage):
    l_scr, g_scr, wh_scr, wl_scr, gh_scr, gl_scr = scr
    _, cold, _ = scalars(refs[3])

    def body(at, usage):
        logits = shifted(l_scr[at])
        e = jnp.exp((logits + noise_ref[at]) * cold)
        gw = g_scr[at]
        scale = 1.0 / jnp.sum(e, axis=1, keepdims=True)
        inner = jnp.sum(e * gw, axis=1, keepdims=True) * scale
        w = e * scale
        code_ref[at] = w
        gd = w * (gw - inner)
        wh_scr[at], wl_scr[at] = halves(w)
        gh_scr[at], gl_scr[at] = halves(gd)
        return usage + folded(normal(jnp.exp(logits)))

    return over_rows(code_ref.shape[0], body, usage)


def backward_rows(scr, code_ref):
    _, g_scr, wh_scr, wl_scr, gh_scr, gl_scr = scr

    def body(at, carry):
        w = code_ref[at]
        gw = g_scr[at]
        gd = w * (gw - jnp.sum(w * gw, axis=1, keepdims=True))
        wh_scr[at], wl_scr[at] = halves(w)
        gh_scr[at], gl_scr[at] = halves(gd)
        return carry

    over_rows(code_ref.shape[0], body, 0)


def gradients(refs, shared, scr, state, acc_ref):
    _, books_scr, weight_scr = shared
    wh_scr, wl_scr, gh_scr, gl_scr = scr[2:6]
    fh, fl, z, square, zh, zl, ch, cl = state
    rows, feats = fh.shape
    dim, codes = refs[2].shape
    wh, wl = wh_scr[0:rows], wl_scr[0:rows]
    gh, gl = gh_scr[0:rows], gl_scr[0:rows]
    p = dot(jnp.concatenate([ch, cl], axis=0), wh)
    acc_ref[0:64] += p[0:dim] + p[dim : 2 * dim] + dot(ch, wl)
    left = jnp.concatenate([zh, zl, jnp.ones((16, rows), BF16)], axis=0)
    p = dot(left, gh) + dot(left, gl)
    acc_ref[64:128] += p[0:dim] + p[dim : 2 * dim]
    acc_ref[128:136] += p[2 * dim : 2 * dim + 8]
    p = dot(books_scr[...], gh, 1, 1) + dot(books_scr[...], gl, 1, 1)
    row_d = p[2 * dim : 2 * dim + 1]
    gz = 2.0 * (row_d * z - (p[0:dim] + p[dim : 2 * dim]))
    zh, zl = halves(gz)
    p = dot(jnp.concatenate([zh, zl], axis=0), fh)
    acc_ref[144:208, 0:feats] += p[0:dim] + p[dim : 2 * dim] + dot(zh, fl)
    acc_ref[144:208, feats : feats + 128] += jnp.broadcast_to(
        jnp.sum(gz, axis=1, keepdims=True), (dim, 128)
    )
    total = jnp.sum(square * row_d, axis=1, keepdims=True)
    acc_ref[208:216] += jnp.broadcast_to(total, (8, codes))
    return dot(jnp.concatenate([zh, zh, zl], axis=0), weight_scr[...], 0, 0)


def shared_scratch(dim, codes, feats):
    return [
        pltpu.VMEM((3 * dim + 16, codes), BF16),
        pltpu.VMEM((2 * dim + 16, codes), BF16),
        pltpu.VMEM((3 * dim, feats), BF16),
    ]


def tile_scratch(rows, codes):
    return [pltpu.VMEM((rows, codes), F32)] * 2 + [pltpu.VMEM((rows, codes), BF16)] * 4


def settings(limit=VMEM_LIMIT):
    return pltpu.CompilerParams(vmem_limit_bytes=limit)


def cost(rows, feats, dim, codes, tenths):
    return pl.CostEstimate(
        flops=rows * 24 * tenths * (5 * dim * codes + 3 * dim * feats) // 10,
        bytes_accessed=4 * rows * (2 * feats + 2 * codes + dim),
        transcendentals=2 * rows * codes,
    )


SMEM = pl.BlockSpec(memory_space=pltpu.SMEM)
VMEM = pl.BlockSpec(memory_space=pltpu.VMEM)
HBM = pl.BlockSpec(memory_space=pltpu.HBM)


def fixed(shape):
    return pl.BlockSpec(shape, lambda *_: (0,) * len(shape))


class Lane:
    def __init__(self, runs):
        self.runs = list(runs)
        self.bounds = [0]
        for _, _, slots in self.runs:
            self.bounds.append(self.bounds[-1] + slots)

    def total(self):
        return self.bounds[-1]

    def entry(self, i, share):
        entry = 0
        for (step, first, _), start in zip(self.runs, self.bounds):
            here = step * share + first + i - start
            entry = here if start == 0 else jnp.where(i >= start, here, entry)
        return entry

    def image(self, shape, share):
        return pl.BlockSpec(
            (None, *shape), lambda i, table_ref: (table_ref[0, self.entry(i, share)], 0, 0)
        )

    def blocks(self, shape):
        return [
            pl.BlockSpec(
                shape,
                lambda i, _, start=start, last=slots - 1: (jnp.clip(i - start, 0, last), 0),
            )
            for (_, _, slots), start in zip(self.runs, self.bounds)
        ]

    def each(self, step, body):
        for i, (low, high) in enumerate(zip(self.bounds, self.bounds[1:])):
            pl.when((step >= low) & (step < high))(functools.partial(body, i))


def split(runs, ways):
    whole = Lane(runs)
    lanes, current = [], []
    for run in whole.runs:
        current.append(run)
        if Lane(current).total() * ways == whole.total():
            lanes.append(Lane(current))
            current = []
    return lanes if len(lanes) == ways and not current else [whole]


def take(refs, *sizes):
    groups, at = [], 0
    for size in sizes:
        groups.append(refs[at : at + size])
        at += size
    return groups


def by_lane(refs, lanes):
    return take(refs, *[len(lane.runs) for lane in lanes])


def keep_codes(step, lanes, sends, code_scrs):
    for lane, refs, code_scr in zip(lanes, by_lane(sends, lanes), code_scrs):
        if len(lane.runs) > 1:

            def keep(i, refs=refs, code_scr=code_scr):
                refs[i][...] = code_scr[...]

            lane.each(step, keep)


def code_targets(lanes, sends, code_scrs):
    return [
        refs[0] if len(lane.runs) == 1 else code_scr
        for lane, refs, code_scr in zip(lanes, by_lane(sends, lanes), code_scrs)
    ]


class Gradients:
    def __init__(self, out_ref, scr, sems):
        self.out_ref, self.scr, self.sems = out_ref, scr, sems

    def copy(self, lane, slot, image):
        return pltpu.make_async_copy(
            self.scr.at[lane, slot], self.out_ref.at[image], self.sems.at[lane, slot]
        )

    def ready(self, step, lanes):
        @pl.when(step >= 2)
        def _():
            for lane in range(lanes):
                self.copy(lane, lax.rem(step, 2), 0).wait()

    def store(self, step, values, images):
        slot = lax.rem(step, 2)
        for lane, (value, image) in enumerate(zip(values, images)):
            self.scr[lane, slot] = value
            self.copy(lane, slot, image).start()

    def end(self, step, lanes, steps):
        @pl.when(step == steps - 1)
        def _():
            for lane in range(lanes):
                for slot in range(min(2, steps)):
                    self.copy(lane, slot, 0).wait()


def gradient_scratch(lanes, strip, width):
    return [pltpu.VMEM((lanes, 2, strip, width), F32), pltpu.SemaphoreType.DMA((lanes, 2))]


def places_of(table_ref, wide, shapes, groups, count):
    places = []
    base = 0
    entry = wide + 1
    for _ in range(count):
        for size in range(2):
            strip = shapes[size][1]
            for _ in range(groups[size]):
                places.append((size, table_ref[0, entry], base, strip))
                base += strip
                entry += 1
    return places, base


def small_forward_kernel(count, groups, *refs):
    sources = refs[0:10]
    log_ref, heat_ref = refs[10:12]
    sends = refs[12 : 12 + count]
    table_ref, usage_ref, scalar_ref = refs[12 + count : 15 + count]
    held = refs[15 + count : 25 + count]
    sems, feat_scr, noise_scr = refs[25 + count : 28 + count]
    scr = refs[28 + count :]
    copies = [
        pltpu.make_async_copy(there, here, sems.at[i])
        for i, (there, here) in enumerate(zip(sources, held))
    ]
    for copy in copies:
        copy.start()
    orders, feats, noises, params = held[0:3], held[3:5], held[5:7], (*held[7:10], scalar_ref)
    me = lax.axis_index("space")
    set_scalars(log_ref, heat_ref, scalar_ref)
    for copy in copies[7:10]:
        copy.wait()
    shared, tile_scr = take(scr, 3, 6)
    prepare(params, *shared)
    for copy in copies[0:5]:
        copy.wait()
    wide = orders[2].shape[1]
    share = wide // count
    entry = wide + 1
    table_ref[0, wide] = me
    for step in range(count):
        there = partner(me, step, count)
        for j in range(share):
            table_ref[0, step * share + j] = orders[2][0, there * share + j]
        for size in range(2):
            for j in range(groups[size]):
                table_ref[0, entry] = orders[size][0, there * groups[size] + j]
                entry += 1
    places, _ = places_of(table_ref, wide, [f.shape for f in feats], groups, count)
    for size, image, at, strip in places:
        feat_scr[at : at + strip] = feats[size][image]
    for copy in copies[5:7]:
        copy.wait()
    for size, image, at, strip in places:
        noise_scr[at : at + strip] = noises[size][image]
    forward_products(params, shared, feat_scr[...], tile_scr[0])
    usage = jnp.zeros(usage_ref.shape, F32)
    part = sends[0].shape[0]
    for step in range(count):
        rows = pl.ds(step * part, part)
        usage = forward_rows(
            params, tile_scr[0].at[rows], noise_scr.at[rows], sends[step], usage
        )
    usage_ref[...] = usage


def small_forward(count, orders, feats, noises, params):
    dim, codes = params[2].shape
    width = feats[0].shape[2]
    groups = tuple(f.shape[0] // count for f in feats)
    part = sum(g * f.shape[1] for g, f in zip(groups, feats))
    rows = part * count
    arrays = [*orders, *feats, *noises, *params[0:3]]
    return pl.pallas_call(
        functools.partial(small_forward_kernel, count, groups),
        out_shape=[jax.ShapeDtypeStruct((part, codes), F32)] * count
        + [
            jax.ShapeDtypeStruct((1, sum(o.shape[1] for o in orders) + 1), jnp.int32),
            pltpu.HBM((8, codes), F32),
            pltpu.HBM((8, 128), F32),
        ],
        in_specs=[HBM] * 10 + [SMEM] * 2,
        out_specs=[VMEM] * count + [SMEM, VMEM, VMEM],
        scratch_shapes=[
            (pltpu.SMEM if i < 3 else pltpu.VMEM)(a.shape, a.dtype)
            for i, a in enumerate(arrays)
        ]
        + [
            pltpu.SemaphoreType.DMA((10,)),
            pltpu.VMEM((rows, width), F32),
            pltpu.VMEM((rows, codes), F32),
        ]
        + shared_scratch(dim, codes, width)
        + tile_scratch(rows, codes),
        compiler_params=settings(),
        cost_estimate=cost(rows, width, dim, codes, 4),
        name="small_forward",
    )(*in_hbm(arrays), *params[3:5])


def small_backward_kernel(count, devices, wide, groups, *refs):
    table_ref = refs[0]
    feats, cots = refs[1:3], refs[3:5]
    parts = refs[5 : 5 + count]
    params = refs[5 + count : 9 + count]
    acc_in, usage_ref = refs[9 + count : 11 + count]
    grads = refs[11 + count : 13 + count]
    shards = refs[13 + count : 13 + count + devices]
    rest = refs[13 + count + devices :]
    acc_ref, sum_scr, feat_scr, cot_scr, code_scr = rest[0:5]
    scr = rest[5:]
    places, base = places_of(table_ref, wide, [f.shape for f in feats], groups, count)
    for size, image, at, strip in places:
        feat_scr[at : at + strip] = feats[size][image]
        cot_scr[at : at + strip] = cots[size][image]
    part = base // count
    for step in range(count):
        code_scr[step * part : (step + 1) * part] = parts[step][...]
    shared, tile_scr = take(scr, 3, 6)
    prepare(params, *shared)
    acc_ref[...] = acc_in[...]
    state = products(params, shared, tile_scr, feat_scr[...], cot_scr[...].T, False)
    backward_rows(tile_scr, code_scr)
    feat_scr[...] = gradients(params, shared, tile_scr, state, acc_ref)
    lay_out(params, acc_ref, usage_ref, sum_scr, shards)
    for size, image, at, strip in places:
        grads[size][image] = feat_scr[at : at + strip]


def small_backward(count, devices, wide, table, feats, cots, parts, params, acc, usage):
    dim, codes = params[2].shape
    width = feats[0].shape[2]
    groups = tuple(f.shape[0] // count for f in feats)
    rows = parts[0].shape[0] * count
    return pl.pallas_call(
        functools.partial(small_backward_kernel, count, devices, wide, groups),
        out_shape=[pltpu.HBM(f.shape, F32) for f in feats]
        + [jax.ShapeDtypeStruct((64 // devices, LANES), F32)] * devices,
        in_specs=[SMEM] + [VMEM] * (10 + count),
        out_specs=[VMEM] * (2 + devices),
        scratch_shapes=[
            pltpu.VMEM(acc.shape, F32),
            pltpu.VMEM((64, LANES), F32),
            pltpu.VMEM((rows, width), F32),
            pltpu.VMEM((rows, dim), F32),
            pltpu.VMEM((rows, codes), F32),
        ]
        + shared_scratch(dim, codes, width)
        + tile_scratch(rows, codes),
        compiler_params=settings(),
        cost_estimate=cost(rows, width, dim, codes, 6),
        name="small_backward",
    )(
        table,
        *in_hbm([*feats, *cots]),
        *parts,
        *in_hbm([*params, acc, usage]),
    )


def wide_forward_kernel(lanes, joined, *refs):
    n = len(lanes)
    arrays = 1 if joined else sum(len(lane.runs) for lane in lanes)
    _, feats, noises, params, usage_in, sends, rest = take(
        refs, 1, n, n, 4, 1, arrays, len(refs)
    )
    (usage_ref,), code_scrs, shared, l_scrs = take(rest, 1, n, 3, n)
    step = pl.program_id(0)

    @pl.when(step == 0)
    def _():
        prepare(params, *shared)
        usage_ref[...] = usage_in[0][...]

    if joined:
        strip = code_scrs[0].shape[0]
        targets = [sends[0].at[pl.ds(i * strip, strip)] for i in range(n)]
    else:
        targets = code_targets(lanes, sends, code_scrs)
    for feat_ref, l_scr in zip(feats, l_scrs):
        forward_products(params, shared, feat_ref[...], l_scr)
    usage = usage_ref[...]
    for l_scr, noise_ref, target in zip(l_scrs, noises, targets):
        usage = forward_rows(params, l_scr, noise_ref, target, usage)
    usage_ref[...] = usage
    if not joined:
        keep_codes(step, lanes, sends, code_scrs)


def wide_forward(count, lanes, joined, table, feat, noise, params, usage, tenths):
    dim, codes = params[2].shape
    images, strip, width = feat.shape
    share = images // count
    n, steps = len(lanes), lanes[0].total()
    if joined:
        blocks = [fixed((n * strip, codes))]
        sizes = [n]
    else:
        blocks = [block for lane in lanes for block in lane.blocks((strip, codes))]
        sizes = [run[2] for lane in lanes for run in lane.runs]
    return pl.pallas_call(
        functools.partial(wide_forward_kernel, lanes, joined),
        grid_spec=pltpu.PrefetchScalarGridSpec(
            num_scalar_prefetch=1,
            grid=(steps,),
            in_specs=[lane.image((strip, width), share) for lane in lanes]
            + [lane.image((strip, codes), share) for lane in lanes]
            + [fixed(p.shape) for p in params]
            + [fixed(usage.shape)],
            out_specs=blocks + [fixed(usage.shape)],
            scratch_shapes=[pltpu.VMEM((strip, codes), F32)] * n
            + shared_scratch(dim, codes, width)
            + [pltpu.VMEM((strip, codes), F32)] * n,
        ),
        out_shape=[jax.ShapeDtypeStruct((strip * slots, codes), F32) for slots in sizes]
        + [pltpu.HBM(usage.shape, F32)],
        input_output_aliases={5 + 2 * n: len(sizes)},
        compiler_params=settings(),
        cost_estimate=cost(n * steps * strip, width, dim, codes, tenths),
        name="wide_forward",
    )(table, *in_hbm([feat] * n + [noise] * n + [*params, usage]))


def wide_both_kernel(lanes, share, new, *refs):
    n = len(lanes)
    arrays = sum(len(lane.runs) for lane in lanes)
    table, feats, noises, cots, params, before, sends, rest = take(
        refs, 1, n, n, n, 4, 0 if new else 2, arrays, len(refs)
    )
    (grad_out, acc_ref), code_scrs, (grad_scr, sems), shared, rest = take(
        rest, 2, n, 2, 3, 6 * n
    )
    scrs = take(rest, *[6] * n)
    grads = Gradients(grad_out, grad_scr, sems)
    step, steps = pl.program_id(0), lanes[0].total()

    @pl.when(step == 0)
    def _():
        prepare(params, *shared)
        acc_ref[...] = jnp.zeros(acc_ref.shape, F32) if new else before[0][...]

    grads.ready(step, n)
    targets = code_targets(lanes, sends, code_scrs)
    states = [
        products(params, shared, scr, feat_ref[...], cot_ref[...], True)
        for scr, feat_ref, cot_ref in zip(scrs, feats, cots)
    ]
    usage = acc_ref[136:144]
    for scr, noise_ref, target in zip(scrs, noises, targets):
        usage = both_rows(params, scr, noise_ref, target, usage)
    acc_ref[136:144] = usage
    values = [
        gradients(params, shared, scr, state, acc_ref) for scr, state in zip(scrs, states)
    ]
    grads.store(step, values, [table[0][0, lane.entry(step, share)] for lane in lanes])
    keep_codes(step, lanes, sends, code_scrs)
    grads.end(step, n, steps)


def wide_both(count, lanes, table, feat, noise, cot, params, acc, grad, tenths):
    dim, codes = params[2].shape
    images, strip, width = feat.shape
    share = images // count
    n, steps = len(lanes), lanes[0].total()
    acc_shape = (ACC_ROWS, codes)
    new = acc is None
    sizes = [run[2] for lane in lanes for run in lane.runs]
    return pl.pallas_call(
        functools.partial(wide_both_kernel, lanes, share, new),
        grid_spec=pltpu.PrefetchScalarGridSpec(
            num_scalar_prefetch=1,
            grid=(steps,),
            in_specs=[lane.image((strip, width), share) for lane in lanes]
            + [lane.image((strip, codes), share) for lane in lanes]
            + [lane.image((dim, strip), share) for lane in lanes]
            + [fixed(p.shape) for p in params]
            + ([] if new else [fixed(acc_shape), HBM]),
            out_specs=[block for lane in lanes for block in lane.blocks((strip, codes))]
            + [HBM, fixed(acc_shape)],
            scratch_shapes=[pltpu.VMEM((strip, codes), F32)] * n
            + gradient_scratch(n, strip, width)
            + shared_scratch(dim, codes, width)
            + tile_scratch(strip, codes) * n,
        ),
        out_shape=[jax.ShapeDtypeStruct((strip * slots, codes), F32) for slots in sizes]
        + [pltpu.HBM(feat.shape, F32), pltpu.HBM(acc_shape, F32)],
        input_output_aliases=(
            {} if new else {5 + 3 * n: len(sizes) + 1, 6 + 3 * n: len(sizes)}
        ),
        compiler_params=settings(),
        cost_estimate=cost(n * steps * strip, width, dim, codes, tenths),
        name="wide_both",
    )(
        table,
        *in_hbm([feat] * n + [noise] * n + [cot] * n + [*params]),
        *in_hbm([] if new else [acc, grad]),
    )


def wide_backward_kernel(lanes, share, *refs):
    n = len(lanes)
    arrays = sum(len(lane.runs) for lane in lanes)
    table, feats, cots, parts, params, (acc_in, _), rest = take(
        refs, 1, n, n, arrays, 4, 2, len(refs)
    )
    (grad_out, acc_ref), code_scrs, (grad_scr, sems), shared, rest = take(
        rest, 2, n, 2, 3, 6 * n
    )
    scrs = take(rest, *[6] * n)
    grads = Gradients(grad_out, grad_scr, sems)
    step, steps = pl.program_id(0), lanes[0].total()

    @pl.when(step == 0)
    def _():
        prepare(params, *shared)
        acc_ref[...] = acc_in[...]

    grads.ready(step, n)
    for lane, refs_of, code_scr in zip(lanes, by_lane(parts, lanes), code_scrs):
        if len(lane.runs) > 1:

            def fetch(i, refs_of=refs_of, code_scr=code_scr):
                code_scr[...] = refs_of[i][...]

            lane.each(step, fetch)
    states = [
        products(params, shared, scr, feat_ref[...], cot_ref[...], False)
        for scr, feat_ref, cot_ref in zip(scrs, feats, cots)
    ]
    for scr, code_ref in zip(scrs, code_targets(lanes, parts, code_scrs)):
        backward_rows(scr, code_ref)
    values = [
        gradients(params, shared, scr, state, acc_ref) for scr, state in zip(scrs, states)
    ]
    grads.store(step, values, [table[0][0, lane.entry(step, share)] for lane in lanes])
    grads.end(step, n, steps)


def wide_backward(count, lanes, parts, table, feat, cot, params, acc, grad):
    dim, codes = params[2].shape
    images, strip, width = feat.shape
    share = images // count
    n, steps = len(lanes), lanes[0].total()
    return pl.pallas_call(
        functools.partial(wide_backward_kernel, lanes, share),
        grid_spec=pltpu.PrefetchScalarGridSpec(
            num_scalar_prefetch=1,
            grid=(steps,),
            in_specs=[lane.image((strip, width), share) for lane in lanes]
            + [lane.image((dim, strip), share) for lane in lanes]
            + [block for lane in lanes for block in lane.blocks((strip, codes))]
            + [fixed(p.shape) for p in params]
            + [fixed(acc.shape), HBM],
            out_specs=[HBM, fixed(acc.shape)],
            scratch_shapes=[pltpu.VMEM((strip, codes), F32)] * n
            + gradient_scratch(n, strip, width)
            + shared_scratch(dim, codes, width)
            + tile_scratch(strip, codes) * n,
        ),
        out_shape=[pltpu.HBM(feat.shape, F32), pltpu.HBM(acc.shape, F32)],
        input_output_aliases={5 + 2 * n + len(parts): 1, 6 + 2 * n + len(parts): 0},
        compiler_params=settings(),
        cost_estimate=cost(n * steps * strip, width, dim, codes, 6),
        name="wide_backward",
    )(
        table,
        *in_hbm([feat] * n + [cot] * n),
        *parts,
        *in_hbm([*params, acc, grad]),
    )


def shard_at(index, parts):
    height = 64 // parts
    return pl.ds(pl.multiple_of(index * height, height), height)


def lay_out(params, acc_ref, usage_ref, sum_scr, shards):
    weight_ref, bias_ref, book_ref, scalar_ref = params
    codes = book_ref.shape[1]
    width = weight_ref.shape[1]
    devices = len(shards)
    me = lax.rem(lax.axis_index("dp"), devices)
    precision, _, factor = scalars(scalar_ref)
    book = book_ref[...]
    column = acc_ref[128:129]
    moment = acc_ref[64:128] * (1.0 / precision)
    book_sum = acc_ref[0:64] * (1.0 / factor) + 2.0 * (column * book - moment)
    slope = jnp.sum(
        jnp.sum(book * book, axis=0, keepdims=True) * column, axis=1, keepdims=True
    ) - 2.0 * jnp.sum(jnp.sum(book * moment, axis=0, keepdims=True), axis=1, keepdims=True)
    slope = slope + acc_ref[208:209, 0:1] / (-0.5 * precision)
    usage = jnp.sum(acc_ref[136:144] + usage_ref[...], axis=0, keepdims=True)
    dim = book_ref.shape[0]
    eye = lax.broadcasted_iota(jnp.int32, (dim, dim), 0) == lax.broadcasted_iota(
        jnp.int32, (dim, dim), 1
    )
    bias = acc_ref[144:208, width : width + dim]
    bias = jnp.sum(jnp.where(eye, bias, 0.0), axis=0, keepdims=True)
    rest = codes + width
    sum_scr[:, 0:codes] = book_sum
    sum_scr[:, codes:rest] = acc_ref[144:208, 0:width]
    sum_scr[:, rest : rest + 128] = jnp.broadcast_to(slope, (64, 128))
    rows = codes // 128
    for i in range(rows):
        sum_scr[i : i + 1, rest : rest + 128] = usage[:, i * 128 : (i + 1) * 128]
    sum_scr[rows : rows + 1, rest : rest + dim] = bias
    for i in range(devices):
        shards[i][...] = sum_scr[shard_at(partner(me, i, devices), devices)]


def own_kernel(n, *refs):
    table, feats, noises, cots, params, (acc_in, _), rest = take(
        refs, 1, n, n, n, 4, 2, len(refs)
    )
    (code_ref, grad_out, acc_ref), (grad_scr, sems), shared, rest = take(rest, 3, 2, 3, 6 * n)
    scrs = take(rest, *[6] * n)
    grads = Gradients(grad_out, grad_scr, sems)
    step = pl.program_id(0)

    @pl.when(step == 0)
    def _():
        prepare(params, *shared)
        acc_ref[...] = acc_in[...]

    grads.ready(step, n)
    states = [
        products(params, shared, scr, feat_ref[...], cot_ref[...], True)
        for scr, feat_ref, cot_ref in zip(scrs, feats, cots)
    ]
    usage = acc_ref[136:144]
    for i, (scr, noise_ref) in enumerate(zip(scrs, noises)):
        usage = both_rows(params, scr, noise_ref, code_ref.at[i], usage)
    acc_ref[136:144] = usage
    values = [
        gradients(params, shared, scr, state, acc_ref) for scr, state in zip(scrs, states)
    ]
    grads.store(step, values, [table[0][0, step * n + i] for i in range(n)])
    grads.end(step, n, pl.num_programs(0))


def run_own(count, table, feat, noise, cot, params, acc, grad):
    dim, codes = params[2].shape
    images, strip, width = feat.shape
    share = images // count
    n = 1

    def image(lane, shape):
        return pl.BlockSpec(
            (None, *shape), lambda i, table_ref: (table_ref[0, i * n + lane], 0, 0)
        )

    return pl.pallas_call(
        functools.partial(own_kernel, n),
        grid_spec=pltpu.PrefetchScalarGridSpec(
            num_scalar_prefetch=1,
            grid=(share // n,),
            in_specs=[image(lane, (strip, width)) for lane in range(n)]
            + [image(lane, (strip, codes)) for lane in range(n)]
            + [image(lane, (dim, strip)) for lane in range(n)]
            + [fixed(p.shape) for p in params]
            + [fixed(acc.shape), HBM],
            out_specs=[
                pl.BlockSpec(
                    (n, strip, codes),
                    lambda i, table_ref: (i, table_ref[0, count * share], 0),
                ),
                HBM,
                fixed(acc.shape),
            ],
            scratch_shapes=gradient_scratch(n, strip, width)
            + shared_scratch(dim, codes, width)
            + tile_scratch(strip, codes) * n,
        ),
        out_shape=[
            pltpu.HBM((share, strip * count, codes), F32),
            pltpu.HBM(feat.shape, F32),
            pltpu.HBM(acc.shape, F32),
        ],
        input_output_aliases={5 + 3 * n: 2, 6 + 3 * n: 1},
        compiler_params=settings(),
        cost_estimate=cost(share * strip, width, dim, codes, 10),
        name="own_images",
    )(table, *in_hbm([feat] * n + [noise] * n + [cot] * n + [*params, acc, grad]))


def place_kernel(count, runs, *refs):
    parts = refs[0 : len(runs)]
    out_ref, sem = refs[len(runs) + 1 : len(runs) + 3]
    me = lax.axis_index("space")
    copies = []
    for part, (step, first, slots) in zip(parts, runs):
        strip = part.shape[0] // slots
        row = pl.multiple_of(source(me, step, count) * strip, strip)
        for j in range(slots):
            copies.append(
                pltpu.make_async_copy(
                    part.at[pl.ds(j * strip, strip)],
                    out_ref.at[first + j, pl.ds(row, strip)],
                    sem.at[len(copies)],
                )
            )
    for copy in copies:
        copy.start()
    for copy in copies:
        copy.wait()


def place_wide(count, runs, parts, whole):
    return pl.pallas_call(
        functools.partial(place_kernel, count, runs),
        out_shape=pltpu.HBM(whole.shape, F32),
        in_specs=[VMEM] * len(runs) + [HBM],
        out_specs=HBM,
        scratch_shapes=[pltpu.SemaphoreType.DMA((sum(r[2] for r in runs),))],
        input_output_aliases={len(runs): 0},
        compiler_params=settings(VMEM_LIMIT // 2),
        cost_estimate=pl.CostEstimate(
            flops=0, bytes_accessed=2 * sum(p.size * 4 for p in parts), transcendentals=0
        ),
        name="place_wide",
    )(*[pltpu.with_memory_space_constraint(p, pltpu.VMEM) for p in parts], *in_hbm([whole]))


def join_kernel(count, *refs):
    parts = refs[0:count]
    outs = refs[count:]
    me = lax.axis_index("space")
    for step in range(count):
        here = source(me, step, count)
        base = 0
        for out in outs:
            for j in range(out.shape[0]):
                strip = out.shape[2]
                out[j, here] = parts[step][base : base + strip]
                base += strip


def join_small(count, parts, shapes):
    codes = parts[0].shape[1]
    return pl.pallas_call(
        functools.partial(join_kernel, count),
        out_shape=[
            jax.ShapeDtypeStruct((images // count, count, strip, codes), F32)
            for images, strip, _ in shapes
        ],
        compiler_params=settings(VMEM_LIMIT // 2),
        name="join_small",
    )(*parts)


def tree(values):
    while len(values) > 1:
        values = [
            values[i] + values[i + 1] if i + 1 < len(values) else values[i]
            for i in range(0, len(values), 2)
        ]
    return values[0]


def sum_kernel(*refs):
    refs[-1][...] = tree([ref[...] for ref in refs[:-1]])


def add_all(parts):
    return pl.pallas_call(
        sum_kernel,
        out_shape=jax.ShapeDtypeStruct(parts[0].shape, F32),
        compiler_params=settings(VMEM_LIMIT // 2),
        name="add_parts",
    )(*parts)


def final_kernel(devices, pixels, *refs):
    shards = refs[0:devices]
    weight_ref, bias_ref, book_ref, log_ref, usage_ref = refs[devices : devices + 5]
    weight_out, bias_out, book_out, log_out, usage_out = refs[devices + 5 : devices + 10]
    sum_scr = refs[devices + 10]
    me = lax.rem(lax.axis_index("dp"), devices)
    for i in range(devices):
        sum_scr[shard_at(source(me, i, devices), devices)] = shards[i][...]
    dim, codes = book_ref.shape
    width = weight_ref.shape[1]
    scale = 0.5 * lax.rsqrt(jnp.full((8, 128), pixels, F32))[0:1, 0:1]
    book_out[...] = 0.5 * book_ref[...] + scale * sum_scr[:, 0:codes]
    rest = codes + width
    weight_out[...] = 0.5 * weight_ref[...] + scale * sum_scr[:, codes:rest]
    rows = codes // 128
    bias_out[...] = 0.5 * bias_ref[...] + scale * sum_scr[rows : rows + 1, rest : rest + dim]
    usage = jnp.concatenate(
        [sum_scr[i : i + 1, rest : rest + 128] for i in range(rows)], axis=1
    )
    usage_out[...] = 0.5 * usage_ref[...] + 0.5 * (codes / pixels) * usage
    log_out[...] = 0.5 * log_ref[...] + scale * sum_scr[rows + 1 : rows + 2, rest : rest + 1]


def finish(devices, pixels, shards, weight, bias, book, log, usage):
    outs = (weight.T, bias.reshape(1, -1), book.T, log.reshape(1, 1), usage.reshape(1, -1))
    outs = pl.pallas_call(
        functools.partial(final_kernel, devices, pixels),
        out_shape=[jax.ShapeDtypeStruct(out.shape, F32) for out in outs],
        scratch_shapes=[pltpu.VMEM((64, LANES), F32)],
        compiler_params=settings(VMEM_LIMIT // 2),
        name="new_averages",
    )(*shards, *outs)
    return outs[0].T, outs[1].reshape(-1), outs[2].T, outs[3].reshape(-1), outs[4].reshape(-1)


def exchange(value, bit, size, pairs):
    while bit < size:
        value = value + pairs(value, bit)
        bit = 2 * bit
    return value


def per_device(
    feat_small,
    feat_mid,
    feat_wide,
    noise_small,
    noise_mid,
    noise_wide,
    cot_small,
    cot_mid,
    cot_wide,
    order_small,
    order_mid,
    order_wide,
    weight,
    bias,
    book,
    log,
    heat,
    weight_mean,
    bias_mean,
    book_mean,
    log_mean,
    usage_mean,
):
    count = lax.axis_size("space")
    devices = lax.axis_size("dp")
    params = (weight.T, bias.reshape(1, -1), book.T, log, heat)
    feats = (feat_small, feat_mid, feat_wide)
    pixels = sum(f.shape[0] * f.shape[1] for f in feats) * count * devices
    share = feat_wide.shape[0] // count
    cot_wide = jnp.swapaxes(cot_wide, 1, 2)

    def send(values):
        return [lax.ppermute(v, "space", route(i + 1, count)) for i, v in enumerate(values)]

    def after(part, codes):
        return lax.optimization_barrier((part, codes))

    turned = devices % 2 == 0

    def around(codes, step):
        turn = 1 if turned else 0
        pairs = [
            (i * count + j, (i ^ turn) * count + k)
            for i in range(devices)
            for j, k in route(step, count)
        ]
        return lax.ppermute(codes, ("dp", "space"), pairs)

    def back(codes):
        if not turned:
            return codes
        return lax.ppermute(codes, "dp", [(i, i ^ 1) for i in range(devices)])

    orders = (order_small, order_mid, order_wide)
    *small, table, usage, scalar = small_forward(
        count, orders, feats[0:2], (noise_small, noise_mid), params
    )
    params = (*params[0:3], scalar)
    small_arrived = send(small[1:])
    near = min(4, devices)
    last = count - 1
    early = [(step, 0, 1) for step in range(1, count)]
    direct = [(step, 1, share - 1) for step in range(1, last)]
    late = [(last, 1, share - 2), (last, share - 1, 1)]
    *early_codes, usage = wide_forward(
        count, split(early, 3), False, table, feat_wide, noise_wide, params, usage, 4
    )
    leaving = list(early_codes)
    small_arrived[-1], leaving[-1] = after(small_arrived[-1], leaving[-1])
    early_arrived = send(leaving)
    *codes, grad, acc = wide_both(
        count, split(direct, 2), table, feat_wide, noise_wide, cot_wide, params, None, None, 10
    )
    direct_arrived = send(codes)
    codes_small, codes_mid = join_small(
        count, [small[0]] + small_arrived, [f.shape for f in feats[0:2]]
    )
    codes_small, codes_mid, acc = lax.optimization_barrier((codes_small, codes_mid, acc))
    late_codes, turned_codes, grad, acc = wide_both(
        count, [Lane(late)], table, feat_wide, noise_wide, cot_wide, params, acc, grad, 2
    )
    early_arrived[-1], late_codes = after(early_arrived[-1], late_codes)
    late_arrived = lax.ppermute(late_codes, "space", route(last, count))
    early_arrived[0], turned_codes = after(early_arrived[0], turned_codes)
    turned_arrived = around(turned_codes, last)
    early_arrived, acc = lax.optimization_barrier((early_arrived, acc))
    whole, grad, acc = run_own(
        count, table, feat_wide, noise_wide, cot_wide, params, acc, grad
    )
    whole = place_wide(count, early, early_arrived, whole)
    grad, acc = wide_backward(
        count, split(early, 3), early_codes, table, feat_wide, cot_wide, params, acc, grad
    )
    grad_small, grad_mid, *shards = small_backward(
        count,
        near,
        feat_wide.shape[0],
        table,
        feats[0:2],
        (cot_small, cot_mid),
        small,
        params,
        acc,
        usage,
    )
    group = [
        [(i, i - i % near + partner(i % near, step, near)) for i in range(devices)]
        for step in range(near)
    ]
    parts = [lax.ppermute(shards[i], "dp", group[i]) for i in range(1, near)]
    mine = add_all([shards[0]] + parts)

    def along(value, offset):
        return lax.ppermute(value, "dp", [(i, i ^ offset) for i in range(devices)])

    def across(value, offset):
        turn = near if devices > near else 0
        pairs = [
            (i * count + j, (i ^ turn) * count + (j ^ offset))
            for i in range(devices)
            for j in range(count)
        ]
        return lax.ppermute(value, ("dp", "space"), pairs)

    mine = exchange(mine, near, devices, along)
    turned_arrived, mine = lax.optimization_barrier((turned_arrived, mine))
    turned_arrived = back(turned_arrived)
    mine = exchange(mine, 1, count, across)
    turned_arrived, mine = lax.optimization_barrier((turned_arrived, mine))
    shards = [mine] + [lax.ppermute(mine, "dp", group[i]) for i in range(1, near)]
    updated = finish(
        near, pixels, shards, weight_mean, bias_mean, book_mean, log_mean, usage_mean
    )
    whole = place_wide(count, late[1:], [turned_arrived], whole)
    for run, part in zip(direct + late[:1], [*direct_arrived, late_arrived]):
        whole = place_wide(count, [run], [part], whole)
    codes = whole.shape[2]
    return (
        codes_small.reshape(codes_small.shape[0], -1, codes),
        codes_mid.reshape(codes_mid.shape[0], -1, codes),
        whole,
        grad_small,
        grad_mid,
        grad,
        *updated,
    )


def solution(mesh):
    strips = P("dp", "space", None)
    placed = (strips,) * 9 + (P("dp", None),) * 3 + (P(),) * 10
    return jax.shard_map(
        per_device,
        mesh=mesh,
        in_specs=placed,
        out_specs=(P(("dp", "space"), None, None),) * 3 + (strips,) * 3 + (P(),) * 5,
        check_vma=False,
    )
```

```python
import functools

import jax
import jax.numpy as jnp
from jax import lax
from jax.experimental import pallas as pl
from jax.experimental.pallas import tpu as pltpu
from jax.sharding import PartitionSpec as P

F32 = jnp.float32
BF16 = jnp.bfloat16
VMEM_LIMIT = 24 * 1024 * 1024
ACC_ROWS = 64 + 64 + 8 + 8 + 64 + 8
LANES = 896


def partner(index, step, count):
    if count & (count - 1) == 0:
        return index ^ step
    return lax.rem(index + step, count)


def route(step, count):
    if count & (count - 1) == 0:
        return [(i, i ^ step) for i in range(count)]
    return [(i, (i + step) % count) for i in range(count)]


def source(index, step, count):
    if count & (count - 1) == 0:
        return index ^ step
    return lax.rem(index + (count - step), count)


def in_hbm(arrays):
    return [pltpu.with_memory_space_constraint(a, pltpu.HBM) for a in arrays]


def halves(x):
    high = x.astype(BF16)
    return high, (x - high.astype(F32)).astype(BF16)


def dot(left, right, left_dim=1, right_dim=0):
    return lax.dot_general(
        left, right, (((left_dim,), (right_dim,)), ((), ())), preferred_element_type=F32
    )


def set_scalars(log_ref, heat_ref, out_ref):
    precision = jnp.exp(jnp.full((8, 128), log_ref[0], F32))
    heat = jnp.full((8, 128), heat_ref[0], F32)
    row = lax.broadcasted_iota(jnp.int32, (8, 128), 0)
    factor = -0.5 * precision / heat
    out_ref[...] = jnp.where(row == 0, precision, jnp.where(row == 1, 1.0 / heat, factor))


def scalars(ref):
    return ref[0:1, 0:1], ref[1:2, 0:1], ref[2:3, 0:1]


def beside(x):
    high = x.astype(BF16).astype(F32)
    lane = lax.broadcasted_iota(jnp.int32, x.shape, 1)
    return jnp.where(lane < x.shape[1] // 2, high, x - high).astype(BF16)


def doubled(x):
    return x + pltpu.roll(x, x.shape[1] // 2, 1)


def twice(x):
    return jnp.concatenate([x, x], axis=1)


def prepare(refs, mix_scr, book_scr, norm_scr, books_scr, weight_scr):
    weight_ref, bias_ref, book_ref, scalar_ref = refs
    dim, codes = book_ref.shape
    precision, _, _ = scalars(scalar_ref)
    book = book_ref[...]
    high, low = halves(book)
    for i, part in enumerate((high, high, low, low)):
        book_scr[i * dim : (i + 1) * dim] = part
    norm = -0.5 * precision * jnp.sum(book * book, axis=0, keepdims=True)
    norm_scr[...] = jnp.broadcast_to(norm, norm_scr.shape)
    books_scr[:, 0 : 2 * dim] = beside(twice(book.T))
    books_scr[:, 2 * dim : 2 * dim + 128] = jnp.ones((codes, 128), BF16)
    weight = weight_ref[...]
    high, low = halves(weight)
    for i, part in enumerate((high, high, low, low)):
        weight_scr[i * dim : (i + 1) * dim] = part
    mix_scr[...] = beside(twice(weight.T))


def latents(refs, shared, feat):
    precision, _, _ = scalars(refs[3])
    mix = shared[0][...]
    fh, fl = halves(feat)
    z = doubled(dot(fh, mix) + dot(fl, mix)) + twice(refs[1][...])
    square = -0.25 * precision * jnp.sum(z * z, axis=1, keepdims=True)
    return fh, fl, z, square


def over_rows(rows, body, carry):
    step = next(s for s in (32, 16, 8) if rows % s == 0)

    def at(i, carry):
        return body(pl.ds(pl.multiple_of(i * step, step), step), carry)

    return lax.fori_loop(0, rows // step, at, carry, unroll=True)


def folded(x):
    return jnp.sum(x.reshape(x.shape[0] // 8, 8, x.shape[1]), axis=0)


def normal(e):
    return e * (1.0 / jnp.sum(e, axis=1, keepdims=True))


def shifted(logits):
    return logits - jnp.max(logits, axis=1, keepdims=True)


def forward_products(refs, shared, feat, l_scr):
    precision, _, _ = scalars(refs[3])
    _, _, z, square = latents(refs, shared, feat)
    p = dot(twice(beside(precision * z)), shared[1][...])
    l_scr[0 : feat.shape[0]] = p + (square + shared[2][0:1])


def forward_rows(refs, l_scr, noise_ref, code_ref, usage):
    _, cold, _ = scalars(refs[3])

    def body(at, usage):
        logits = shifted(l_scr[at])
        code_ref[at] = normal(jnp.exp((logits + noise_ref[at]) * cold))
        return usage + folded(normal(jnp.exp(logits)))

    return over_rows(code_ref.shape[0], body, usage)


def products(refs, shared, scr, feat, cot, forward):
    l_scr, g_scr = scr[0:2]
    rows = feat.shape[0]
    precision, _, factor = scalars(refs[3])
    fh, fl, z, square = latents(refs, shared, feat)
    zz = beside(precision * z)
    ct = jnp.concatenate(halves(factor * cot), axis=0)
    cc = twice(ct.T)
    if forward:
        p = dot(jnp.concatenate([twice(zz), cc], axis=0), shared[1][...])
        l_scr[0:rows] = p[0:rows] + (square + shared[2][0:1])
        g_scr[0:rows] = p[rows : 2 * rows]
    else:
        g_scr[0:rows] = dot(cc, shared[1][...])
    return fh, fl, z, square, zz, ct


def both_rows(refs, scr, noise_ref, code_ref, usage):
    l_scr, g_scr, wh_scr, wl_scr, gh_scr, gl_scr = scr
    _, cold, _ = scalars(refs[3])

    def body(at, usage):
        logits = shifted(l_scr[at])
        e = jnp.exp((logits + noise_ref[at]) * cold)
        gw = g_scr[at]
        scale = 1.0 / jnp.sum(e, axis=1, keepdims=True)
        inner = jnp.sum(e * gw, axis=1, keepdims=True) * scale
        w = e * scale
        code_ref[at] = w
        gd = w * (gw - inner)
        wh_scr[at], wl_scr[at] = halves(w)
        gh_scr[at], gl_scr[at] = halves(gd)
        return usage + folded(normal(jnp.exp(logits)))

    return over_rows(code_ref.shape[0], body, usage)


def backward_rows(scr, code_ref):
    _, g_scr, wh_scr, wl_scr, gh_scr, gl_scr = scr

    def body(at, carry):
        w = code_ref[at]
        gw = g_scr[at]
        gd = w * (gw - jnp.sum(w * gw, axis=1, keepdims=True))
        wh_scr[at], wl_scr[at] = halves(w)
        gh_scr[at], gl_scr[at] = halves(gd)
        return carry

    over_rows(code_ref.shape[0], body, 0)


def gradients(refs, shared, scr, state, acc_ref):
    books_scr, weight_scr = shared[3:5]
    wh_scr, wl_scr, gh_scr, gl_scr = scr[2:6]
    fh, fl, z, square, zz, ct = state
    rows, feats = fh.shape
    dim, codes = refs[2].shape
    wh, wl = wh_scr[0:rows], wl_scr[0:rows]
    gh, gl = gh_scr[0:rows], gl_scr[0:rows]
    p = dot(ct, wh)
    acc_ref[0:64] += p[0:dim] + p[dim : 2 * dim] + dot(ct[0:dim], wl)
    left = jnp.concatenate([zz.T, jnp.ones((16, rows), BF16)], axis=0)
    p = dot(left, gh) + dot(left, gl)
    acc_ref[64:128] += p[0:dim] + p[dim : 2 * dim]
    acc_ref[128:136] += p[2 * dim : 2 * dim + 8]
    books = books_scr[...]
    p = dot(gh, books) + dot(gl, books)
    row_d = p[:, 2 * dim : 2 * dim + 128]
    gz = 2.0 * (row_d * z - doubled(p[:, 0 : 2 * dim]))
    gg = beside(gz)
    gt = gg.T
    p = dot(gt, fh)
    acc_ref[144:208, 0:feats] += p[0:dim] + p[dim : 2 * dim] + dot(gt[0:dim], fl)
    acc_ref[208:216, 0:128] += folded(gz)
    acc_ref[208:216, 128:256] += folded(square * row_d)
    return dot(twice(gg), weight_scr[...])


def shared_scratch(dim, codes, feats):
    return [
        pltpu.VMEM((feats, 2 * dim), BF16),
        pltpu.VMEM((4 * dim, codes), BF16),
        pltpu.VMEM((8, codes), F32),
        pltpu.VMEM((codes, 2 * dim + 128), BF16),
        pltpu.VMEM((4 * dim, feats), BF16),
    ]


def tile_scratch(rows, codes):
    return [pltpu.VMEM((rows, codes), F32)] * 2 + [pltpu.VMEM((rows, codes), BF16)] * 4


def settings(limit=VMEM_LIMIT):
    return pltpu.CompilerParams(vmem_limit_bytes=limit)


def cost(rows, feats, dim, codes, tenths):
    return pl.CostEstimate(
        flops=rows * 24 * tenths * (5 * dim * codes + 3 * dim * feats) // 10,
        bytes_accessed=4 * rows * (2 * feats + 2 * codes + dim),
        transcendentals=2 * rows * codes,
    )


SMEM = pl.BlockSpec(memory_space=pltpu.SMEM)
VMEM = pl.BlockSpec(memory_space=pltpu.VMEM)
HBM = pl.BlockSpec(memory_space=pltpu.HBM)


def fixed(shape):
    return pl.BlockSpec(shape, lambda *_: (0,) * len(shape))


class Lane:
    def __init__(self, runs):
        self.runs = list(runs)
        self.bounds = [0]
        for _, _, slots in self.runs:
            self.bounds.append(self.bounds[-1] + slots)

    def total(self):
        return self.bounds[-1]

    def entry(self, i, share):
        entry = 0
        for (step, first, _), start in zip(self.runs, self.bounds):
            here = step * share + first + i - start
            entry = here if start == 0 else jnp.where(i >= start, here, entry)
        return entry

    def image(self, shape, share):
        return pl.BlockSpec(
            (None, *shape), lambda i, table_ref: (table_ref[0, self.entry(i, share)], 0, 0)
        )

    def blocks(self, shape):
        return [
            pl.BlockSpec(
                shape,
                lambda i, _, start=start, last=slots - 1: (jnp.clip(i - start, 0, last), 0),
            )
            for (_, _, slots), start in zip(self.runs, self.bounds)
        ]

    def each(self, step, body):
        for i, (low, high) in enumerate(zip(self.bounds, self.bounds[1:])):
            pl.when((step >= low) & (step < high))(functools.partial(body, i))


def split(runs, ways):
    whole = Lane(runs)
    lanes, current = [], []
    for run in whole.runs:
        current.append(run)
        if Lane(current).total() * ways == whole.total():
            lanes.append(Lane(current))
            current = []
    return lanes if len(lanes) == ways and not current else [whole]


def take(refs, *sizes):
    groups, at = [], 0
    for size in sizes:
        groups.append(refs[at : at + size])
        at += size
    return groups


def by_lane(refs, lanes):
    return take(refs, *[len(lane.runs) for lane in lanes])


def keep_codes(step, lanes, sends, code_scrs):
    for lane, refs, code_scr in zip(lanes, by_lane(sends, lanes), code_scrs):
        if len(lane.runs) > 1:

            def keep(i, refs=refs, code_scr=code_scr):
                refs[i][...] = code_scr[...]

            lane.each(step, keep)


def code_targets(lanes, sends, code_scrs):
    return [
        refs[0] if len(lane.runs) == 1 else code_scr
        for lane, refs, code_scr in zip(lanes, by_lane(sends, lanes), code_scrs)
    ]


class Gradients:
    def __init__(self, out_ref, scr, sems):
        self.out_ref, self.scr, self.sems = out_ref, scr, sems

    def copy(self, lane, slot, image):
        return pltpu.make_async_copy(
            self.scr.at[lane, slot], self.out_ref.at[image], self.sems.at[lane, slot]
        )

    def ready(self, step, lanes):
        @pl.when(step >= 2)
        def _():
            for lane in range(lanes):
                self.copy(lane, lax.rem(step, 2), 0).wait()

    def store(self, step, values, images):
        slot = lax.rem(step, 2)
        for lane, (value, image) in enumerate(zip(values, images)):
            self.scr[lane, slot] = value
            self.copy(lane, slot, image).start()

    def end(self, step, lanes, steps):
        @pl.when(step == steps - 1)
        def _():
            for lane in range(lanes):
                for slot in range(min(2, steps)):
                    self.copy(lane, slot, 0).wait()


def gradient_scratch(lanes, strip, width):
    return [pltpu.VMEM((lanes, 2, strip, width), F32), pltpu.SemaphoreType.DMA((lanes, 2))]


def places_of(table_ref, wide, shapes, groups, count):
    places = []
    base = 0
    entry = wide + 1
    for _ in range(count):
        for size in range(2):
            strip = shapes[size][1]
            for _ in range(groups[size]):
                places.append((size, table_ref[0, entry], base, strip))
                base += strip
                entry += 1
    return places, base


def small_forward_kernel(count, groups, *refs):
    sources = refs[0:10]
    log_ref, heat_ref = refs[10:12]
    sends = refs[12 : 12 + count]
    table_ref, usage_ref, scalar_ref = refs[12 + count : 15 + count]
    held = refs[15 + count : 25 + count]
    sems, feat_scr, noise_scr = refs[25 + count : 28 + count]
    scr = refs[28 + count :]
    copies = [
        pltpu.make_async_copy(there, here, sems.at[i])
        for i, (there, here) in enumerate(zip(sources, held))
    ]
    for copy in copies:
        copy.start()
    orders, feats, noises, params = held[0:3], held[3:5], held[5:7], (*held[7:10], scalar_ref)
    me = lax.axis_index("space")
    set_scalars(log_ref, heat_ref, scalar_ref)
    for copy in copies[7:10]:
        copy.wait()
    shared, tile_scr = take(scr, 5, 6)
    prepare(params, *shared)
    for copy in copies[0:5]:
        copy.wait()
    wide = orders[2].shape[1]
    share = wide // count
    entry = wide + 1
    table_ref[0, wide] = me
    for step in range(count):
        there = partner(me, step, count)
        for j in range(share):
            table_ref[0, step * share + j] = orders[2][0, there * share + j]
        for size in range(2):
            for j in range(groups[size]):
                table_ref[0, entry] = orders[size][0, there * groups[size] + j]
                entry += 1
    places, _ = places_of(table_ref, wide, [f.shape for f in feats], groups, count)
    for size, image, at, strip in places:
        feat_scr[at : at + strip] = feats[size][image]
    for copy in copies[5:7]:
        copy.wait()
    for size, image, at, strip in places:
        noise_scr[at : at + strip] = noises[size][image]
    forward_products(params, shared, feat_scr[...], tile_scr[0])
    usage = jnp.zeros(usage_ref.shape, F32)
    part = sends[0].shape[0]
    for step in range(count):
        rows = pl.ds(step * part, part)
        usage = forward_rows(
            params, tile_scr[0].at[rows], noise_scr.at[rows], sends[step], usage
        )
    usage_ref[...] = usage


def small_forward(count, orders, feats, noises, params):
    dim, codes = params[2].shape
    width = feats[0].shape[2]
    groups = tuple(f.shape[0] // count for f in feats)
    part = sum(g * f.shape[1] for g, f in zip(groups, feats))
    rows = part * count
    arrays = [*orders, *feats, *noises, *params[0:3]]
    return pl.pallas_call(
        functools.partial(small_forward_kernel, count, groups),
        out_shape=[jax.ShapeDtypeStruct((part, codes), F32)] * count
        + [
            jax.ShapeDtypeStruct((1, sum(o.shape[1] for o in orders) + 1), jnp.int32),
            pltpu.HBM((8, codes), F32),
            pltpu.HBM((8, 128), F32),
        ],
        in_specs=[HBM] * 10 + [SMEM] * 2,
        out_specs=[VMEM] * count + [SMEM, VMEM, VMEM],
        scratch_shapes=[
            (pltpu.SMEM if i < 3 else pltpu.VMEM)(a.shape, a.dtype)
            for i, a in enumerate(arrays)
        ]
        + [
            pltpu.SemaphoreType.DMA((10,)),
            pltpu.VMEM((rows, width), F32),
            pltpu.VMEM((rows, codes), F32),
        ]
        + shared_scratch(dim, codes, width)
        + tile_scratch(rows, codes),
        compiler_params=settings(),
        cost_estimate=cost(rows, width, dim, codes, 4),
        name="small_forward",
    )(*in_hbm(arrays), *params[3:5])


def small_backward_kernel(count, devices, wide, groups, *refs):
    table_ref = refs[0]
    feats, cots = refs[1:3], refs[3:5]
    parts = refs[5 : 5 + count]
    params = refs[5 + count : 9 + count]
    acc_in, usage_ref = refs[9 + count : 11 + count]
    grads = refs[11 + count : 13 + count]
    shards = refs[13 + count : 13 + count + devices]
    rest = refs[13 + count + devices :]
    acc_ref, sum_scr, feat_scr, cot_scr, code_scr = rest[0:5]
    scr = rest[5:]
    places, base = places_of(table_ref, wide, [f.shape for f in feats], groups, count)
    for size, image, at, strip in places:
        feat_scr[at : at + strip] = feats[size][image]
        cot_scr[at : at + strip] = cots[size][image]
    part = base // count
    for step in range(count):
        code_scr[step * part : (step + 1) * part] = parts[step][...]
    shared, tile_scr = take(scr, 5, 6)
    prepare(params, *shared)
    acc_ref[...] = acc_in[...]
    state = products(params, shared, tile_scr, feat_scr[...], cot_scr[...].T, False)
    backward_rows(tile_scr, code_scr)
    feat_scr[...] = gradients(params, shared, tile_scr, state, acc_ref)
    lay_out(params, acc_ref, usage_ref, sum_scr, shards)
    for size, image, at, strip in places:
        grads[size][image] = feat_scr[at : at + strip]


def small_backward(count, devices, wide, table, feats, cots, parts, params, acc, usage):
    dim, codes = params[2].shape
    width = feats[0].shape[2]
    groups = tuple(f.shape[0] // count for f in feats)
    rows = parts[0].shape[0] * count
    return pl.pallas_call(
        functools.partial(small_backward_kernel, count, devices, wide, groups),
        out_shape=[pltpu.HBM(f.shape, F32) for f in feats]
        + [jax.ShapeDtypeStruct((64 // devices, LANES), F32)] * devices,
        in_specs=[SMEM] + [VMEM] * (10 + count),
        out_specs=[VMEM] * (2 + devices),
        scratch_shapes=[
            pltpu.VMEM(acc.shape, F32),
            pltpu.VMEM((64, LANES), F32),
            pltpu.VMEM((rows, width), F32),
            pltpu.VMEM((rows, dim), F32),
            pltpu.VMEM((rows, codes), F32),
        ]
        + shared_scratch(dim, codes, width)
        + tile_scratch(rows, codes),
        compiler_params=settings(),
        cost_estimate=cost(rows, width, dim, codes, 6),
        name="small_backward",
    )(
        table,
        *in_hbm([*feats, *cots]),
        *parts,
        *in_hbm([*params, acc, usage]),
    )


def wide_forward_kernel(lanes, joined, *refs):
    n = len(lanes)
    arrays = 1 if joined else sum(len(lane.runs) for lane in lanes)
    _, feats, noises, params, usage_in, sends, rest = take(
        refs, 1, n, n, 4, 1, arrays, len(refs)
    )
    (usage_ref,), code_scrs, shared, l_scrs = take(rest, 1, n, 5, n)
    step = pl.program_id(0)

    @pl.when(step == 0)
    def _():
        prepare(params, *shared)
        usage_ref[...] = usage_in[0][...]

    if joined:
        strip = code_scrs[0].shape[0]
        targets = [sends[0].at[pl.ds(i * strip, strip)] for i in range(n)]
    else:
        targets = code_targets(lanes, sends, code_scrs)
    for feat_ref, l_scr in zip(feats, l_scrs):
        forward_products(params, shared, feat_ref[...], l_scr)
    usage = usage_ref[...]
    for l_scr, noise_ref, target in zip(l_scrs, noises, targets):
        usage = forward_rows(params, l_scr, noise_ref, target, usage)
    usage_ref[...] = usage
    if not joined:
        keep_codes(step, lanes, sends, code_scrs)


def wide_forward(count, lanes, joined, table, feat, noise, params, usage, tenths):
    dim, codes = params[2].shape
    images, strip, width = feat.shape
    share = images // count
    n, steps = len(lanes), lanes[0].total()
    if joined:
        blocks = [fixed((n * strip, codes))]
        sizes = [n]
    else:
        blocks = [block for lane in lanes for block in lane.blocks((strip, codes))]
        sizes = [run[2] for lane in lanes for run in lane.runs]
    return pl.pallas_call(
        functools.partial(wide_forward_kernel, lanes, joined),
        grid_spec=pltpu.PrefetchScalarGridSpec(
            num_scalar_prefetch=1,
            grid=(steps,),
            in_specs=[lane.image((strip, width), share) for lane in lanes]
            + [lane.image((strip, codes), share) for lane in lanes]
            + [fixed(p.shape) for p in params]
            + [fixed(usage.shape)],
            out_specs=blocks + [fixed(usage.shape)],
            scratch_shapes=[pltpu.VMEM((strip, codes), F32)] * n
            + shared_scratch(dim, codes, width)
            + [pltpu.VMEM((strip, codes), F32)] * n,
        ),
        out_shape=[jax.ShapeDtypeStruct((strip * slots, codes), F32) for slots in sizes]
        + [pltpu.HBM(usage.shape, F32)],
        input_output_aliases={5 + 2 * n: len(sizes)},
        compiler_params=settings(),
        cost_estimate=cost(n * steps * strip, width, dim, codes, tenths),
        name="wide_forward",
    )(table, *in_hbm([feat] * n + [noise] * n + [*params, usage]))


def wide_both_kernel(lanes, share, new, *refs):
    n = len(lanes)
    arrays = sum(len(lane.runs) for lane in lanes)
    table, feats, noises, cots, params, before, sends, rest = take(
        refs, 1, n, n, n, 4, 0 if new else 2, arrays, len(refs)
    )
    (grad_out, acc_ref), code_scrs, (grad_scr, sems), shared, rest = take(
        rest, 2, n, 2, 5, 6 * n
    )
    scrs = take(rest, *[6] * n)
    grads = Gradients(grad_out, grad_scr, sems)
    step, steps = pl.program_id(0), lanes[0].total()

    @pl.when(step == 0)
    def _():
        prepare(params, *shared)
        acc_ref[...] = jnp.zeros(acc_ref.shape, F32) if new else before[0][...]

    grads.ready(step, n)
    targets = code_targets(lanes, sends, code_scrs)
    states = [
        products(params, shared, scr, feat_ref[...], cot_ref[...], True)
        for scr, feat_ref, cot_ref in zip(scrs, feats, cots)
    ]
    usage = acc_ref[136:144]
    for scr, noise_ref, target in zip(scrs, noises, targets):
        usage = both_rows(params, scr, noise_ref, target, usage)
    acc_ref[136:144] = usage
    values = [
        gradients(params, shared, scr, state, acc_ref) for scr, state in zip(scrs, states)
    ]
    grads.store(step, values, [table[0][0, lane.entry(step, share)] for lane in lanes])
    keep_codes(step, lanes, sends, code_scrs)
    grads.end(step, n, steps)


def wide_both(count, lanes, table, feat, noise, cot, params, acc, grad, tenths):
    dim, codes = params[2].shape
    images, strip, width = feat.shape
    share = images // count
    n, steps = len(lanes), lanes[0].total()
    acc_shape = (ACC_ROWS, codes)
    new = acc is None
    sizes = [run[2] for lane in lanes for run in lane.runs]
    return pl.pallas_call(
        functools.partial(wide_both_kernel, lanes, share, new),
        grid_spec=pltpu.PrefetchScalarGridSpec(
            num_scalar_prefetch=1,
            grid=(steps,),
            in_specs=[lane.image((strip, width), share) for lane in lanes]
            + [lane.image((strip, codes), share) for lane in lanes]
            + [lane.image((dim, strip), share) for lane in lanes]
            + [fixed(p.shape) for p in params]
            + ([] if new else [fixed(acc_shape), HBM]),
            out_specs=[block for lane in lanes for block in lane.blocks((strip, codes))]
            + [HBM, fixed(acc_shape)],
            scratch_shapes=[pltpu.VMEM((strip, codes), F32)] * n
            + gradient_scratch(n, strip, width)
            + shared_scratch(dim, codes, width)
            + tile_scratch(strip, codes) * n,
        ),
        out_shape=[jax.ShapeDtypeStruct((strip * slots, codes), F32) for slots in sizes]
        + [pltpu.HBM(feat.shape, F32), pltpu.HBM(acc_shape, F32)],
        input_output_aliases=(
            {} if new else {5 + 3 * n: len(sizes) + 1, 6 + 3 * n: len(sizes)}
        ),
        compiler_params=settings(),
        cost_estimate=cost(n * steps * strip, width, dim, codes, tenths),
        name="wide_both",
    )(
        table,
        *in_hbm([feat] * n + [noise] * n + [cot] * n + [*params]),
        *in_hbm([] if new else [acc, grad]),
    )


def wide_backward_kernel(lanes, share, *refs):
    n = len(lanes)
    arrays = sum(len(lane.runs) for lane in lanes)
    table, feats, cots, parts, params, (acc_in, _), rest = take(
        refs, 1, n, n, arrays, 4, 2, len(refs)
    )
    (grad_out, acc_ref), code_scrs, (grad_scr, sems), shared, rest = take(
        rest, 2, n, 2, 5, 6 * n
    )
    scrs = take(rest, *[6] * n)
    grads = Gradients(grad_out, grad_scr, sems)
    step, steps = pl.program_id(0), lanes[0].total()

    @pl.when(step == 0)
    def _():
        prepare(params, *shared)
        acc_ref[...] = acc_in[...]

    grads.ready(step, n)
    for lane, refs_of, code_scr in zip(lanes, by_lane(parts, lanes), code_scrs):
        if len(lane.runs) > 1:

            def fetch(i, refs_of=refs_of, code_scr=code_scr):
                code_scr[...] = refs_of[i][...]

            lane.each(step, fetch)
    states = [
        products(params, shared, scr, feat_ref[...], cot_ref[...], False)
        for scr, feat_ref, cot_ref in zip(scrs, feats, cots)
    ]
    for scr, code_ref in zip(scrs, code_targets(lanes, parts, code_scrs)):
        backward_rows(scr, code_ref)
    values = [
        gradients(params, shared, scr, state, acc_ref) for scr, state in zip(scrs, states)
    ]
    grads.store(step, values, [table[0][0, lane.entry(step, share)] for lane in lanes])
    grads.end(step, n, steps)


def wide_backward(count, lanes, parts, table, feat, cot, params, acc, grad):
    dim, codes = params[2].shape
    images, strip, width = feat.shape
    share = images // count
    n, steps = len(lanes), lanes[0].total()
    return pl.pallas_call(
        functools.partial(wide_backward_kernel, lanes, share),
        grid_spec=pltpu.PrefetchScalarGridSpec(
            num_scalar_prefetch=1,
            grid=(steps,),
            in_specs=[lane.image((strip, width), share) for lane in lanes]
            + [lane.image((dim, strip), share) for lane in lanes]
            + [block for lane in lanes for block in lane.blocks((strip, codes))]
            + [fixed(p.shape) for p in params]
            + [fixed(acc.shape), HBM],
            out_specs=[HBM, fixed(acc.shape)],
            scratch_shapes=[pltpu.VMEM((strip, codes), F32)] * n
            + gradient_scratch(n, strip, width)
            + shared_scratch(dim, codes, width)
            + tile_scratch(strip, codes) * n,
        ),
        out_shape=[pltpu.HBM(feat.shape, F32), pltpu.HBM(acc.shape, F32)],
        input_output_aliases={5 + 2 * n + len(parts): 1, 6 + 2 * n + len(parts): 0},
        compiler_params=settings(),
        cost_estimate=cost(n * steps * strip, width, dim, codes, 6),
        name="wide_backward",
    )(
        table,
        *in_hbm([feat] * n + [cot] * n),
        *parts,
        *in_hbm([*params, acc, grad]),
    )


def shard_at(index, parts):
    height = 64 // parts
    return pl.ds(pl.multiple_of(index * height, height), height)


def lay_out(params, acc_ref, usage_ref, sum_scr, shards):
    weight_ref, bias_ref, book_ref, scalar_ref = params
    codes = book_ref.shape[1]
    width = weight_ref.shape[1]
    devices = len(shards)
    me = lax.rem(lax.axis_index("dp"), devices)
    precision, _, factor = scalars(scalar_ref)
    book = book_ref[...]
    column = acc_ref[128:129]
    moment = acc_ref[64:128] * (1.0 / precision)
    book_sum = acc_ref[0:64] * (1.0 / factor) + 2.0 * (column * book - moment)
    slope = jnp.sum(
        jnp.sum(book * book, axis=0, keepdims=True) * column, axis=1, keepdims=True
    ) - 2.0 * jnp.sum(jnp.sum(book * moment, axis=0, keepdims=True), axis=1, keepdims=True)
    dim = book_ref.shape[0]
    bias = jnp.sum(acc_ref[208:216, 0:dim], axis=0, keepdims=True)
    squares = jnp.sum(acc_ref[208:216, 128:129], axis=0, keepdims=True)
    slope = slope + squares / (-0.5 * precision)
    usage = jnp.sum(acc_ref[136:144] + usage_ref[...], axis=0, keepdims=True)
    rest = codes + width
    sum_scr[:, 0:codes] = book_sum
    sum_scr[:, codes:rest] = acc_ref[144:208, 0:width]
    sum_scr[:, rest : rest + 128] = jnp.broadcast_to(slope, (64, 128))
    rows = codes // 128
    for i in range(rows):
        sum_scr[i : i + 1, rest : rest + 128] = usage[:, i * 128 : (i + 1) * 128]
    sum_scr[rows : rows + 1, rest : rest + dim] = bias
    for i in range(devices):
        shards[i][...] = sum_scr[shard_at(partner(me, i, devices), devices)]


def own_kernel(n, *refs):
    table, feats, noises, cots, params, (acc_in, _), rest = take(
        refs, 1, n, n, n, 4, 2, len(refs)
    )
    (code_ref, grad_out, acc_ref), (grad_scr, sems), shared, rest = take(rest, 3, 2, 5, 6 * n)
    scrs = take(rest, *[6] * n)
    grads = Gradients(grad_out, grad_scr, sems)
    step = pl.program_id(0)

    @pl.when(step == 0)
    def _():
        prepare(params, *shared)
        acc_ref[...] = acc_in[...]

    grads.ready(step, n)
    states = [
        products(params, shared, scr, feat_ref[...], cot_ref[...], True)
        for scr, feat_ref, cot_ref in zip(scrs, feats, cots)
    ]
    usage = acc_ref[136:144]
    for i, (scr, noise_ref) in enumerate(zip(scrs, noises)):
        usage = both_rows(params, scr, noise_ref, code_ref.at[i], usage)
    acc_ref[136:144] = usage
    values = [
        gradients(params, shared, scr, state, acc_ref) for scr, state in zip(scrs, states)
    ]
    grads.store(step, values, [table[0][0, step * n + i] for i in range(n)])
    grads.end(step, n, pl.num_programs(0))


def run_own(count, table, feat, noise, cot, params, acc, grad):
    dim, codes = params[2].shape
    images, strip, width = feat.shape
    share = images // count
    n = 1

    def image(lane, shape):
        return pl.BlockSpec(
            (None, *shape), lambda i, table_ref: (table_ref[0, i * n + lane], 0, 0)
        )

    return pl.pallas_call(
        functools.partial(own_kernel, n),
        grid_spec=pltpu.PrefetchScalarGridSpec(
            num_scalar_prefetch=1,
            grid=(share // n,),
            in_specs=[image(lane, (strip, width)) for lane in range(n)]
            + [image(lane, (strip, codes)) for lane in range(n)]
            + [image(lane, (dim, strip)) for lane in range(n)]
            + [fixed(p.shape) for p in params]
            + [fixed(acc.shape), HBM],
            out_specs=[
                pl.BlockSpec(
                    (n, strip, codes),
                    lambda i, table_ref: (i, table_ref[0, count * share], 0),
                ),
                HBM,
                fixed(acc.shape),
            ],
            scratch_shapes=gradient_scratch(n, strip, width)
            + shared_scratch(dim, codes, width)
            + tile_scratch(strip, codes) * n,
        ),
        out_shape=[
            pltpu.HBM((share, strip * count, codes), F32),
            pltpu.HBM(feat.shape, F32),
            pltpu.HBM(acc.shape, F32),
        ],
        input_output_aliases={5 + 3 * n: 2, 6 + 3 * n: 1},
        compiler_params=settings(),
        cost_estimate=cost(share * strip, width, dim, codes, 10),
        name="own_images",
    )(table, *in_hbm([feat] * n + [noise] * n + [cot] * n + [*params, acc, grad]))


def place_kernel(count, runs, *refs):
    parts = refs[0 : len(runs)]
    out_ref, sem = refs[len(runs) + 1 : len(runs) + 3]
    me = lax.axis_index("space")
    copies = []
    for part, (step, first, slots) in zip(parts, runs):
        strip = part.shape[0] // slots
        row = pl.multiple_of(source(me, step, count) * strip, strip)
        for j in range(slots):
            copies.append(
                pltpu.make_async_copy(
                    part.at[pl.ds(j * strip, strip)],
                    out_ref.at[first + j, pl.ds(row, strip)],
                    sem.at[len(copies)],
                )
            )
    for copy in copies:
        copy.start()
    for copy in copies:
        copy.wait()


def place_wide(count, runs, parts, whole):
    return pl.pallas_call(
        functools.partial(place_kernel, count, runs),
        out_shape=pltpu.HBM(whole.shape, F32),
        in_specs=[VMEM] * len(runs) + [HBM],
        out_specs=HBM,
        scratch_shapes=[pltpu.SemaphoreType.DMA((sum(r[2] for r in runs),))],
        input_output_aliases={len(runs): 0},
        compiler_params=settings(VMEM_LIMIT // 2),
        cost_estimate=pl.CostEstimate(
            flops=0, bytes_accessed=2 * sum(p.size * 4 for p in parts), transcendentals=0
        ),
        name="place_wide",
    )(*[pltpu.with_memory_space_constraint(p, pltpu.VMEM) for p in parts], *in_hbm([whole]))


def join_kernel(count, *refs):
    parts = refs[0:count]
    outs = refs[count:]
    me = lax.axis_index("space")
    for step in range(count):
        here = source(me, step, count)
        base = 0
        for out in outs:
            for j in range(out.shape[0]):
                strip = out.shape[2]
                out[j, here] = parts[step][base : base + strip]
                base += strip


def join_small(count, parts, shapes):
    codes = parts[0].shape[1]
    return pl.pallas_call(
        functools.partial(join_kernel, count),
        out_shape=[
            jax.ShapeDtypeStruct((images // count, count, strip, codes), F32)
            for images, strip, _ in shapes
        ],
        compiler_params=settings(VMEM_LIMIT // 2),
        name="join_small",
    )(*parts)


def tree(values):
    while len(values) > 1:
        values = [
            values[i] + values[i + 1] if i + 1 < len(values) else values[i]
            for i in range(0, len(values), 2)
        ]
    return values[0]


def sum_kernel(*refs):
    refs[-1][...] = tree([ref[...] for ref in refs[:-1]])


def add_all(parts):
    return pl.pallas_call(
        sum_kernel,
        out_shape=jax.ShapeDtypeStruct(parts[0].shape, F32),
        compiler_params=settings(VMEM_LIMIT // 2),
        name="add_parts",
    )(*parts)


def final_kernel(devices, pixels, *refs):
    shards = refs[0:devices]
    weight_ref, bias_ref, book_ref, log_ref, usage_ref = refs[devices : devices + 5]
    weight_out, bias_out, book_out, log_out, usage_out = refs[devices + 5 : devices + 10]
    sum_scr = refs[devices + 10]
    me = lax.rem(lax.axis_index("dp"), devices)
    for i in range(devices):
        sum_scr[shard_at(source(me, i, devices), devices)] = shards[i][...]
    dim, codes = book_ref.shape
    width = weight_ref.shape[1]
    scale = 0.5 * lax.rsqrt(jnp.full((8, 128), pixels, F32))[0:1, 0:1]
    book_out[...] = 0.5 * book_ref[...] + scale * sum_scr[:, 0:codes]
    rest = codes + width
    weight_out[...] = 0.5 * weight_ref[...] + scale * sum_scr[:, codes:rest]
    rows = codes // 128
    bias_out[...] = 0.5 * bias_ref[...] + scale * sum_scr[rows : rows + 1, rest : rest + dim]
    usage = jnp.concatenate(
        [sum_scr[i : i + 1, rest : rest + 128] for i in range(rows)], axis=1
    )
    usage_out[...] = 0.5 * usage_ref[...] + 0.5 * (codes / pixels) * usage
    log_out[...] = 0.5 * log_ref[...] + scale * sum_scr[rows + 1 : rows + 2, rest : rest + 1]


def finish(devices, pixels, shards, weight, bias, book, log, usage):
    outs = (weight.T, bias.reshape(1, -1), book.T, log.reshape(1, 1), usage.reshape(1, -1))
    outs = pl.pallas_call(
        functools.partial(final_kernel, devices, pixels),
        out_shape=[jax.ShapeDtypeStruct(out.shape, F32) for out in outs],
        scratch_shapes=[pltpu.VMEM((64, LANES), F32)],
        compiler_params=settings(VMEM_LIMIT // 2),
        name="new_averages",
    )(*shards, *outs)
    return outs[0].T, outs[1].reshape(-1), outs[2].T, outs[3].reshape(-1), outs[4].reshape(-1)


def exchange(value, bit, size, pairs):
    while bit < size:
        value = value + pairs(value, bit)
        bit = 2 * bit
    return value


def per_device(
    feat_small,
    feat_mid,
    feat_wide,
    noise_small,
    noise_mid,
    noise_wide,
    cot_small,
    cot_mid,
    cot_wide,
    order_small,
    order_mid,
    order_wide,
    weight,
    bias,
    book,
    log,
    heat,
    weight_mean,
    bias_mean,
    book_mean,
    log_mean,
    usage_mean,
):
    count = lax.axis_size("space")
    devices = lax.axis_size("dp")
    params = (weight.T, bias.reshape(1, -1), book.T, log, heat)
    feats = (feat_small, feat_mid, feat_wide)
    pixels = sum(f.shape[0] * f.shape[1] for f in feats) * count * devices
    share = feat_wide.shape[0] // count
    cot_wide = jnp.swapaxes(cot_wide, 1, 2)

    def send(values):
        return [lax.ppermute(v, "space", route(i + 1, count)) for i, v in enumerate(values)]

    def after(part, codes):
        return lax.optimization_barrier((part, codes))

    orders = (order_small, order_mid, order_wide)
    *small, table, usage, scalar = small_forward(
        count, orders, feats[0:2], (noise_small, noise_mid), params
    )
    params = (*params[0:3], scalar)
    small_arrived = send(small[1:])
    near = min(4, devices)
    last = count - 1
    early = [(step, 0, 1) for step in range(1, count)]
    direct = [(step, 1, share - 1) for step in range(1, last)]
    late = [(last, 1, share - 1)]
    *early_codes, usage = wide_forward(
        count, split(early, 3), False, table, feat_wide, noise_wide, params, usage, 4
    )
    usage, scalar = lax.optimization_barrier((usage, scalar))
    params = (*params[0:3], scalar)
    leaving = list(early_codes)
    small_arrived[-1], leaving[-1] = after(small_arrived[-1], leaving[-1])
    early_arrived = send(leaving)
    *codes, grad, acc = wide_both(
        count, split(direct, 2), table, feat_wide, noise_wide, cot_wide, params, None, None, 10
    )
    late_arrived = send(codes)
    codes_small, codes_mid = join_small(
        count, [small[0]] + small_arrived, [f.shape for f in feats[0:2]]
    )
    codes_small, codes_mid, acc = lax.optimization_barrier((codes_small, codes_mid, acc))
    late_codes, grad, acc = wide_both(
        count, [Lane(late)], table, feat_wide, noise_wide, cot_wide, params, acc, grad, 2
    )
    early_arrived[-1], late_codes = after(early_arrived[-1], late_codes)
    late_arrived.append(lax.ppermute(late_codes, "space", route(last, count)))
    early_arrived, acc = lax.optimization_barrier((early_arrived, acc))
    whole, grad, acc = run_own(
        count, table, feat_wide, noise_wide, cot_wide, params, acc, grad
    )
    whole = place_wide(count, early, early_arrived, whole)
    whole, acc = lax.optimization_barrier((whole, acc))
    grad, acc = wide_backward(
        count, split(early, 3), early_codes, table, feat_wide, cot_wide, params, acc, grad
    )
    grad_small, grad_mid, *shards = small_backward(
        count,
        near,
        feat_wide.shape[0],
        table,
        feats[0:2],
        (cot_small, cot_mid),
        small,
        params,
        acc,
        usage,
    )
    group = [
        [(i, i - i % near + partner(i % near, step, near)) for i in range(devices)]
        for step in range(near)
    ]
    parts = [lax.ppermute(shards[i], "dp", group[i]) for i in range(1, near)]
    mine = add_all([shards[0]] + parts)

    def along(value, offset):
        return lax.ppermute(value, "dp", [(i, i ^ offset) for i in range(devices)])

    def across(value, offset):
        turn = near if devices > near else 0
        pairs = [
            (i * count + j, (i ^ turn) * count + (j ^ offset))
            for i in range(devices)
            for j in range(count)
        ]
        return lax.ppermute(value, ("dp", "space"), pairs)

    mine = exchange(mine, near, devices, along)
    mine = exchange(mine, 1, count, across)
    shards = [mine] + [lax.ppermute(mine, "dp", group[i]) for i in range(1, near)]
    updated = finish(
        near, pixels, shards, weight_mean, bias_mean, book_mean, log_mean, usage_mean
    )
    for run, part in zip(direct + late, late_arrived):
        whole = place_wide(count, [run], [part], whole)
    codes = whole.shape[2]
    return (
        codes_small.reshape(codes_small.shape[0], -1, codes),
        codes_mid.reshape(codes_mid.shape[0], -1, codes),
        whole,
        grad_small,
        grad_mid,
        grad,
        *updated,
    )


def solution(mesh):
    strips = P("dp", "space", None)
    placed = (strips,) * 9 + (P("dp", None),) * 3 + (P(),) * 10
    return jax.shard_map(
        per_device,
        mesh=mesh,
        in_specs=placed,
        out_specs=(P(("dp", "space"), None, None),) * 3 + (strips,) * 3 + (P(),) * 5,
        check_vma=False,
    )
```

```python
import functools

import jax
import jax.numpy as jnp
from jax import lax
from jax.experimental import pallas as pl
from jax.experimental.pallas import tpu as pltpu
from jax.sharding import PartitionSpec as P

F32 = jnp.float32
BF16 = jnp.bfloat16
VMEM_LIMIT = 24 * 1024 * 1024
ACC_ROWS = 64 + 64 + 8 + 8 + 64 + 8
LANES = 896


def partner(index, step, count):
    if count & (count - 1) == 0:
        return index ^ step
    return lax.rem(index + step, count)


def route(step, count):
    if count & (count - 1) == 0:
        return [(i, i ^ step) for i in range(count)]
    return [(i, (i + step) % count) for i in range(count)]


def source(index, step, count):
    if count & (count - 1) == 0:
        return index ^ step
    return lax.rem(index + (count - step), count)


def in_hbm(arrays):
    return [pltpu.with_memory_space_constraint(a, pltpu.HBM) for a in arrays]


def halves(x):
    high = x.astype(BF16)
    return high, (x - high.astype(F32)).astype(BF16)


def dot(left, right, left_dim=1, right_dim=0):
    return lax.dot_general(
        left, right, (((left_dim,), (right_dim,)), ((), ())), preferred_element_type=F32
    )


def set_scalars(log_ref, heat_ref, out_ref):
    precision = jnp.exp(jnp.full((8, 128), log_ref[0], F32))
    heat = jnp.full((8, 128), heat_ref[0], F32)
    row = lax.broadcasted_iota(jnp.int32, (8, 128), 0)
    factor = -0.5 * precision / heat
    out_ref[...] = jnp.where(row == 0, precision, jnp.where(row == 1, 1.0 / heat, factor))


def scalars(ref):
    return ref[0:1, 0:1], ref[1:2, 0:1], ref[2:3, 0:1]


def prepare(refs, book_scr, books_scr, weight_scr):
    weight_ref, bias_ref, book_ref, scalar_ref = refs
    dim, codes = book_ref.shape
    precision, _, _ = scalars(scalar_ref)
    book = book_ref[...]
    high, low = halves(book)
    norm = -0.5 * precision * jnp.sum(book * book, axis=0, keepdims=True)
    n0 = norm.astype(BF16).astype(F32)
    n1 = (norm - n0).astype(BF16).astype(F32)
    n2 = norm - n0 - n1
    row = lax.broadcasted_iota(jnp.int32, (16, codes), 0)
    extra = jnp.where(
        row < 3,
        1.0,
        jnp.where(row == 3, n0, jnp.where(row == 4, n1, jnp.where(row == 5, n2, 0.0))),
    ).astype(BF16)
    book_scr[0:dim] = high
    book_scr[dim : 2 * dim] = low
    book_scr[2 * dim : 3 * dim] = high
    book_scr[3 * dim : 3 * dim + 16] = extra
    books_scr[0:dim] = high
    books_scr[dim : 2 * dim] = low
    books_scr[2 * dim : 2 * dim + 16] = jnp.ones((16, codes), BF16)
    high, low = halves(weight_ref[...])
    weight_scr[0:dim] = high
    weight_scr[dim : 2 * dim] = low
    weight_scr[2 * dim : 3 * dim] = high


def latents(refs, shared, feat):
    weight_ref, bias_ref, book_ref, scalar_ref = refs
    weight_scr = shared[2]
    dim = book_ref.shape[0]
    precision, _, _ = scalars(scalar_ref)
    eye = lax.broadcasted_iota(jnp.int32, (dim, dim), 0) == lax.broadcasted_iota(
        jnp.int32, (dim, dim), 1
    )
    bias = jnp.sum(jnp.where(eye, bias_ref[...], 0.0), axis=1, keepdims=True)
    fh, fl = halves(feat)
    both = weight_scr[0 : 2 * dim]
    z2 = dot(both, fh, 1, 1) + dot(both, fl, 1, 1)
    z = z2[0:dim] + z2[dim : 2 * dim] + bias
    square = -0.5 * precision * jnp.sum(z * z, axis=0, keepdims=True)
    return fh, fl, z, square


def logit_rows(zh, zl, square):
    rows = zh.shape[1]
    s0 = square.astype(BF16).astype(F32)
    s1 = (square - s0).astype(BF16).astype(F32)
    s2 = square - s0 - s1
    row = lax.broadcasted_iota(jnp.int32, (16, rows), 0)
    extra = jnp.where(
        row == 0,
        s0,
        jnp.where(row == 1, s1, jnp.where(row == 2, s2, jnp.where(row < 6, 1.0, 0.0))),
    ).astype(BF16)
    return jnp.concatenate([zh, zh, zl, extra], axis=0)


def cot_rows(ch, cl):
    return jnp.concatenate([ch, ch, cl, jnp.zeros((16, ch.shape[1]), BF16)], axis=0)


def over_rows(rows, body, carry):
    step = next(s for s in (32, 16, 8) if rows % s == 0)

    def at(i, carry):
        return body(pl.ds(pl.multiple_of(i * step, step), step), carry)

    return lax.fori_loop(0, rows // step, at, carry, unroll=True)


def folded(x):
    return jnp.sum(x.reshape(x.shape[0] // 8, 8, x.shape[1]), axis=0)


def probabilities(logits):
    top = jnp.max(logits, axis=1, keepdims=True)
    e = jnp.exp(logits - top)
    return e * (1.0 / jnp.sum(e, axis=1, keepdims=True))


def forward_products(refs, shared, feat, l_scr):
    precision, _, _ = scalars(refs[3])
    _, _, z, square = latents(refs, shared, feat)
    zh, zl = halves(precision * z)
    l_scr[0 : feat.shape[0]] = dot(logit_rows(zh, zl, square), shared[0][...], 0, 0)


def forward_rows(refs, l_scr, noise_ref, code_ref, usage):
    _, cold, _ = scalars(refs[3])

    def body(at, usage):
        logits = l_scr[at]
        code_ref[at] = probabilities((logits + noise_ref[at]) * cold)
        return usage + folded(probabilities(logits))

    return over_rows(code_ref.shape[0], body, usage)


def products(refs, shared, scr, feat, cot, forward):
    l_scr, g_scr = scr[0:2]
    rows = feat.shape[0]
    precision, _, factor = scalars(refs[3])
    fh, fl, z, square = latents(refs, shared, feat)
    zh, zl = halves(precision * z)
    ch, cl = halves(factor * cot)
    if forward:
        left = jnp.concatenate([logit_rows(zh, zl, square), cot_rows(ch, cl)], axis=1)
        p = dot(left, shared[0][...], 0, 0)
        l_scr[0:rows] = p[0:rows]
        g_scr[0:rows] = p[rows : 2 * rows]
    else:
        g_scr[0:rows] = dot(cot_rows(ch, cl), shared[0][...], 0, 0)
    return fh, fl, z, square, zh, zl, ch, cl


def both_rows(refs, scr, noise_ref, code_ref, usage):
    l_scr, g_scr, wh_scr, wl_scr, gh_scr, gl_scr = scr
    _, cold, _ = scalars(refs[3])

    def body(at, usage):
        logits = l_scr[at]
        s = (logits + noise_ref[at]) * cold
        e = jnp.exp(s - jnp.max(s, axis=1, keepdims=True))
        gw = g_scr[at]
        scale = 1.0 / jnp.sum(e, axis=1, keepdims=True)
        inner = jnp.sum(e * gw, axis=1, keepdims=True) * scale
        w = e * scale
        code_ref[at] = w
        gd = w * (gw - inner)
        wh_scr[at], wl_scr[at] = halves(w)
        gh_scr[at], gl_scr[at] = halves(gd)
        return usage + folded(probabilities(logits))

    return over_rows(code_ref.shape[0], body, usage)


def backward_rows(scr, code_ref):
    _, g_scr, wh_scr, wl_scr, gh_scr, gl_scr = scr

    def body(at, carry):
        w = code_ref[at]
        gw = g_scr[at]
        gd = w * (gw - jnp.sum(w * gw, axis=1, keepdims=True))
        wh_scr[at], wl_scr[at] = halves(w)
        gh_scr[at], gl_scr[at] = halves(gd)
        return carry

    over_rows(code_ref.shape[0], body, 0)


def gradients(refs, shared, scr, state, acc_ref):
    _, books_scr, weight_scr = shared
    wh_scr, wl_scr, gh_scr, gl_scr = scr[2:6]
    fh, fl, z, square, zh, zl, ch, cl = state
    rows, feats = fh.shape
    dim, codes = refs[2].shape
    wh, wl = wh_scr[0:rows], wl_scr[0:rows]
    gh, gl = gh_scr[0:rows], gl_scr[0:rows]
    p = dot(jnp.concatenate([ch, cl], axis=0), wh)
    acc_ref[0:64] += p[0:dim] + p[dim : 2 * dim] + dot(ch, wl)
    left = jnp.concatenate([zh, zl, jnp.ones((16, rows), BF16)], axis=0)
    p = dot(left, gh) + dot(left, gl)
    acc_ref[64:128] += p[0:dim] + p[dim : 2 * dim]
    acc_ref[128:136] += p[2 * dim : 2 * dim + 8]
    p = dot(books_scr[...], gh, 1, 1) + dot(books_scr[...], gl, 1, 1)
    row_d = p[2 * dim : 2 * dim + 1]
    gz = 2.0 * (row_d * z - (p[0:dim] + p[dim : 2 * dim]))
    zh, zl = halves(gz)
    p = dot(jnp.concatenate([zh, zl], axis=0), fh)
    acc_ref[144:208, 0:feats] += p[0:dim] + p[dim : 2 * dim] + dot(zh, fl)
    acc_ref[144:208, feats : feats + 128] += jnp.broadcast_to(
        jnp.sum(gz, axis=1, keepdims=True), (dim, 128)
    )
    total = jnp.sum(square * row_d, axis=1, keepdims=True)
    acc_ref[208:216] += jnp.broadcast_to(total, (8, codes))
    return dot(jnp.concatenate([zh, zh, zl], axis=0), weight_scr[...], 0, 0)


def shared_scratch(dim, codes, feats):
    return [
        pltpu.VMEM((3 * dim + 16, codes), BF16),
        pltpu.VMEM((2 * dim + 16, codes), BF16),
        pltpu.VMEM((3 * dim, feats), BF16),
    ]


def tile_scratch(rows, codes):
    return [pltpu.VMEM((rows, codes), F32)] * 2 + [pltpu.VMEM((rows, codes), BF16)] * 4


def settings(limit=VMEM_LIMIT):
    return pltpu.CompilerParams(vmem_limit_bytes=limit)


def cost(rows, feats, dim, codes, tenths):
    return pl.CostEstimate(
        flops=rows * 24 * tenths * (5 * dim * codes + 3 * dim * feats) // 10,
        bytes_accessed=4 * rows * (2 * feats + 2 * codes + dim),
        transcendentals=2 * rows * codes,
    )


SMEM = pl.BlockSpec(memory_space=pltpu.SMEM)
VMEM = pl.BlockSpec(memory_space=pltpu.VMEM)
HBM = pl.BlockSpec(memory_space=pltpu.HBM)


def fixed(shape):
    return pl.BlockSpec(shape, lambda *_: (0,) * len(shape))


class Lane:
    def __init__(self, runs):
        self.runs = list(runs)
        self.bounds = [0]
        for _, _, slots in self.runs:
            self.bounds.append(self.bounds[-1] + slots)

    def total(self):
        return self.bounds[-1]

    def entry(self, i, share):
        entry = 0
        for (step, first, _), start in zip(self.runs, self.bounds):
            here = step * share + first + i - start
            entry = here if start == 0 else jnp.where(i >= start, here, entry)
        return entry

    def image(self, shape, share):
        return pl.BlockSpec(
            (None, *shape), lambda i, table_ref: (table_ref[0, self.entry(i, share)], 0, 0)
        )

    def blocks(self, shape):
        return [
            pl.BlockSpec(
                shape,
                lambda i, _, start=start, last=slots - 1: (jnp.clip(i - start, 0, last), 0),
            )
            for (_, _, slots), start in zip(self.runs, self.bounds)
        ]

    def each(self, step, body):
        for i, (low, high) in enumerate(zip(self.bounds, self.bounds[1:])):
            pl.when((step >= low) & (step < high))(functools.partial(body, i))


def split(runs, ways):
    whole = Lane(runs)
    lanes, current = [], []
    for run in whole.runs:
        current.append(run)
        if Lane(current).total() * ways == whole.total():
            lanes.append(Lane(current))
            current = []
    return lanes if len(lanes) == ways and not current else [whole]


def take(refs, *sizes):
    groups, at = [], 0
    for size in sizes:
        groups.append(refs[at : at + size])
        at += size
    return groups


def by_lane(refs, lanes):
    return take(refs, *[len(lane.runs) for lane in lanes])


def keep_codes(step, lanes, sends, code_scrs):
    for lane, refs, code_scr in zip(lanes, by_lane(sends, lanes), code_scrs):
        if len(lane.runs) > 1:

            def keep(i, refs=refs, code_scr=code_scr):
                refs[i][...] = code_scr[...]

            lane.each(step, keep)


def code_targets(lanes, sends, code_scrs):
    return [
        refs[0] if len(lane.runs) == 1 else code_scr
        for lane, refs, code_scr in zip(lanes, by_lane(sends, lanes), code_scrs)
    ]


class Gradients:
    def __init__(self, out_ref, scr, sems):
        self.out_ref, self.scr, self.sems = out_ref, scr, sems

    def copy(self, lane, slot, image):
        return pltpu.make_async_copy(
            self.scr.at[lane, slot], self.out_ref.at[image], self.sems.at[lane, slot]
        )

    def ready(self, step, lanes):
        @pl.when(step >= 2)
        def _():
            for lane in range(lanes):
                self.copy(lane, lax.rem(step, 2), 0).wait()

    def store(self, step, values, images):
        slot = lax.rem(step, 2)
        for lane, (value, image) in enumerate(zip(values, images)):
            self.scr[lane, slot] = value
            self.copy(lane, slot, image).start()

    def end(self, step, lanes, steps):
        @pl.when(step == steps - 1)
        def _():
            for lane in range(lanes):
                for slot in range(min(2, steps)):
                    self.copy(lane, slot, 0).wait()


def gradient_scratch(lanes, strip, width):
    return [pltpu.VMEM((lanes, 2, strip, width), F32), pltpu.SemaphoreType.DMA((lanes, 2))]


def places_of(table_ref, wide, shapes, groups, count):
    places = []
    base = 0
    entry = wide + 1
    for _ in range(count):
        for size in range(2):
            strip = shapes[size][1]
            for _ in range(groups[size]):
                places.append((size, table_ref[0, entry], base, strip))
                base += strip
                entry += 1
    return places, base


def small_forward_kernel(count, steps, groups, first, *refs):
    sources, (log_ref, heat_ref), sends, (usage_ref, scalar_ref), table, held, rest = take(
        refs, 10, 2, len(steps), 2, 1 if first else 0, 10, len(refs)
    )
    (sems, feat_scr), shared, (l_scr, noise_scr) = take(rest, 2, 3, 2)
    copies = [
        pltpu.make_async_copy(there, here, sems.at[i])
        for i, (there, here) in enumerate(zip(sources, held))
    ]
    for copy in copies:
        copy.start()
    params, orders, feats, noises = (*held[0:3], scalar_ref), held[3:6], held[6:8], held[8:10]
    me = lax.axis_index("space")
    set_scalars(log_ref, heat_ref, scalar_ref)
    for copy in copies[0:3]:
        copy.wait()
    prepare(params, *shared)
    for copy in copies[3:8]:
        copy.wait()
    strips = []
    at = 0
    for k, step in enumerate(steps):
        there = partner(me, step, count)
        row = 0
        for size in range(2):
            strip = feats[size].shape[1]
            for j in range(groups[size]):
                image = orders[size][0, there * groups[size] + j]
                strips.append((k, row, size, image, at, strip))
                row += strip
                at += strip
    for _, _, size, image, at, strip in strips:
        feat_scr[at : at + strip] = feats[size][image]
    forward_products(params, shared, feat_scr[...], l_scr)
    for copy in copies[8:10]:
        copy.wait()
    usage = jnp.zeros(usage_ref.shape, F32)
    part = sends[0].shape[0]
    if all(noise.shape[1] % 8 == 0 for noise in noises):
        for k, row, size, image, at, strip in strips:
            rows = pl.ds(at, strip)
            target = sends[k].at[pl.ds(row, strip)]
            usage = forward_rows(params, l_scr.at[rows], noises[size].at[image], target, usage)
    else:
        for _, _, size, image, at, strip in strips:
            noise_scr[at : at + strip] = noises[size][image]
        for k, send in enumerate(sends):
            rows = pl.ds(k * part, part)
            usage = forward_rows(params, l_scr.at[rows], noise_scr.at[rows], send, usage)
    usage_ref[...] = usage
    if first:
        wide = orders[2].shape[1]
        share = wide // count
        entry = wide + 1
        table[0][0, wide] = me
        for step in range(count):
            there = partner(me, step, count)
            for j in range(share):
                table[0][0, step * share + j] = orders[2][0, there * share + j]
            for size in range(2):
                for j in range(groups[size]):
                    table[0][0, entry] = orders[size][0, there * groups[size] + j]
                    entry += 1


def small_forward(count, steps, first, orders, feats, noises, params):
    dim, codes = params[2].shape
    width = feats[0].shape[2]
    groups = tuple(f.shape[0] // count for f in feats)
    part = sum(g * f.shape[1] for g, f in zip(groups, feats))
    rows = part * len(steps)
    arrays = [*params[0:3], *orders, *feats, *noises]
    entries = sum(o.shape[1] for o in orders) + 1
    return pl.pallas_call(
        functools.partial(small_forward_kernel, count, steps, groups, first),
        out_shape=[jax.ShapeDtypeStruct((part, codes), F32)] * len(steps)
        + [pltpu.HBM((8, codes), F32), pltpu.HBM((8, 128), F32)]
        + ([jax.ShapeDtypeStruct((1, entries), jnp.int32)] if first else []),
        in_specs=[HBM] * 10 + [SMEM] * 2,
        out_specs=[VMEM] * (len(steps) + 2) + ([SMEM] if first else []),
        scratch_shapes=[
            (pltpu.SMEM if 3 <= i < 6 else pltpu.VMEM)(a.shape, a.dtype)
            for i, a in enumerate(arrays)
        ]
        + [pltpu.SemaphoreType.DMA((10,)), pltpu.VMEM((rows, width), F32)]
        + shared_scratch(dim, codes, width)
        + [pltpu.VMEM((rows, codes), F32)] * 2,
        compiler_params=settings(),
        cost_estimate=cost(rows, width, dim, codes, 4),
        name="small_forward",
    )(*in_hbm(arrays), *params[3:5])


def small_backward_kernel(count, devices, wide, groups, *refs):
    table_ref = refs[0]
    feats, cots = refs[1:3], refs[3:5]
    parts = refs[5 : 5 + count]
    params = refs[5 + count : 9 + count]
    acc_in, *usages = refs[9 + count : 12 + count]
    grads = refs[12 + count : 14 + count]
    shards = refs[14 + count : 14 + count + devices]
    rest = refs[14 + count + devices :]
    acc_ref, sum_scr, feat_scr, cot_scr, code_scr = rest[0:5]
    scr = rest[5:]
    places, base = places_of(table_ref, wide, [f.shape for f in feats], groups, count)
    for size, image, at, strip in places:
        feat_scr[at : at + strip] = feats[size][image]
        cot_scr[at : at + strip] = cots[size][image]
    part = base // count
    for step in range(count):
        code_scr[step * part : (step + 1) * part] = parts[step][...]
    shared, tile_scr = take(scr, 3, 6)
    prepare(params, *shared)
    acc_ref[...] = acc_in[...]
    state = products(params, shared, tile_scr, feat_scr[...], cot_scr[...].T, False)
    backward_rows(tile_scr, code_scr)
    feat_scr[...] = gradients(params, shared, tile_scr, state, acc_ref)
    acc_ref[136:144] += usages[0][...] + usages[1][...]
    lay_out(params, acc_ref, sum_scr, shards)
    for size, image, at, strip in places:
        grads[size][image] = feat_scr[at : at + strip]


def small_backward(count, devices, wide, table, feats, cots, parts, params, acc, usages):
    dim, codes = params[2].shape
    width = feats[0].shape[2]
    groups = tuple(f.shape[0] // count for f in feats)
    rows = parts[0].shape[0] * count
    return pl.pallas_call(
        functools.partial(small_backward_kernel, count, devices, wide, groups),
        out_shape=[pltpu.HBM(f.shape, F32) for f in feats]
        + [jax.ShapeDtypeStruct((64 // devices, LANES), F32)] * devices,
        in_specs=[SMEM] + [VMEM] * (11 + count),
        out_specs=[VMEM] * (2 + devices),
        scratch_shapes=[
            pltpu.VMEM(acc.shape, F32),
            pltpu.VMEM((64, LANES), F32),
            pltpu.VMEM((rows, width), F32),
            pltpu.VMEM((rows, dim), F32),
            pltpu.VMEM((rows, codes), F32),
        ]
        + shared_scratch(dim, codes, width)
        + tile_scratch(rows, codes),
        compiler_params=settings(),
        cost_estimate=cost(rows, width, dim, codes, 6),
        name="small_backward",
    )(
        table,
        *in_hbm([*feats, *cots]),
        *parts,
        *in_hbm([*params, acc, *usages]),
    )


def wide_forward_kernel(lanes, joined, *refs):
    n = len(lanes)
    arrays = 1 if joined else sum(len(lane.runs) for lane in lanes)
    _, feats, noises, params, usage_in, sends, rest = take(
        refs, 1, n, n, 4, 1, arrays, len(refs)
    )
    (usage_ref,), code_scrs, shared, l_scrs = take(rest, 1, n, 3, n)
    step = pl.program_id(0)

    @pl.when(step == 0)
    def _():
        prepare(params, *shared)
        usage_ref[...] = usage_in[0][...]

    if joined:
        strip = code_scrs[0].shape[0]
        targets = [sends[0].at[pl.ds(i * strip, strip)] for i in range(n)]
    else:
        targets = code_targets(lanes, sends, code_scrs)
    for feat_ref, l_scr in zip(feats, l_scrs):
        forward_products(params, shared, feat_ref[...], l_scr)
    usage = usage_ref[...]
    for l_scr, noise_ref, target in zip(l_scrs, noises, targets):
        usage = forward_rows(params, l_scr, noise_ref, target, usage)
    usage_ref[...] = usage
    if not joined:
        keep_codes(step, lanes, sends, code_scrs)


def wide_forward(count, lanes, joined, table, feat, noise, params, usage, tenths):
    dim, codes = params[2].shape
    images, strip, width = feat.shape
    share = images // count
    n, steps = len(lanes), lanes[0].total()
    if joined:
        blocks = [fixed((n * strip, codes))]
        sizes = [n]
    else:
        blocks = [block for lane in lanes for block in lane.blocks((strip, codes))]
        sizes = [run[2] for lane in lanes for run in lane.runs]
    return pl.pallas_call(
        functools.partial(wide_forward_kernel, lanes, joined),
        grid_spec=pltpu.PrefetchScalarGridSpec(
            num_scalar_prefetch=1,
            grid=(steps,),
            in_specs=[lane.image((strip, width), share) for lane in lanes]
            + [lane.image((strip, codes), share) for lane in lanes]
            + [fixed(p.shape) for p in params]
            + [fixed(usage.shape)],
            out_specs=blocks + [fixed(usage.shape)],
            scratch_shapes=[pltpu.VMEM((strip, codes), F32)] * n
            + shared_scratch(dim, codes, width)
            + [pltpu.VMEM((strip, codes), F32)] * n,
        ),
        out_shape=[jax.ShapeDtypeStruct((strip * slots, codes), F32) for slots in sizes]
        + [pltpu.HBM(usage.shape, F32)],
        input_output_aliases={5 + 2 * n: len(sizes)},
        compiler_params=settings(),
        cost_estimate=cost(n * steps * strip, width, dim, codes, tenths),
        name="wide_forward",
    )(table, *in_hbm([feat] * n + [noise] * n + [*params, usage]))


def wide_both_kernel(lanes, share, *refs):
    n = len(lanes)
    arrays = sum(len(lane.runs) for lane in lanes)
    table, feats, noises, cots, params, sends, rest = take(
        refs, 1, n, n, n, 4, arrays, len(refs)
    )
    (grad_out, acc_ref), code_scrs, (grad_scr, sems), shared, rest = take(
        rest, 2, n, 2, 3, 6 * n
    )
    scrs = take(rest, *[6] * n)
    grads = Gradients(grad_out, grad_scr, sems)
    step, steps = pl.program_id(0), lanes[0].total()

    @pl.when(step == 0)
    def _():
        prepare(params, *shared)
        acc_ref[...] = jnp.zeros(acc_ref.shape, F32)

    grads.ready(step, n)
    targets = code_targets(lanes, sends, code_scrs)
    states = [
        products(params, shared, scr, feat_ref[...], cot_ref[...], True)
        for scr, feat_ref, cot_ref in zip(scrs, feats, cots)
    ]
    usage = acc_ref[136:144]
    for scr, noise_ref, target in zip(scrs, noises, targets):
        usage = both_rows(params, scr, noise_ref, target, usage)
    acc_ref[136:144] = usage
    values = [
        gradients(params, shared, scr, state, acc_ref) for scr, state in zip(scrs, states)
    ]
    grads.store(step, values, [table[0][0, lane.entry(step, share)] for lane in lanes])
    keep_codes(step, lanes, sends, code_scrs)
    grads.end(step, n, steps)


def wide_both(count, lanes, table, feat, noise, cot, params):
    dim, codes = params[2].shape
    images, strip, width = feat.shape
    share = images // count
    n, steps = len(lanes), lanes[0].total()
    acc_shape = (ACC_ROWS, codes)
    sizes = [run[2] for lane in lanes for run in lane.runs]
    return pl.pallas_call(
        functools.partial(wide_both_kernel, lanes, share),
        grid_spec=pltpu.PrefetchScalarGridSpec(
            num_scalar_prefetch=1,
            grid=(steps,),
            in_specs=[lane.image((strip, width), share) for lane in lanes]
            + [lane.image((strip, codes), share) for lane in lanes]
            + [lane.image((dim, strip), share) for lane in lanes]
            + [fixed(p.shape) for p in params],
            out_specs=[block for lane in lanes for block in lane.blocks((strip, codes))]
            + [HBM, fixed(acc_shape)],
            scratch_shapes=[pltpu.VMEM((strip, codes), F32)] * n
            + gradient_scratch(n, strip, width)
            + shared_scratch(dim, codes, width)
            + tile_scratch(strip, codes) * n,
        ),
        out_shape=[jax.ShapeDtypeStruct((strip * slots, codes), F32) for slots in sizes]
        + [pltpu.HBM(feat.shape, F32), pltpu.HBM(acc_shape, F32)],
        compiler_params=settings(),
        cost_estimate=cost(n * steps * strip, width, dim, codes, 10),
        name="wide_both",
    )(table, *in_hbm([feat] * n + [noise] * n + [cot] * n + [*params]))


def wide_backward_kernel(lanes, share, *refs):
    n = len(lanes)
    arrays = sum(len(lane.runs) for lane in lanes)
    table, feats, cots, parts, params, (acc_in, _), rest = take(
        refs, 1, n, n, arrays, 4, 2, len(refs)
    )
    (grad_out, acc_ref), code_scrs, (grad_scr, sems), shared, rest = take(
        rest, 2, n, 2, 3, 6 * n
    )
    scrs = take(rest, *[6] * n)
    grads = Gradients(grad_out, grad_scr, sems)
    step, steps = pl.program_id(0), lanes[0].total()

    @pl.when(step == 0)
    def _():
        prepare(params, *shared)
        acc_ref[...] = acc_in[...]

    grads.ready(step, n)
    for lane, refs_of, code_scr in zip(lanes, by_lane(parts, lanes), code_scrs):
        if len(lane.runs) > 1:

            def fetch(i, refs_of=refs_of, code_scr=code_scr):
                code_scr[...] = refs_of[i][...]

            lane.each(step, fetch)
    states = [
        products(params, shared, scr, feat_ref[...], cot_ref[...], False)
        for scr, feat_ref, cot_ref in zip(scrs, feats, cots)
    ]
    for scr, code_ref in zip(scrs, code_targets(lanes, parts, code_scrs)):
        backward_rows(scr, code_ref)
    values = [
        gradients(params, shared, scr, state, acc_ref) for scr, state in zip(scrs, states)
    ]
    grads.store(step, values, [table[0][0, lane.entry(step, share)] for lane in lanes])
    grads.end(step, n, steps)


def wide_backward(count, lanes, parts, table, feat, cot, params, acc, grad):
    dim, codes = params[2].shape
    images, strip, width = feat.shape
    share = images // count
    n, steps = len(lanes), lanes[0].total()
    return pl.pallas_call(
        functools.partial(wide_backward_kernel, lanes, share),
        grid_spec=pltpu.PrefetchScalarGridSpec(
            num_scalar_prefetch=1,
            grid=(steps,),
            in_specs=[lane.image((strip, width), share) for lane in lanes]
            + [lane.image((dim, strip), share) for lane in lanes]
            + [block for lane in lanes for block in lane.blocks((strip, codes))]
            + [fixed(p.shape) for p in params]
            + [fixed(acc.shape), HBM],
            out_specs=[HBM, fixed(acc.shape)],
            scratch_shapes=[pltpu.VMEM((strip, codes), F32)] * n
            + gradient_scratch(n, strip, width)
            + shared_scratch(dim, codes, width)
            + tile_scratch(strip, codes) * n,
        ),
        out_shape=[pltpu.HBM(feat.shape, F32), pltpu.HBM(acc.shape, F32)],
        input_output_aliases={5 + 2 * n + len(parts): 1, 6 + 2 * n + len(parts): 0},
        compiler_params=settings(),
        cost_estimate=cost(n * steps * strip, width, dim, codes, 6),
        name="wide_backward",
    )(
        table,
        *in_hbm([feat] * n + [cot] * n),
        *parts,
        *in_hbm([*params, acc, grad]),
    )


def shard_at(index, parts):
    height = 64 // parts
    return pl.ds(pl.multiple_of(index * height, height), height)


def lay_out(params, acc_ref, sum_scr, shards):
    weight_ref, bias_ref, book_ref, scalar_ref = params
    codes = book_ref.shape[1]
    width = weight_ref.shape[1]
    devices = len(shards)
    me = lax.rem(lax.axis_index("dp"), devices)
    precision, _, factor = scalars(scalar_ref)
    book = book_ref[...]
    column = acc_ref[128:129]
    moment = acc_ref[64:128] * (1.0 / precision)
    book_sum = acc_ref[0:64] * (1.0 / factor) + 2.0 * (column * book - moment)
    slope = jnp.sum(
        jnp.sum(book * book, axis=0, keepdims=True) * column, axis=1, keepdims=True
    ) - 2.0 * jnp.sum(jnp.sum(book * moment, axis=0, keepdims=True), axis=1, keepdims=True)
    slope = slope + acc_ref[208:209, 0:1] / (-0.5 * precision)
    usage = jnp.sum(acc_ref[136:144], axis=0, keepdims=True)
    dim = book_ref.shape[0]
    eye = lax.broadcasted_iota(jnp.int32, (dim, dim), 0) == lax.broadcasted_iota(
        jnp.int32, (dim, dim), 1
    )
    bias = acc_ref[144:208, width : width + dim]
    bias = jnp.sum(jnp.where(eye, bias, 0.0), axis=0, keepdims=True)
    rest = codes + width
    sum_scr[:, 0:codes] = book_sum
    sum_scr[:, codes:rest] = acc_ref[144:208, 0:width]
    sum_scr[:, rest : rest + 128] = jnp.broadcast_to(slope, (64, 128))
    rows = codes // 128
    for i in range(rows):
        sum_scr[i : i + 1, rest : rest + 128] = usage[:, i * 128 : (i + 1) * 128]
    sum_scr[rows : rows + 1, rest : rest + dim] = bias
    for i in range(devices):
        shards[i][...] = sum_scr[shard_at(partner(me, i, devices), devices)]


def own_kernel(n, *refs):
    table, feats, noises, cots, params, (acc_in, _), rest = take(
        refs, 1, n, n, n, 4, 2, len(refs)
    )
    (code_ref, grad_out, acc_ref), (grad_scr, sems), shared, rest = take(rest, 3, 2, 3, 6 * n)
    scrs = take(rest, *[6] * n)
    grads = Gradients(grad_out, grad_scr, sems)
    step = pl.program_id(0)

    @pl.when(step == 0)
    def _():
        prepare(params, *shared)
        acc_ref[...] = acc_in[...]

    grads.ready(step, n)
    states = [
        products(params, shared, scr, feat_ref[...], cot_ref[...], True)
        for scr, feat_ref, cot_ref in zip(scrs, feats, cots)
    ]
    usage = acc_ref[136:144]
    for i, (scr, noise_ref) in enumerate(zip(scrs, noises)):
        usage = both_rows(params, scr, noise_ref, code_ref.at[i], usage)
    acc_ref[136:144] = usage
    values = [
        gradients(params, shared, scr, state, acc_ref) for scr, state in zip(scrs, states)
    ]
    grads.store(step, values, [table[0][0, step * n + i] for i in range(n)])
    grads.end(step, n, pl.num_programs(0))


def run_own(count, table, feat, noise, cot, params, acc, grad):
    dim, codes = params[2].shape
    images, strip, width = feat.shape
    share = images // count
    n = 2 if share % 2 == 0 else 1

    def image(lane, shape):
        return pl.BlockSpec(
            (None, *shape), lambda i, table_ref: (table_ref[0, i * n + lane], 0, 0)
        )

    return pl.pallas_call(
        functools.partial(own_kernel, n),
        grid_spec=pltpu.PrefetchScalarGridSpec(
            num_scalar_prefetch=1,
            grid=(share // n,),
            in_specs=[image(lane, (strip, width)) for lane in range(n)]
            + [image(lane, (strip, codes)) for lane in range(n)]
            + [image(lane, (dim, strip)) for lane in range(n)]
            + [fixed(p.shape) for p in params]
            + [fixed(acc.shape), HBM],
            out_specs=[
                pl.BlockSpec(
                    (n, strip, codes),
                    lambda i, table_ref: (i, table_ref[0, count * share], 0),
                ),
                HBM,
                fixed(acc.shape),
            ],
            scratch_shapes=gradient_scratch(n, strip, width)
            + shared_scratch(dim, codes, width)
            + tile_scratch(strip, codes) * n,
        ),
        out_shape=[
            pltpu.HBM((share, strip * count, codes), F32),
            pltpu.HBM(feat.shape, F32),
            pltpu.HBM(acc.shape, F32),
        ],
        input_output_aliases={5 + 3 * n: 2, 6 + 3 * n: 1},
        compiler_params=settings(),
        cost_estimate=cost(share * strip, width, dim, codes, 10),
        name="own_images",
    )(table, *in_hbm([feat] * n + [noise] * n + [cot] * n + [*params, acc, grad]))


def place_kernel(count, runs, *refs):
    parts = refs[0 : len(runs)]
    out_ref, sem = refs[len(runs) + 1 : len(runs) + 3]
    me = lax.axis_index("space")
    copies = []
    for part, (step, first, slots) in zip(parts, runs):
        strip = part.shape[0] // slots
        row = pl.multiple_of(source(me, step, count) * strip, strip)
        for j in range(slots):
            copies.append(
                pltpu.make_async_copy(
                    part.at[pl.ds(j * strip, strip)],
                    out_ref.at[first + j, pl.ds(row, strip)],
                    sem.at[len(copies)],
                )
            )
    for copy in copies:
        copy.start()
    for copy in copies:
        copy.wait()


def place_wide(count, runs, parts, whole):
    return pl.pallas_call(
        functools.partial(place_kernel, count, runs),
        out_shape=pltpu.HBM(whole.shape, F32),
        in_specs=[VMEM] * len(runs) + [HBM],
        out_specs=HBM,
        scratch_shapes=[pltpu.SemaphoreType.DMA((sum(r[2] for r in runs),))],
        input_output_aliases={len(runs): 0},
        compiler_params=settings(VMEM_LIMIT // 2),
        cost_estimate=pl.CostEstimate(
            flops=0, bytes_accessed=2 * sum(p.size * 4 for p in parts), transcendentals=0
        ),
        name="place_wide",
    )(*[pltpu.with_memory_space_constraint(p, pltpu.VMEM) for p in parts], *in_hbm([whole]))


def join_kernel(count, *refs):
    parts = refs[0:count]
    outs = refs[count:]
    me = lax.axis_index("space")
    for step in range(count):
        here = source(me, step, count)
        base = 0
        for out in outs:
            for j in range(out.shape[0]):
                strip = out.shape[2]
                out[j, here] = parts[step][base : base + strip]
                base += strip


def join_small(count, parts, shapes):
    codes = parts[0].shape[1]
    return pl.pallas_call(
        functools.partial(join_kernel, count),
        out_shape=[
            jax.ShapeDtypeStruct((images // count, count, strip, codes), F32)
            for images, strip, _ in shapes
        ],
        compiler_params=settings(VMEM_LIMIT // 2),
        name="join_small",
    )(*parts)


def tree(values):
    while len(values) > 1:
        values = [
            values[i] + values[i + 1] if i + 1 < len(values) else values[i]
            for i in range(0, len(values), 2)
        ]
    return values[0]


def sum_kernel(*refs):
    refs[-1][...] = tree([ref[...] for ref in refs[:-1]])


def add_all(parts):
    return pl.pallas_call(
        sum_kernel,
        out_shape=jax.ShapeDtypeStruct(parts[0].shape, F32),
        compiler_params=settings(VMEM_LIMIT // 2),
        name="add_parts",
    )(*parts)


def final_kernel(devices, pixels, *refs):
    shards = refs[0:devices]
    weight_ref, bias_ref, book_ref, log_ref, usage_ref = refs[devices : devices + 5]
    weight_out, bias_out, book_out, log_out, usage_out = refs[devices + 5 : devices + 10]
    sum_scr = refs[devices + 10]
    me = lax.rem(lax.axis_index("dp"), devices)
    for i in range(devices):
        sum_scr[shard_at(source(me, i, devices), devices)] = shards[i][...]
    dim, codes = book_ref.shape
    width = weight_ref.shape[1]
    scale = 0.5 * lax.rsqrt(jnp.full((8, 128), pixels, F32))[0:1, 0:1]
    book_out[...] = 0.5 * book_ref[...] + scale * sum_scr[:, 0:codes]
    rest = codes + width
    weight_out[...] = 0.5 * weight_ref[...] + scale * sum_scr[:, codes:rest]
    rows = codes // 128
    bias_out[...] = 0.5 * bias_ref[...] + scale * sum_scr[rows : rows + 1, rest : rest + dim]
    usage = jnp.concatenate(
        [sum_scr[i : i + 1, rest : rest + 128] for i in range(rows)], axis=1
    )
    usage_out[...] = 0.5 * usage_ref[...] + 0.5 * (codes / pixels) * usage
    log_out[...] = 0.5 * log_ref[...] + scale * sum_scr[rows + 1 : rows + 2, rest : rest + 1]


def finish(devices, pixels, shards, weight, bias, book, log, usage):
    outs = (weight.T, bias.reshape(1, -1), book.T, log.reshape(1, 1), usage.reshape(1, -1))
    outs = pl.pallas_call(
        functools.partial(final_kernel, devices, pixels),
        out_shape=[jax.ShapeDtypeStruct(out.shape, F32) for out in outs],
        scratch_shapes=[pltpu.VMEM((64, LANES), F32)],
        compiler_params=settings(VMEM_LIMIT // 2),
        name="new_averages",
    )(*shards, *outs)
    return outs[0].T, outs[1].reshape(-1), outs[2].T, outs[3].reshape(-1), outs[4].reshape(-1)


def exchange(value, bit, size, pairs):
    while bit < size:
        value = value + pairs(value, bit)
        bit = 2 * bit
    return value


def per_device(
    feat_small,
    feat_mid,
    feat_wide,
    noise_small,
    noise_mid,
    noise_wide,
    cot_small,
    cot_mid,
    cot_wide,
    order_small,
    order_mid,
    order_wide,
    weight,
    bias,
    book,
    log,
    heat,
    weight_mean,
    bias_mean,
    book_mean,
    log_mean,
    usage_mean,
):
    count = lax.axis_size("space")
    devices = lax.axis_size("dp")
    params = (weight.T, bias.reshape(1, -1), book.T, log, heat)
    feats = (feat_small, feat_mid, feat_wide)
    pixels = sum(f.shape[0] * f.shape[1] for f in feats) * count * devices
    share = feat_wide.shape[0] // count
    cot_wide = jnp.swapaxes(cot_wide, 1, 2)

    def send(values):
        return [lax.ppermute(v, "space", route(i + 1, count)) for i, v in enumerate(values)]

    def follow(codes, before):
        before[:], codes[-1] = lax.optimization_barrier((before, codes[-1]))
        return send(codes)

    orders = (order_small, order_mid, order_wide)
    noises = (noise_small, noise_mid)
    *small, usage, scalar, table = small_forward(
        count, range(1, count), True, orders, feats[0:2], noises, params
    )
    arrived = [send(small)]
    own_params = params
    params = (*params[0:3], scalar)
    near = min(4, devices)
    last = count - 1
    early = [(step, 0, 1) for step in range(1, count)]
    direct = [(step, 1, share - 1) for step in range(1, last)]
    late = [(last, 1, share - 1)]
    *early_codes, usage = wide_forward(
        count, split(early, 3), False, table, feat_wide, noise_wide, params, usage, 4
    )
    arrived.append(follow(list(early_codes), arrived[0]))
    *codes, grad, acc = wide_both(
        count, split(direct, 2), table, feat_wide, noise_wide, cot_wide, params
    )
    late_lanes = [Lane([(last, slot, 1)]) for slot in range(1, share)]
    late_codes, usage = wide_forward(
        count, late_lanes, True, table, feat_wide, noise_wide, params, usage, 1
    )
    arrived.append(follow([*codes, late_codes], arrived[1]))
    arrived[1], acc = lax.optimization_barrier((arrived[1], acc))
    whole, grad, acc = run_own(
        count, table, feat_wide, noise_wide, cot_wide, params, acc, grad
    )
    whole = place_wide(count, early, arrived[1], whole)
    acc, own_params = lax.optimization_barrier((acc, own_params))
    own, own_usage, _ = small_forward(
        count, range(1), False, orders, feats[0:2], noises, own_params
    )
    small = [own, *small]
    codes_small, codes_mid = join_small(
        count, [own] + arrived[0], [f.shape for f in feats[0:2]]
    )
    whole, codes_small, codes_mid, acc = lax.optimization_barrier(
        (whole, codes_small, codes_mid, acc)
    )
    grad, acc = wide_backward(
        count,
        split(early + late, 2),
        [*early_codes, late_codes],
        table,
        feat_wide,
        cot_wide,
        params,
        acc,
        grad,
    )
    grad_small, grad_mid, *shards = small_backward(
        count,
        near,
        feat_wide.shape[0],
        table,
        feats[0:2],
        (cot_small, cot_mid),
        small,
        params,
        acc,
        (usage, own_usage),
    )
    group = [
        [(i, i - i % near + partner(i % near, step, near)) for i in range(devices)]
        for step in range(near)
    ]
    parts = [lax.ppermute(shards[i], "dp", group[i]) for i in range(1, near)]
    mine = add_all([shards[0]] + parts)

    def along(value, offset):
        return lax.ppermute(value, "dp", [(i, i ^ offset) for i in range(devices)])

    def across(value, offset):
        turn = near if devices > near else 0
        pairs = [
            (i * count + j, (i ^ turn) * count + (j ^ offset))
            for i in range(devices)
            for j in range(count)
        ]
        return lax.ppermute(value, ("dp", "space"), pairs)

    mine = exchange(mine, near, devices, along)
    mine = exchange(mine, 1, count, across)
    shards = [mine] + [lax.ppermute(mine, "dp", group[i]) for i in range(1, near)]
    updated = finish(
        near, pixels, shards, weight_mean, bias_mean, book_mean, log_mean, usage_mean
    )
    for run, part in zip(direct + late, arrived[2]):
        whole = place_wide(count, [run], [part], whole)
    codes = whole.shape[2]
    return (
        codes_small.reshape(codes_small.shape[0], -1, codes),
        codes_mid.reshape(codes_mid.shape[0], -1, codes),
        whole,
        grad_small,
        grad_mid,
        grad,
        *updated,
    )


def solution(mesh):
    strips = P("dp", "space", None)
    placed = (strips,) * 9 + (P("dp", None),) * 3 + (P(),) * 10
    return jax.shard_map(
        per_device,
        mesh=mesh,
        in_specs=placed,
        out_specs=(P(("dp", "space"), None, None),) * 3 + (strips,) * 3 + (P(),) * 5,
        check_vma=False,
    )
```

```python
import functools

import jax
import jax.numpy as jnp
from jax import lax
from jax.experimental import pallas as pl
from jax.experimental.pallas import tpu as pltpu
from jax.sharding import PartitionSpec as P

F32 = jnp.float32
BF16 = jnp.bfloat16
VMEM_LIMIT = 24 * 1024 * 1024
ACC_ROWS = 64 + 64 + 8 + 8 + 64 + 8
LANES = 896


def partner(index, step, count):
    if count & (count - 1) == 0:
        return index ^ step
    return lax.rem(index + step, count)


def route(step, count):
    if count & (count - 1) == 0:
        return [(i, i ^ step) for i in range(count)]
    return [(i, (i + step) % count) for i in range(count)]


def source(index, step, count):
    if count & (count - 1) == 0:
        return index ^ step
    return lax.rem(index + (count - step), count)


def in_hbm(arrays):
    return [pltpu.with_memory_space_constraint(a, pltpu.HBM) for a in arrays]


def halves(x):
    high = x.astype(BF16)
    return high, (x - high.astype(F32)).astype(BF16)


def dot(left, right, left_dim=1, right_dim=0):
    return lax.dot_general(
        left, right, (((left_dim,), (right_dim,)), ((), ())), preferred_element_type=F32
    )


def set_scalars(log_ref, heat_ref, out_ref):
    precision = jnp.exp(jnp.full((8, 128), log_ref[0], F32))
    heat = jnp.full((8, 128), heat_ref[0], F32)
    row = lax.broadcasted_iota(jnp.int32, (8, 128), 0)
    factor = -0.5 * precision / heat
    out_ref[...] = jnp.where(row == 0, precision, jnp.where(row == 1, 1.0 / heat, factor))


def scalars(ref):
    return ref[0:1, 0:1], ref[1:2, 0:1], ref[2:3, 0:1]


def prepare(refs, book_scr, books_scr, weight_scr, backward=True):
    weight_ref, bias_ref, book_ref, scalar_ref = refs
    dim, codes = book_ref.shape
    precision, _, _ = scalars(scalar_ref)
    book = book_ref[...]
    high, low = halves(book)
    norm = -0.5 * precision * jnp.sum(book * book, axis=0, keepdims=True)
    n0 = norm.astype(BF16).astype(F32)
    n1 = (norm - n0).astype(BF16).astype(F32)
    n2 = norm - n0 - n1
    row = lax.broadcasted_iota(jnp.int32, (16, codes), 0)
    extra = jnp.where(
        row < 3,
        1.0,
        jnp.where(row == 3, n0, jnp.where(row == 4, n1, jnp.where(row == 5, n2, 0.0))),
    ).astype(BF16)
    book_scr[0:dim] = high
    book_scr[dim : 2 * dim] = low
    book_scr[2 * dim : 3 * dim] = high
    book_scr[3 * dim : 3 * dim + 16] = extra
    if backward:
        books_scr[0:dim] = high
        books_scr[dim : 2 * dim] = low
        books_scr[2 * dim : 2 * dim + 16] = jnp.ones((16, codes), BF16)
    high, low = halves(weight_ref[...])
    weight_scr[0:dim] = high
    weight_scr[dim : 2 * dim] = low
    weight_scr[2 * dim : 3 * dim] = high


def latents(refs, shared, feat):
    weight_ref, bias_ref, book_ref, scalar_ref = refs
    weight_scr = shared[2]
    dim = book_ref.shape[0]
    precision, _, _ = scalars(scalar_ref)
    eye = lax.broadcasted_iota(jnp.int32, (dim, dim), 0) == lax.broadcasted_iota(
        jnp.int32, (dim, dim), 1
    )
    bias = jnp.sum(jnp.where(eye, bias_ref[...], 0.0), axis=1, keepdims=True)
    fh, fl = halves(feat)
    both = weight_scr[0 : 2 * dim]
    z2 = dot(both, fh, 1, 1) + dot(both, fl, 1, 1)
    z = z2[0:dim] + z2[dim : 2 * dim] + bias
    square = -0.5 * precision * jnp.sum(z * z, axis=0, keepdims=True)
    return fh, fl, z, square


def logit_rows(zh, zl, square):
    rows = zh.shape[1]
    s0 = square.astype(BF16).astype(F32)
    s1 = (square - s0).astype(BF16).astype(F32)
    s2 = square - s0 - s1
    row = lax.broadcasted_iota(jnp.int32, (16, rows), 0)
    extra = jnp.where(
        row == 0,
        s0,
        jnp.where(row == 1, s1, jnp.where(row == 2, s2, jnp.where(row < 6, 1.0, 0.0))),
    ).astype(BF16)
    return jnp.concatenate([zh, zh, zl, extra], axis=0)


def cot_rows(ch, cl):
    return jnp.concatenate([ch, ch, cl, jnp.zeros((16, ch.shape[1]), BF16)], axis=0)


def over_rows(rows, body, carry):
    step = next(s for s in (32, 16, 8) if rows % s == 0)

    def at(i, carry):
        return body(pl.ds(pl.multiple_of(i * step, step), step), carry)

    return lax.fori_loop(0, rows // step, at, carry, unroll=True)


def folded(x):
    return jnp.sum(x.reshape(x.shape[0] // 8, 8, x.shape[1]), axis=0)


def probabilities(logits):
    top = jnp.max(logits, axis=1, keepdims=True)
    e = jnp.exp(logits - top)
    return e * (1.0 / jnp.sum(e, axis=1, keepdims=True))


def forward_products(refs, shared, feat, l_scr):
    precision, _, _ = scalars(refs[3])
    _, _, z, square = latents(refs, shared, feat)
    zh, zl = halves(precision * z)
    l_scr[0 : feat.shape[0]] = dot(logit_rows(zh, zl, square), shared[0][...], 0, 0)


def forward_rows(refs, l_scr, noise_ref, code_ref, usage):
    _, cold, _ = scalars(refs[3])

    def body(at, usage):
        logits = l_scr[at]
        code_ref[at] = probabilities((logits + noise_ref[at]) * cold)
        return usage + folded(probabilities(logits))

    return over_rows(code_ref.shape[0], body, usage)


def products(refs, shared, scr, feat, cot, forward):
    l_scr, g_scr = scr[0:2]
    rows = feat.shape[0]
    precision, _, factor = scalars(refs[3])
    fh, fl, z, square = latents(refs, shared, feat)
    zh, zl = halves(precision * z)
    ch, cl = halves(factor * cot)
    if forward:
        left = jnp.concatenate([logit_rows(zh, zl, square), cot_rows(ch, cl)], axis=1)
        p = dot(left, shared[0][...], 0, 0)
        l_scr[0:rows] = p[0:rows]
        g_scr[0:rows] = p[rows : 2 * rows]
    else:
        g_scr[0:rows] = dot(cot_rows(ch, cl), shared[0][...], 0, 0)
    return fh, fl, z, square, zh, zl, ch, cl


def both_rows(refs, scr, noise_ref, code_ref, usage):
    l_scr, g_scr, wh_scr, wl_scr, gh_scr, gl_scr = scr
    _, cold, _ = scalars(refs[3])

    def body(at, usage):
        logits = l_scr[at]
        s = (logits + noise_ref[at]) * cold
        e = jnp.exp(s - jnp.max(s, axis=1, keepdims=True))
        gw = g_scr[at]
        scale = 1.0 / jnp.sum(e, axis=1, keepdims=True)
        inner = jnp.sum(e * gw, axis=1, keepdims=True) * scale
        w = e * scale
        code_ref[at] = w
        gd = w * (gw - inner)
        wh_scr[at], wl_scr[at] = halves(w)
        gh_scr[at], gl_scr[at] = halves(gd)
        return usage + folded(probabilities(logits))

    return over_rows(code_ref.shape[0], body, usage)


def backward_rows(scr, code_ref):
    _, g_scr, wh_scr, wl_scr, gh_scr, gl_scr = scr

    def body(at, carry):
        w = code_ref[at]
        gw = g_scr[at]
        gd = w * (gw - jnp.sum(w * gw, axis=1, keepdims=True))
        wh_scr[at], wl_scr[at] = halves(w)
        gh_scr[at], gl_scr[at] = halves(gd)
        return carry

    over_rows(code_ref.shape[0], body, 0)


def gradients(refs, shared, scr, state, acc_ref):
    _, books_scr, weight_scr = shared
    wh_scr, wl_scr, gh_scr, gl_scr = scr[2:6]
    fh, fl, z, square, zh, zl, ch, cl = state
    rows, feats = fh.shape
    dim, codes = refs[2].shape
    wh, wl = wh_scr[0:rows], wl_scr[0:rows]
    gh, gl = gh_scr[0:rows], gl_scr[0:rows]
    p = dot(jnp.concatenate([ch, cl], axis=0), wh)
    acc_ref[0:64] += p[0:dim] + p[dim : 2 * dim] + dot(ch, wl)
    left = jnp.concatenate([zh, zl, jnp.ones((16, rows), BF16)], axis=0)
    p = dot(left, gh) + dot(left, gl)
    acc_ref[64:128] += p[0:dim] + p[dim : 2 * dim]
    acc_ref[128:136] += p[2 * dim : 2 * dim + 8]
    p = dot(books_scr[...], gh, 1, 1) + dot(books_scr[...], gl, 1, 1)
    row_d = p[2 * dim : 2 * dim + 1]
    gz = 2.0 * (row_d * z - (p[0:dim] + p[dim : 2 * dim]))
    zh, zl = halves(gz)
    p = dot(jnp.concatenate([zh, zl], axis=0), fh)
    acc_ref[144:208, 0:feats] += p[0:dim] + p[dim : 2 * dim] + dot(zh, fl)
    acc_ref[144:208, feats : feats + 128] += jnp.broadcast_to(
        jnp.sum(gz, axis=1, keepdims=True), (dim, 128)
    )
    total = jnp.sum(square * row_d, axis=1, keepdims=True)
    acc_ref[208:216] += jnp.broadcast_to(total, (8, codes))
    return dot(jnp.concatenate([zh, zh, zl], axis=0), weight_scr[...], 0, 0)


def shared_scratch(dim, codes, feats):
    return [
        pltpu.VMEM((3 * dim + 16, codes), BF16),
        pltpu.VMEM((2 * dim + 16, codes), BF16),
        pltpu.VMEM((3 * dim, feats), BF16),
    ]


def tile_scratch(rows, codes):
    return [pltpu.VMEM((rows, codes), F32)] * 2 + [pltpu.VMEM((rows, codes), BF16)] * 4


def settings(limit=VMEM_LIMIT):
    return pltpu.CompilerParams(vmem_limit_bytes=limit)


def cost(rows, feats, dim, codes, tenths):
    return pl.CostEstimate(
        flops=rows * 24 * tenths * (5 * dim * codes + 3 * dim * feats) // 10,
        bytes_accessed=4 * rows * (2 * feats + 2 * codes + dim),
        transcendentals=2 * rows * codes,
    )


SMEM = pl.BlockSpec(memory_space=pltpu.SMEM)
VMEM = pl.BlockSpec(memory_space=pltpu.VMEM)
HBM = pl.BlockSpec(memory_space=pltpu.HBM)


def fixed(shape):
    return pl.BlockSpec(shape, lambda *_: (0,) * len(shape))


class Lane:
    def __init__(self, runs):
        self.runs = list(runs)
        self.bounds = [0]
        for _, _, slots in self.runs:
            self.bounds.append(self.bounds[-1] + slots)

    def total(self):
        return self.bounds[-1]

    def index(self, i, order_ref, count):
        share = order_ref.shape[1] // count
        step, slot = 0, 0
        for (whose, first, _), start in zip(self.runs, self.bounds):
            here = first + i - start
            step = whose if start == 0 else jnp.where(i >= start, whose, step)
            slot = here if start == 0 else jnp.where(i >= start, here, slot)
        there = partner(lax.axis_index("space"), step, count)
        return order_ref[0, there * share + slot]

    def image(self, shape, count):
        return pl.BlockSpec(
            (None, *shape), lambda i, order_ref: (self.index(i, order_ref, count), 0, 0)
        )

    def blocks(self, shape):
        return [
            pl.BlockSpec(
                shape,
                lambda i, _, start=start, last=slots - 1: (jnp.clip(i - start, 0, last), 0),
            )
            for (_, _, slots), start in zip(self.runs, self.bounds)
        ]

    def each(self, step, body):
        for i, (low, high) in enumerate(zip(self.bounds, self.bounds[1:])):
            pl.when((step >= low) & (step < high))(functools.partial(body, i))


def split(runs, ways):
    whole = Lane(runs)
    lanes, current = [], []
    for run in whole.runs:
        current.append(run)
        if Lane(current).total() * ways == whole.total():
            lanes.append(Lane(current))
            current = []
    return lanes if len(lanes) == ways and not current else [whole]


def take(refs, *sizes):
    groups, at = [], 0
    for size in sizes:
        groups.append(refs[at : at + size])
        at += size
    return groups


def by_lane(refs, lanes):
    return take(refs, *[len(lane.runs) for lane in lanes])


def keep_codes(step, lanes, sends, code_scrs):
    for lane, refs, code_scr in zip(lanes, by_lane(sends, lanes), code_scrs):
        if len(lane.runs) > 1:

            def keep(i, refs=refs, code_scr=code_scr):
                refs[i][...] = code_scr[...]

            lane.each(step, keep)


def code_targets(lanes, sends, code_scrs):
    return [
        refs[0] if len(lane.runs) == 1 else code_scr
        for lane, refs, code_scr in zip(lanes, by_lane(sends, lanes), code_scrs)
    ]


class Gradients:
    def __init__(self, out_ref, scr, sems):
        self.out_ref, self.scr, self.sems = out_ref, scr, sems

    def copy(self, lane, slot, image):
        return pltpu.make_async_copy(
            self.scr.at[lane, slot], self.out_ref.at[image], self.sems.at[lane, slot]
        )

    def ready(self, step, lanes):
        @pl.when(step >= 2)
        def _():
            for lane in range(lanes):
                self.copy(lane, lax.rem(step, 2), 0).wait()

    def store(self, step, values, images):
        slot = lax.rem(step, 2)
        for lane, (value, image) in enumerate(zip(values, images)):
            self.scr[lane, slot] = value
            self.copy(lane, slot, image).start()

    def end(self, step, lanes, steps):
        @pl.when(step == steps - 1)
        def _():
            for lane in range(lanes):
                for slot in range(min(2, steps)):
                    self.copy(lane, slot, 0).wait()


def gradient_scratch(lanes, strip, width):
    return [pltpu.VMEM((lanes, 2, strip, width), F32), pltpu.SemaphoreType.DMA((lanes, 2))]


def places_of(orders, shapes, groups, steps, count):
    me = lax.axis_index("space")
    strips = []
    at = 0
    for k, step in enumerate(steps):
        there = partner(me, step, count)
        row = 0
        for size in range(2):
            strip = shapes[size][1]
            for j in range(groups[size]):
                image = orders[size][0, there * groups[size] + j]
                strips.append((k, row, size, image, at, strip))
                row += strip
                at += strip
    return strips


def small_forward_kernel(count, steps, groups, *refs):
    sources, (log_ref, heat_ref), sends, (usage_ref, scalar_ref), held, rest = take(
        refs, 9, 2, len(steps), 2, 9, len(refs)
    )
    (sems, feat_scr), shared, (l_scr, noise_scr) = take(rest, 2, 3, 2)
    copies = [
        pltpu.make_async_copy(there, here, sems.at[i])
        for i, (there, here) in enumerate(zip(sources, held))
    ]
    for copy in copies:
        copy.start()
    params, orders, feats, noises = (*held[0:3], scalar_ref), held[3:5], held[5:7], held[7:9]
    set_scalars(log_ref, heat_ref, scalar_ref)
    for copy in copies[0:3]:
        copy.wait()
    prepare(params, *shared, backward=False)
    for copy in copies[3:7]:
        copy.wait()
    strips = places_of(orders, [f.shape for f in feats], groups, steps, count)
    for _, _, size, image, at, strip in strips:
        feat_scr[at : at + strip] = feats[size][image]
    forward_products(params, shared, feat_scr[...], l_scr)
    for copy in copies[7:9]:
        copy.wait()
    usage = jnp.zeros(usage_ref.shape, F32)
    part = sends[0].shape[0]
    if all(noise.shape[1] % 8 == 0 for noise in noises):
        for k, row, size, image, at, strip in strips:
            rows = pl.ds(at, strip)
            target = sends[k].at[pl.ds(row, strip)]
            usage = forward_rows(params, l_scr.at[rows], noises[size].at[image], target, usage)
    else:
        for _, _, size, image, at, strip in strips:
            noise_scr[at : at + strip] = noises[size][image]
        for k, send in enumerate(sends):
            rows = pl.ds(k * part, part)
            usage = forward_rows(params, l_scr.at[rows], noise_scr.at[rows], send, usage)
    usage_ref[...] = usage


def small_forward(count, steps, orders, feats, noises, params):
    dim, codes = params[2].shape
    width = feats[0].shape[2]
    groups = tuple(f.shape[0] // count for f in feats)
    part = sum(g * f.shape[1] for g, f in zip(groups, feats))
    rows = part * len(steps)
    arrays = [*params[0:3], *orders, *feats, *noises]
    return pl.pallas_call(
        functools.partial(small_forward_kernel, count, steps, groups),
        out_shape=[jax.ShapeDtypeStruct((part, codes), F32)] * len(steps)
        + [jax.ShapeDtypeStruct((8, codes), F32), jax.ShapeDtypeStruct((8, 128), F32)],
        in_specs=[HBM] * 9 + [SMEM] * 2,
        out_specs=[VMEM] * (len(steps) + 2),
        scratch_shapes=[
            (pltpu.SMEM if 3 <= i < 5 else pltpu.VMEM)(a.shape, a.dtype)
            for i, a in enumerate(arrays)
        ]
        + [pltpu.SemaphoreType.DMA((9,)), pltpu.VMEM((rows, width), F32)]
        + shared_scratch(dim, codes, width)
        + [pltpu.VMEM((rows, codes), F32)] * 2,
        compiler_params=settings(),
        cost_estimate=cost(rows, width, dim, codes, 4),
        name="small_forward",
    )(*in_hbm(arrays), *params[3:5])


def small_backward_kernel(count, devices, groups, *refs):
    orders, feats, cots, parts, params, (acc_in, *usages), grads, shards, rest = take(
        refs, 2, 2, 2, count, 4, 3, 2, devices, len(refs)
    )
    acc_ref, sum_scr, feat_scr, cot_scr, code_scr = rest[0:5]
    scr = rest[5:]
    strips = places_of(orders, [f.shape for f in feats], groups, range(count), count)
    for _, _, size, image, at, strip in strips:
        feat_scr[at : at + strip] = feats[size][image]
        cot_scr[at : at + strip] = cots[size][image]
    part = parts[0].shape[0]
    for step in range(count):
        code_scr[step * part : (step + 1) * part] = parts[step][...]
    shared, tile_scr = take(scr, 3, 6)
    prepare(params, *shared)
    acc_ref[...] = acc_in[...]
    state = products(params, shared, tile_scr, feat_scr[...], cot_scr[...].T, False)
    backward_rows(tile_scr, code_scr)
    feat_scr[...] = gradients(params, shared, tile_scr, state, acc_ref)
    acc_ref[136:144] += usages[0][...] + usages[1][...]
    lay_out(params, acc_ref, sum_scr, shards)
    for _, _, size, image, at, strip in strips:
        grads[size][image] = feat_scr[at : at + strip]


def small_backward(count, devices, orders, feats, cots, parts, params, acc, usages):
    dim, codes = params[2].shape
    width = feats[0].shape[2]
    groups = tuple(f.shape[0] // count for f in feats)
    rows = parts[0].shape[0] * count
    return pl.pallas_call(
        functools.partial(small_backward_kernel, count, devices, groups),
        out_shape=[pltpu.HBM(f.shape, F32) for f in feats]
        + [jax.ShapeDtypeStruct((64 // devices, LANES), F32)] * devices,
        in_specs=[SMEM] * 2 + [VMEM] * (11 + count),
        out_specs=[VMEM] * (2 + devices),
        scratch_shapes=[
            pltpu.VMEM(acc.shape, F32),
            pltpu.VMEM((64, LANES), F32),
            pltpu.VMEM((rows, width), F32),
            pltpu.VMEM((rows, dim), F32),
            pltpu.VMEM((rows, codes), F32),
        ]
        + shared_scratch(dim, codes, width)
        + tile_scratch(rows, codes),
        compiler_params=settings(),
        cost_estimate=cost(rows, width, dim, codes, 6),
        name="small_backward",
    )(
        *orders,
        *in_hbm([*feats, *cots]),
        *parts,
        *in_hbm(params[0:3]),
        params[3],
        acc,
        *usages,
    )


def wide_forward_kernel(lanes, joined, *refs):
    n = len(lanes)
    arrays = 1 if joined else sum(len(lane.runs) for lane in lanes)
    _, feats, noises, params, usage_in, sends, rest = take(
        refs, 1, n, n, 4, 1, arrays, len(refs)
    )
    (usage_ref,), code_scrs, shared, l_scrs = take(rest, 1, n, 3, n)
    step = pl.program_id(0)

    @pl.when(step == 0)
    def _():
        prepare(params, *shared, backward=False)
        usage_ref[...] = usage_in[0][...]

    if joined:
        strip = code_scrs[0].shape[0]
        targets = [sends[0].at[pl.ds(i * strip, strip)] for i in range(n)]
    else:
        targets = code_targets(lanes, sends, code_scrs)
    for feat_ref, l_scr in zip(feats, l_scrs):
        forward_products(params, shared, feat_ref[...], l_scr)
    usage = usage_ref[...]
    for l_scr, noise_ref, target in zip(l_scrs, noises, targets):
        usage = forward_rows(params, l_scr, noise_ref, target, usage)
    usage_ref[...] = usage
    if not joined:
        keep_codes(step, lanes, sends, code_scrs)


def wide_forward(count, lanes, joined, order, feat, noise, params, usage, tenths):
    dim, codes = params[2].shape
    images, strip, width = feat.shape
    n, steps = len(lanes), lanes[0].total()
    if joined:
        blocks = [fixed((n * strip, codes))]
        sizes = [n]
    else:
        blocks = [block for lane in lanes for block in lane.blocks((strip, codes))]
        sizes = [run[2] for lane in lanes for run in lane.runs]
    return pl.pallas_call(
        functools.partial(wide_forward_kernel, lanes, joined),
        grid_spec=pltpu.PrefetchScalarGridSpec(
            num_scalar_prefetch=1,
            grid=(steps,),
            in_specs=[lane.image((strip, width), count) for lane in lanes]
            + [lane.image((strip, codes), count) for lane in lanes]
            + [fixed(p.shape) for p in params]
            + [fixed(usage.shape)],
            out_specs=blocks + [fixed(usage.shape)],
            scratch_shapes=[pltpu.VMEM((strip, codes), F32)] * n
            + shared_scratch(dim, codes, width)
            + [pltpu.VMEM((strip, codes), F32)] * n,
        ),
        out_shape=[jax.ShapeDtypeStruct((strip * slots, codes), F32) for slots in sizes]
        + [jax.ShapeDtypeStruct(usage.shape, F32)],
        input_output_aliases={5 + 2 * n: len(sizes)},
        compiler_params=settings(),
        cost_estimate=cost(n * steps * strip, width, dim, codes, tenths),
        name="wide_forward",
    )(order, *in_hbm([feat] * n + [noise] * n + [*params[0:3]]), params[3], usage)


def wide_both_kernel(lanes, count, *refs):
    n = len(lanes)
    arrays = sum(len(lane.runs) for lane in lanes)
    order, feats, noises, cots, params, sends, rest = take(
        refs, 1, n, n, n, 4, arrays, len(refs)
    )
    (grad_out, acc_ref), code_scrs, (grad_scr, sems), shared, rest = take(
        rest, 2, n, 2, 3, 6 * n
    )
    scrs = take(rest, *[6] * n)
    grads = Gradients(grad_out, grad_scr, sems)
    step, steps = pl.program_id(0), lanes[0].total()

    @pl.when(step == 0)
    def _():
        prepare(params, *shared)
        acc_ref[...] = jnp.zeros(acc_ref.shape, F32)

    grads.ready(step, n)
    targets = code_targets(lanes, sends, code_scrs)
    states = [
        products(params, shared, scr, feat_ref[...], cot_ref[...], True)
        for scr, feat_ref, cot_ref in zip(scrs, feats, cots)
    ]
    usage = acc_ref[136:144]
    for scr, noise_ref, target in zip(scrs, noises, targets):
        usage = both_rows(params, scr, noise_ref, target, usage)
    acc_ref[136:144] = usage
    values = [
        gradients(params, shared, scr, state, acc_ref) for scr, state in zip(scrs, states)
    ]
    grads.store(step, values, [lane.index(step, order[0], count) for lane in lanes])
    keep_codes(step, lanes, sends, code_scrs)
    grads.end(step, n, steps)


def wide_both(count, lanes, order, feat, noise, cot, params):
    dim, codes = params[2].shape
    images, strip, width = feat.shape
    n, steps = len(lanes), lanes[0].total()
    acc_shape = (ACC_ROWS, codes)
    sizes = [run[2] for lane in lanes for run in lane.runs]
    return pl.pallas_call(
        functools.partial(wide_both_kernel, lanes, count),
        grid_spec=pltpu.PrefetchScalarGridSpec(
            num_scalar_prefetch=1,
            grid=(steps,),
            in_specs=[lane.image((strip, width), count) for lane in lanes]
            + [lane.image((strip, codes), count) for lane in lanes]
            + [lane.image((dim, strip), count) for lane in lanes]
            + [fixed(p.shape) for p in params],
            out_specs=[block for lane in lanes for block in lane.blocks((strip, codes))]
            + [HBM, fixed(acc_shape)],
            scratch_shapes=[pltpu.VMEM((strip, codes), F32)] * n
            + gradient_scratch(n, strip, width)
            + shared_scratch(dim, codes, width)
            + tile_scratch(strip, codes) * n,
        ),
        out_shape=[jax.ShapeDtypeStruct((strip * slots, codes), F32) for slots in sizes]
        + [pltpu.HBM(feat.shape, F32), jax.ShapeDtypeStruct(acc_shape, F32)],
        compiler_params=settings(),
        cost_estimate=cost(n * steps * strip, width, dim, codes, 10),
        name="wide_both",
    )(order, *in_hbm([feat] * n + [noise] * n + [cot] * n + [*params[0:3]]), params[3])


def wide_backward_kernel(lanes, count, *refs):
    n = len(lanes)
    arrays = sum(len(lane.runs) for lane in lanes)
    order, feats, cots, parts, params, (acc_in, _), rest = take(
        refs, 1, n, n, arrays, 4, 2, len(refs)
    )
    (grad_out, acc_ref), code_scrs, (grad_scr, sems), shared, rest = take(
        rest, 2, n, 2, 3, 6 * n
    )
    scrs = take(rest, *[6] * n)
    grads = Gradients(grad_out, grad_scr, sems)
    step, steps = pl.program_id(0), lanes[0].total()

    @pl.when(step == 0)
    def _():
        prepare(params, *shared)
        acc_ref[...] = acc_in[...]

    grads.ready(step, n)
    for lane, refs_of, code_scr in zip(lanes, by_lane(parts, lanes), code_scrs):
        if len(lane.runs) > 1:

            def fetch(i, refs_of=refs_of, code_scr=code_scr):
                code_scr[...] = refs_of[i][...]

            lane.each(step, fetch)
    states = [
        products(params, shared, scr, feat_ref[...], cot_ref[...], False)
        for scr, feat_ref, cot_ref in zip(scrs, feats, cots)
    ]
    for scr, code_ref in zip(scrs, code_targets(lanes, parts, code_scrs)):
        backward_rows(scr, code_ref)
    values = [
        gradients(params, shared, scr, state, acc_ref) for scr, state in zip(scrs, states)
    ]
    grads.store(step, values, [lane.index(step, order[0], count) for lane in lanes])
    grads.end(step, n, steps)


def wide_backward(count, lanes, parts, order, feat, cot, params, acc, grad):
    dim, codes = params[2].shape
    images, strip, width = feat.shape
    n, steps = len(lanes), lanes[0].total()
    return pl.pallas_call(
        functools.partial(wide_backward_kernel, lanes, count),
        grid_spec=pltpu.PrefetchScalarGridSpec(
            num_scalar_prefetch=1,
            grid=(steps,),
            in_specs=[lane.image((strip, width), count) for lane in lanes]
            + [lane.image((dim, strip), count) for lane in lanes]
            + [block for lane in lanes for block in lane.blocks((strip, codes))]
            + [fixed(p.shape) for p in params]
            + [fixed(acc.shape), HBM],
            out_specs=[HBM, fixed(acc.shape)],
            scratch_shapes=[pltpu.VMEM((strip, codes), F32)] * n
            + gradient_scratch(n, strip, width)
            + shared_scratch(dim, codes, width)
            + tile_scratch(strip, codes) * n,
        ),
        out_shape=[pltpu.HBM(feat.shape, F32), jax.ShapeDtypeStruct(acc.shape, F32)],
        input_output_aliases={5 + 2 * n + len(parts): 1, 6 + 2 * n + len(parts): 0},
        compiler_params=settings(),
        cost_estimate=cost(n * steps * strip, width, dim, codes, 6),
        name="wide_backward",
    )(
        order,
        *in_hbm([feat] * n + [cot] * n),
        *parts,
        *in_hbm(params[0:3]),
        params[3],
        acc,
        *in_hbm([grad]),
    )


def shard_at(index, parts):
    height = 64 // parts
    return pl.ds(pl.multiple_of(index * height, height), height)


def lay_out(params, acc_ref, sum_scr, shards):
    weight_ref, bias_ref, book_ref, scalar_ref = params
    codes = book_ref.shape[1]
    width = weight_ref.shape[1]
    devices = len(shards)
    me = lax.rem(lax.axis_index("dp"), devices)
    precision, _, factor = scalars(scalar_ref)
    book = book_ref[...]
    column = acc_ref[128:129]
    moment = acc_ref[64:128] * (1.0 / precision)
    book_sum = acc_ref[0:64] * (1.0 / factor) + 2.0 * (column * book - moment)
    slope = jnp.sum(
        jnp.sum(book * book, axis=0, keepdims=True) * column, axis=1, keepdims=True
    ) - 2.0 * jnp.sum(jnp.sum(book * moment, axis=0, keepdims=True), axis=1, keepdims=True)
    slope = slope + acc_ref[208:209, 0:1] / (-0.5 * precision)
    usage = jnp.sum(acc_ref[136:144], axis=0, keepdims=True)
    dim = book_ref.shape[0]
    eye = lax.broadcasted_iota(jnp.int32, (dim, dim), 0) == lax.broadcasted_iota(
        jnp.int32, (dim, dim), 1
    )
    bias = acc_ref[144:208, width : width + dim]
    bias = jnp.sum(jnp.where(eye, bias, 0.0), axis=0, keepdims=True)
    rest = codes + width
    sum_scr[:, 0:codes] = book_sum
    sum_scr[:, codes:rest] = acc_ref[144:208, 0:width]
    sum_scr[:, rest : rest + 128] = jnp.broadcast_to(slope, (64, 128))
    rows = codes // 128
    for i in range(rows):
        sum_scr[i : i + 1, rest : rest + 128] = usage[:, i * 128 : (i + 1) * 128]
    sum_scr[rows : rows + 1, rest : rest + dim] = bias
    for i in range(devices):
        shards[i][...] = sum_scr[shard_at(partner(me, i, devices), devices)]


def own_kernel(n, count, *refs):
    order, feats, noises, cots, params, (acc_in, _), rest = take(
        refs, 1, n, n, n, 4, 2, len(refs)
    )
    (code_ref, grad_out, acc_ref), (grad_scr, sems), shared, rest = take(rest, 3, 2, 3, 6 * n)
    scrs = take(rest, *[6] * n)
    grads = Gradients(grad_out, grad_scr, sems)
    step = pl.program_id(0)

    @pl.when(step == 0)
    def _():
        prepare(params, *shared)
        acc_ref[...] = acc_in[...]

    grads.ready(step, n)
    states = [
        products(params, shared, scr, feat_ref[...], cot_ref[...], True)
        for scr, feat_ref, cot_ref in zip(scrs, feats, cots)
    ]
    usage = acc_ref[136:144]
    for i, (scr, noise_ref) in enumerate(zip(scrs, noises)):
        usage = both_rows(params, scr, noise_ref, code_ref.at[i], usage)
    acc_ref[136:144] = usage
    values = [
        gradients(params, shared, scr, state, acc_ref) for scr, state in zip(scrs, states)
    ]
    grads.store(step, values, [own_image(step, i, n, order[0], count) for i in range(n)])
    grads.end(step, n, pl.num_programs(0))


def own_image(step, lane, n, order_ref, count):
    share = order_ref.shape[1] // count
    return order_ref[0, lax.axis_index("space") * share + step * n + lane]


def run_own(count, order, feat, noise, cot, params, acc, grad):
    dim, codes = params[2].shape
    images, strip, width = feat.shape
    share = images // count
    n = 2 if share % 2 == 0 else 1

    def image(lane, shape):
        return pl.BlockSpec(
            (None, *shape), lambda i, order_ref: (own_image(i, lane, n, order_ref, count), 0, 0)
        )

    return pl.pallas_call(
        functools.partial(own_kernel, n, count),
        grid_spec=pltpu.PrefetchScalarGridSpec(
            num_scalar_prefetch=1,
            grid=(share // n,),
            in_specs=[image(lane, (strip, width)) for lane in range(n)]
            + [image(lane, (strip, codes)) for lane in range(n)]
            + [image(lane, (dim, strip)) for lane in range(n)]
            + [fixed(p.shape) for p in params]
            + [fixed(acc.shape), HBM],
            out_specs=[
                pl.BlockSpec(
                    (n, strip, codes),
                    lambda i, _: (i, lax.axis_index("space"), 0),
                ),
                HBM,
                fixed(acc.shape),
            ],
            scratch_shapes=gradient_scratch(n, strip, width)
            + shared_scratch(dim, codes, width)
            + tile_scratch(strip, codes) * n,
        ),
        out_shape=[
            pltpu.HBM((share, strip * count, codes), F32),
            pltpu.HBM(feat.shape, F32),
            jax.ShapeDtypeStruct(acc.shape, F32),
        ],
        input_output_aliases={5 + 3 * n: 2, 6 + 3 * n: 1},
        compiler_params=settings(),
        cost_estimate=cost(share * strip, width, dim, codes, 10),
        name="own_images",
    )(
        order,
        *in_hbm([feat] * n + [noise] * n + [cot] * n + [*params[0:3]]),
        params[3],
        acc,
        *in_hbm([grad]),
    )


def place_kernel(count, runs, *refs):
    parts = refs[0 : len(runs)]
    out_ref, sem = refs[len(runs) + 1 : len(runs) + 3]
    me = lax.axis_index("space")
    copies = []
    for part, (step, first, slots) in zip(parts, runs):
        strip = part.shape[0] // slots
        row = pl.multiple_of(source(me, step, count) * strip, strip)
        for j in range(slots):
            copies.append(
                pltpu.make_async_copy(
                    part.at[pl.ds(j * strip, strip)],
                    out_ref.at[first + j, pl.ds(row, strip)],
                    sem.at[len(copies)],
                )
            )
    for copy in copies:
        copy.start()
    for copy in copies:
        copy.wait()


def place_wide(count, runs, parts, whole):
    return pl.pallas_call(
        functools.partial(place_kernel, count, runs),
        out_shape=pltpu.HBM(whole.shape, F32),
        in_specs=[VMEM] * len(runs) + [HBM],
        out_specs=HBM,
        scratch_shapes=[pltpu.SemaphoreType.DMA((sum(r[2] for r in runs),))],
        input_output_aliases={len(runs): 0},
        compiler_params=settings(VMEM_LIMIT // 2),
        cost_estimate=pl.CostEstimate(
            flops=0, bytes_accessed=2 * sum(p.size * 4 for p in parts), transcendentals=0
        ),
        name="place_wide",
    )(*[pltpu.with_memory_space_constraint(p, pltpu.VMEM) for p in parts], *in_hbm([whole]))


def join_kernel(count, *refs):
    parts = refs[0:count]
    outs = refs[count:]
    me = lax.axis_index("space")
    for step in range(count):
        here = source(me, step, count)
        base = 0
        for out in outs:
            for j in range(out.shape[0]):
                strip = out.shape[2]
                out[j, here] = parts[step][base : base + strip]
                base += strip


def join_small(count, parts, shapes):
    codes = parts[0].shape[1]
    return pl.pallas_call(
        functools.partial(join_kernel, count),
        out_shape=[
            jax.ShapeDtypeStruct((images // count, count, strip, codes), F32)
            for images, strip, _ in shapes
        ],
        compiler_params=settings(VMEM_LIMIT // 2),
        name="join_small",
    )(*parts)


def tree(values):
    while len(values) > 1:
        values = [
            values[i] + values[i + 1] if i + 1 < len(values) else values[i]
            for i in range(0, len(values), 2)
        ]
    return values[0]


def sum_kernel(*refs):
    refs[-1][...] = tree([ref[...] for ref in refs[:-1]])


def add_all(parts):
    return pl.pallas_call(
        sum_kernel,
        out_shape=jax.ShapeDtypeStruct(parts[0].shape, F32),
        compiler_params=settings(VMEM_LIMIT // 2),
        name="add_parts",
    )(*parts)


def final_kernel(devices, pixels, *refs):
    shards = refs[0:devices]
    weight_ref, bias_ref, book_ref, log_ref, usage_ref = refs[devices : devices + 5]
    weight_out, bias_out, book_out, log_out, usage_out = refs[devices + 5 : devices + 10]
    sum_scr = refs[devices + 10]
    me = lax.rem(lax.axis_index("dp"), devices)
    for i in range(devices):
        sum_scr[shard_at(source(me, i, devices), devices)] = shards[i][...]
    dim, codes = book_ref.shape
    width = weight_ref.shape[1]
    scale = 0.5 * lax.rsqrt(jnp.full((8, 128), pixels, F32))[0:1, 0:1]
    book_out[...] = 0.5 * book_ref[...] + scale * sum_scr[:, 0:codes]
    rest = codes + width
    weight_out[...] = 0.5 * weight_ref[...] + scale * sum_scr[:, codes:rest]
    rows = codes // 128
    bias_out[...] = 0.5 * bias_ref[...] + scale * sum_scr[rows : rows + 1, rest : rest + dim]
    usage = jnp.concatenate(
        [sum_scr[i : i + 1, rest : rest + 128] for i in range(rows)], axis=1
    )
    usage_out[...] = 0.5 * usage_ref[...] + 0.5 * (codes / pixels) * usage
    log_out[...] = 0.5 * log_ref[...] + scale * sum_scr[rows + 1 : rows + 2, rest : rest + 1]


def finish(devices, pixels, shards, weight, bias, book, log, usage):
    outs = (weight.T, bias.reshape(1, -1), book.T, log.reshape(1, 1), usage.reshape(1, -1))
    outs = pl.pallas_call(
        functools.partial(final_kernel, devices, pixels),
        out_shape=[jax.ShapeDtypeStruct(out.shape, F32) for out in outs],
        scratch_shapes=[pltpu.VMEM((64, LANES), F32)],
        compiler_params=settings(VMEM_LIMIT // 2),
        name="new_averages",
    )(*shards, *outs)
    return outs[0].T, outs[1].reshape(-1), outs[2].T, outs[3].reshape(-1), outs[4].reshape(-1)


def exchange(value, bit, size, pairs):
    while bit < size:
        value = value + pairs(value, bit)
        bit = 2 * bit
    return value


def per_device(
    feat_small,
    feat_mid,
    feat_wide,
    noise_small,
    noise_mid,
    noise_wide,
    cot_small,
    cot_mid,
    cot_wide,
    order_small,
    order_mid,
    order_wide,
    weight,
    bias,
    book,
    log,
    heat,
    weight_mean,
    bias_mean,
    book_mean,
    log_mean,
    usage_mean,
):
    count = lax.axis_size("space")
    devices = lax.axis_size("dp")
    params = (weight.T, bias.reshape(1, -1), book.T, log, heat)
    feats = (feat_small, feat_mid, feat_wide)
    pixels = sum(f.shape[0] * f.shape[1] for f in feats) * count * devices
    share = feat_wide.shape[0] // count
    cot_wide = jnp.swapaxes(cot_wide, 1, 2)

    def send(values):
        return [lax.ppermute(v, "space", route(i + 1, count)) for i, v in enumerate(values)]

    def follow(codes, before):
        before[:], codes[-1] = lax.optimization_barrier((before, codes[-1]))
        return send(codes)

    orders = (order_small, order_mid)
    noises = (noise_small, noise_mid)
    *small, usage, scalar = small_forward(
        count, range(1, count), orders, feats[0:2], noises, params
    )
    arrived = [send(small)]
    own_params = params
    params = (*params[0:3], scalar)
    near = min(4, devices)
    last = count - 1
    early = [(step, 0, 1) for step in range(1, count)]
    direct = [(step, 1, share - 1) for step in range(1, last)]
    late = [(last, 1, share - 1)]
    *early_codes, usage = wide_forward(
        count, split(early, 3), False, order_wide, feat_wide, noise_wide, params, usage, 4
    )
    arrived.append(follow(list(early_codes), arrived[0]))
    *codes, grad, acc = wide_both(
        count, split(direct, 2), order_wide, feat_wide, noise_wide, cot_wide, params
    )
    late_lanes = [Lane([(last, slot, 1)]) for slot in range(1, share)]
    late_codes, usage = wide_forward(
        count, late_lanes, True, order_wide, feat_wide, noise_wide, params, usage, 1
    )
    arrived.append(follow([*codes, late_codes], arrived[1]))
    arrived[1], acc = lax.optimization_barrier((arrived[1], acc))
    whole, grad, acc = run_own(
        count, order_wide, feat_wide, noise_wide, cot_wide, params, acc, grad
    )
    whole = place_wide(count, early, arrived[1], whole)
    acc, own_params = lax.optimization_barrier((acc, own_params))
    own, own_usage, _ = small_forward(
        count, range(1), orders, feats[0:2], noises, own_params
    )
    small = [own, *small]
    codes_small, codes_mid = join_small(
        count, [own] + arrived[0], [f.shape for f in feats[0:2]]
    )
    whole, codes_small, codes_mid, acc = lax.optimization_barrier(
        (whole, codes_small, codes_mid, acc)
    )
    grad, acc = wide_backward(
        count,
        split(early + late, 2),
        [*early_codes, late_codes],
        order_wide,
        feat_wide,
        cot_wide,
        params,
        acc,
        grad,
    )
    grad_small, grad_mid, *shards = small_backward(
        count,
        near,
        orders,
        feats[0:2],
        (cot_small, cot_mid),
        small,
        params,
        acc,
        (usage, own_usage),
    )
    group = [
        [(i, i - i % near + partner(i % near, step, near)) for i in range(devices)]
        for step in range(near)
    ]
    parts = [lax.ppermute(shards[i], "dp", group[i]) for i in range(1, near)]
    mine = add_all([shards[0]] + parts)

    def along(value, offset):
        return lax.ppermute(value, "dp", [(i, i ^ offset) for i in range(devices)])

    def across(value, offset):
        turn = near if devices > near else 0
        pairs = [
            (i * count + j, (i ^ turn) * count + (j ^ offset))
            for i in range(devices)
            for j in range(count)
        ]
        return lax.ppermute(value, ("dp", "space"), pairs)

    mine = exchange(mine, near, devices, along)
    mine = exchange(mine, 1, count, across)
    shards = [mine] + [lax.ppermute(mine, "dp", group[i]) for i in range(1, near)]
    updated = finish(
        near, pixels, shards, weight_mean, bias_mean, book_mean, log_mean, usage_mean
    )
    for run, part in zip(direct + late, arrived[2]):
        whole = place_wide(count, [run], [part], whole)
    codes = whole.shape[2]
    return (
        codes_small.reshape(codes_small.shape[0], -1, codes),
        codes_mid.reshape(codes_mid.shape[0], -1, codes),
        whole,
        grad_small,
        grad_mid,
        grad,
        *updated,
    )


def solution(mesh):
    strips = P("dp", "space", None)
    placed = (strips,) * 9 + (P("dp", None),) * 3 + (P(),) * 10
    return jax.shard_map(
        per_device,
        mesh=mesh,
        in_specs=placed,
        out_specs=(P(("dp", "space"), None, None),) * 3 + (strips,) * 3 + (P(),) * 5,
        check_vma=False,
    )
```

```python
import functools

import jax
import jax.numpy as jnp
from jax import lax
from jax.experimental import pallas as pl
from jax.experimental.pallas import tpu as pltpu
from jax.sharding import PartitionSpec as P

F32 = jnp.float32
BF16 = jnp.bfloat16
VMEM_LIMIT = 24 * 1024 * 1024
ACC_ROWS = 64 + 64 + 8 + 8 + 64 + 8
LANES = 896


def partner(index, step, count):
    if count & (count - 1) == 0:
        return index ^ step
    return lax.rem(index + step, count)


def route(step, count):
    if count & (count - 1) == 0:
        return [(i, i ^ step) for i in range(count)]
    return [(i, (i + step) % count) for i in range(count)]


def source(index, step, count):
    if count & (count - 1) == 0:
        return index ^ step
    return lax.rem(index + (count - step), count)


def in_hbm(arrays):
    return [pltpu.with_memory_space_constraint(a, pltpu.HBM) for a in arrays]


def halves(x):
    high = x.astype(BF16)
    return high, (x - high.astype(F32)).astype(BF16)


def dot(left, right, left_dim=1, right_dim=0):
    return lax.dot_general(
        left, right, (((left_dim,), (right_dim,)), ((), ())), preferred_element_type=F32
    )


def set_scalars(log_ref, heat_ref, out_ref):
    precision = jnp.exp(jnp.full((8, 128), log_ref[0], F32))
    heat = jnp.full((8, 128), heat_ref[0], F32)
    row = lax.broadcasted_iota(jnp.int32, (8, 128), 0)
    factor = -0.5 * precision / heat
    out_ref[...] = jnp.where(row == 0, precision, jnp.where(row == 1, 1.0 / heat, factor))


def scalars(ref):
    return ref[0:1, 0:1], ref[1:2, 0:1], ref[2:3, 0:1]


def prepare(refs, book_scr, books_scr, weight_scr, backward=True):
    weight_ref, bias_ref, book_ref, scalar_ref = refs
    dim, codes = book_ref.shape
    precision, _, _ = scalars(scalar_ref)
    book = book_ref[...]
    high, low = halves(book)
    norm = -0.5 * precision * jnp.sum(book * book, axis=0, keepdims=True)
    n0 = norm.astype(BF16).astype(F32)
    n1 = (norm - n0).astype(BF16).astype(F32)
    n2 = norm - n0 - n1
    row = lax.broadcasted_iota(jnp.int32, (16, codes), 0)
    extra = jnp.where(
        row < 3,
        1.0,
        jnp.where(row == 3, n0, jnp.where(row == 4, n1, jnp.where(row == 5, n2, 0.0))),
    ).astype(BF16)
    book_scr[0:dim] = high
    book_scr[dim : 2 * dim] = low
    book_scr[2 * dim : 3 * dim] = high
    book_scr[3 * dim : 3 * dim + 16] = extra
    if backward:
        books_scr[0:dim] = high
        books_scr[dim : 2 * dim] = low
        books_scr[2 * dim : 2 * dim + 16] = jnp.ones((16, codes), BF16)
    high, low = halves(weight_ref[...])
    weight_scr[0:dim] = high
    weight_scr[dim : 2 * dim] = low
    weight_scr[2 * dim : 3 * dim] = high


def latents(refs, shared, feat):
    weight_ref, bias_ref, book_ref, scalar_ref = refs
    weight_scr = shared[2]
    dim = book_ref.shape[0]
    precision, _, _ = scalars(scalar_ref)
    eye = lax.broadcasted_iota(jnp.int32, (dim, dim), 0) == lax.broadcasted_iota(
        jnp.int32, (dim, dim), 1
    )
    bias = jnp.sum(jnp.where(eye, bias_ref[...], 0.0), axis=1, keepdims=True)
    fh, fl = halves(feat)
    both = weight_scr[0 : 2 * dim]
    z2 = dot(both, fh, 1, 1) + dot(both, fl, 1, 1)
    z = z2[0:dim] + z2[dim : 2 * dim] + bias
    square = -0.5 * precision * jnp.sum(z * z, axis=0, keepdims=True)
    return fh, fl, z, square


def logit_rows(zh, zl, square):
    rows = zh.shape[1]
    s0 = square.astype(BF16).astype(F32)
    s1 = (square - s0).astype(BF16).astype(F32)
    s2 = square - s0 - s1
    row = lax.broadcasted_iota(jnp.int32, (16, rows), 0)
    extra = jnp.where(
        row == 0,
        s0,
        jnp.where(row == 1, s1, jnp.where(row == 2, s2, jnp.where(row < 6, 1.0, 0.0))),
    ).astype(BF16)
    return jnp.concatenate([zh, zh, zl, extra], axis=0)


def cot_rows(ch, cl):
    return jnp.concatenate([ch, ch, cl, jnp.zeros((16, ch.shape[1]), BF16)], axis=0)


def over_rows(rows, body, carry):
    step = next(s for s in (32, 16, 8) if rows % s == 0)

    def at(i, carry):
        return body(pl.ds(pl.multiple_of(i * step, step), step), carry)

    return lax.fori_loop(0, rows // step, at, carry, unroll=True)


def folded(x):
    return jnp.sum(x.reshape(x.shape[0] // 8, 8, x.shape[1]), axis=0)


def probabilities(logits):
    top = jnp.max(logits, axis=1, keepdims=True)
    e = jnp.exp(logits - top)
    return e * (1.0 / jnp.sum(e, axis=1, keepdims=True))


def forward_products(refs, shared, feat, l_scr):
    precision, _, _ = scalars(refs[3])
    _, _, z, square = latents(refs, shared, feat)
    zh, zl = halves(precision * z)
    l_scr[0 : feat.shape[0]] = dot(logit_rows(zh, zl, square), shared[0][...], 0, 0)


def forward_rows(refs, l_scr, noise_ref, code_ref, usage):
    _, cold, _ = scalars(refs[3])

    def body(at, usage):
        logits = l_scr[at]
        code_ref[at] = probabilities((logits + noise_ref[at]) * cold)
        return usage + folded(probabilities(logits))

    return over_rows(code_ref.shape[0], body, usage)


def products(refs, shared, scr, feat, cot, forward):
    l_scr, g_scr = scr[0:2]
    rows = feat.shape[0]
    precision, _, factor = scalars(refs[3])
    fh, fl, z, square = latents(refs, shared, feat)
    zh, zl = halves(precision * z)
    ch, cl = halves(factor * cot)
    if forward:
        left = jnp.concatenate([logit_rows(zh, zl, square), cot_rows(ch, cl)], axis=1)
        p = dot(left, shared[0][...], 0, 0)
        l_scr[0:rows] = p[0:rows]
        g_scr[0:rows] = p[rows : 2 * rows]
    else:
        g_scr[0:rows] = dot(cot_rows(ch, cl), shared[0][...], 0, 0)
    return fh, fl, z, square, zh, zl, ch, cl


def both_rows(refs, scr, noise_ref, code_ref, usage):
    l_scr, g_scr, wh_scr, wl_scr, gh_scr, gl_scr = scr
    _, cold, _ = scalars(refs[3])

    def body(at, usage):
        logits = l_scr[at]
        s = (logits + noise_ref[at]) * cold
        e = jnp.exp(s - jnp.max(s, axis=1, keepdims=True))
        gw = g_scr[at]
        scale = 1.0 / jnp.sum(e, axis=1, keepdims=True)
        inner = jnp.sum(e * gw, axis=1, keepdims=True) * scale
        w = e * scale
        code_ref[at] = w
        gd = w * (gw - inner)
        wh_scr[at], wl_scr[at] = halves(w)
        gh_scr[at], gl_scr[at] = halves(gd)
        return usage + folded(probabilities(logits))

    return over_rows(code_ref.shape[0], body, usage)


def backward_rows(scr, code_ref):
    _, g_scr, wh_scr, wl_scr, gh_scr, gl_scr = scr

    def body(at, carry):
        w = code_ref[at]
        gw = g_scr[at]
        gd = w * (gw - jnp.sum(w * gw, axis=1, keepdims=True))
        wh_scr[at], wl_scr[at] = halves(w)
        gh_scr[at], gl_scr[at] = halves(gd)
        return carry

    over_rows(code_ref.shape[0], body, 0)


def gradients(refs, shared, scr, state, acc_ref):
    _, books_scr, weight_scr = shared
    wh_scr, wl_scr, gh_scr, gl_scr = scr[2:6]
    fh, fl, z, square, zh, zl, ch, cl = state
    rows, feats = fh.shape
    dim, codes = refs[2].shape
    wh, wl = wh_scr[0:rows], wl_scr[0:rows]
    gh, gl = gh_scr[0:rows], gl_scr[0:rows]
    p = dot(jnp.concatenate([ch, cl], axis=0), wh)
    acc_ref[0:64] += p[0:dim] + p[dim : 2 * dim] + dot(ch, wl)
    left = jnp.concatenate([zh, zl, jnp.ones((16, rows), BF16)], axis=0)
    p = dot(left, gh) + dot(left, gl)
    acc_ref[64:128] += p[0:dim] + p[dim : 2 * dim]
    acc_ref[128:136] += p[2 * dim : 2 * dim + 8]
    p = dot(books_scr[...], gh, 1, 1) + dot(books_scr[...], gl, 1, 1)
    row_d = p[2 * dim : 2 * dim + 1]
    gz = 2.0 * (row_d * z - (p[0:dim] + p[dim : 2 * dim]))
    zh, zl = halves(gz)
    p = dot(jnp.concatenate([zh, zl], axis=0), fh)
    acc_ref[144:208, 0:feats] += p[0:dim] + p[dim : 2 * dim] + dot(zh, fl)
    acc_ref[144:208, feats : feats + 128] += jnp.broadcast_to(
        jnp.sum(gz, axis=1, keepdims=True), (dim, 128)
    )
    total = jnp.sum(square * row_d, axis=1, keepdims=True)
    acc_ref[208:216] += jnp.broadcast_to(total, (8, codes))
    return dot(jnp.concatenate([zh, zh, zl], axis=0), weight_scr[...], 0, 0)


def shared_scratch(dim, codes, feats):
    return [
        pltpu.VMEM((3 * dim + 16, codes), BF16),
        pltpu.VMEM((2 * dim + 16, codes), BF16),
        pltpu.VMEM((3 * dim, feats), BF16),
    ]


def tile_scratch(rows, codes):
    return [pltpu.VMEM((rows, codes), F32)] * 2 + [pltpu.VMEM((rows, codes), BF16)] * 4


def settings(limit=VMEM_LIMIT):
    return pltpu.CompilerParams(vmem_limit_bytes=limit)


def cost(rows, feats, dim, codes, tenths):
    return pl.CostEstimate(
        flops=rows * 24 * tenths * (5 * dim * codes + 3 * dim * feats) // 10,
        bytes_accessed=4 * rows * (2 * feats + 2 * codes + dim),
        transcendentals=2 * rows * codes,
    )


SMEM = pl.BlockSpec(memory_space=pltpu.SMEM)
VMEM = pl.BlockSpec(memory_space=pltpu.VMEM)
HBM = pl.BlockSpec(memory_space=pltpu.HBM)


def fixed(shape):
    return pl.BlockSpec(shape, lambda *_: (0,) * len(shape))


class Lane:
    def __init__(self, runs):
        self.runs = list(runs)
        self.bounds = [0]
        for _, _, slots in self.runs:
            self.bounds.append(self.bounds[-1] + slots)

    def total(self):
        return self.bounds[-1]

    def index(self, i, order_ref, count):
        share = order_ref.shape[1] // count
        step, slot = 0, 0
        for (whose, first, _), start in zip(self.runs, self.bounds):
            here = first + i - start
            step = whose if start == 0 else jnp.where(i >= start, whose, step)
            slot = here if start == 0 else jnp.where(i >= start, here, slot)
        there = partner(lax.axis_index("space"), step, count)
        return order_ref[0, there * share + slot]

    def image(self, shape, count):
        return pl.BlockSpec(
            (None, *shape), lambda i, order_ref: (self.index(i, order_ref, count), 0, 0)
        )

    def blocks(self, shape):
        return [
            pl.BlockSpec(
                shape,
                lambda i, _, start=start, last=slots - 1: (jnp.clip(i - start, 0, last), 0),
            )
            for (_, _, slots), start in zip(self.runs, self.bounds)
        ]

    def each(self, step, body):
        for i, (low, high) in enumerate(zip(self.bounds, self.bounds[1:])):
            pl.when((step >= low) & (step < high))(functools.partial(body, i))


def split(runs, ways):
    whole = Lane(runs)
    lanes, current = [], []
    for run in whole.runs:
        current.append(run)
        if Lane(current).total() * ways == whole.total():
            lanes.append(Lane(current))
            current = []
    return lanes if len(lanes) == ways and not current else [whole]


def take(refs, *sizes):
    groups, at = [], 0
    for size in sizes:
        groups.append(refs[at : at + size])
        at += size
    return groups


def by_lane(refs, lanes):
    return take(refs, *[len(lane.runs) for lane in lanes])


def keep_codes(step, lanes, sends, code_scrs):
    for lane, refs, code_scr in zip(lanes, by_lane(sends, lanes), code_scrs):
        if len(lane.runs) > 1:

            def keep(i, refs=refs, code_scr=code_scr):
                refs[i][...] = code_scr[...]

            lane.each(step, keep)


def code_targets(lanes, sends, code_scrs):
    return [
        refs[0] if len(lane.runs) == 1 else code_scr
        for lane, refs, code_scr in zip(lanes, by_lane(sends, lanes), code_scrs)
    ]


class Gradients:
    def __init__(self, out_ref, scr, sems):
        self.out_ref, self.scr, self.sems = out_ref, scr, sems

    def copy(self, lane, slot, image):
        return pltpu.make_async_copy(
            self.scr.at[lane, slot], self.out_ref.at[image], self.sems.at[lane, slot]
        )

    def ready(self, step, lanes):
        @pl.when(step >= 2)
        def _():
            for lane in range(lanes):
                self.copy(lane, lax.rem(step, 2), 0).wait()

    def store(self, step, values, images):
        slot = lax.rem(step, 2)
        for lane, (value, image) in enumerate(zip(values, images)):
            self.scr[lane, slot] = value
            self.copy(lane, slot, image).start()

    def end(self, step, lanes, steps):
        @pl.when(step == steps - 1)
        def _():
            for lane in range(lanes):
                for slot in range(min(2, steps)):
                    self.copy(lane, slot, 0).wait()


def gradient_scratch(lanes, strip, width):
    return [pltpu.VMEM((lanes, 2, strip, width), F32), pltpu.SemaphoreType.DMA((lanes, 2))]


def places_of(orders, shapes, groups, steps, count):
    me = lax.axis_index("space")
    strips = []
    at = 0
    for k, step in enumerate(steps):
        there = partner(me, step, count)
        row = 0
        for size in range(2):
            strip = shapes[size][1]
            for j in range(groups[size]):
                image = orders[size][0, there * groups[size] + j]
                strips.append((k, row, size, image, at, strip))
                row += strip
                at += strip
    return strips


def small_forward_kernel(count, steps, groups, *refs):
    sources, wide_in, (log_ref, heat_ref), sends, (usage_ref, scalar_ref), wide_out, held, rest = (
        take(refs, 9, 1, 2, len(steps), 2, 1, 9, len(refs))
    )
    (sems, feat_scr), shared, (l_scr, noise_scr) = take(rest, 2, 3, 2)
    copies = [
        pltpu.make_async_copy(there, here, sems.at[i])
        for i, (there, here) in enumerate(zip([*sources, *wide_in], [*held, *wide_out]))
    ]
    for copy in copies:
        copy.start()
    params, orders, feats, noises = (*held[0:3], scalar_ref), held[3:5], held[5:7], held[7:9]
    set_scalars(log_ref, heat_ref, scalar_ref)
    for copy in copies[0:3]:
        copy.wait()
    prepare(params, *shared, backward=False)
    for copy in copies[3:7]:
        copy.wait()
    strips = places_of(orders, [f.shape for f in feats], groups, steps, count)
    for _, _, size, image, at, strip in strips:
        feat_scr[at : at + strip] = feats[size][image]
    forward_products(params, shared, feat_scr[...], l_scr)
    for copy in copies[7:9]:
        copy.wait()
    usage = jnp.zeros(usage_ref.shape, F32)
    part = sends[0].shape[0]
    if all(noise.shape[1] % 8 == 0 for noise in noises):
        for k, row, size, image, at, strip in strips:
            rows = pl.ds(at, strip)
            target = sends[k].at[pl.ds(row, strip)]
            usage = forward_rows(params, l_scr.at[rows], noises[size].at[image], target, usage)
    else:
        for _, _, size, image, at, strip in strips:
            noise_scr[at : at + strip] = noises[size][image]
        for k, send in enumerate(sends):
            rows = pl.ds(k * part, part)
            usage = forward_rows(params, l_scr.at[rows], noise_scr.at[rows], send, usage)
    usage_ref[...] = usage
    copies[9].wait()


def small_forward(count, steps, orders, feats, noises, params):
    dim, codes = params[2].shape
    width = feats[0].shape[2]
    groups = tuple(f.shape[0] // count for f in feats)
    part = sum(g * f.shape[1] for g, f in zip(groups, feats))
    rows = part * len(steps)
    arrays = [*params[0:3], *orders[0:2], *feats, *noises]
    return pl.pallas_call(
        functools.partial(small_forward_kernel, count, steps, groups),
        out_shape=[jax.ShapeDtypeStruct((part, codes), F32)] * len(steps)
        + [
            jax.ShapeDtypeStruct((8, codes), F32),
            jax.ShapeDtypeStruct((8, 128), F32),
            jax.ShapeDtypeStruct(orders[2].shape, jnp.int32),
        ],
        in_specs=[HBM] * 10 + [SMEM] * 2,
        out_specs=[VMEM] * (len(steps) + 3),
        scratch_shapes=[
            (pltpu.SMEM if 3 <= i < 5 else pltpu.VMEM)(a.shape, a.dtype)
            for i, a in enumerate(arrays)
        ]
        + [pltpu.SemaphoreType.DMA((10,)), pltpu.VMEM((rows, width), F32)]
        + shared_scratch(dim, codes, width)
        + [pltpu.VMEM((rows, codes), F32)] * 2,
        compiler_params=settings(),
        cost_estimate=cost(rows, width, dim, codes, 4),
        name="small_forward",
    )(*in_hbm([*arrays, orders[2]]), *params[3:5])


def small_backward_kernel(count, steps, devices, groups, *refs):
    orders, feats, cots, parts, params, (acc_in, *usages), grads, shards, rest = take(
        refs, 2, 2, 2, count, 4, 3, 2, devices, len(refs)
    )
    acc_ref, sum_scr, feat_scr, cot_scr, code_scr = rest[0:5]
    scr = rest[5:]
    strips = places_of(orders, [f.shape for f in feats], groups, steps, count)
    for _, _, size, image, at, strip in strips:
        feat_scr[at : at + strip] = feats[size][image]
        cot_scr[at : at + strip] = cots[size][image]
    part = parts[0].shape[0]
    for step in range(count):
        code_scr[step * part : (step + 1) * part] = parts[step][...]
    shared, tile_scr = take(scr, 3, 6)
    prepare(params, *shared)
    acc_ref[...] = acc_in[...]
    state = products(params, shared, tile_scr, feat_scr[...], cot_scr[...].T, False)
    backward_rows(tile_scr, code_scr)
    feat_scr[...] = gradients(params, shared, tile_scr, state, acc_ref)
    acc_ref[136:144] += usages[0][...] + usages[1][...]
    lay_out(params, acc_ref, sum_scr, shards)
    for _, _, size, image, at, strip in strips:
        grads[size][image] = feat_scr[at : at + strip]


def small_backward(count, steps, devices, orders, feats, cots, parts, params, acc, usages):
    dim, codes = params[2].shape
    width = feats[0].shape[2]
    groups = tuple(f.shape[0] // count for f in feats)
    rows = parts[0].shape[0] * count
    return pl.pallas_call(
        functools.partial(small_backward_kernel, count, steps, devices, groups),
        out_shape=[pltpu.HBM(f.shape, F32) for f in feats]
        + [jax.ShapeDtypeStruct((64 // devices, LANES), F32)] * devices,
        in_specs=[SMEM] * 2 + [VMEM] * (11 + count),
        out_specs=[VMEM] * (2 + devices),
        scratch_shapes=[
            pltpu.VMEM(acc.shape, F32),
            pltpu.VMEM((64, LANES), F32),
            pltpu.VMEM((rows, width), F32),
            pltpu.VMEM((rows, dim), F32),
            pltpu.VMEM((rows, codes), F32),
        ]
        + shared_scratch(dim, codes, width)
        + tile_scratch(rows, codes),
        compiler_params=settings(),
        cost_estimate=cost(rows, width, dim, codes, 6),
        name="small_backward",
    )(
        *orders,
        *in_hbm([*feats, *cots]),
        *parts,
        *in_hbm(params[0:3]),
        params[3],
        acc,
        *usages,
    )


def wide_forward_kernel(lanes, joined, *refs):
    n = len(lanes)
    arrays = 1 if joined else sum(len(lane.runs) for lane in lanes)
    _, feats, noises, params, usage_in, sends, rest = take(
        refs, 1, n, n, 4, 1, arrays, len(refs)
    )
    (usage_ref,), code_scrs, shared, l_scrs = take(rest, 1, n, 3, n)
    step = pl.program_id(0)

    @pl.when(step == 0)
    def _():
        prepare(params, *shared, backward=False)
        usage_ref[...] = usage_in[0][...]

    if joined:
        strip = code_scrs[0].shape[0]
        targets = [sends[0].at[pl.ds(i * strip, strip)] for i in range(n)]
    else:
        targets = code_targets(lanes, sends, code_scrs)
    for feat_ref, l_scr in zip(feats, l_scrs):
        forward_products(params, shared, feat_ref[...], l_scr)
    usage = usage_ref[...]
    for l_scr, noise_ref, target in zip(l_scrs, noises, targets):
        usage = forward_rows(params, l_scr, noise_ref, target, usage)
    usage_ref[...] = usage
    if not joined:
        keep_codes(step, lanes, sends, code_scrs)


def wide_forward(count, lanes, joined, order, feat, noise, params, usage, tenths):
    dim, codes = params[2].shape
    images, strip, width = feat.shape
    n, steps = len(lanes), lanes[0].total()
    if joined:
        blocks = [fixed((n * strip, codes))]
        sizes = [n]
    else:
        blocks = [block for lane in lanes for block in lane.blocks((strip, codes))]
        sizes = [run[2] for lane in lanes for run in lane.runs]
    return pl.pallas_call(
        functools.partial(wide_forward_kernel, lanes, joined),
        grid_spec=pltpu.PrefetchScalarGridSpec(
            num_scalar_prefetch=1,
            grid=(steps,),
            in_specs=[lane.image((strip, width), count) for lane in lanes]
            + [lane.image((strip, codes), count) for lane in lanes]
            + [fixed(p.shape) for p in params]
            + [fixed(usage.shape)],
            out_specs=blocks + [fixed(usage.shape)],
            scratch_shapes=[pltpu.VMEM((strip, codes), F32)] * n
            + shared_scratch(dim, codes, width)
            + [pltpu.VMEM((strip, codes), F32)] * n,
        ),
        out_shape=[jax.ShapeDtypeStruct((strip * slots, codes), F32) for slots in sizes]
        + [jax.ShapeDtypeStruct(usage.shape, F32)],
        input_output_aliases={5 + 2 * n: len(sizes)},
        compiler_params=settings(),
        cost_estimate=cost(n * steps * strip, width, dim, codes, tenths),
        name="wide_forward",
    )(order, *in_hbm([feat] * n + [noise] * n + [*params[0:3]]), params[3], usage)


def wide_both_kernel(lanes, count, *refs):
    n = len(lanes)
    arrays = sum(len(lane.runs) for lane in lanes)
    order, feats, noises, cots, params, sends, rest = take(
        refs, 1, n, n, n, 4, arrays, len(refs)
    )
    (grad_out, acc_ref), code_scrs, (grad_scr, sems), shared, rest = take(
        rest, 2, n, 2, 3, 6 * n
    )
    scrs = take(rest, *[6] * n)
    grads = Gradients(grad_out, grad_scr, sems)
    step, steps = pl.program_id(0), lanes[0].total()

    @pl.when(step == 0)
    def _():
        prepare(params, *shared)
        acc_ref[...] = jnp.zeros(acc_ref.shape, F32)

    grads.ready(step, n)
    targets = code_targets(lanes, sends, code_scrs)
    states = [
        products(params, shared, scr, feat_ref[...], cot_ref[...], True)
        for scr, feat_ref, cot_ref in zip(scrs, feats, cots)
    ]
    usage = acc_ref[136:144]
    for scr, noise_ref, target in zip(scrs, noises, targets):
        usage = both_rows(params, scr, noise_ref, target, usage)
    acc_ref[136:144] = usage
    values = [
        gradients(params, shared, scr, state, acc_ref) for scr, state in zip(scrs, states)
    ]
    grads.store(step, values, [lane.index(step, order[0], count) for lane in lanes])
    keep_codes(step, lanes, sends, code_scrs)
    grads.end(step, n, steps)


def wide_both(count, lanes, order, feat, noise, cot, params):
    dim, codes = params[2].shape
    images, strip, width = feat.shape
    n, steps = len(lanes), lanes[0].total()
    acc_shape = (ACC_ROWS, codes)
    sizes = [run[2] for lane in lanes for run in lane.runs]
    return pl.pallas_call(
        functools.partial(wide_both_kernel, lanes, count),
        grid_spec=pltpu.PrefetchScalarGridSpec(
            num_scalar_prefetch=1,
            grid=(steps,),
            in_specs=[lane.image((strip, width), count) for lane in lanes]
            + [lane.image((strip, codes), count) for lane in lanes]
            + [lane.image((dim, strip), count) for lane in lanes]
            + [fixed(p.shape) for p in params],
            out_specs=[block for lane in lanes for block in lane.blocks((strip, codes))]
            + [HBM, fixed(acc_shape)],
            scratch_shapes=[pltpu.VMEM((strip, codes), F32)] * n
            + gradient_scratch(n, strip, width)
            + shared_scratch(dim, codes, width)
            + tile_scratch(strip, codes) * n,
        ),
        out_shape=[jax.ShapeDtypeStruct((strip * slots, codes), F32) for slots in sizes]
        + [pltpu.HBM(feat.shape, F32), jax.ShapeDtypeStruct(acc_shape, F32)],
        compiler_params=settings(),
        cost_estimate=cost(n * steps * strip, width, dim, codes, 10),
        name="wide_both",
    )(order, *in_hbm([feat] * n + [noise] * n + [cot] * n + [*params[0:3]]), params[3])


def wide_backward_kernel(lanes, count, *refs):
    n = len(lanes)
    arrays = sum(len(lane.runs) for lane in lanes)
    order, feats, cots, parts, params, (acc_in, _), rest = take(
        refs, 1, n, n, arrays, 4, 2, len(refs)
    )
    (grad_out, acc_ref), code_scrs, (grad_scr, sems), shared, rest = take(
        rest, 2, n, 2, 3, 6 * n
    )
    scrs = take(rest, *[6] * n)
    grads = Gradients(grad_out, grad_scr, sems)
    step, steps = pl.program_id(0), lanes[0].total()

    @pl.when(step == 0)
    def _():
        prepare(params, *shared)
        acc_ref[...] = acc_in[...]

    grads.ready(step, n)
    for lane, refs_of, code_scr in zip(lanes, by_lane(parts, lanes), code_scrs):
        if len(lane.runs) > 1:

            def fetch(i, refs_of=refs_of, code_scr=code_scr):
                code_scr[...] = refs_of[i][...]

            lane.each(step, fetch)
    states = [
        products(params, shared, scr, feat_ref[...], cot_ref[...], False)
        for scr, feat_ref, cot_ref in zip(scrs, feats, cots)
    ]
    for scr, code_ref in zip(scrs, code_targets(lanes, parts, code_scrs)):
        backward_rows(scr, code_ref)
    values = [
        gradients(params, shared, scr, state, acc_ref) for scr, state in zip(scrs, states)
    ]
    grads.store(step, values, [lane.index(step, order[0], count) for lane in lanes])
    grads.end(step, n, steps)


def wide_backward(count, lanes, parts, order, feat, cot, params, acc, grad):
    dim, codes = params[2].shape
    images, strip, width = feat.shape
    n, steps = len(lanes), lanes[0].total()
    return pl.pallas_call(
        functools.partial(wide_backward_kernel, lanes, count),
        grid_spec=pltpu.PrefetchScalarGridSpec(
            num_scalar_prefetch=1,
            grid=(steps,),
            in_specs=[lane.image((strip, width), count) for lane in lanes]
            + [lane.image((dim, strip), count) for lane in lanes]
            + [block for lane in lanes for block in lane.blocks((strip, codes))]
            + [fixed(p.shape) for p in params]
            + [fixed(acc.shape), HBM],
            out_specs=[HBM, fixed(acc.shape)],
            scratch_shapes=[pltpu.VMEM((strip, codes), F32)] * n
            + gradient_scratch(n, strip, width)
            + shared_scratch(dim, codes, width)
            + tile_scratch(strip, codes) * n,
        ),
        out_shape=[pltpu.HBM(feat.shape, F32), jax.ShapeDtypeStruct(acc.shape, F32)],
        input_output_aliases={5 + 2 * n + len(parts): 1, 6 + 2 * n + len(parts): 0},
        compiler_params=settings(),
        cost_estimate=cost(n * steps * strip, width, dim, codes, 6),
        name="wide_backward",
    )(
        order,
        *in_hbm([feat] * n + [cot] * n),
        *parts,
        *in_hbm(params[0:3]),
        params[3],
        acc,
        *in_hbm([grad]),
    )


def shard_at(index, parts):
    height = 64 // parts
    return pl.ds(pl.multiple_of(index * height, height), height)


def lay_out(params, acc_ref, sum_scr, shards):
    weight_ref, bias_ref, book_ref, scalar_ref = params
    codes = book_ref.shape[1]
    width = weight_ref.shape[1]
    devices = len(shards)
    me = lax.rem(lax.axis_index("dp"), devices)
    precision, _, factor = scalars(scalar_ref)
    book = book_ref[...]
    column = acc_ref[128:129]
    moment = acc_ref[64:128] * (1.0 / precision)
    book_sum = acc_ref[0:64] * (1.0 / factor) + 2.0 * (column * book - moment)
    slope = jnp.sum(
        jnp.sum(book * book, axis=0, keepdims=True) * column, axis=1, keepdims=True
    ) - 2.0 * jnp.sum(jnp.sum(book * moment, axis=0, keepdims=True), axis=1, keepdims=True)
    slope = slope + acc_ref[208:209, 0:1] / (-0.5 * precision)
    usage = jnp.sum(acc_ref[136:144], axis=0, keepdims=True)
    dim = book_ref.shape[0]
    eye = lax.broadcasted_iota(jnp.int32, (dim, dim), 0) == lax.broadcasted_iota(
        jnp.int32, (dim, dim), 1
    )
    bias = acc_ref[144:208, width : width + dim]
    bias = jnp.sum(jnp.where(eye, bias, 0.0), axis=0, keepdims=True)
    rest = codes + width
    sum_scr[:, 0:codes] = book_sum
    sum_scr[:, codes:rest] = acc_ref[144:208, 0:width]
    sum_scr[:, rest : rest + 128] = jnp.broadcast_to(slope, (64, 128))
    rows = codes // 128
    for i in range(rows):
        sum_scr[i : i + 1, rest : rest + 128] = usage[:, i * 128 : (i + 1) * 128]
    sum_scr[rows : rows + 1, rest : rest + dim] = bias
    for i in range(devices):
        shards[i][...] = sum_scr[shard_at(partner(me, i, devices), devices)]


def own_kernel(n, count, *refs):
    order, feats, noises, cots, params, (acc_in, _), rest = take(
        refs, 1, n, n, n, 4, 2, len(refs)
    )
    (code_ref, grad_out, acc_ref), (grad_scr, sems), shared, rest = take(rest, 3, 2, 3, 6 * n)
    scrs = take(rest, *[6] * n)
    grads = Gradients(grad_out, grad_scr, sems)
    step = pl.program_id(0)

    @pl.when(step == 0)
    def _():
        prepare(params, *shared)
        acc_ref[...] = acc_in[...]

    grads.ready(step, n)
    states = [
        products(params, shared, scr, feat_ref[...], cot_ref[...], True)
        for scr, feat_ref, cot_ref in zip(scrs, feats, cots)
    ]
    usage = acc_ref[136:144]
    for i, (scr, noise_ref) in enumerate(zip(scrs, noises)):
        usage = both_rows(params, scr, noise_ref, code_ref.at[i], usage)
    acc_ref[136:144] = usage
    values = [
        gradients(params, shared, scr, state, acc_ref) for scr, state in zip(scrs, states)
    ]
    grads.store(step, values, [own_image(step, i, n, order[0], count) for i in range(n)])
    grads.end(step, n, pl.num_programs(0))


def own_image(step, lane, n, order_ref, count):
    share = order_ref.shape[1] // count
    return order_ref[0, lax.axis_index("space") * share + step * n + lane]


def run_own(count, order, feat, noise, cot, params, acc, grad):
    dim, codes = params[2].shape
    images, strip, width = feat.shape
    share = images // count
    n = 2 if share % 2 == 0 else 1

    def image(lane, shape):
        return pl.BlockSpec(
            (None, *shape), lambda i, order_ref: (own_image(i, lane, n, order_ref, count), 0, 0)
        )

    return pl.pallas_call(
        functools.partial(own_kernel, n, count),
        grid_spec=pltpu.PrefetchScalarGridSpec(
            num_scalar_prefetch=1,
            grid=(share // n,),
            in_specs=[image(lane, (strip, width)) for lane in range(n)]
            + [image(lane, (strip, codes)) for lane in range(n)]
            + [image(lane, (dim, strip)) for lane in range(n)]
            + [fixed(p.shape) for p in params]
            + [fixed(acc.shape), HBM],
            out_specs=[
                pl.BlockSpec(
                    (n, strip, codes),
                    lambda i, _: (i, lax.axis_index("space"), 0),
                ),
                HBM,
                fixed(acc.shape),
            ],
            scratch_shapes=gradient_scratch(n, strip, width)
            + shared_scratch(dim, codes, width)
            + tile_scratch(strip, codes) * n,
        ),
        out_shape=[
            pltpu.HBM((share, strip * count, codes), F32),
            pltpu.HBM(feat.shape, F32),
            jax.ShapeDtypeStruct(acc.shape, F32),
        ],
        input_output_aliases={5 + 3 * n: 2, 6 + 3 * n: 1},
        compiler_params=settings(),
        cost_estimate=cost(share * strip, width, dim, codes, 10),
        name="own_images",
    )(
        order,
        *in_hbm([feat] * n + [noise] * n + [cot] * n + [*params[0:3]]),
        params[3],
        acc,
        *in_hbm([grad]),
    )


def place_kernel(count, runs, *refs):
    parts = refs[0 : len(runs)]
    out_ref, sem = refs[len(runs) + 1 : len(runs) + 3]
    me = lax.axis_index("space")
    copies = []
    for part, (step, first, slots) in zip(parts, runs):
        strip = part.shape[0] // slots
        row = pl.multiple_of(source(me, step, count) * strip, strip)
        for j in range(slots):
            copies.append(
                pltpu.make_async_copy(
                    part.at[pl.ds(j * strip, strip)],
                    out_ref.at[first + j, pl.ds(row, strip)],
                    sem.at[len(copies)],
                )
            )
    for copy in copies:
        copy.start()
    for copy in copies:
        copy.wait()


def place_wide(count, runs, parts, whole):
    return pl.pallas_call(
        functools.partial(place_kernel, count, runs),
        out_shape=pltpu.HBM(whole.shape, F32),
        in_specs=[VMEM] * len(runs) + [HBM],
        out_specs=HBM,
        scratch_shapes=[pltpu.SemaphoreType.DMA((sum(r[2] for r in runs),))],
        input_output_aliases={len(runs): 0},
        compiler_params=settings(VMEM_LIMIT // 2),
        cost_estimate=pl.CostEstimate(
            flops=0, bytes_accessed=2 * sum(p.size * 4 for p in parts), transcendentals=0
        ),
        name="place_wide",
    )(*[pltpu.with_memory_space_constraint(p, pltpu.VMEM) for p in parts], *in_hbm([whole]))


def join_kernel(count, steps, *refs):
    parts = refs[0:count]
    outs = refs[count:]
    me = lax.axis_index("space")
    for part, step in zip(parts, steps):
        here = source(me, step, count)
        base = 0
        for out in outs:
            for j in range(out.shape[0]):
                strip = out.shape[2]
                out[j, here] = part[base : base + strip]
                base += strip


def join_small(count, steps, parts, shapes):
    codes = parts[0].shape[1]
    return pl.pallas_call(
        functools.partial(join_kernel, count, steps),
        out_shape=[
            jax.ShapeDtypeStruct((images // count, count, strip, codes), F32)
            for images, strip, _ in shapes
        ],
        compiler_params=settings(VMEM_LIMIT // 2),
        name="join_small",
    )(*parts)


def tree(values):
    while len(values) > 1:
        values = [
            values[i] + values[i + 1] if i + 1 < len(values) else values[i]
            for i in range(0, len(values), 2)
        ]
    return values[0]


def sum_kernel(*refs):
    refs[-1][...] = tree([ref[...] for ref in refs[:-1]])


def add_all(parts):
    return pl.pallas_call(
        sum_kernel,
        out_shape=jax.ShapeDtypeStruct(parts[0].shape, F32),
        compiler_params=settings(VMEM_LIMIT // 2),
        name="add_parts",
    )(*parts)


def final_kernel(devices, pixels, *refs):
    shards = refs[0:devices]
    weight_ref, bias_ref, book_ref, log_ref, usage_ref = refs[devices : devices + 5]
    weight_out, bias_out, book_out, log_out, usage_out = refs[devices + 5 : devices + 10]
    sum_scr = refs[devices + 10]
    me = lax.rem(lax.axis_index("dp"), devices)
    for i in range(devices):
        sum_scr[shard_at(source(me, i, devices), devices)] = shards[i][...]
    dim, codes = book_ref.shape
    width = weight_ref.shape[1]
    scale = 0.5 * lax.rsqrt(jnp.full((8, 128), pixels, F32))[0:1, 0:1]
    book_out[...] = 0.5 * book_ref[...] + scale * sum_scr[:, 0:codes]
    rest = codes + width
    weight_out[...] = 0.5 * weight_ref[...] + scale * sum_scr[:, codes:rest]
    rows = codes // 128
    bias_out[...] = 0.5 * bias_ref[...] + scale * sum_scr[rows : rows + 1, rest : rest + dim]
    usage = jnp.concatenate(
        [sum_scr[i : i + 1, rest : rest + 128] for i in range(rows)], axis=1
    )
    usage_out[...] = 0.5 * usage_ref[...] + 0.5 * (codes / pixels) * usage
    log_out[...] = 0.5 * log_ref[...] + scale * sum_scr[rows + 1 : rows + 2, rest : rest + 1]


def finish(devices, pixels, shards, weight, bias, book, log, usage):
    outs = (weight.T, bias.reshape(1, -1), book.T, log.reshape(1, 1), usage.reshape(1, -1))
    outs = pl.pallas_call(
        functools.partial(final_kernel, devices, pixels),
        out_shape=[jax.ShapeDtypeStruct(out.shape, F32) for out in outs],
        scratch_shapes=[pltpu.VMEM((64, LANES), F32)],
        compiler_params=settings(VMEM_LIMIT // 2),
        name="new_averages",
    )(*shards, *outs)
    return outs[0].T, outs[1].reshape(-1), outs[2].T, outs[3].reshape(-1), outs[4].reshape(-1)


def exchange(value, bit, size, pairs):
    while bit < size:
        value = value + pairs(value, bit)
        bit = 2 * bit
    return value


def per_device(
    feat_small,
    feat_mid,
    feat_wide,
    noise_small,
    noise_mid,
    noise_wide,
    cot_small,
    cot_mid,
    cot_wide,
    order_small,
    order_mid,
    order_wide,
    weight,
    bias,
    book,
    log,
    heat,
    weight_mean,
    bias_mean,
    book_mean,
    log_mean,
    usage_mean,
):
    count = lax.axis_size("space")
    devices = lax.axis_size("dp")
    params = (weight.T, bias.reshape(1, -1), book.T, log, heat)
    feats = (feat_small, feat_mid, feat_wide)
    pixels = sum(f.shape[0] * f.shape[1] for f in feats) * count * devices
    share = feat_wide.shape[0] // count
    cot_wide = jnp.swapaxes(cot_wide, 1, 2)

    def send(values):
        return [lax.ppermute(v, "space", route(i, count)) for i, v in zip(turns, values)]

    def follow(codes, before):
        before[:], codes[-1] = lax.optimization_barrier((before, codes[-1]))
        return send(codes)

    last = count // 2
    turns = [step for step in range(count - 1, 0, -1) if step != last] + [last]
    orders = (order_small, order_mid, order_wide)
    noises = (noise_small, noise_mid)
    *small, usage, scalar, order_wide = small_forward(
        count, turns, orders, feats[0:2], noises, params
    )
    arrived = [send(small)]
    own_params = params
    params = (*params[0:3], scalar)
    near = min(4, devices)
    early = [(step, 0, 1) for step in turns]
    direct = [(step, 1, share - 1) for step in turns[:-1]]
    late = [(last, 1, share - 1)]
    *early_codes, usage = wide_forward(
        count, split(early, 3), False, order_wide, feat_wide, noise_wide, params, usage, 4
    )
    arrived.append(follow(list(early_codes), arrived[0]))
    *codes, grad, acc = wide_both(
        count, split(direct, 2), order_wide, feat_wide, noise_wide, cot_wide, params
    )
    late_lanes = [Lane([(last, slot, 1)]) for slot in range(1, share)]
    late_codes, usage = wide_forward(
        count, late_lanes, True, order_wide, feat_wide, noise_wide, params, usage, 1
    )
    arrived.append(follow([*codes, late_codes], arrived[1]))
    arrived[1], acc = lax.optimization_barrier((arrived[1], acc))
    whole, grad, acc = run_own(
        count, order_wide, feat_wide, noise_wide, cot_wide, params, acc, grad
    )
    whole = place_wide(count, early, arrived[1], whole)
    acc, own_params = lax.optimization_barrier((acc, own_params))
    own, own_usage, _, _ = small_forward(
        count, range(1), orders, feats[0:2], noises, own_params
    )
    small = [own, *small]
    codes_small, codes_mid = join_small(
        count, [0, *turns], [own] + arrived[0], [f.shape for f in feats[0:2]]
    )
    whole, codes_small, codes_mid, acc = lax.optimization_barrier(
        (whole, codes_small, codes_mid, acc)
    )
    grad, acc = wide_backward(
        count,
        split(early + late, 2),
        [*early_codes, late_codes],
        order_wide,
        feat_wide,
        cot_wide,
        params,
        acc,
        grad,
    )
    grad_small, grad_mid, *shards = small_backward(
        count,
        [0, *turns],
        near,
        orders[0:2],
        feats[0:2],
        (cot_small, cot_mid),
        small,
        params,
        acc,
        (usage, own_usage),
    )
    group = [
        [(i, i - i % near + partner(i % near, step, near)) for i in range(devices)]
        for step in range(near)
    ]
    parts = [lax.ppermute(shards[i], "dp", group[i]) for i in range(1, near)]
    mine = add_all([shards[0]] + parts)

    def along(value, offset):
        return lax.ppermute(value, "dp", [(i, i ^ offset) for i in range(devices)])

    def across(value, offset):
        turn = near if devices > near else 0
        pairs = [
            (i * count + j, (i ^ turn) * count + (j ^ offset))
            for i in range(devices)
            for j in range(count)
        ]
        return lax.ppermute(value, ("dp", "space"), pairs)

    mine = exchange(mine, near, devices, along)
    mine = exchange(mine, 1, count, across)
    shards = [mine] + [lax.ppermute(mine, "dp", group[i]) for i in range(1, near)]
    updated = finish(
        near, pixels, shards, weight_mean, bias_mean, book_mean, log_mean, usage_mean
    )
    for run, part in zip(direct + late, arrived[2]):
        whole = place_wide(count, [run], [part], whole)
    codes = whole.shape[2]
    return (
        codes_small.reshape(codes_small.shape[0], -1, codes),
        codes_mid.reshape(codes_mid.shape[0], -1, codes),
        whole,
        grad_small,
        grad_mid,
        grad,
        *updated,
    )


def solution(mesh):
    strips = P("dp", "space", None)
    placed = (strips,) * 9 + (P("dp", None),) * 3 + (P(),) * 10
    return jax.shard_map(
        per_device,
        mesh=mesh,
        in_specs=placed,
        out_specs=(P(("dp", "space"), None, None),) * 3 + (strips,) * 3 + (P(),) * 5,
        check_vma=False,
    )
```

```python
import functools

import jax
import jax.numpy as jnp
from jax import lax
from jax.experimental import pallas as pl
from jax.experimental.pallas import tpu as pltpu
from jax.sharding import PartitionSpec as P

F32 = jnp.float32
BF16 = jnp.bfloat16
VMEM_LIMIT = 24 * 1024 * 1024
ACC_ROWS = 64 + 64 + 8 + 8 + 64 + 8
LANES = 896


def partner(index, step, count):
    if count & (count - 1) == 0:
        return index ^ step
    return lax.rem(index + step, count)


def route(step, count):
    if count & (count - 1) == 0:
        return [(i, i ^ step) for i in range(count)]
    return [(i, (i + step) % count) for i in range(count)]


def source(index, step, count):
    if count & (count - 1) == 0:
        return index ^ step
    return lax.rem(index + (count - step), count)


def in_hbm(arrays):
    return [pltpu.with_memory_space_constraint(a, pltpu.HBM) for a in arrays]


def halves(x):
    high = x.astype(BF16)
    return high, (x - high.astype(F32)).astype(BF16)


def dot(left, right, left_dim=1, right_dim=0):
    return lax.dot_general(
        left, right, (((left_dim,), (right_dim,)), ((), ())), preferred_element_type=F32
    )


def set_scalars(log_ref, heat_ref, out_ref):
    precision = jnp.exp(jnp.full((8, 128), log_ref[0], F32))
    heat = jnp.full((8, 128), heat_ref[0], F32)
    row = lax.broadcasted_iota(jnp.int32, (8, 128), 0)
    factor = -0.5 * precision / heat
    out_ref[...] = jnp.where(row == 0, precision, jnp.where(row == 1, 1.0 / heat, factor))


def scalars(ref):
    return ref[0:1, 0:1], ref[1:2, 0:1], ref[2:3, 0:1]


def prepare(refs, book_scr, books_scr, weight_scr, backward=True):
    weight_ref, bias_ref, book_ref, scalar_ref = refs
    dim, codes = book_ref.shape
    precision, _, _ = scalars(scalar_ref)
    book = book_ref[...]
    high, low = halves(book)
    norm = -0.5 * precision * jnp.sum(book * book, axis=0, keepdims=True)
    n0 = norm.astype(BF16).astype(F32)
    n1 = (norm - n0).astype(BF16).astype(F32)
    n2 = norm - n0 - n1
    row = lax.broadcasted_iota(jnp.int32, (16, codes), 0)
    extra = jnp.where(
        row < 3,
        1.0,
        jnp.where(row == 3, n0, jnp.where(row == 4, n1, jnp.where(row == 5, n2, 0.0))),
    ).astype(BF16)
    book_scr[0:dim] = high
    book_scr[dim : 2 * dim] = low
    book_scr[2 * dim : 3 * dim] = high
    book_scr[3 * dim : 3 * dim + 16] = extra
    if backward:
        books_scr[0:dim] = high
        books_scr[dim : 2 * dim] = low
        books_scr[2 * dim : 2 * dim + 16] = jnp.ones((16, codes), BF16)
    high, low = halves(weight_ref[...])
    weight_scr[0:dim] = high
    weight_scr[dim : 2 * dim] = low
    weight_scr[2 * dim : 3 * dim] = high


def latents(refs, shared, feat):
    weight_ref, bias_ref, book_ref, scalar_ref = refs
    weight_scr = shared[2]
    dim = book_ref.shape[0]
    precision, _, _ = scalars(scalar_ref)
    eye = lax.broadcasted_iota(jnp.int32, (dim, dim), 0) == lax.broadcasted_iota(
        jnp.int32, (dim, dim), 1
    )
    bias = jnp.sum(jnp.where(eye, bias_ref[...], 0.0), axis=1, keepdims=True)
    fh, fl = halves(feat)
    both = weight_scr[0 : 2 * dim]
    z2 = dot(both, fh, 1, 1) + dot(both, fl, 1, 1)
    z = z2[0:dim] + z2[dim : 2 * dim] + bias
    square = -0.5 * precision * jnp.sum(z * z, axis=0, keepdims=True)
    return fh, fl, z, square


def logit_rows(zh, zl, square):
    rows = zh.shape[1]
    s0 = square.astype(BF16).astype(F32)
    s1 = (square - s0).astype(BF16).astype(F32)
    s2 = square - s0 - s1
    row = lax.broadcasted_iota(jnp.int32, (16, rows), 0)
    extra = jnp.where(
        row == 0,
        s0,
        jnp.where(row == 1, s1, jnp.where(row == 2, s2, jnp.where(row < 6, 1.0, 0.0))),
    ).astype(BF16)
    return jnp.concatenate([zh, zh, zl, extra], axis=0)


def cot_rows(ch, cl):
    return jnp.concatenate([ch, ch, cl, jnp.zeros((16, ch.shape[1]), BF16)], axis=0)


def over_rows(rows, body, carry):
    step = next(s for s in (32, 16, 8) if rows % s == 0)

    def at(i, carry):
        return body(pl.ds(pl.multiple_of(i * step, step), step), carry)

    return lax.fori_loop(0, rows // step, at, carry, unroll=True)


def folded(x):
    return jnp.sum(x.reshape(x.shape[0] // 8, 8, x.shape[1]), axis=0)


def probabilities(logits):
    top = jnp.max(logits, axis=1, keepdims=True)
    e = jnp.exp(logits - top)
    return e * (1.0 / jnp.sum(e, axis=1, keepdims=True))


def forward_products(refs, shared, feat, l_scr):
    precision, _, _ = scalars(refs[3])
    _, _, z, square = latents(refs, shared, feat)
    zh, zl = halves(precision * z)
    l_scr[0 : feat.shape[0]] = dot(logit_rows(zh, zl, square), shared[0][...], 0, 0)


def forward_rows(refs, l_scr, noise_ref, code_ref, usage):
    _, cold, _ = scalars(refs[3])

    def body(at, usage):
        logits = l_scr[at]
        code_ref[at] = probabilities((logits + noise_ref[at]) * cold)
        return usage + folded(probabilities(logits))

    return over_rows(code_ref.shape[0], body, usage)


def products(refs, shared, scr, feat, cot, forward):
    l_scr, g_scr = scr[0:2]
    rows = feat.shape[0]
    precision, _, factor = scalars(refs[3])
    fh, fl, z, square = latents(refs, shared, feat)
    zh, zl = halves(precision * z)
    ch, cl = halves(factor * cot)
    if forward:
        left = jnp.concatenate([logit_rows(zh, zl, square), cot_rows(ch, cl)], axis=1)
        p = dot(left, shared[0][...], 0, 0)
        l_scr[0:rows] = p[0:rows]
        g_scr[0:rows] = p[rows : 2 * rows]
    else:
        g_scr[0:rows] = dot(cot_rows(ch, cl), shared[0][...], 0, 0)
    return fh, fl, z, square, zh, zl, ch, cl


def both_rows(refs, scr, noise_ref, code_ref, usage):
    l_scr, g_scr, wh_scr, wl_scr, gh_scr, gl_scr = scr
    _, cold, _ = scalars(refs[3])

    def body(at, usage):
        logits = l_scr[at]
        s = (logits + noise_ref[at]) * cold
        e = jnp.exp(s - jnp.max(s, axis=1, keepdims=True))
        gw = g_scr[at]
        scale = 1.0 / jnp.sum(e, axis=1, keepdims=True)
        inner = jnp.sum(e * gw, axis=1, keepdims=True) * scale
        w = e * scale
        code_ref[at] = w
        gd = w * (gw - inner)
        wh_scr[at], wl_scr[at] = halves(w)
        gh_scr[at], gl_scr[at] = halves(gd)
        return usage + folded(probabilities(logits))

    return over_rows(code_ref.shape[0], body, usage)


def backward_rows(scr, code_ref):
    _, g_scr, wh_scr, wl_scr, gh_scr, gl_scr = scr

    def body(at, carry):
        w = code_ref[at]
        gw = g_scr[at]
        gd = w * (gw - jnp.sum(w * gw, axis=1, keepdims=True))
        wh_scr[at], wl_scr[at] = halves(w)
        gh_scr[at], gl_scr[at] = halves(gd)
        return carry

    over_rows(code_ref.shape[0], body, 0)


def gradients(refs, shared, scr, state, acc_ref):
    _, books_scr, weight_scr = shared
    wh_scr, wl_scr, gh_scr, gl_scr = scr[2:6]
    fh, fl, z, square, zh, zl, ch, cl = state
    rows, feats = fh.shape
    dim, codes = refs[2].shape
    wh, wl = wh_scr[0:rows], wl_scr[0:rows]
    gh, gl = gh_scr[0:rows], gl_scr[0:rows]
    p = dot(jnp.concatenate([ch, cl], axis=0), wh)
    acc_ref[0:64] += p[0:dim] + p[dim : 2 * dim] + dot(ch, wl)
    left = jnp.concatenate([zh, zl, jnp.ones((16, rows), BF16)], axis=0)
    p = dot(left, gh) + dot(left, gl)
    acc_ref[64:128] += p[0:dim] + p[dim : 2 * dim]
    acc_ref[128:136] += p[2 * dim : 2 * dim + 8]
    p = dot(books_scr[...], gh, 1, 1) + dot(books_scr[...], gl, 1, 1)
    row_d = p[2 * dim : 2 * dim + 1]
    gz = 2.0 * (row_d * z - (p[0:dim] + p[dim : 2 * dim]))
    zh, zl = halves(gz)
    p = dot(jnp.concatenate([zh, zl], axis=0), fh)
    acc_ref[144:208, 0:feats] += p[0:dim] + p[dim : 2 * dim] + dot(zh, fl)
    acc_ref[144:208, feats : feats + 128] += jnp.broadcast_to(
        jnp.sum(gz, axis=1, keepdims=True), (dim, 128)
    )
    total = jnp.sum(square * row_d, axis=1, keepdims=True)
    acc_ref[208:216] += jnp.broadcast_to(total, (8, codes))
    return dot(jnp.concatenate([zh, zh, zl], axis=0), weight_scr[...], 0, 0)


def shared_scratch(dim, codes, feats):
    return [
        pltpu.VMEM((3 * dim + 16, codes), BF16),
        pltpu.VMEM((2 * dim + 16, codes), BF16),
        pltpu.VMEM((3 * dim, feats), BF16),
    ]


def tile_scratch(rows, codes):
    return [pltpu.VMEM((rows, codes), F32)] * 2 + [pltpu.VMEM((rows, codes), BF16)] * 4


def settings(limit=VMEM_LIMIT):
    return pltpu.CompilerParams(vmem_limit_bytes=limit)


def cost(rows, feats, dim, codes, tenths):
    return pl.CostEstimate(
        flops=rows * 24 * tenths * (5 * dim * codes + 3 * dim * feats) // 10,
        bytes_accessed=4 * rows * (2 * feats + 2 * codes + dim),
        transcendentals=2 * rows * codes,
    )


SMEM = pl.BlockSpec(memory_space=pltpu.SMEM)
VMEM = pl.BlockSpec(memory_space=pltpu.VMEM)
HBM = pl.BlockSpec(memory_space=pltpu.HBM)


def fixed(shape):
    return pl.BlockSpec(shape, lambda *_: (0,) * len(shape))


class Lane:
    def __init__(self, runs):
        self.runs = list(runs)
        self.bounds = [0]
        for _, _, slots in self.runs:
            self.bounds.append(self.bounds[-1] + slots)

    def total(self):
        return self.bounds[-1]

    def index(self, i, order_ref, count):
        share = order_ref.shape[1] // count
        step, slot = 0, 0
        for (whose, first, _), start in zip(self.runs, self.bounds):
            here = first + i - start
            step = whose if start == 0 else jnp.where(i >= start, whose, step)
            slot = here if start == 0 else jnp.where(i >= start, here, slot)
        there = partner(lax.axis_index("space"), step, count)
        return order_ref[0, there * share + slot]

    def image(self, shape, count):
        return pl.BlockSpec(
            (None, *shape), lambda i, order_ref: (self.index(i, order_ref, count), 0, 0)
        )

    def blocks(self, shape):
        return [
            pl.BlockSpec(
                shape,
                lambda i, _, start=start, last=slots - 1: (jnp.clip(i - start, 0, last), 0),
            )
            for (_, _, slots), start in zip(self.runs, self.bounds)
        ]

    def each(self, step, body):
        for i, (low, high) in enumerate(zip(self.bounds, self.bounds[1:])):
            pl.when((step >= low) & (step < high))(functools.partial(body, i))


def split(runs, ways):
    whole = Lane(runs)
    lanes, current = [], []
    for run in whole.runs:
        current.append(run)
        if Lane(current).total() * ways == whole.total():
            lanes.append(Lane(current))
            current = []
    return lanes if len(lanes) == ways and not current else [whole]


def take(refs, *sizes):
    groups, at = [], 0
    for size in sizes:
        groups.append(refs[at : at + size])
        at += size
    return groups


def by_lane(refs, lanes):
    return take(refs, *[len(lane.runs) for lane in lanes])


def keep_codes(step, lanes, sends, code_scrs):
    for lane, refs, code_scr in zip(lanes, by_lane(sends, lanes), code_scrs):
        if len(lane.runs) > 1:

            def keep(i, refs=refs, code_scr=code_scr):
                refs[i][...] = code_scr[...]

            lane.each(step, keep)


def code_targets(lanes, sends, code_scrs):
    return [
        refs[0] if len(lane.runs) == 1 else code_scr
        for lane, refs, code_scr in zip(lanes, by_lane(sends, lanes), code_scrs)
    ]


class Gradients:
    def __init__(self, out_ref, scr, sems):
        self.out_ref, self.scr, self.sems = out_ref, scr, sems

    def copy(self, lane, slot, image):
        return pltpu.make_async_copy(
            self.scr.at[lane, slot], self.out_ref.at[image], self.sems.at[lane, slot]
        )

    def ready(self, step, lanes):
        @pl.when(step >= 2)
        def _():
            for lane in range(lanes):
                self.copy(lane, lax.rem(step, 2), 0).wait()

    def store(self, step, values, images):
        slot = lax.rem(step, 2)
        for lane, (value, image) in enumerate(zip(values, images)):
            self.scr[lane, slot] = value
            self.copy(lane, slot, image).start()

    def end(self, step, lanes, steps):
        @pl.when(step == steps - 1)
        def _():
            for lane in range(lanes):
                for slot in range(min(2, steps)):
                    self.copy(lane, slot, 0).wait()


def gradient_scratch(lanes, strip, width):
    return [pltpu.VMEM((lanes, 2, strip, width), F32), pltpu.SemaphoreType.DMA((lanes, 2))]


def places_of(orders, shapes, groups, steps, count):
    me = lax.axis_index("space")
    strips = []
    at = 0
    for k, step in enumerate(steps):
        there = partner(me, step, count)
        row = 0
        for size in range(2):
            strip = shapes[size][1]
            for j in range(groups[size]):
                image = orders[size][0, there * groups[size] + j]
                strips.append((k, row, size, image, at, strip))
                row += strip
                at += strip
    return strips


def small_forward_kernel(count, steps, groups, *refs):
    sources, wide_in, (log_ref, heat_ref), sends, (usage_ref, scalar_ref), wide_out, held, rest = (
        take(refs, 9, 1, 2, len(steps), 2, 1, 9, len(refs))
    )
    (sems, feat_scr), shared, (l_scr, noise_scr) = take(rest, 2, 3, 2)
    copies = [
        pltpu.make_async_copy(there, here, sems.at[i])
        for i, (there, here) in enumerate(zip([*sources, *wide_in], [*held, *wide_out]))
    ]
    for copy in copies:
        copy.start()
    params, orders, feats, noises = (*held[0:3], scalar_ref), held[3:5], held[5:7], held[7:9]
    set_scalars(log_ref, heat_ref, scalar_ref)
    for copy in copies[0:7]:
        copy.wait()
    prepare(params, *shared, backward=False)
    strips = places_of(orders, [f.shape for f in feats], groups, steps, count)
    for _, _, size, image, at, strip in strips:
        feat_scr[at : at + strip] = feats[size][image]
    forward_products(params, shared, feat_scr[...], l_scr)
    for copy in copies[7:9]:
        copy.wait()
    usage = jnp.zeros(usage_ref.shape, F32)
    part = sends[0].shape[0]
    if all(noise.shape[1] % 8 == 0 for noise in noises):
        for k, row, size, image, at, strip in strips:
            rows = pl.ds(at, strip)
            target = sends[k].at[pl.ds(row, strip)]
            usage = forward_rows(params, l_scr.at[rows], noises[size].at[image], target, usage)
    else:
        for _, _, size, image, at, strip in strips:
            noise_scr[at : at + strip] = noises[size][image]
        for k, send in enumerate(sends):
            rows = pl.ds(k * part, part)
            usage = forward_rows(params, l_scr.at[rows], noise_scr.at[rows], send, usage)
    usage_ref[...] = usage
    copies[9].wait()


def small_forward(count, steps, orders, feats, noises, params):
    dim, codes = params[2].shape
    width = feats[0].shape[2]
    groups = tuple(f.shape[0] // count for f in feats)
    part = sum(g * f.shape[1] for g, f in zip(groups, feats))
    rows = part * len(steps)
    arrays = [*params[0:3], *orders[0:2], *feats, *noises]
    return pl.pallas_call(
        functools.partial(small_forward_kernel, count, steps, groups),
        out_shape=[jax.ShapeDtypeStruct((part, codes), F32)] * len(steps)
        + [
            jax.ShapeDtypeStruct((8, codes), F32),
            jax.ShapeDtypeStruct((8, 128), F32),
            jax.ShapeDtypeStruct(orders[2].shape, jnp.int32),
        ],
        in_specs=[HBM] * 10 + [SMEM] * 2,
        out_specs=[VMEM] * (len(steps) + 3),
        scratch_shapes=[
            (pltpu.SMEM if 3 <= i < 5 else pltpu.VMEM)(a.shape, a.dtype)
            for i, a in enumerate(arrays)
        ]
        + [pltpu.SemaphoreType.DMA((10,)), pltpu.VMEM((rows, width), F32)]
        + shared_scratch(dim, codes, width)
        + [pltpu.VMEM((rows, codes), F32)] * 2,
        compiler_params=settings(),
        cost_estimate=cost(rows, width, dim, codes, 4),
        name="small_forward",
    )(*in_hbm([*arrays, orders[2]]), *params[3:5])


def small_backward_kernel(count, steps, devices, groups, *refs):
    orders, feats, cots, parts, params, (acc_in, *usages), grads, shards, rest = take(
        refs, 2, 2, 2, count, 4, 3, 2, devices, len(refs)
    )
    acc_ref, sum_scr, feat_scr, cot_scr, code_scr = rest[0:5]
    scr = rest[5:]
    strips = places_of(orders, [f.shape for f in feats], groups, steps, count)
    for _, _, size, image, at, strip in strips:
        feat_scr[at : at + strip] = feats[size][image]
        cot_scr[at : at + strip] = cots[size][image]
    part = parts[0].shape[0]
    for step in range(count):
        code_scr[step * part : (step + 1) * part] = parts[step][...]
    shared, tile_scr = take(scr, 3, 6)
    prepare(params, *shared)
    acc_ref[...] = acc_in[...]
    state = products(params, shared, tile_scr, feat_scr[...], cot_scr[...].T, False)
    backward_rows(tile_scr, code_scr)
    feat_scr[...] = gradients(params, shared, tile_scr, state, acc_ref)
    acc_ref[136:144] += usages[0][...] + usages[1][...]
    lay_out(params, acc_ref, sum_scr, shards)
    for _, _, size, image, at, strip in strips:
        grads[size][image] = feat_scr[at : at + strip]


def small_backward(count, steps, devices, orders, feats, cots, parts, params, acc, usages):
    dim, codes = params[2].shape
    width = feats[0].shape[2]
    groups = tuple(f.shape[0] // count for f in feats)
    rows = parts[0].shape[0] * count
    return pl.pallas_call(
        functools.partial(small_backward_kernel, count, steps, devices, groups),
        out_shape=[pltpu.HBM(f.shape, F32) for f in feats]
        + [jax.ShapeDtypeStruct((64 // devices, LANES), F32)] * devices,
        in_specs=[SMEM] * 2 + [VMEM] * (11 + count),
        out_specs=[VMEM] * (2 + devices),
        scratch_shapes=[
            pltpu.VMEM(acc.shape, F32),
            pltpu.VMEM((64, LANES), F32),
            pltpu.VMEM((rows, width), F32),
            pltpu.VMEM((rows, dim), F32),
            pltpu.VMEM((rows, codes), F32),
        ]
        + shared_scratch(dim, codes, width)
        + tile_scratch(rows, codes),
        compiler_params=settings(),
        cost_estimate=cost(rows, width, dim, codes, 6),
        name="small_backward",
    )(
        *orders,
        *in_hbm([*feats, *cots]),
        *parts,
        *in_hbm(params[0:3]),
        params[3],
        acc,
        *usages,
    )


def wide_forward_kernel(lanes, joined, *refs):
    n = len(lanes)
    arrays = 1 if joined else sum(len(lane.runs) for lane in lanes)
    _, feats, noises, params, usage_in, sends, rest = take(
        refs, 1, n, n, 4, 1, arrays, len(refs)
    )
    (usage_ref,), code_scrs, shared, l_scrs = take(rest, 1, n, 3, n)
    step = pl.program_id(0)

    @pl.when(step == 0)
    def _():
        prepare(params, *shared, backward=False)
        usage_ref[...] = usage_in[0][...]

    if joined:
        strip = code_scrs[0].shape[0]
        targets = [sends[0].at[pl.ds(i * strip, strip)] for i in range(n)]
    else:
        targets = code_targets(lanes, sends, code_scrs)
    for feat_ref, l_scr in zip(feats, l_scrs):
        forward_products(params, shared, feat_ref[...], l_scr)
    usage = usage_ref[...]
    for l_scr, noise_ref, target in zip(l_scrs, noises, targets):
        usage = forward_rows(params, l_scr, noise_ref, target, usage)
    usage_ref[...] = usage
    if not joined:
        keep_codes(step, lanes, sends, code_scrs)


def wide_forward(count, lanes, joined, order, feat, noise, params, usage, tenths):
    dim, codes = params[2].shape
    images, strip, width = feat.shape
    n, steps = len(lanes), lanes[0].total()
    if joined:
        blocks = [fixed((n * strip, codes))]
        sizes = [n]
    else:
        blocks = [block for lane in lanes for block in lane.blocks((strip, codes))]
        sizes = [run[2] for lane in lanes for run in lane.runs]
    return pl.pallas_call(
        functools.partial(wide_forward_kernel, lanes, joined),
        grid_spec=pltpu.PrefetchScalarGridSpec(
            num_scalar_prefetch=1,
            grid=(steps,),
            in_specs=[lane.image((strip, width), count) for lane in lanes]
            + [lane.image((strip, codes), count) for lane in lanes]
            + [fixed(p.shape) for p in params]
            + [fixed(usage.shape)],
            out_specs=blocks + [fixed(usage.shape)],
            scratch_shapes=[pltpu.VMEM((strip, codes), F32)] * n
            + shared_scratch(dim, codes, width)
            + [pltpu.VMEM((strip, codes), F32)] * n,
        ),
        out_shape=[jax.ShapeDtypeStruct((strip * slots, codes), F32) for slots in sizes]
        + [jax.ShapeDtypeStruct(usage.shape, F32)],
        input_output_aliases={5 + 2 * n: len(sizes)},
        compiler_params=settings(),
        cost_estimate=cost(n * steps * strip, width, dim, codes, tenths),
        name="wide_forward",
    )(order, *in_hbm([feat] * n + [noise] * n + [*params[0:3]]), params[3], usage)


def wide_both_kernel(lanes, count, *refs):
    n = len(lanes)
    arrays = sum(len(lane.runs) for lane in lanes)
    order, feats, noises, cots, params, sends, rest = take(
        refs, 1, n, n, n, 4, arrays, len(refs)
    )
    (grad_out, acc_ref), code_scrs, (grad_scr, sems), shared, rest = take(
        rest, 2, n, 2, 3, 6 * n
    )
    scrs = take(rest, *[6] * n)
    grads = Gradients(grad_out, grad_scr, sems)
    step, steps = pl.program_id(0), lanes[0].total()

    @pl.when(step == 0)
    def _():
        prepare(params, *shared)
        acc_ref[...] = jnp.zeros(acc_ref.shape, F32)

    grads.ready(step, n)
    targets = code_targets(lanes, sends, code_scrs)
    states = [
        products(params, shared, scr, feat_ref[...], cot_ref[...], True)
        for scr, feat_ref, cot_ref in zip(scrs, feats, cots)
    ]
    usage = acc_ref[136:144]
    for scr, noise_ref, target in zip(scrs, noises, targets):
        usage = both_rows(params, scr, noise_ref, target, usage)
    acc_ref[136:144] = usage
    values = [
        gradients(params, shared, scr, state, acc_ref) for scr, state in zip(scrs, states)
    ]
    grads.store(step, values, [lane.index(step, order[0], count) for lane in lanes])
    keep_codes(step, lanes, sends, code_scrs)
    grads.end(step, n, steps)


def wide_both(count, lanes, order, feat, noise, cot, params):
    dim, codes = params[2].shape
    images, strip, width = feat.shape
    n, steps = len(lanes), lanes[0].total()
    acc_shape = (ACC_ROWS, codes)
    sizes = [run[2] for lane in lanes for run in lane.runs]
    return pl.pallas_call(
        functools.partial(wide_both_kernel, lanes, count),
        grid_spec=pltpu.PrefetchScalarGridSpec(
            num_scalar_prefetch=1,
            grid=(steps,),
            in_specs=[lane.image((strip, width), count) for lane in lanes]
            + [lane.image((strip, codes), count) for lane in lanes]
            + [lane.image((dim, strip), count) for lane in lanes]
            + [fixed(p.shape) for p in params],
            out_specs=[block for lane in lanes for block in lane.blocks((strip, codes))]
            + [HBM, fixed(acc_shape)],
            scratch_shapes=[pltpu.VMEM((strip, codes), F32)] * n
            + gradient_scratch(n, strip, width)
            + shared_scratch(dim, codes, width)
            + tile_scratch(strip, codes) * n,
        ),
        out_shape=[jax.ShapeDtypeStruct((strip * slots, codes), F32) for slots in sizes]
        + [pltpu.HBM(feat.shape, F32), jax.ShapeDtypeStruct(acc_shape, F32)],
        compiler_params=settings(),
        cost_estimate=cost(n * steps * strip, width, dim, codes, 10),
        name="wide_both",
    )(order, *in_hbm([feat] * n + [noise] * n + [cot] * n + [*params[0:3]]), params[3])


def wide_backward_kernel(lanes, count, *refs):
    n = len(lanes)
    arrays = sum(len(lane.runs) for lane in lanes)
    order, feats, cots, parts, params, (acc_in, _), rest = take(
        refs, 1, n, n, arrays, 4, 2, len(refs)
    )
    (grad_out, acc_ref), code_scrs, (grad_scr, sems), shared, rest = take(
        rest, 2, n, 2, 3, 6 * n
    )
    scrs = take(rest, *[6] * n)
    grads = Gradients(grad_out, grad_scr, sems)
    step, steps = pl.program_id(0), lanes[0].total()

    @pl.when(step == 0)
    def _():
        prepare(params, *shared)
        acc_ref[...] = acc_in[...]

    grads.ready(step, n)
    for lane, refs_of, code_scr in zip(lanes, by_lane(parts, lanes), code_scrs):
        if len(lane.runs) > 1:

            def fetch(i, refs_of=refs_of, code_scr=code_scr):
                code_scr[...] = refs_of[i][...]

            lane.each(step, fetch)
    states = [
        products(params, shared, scr, feat_ref[...], cot_ref[...], False)
        for scr, feat_ref, cot_ref in zip(scrs, feats, cots)
    ]
    for scr, code_ref in zip(scrs, code_targets(lanes, parts, code_scrs)):
        backward_rows(scr, code_ref)
    values = [
        gradients(params, shared, scr, state, acc_ref) for scr, state in zip(scrs, states)
    ]
    grads.store(step, values, [lane.index(step, order[0], count) for lane in lanes])
    grads.end(step, n, steps)


def wide_backward(count, lanes, parts, order, feat, cot, params, acc, grad):
    dim, codes = params[2].shape
    images, strip, width = feat.shape
    n, steps = len(lanes), lanes[0].total()
    return pl.pallas_call(
        functools.partial(wide_backward_kernel, lanes, count),
        grid_spec=pltpu.PrefetchScalarGridSpec(
            num_scalar_prefetch=1,
            grid=(steps,),
            in_specs=[lane.image((strip, width), count) for lane in lanes]
            + [lane.image((dim, strip), count) for lane in lanes]
            + [block for lane in lanes for block in lane.blocks((strip, codes))]
            + [fixed(p.shape) for p in params]
            + [fixed(acc.shape), HBM],
            out_specs=[HBM, fixed(acc.shape)],
            scratch_shapes=[pltpu.VMEM((strip, codes), F32)] * n
            + gradient_scratch(n, strip, width)
            + shared_scratch(dim, codes, width)
            + tile_scratch(strip, codes) * n,
        ),
        out_shape=[pltpu.HBM(feat.shape, F32), jax.ShapeDtypeStruct(acc.shape, F32)],
        input_output_aliases={5 + 2 * n + len(parts): 1, 6 + 2 * n + len(parts): 0},
        compiler_params=settings(),
        cost_estimate=cost(n * steps * strip, width, dim, codes, 6),
        name="wide_backward",
    )(
        order,
        *in_hbm([feat] * n + [cot] * n),
        *parts,
        *in_hbm(params[0:3]),
        params[3],
        acc,
        *in_hbm([grad]),
    )


def shard_at(index, parts):
    height = 64 // parts
    return pl.ds(pl.multiple_of(index * height, height), height)


def lay_out(params, acc_ref, sum_scr, shards):
    weight_ref, bias_ref, book_ref, scalar_ref = params
    codes = book_ref.shape[1]
    width = weight_ref.shape[1]
    devices = len(shards)
    me = lax.rem(lax.axis_index("dp"), devices)
    precision, _, factor = scalars(scalar_ref)
    book = book_ref[...]
    column = acc_ref[128:129]
    moment = acc_ref[64:128] * (1.0 / precision)
    book_sum = acc_ref[0:64] * (1.0 / factor) + 2.0 * (column * book - moment)
    slope = jnp.sum(
        jnp.sum(book * book, axis=0, keepdims=True) * column, axis=1, keepdims=True
    ) - 2.0 * jnp.sum(jnp.sum(book * moment, axis=0, keepdims=True), axis=1, keepdims=True)
    slope = slope + acc_ref[208:209, 0:1] / (-0.5 * precision)
    usage = jnp.sum(acc_ref[136:144], axis=0, keepdims=True)
    dim = book_ref.shape[0]
    eye = lax.broadcasted_iota(jnp.int32, (dim, dim), 0) == lax.broadcasted_iota(
        jnp.int32, (dim, dim), 1
    )
    bias = acc_ref[144:208, width : width + dim]
    bias = jnp.sum(jnp.where(eye, bias, 0.0), axis=0, keepdims=True)
    rest = codes + width
    sum_scr[:, 0:codes] = book_sum
    sum_scr[:, codes:rest] = acc_ref[144:208, 0:width]
    sum_scr[:, rest : rest + 128] = jnp.broadcast_to(slope, (64, 128))
    rows = codes // 128
    for i in range(rows):
        sum_scr[i : i + 1, rest : rest + 128] = usage[:, i * 128 : (i + 1) * 128]
    sum_scr[rows : rows + 1, rest : rest + dim] = bias
    for i in range(devices):
        shards[i][...] = sum_scr[shard_at(partner(me, i, devices), devices)]


def own_kernel(n, count, *refs):
    order, feats, noises, cots, params, (acc_in, _), rest = take(
        refs, 1, n, n, n, 4, 2, len(refs)
    )
    (code_ref, grad_out, acc_ref), (grad_scr, sems), shared, rest = take(rest, 3, 2, 3, 6 * n)
    scrs = take(rest, *[6] * n)
    grads = Gradients(grad_out, grad_scr, sems)
    step = pl.program_id(0)

    @pl.when(step == 0)
    def _():
        prepare(params, *shared)
        acc_ref[...] = acc_in[...]

    grads.ready(step, n)
    states = [
        products(params, shared, scr, feat_ref[...], cot_ref[...], True)
        for scr, feat_ref, cot_ref in zip(scrs, feats, cots)
    ]
    usage = acc_ref[136:144]
    for i, (scr, noise_ref) in enumerate(zip(scrs, noises)):
        usage = both_rows(params, scr, noise_ref, code_ref.at[i], usage)
    acc_ref[136:144] = usage
    values = [
        gradients(params, shared, scr, state, acc_ref) for scr, state in zip(scrs, states)
    ]
    grads.store(step, values, [own_image(step, i, n, order[0], count) for i in range(n)])
    grads.end(step, n, pl.num_programs(0))


def own_image(step, lane, n, order_ref, count):
    share = order_ref.shape[1] // count
    return order_ref[0, lax.axis_index("space") * share + step * n + lane]


def run_own(count, order, feat, noise, cot, params, acc, grad):
    dim, codes = params[2].shape
    images, strip, width = feat.shape
    share = images // count
    n = 2 if share % 2 == 0 else 1

    def image(lane, shape):
        return pl.BlockSpec(
            (None, *shape), lambda i, order_ref: (own_image(i, lane, n, order_ref, count), 0, 0)
        )

    return pl.pallas_call(
        functools.partial(own_kernel, n, count),
        grid_spec=pltpu.PrefetchScalarGridSpec(
            num_scalar_prefetch=1,
            grid=(share // n,),
            in_specs=[image(lane, (strip, width)) for lane in range(n)]
            + [image(lane, (strip, codes)) for lane in range(n)]
            + [image(lane, (dim, strip)) for lane in range(n)]
            + [fixed(p.shape) for p in params]
            + [fixed(acc.shape), HBM],
            out_specs=[
                pl.BlockSpec(
                    (n, strip, codes),
                    lambda i, _: (i, lax.axis_index("space"), 0),
                ),
                HBM,
                fixed(acc.shape),
            ],
            scratch_shapes=gradient_scratch(n, strip, width)
            + shared_scratch(dim, codes, width)
            + tile_scratch(strip, codes) * n,
        ),
        out_shape=[
            pltpu.HBM((share, strip * count, codes), F32),
            pltpu.HBM(feat.shape, F32),
            jax.ShapeDtypeStruct(acc.shape, F32),
        ],
        input_output_aliases={5 + 3 * n: 2, 6 + 3 * n: 1},
        compiler_params=settings(),
        cost_estimate=cost(share * strip, width, dim, codes, 10),
        name="own_images",
    )(
        order,
        *in_hbm([feat] * n + [noise] * n + [cot] * n + [*params[0:3]]),
        params[3],
        acc,
        *in_hbm([grad]),
    )


def place_kernel(count, runs, *refs):
    parts = refs[0 : len(runs)]
    out_ref, sem = refs[len(runs) + 1 : len(runs) + 3]
    me = lax.axis_index("space")
    copies = []
    for part, (step, first, slots) in zip(parts, runs):
        strip = part.shape[0] // slots
        row = pl.multiple_of(source(me, step, count) * strip, strip)
        for j in range(slots):
            copies.append(
                pltpu.make_async_copy(
                    part.at[pl.ds(j * strip, strip)],
                    out_ref.at[first + j, pl.ds(row, strip)],
                    sem.at[len(copies)],
                )
            )
    for copy in copies:
        copy.start()
    for copy in copies:
        copy.wait()


def place_wide(count, runs, parts, whole):
    return pl.pallas_call(
        functools.partial(place_kernel, count, runs),
        out_shape=pltpu.HBM(whole.shape, F32),
        in_specs=[VMEM] * len(runs) + [HBM],
        out_specs=HBM,
        scratch_shapes=[pltpu.SemaphoreType.DMA((sum(r[2] for r in runs),))],
        input_output_aliases={len(runs): 0},
        compiler_params=settings(VMEM_LIMIT // 2),
        cost_estimate=pl.CostEstimate(
            flops=0, bytes_accessed=2 * sum(p.size * 4 for p in parts), transcendentals=0
        ),
        name="place_wide",
    )(*[pltpu.with_memory_space_constraint(p, pltpu.VMEM) for p in parts], *in_hbm([whole]))


def join_kernel(count, steps, *refs):
    parts = refs[0:count]
    outs = refs[count:]
    me = lax.axis_index("space")
    for part, step in zip(parts, steps):
        here = source(me, step, count)
        base = 0
        for out in outs:
            for j in range(out.shape[0]):
                strip = out.shape[2]
                out[j, here] = part[base : base + strip]
                base += strip


def join_small(count, steps, parts, shapes):
    codes = parts[0].shape[1]
    return pl.pallas_call(
        functools.partial(join_kernel, count, steps),
        out_shape=[
            jax.ShapeDtypeStruct((images // count, count, strip, codes), F32)
            for images, strip, _ in shapes
        ],
        compiler_params=settings(VMEM_LIMIT // 2),
        name="join_small",
    )(*parts)


def tree(values):
    while len(values) > 1:
        values = [
            values[i] + values[i + 1] if i + 1 < len(values) else values[i]
            for i in range(0, len(values), 2)
        ]
    return values[0]


def sum_kernel(*refs):
    refs[-1][...] = tree([ref[...] for ref in refs[:-1]])


def add_all(parts):
    return pl.pallas_call(
        sum_kernel,
        out_shape=jax.ShapeDtypeStruct(parts[0].shape, F32),
        compiler_params=settings(VMEM_LIMIT // 2),
        name="add_parts",
    )(*parts)


def final_kernel(devices, pixels, *refs):
    shards = refs[0:devices]
    weight_ref, bias_ref, book_ref, log_ref, usage_ref = refs[devices : devices + 5]
    weight_out, bias_out, book_out, log_out, usage_out = refs[devices + 5 : devices + 10]
    sum_scr = refs[devices + 10]
    me = lax.rem(lax.axis_index("dp"), devices)
    for i in range(devices):
        sum_scr[shard_at(source(me, i, devices), devices)] = shards[i][...]
    dim, codes = book_ref.shape
    width = weight_ref.shape[1]
    scale = 0.5 * lax.rsqrt(jnp.full((8, 128), pixels, F32))[0:1, 0:1]
    book_out[...] = 0.5 * book_ref[...] + scale * sum_scr[:, 0:codes]
    rest = codes + width
    weight_out[...] = 0.5 * weight_ref[...] + scale * sum_scr[:, codes:rest]
    rows = codes // 128
    bias_out[...] = 0.5 * bias_ref[...] + scale * sum_scr[rows : rows + 1, rest : rest + dim]
    usage = jnp.concatenate(
        [sum_scr[i : i + 1, rest : rest + 128] for i in range(rows)], axis=1
    )
    usage_out[...] = 0.5 * usage_ref[...] + 0.5 * (codes / pixels) * usage
    log_out[...] = 0.5 * log_ref[...] + scale * sum_scr[rows + 1 : rows + 2, rest : rest + 1]


def finish(devices, pixels, shards, weight, bias, book, log, usage):
    outs = (weight.T, bias.reshape(1, -1), book.T, log.reshape(1, 1), usage.reshape(1, -1))
    outs = pl.pallas_call(
        functools.partial(final_kernel, devices, pixels),
        out_shape=[jax.ShapeDtypeStruct(out.shape, F32) for out in outs],
        scratch_shapes=[pltpu.VMEM((64, LANES), F32)],
        compiler_params=settings(VMEM_LIMIT // 2),
        name="new_averages",
    )(*shards, *outs)
    return outs[0].T, outs[1].reshape(-1), outs[2].T, outs[3].reshape(-1), outs[4].reshape(-1)


def exchange(value, bit, size, pairs):
    while bit < size:
        value = value + pairs(value, bit)
        bit = 2 * bit
    return value


def per_device(
    feat_small,
    feat_mid,
    feat_wide,
    noise_small,
    noise_mid,
    noise_wide,
    cot_small,
    cot_mid,
    cot_wide,
    order_small,
    order_mid,
    order_wide,
    weight,
    bias,
    book,
    log,
    heat,
    weight_mean,
    bias_mean,
    book_mean,
    log_mean,
    usage_mean,
):
    count = lax.axis_size("space")
    devices = lax.axis_size("dp")
    params = (weight.T, bias.reshape(1, -1), book.T, log, heat)
    feats = (feat_small, feat_mid, feat_wide)
    pixels = sum(f.shape[0] * f.shape[1] for f in feats) * count * devices
    share = feat_wide.shape[0] // count
    cot_wide = jnp.swapaxes(cot_wide, 1, 2)

    def send(values):
        return [lax.ppermute(v, "space", route(i, count)) for i, v in zip(turns, values)]

    def follow(codes, before, parts):
        before[:parts], codes[-1] = lax.optimization_barrier((before[:parts], codes[-1]))
        return send(codes)

    last = count - 1
    turns = list(range(1, count))
    orders = (order_small, order_mid, order_wide)
    noises = (noise_small, noise_mid)
    *small, usage, scalar, order_wide = small_forward(
        count, turns, orders, feats[0:2], noises, params
    )
    arrived = [send(small)]
    own_params = params
    params = (*params[0:3], scalar)
    near = min(4, devices)
    early = [(step, 0, 1) for step in turns]
    direct = [(step, 1, share - 1) for step in turns[:-1]]
    late = [(last, 1, share - 1)]
    *early_codes, usage = wide_forward(
        count, split(early, 3), False, order_wide, feat_wide, noise_wide, params, usage, 4
    )
    arrived.append(follow(list(early_codes), arrived[0], count - 1))
    *codes, grad, acc = wide_both(
        count, split(direct, 2), order_wide, feat_wide, noise_wide, cot_wide, params
    )
    late_lanes = [Lane([(last, slot, 1)]) for slot in range(1, share)]
    late_codes, usage = wide_forward(
        count, late_lanes, True, order_wide, feat_wide, noise_wide, params, usage, 1
    )
    arrived.append(follow([*codes, late_codes], arrived[1], 1))
    arrived[1], acc = lax.optimization_barrier((arrived[1], acc))
    whole, grad, acc = run_own(
        count, order_wide, feat_wide, noise_wide, cot_wide, params, acc, grad
    )
    whole = place_wide(count, early, arrived[1], whole)
    acc, own_params = lax.optimization_barrier((acc, own_params))
    own, own_usage, _, _ = small_forward(
        count, range(1), orders, feats[0:2], noises, own_params
    )
    small = [own, *small]
    codes_small, codes_mid = join_small(
        count, [0, *turns], [own] + arrived[0], [f.shape for f in feats[0:2]]
    )
    whole, codes_small, codes_mid, acc = lax.optimization_barrier(
        (whole, codes_small, codes_mid, acc)
    )
    grad, acc = wide_backward(
        count,
        split(early + late, 2),
        [*early_codes, late_codes],
        order_wide,
        feat_wide,
        cot_wide,
        params,
        acc,
        grad,
    )
    grad_small, grad_mid, *shards = small_backward(
        count,
        [0, *turns],
        near,
        orders[0:2],
        feats[0:2],
        (cot_small, cot_mid),
        small,
        params,
        acc,
        (usage, own_usage),
    )
    group = [
        [(i, i - i % near + partner(i % near, step, near)) for i in range(devices)]
        for step in range(near)
    ]
    parts = [lax.ppermute(shards[i], "dp", group[i]) for i in range(1, near)]
    mine = add_all([shards[0]] + parts)

    def along(value, offset):
        return lax.ppermute(value, "dp", [(i, i ^ offset) for i in range(devices)])

    def across(value, offset):
        turn = near if devices > near else 0
        pairs = [
            (i * count + j, (i ^ turn) * count + (j ^ offset))
            for i in range(devices)
            for j in range(count)
        ]
        return lax.ppermute(value, ("dp", "space"), pairs)

    mine = exchange(mine, near, devices, along)
    mine = exchange(mine, 1, count, across)
    shards = [mine] + [lax.ppermute(mine, "dp", group[i]) for i in range(1, near)]
    updated = finish(
        near, pixels, shards, weight_mean, bias_mean, book_mean, log_mean, usage_mean
    )
    for run, part in zip(direct + late, arrived[2]):
        whole = place_wide(count, [run], [part], whole)
    codes = whole.shape[2]
    return (
        codes_small.reshape(codes_small.shape[0], -1, codes),
        codes_mid.reshape(codes_mid.shape[0], -1, codes),
        whole,
        grad_small,
        grad_mid,
        grad,
        *updated,
    )


def solution(mesh):
    strips = P("dp", "space", None)
    placed = (strips,) * 9 + (P("dp", None),) * 3 + (P(),) * 10
    return jax.shard_map(
        per_device,
        mesh=mesh,
        in_specs=placed,
        out_specs=(P(("dp", "space"), None, None),) * 3 + (strips,) * 3 + (P(),) * 5,
        check_vma=False,
    )
```

```python
import functools

import jax
import jax.numpy as jnp
from jax import lax
from jax.experimental import pallas as pl
from jax.experimental.pallas import tpu as pltpu
from jax.sharding import PartitionSpec as P

F32 = jnp.float32
BF16 = jnp.bfloat16
VMEM_LIMIT = 24 * 1024 * 1024
ACC_ROWS = 64 + 64 + 8 + 8 + 64 + 8
LANES = 896


def partner(index, step, count):
    if count & (count - 1) == 0:
        return index ^ step
    return lax.rem(index + step, count)


def route(step, count):
    if count & (count - 1) == 0:
        return [(i, i ^ step) for i in range(count)]
    return [(i, (i + step) % count) for i in range(count)]


def source(index, step, count):
    if count & (count - 1) == 0:
        return index ^ step
    return lax.rem(index + (count - step), count)


def in_hbm(arrays):
    return [pltpu.with_memory_space_constraint(a, pltpu.HBM) for a in arrays]


def halves(x):
    high = x.astype(BF16)
    return high, (x - high.astype(F32)).astype(BF16)


def dot(left, right, left_dim=1, right_dim=0):
    return lax.dot_general(
        left, right, (((left_dim,), (right_dim,)), ((), ())), preferred_element_type=F32
    )


def set_scalars(log_ref, heat_ref, out_ref):
    precision = jnp.exp(jnp.full((8, 128), log_ref[0], F32))
    heat = jnp.full((8, 128), heat_ref[0], F32)
    row = lax.broadcasted_iota(jnp.int32, (8, 128), 0)
    factor = -0.5 * precision / heat
    out_ref[...] = jnp.where(row == 0, precision, jnp.where(row == 1, 1.0 / heat, factor))


def scalars(ref):
    return ref[0:1, 0:1], ref[1:2, 0:1], ref[2:3, 0:1]


def prepare(refs, book_scr, books_scr, weight_scr, backward=True):
    weight_ref, bias_ref, book_ref, scalar_ref = refs
    dim, codes = book_ref.shape
    precision, _, _ = scalars(scalar_ref)
    book = book_ref[...]
    high, low = halves(book)
    norm = -0.5 * precision * jnp.sum(book * book, axis=0, keepdims=True)
    n0 = norm.astype(BF16).astype(F32)
    n1 = (norm - n0).astype(BF16).astype(F32)
    n2 = norm - n0 - n1
    row = lax.broadcasted_iota(jnp.int32, (16, codes), 0)
    extra = jnp.where(
        row < 3,
        1.0,
        jnp.where(row == 3, n0, jnp.where(row == 4, n1, jnp.where(row == 5, n2, 0.0))),
    ).astype(BF16)
    book_scr[0:dim] = high
    book_scr[dim : 2 * dim] = low
    book_scr[2 * dim : 3 * dim] = high
    book_scr[3 * dim : 3 * dim + 16] = extra
    if backward:
        books_scr[0:dim] = high
        books_scr[dim : 2 * dim] = low
        books_scr[2 * dim : 2 * dim + 16] = jnp.ones((16, codes), BF16)
    high, low = halves(weight_ref[...])
    weight_scr[0:dim] = high
    weight_scr[dim : 2 * dim] = low
    weight_scr[2 * dim : 3 * dim] = high


def latents(refs, shared, feat):
    weight_ref, bias_ref, book_ref, scalar_ref = refs
    weight_scr = shared[2]
    dim = book_ref.shape[0]
    precision, _, _ = scalars(scalar_ref)
    eye = lax.broadcasted_iota(jnp.int32, (dim, dim), 0) == lax.broadcasted_iota(
        jnp.int32, (dim, dim), 1
    )
    bias = jnp.sum(jnp.where(eye, bias_ref[...], 0.0), axis=1, keepdims=True)
    fh, fl = halves(feat)
    both = weight_scr[0 : 2 * dim]
    z2 = dot(both, fh, 1, 1) + dot(both, fl, 1, 1)
    z = z2[0:dim] + z2[dim : 2 * dim] + bias
    square = -0.5 * precision * jnp.sum(z * z, axis=0, keepdims=True)
    return fh, fl, z, square


def logit_rows(zh, zl, square):
    rows = zh.shape[1]
    s0 = square.astype(BF16).astype(F32)
    s1 = (square - s0).astype(BF16).astype(F32)
    s2 = square - s0 - s1
    row = lax.broadcasted_iota(jnp.int32, (16, rows), 0)
    extra = jnp.where(
        row == 0,
        s0,
        jnp.where(row == 1, s1, jnp.where(row == 2, s2, jnp.where(row < 6, 1.0, 0.0))),
    ).astype(BF16)
    return jnp.concatenate([zh, zh, zl, extra], axis=0)


def cot_rows(ch, cl):
    return jnp.concatenate([ch, ch, cl, jnp.zeros((16, ch.shape[1]), BF16)], axis=0)


def over_rows(rows, body, carry):
    step = next(s for s in (32, 16, 8) if rows % s == 0)

    def at(i, carry):
        return body(pl.ds(pl.multiple_of(i * step, step), step), carry)

    return lax.fori_loop(0, rows // step, at, carry, unroll=True)


def folded(x):
    return jnp.sum(x.reshape(x.shape[0] // 8, 8, x.shape[1]), axis=0)


def probabilities(logits):
    top = jnp.max(logits, axis=1, keepdims=True)
    e = jnp.exp(logits - top)
    return e * (1.0 / jnp.sum(e, axis=1, keepdims=True))


def forward_products(refs, shared, feat, l_scr):
    precision, _, _ = scalars(refs[3])
    _, _, z, square = latents(refs, shared, feat)
    zh, zl = halves(precision * z)
    l_scr[0 : feat.shape[0]] = dot(logit_rows(zh, zl, square), shared[0][...], 0, 0)


def forward_rows(refs, l_scr, noise_ref, code_ref, usage):
    _, cold, _ = scalars(refs[3])

    def body(at, usage):
        logits = l_scr[at]
        code_ref[at] = probabilities((logits + noise_ref[at]) * cold)
        return usage + folded(probabilities(logits))

    return over_rows(code_ref.shape[0], body, usage)


def products(refs, shared, scr, feat, cot, forward):
    l_scr, g_scr = scr[0:2]
    rows = feat.shape[0]
    precision, _, factor = scalars(refs[3])
    fh, fl, z, square = latents(refs, shared, feat)
    zh, zl = halves(precision * z)
    ch, cl = halves(factor * cot)
    if forward:
        left = jnp.concatenate([logit_rows(zh, zl, square), cot_rows(ch, cl)], axis=1)
        p = dot(left, shared[0][...], 0, 0)
        l_scr[0:rows] = p[0:rows]
        g_scr[0:rows] = p[rows : 2 * rows]
    else:
        g_scr[0:rows] = dot(cot_rows(ch, cl), shared[0][...], 0, 0)
    return fh, fl, z, square, zh, zl, ch, cl


def both_rows(refs, scr, noise_ref, code_ref, usage):
    l_scr, g_scr, wh_scr, wl_scr, gh_scr, gl_scr = scr
    _, cold, _ = scalars(refs[3])

    def body(at, usage):
        logits = l_scr[at]
        s = (logits + noise_ref[at]) * cold
        e = jnp.exp(s - jnp.max(s, axis=1, keepdims=True))
        gw = g_scr[at]
        scale = 1.0 / jnp.sum(e, axis=1, keepdims=True)
        inner = jnp.sum(e * gw, axis=1, keepdims=True) * scale
        w = e * scale
        code_ref[at] = w
        gd = w * (gw - inner)
        wh_scr[at], wl_scr[at] = halves(w)
        gh_scr[at], gl_scr[at] = halves(gd)
        return usage + folded(probabilities(logits))

    return over_rows(code_ref.shape[0], body, usage)


def backward_rows(scr, code_ref):
    _, g_scr, wh_scr, wl_scr, gh_scr, gl_scr = scr

    def body(at, carry):
        w = code_ref[at]
        gw = g_scr[at]
        gd = w * (gw - jnp.sum(w * gw, axis=1, keepdims=True))
        wh_scr[at], wl_scr[at] = halves(w)
        gh_scr[at], gl_scr[at] = halves(gd)
        return carry

    over_rows(code_ref.shape[0], body, 0)


def gradients(refs, shared, scr, state, acc_ref):
    _, books_scr, weight_scr = shared
    wh_scr, wl_scr, gh_scr, gl_scr = scr[2:6]
    fh, fl, z, square, zh, zl, ch, cl = state
    rows, feats = fh.shape
    dim, codes = refs[2].shape
    wh, wl = wh_scr[0:rows], wl_scr[0:rows]
    gh, gl = gh_scr[0:rows], gl_scr[0:rows]
    p = dot(jnp.concatenate([ch, cl], axis=0), wh)
    acc_ref[0:64] += p[0:dim] + p[dim : 2 * dim] + dot(ch, wl)
    left = jnp.concatenate([zh, zl, jnp.ones((16, rows), BF16)], axis=0)
    p = dot(left, gh) + dot(left, gl)
    acc_ref[64:128] += p[0:dim] + p[dim : 2 * dim]
    acc_ref[128:136] += p[2 * dim : 2 * dim + 8]
    p = dot(books_scr[...], gh, 1, 1) + dot(books_scr[...], gl, 1, 1)
    row_d = p[2 * dim : 2 * dim + 1]
    gz = 2.0 * (row_d * z - (p[0:dim] + p[dim : 2 * dim]))
    zh, zl = halves(gz)
    p = dot(jnp.concatenate([zh, zl], axis=0), fh)
    acc_ref[144:208, 0:feats] += p[0:dim] + p[dim : 2 * dim] + dot(zh, fl)
    acc_ref[144:208, feats : feats + 128] += jnp.broadcast_to(
        jnp.sum(gz, axis=1, keepdims=True), (dim, 128)
    )
    total = jnp.sum(square * row_d, axis=1, keepdims=True)
    acc_ref[208:216] += jnp.broadcast_to(total, (8, codes))
    return dot(jnp.concatenate([zh, zh, zl], axis=0), weight_scr[...], 0, 0)


def shared_scratch(dim, codes, feats):
    return [
        pltpu.VMEM((3 * dim + 16, codes), BF16),
        pltpu.VMEM((2 * dim + 16, codes), BF16),
        pltpu.VMEM((3 * dim, feats), BF16),
    ]


def tile_scratch(rows, codes):
    return [pltpu.VMEM((rows, codes), F32)] * 2 + [pltpu.VMEM((rows, codes), BF16)] * 4


def settings(limit=VMEM_LIMIT):
    return pltpu.CompilerParams(vmem_limit_bytes=limit)


def cost(rows, feats, dim, codes, tenths):
    return pl.CostEstimate(
        flops=rows * 24 * tenths * (5 * dim * codes + 3 * dim * feats) // 10,
        bytes_accessed=4 * rows * (2 * feats + 2 * codes + dim),
        transcendentals=2 * rows * codes,
    )


SMEM = pl.BlockSpec(memory_space=pltpu.SMEM)
VMEM = pl.BlockSpec(memory_space=pltpu.VMEM)
HBM = pl.BlockSpec(memory_space=pltpu.HBM)


def fixed(shape):
    return pl.BlockSpec(shape, lambda *_: (0,) * len(shape))


class Lane:
    def __init__(self, runs):
        self.runs = list(runs)
        self.bounds = [0]
        for _, _, slots in self.runs:
            self.bounds.append(self.bounds[-1] + slots)

    def total(self):
        return self.bounds[-1]

    def index(self, i, order_ref, count):
        share = order_ref.shape[1] // count
        step, slot = 0, 0
        for (whose, first, _), start in zip(self.runs, self.bounds):
            here = first + i - start
            step = whose if start == 0 else jnp.where(i >= start, whose, step)
            slot = here if start == 0 else jnp.where(i >= start, here, slot)
        there = partner(lax.axis_index("space"), step, count)
        return order_ref[0, there * share + slot]

    def image(self, shape, count):
        return pl.BlockSpec(
            (None, *shape), lambda i, order_ref: (self.index(i, order_ref, count), 0, 0)
        )

    def blocks(self, shape):
        return [
            pl.BlockSpec(
                shape,
                lambda i, _, start=start, last=slots - 1: (jnp.clip(i - start, 0, last), 0),
            )
            for (_, _, slots), start in zip(self.runs, self.bounds)
        ]

    def each(self, step, body):
        for i, (low, high) in enumerate(zip(self.bounds, self.bounds[1:])):
            pl.when((step >= low) & (step < high))(functools.partial(body, i))


def split(runs, ways):
    whole = Lane(runs)
    lanes, current = [], []
    for run in whole.runs:
        current.append(run)
        if Lane(current).total() * ways == whole.total():
            lanes.append(Lane(current))
            current = []
    return lanes if len(lanes) == ways and not current else [whole]


def take(refs, *sizes):
    groups, at = [], 0
    for size in sizes:
        groups.append(refs[at : at + size])
        at += size
    return groups


def by_lane(refs, lanes):
    return take(refs, *[len(lane.runs) for lane in lanes])


def keep_codes(step, lanes, sends, code_scrs):
    for lane, refs, code_scr in zip(lanes, by_lane(sends, lanes), code_scrs):
        if len(lane.runs) > 1:

            def keep(i, refs=refs, code_scr=code_scr):
                refs[i][...] = code_scr[...]

            lane.each(step, keep)


def code_targets(lanes, sends, code_scrs):
    return [
        refs[0] if len(lane.runs) == 1 else code_scr
        for lane, refs, code_scr in zip(lanes, by_lane(sends, lanes), code_scrs)
    ]


class Gradients:
    def __init__(self, out_ref, scr, sems):
        self.out_ref, self.scr, self.sems = out_ref, scr, sems

    def copy(self, lane, slot, image):
        return pltpu.make_async_copy(
            self.scr.at[lane, slot], self.out_ref.at[image], self.sems.at[lane, slot]
        )

    def ready(self, step, lanes):
        @pl.when(step >= 2)
        def _():
            for lane in range(lanes):
                self.copy(lane, lax.rem(step, 2), 0).wait()

    def store(self, step, values, images):
        slot = lax.rem(step, 2)
        for lane, (value, image) in enumerate(zip(values, images)):
            self.scr[lane, slot] = value
            self.copy(lane, slot, image).start()

    def end(self, step, lanes, steps):
        @pl.when(step == steps - 1)
        def _():
            for lane in range(lanes):
                for slot in range(min(2, steps)):
                    self.copy(lane, slot, 0).wait()


def gradient_scratch(lanes, strip, width):
    return [pltpu.VMEM((lanes, 2, strip, width), F32), pltpu.SemaphoreType.DMA((lanes, 2))]


def places_of(orders, shapes, groups, steps, count):
    me = lax.axis_index("space")
    strips = []
    at = 0
    for k, step in enumerate(steps):
        there = partner(me, step, count)
        row = 0
        for size in range(2):
            strip = shapes[size][1]
            for j in range(groups[size]):
                image = orders[size][0, there * groups[size] + j]
                strips.append((k, row, size, image, at, strip))
                row += strip
                at += strip
    return strips


def small_forward_kernel(count, steps, groups, *refs):
    sources, wide_in, (log_ref, heat_ref), sends, (usage_ref, scalar_ref), wide_out, held, rest = (
        take(refs, 9, 1, 2, len(steps), 2, 1, 9, len(refs))
    )
    (sems, feat_scr), shared, (l_scr, noise_scr) = take(rest, 2, 3, 2)
    copies = [
        pltpu.make_async_copy(there, here, sems.at[i])
        for i, (there, here) in enumerate(zip([*sources, *wide_in], [*held, *wide_out]))
    ]
    for copy in copies:
        copy.start()
    params, orders, feats, noises = (*held[0:3], scalar_ref), held[3:5], held[5:7], held[7:9]
    set_scalars(log_ref, heat_ref, scalar_ref)
    for copy in copies[0:7]:
        copy.wait()
    prepare(params, *shared, backward=False)
    strips = places_of(orders, [f.shape for f in feats], groups, steps, count)
    for _, _, size, image, at, strip in strips:
        feat_scr[at : at + strip] = feats[size][image]
    forward_products(params, shared, feat_scr[...], l_scr)
    for copy in copies[7:9]:
        copy.wait()
    usage = jnp.zeros(usage_ref.shape, F32)
    part = sends[0].shape[0]
    if all(noise.shape[1] % 8 == 0 for noise in noises):
        for k, row, size, image, at, strip in strips:
            rows = pl.ds(at, strip)
            target = sends[k].at[pl.ds(row, strip)]
            usage = forward_rows(params, l_scr.at[rows], noises[size].at[image], target, usage)
    else:
        for _, _, size, image, at, strip in strips:
            noise_scr[at : at + strip] = noises[size][image]
        for k, send in enumerate(sends):
            rows = pl.ds(k * part, part)
            usage = forward_rows(params, l_scr.at[rows], noise_scr.at[rows], send, usage)
    usage_ref[...] = usage
    copies[9].wait()


def small_forward(count, steps, orders, feats, noises, params):
    dim, codes = params[2].shape
    width = feats[0].shape[2]
    groups = tuple(f.shape[0] // count for f in feats)
    part = sum(g * f.shape[1] for g, f in zip(groups, feats))
    rows = part * len(steps)
    arrays = [*params[0:3], *orders[0:2], *feats, *noises]
    return pl.pallas_call(
        functools.partial(small_forward_kernel, count, steps, groups),
        out_shape=[jax.ShapeDtypeStruct((part, codes), F32)] * len(steps)
        + [
            jax.ShapeDtypeStruct((8, codes), F32),
            jax.ShapeDtypeStruct((8, 128), F32),
            jax.ShapeDtypeStruct(orders[2].shape, jnp.int32),
        ],
        in_specs=[HBM] * 10 + [SMEM] * 2,
        out_specs=[VMEM] * (len(steps) + 3),
        scratch_shapes=[
            (pltpu.SMEM if 3 <= i < 5 else pltpu.VMEM)(a.shape, a.dtype)
            for i, a in enumerate(arrays)
        ]
        + [pltpu.SemaphoreType.DMA((10,)), pltpu.VMEM((rows, width), F32)]
        + shared_scratch(dim, codes, width)
        + [pltpu.VMEM((rows, codes), F32)] * 2,
        compiler_params=settings(),
        cost_estimate=cost(rows, width, dim, codes, 4),
        name="small_forward",
    )(*in_hbm([*arrays, orders[2]]), *params[3:5])


def small_backward_kernel(count, steps, devices, groups, *refs):
    orders, feats, cots, parts, params, (acc_in, *usages), grads, shards, rest = take(
        refs, 2, 2, 2, count, 4, 3, 2, devices, len(refs)
    )
    acc_ref, sum_scr, feat_scr, cot_scr, code_scr = rest[0:5]
    scr = rest[5:]
    strips = places_of(orders, [f.shape for f in feats], groups, steps, count)
    for _, _, size, image, at, strip in strips:
        feat_scr[at : at + strip] = feats[size][image]
        cot_scr[at : at + strip] = cots[size][image]
    part = parts[0].shape[0]
    for step in range(count):
        code_scr[step * part : (step + 1) * part] = parts[step][...]
    shared, tile_scr = take(scr, 3, 6)
    prepare(params, *shared)
    acc_ref[...] = acc_in[...]
    state = products(params, shared, tile_scr, feat_scr[...], cot_scr[...].T, False)
    backward_rows(tile_scr, code_scr)
    feat_scr[...] = gradients(params, shared, tile_scr, state, acc_ref)
    acc_ref[136:144] += usages[0][...] + usages[1][...]
    lay_out(params, acc_ref, sum_scr, shards)
    for _, _, size, image, at, strip in strips:
        grads[size][image] = feat_scr[at : at + strip]


def small_backward(count, steps, devices, orders, feats, cots, parts, params, acc, usages):
    dim, codes = params[2].shape
    width = feats[0].shape[2]
    groups = tuple(f.shape[0] // count for f in feats)
    rows = parts[0].shape[0] * count
    return pl.pallas_call(
        functools.partial(small_backward_kernel, count, steps, devices, groups),
        out_shape=[pltpu.HBM(f.shape, F32) for f in feats]
        + [jax.ShapeDtypeStruct((64 // devices, LANES), F32)] * devices,
        in_specs=[SMEM] * 2 + [VMEM] * (11 + count),
        out_specs=[VMEM] * (2 + devices),
        scratch_shapes=[
            pltpu.VMEM(acc.shape, F32),
            pltpu.VMEM((64, LANES), F32),
            pltpu.VMEM((rows, width), F32),
            pltpu.VMEM((rows, dim), F32),
            pltpu.VMEM((rows, codes), F32),
        ]
        + shared_scratch(dim, codes, width)
        + tile_scratch(rows, codes),
        compiler_params=settings(),
        cost_estimate=cost(rows, width, dim, codes, 6),
        name="small_backward",
    )(
        *orders,
        *in_hbm([*feats, *cots]),
        *parts,
        *in_hbm(params[0:3]),
        params[3],
        acc,
        *usages,
    )


def wide_forward_kernel(lanes, joined, *refs):
    n = len(lanes)
    arrays = 1 if joined else sum(len(lane.runs) for lane in lanes)
    _, feats, noises, params, usage_in, sends, rest = take(
        refs, 1, n, n, 4, 1, arrays, len(refs)
    )
    (usage_ref,), code_scrs, shared, l_scrs = take(rest, 1, n, 3, n)
    step = pl.program_id(0)

    @pl.when(step == 0)
    def _():
        prepare(params, *shared, backward=False)
        usage_ref[...] = usage_in[0][...]

    if joined:
        strip = code_scrs[0].shape[0]
        targets = [sends[0].at[pl.ds(i * strip, strip)] for i in range(n)]
    else:
        targets = code_targets(lanes, sends, code_scrs)
    for feat_ref, l_scr in zip(feats, l_scrs):
        forward_products(params, shared, feat_ref[...], l_scr)
    usage = usage_ref[...]
    for l_scr, noise_ref, target in zip(l_scrs, noises, targets):
        usage = forward_rows(params, l_scr, noise_ref, target, usage)
    usage_ref[...] = usage
    if not joined:
        keep_codes(step, lanes, sends, code_scrs)


def wide_forward(count, lanes, joined, order, feat, noise, params, usage, tenths):
    dim, codes = params[2].shape
    images, strip, width = feat.shape
    n, steps = len(lanes), lanes[0].total()
    if joined:
        blocks = [fixed((n * strip, codes))]
        sizes = [n]
    else:
        blocks = [block for lane in lanes for block in lane.blocks((strip, codes))]
        sizes = [run[2] for lane in lanes for run in lane.runs]
    return pl.pallas_call(
        functools.partial(wide_forward_kernel, lanes, joined),
        grid_spec=pltpu.PrefetchScalarGridSpec(
            num_scalar_prefetch=1,
            grid=(steps,),
            in_specs=[lane.image((strip, width), count) for lane in lanes]
            + [lane.image((strip, codes), count) for lane in lanes]
            + [fixed(p.shape) for p in params]
            + [fixed(usage.shape)],
            out_specs=blocks + [fixed(usage.shape)],
            scratch_shapes=[pltpu.VMEM((strip, codes), F32)] * n
            + shared_scratch(dim, codes, width)
            + [pltpu.VMEM((strip, codes), F32)] * n,
        ),
        out_shape=[jax.ShapeDtypeStruct((strip * slots, codes), F32) for slots in sizes]
        + [jax.ShapeDtypeStruct(usage.shape, F32)],
        input_output_aliases={5 + 2 * n: len(sizes)},
        compiler_params=settings(),
        cost_estimate=cost(n * steps * strip, width, dim, codes, tenths),
        name="wide_forward",
    )(order, *in_hbm([feat] * n + [noise] * n + [*params[0:3]]), params[3], usage)


def wide_both_kernel(lanes, count, *refs):
    n = len(lanes)
    arrays = sum(len(lane.runs) for lane in lanes)
    order, feats, noises, cots, params, sends, rest = take(
        refs, 1, n, n, n, 4, arrays, len(refs)
    )
    (grad_out, acc_ref), code_scrs, (grad_scr, sems), shared, rest = take(
        rest, 2, n, 2, 3, 6 * n
    )
    scrs = take(rest, *[6] * n)
    grads = Gradients(grad_out, grad_scr, sems)
    step, steps = pl.program_id(0), lanes[0].total()

    @pl.when(step == 0)
    def _():
        prepare(params, *shared)
        acc_ref[...] = jnp.zeros(acc_ref.shape, F32)

    grads.ready(step, n)
    targets = code_targets(lanes, sends, code_scrs)
    states = [
        products(params, shared, scr, feat_ref[...], cot_ref[...], True)
        for scr, feat_ref, cot_ref in zip(scrs, feats, cots)
    ]
    usage = acc_ref[136:144]
    for scr, noise_ref, target in zip(scrs, noises, targets):
        usage = both_rows(params, scr, noise_ref, target, usage)
    acc_ref[136:144] = usage
    values = [
        gradients(params, shared, scr, state, acc_ref) for scr, state in zip(scrs, states)
    ]
    grads.store(step, values, [lane.index(step, order[0], count) for lane in lanes])
    keep_codes(step, lanes, sends, code_scrs)
    grads.end(step, n, steps)


def wide_both(count, lanes, order, feat, noise, cot, params):
    dim, codes = params[2].shape
    images, strip, width = feat.shape
    n, steps = len(lanes), lanes[0].total()
    acc_shape = (ACC_ROWS, codes)
    sizes = [run[2] for lane in lanes for run in lane.runs]
    return pl.pallas_call(
        functools.partial(wide_both_kernel, lanes, count),
        grid_spec=pltpu.PrefetchScalarGridSpec(
            num_scalar_prefetch=1,
            grid=(steps,),
            in_specs=[lane.image((strip, width), count) for lane in lanes]
            + [lane.image((strip, codes), count) for lane in lanes]
            + [lane.image((dim, strip), count) for lane in lanes]
            + [fixed(p.shape) for p in params],
            out_specs=[block for lane in lanes for block in lane.blocks((strip, codes))]
            + [HBM, fixed(acc_shape)],
            scratch_shapes=[pltpu.VMEM((strip, codes), F32)] * n
            + gradient_scratch(n, strip, width)
            + shared_scratch(dim, codes, width)
            + tile_scratch(strip, codes) * n,
        ),
        out_shape=[jax.ShapeDtypeStruct((strip * slots, codes), F32) for slots in sizes]
        + [pltpu.HBM(feat.shape, F32), jax.ShapeDtypeStruct(acc_shape, F32)],
        compiler_params=settings(),
        cost_estimate=cost(n * steps * strip, width, dim, codes, 10),
        name="wide_both",
    )(order, *in_hbm([feat] * n + [noise] * n + [cot] * n + [*params[0:3]]), params[3])


def wide_backward_kernel(lanes, count, *refs):
    n = len(lanes)
    arrays = sum(len(lane.runs) for lane in lanes)
    order, feats, cots, parts, params, (acc_in, _), rest = take(
        refs, 1, n, n, arrays, 4, 2, len(refs)
    )
    (grad_out, acc_ref), code_scrs, (grad_scr, sems), shared, rest = take(
        rest, 2, n, 2, 3, 6 * n
    )
    scrs = take(rest, *[6] * n)
    grads = Gradients(grad_out, grad_scr, sems)
    step, steps = pl.program_id(0), lanes[0].total()

    @pl.when(step == 0)
    def _():
        prepare(params, *shared)
        acc_ref[...] = acc_in[...]

    grads.ready(step, n)
    for lane, refs_of, code_scr in zip(lanes, by_lane(parts, lanes), code_scrs):
        if len(lane.runs) > 1:

            def fetch(i, refs_of=refs_of, code_scr=code_scr):
                code_scr[...] = refs_of[i][...]

            lane.each(step, fetch)
    states = [
        products(params, shared, scr, feat_ref[...], cot_ref[...], False)
        for scr, feat_ref, cot_ref in zip(scrs, feats, cots)
    ]
    for scr, code_ref in zip(scrs, code_targets(lanes, parts, code_scrs)):
        backward_rows(scr, code_ref)
    values = [
        gradients(params, shared, scr, state, acc_ref) for scr, state in zip(scrs, states)
    ]
    grads.store(step, values, [lane.index(step, order[0], count) for lane in lanes])
    grads.end(step, n, steps)


def wide_backward(count, lanes, parts, order, feat, cot, params, acc, grad):
    dim, codes = params[2].shape
    images, strip, width = feat.shape
    n, steps = len(lanes), lanes[0].total()
    return pl.pallas_call(
        functools.partial(wide_backward_kernel, lanes, count),
        grid_spec=pltpu.PrefetchScalarGridSpec(
            num_scalar_prefetch=1,
            grid=(steps,),
            in_specs=[lane.image((strip, width), count) for lane in lanes]
            + [lane.image((dim, strip), count) for lane in lanes]
            + [block for lane in lanes for block in lane.blocks((strip, codes))]
            + [fixed(p.shape) for p in params]
            + [fixed(acc.shape), HBM],
            out_specs=[HBM, fixed(acc.shape)],
            scratch_shapes=[pltpu.VMEM((strip, codes), F32)] * n
            + gradient_scratch(n, strip, width)
            + shared_scratch(dim, codes, width)
            + tile_scratch(strip, codes) * n,
        ),
        out_shape=[pltpu.HBM(feat.shape, F32), jax.ShapeDtypeStruct(acc.shape, F32)],
        input_output_aliases={5 + 2 * n + len(parts): 1, 6 + 2 * n + len(parts): 0},
        compiler_params=settings(),
        cost_estimate=cost(n * steps * strip, width, dim, codes, 6),
        name="wide_backward",
    )(
        order,
        *in_hbm([feat] * n + [cot] * n),
        *parts,
        *in_hbm(params[0:3]),
        params[3],
        acc,
        *in_hbm([grad]),
    )


def shard_at(index, parts):
    height = 64 // parts
    return pl.ds(pl.multiple_of(index * height, height), height)


def lay_out(params, acc_ref, sum_scr, shards):
    weight_ref, bias_ref, book_ref, scalar_ref = params
    codes = book_ref.shape[1]
    width = weight_ref.shape[1]
    devices = len(shards)
    me = lax.rem(lax.axis_index("dp"), devices)
    precision, _, factor = scalars(scalar_ref)
    book = book_ref[...]
    column = acc_ref[128:129]
    moment = acc_ref[64:128] * (1.0 / precision)
    book_sum = acc_ref[0:64] * (1.0 / factor) + 2.0 * (column * book - moment)
    slope = jnp.sum(
        jnp.sum(book * book, axis=0, keepdims=True) * column, axis=1, keepdims=True
    ) - 2.0 * jnp.sum(jnp.sum(book * moment, axis=0, keepdims=True), axis=1, keepdims=True)
    slope = slope + acc_ref[208:209, 0:1] / (-0.5 * precision)
    usage = jnp.sum(acc_ref[136:144], axis=0, keepdims=True)
    dim = book_ref.shape[0]
    eye = lax.broadcasted_iota(jnp.int32, (dim, dim), 0) == lax.broadcasted_iota(
        jnp.int32, (dim, dim), 1
    )
    bias = acc_ref[144:208, width : width + dim]
    bias = jnp.sum(jnp.where(eye, bias, 0.0), axis=0, keepdims=True)
    rest = codes + width
    sum_scr[:, 0:codes] = book_sum
    sum_scr[:, codes:rest] = acc_ref[144:208, 0:width]
    sum_scr[:, rest : rest + 128] = jnp.broadcast_to(slope, (64, 128))
    rows = codes // 128
    for i in range(rows):
        sum_scr[i : i + 1, rest : rest + 128] = usage[:, i * 128 : (i + 1) * 128]
    sum_scr[rows : rows + 1, rest : rest + dim] = bias
    for i in range(devices):
        shards[i][...] = sum_scr[shard_at(partner(me, i, devices), devices)]


def own_kernel(n, count, *refs):
    order, feats, noises, cots, params, (acc_in, _), rest = take(
        refs, 1, n, n, n, 4, 2, len(refs)
    )
    (code_ref, grad_out, acc_ref), (grad_scr, sems), shared, rest = take(rest, 3, 2, 3, 6 * n)
    scrs = take(rest, *[6] * n)
    grads = Gradients(grad_out, grad_scr, sems)
    step = pl.program_id(0)

    @pl.when(step == 0)
    def _():
        prepare(params, *shared)
        acc_ref[...] = acc_in[...]

    grads.ready(step, n)
    states = [
        products(params, shared, scr, feat_ref[...], cot_ref[...], True)
        for scr, feat_ref, cot_ref in zip(scrs, feats, cots)
    ]
    usage = acc_ref[136:144]
    for i, (scr, noise_ref) in enumerate(zip(scrs, noises)):
        usage = both_rows(params, scr, noise_ref, code_ref.at[i], usage)
    acc_ref[136:144] = usage
    values = [
        gradients(params, shared, scr, state, acc_ref) for scr, state in zip(scrs, states)
    ]
    grads.store(step, values, [own_image(step, i, n, order[0], count) for i in range(n)])
    grads.end(step, n, pl.num_programs(0))


def own_image(step, lane, n, order_ref, count):
    share = order_ref.shape[1] // count
    return order_ref[0, lax.axis_index("space") * share + step * n + lane]


def run_own(count, order, feat, noise, cot, params, acc, grad):
    dim, codes = params[2].shape
    images, strip, width = feat.shape
    share = images // count
    n = 2 if share % 2 == 0 else 1

    def image(lane, shape):
        return pl.BlockSpec(
            (None, *shape), lambda i, order_ref: (own_image(i, lane, n, order_ref, count), 0, 0)
        )

    return pl.pallas_call(
        functools.partial(own_kernel, n, count),
        grid_spec=pltpu.PrefetchScalarGridSpec(
            num_scalar_prefetch=1,
            grid=(share // n,),
            in_specs=[image(lane, (strip, width)) for lane in range(n)]
            + [image(lane, (strip, codes)) for lane in range(n)]
            + [image(lane, (dim, strip)) for lane in range(n)]
            + [fixed(p.shape) for p in params]
            + [fixed(acc.shape), HBM],
            out_specs=[
                pl.BlockSpec(
                    (n, strip, codes),
                    lambda i, _: (i, lax.axis_index("space"), 0),
                ),
                HBM,
                fixed(acc.shape),
            ],
            scratch_shapes=gradient_scratch(n, strip, width)
            + shared_scratch(dim, codes, width)
            + tile_scratch(strip, codes) * n,
        ),
        out_shape=[
            pltpu.HBM((share, strip * count, codes), F32),
            pltpu.HBM(feat.shape, F32),
            jax.ShapeDtypeStruct(acc.shape, F32),
        ],
        input_output_aliases={5 + 3 * n: 2, 6 + 3 * n: 1},
        compiler_params=settings(),
        cost_estimate=cost(share * strip, width, dim, codes, 10),
        name="own_images",
    )(
        order,
        *in_hbm([feat] * n + [noise] * n + [cot] * n + [*params[0:3]]),
        params[3],
        acc,
        *in_hbm([grad]),
    )


def place_kernel(count, runs, *refs):
    parts = refs[0 : len(runs)]
    out_ref, sem = refs[len(runs) + 1 : len(runs) + 3]
    me = lax.axis_index("space")
    copies = []
    for part, (step, first, slots) in zip(parts, runs):
        strip = part.shape[0] // slots
        row = pl.multiple_of(source(me, step, count) * strip, strip)
        for j in range(slots):
            copies.append(
                pltpu.make_async_copy(
                    part.at[pl.ds(j * strip, strip)],
                    out_ref.at[first + j, pl.ds(row, strip)],
                    sem.at[len(copies)],
                )
            )
    for copy in copies:
        copy.start()
    for copy in copies:
        copy.wait()


def place_wide(count, runs, parts, whole):
    return pl.pallas_call(
        functools.partial(place_kernel, count, runs),
        out_shape=pltpu.HBM(whole.shape, F32),
        in_specs=[VMEM] * len(runs) + [HBM],
        out_specs=HBM,
        scratch_shapes=[pltpu.SemaphoreType.DMA((sum(r[2] for r in runs),))],
        input_output_aliases={len(runs): 0},
        compiler_params=settings(VMEM_LIMIT // 2),
        cost_estimate=pl.CostEstimate(
            flops=0, bytes_accessed=2 * sum(p.size * 4 for p in parts), transcendentals=0
        ),
        name="place_wide",
    )(*[pltpu.with_memory_space_constraint(p, pltpu.VMEM) for p in parts], *in_hbm([whole]))


def join_kernel(count, steps, *refs):
    parts = refs[0:count]
    outs = refs[count:]
    me = lax.axis_index("space")
    for part, step in zip(parts, steps):
        here = source(me, step, count)
        base = 0
        for out in outs:
            for j in range(out.shape[0]):
                strip = out.shape[2]
                out[j, here] = part[base : base + strip]
                base += strip


def join_small(count, steps, parts, shapes):
    codes = parts[0].shape[1]
    return pl.pallas_call(
        functools.partial(join_kernel, count, steps),
        out_shape=[
            jax.ShapeDtypeStruct((images // count, count, strip, codes), F32)
            for images, strip, _ in shapes
        ],
        compiler_params=settings(VMEM_LIMIT // 2),
        name="join_small",
    )(*parts)


def tree(values):
    while len(values) > 1:
        values = [
            values[i] + values[i + 1] if i + 1 < len(values) else values[i]
            for i in range(0, len(values), 2)
        ]
    return values[0]


def sum_kernel(*refs):
    refs[-1][...] = tree([ref[...] for ref in refs[:-1]])


def add_all(parts):
    return pl.pallas_call(
        sum_kernel,
        out_shape=jax.ShapeDtypeStruct(parts[0].shape, F32),
        compiler_params=settings(VMEM_LIMIT // 2),
        name="add_parts",
    )(*parts)


def final_kernel(devices, pixels, *refs):
    shards = refs[0:devices]
    weight_ref, bias_ref, book_ref, log_ref, usage_ref = refs[devices : devices + 5]
    weight_out, bias_out, book_out, log_out, usage_out = refs[devices + 5 : devices + 10]
    sum_scr = refs[devices + 10]
    me = lax.rem(lax.axis_index("dp"), devices)
    for i in range(devices):
        sum_scr[shard_at(source(me, i, devices), devices)] = shards[i][...]
    dim, codes = book_ref.shape
    width = weight_ref.shape[1]
    scale = 0.5 * lax.rsqrt(jnp.full((8, 128), pixels, F32))[0:1, 0:1]
    book_out[...] = 0.5 * book_ref[...] + scale * sum_scr[:, 0:codes]
    rest = codes + width
    weight_out[...] = 0.5 * weight_ref[...] + scale * sum_scr[:, codes:rest]
    rows = codes // 128
    bias_out[...] = 0.5 * bias_ref[...] + scale * sum_scr[rows : rows + 1, rest : rest + dim]
    usage = jnp.concatenate(
        [sum_scr[i : i + 1, rest : rest + 128] for i in range(rows)], axis=1
    )
    usage_out[...] = 0.5 * usage_ref[...] + 0.5 * (codes / pixels) * usage
    log_out[...] = 0.5 * log_ref[...] + scale * sum_scr[rows + 1 : rows + 2, rest : rest + 1]


def finish(devices, pixels, shards, weight, bias, book, log, usage):
    outs = (weight.T, bias.reshape(1, -1), book.T, log.reshape(1, 1), usage.reshape(1, -1))
    outs = pl.pallas_call(
        functools.partial(final_kernel, devices, pixels),
        out_shape=[jax.ShapeDtypeStruct(out.shape, F32) for out in outs],
        scratch_shapes=[pltpu.VMEM((64, LANES), F32)],
        compiler_params=settings(VMEM_LIMIT // 2),
        name="new_averages",
    )(*shards, *outs)
    return outs[0].T, outs[1].reshape(-1), outs[2].T, outs[3].reshape(-1), outs[4].reshape(-1)


def exchange(value, bit, size, pairs):
    while bit < size:
        value = value + pairs(value, bit)
        bit = 2 * bit
    return value


def per_device(
    feat_small,
    feat_mid,
    feat_wide,
    noise_small,
    noise_mid,
    noise_wide,
    cot_small,
    cot_mid,
    cot_wide,
    order_small,
    order_mid,
    order_wide,
    weight,
    bias,
    book,
    log,
    heat,
    weight_mean,
    bias_mean,
    book_mean,
    log_mean,
    usage_mean,
):
    count = lax.axis_size("space")
    devices = lax.axis_size("dp")
    params = (weight.T, bias.reshape(1, -1), book.T, log, heat)
    feats = (feat_small, feat_mid, feat_wide)
    pixels = sum(f.shape[0] * f.shape[1] for f in feats) * count * devices
    share = feat_wide.shape[0] // count
    cot_wide = jnp.swapaxes(cot_wide, 1, 2)

    def send(values):
        return [lax.ppermute(v, "space", route(i, count)) for i, v in zip(turns, values)]

    def follow(codes, before, parts):
        here, codes[-1] = lax.optimization_barrier(([before[i] for i in parts], codes[-1]))
        for i, part in zip(parts, here):
            before[i] = part
        return send(codes)

    last = count - 1
    turns = list(range(1, count))
    orders = (order_small, order_mid, order_wide)
    noises = (noise_small, noise_mid)
    *small, usage, scalar, order_wide = small_forward(
        count, turns, orders, feats[0:2], noises, params
    )
    arrived = [send(small)]
    own_params = params
    params = (*params[0:3], scalar)
    near = min(4, devices)
    early = [(step, 0, 1) for step in turns]
    direct = [(step, 1, share - 1) for step in turns[:-1]]
    late = [(last, 1, share - 1)]
    *early_codes, usage = wide_forward(
        count, split(early, 3), False, order_wide, feat_wide, noise_wide, params, usage, 4
    )
    ahead = [count - 2, *range(count - 2)]
    arrived.append(follow(list(early_codes), arrived[0], ahead))
    *codes, grad, acc = wide_both(
        count, split(direct, 2), order_wide, feat_wide, noise_wide, cot_wide, params
    )
    late_lanes = [Lane([(last, slot, 1)]) for slot in range(1, share)]
    late_codes, usage = wide_forward(
        count, late_lanes, True, order_wide, feat_wide, noise_wide, params, usage, 1
    )
    arrived.append(follow([*codes, late_codes], arrived[1], [0]))
    arrived[1], acc = lax.optimization_barrier((arrived[1], acc))
    whole, grad, acc = run_own(
        count, order_wide, feat_wide, noise_wide, cot_wide, params, acc, grad
    )
    whole = place_wide(count, early, arrived[1], whole)
    acc, own_params = lax.optimization_barrier((acc, own_params))
    own, own_usage, _, _ = small_forward(
        count, range(1), orders, feats[0:2], noises, own_params
    )
    small = [own, *small]
    codes_small, codes_mid = join_small(
        count, [0, *turns], [own] + arrived[0], [f.shape for f in feats[0:2]]
    )
    whole, codes_small, codes_mid, acc = lax.optimization_barrier(
        (whole, codes_small, codes_mid, acc)
    )
    grad, acc = wide_backward(
        count,
        split(early + late, 2),
        [*early_codes, late_codes],
        order_wide,
        feat_wide,
        cot_wide,
        params,
        acc,
        grad,
    )
    grad_small, grad_mid, *shards = small_backward(
        count,
        [0, *turns],
        near,
        orders[0:2],
        feats[0:2],
        (cot_small, cot_mid),
        small,
        params,
        acc,
        (usage, own_usage),
    )
    group = [
        [(i, i - i % near + partner(i % near, step, near)) for i in range(devices)]
        for step in range(near)
    ]
    parts = [lax.ppermute(shards[i], "dp", group[i]) for i in range(1, near)]
    mine = add_all([shards[0]] + parts)

    def along(value, offset):
        return lax.ppermute(value, "dp", [(i, i ^ offset) for i in range(devices)])

    def across(value, offset):
        turn = near if devices > near else 0
        pairs = [
            (i * count + j, (i ^ turn) * count + (j ^ offset))
            for i in range(devices)
            for j in range(count)
        ]
        return lax.ppermute(value, ("dp", "space"), pairs)

    mine = exchange(mine, near, devices, along)
    mine = exchange(mine, 1, count, across)
    shards = [mine] + [lax.ppermute(mine, "dp", group[i]) for i in range(1, near)]
    updated = finish(
        near, pixels, shards, weight_mean, bias_mean, book_mean, log_mean, usage_mean
    )
    for run, part in zip(direct + late, arrived[2]):
        whole = place_wide(count, [run], [part], whole)
    codes = whole.shape[2]
    return (
        codes_small.reshape(codes_small.shape[0], -1, codes),
        codes_mid.reshape(codes_mid.shape[0], -1, codes),
        whole,
        grad_small,
        grad_mid,
        grad,
        *updated,
    )


def solution(mesh):
    strips = P("dp", "space", None)
    placed = (strips,) * 9 + (P("dp", None),) * 3 + (P(),) * 10
    return jax.shard_map(
        per_device,
        mesh=mesh,
        in_specs=placed,
        out_specs=(P(("dp", "space"), None, None),) * 3 + (strips,) * 3 + (P(),) * 5,
        check_vma=False,
    )
```

```python
import functools

import jax
import jax.numpy as jnp
from jax import lax
from jax.experimental import pallas as pl
from jax.experimental.pallas import tpu as pltpu
from jax.sharding import PartitionSpec as P

F32 = jnp.float32
BF16 = jnp.bfloat16
VMEM_LIMIT = 24 * 1024 * 1024
ACC_ROWS = 64 + 64 + 8 + 8 + 64 + 8
LANES = 896


def partner(index, step, count):
    if count & (count - 1) == 0:
        return index ^ step
    return lax.rem(index + step, count)


def route(step, count):
    if count & (count - 1) == 0:
        return [(i, i ^ step) for i in range(count)]
    return [(i, (i + step) % count) for i in range(count)]


def source(index, step, count):
    if count & (count - 1) == 0:
        return index ^ step
    return lax.rem(index + (count - step), count)


def in_hbm(arrays):
    return [pltpu.with_memory_space_constraint(a, pltpu.HBM) for a in arrays]


def halves(x):
    high = x.astype(BF16)
    return high, (x - high.astype(F32)).astype(BF16)


def dot(left, right, left_dim=1, right_dim=0):
    return lax.dot_general(
        left, right, (((left_dim,), (right_dim,)), ((), ())), preferred_element_type=F32
    )


def set_scalars(log_ref, heat_ref, out_ref):
    precision = jnp.exp(jnp.full((8, 128), log_ref[0], F32))
    heat = jnp.full((8, 128), heat_ref[0], F32)
    row = lax.broadcasted_iota(jnp.int32, (8, 128), 0)
    factor = -0.5 * precision / heat
    out_ref[...] = jnp.where(row == 0, precision, jnp.where(row == 1, 1.0 / heat, factor))


def scalars(ref):
    return ref[0:1, 0:1], ref[1:2, 0:1], ref[2:3, 0:1]


def prepare(refs, book_scr, books_scr, weight_scr, backward=True):
    weight_ref, bias_ref, book_ref, scalar_ref = refs
    dim, codes = book_ref.shape
    precision, _, _ = scalars(scalar_ref)
    book = book_ref[...]
    high, low = halves(book)
    norm = -0.5 * precision * jnp.sum(book * book, axis=0, keepdims=True)
    n0 = norm.astype(BF16).astype(F32)
    n1 = (norm - n0).astype(BF16).astype(F32)
    n2 = norm - n0 - n1
    row = lax.broadcasted_iota(jnp.int32, (16, codes), 0)
    extra = jnp.where(
        row < 3,
        1.0,
        jnp.where(row == 3, n0, jnp.where(row == 4, n1, jnp.where(row == 5, n2, 0.0))),
    ).astype(BF16)
    book_scr[0:dim] = high
    book_scr[dim : 2 * dim] = low
    book_scr[2 * dim : 3 * dim] = high
    book_scr[3 * dim : 3 * dim + 16] = extra
    if backward:
        books_scr[0:dim] = high
        books_scr[dim : 2 * dim] = low
        books_scr[2 * dim : 2 * dim + 16] = jnp.ones((16, codes), BF16)
    high, low = halves(weight_ref[...])
    weight_scr[0:dim] = high
    weight_scr[dim : 2 * dim] = low
    weight_scr[2 * dim : 3 * dim] = high


def latents(refs, shared, feat):
    weight_ref, bias_ref, book_ref, scalar_ref = refs
    weight_scr = shared[2]
    dim = book_ref.shape[0]
    precision, _, _ = scalars(scalar_ref)
    eye = lax.broadcasted_iota(jnp.int32, (dim, dim), 0) == lax.broadcasted_iota(
        jnp.int32, (dim, dim), 1
    )
    bias = jnp.sum(jnp.where(eye, bias_ref[...], 0.0), axis=1, keepdims=True)
    fh, fl = halves(feat)
    both = weight_scr[0 : 2 * dim]
    z2 = dot(both, fh, 1, 1) + dot(both, fl, 1, 1)
    z = z2[0:dim] + z2[dim : 2 * dim] + bias
    square = -0.5 * precision * jnp.sum(z * z, axis=0, keepdims=True)
    return fh, fl, z, square


def logit_rows(zh, zl, square):
    rows = zh.shape[1]
    s0 = square.astype(BF16).astype(F32)
    s1 = (square - s0).astype(BF16).astype(F32)
    s2 = square - s0 - s1
    row = lax.broadcasted_iota(jnp.int32, (16, rows), 0)
    extra = jnp.where(
        row == 0,
        s0,
        jnp.where(row == 1, s1, jnp.where(row == 2, s2, jnp.where(row < 6, 1.0, 0.0))),
    ).astype(BF16)
    return jnp.concatenate([zh, zh, zl, extra], axis=0)


def cot_rows(ch, cl):
    return jnp.concatenate([ch, ch, cl, jnp.zeros((16, ch.shape[1]), BF16)], axis=0)


def over_rows(rows, body, carry):
    step = next(s for s in (32, 16, 8) if rows % s == 0)

    def at(i, carry):
        return body(pl.ds(pl.multiple_of(i * step, step), step), carry)

    return lax.fori_loop(0, rows // step, at, carry, unroll=True)


def folded(x):
    return jnp.sum(x.reshape(x.shape[0] // 8, 8, x.shape[1]), axis=0)


def probabilities(logits):
    top = jnp.max(logits, axis=1, keepdims=True)
    e = jnp.exp(logits - top)
    return e * (1.0 / jnp.sum(e, axis=1, keepdims=True))


def forward_products(refs, shared, feat, l_scr):
    precision, _, _ = scalars(refs[3])
    _, _, z, square = latents(refs, shared, feat)
    zh, zl = halves(precision * z)
    l_scr[0 : feat.shape[0]] = dot(logit_rows(zh, zl, square), shared[0][...], 0, 0)


def forward_rows(refs, l_scr, noise_ref, code_ref, usage):
    _, cold, _ = scalars(refs[3])

    def body(at, usage):
        logits = l_scr[at]
        code_ref[at] = probabilities((logits + noise_ref[at]) * cold)
        return usage + folded(probabilities(logits))

    return over_rows(code_ref.shape[0], body, usage)


def products(refs, shared, scr, feat, cot, forward):
    l_scr, g_scr = scr[0:2]
    rows = feat.shape[0]
    precision, _, factor = scalars(refs[3])
    fh, fl, z, square = latents(refs, shared, feat)
    zh, zl = halves(precision * z)
    ch, cl = halves(factor * cot)
    if forward:
        left = jnp.concatenate([logit_rows(zh, zl, square), cot_rows(ch, cl)], axis=1)
        p = dot(left, shared[0][...], 0, 0)
        l_scr[0:rows] = p[0:rows]
        g_scr[0:rows] = p[rows : 2 * rows]
    else:
        g_scr[0:rows] = dot(cot_rows(ch, cl), shared[0][...], 0, 0)
    return fh, fl, z, square, zh, zl, ch, cl


def both_rows(refs, scr, noise_ref, code_ref, usage):
    l_scr, g_scr, wh_scr, wl_scr, gh_scr, gl_scr = scr
    _, cold, _ = scalars(refs[3])

    def body(at, usage):
        logits = l_scr[at]
        s = (logits + noise_ref[at]) * cold
        e = jnp.exp(s - jnp.max(s, axis=1, keepdims=True))
        gw = g_scr[at]
        scale = 1.0 / jnp.sum(e, axis=1, keepdims=True)
        inner = jnp.sum(e * gw, axis=1, keepdims=True) * scale
        w = e * scale
        code_ref[at] = w
        gd = w * (gw - inner)
        wh_scr[at], wl_scr[at] = halves(w)
        gh_scr[at], gl_scr[at] = halves(gd)
        return usage + folded(probabilities(logits))

    return over_rows(code_ref.shape[0], body, usage)


def backward_rows(scr, code_ref):
    _, g_scr, wh_scr, wl_scr, gh_scr, gl_scr = scr

    def body(at, carry):
        w = code_ref[at]
        gw = g_scr[at]
        gd = w * (gw - jnp.sum(w * gw, axis=1, keepdims=True))
        wh_scr[at], wl_scr[at] = halves(w)
        gh_scr[at], gl_scr[at] = halves(gd)
        return carry

    over_rows(code_ref.shape[0], body, 0)


def gradients(refs, shared, scr, state, acc_ref):
    _, books_scr, weight_scr = shared
    wh_scr, wl_scr, gh_scr, gl_scr = scr[2:6]
    fh, fl, z, square, zh, zl, ch, cl = state
    rows, feats = fh.shape
    dim, codes = refs[2].shape
    wh, wl = wh_scr[0:rows], wl_scr[0:rows]
    gh, gl = gh_scr[0:rows], gl_scr[0:rows]
    p = dot(jnp.concatenate([ch, cl], axis=0), wh)
    acc_ref[0:64] += p[0:dim] + p[dim : 2 * dim] + dot(ch, wl)
    left = jnp.concatenate([zh, zl, jnp.ones((16, rows), BF16)], axis=0)
    p = dot(left, gh) + dot(left, gl)
    acc_ref[64:128] += p[0:dim] + p[dim : 2 * dim]
    acc_ref[128:136] += p[2 * dim : 2 * dim + 8]
    p = dot(books_scr[...], gh, 1, 1) + dot(books_scr[...], gl, 1, 1)
    row_d = p[2 * dim : 2 * dim + 1]
    gz = 2.0 * (row_d * z - (p[0:dim] + p[dim : 2 * dim]))
    zh, zl = halves(gz)
    p = dot(jnp.concatenate([zh, zl], axis=0), fh)
    acc_ref[144:208, 0:feats] += p[0:dim] + p[dim : 2 * dim] + dot(zh, fl)
    acc_ref[144:208, feats : feats + 128] += jnp.broadcast_to(
        jnp.sum(gz, axis=1, keepdims=True), (dim, 128)
    )
    total = jnp.sum(square * row_d, axis=1, keepdims=True)
    acc_ref[208:216] += jnp.broadcast_to(total, (8, codes))
    return dot(jnp.concatenate([zh, zh, zl], axis=0), weight_scr[...], 0, 0)


def shared_scratch(dim, codes, feats):
    return [
        pltpu.VMEM((3 * dim + 16, codes), BF16),
        pltpu.VMEM((2 * dim + 16, codes), BF16),
        pltpu.VMEM((3 * dim, feats), BF16),
    ]


def tile_scratch(rows, codes):
    return [pltpu.VMEM((rows, codes), F32)] * 2 + [pltpu.VMEM((rows, codes), BF16)] * 4


def settings(limit=VMEM_LIMIT):
    return pltpu.CompilerParams(vmem_limit_bytes=limit)


def cost(rows, feats, dim, codes, tenths):
    return pl.CostEstimate(
        flops=rows * 24 * tenths * (5 * dim * codes + 3 * dim * feats) // 10,
        bytes_accessed=4 * rows * (2 * feats + 2 * codes + dim),
        transcendentals=2 * rows * codes,
    )


SMEM = pl.BlockSpec(memory_space=pltpu.SMEM)
VMEM = pl.BlockSpec(memory_space=pltpu.VMEM)
HBM = pl.BlockSpec(memory_space=pltpu.HBM)


def fixed(shape):
    return pl.BlockSpec(shape, lambda *_: (0,) * len(shape))


class Lane:
    def __init__(self, runs):
        self.runs = list(runs)
        self.bounds = [0]
        for _, _, slots in self.runs:
            self.bounds.append(self.bounds[-1] + slots)

    def total(self):
        return self.bounds[-1]

    def index(self, i, order_ref, count):
        share = order_ref.shape[1] // count
        step, slot = 0, 0
        for (whose, first, _), start in zip(self.runs, self.bounds):
            here = first + i - start
            step = whose if start == 0 else jnp.where(i >= start, whose, step)
            slot = here if start == 0 else jnp.where(i >= start, here, slot)
        there = partner(lax.axis_index("space"), step, count)
        return order_ref[0, there * share + slot]

    def image(self, shape, count):
        return pl.BlockSpec(
            (None, *shape), lambda i, order_ref: (self.index(i, order_ref, count), 0, 0)
        )

    def blocks(self, shape):
        return [
            pl.BlockSpec(
                shape,
                lambda i, _, start=start, last=slots - 1: (jnp.clip(i - start, 0, last), 0),
            )
            for (_, _, slots), start in zip(self.runs, self.bounds)
        ]

    def each(self, step, body):
        for i, (low, high) in enumerate(zip(self.bounds, self.bounds[1:])):
            pl.when((step >= low) & (step < high))(functools.partial(body, i))


def split(runs, ways):
    whole = Lane(runs)
    lanes, current = [], []
    for run in whole.runs:
        current.append(run)
        if Lane(current).total() * ways == whole.total():
            lanes.append(Lane(current))
            current = []
    return lanes if len(lanes) == ways and not current else [whole]


def take(refs, *sizes):
    groups, at = [], 0
    for size in sizes:
        groups.append(refs[at : at + size])
        at += size
    return groups


def by_lane(refs, lanes):
    return take(refs, *[len(lane.runs) for lane in lanes])


def keep_codes(step, lanes, sends, code_scrs):
    for lane, refs, code_scr in zip(lanes, by_lane(sends, lanes), code_scrs):
        if len(lane.runs) > 1:

            def keep(i, refs=refs, code_scr=code_scr):
                refs[i][...] = code_scr[...]

            lane.each(step, keep)


def code_targets(lanes, sends, code_scrs):
    return [
        refs[0] if len(lane.runs) == 1 else code_scr
        for lane, refs, code_scr in zip(lanes, by_lane(sends, lanes), code_scrs)
    ]


class Gradients:
    def __init__(self, out_ref, scr, sems):
        self.out_ref, self.scr, self.sems = out_ref, scr, sems

    def copy(self, lane, slot, image):
        return pltpu.make_async_copy(
            self.scr.at[lane, slot], self.out_ref.at[image], self.sems.at[lane, slot]
        )

    def ready(self, step, lanes):
        @pl.when(step >= 2)
        def _():
            for lane in range(lanes):
                self.copy(lane, lax.rem(step, 2), 0).wait()

    def store(self, step, values, images):
        slot = lax.rem(step, 2)
        for lane, (value, image) in enumerate(zip(values, images)):
            self.scr[lane, slot] = value
            self.copy(lane, slot, image).start()

    def end(self, step, lanes, steps):
        @pl.when(step == steps - 1)
        def _():
            for lane in range(lanes):
                for slot in range(min(2, steps)):
                    self.copy(lane, slot, 0).wait()


def gradient_scratch(lanes, strip, width):
    return [pltpu.VMEM((lanes, 2, strip, width), F32), pltpu.SemaphoreType.DMA((lanes, 2))]


def places_of(orders, shapes, groups, steps, count):
    me = lax.axis_index("space")
    strips = []
    at = 0
    for k, step in enumerate(steps):
        there = partner(me, step, count)
        row = 0
        for size in range(2):
            strip = shapes[size][1]
            for j in range(groups[size]):
                image = orders[size][0, there * groups[size] + j]
                strips.append((k, row, size, image, at, strip))
                row += strip
                at += strip
    return strips


def small_forward_kernel(count, steps, groups, *refs):
    sources, wide_in, (log_ref, heat_ref), sends, (usage_ref, scalar_ref), wide_out, held, rest = (
        take(refs, 9, 1, 2, len(steps), 2, 1, 9, len(refs))
    )
    (sems, feat_scr), shared, (l_scr, noise_scr) = take(rest, 2, 3, 2)
    copies = [
        pltpu.make_async_copy(there, here, sems.at[i])
        for i, (there, here) in enumerate(zip([*sources, *wide_in], [*held, *wide_out]))
    ]
    for copy in copies:
        copy.start()
    params, orders, feats, noises = (*held[0:3], scalar_ref), held[3:5], held[5:7], held[7:9]
    set_scalars(log_ref, heat_ref, scalar_ref)
    for copy in copies[0:7]:
        copy.wait()
    prepare(params, *shared, backward=False)
    strips = places_of(orders, [f.shape for f in feats], groups, steps, count)
    for _, _, size, image, at, strip in strips:
        feat_scr[at : at + strip] = feats[size][image]
    forward_products(params, shared, feat_scr[...], l_scr)
    for copy in copies[7:9]:
        copy.wait()
    usage = jnp.zeros(usage_ref.shape, F32)
    part = sends[0].shape[0]
    if all(noise.shape[1] % 8 == 0 for noise in noises):
        for k, row, size, image, at, strip in strips:
            rows = pl.ds(at, strip)
            target = sends[k].at[pl.ds(row, strip)]
            usage = forward_rows(params, l_scr.at[rows], noises[size].at[image], target, usage)
    else:
        for _, _, size, image, at, strip in strips:
            noise_scr[at : at + strip] = noises[size][image]
        for k, send in enumerate(sends):
            rows = pl.ds(k * part, part)
            usage = forward_rows(params, l_scr.at[rows], noise_scr.at[rows], send, usage)
    usage_ref[...] = usage
    copies[9].wait()


def small_forward(count, steps, orders, feats, noises, params):
    dim, codes = params[2].shape
    width = feats[0].shape[2]
    groups = tuple(f.shape[0] // count for f in feats)
    part = sum(g * f.shape[1] for g, f in zip(groups, feats))
    rows = part * len(steps)
    arrays = [*params[0:3], *orders[0:2], *feats, *noises]
    return pl.pallas_call(
        functools.partial(small_forward_kernel, count, steps, groups),
        out_shape=[jax.ShapeDtypeStruct((part, codes), F32)] * len(steps)
        + [
            jax.ShapeDtypeStruct((8, codes), F32),
            jax.ShapeDtypeStruct((8, 128), F32),
            jax.ShapeDtypeStruct(orders[2].shape, jnp.int32),
        ],
        in_specs=[HBM] * 10 + [SMEM] * 2,
        out_specs=[VMEM] * (len(steps) + 3),
        scratch_shapes=[
            (pltpu.SMEM if 3 <= i < 5 else pltpu.VMEM)(a.shape, a.dtype)
            for i, a in enumerate(arrays)
        ]
        + [pltpu.SemaphoreType.DMA((10,)), pltpu.VMEM((rows, width), F32)]
        + shared_scratch(dim, codes, width)
        + [pltpu.VMEM((rows, codes), F32)] * 2,
        compiler_params=settings(),
        cost_estimate=cost(rows, width, dim, codes, 4),
        name="small_forward",
    )(*in_hbm([*arrays, orders[2]]), *params[3:5])


def small_backward_kernel(count, steps, devices, groups, *refs):
    orders, feats, cots, parts, params, (acc_in, *usages), grads, shards, rest = take(
        refs, 2, 2, 2, count, 4, 3, 2, devices, len(refs)
    )
    acc_ref, sum_scr, feat_scr, cot_scr, code_scr = rest[0:5]
    scr = rest[5:]
    strips = places_of(orders, [f.shape for f in feats], groups, steps, count)
    for _, _, size, image, at, strip in strips:
        feat_scr[at : at + strip] = feats[size][image]
        cot_scr[at : at + strip] = cots[size][image]
    part = parts[0].shape[0]
    for step in range(count):
        code_scr[step * part : (step + 1) * part] = parts[step][...]
    shared, tile_scr = take(scr, 3, 6)
    prepare(params, *shared)
    acc_ref[...] = acc_in[...]
    state = products(params, shared, tile_scr, feat_scr[...], cot_scr[...].T, False)
    backward_rows(tile_scr, code_scr)
    feat_scr[...] = gradients(params, shared, tile_scr, state, acc_ref)
    acc_ref[136:144] += usages[0][...] + usages[1][...]
    lay_out(params, acc_ref, sum_scr, shards)
    for _, _, size, image, at, strip in strips:
        grads[size][image] = feat_scr[at : at + strip]


def small_backward(count, steps, devices, orders, feats, cots, parts, params, acc, usages):
    dim, codes = params[2].shape
    width = feats[0].shape[2]
    groups = tuple(f.shape[0] // count for f in feats)
    rows = parts[0].shape[0] * count
    return pl.pallas_call(
        functools.partial(small_backward_kernel, count, steps, devices, groups),
        out_shape=[pltpu.HBM(f.shape, F32) for f in feats]
        + [jax.ShapeDtypeStruct((64 // devices, LANES), F32)] * devices,
        in_specs=[SMEM] * 2 + [VMEM] * (11 + count),
        out_specs=[VMEM] * (2 + devices),
        scratch_shapes=[
            pltpu.VMEM(acc.shape, F32),
            pltpu.VMEM((64, LANES), F32),
            pltpu.VMEM((rows, width), F32),
            pltpu.VMEM((rows, dim), F32),
            pltpu.VMEM((rows, codes), F32),
        ]
        + shared_scratch(dim, codes, width)
        + tile_scratch(rows, codes),
        compiler_params=settings(),
        cost_estimate=cost(rows, width, dim, codes, 6),
        name="small_backward",
    )(
        *orders,
        *in_hbm([*feats, *cots]),
        *parts,
        *in_hbm(params[0:3]),
        params[3],
        acc,
        *usages,
    )


def wide_forward_kernel(lanes, joined, relay, more, *refs):
    n = len(lanes)
    arrays = 1 if joined else sum(len(lane.runs) for lane in lanes) + (2 if relay else 0)
    _, feats, noises, params, usage_in, behind, sends, rest = take(
        refs, 1, n, n, 4, 1, 1 if more else 0, arrays, len(refs)
    )
    (usage_ref,), code_scrs, shared, l_scrs = take(rest, 1, n, 3, n)
    step = pl.program_id(0)

    @pl.when(step == 0)
    def _():
        prepare(params, *shared, backward=False)
        usage_ref[...] = usage_in[0][...]

    if joined:
        strip = code_scrs[0].shape[0]
        targets = [sends[0].at[pl.ds(i * strip, strip)] for i in range(n)]
    elif relay:
        strip = code_scrs[0].shape[0]
        targets = [*sends[0 : n - 1], sends[n + 1]]
    else:
        targets = code_targets(lanes, sends, code_scrs)
    for feat_ref, l_scr in zip(feats, l_scrs):
        forward_products(params, shared, feat_ref[...], l_scr)
    usage = usage_ref[...]
    for l_scr, noise_ref, target in zip(l_scrs, noises, targets):
        usage = forward_rows(params, l_scr, noise_ref, target, usage)
    usage_ref[...] = usage
    if relay:
        half = strip // 2
        sends[n - 1][...] = sends[n + 1][half:strip]
        sends[n][...] = sends[n + 1][0:half]
    if more:
        sends[0][n * strip :] = behind[0][...]
    elif not joined:
        keep_codes(step, lanes, sends, code_scrs)


def wide_forward(count, lanes, joined, order, feat, noise, params, usage, tenths, relay=False, more=None):
    dim, codes = params[2].shape
    images, strip, width = feat.shape
    n, steps = len(lanes), lanes[0].total()
    if joined:
        sizes = [n * strip + (0 if more is None else more.shape[0])]
    elif relay:
        sizes = [*[strip] * (n - 1), strip // 2, strip // 2, strip]
    else:
        sizes = [strip * run[2] for lane in lanes for run in lane.runs]
    if joined or relay:
        blocks = [fixed((size, codes)) for size in sizes]
    else:
        blocks = [block for lane in lanes for block in lane.blocks((strip, codes))]
    return pl.pallas_call(
        functools.partial(wide_forward_kernel, lanes, joined, relay, more is not None),
        grid_spec=pltpu.PrefetchScalarGridSpec(
            num_scalar_prefetch=1,
            grid=(steps,),
            in_specs=[lane.image((strip, width), count) for lane in lanes]
            + [lane.image((strip, codes), count) for lane in lanes]
            + [fixed(p.shape) for p in params]
            + [fixed(usage.shape)]
            + ([] if more is None else [fixed(more.shape)]),
            out_specs=blocks + [fixed(usage.shape)],
            scratch_shapes=[pltpu.VMEM((strip, codes), F32)] * n
            + shared_scratch(dim, codes, width)
            + [pltpu.VMEM((strip, codes), F32)] * n,
        ),
        out_shape=[jax.ShapeDtypeStruct((size, codes), F32) for size in sizes]
        + [jax.ShapeDtypeStruct(usage.shape, F32)],
        input_output_aliases={5 + 2 * n: len(sizes)},
        compiler_params=settings(),
        cost_estimate=cost(n * steps * strip, width, dim, codes, tenths),
        name="wide_forward",
    )(
        order,
        *in_hbm([feat] * n + [noise] * n + [*params[0:3]]),
        params[3],
        usage,
        *([] if more is None else [more]),
    )


def wide_both_kernel(lanes, count, *refs):
    n = len(lanes)
    arrays = sum(len(lane.runs) for lane in lanes)
    order, feats, noises, cots, params, sends, rest = take(
        refs, 1, n, n, n, 4, arrays, len(refs)
    )
    (grad_out, acc_ref), code_scrs, (grad_scr, sems), shared, rest = take(
        rest, 2, n, 2, 3, 6 * n
    )
    scrs = take(rest, *[6] * n)
    grads = Gradients(grad_out, grad_scr, sems)
    step, steps = pl.program_id(0), lanes[0].total()

    @pl.when(step == 0)
    def _():
        prepare(params, *shared)
        acc_ref[...] = jnp.zeros(acc_ref.shape, F32)

    grads.ready(step, n)
    targets = code_targets(lanes, sends, code_scrs)
    states = [
        products(params, shared, scr, feat_ref[...], cot_ref[...], True)
        for scr, feat_ref, cot_ref in zip(scrs, feats, cots)
    ]
    usage = acc_ref[136:144]
    for scr, noise_ref, target in zip(scrs, noises, targets):
        usage = both_rows(params, scr, noise_ref, target, usage)
    acc_ref[136:144] = usage
    values = [
        gradients(params, shared, scr, state, acc_ref) for scr, state in zip(scrs, states)
    ]
    grads.store(step, values, [lane.index(step, order[0], count) for lane in lanes])
    keep_codes(step, lanes, sends, code_scrs)
    grads.end(step, n, steps)


def wide_both(count, lanes, order, feat, noise, cot, params):
    dim, codes = params[2].shape
    images, strip, width = feat.shape
    n, steps = len(lanes), lanes[0].total()
    acc_shape = (ACC_ROWS, codes)
    sizes = [run[2] for lane in lanes for run in lane.runs]
    return pl.pallas_call(
        functools.partial(wide_both_kernel, lanes, count),
        grid_spec=pltpu.PrefetchScalarGridSpec(
            num_scalar_prefetch=1,
            grid=(steps,),
            in_specs=[lane.image((strip, width), count) for lane in lanes]
            + [lane.image((strip, codes), count) for lane in lanes]
            + [lane.image((dim, strip), count) for lane in lanes]
            + [fixed(p.shape) for p in params],
            out_specs=[block for lane in lanes for block in lane.blocks((strip, codes))]
            + [HBM, fixed(acc_shape)],
            scratch_shapes=[pltpu.VMEM((strip, codes), F32)] * n
            + gradient_scratch(n, strip, width)
            + shared_scratch(dim, codes, width)
            + tile_scratch(strip, codes) * n,
        ),
        out_shape=[jax.ShapeDtypeStruct((strip * slots, codes), F32) for slots in sizes]
        + [pltpu.HBM(feat.shape, F32), jax.ShapeDtypeStruct(acc_shape, F32)],
        compiler_params=settings(),
        cost_estimate=cost(n * steps * strip, width, dim, codes, 10),
        name="wide_both",
    )(order, *in_hbm([feat] * n + [noise] * n + [cot] * n + [*params[0:3]]), params[3])


def wide_backward_kernel(lanes, count, *refs):
    n = len(lanes)
    arrays = sum(len(lane.runs) for lane in lanes)
    order, feats, cots, parts, params, (acc_in, _), rest = take(
        refs, 1, n, n, arrays, 4, 2, len(refs)
    )
    (grad_out, acc_ref), code_scrs, (grad_scr, sems), shared, rest = take(
        rest, 2, n, 2, 3, 6 * n
    )
    scrs = take(rest, *[6] * n)
    grads = Gradients(grad_out, grad_scr, sems)
    step, steps = pl.program_id(0), lanes[0].total()

    @pl.when(step == 0)
    def _():
        prepare(params, *shared)
        acc_ref[...] = acc_in[...]

    grads.ready(step, n)
    for lane, refs_of, code_scr in zip(lanes, by_lane(parts, lanes), code_scrs):
        if len(lane.runs) > 1:

            def fetch(i, refs_of=refs_of, code_scr=code_scr):
                code_scr[...] = refs_of[i][...]

            lane.each(step, fetch)
    states = [
        products(params, shared, scr, feat_ref[...], cot_ref[...], False)
        for scr, feat_ref, cot_ref in zip(scrs, feats, cots)
    ]
    for scr, code_ref in zip(scrs, code_targets(lanes, parts, code_scrs)):
        backward_rows(scr, code_ref)
    values = [
        gradients(params, shared, scr, state, acc_ref) for scr, state in zip(scrs, states)
    ]
    grads.store(step, values, [lane.index(step, order[0], count) for lane in lanes])
    grads.end(step, n, steps)


def wide_backward(count, lanes, parts, order, feat, cot, params, acc, grad):
    dim, codes = params[2].shape
    images, strip, width = feat.shape
    n, steps = len(lanes), lanes[0].total()
    return pl.pallas_call(
        functools.partial(wide_backward_kernel, lanes, count),
        grid_spec=pltpu.PrefetchScalarGridSpec(
            num_scalar_prefetch=1,
            grid=(steps,),
            in_specs=[lane.image((strip, width), count) for lane in lanes]
            + [lane.image((dim, strip), count) for lane in lanes]
            + [block for lane in lanes for block in lane.blocks((strip, codes))]
            + [fixed(p.shape) for p in params]
            + [fixed(acc.shape), HBM],
            out_specs=[HBM, fixed(acc.shape)],
            scratch_shapes=[pltpu.VMEM((strip, codes), F32)] * n
            + gradient_scratch(n, strip, width)
            + shared_scratch(dim, codes, width)
            + tile_scratch(strip, codes) * n,
        ),
        out_shape=[pltpu.HBM(feat.shape, F32), jax.ShapeDtypeStruct(acc.shape, F32)],
        input_output_aliases={5 + 2 * n + len(parts): 1, 6 + 2 * n + len(parts): 0},
        compiler_params=settings(),
        cost_estimate=cost(n * steps * strip, width, dim, codes, 6),
        name="wide_backward",
    )(
        order,
        *in_hbm([feat] * n + [cot] * n),
        *parts,
        *in_hbm(params[0:3]),
        params[3],
        acc,
        *in_hbm([grad]),
    )


def shard_at(index, parts):
    height = 64 // parts
    return pl.ds(pl.multiple_of(index * height, height), height)


def lay_out(params, acc_ref, sum_scr, shards):
    weight_ref, bias_ref, book_ref, scalar_ref = params
    codes = book_ref.shape[1]
    width = weight_ref.shape[1]
    devices = len(shards)
    me = lax.rem(lax.axis_index("dp"), devices)
    precision, _, factor = scalars(scalar_ref)
    book = book_ref[...]
    column = acc_ref[128:129]
    moment = acc_ref[64:128] * (1.0 / precision)
    book_sum = acc_ref[0:64] * (1.0 / factor) + 2.0 * (column * book - moment)
    slope = jnp.sum(
        jnp.sum(book * book, axis=0, keepdims=True) * column, axis=1, keepdims=True
    ) - 2.0 * jnp.sum(jnp.sum(book * moment, axis=0, keepdims=True), axis=1, keepdims=True)
    slope = slope + acc_ref[208:209, 0:1] / (-0.5 * precision)
    usage = jnp.sum(acc_ref[136:144], axis=0, keepdims=True)
    dim = book_ref.shape[0]
    eye = lax.broadcasted_iota(jnp.int32, (dim, dim), 0) == lax.broadcasted_iota(
        jnp.int32, (dim, dim), 1
    )
    bias = acc_ref[144:208, width : width + dim]
    bias = jnp.sum(jnp.where(eye, bias, 0.0), axis=0, keepdims=True)
    rest = codes + width
    sum_scr[:, 0:codes] = book_sum
    sum_scr[:, codes:rest] = acc_ref[144:208, 0:width]
    sum_scr[:, rest : rest + 128] = jnp.broadcast_to(slope, (64, 128))
    rows = codes // 128
    for i in range(rows):
        sum_scr[i : i + 1, rest : rest + 128] = usage[:, i * 128 : (i + 1) * 128]
    sum_scr[rows : rows + 1, rest : rest + dim] = bias
    for i in range(devices):
        shards[i][...] = sum_scr[shard_at(partner(me, i, devices), devices)]


def own_kernel(n, count, *refs):
    order, feats, noises, cots, params, (acc_in, _), rest = take(
        refs, 1, n, n, n, 4, 2, len(refs)
    )
    (code_ref, grad_out, acc_ref), (grad_scr, sems), shared, rest = take(rest, 3, 2, 3, 6 * n)
    scrs = take(rest, *[6] * n)
    grads = Gradients(grad_out, grad_scr, sems)
    step = pl.program_id(0)

    @pl.when(step == 0)
    def _():
        prepare(params, *shared)
        acc_ref[...] = acc_in[...]

    grads.ready(step, n)
    states = [
        products(params, shared, scr, feat_ref[...], cot_ref[...], True)
        for scr, feat_ref, cot_ref in zip(scrs, feats, cots)
    ]
    usage = acc_ref[136:144]
    for i, (scr, noise_ref) in enumerate(zip(scrs, noises)):
        usage = both_rows(params, scr, noise_ref, code_ref.at[i], usage)
    acc_ref[136:144] = usage
    values = [
        gradients(params, shared, scr, state, acc_ref) for scr, state in zip(scrs, states)
    ]
    grads.store(step, values, [own_image(step, i, n, order[0], count) for i in range(n)])
    grads.end(step, n, pl.num_programs(0))


def own_image(step, lane, n, order_ref, count):
    share = order_ref.shape[1] // count
    return order_ref[0, lax.axis_index("space") * share + step * n + lane]


def run_own(count, order, feat, noise, cot, params, acc, grad):
    dim, codes = params[2].shape
    images, strip, width = feat.shape
    share = images // count
    n = 2 if share % 2 == 0 else 1

    def image(lane, shape):
        return pl.BlockSpec(
            (None, *shape), lambda i, order_ref: (own_image(i, lane, n, order_ref, count), 0, 0)
        )

    return pl.pallas_call(
        functools.partial(own_kernel, n, count),
        grid_spec=pltpu.PrefetchScalarGridSpec(
            num_scalar_prefetch=1,
            grid=(share // n,),
            in_specs=[image(lane, (strip, width)) for lane in range(n)]
            + [image(lane, (strip, codes)) for lane in range(n)]
            + [image(lane, (dim, strip)) for lane in range(n)]
            + [fixed(p.shape) for p in params]
            + [fixed(acc.shape), HBM],
            out_specs=[
                pl.BlockSpec(
                    (n, strip, codes),
                    lambda i, _: (i, lax.axis_index("space"), 0),
                ),
                HBM,
                fixed(acc.shape),
            ],
            scratch_shapes=gradient_scratch(n, strip, width)
            + shared_scratch(dim, codes, width)
            + tile_scratch(strip, codes) * n,
        ),
        out_shape=[
            pltpu.HBM((share, strip * count, codes), F32),
            pltpu.HBM(feat.shape, F32),
            jax.ShapeDtypeStruct(acc.shape, F32),
        ],
        input_output_aliases={5 + 3 * n: 2, 6 + 3 * n: 1},
        compiler_params=settings(),
        cost_estimate=cost(share * strip, width, dim, codes, 10),
        name="own_images",
    )(
        order,
        *in_hbm([feat] * n + [noise] * n + [cot] * n + [*params[0:3]]),
        params[3],
        acc,
        *in_hbm([grad]),
    )


def place_kernel(count, strip, moves, arrays, *refs):
    parts = refs[0:arrays]
    out_ref, sem = refs[arrays + 1 : arrays + 3]
    me = lax.axis_index("space")
    copies = []
    for which, at, step, slot, offset, rows in moves:
        row = pl.multiple_of(source(me, step, count) * strip + offset, rows)
        copies.append(
            pltpu.make_async_copy(
                parts[which].at[pl.ds(at, rows)],
                out_ref.at[slot, pl.ds(row, rows)],
                sem.at[len(copies)],
            )
        )
    for copy in copies:
        copy.start()
    for copy in copies:
        copy.wait()


def moves_of(runs, strip):
    return [
        (k, j * strip, step, first + j, 0, strip)
        for k, (step, first, slots) in enumerate(runs)
        for j in range(slots)
    ]


def place_wide(count, moves, parts, whole):
    return pl.pallas_call(
        functools.partial(place_kernel, count, whole.shape[1] // count, moves, len(parts)),
        out_shape=pltpu.HBM(whole.shape, F32),
        in_specs=[VMEM] * len(parts) + [HBM],
        out_specs=HBM,
        scratch_shapes=[pltpu.SemaphoreType.DMA((len(moves),))],
        input_output_aliases={len(parts): 0},
        compiler_params=settings(VMEM_LIMIT // 2),
        cost_estimate=pl.CostEstimate(
            flops=0, bytes_accessed=2 * sum(p.size * 4 for p in parts), transcendentals=0
        ),
        name="place_wide",
    )(*[pltpu.with_memory_space_constraint(p, pltpu.VMEM) for p in parts], *in_hbm([whole]))


def join_kernel(count, steps, *refs):
    parts = refs[0:count]
    outs = refs[count:]
    me = lax.axis_index("space")
    for part, step in zip(parts, steps):
        here = source(me, step, count)
        base = 0
        for out in outs:
            for j in range(out.shape[0]):
                strip = out.shape[2]
                out[j, here] = part[base : base + strip]
                base += strip


def join_small(count, steps, parts, shapes):
    codes = parts[0].shape[1]
    return pl.pallas_call(
        functools.partial(join_kernel, count, steps),
        out_shape=[
            jax.ShapeDtypeStruct((images // count, count, strip, codes), F32)
            for images, strip, _ in shapes
        ],
        compiler_params=settings(VMEM_LIMIT // 2),
        name="join_small",
    )(*parts)


def tree(values):
    while len(values) > 1:
        values = [
            values[i] + values[i + 1] if i + 1 < len(values) else values[i]
            for i in range(0, len(values), 2)
        ]
    return values[0]


def sum_kernel(*refs):
    refs[-1][...] = tree([ref[...] for ref in refs[:-1]])


def add_all(parts):
    return pl.pallas_call(
        sum_kernel,
        out_shape=jax.ShapeDtypeStruct(parts[0].shape, F32),
        compiler_params=settings(VMEM_LIMIT // 2),
        name="add_parts",
    )(*parts)


def final_kernel(devices, pixels, *refs):
    shards = refs[0:devices]
    weight_ref, bias_ref, book_ref, log_ref, usage_ref = refs[devices : devices + 5]
    weight_out, bias_out, book_out, log_out, usage_out = refs[devices + 5 : devices + 10]
    sum_scr = refs[devices + 10]
    me = lax.rem(lax.axis_index("dp"), devices)
    for i in range(devices):
        sum_scr[shard_at(source(me, i, devices), devices)] = shards[i][...]
    dim, codes = book_ref.shape
    width = weight_ref.shape[1]
    scale = 0.5 * lax.rsqrt(jnp.full((8, 128), pixels, F32))[0:1, 0:1]
    book_out[...] = 0.5 * book_ref[...] + scale * sum_scr[:, 0:codes]
    rest = codes + width
    weight_out[...] = 0.5 * weight_ref[...] + scale * sum_scr[:, codes:rest]
    rows = codes // 128
    bias_out[...] = 0.5 * bias_ref[...] + scale * sum_scr[rows : rows + 1, rest : rest + dim]
    usage = jnp.concatenate(
        [sum_scr[i : i + 1, rest : rest + 128] for i in range(rows)], axis=1
    )
    usage_out[...] = 0.5 * usage_ref[...] + 0.5 * (codes / pixels) * usage
    log_out[...] = 0.5 * log_ref[...] + scale * sum_scr[rows + 1 : rows + 2, rest : rest + 1]


def finish(devices, pixels, shards, weight, bias, book, log, usage):
    outs = (weight.T, bias.reshape(1, -1), book.T, log.reshape(1, 1), usage.reshape(1, -1))
    outs = pl.pallas_call(
        functools.partial(final_kernel, devices, pixels),
        out_shape=[jax.ShapeDtypeStruct(out.shape, F32) for out in outs],
        scratch_shapes=[pltpu.VMEM((64, LANES), F32)],
        compiler_params=settings(VMEM_LIMIT // 2),
        name="new_averages",
    )(*shards, *outs)
    return outs[0].T, outs[1].reshape(-1), outs[2].T, outs[3].reshape(-1), outs[4].reshape(-1)


def exchange(value, bit, size, pairs):
    while bit < size:
        value = value + pairs(value, bit)
        bit = 2 * bit
    return value


def per_device(
    feat_small,
    feat_mid,
    feat_wide,
    noise_small,
    noise_mid,
    noise_wide,
    cot_small,
    cot_mid,
    cot_wide,
    order_small,
    order_mid,
    order_wide,
    weight,
    bias,
    book,
    log,
    heat,
    weight_mean,
    bias_mean,
    book_mean,
    log_mean,
    usage_mean,
):
    count = lax.axis_size("space")
    devices = lax.axis_size("dp")
    params = (weight.T, bias.reshape(1, -1), book.T, log, heat)
    feats = (feat_small, feat_mid, feat_wide)
    pixels = sum(f.shape[0] * f.shape[1] for f in feats) * count * devices
    share = feat_wide.shape[0] // count
    cot_wide = jnp.swapaxes(cot_wide, 1, 2)

    def send(values):
        return [lax.ppermute(v, "space", route(i, count)) for i, v in zip(turns, values)]

    def follow(codes, before, parts):
        here, codes[-1] = lax.optimization_barrier(([before[i] for i in parts], codes[-1]))
        for i, part in zip(parts, here):
            before[i] = part
        return send(codes)

    last = count - 1
    turns = list(range(1, count))
    orders = (order_small, order_mid, order_wide)
    noises = (noise_small, noise_mid)
    *small, usage, scalar, order_wide = small_forward(
        count, turns, orders, feats[0:2], noises, params
    )
    arrived = [send(small)]
    own_params = params
    params = (*params[0:3], scalar)
    near = min(4, devices)
    strip = feat_wide.shape[1]
    relay = count == 4 and devices % 2 == 0
    early = [(step, 0, 1) for step in turns]
    direct = [(step, 1, share - 1) for step in turns[:-1]]
    early_moves = moves_of(early, strip)
    late = [(last, 2, share - 2)] if relay else [(last, 1, share - 1)]
    late_moves = moves_of(late, strip)
    extra = [(last, 1, 1)] if relay else []
    lanes = [Lane([run]) for run in early + extra] if relay else split(early, 3)
    *early_codes, usage = wide_forward(
        count, lanes, False, order_wide, feat_wide, noise_wide, params, usage, 4, relay
    )
    known = early_codes
    rest = None
    if relay:
        *early_codes, rest, passed, whole_strip = early_codes
        known = [*early_codes, whole_strip]
        half = strip // 2
        early_moves = [*early_moves, (len(early), 0, last, 1, 0, half)]
        late_moves = [*late_moves, (0, (share - 2) * strip, last, 1, half, half)]
    ahead = [count - 2, *range(count - 2)]
    arrived.append(follow(list(early_codes), arrived[0], ahead))

    def beside(value, step):
        pairs = [
            (i * count + j, (i ^ 1) * count + k)
            for i in range(devices)
            for j, k in route(step, count)
        ]
        return lax.ppermute(value, ("dp", "space"), pairs)

    *codes, grad, acc = wide_both(
        count, split(direct, 2), order_wide, feat_wide, noise_wide, cot_wide, params
    )
    if relay:
        passed, usage = lax.optimization_barrier((beside(passed, turns[0]), usage))
    late_lanes = [Lane([(last, slot, 1)]) for slot in range(late[0][1], share)]
    late_codes, usage = wide_forward(
        count,
        late_lanes,
        True,
        order_wide,
        feat_wide,
        noise_wide,
        params,
        usage,
        1,
        more=rest,
    )
    if relay:
        passed = beside(passed, turns[1])
    arrived.append(follow([*codes, late_codes], arrived[1], [0]))
    arrived[1], acc = lax.optimization_barrier((arrived[1], acc))
    whole, grad, acc = run_own(
        count, order_wide, feat_wide, noise_wide, cot_wide, params, acc, grad
    )
    if relay:
        passed, acc = lax.optimization_barrier((passed, acc))
        arrived[1].append(passed)
    whole = place_wide(count, early_moves, arrived[1], whole)
    acc, own_params = lax.optimization_barrier((acc, own_params))
    own, own_usage, _, _ = small_forward(
        count, range(1), orders, feats[0:2], noises, own_params
    )
    small = [own, *small]
    codes_small, codes_mid = join_small(
        count, [0, *turns], [own] + arrived[0], [f.shape for f in feats[0:2]]
    )
    whole, codes_small, codes_mid, acc = lax.optimization_barrier(
        (whole, codes_small, codes_mid, acc)
    )
    grad, acc = wide_backward(
        count,
        split(early + extra + late, 2),
        [*known, late_codes],
        order_wide,
        feat_wide,
        cot_wide,
        params,
        acc,
        grad,
    )
    grad_small, grad_mid, *shards = small_backward(
        count,
        [0, *turns],
        near,
        orders[0:2],
        feats[0:2],
        (cot_small, cot_mid),
        small,
        params,
        acc,
        (usage, own_usage),
    )
    group = [
        [(i, i - i % near + partner(i % near, step, near)) for i in range(devices)]
        for step in range(near)
    ]
    parts = [lax.ppermute(shards[i], "dp", group[i]) for i in range(1, near)]
    mine = add_all([shards[0]] + parts)

    def along(value, offset):
        return lax.ppermute(value, "dp", [(i, i ^ offset) for i in range(devices)])

    def across(value, offset):
        turn = near if devices > near else 0
        pairs = [
            (i * count + j, (i ^ turn) * count + (j ^ offset))
            for i in range(devices)
            for j in range(count)
        ]
        return lax.ppermute(value, ("dp", "space"), pairs)

    mine = exchange(mine, near, devices, along)
    mine = exchange(mine, 1, count, across)
    shards = [mine] + [lax.ppermute(mine, "dp", group[i]) for i in range(1, near)]
    updated = finish(
        near, pixels, shards, weight_mean, bias_mean, book_mean, log_mean, usage_mean
    )
    moves = [moves_of([run], strip) for run in direct] + [late_moves]
    for move, part in zip(moves, arrived[2]):
        whole = place_wide(count, move, [part], whole)
    codes = whole.shape[2]
    return (
        codes_small.reshape(codes_small.shape[0], -1, codes),
        codes_mid.reshape(codes_mid.shape[0], -1, codes),
        whole,
        grad_small,
        grad_mid,
        grad,
        *updated,
    )


def solution(mesh):
    strips = P("dp", "space", None)
    placed = (strips,) * 9 + (P("dp", None),) * 3 + (P(),) * 10
    return jax.shard_map(
        per_device,
        mesh=mesh,
        in_specs=placed,
        out_specs=(P(("dp", "space"), None, None),) * 3 + (strips,) * 3 + (P(),) * 5,
        check_vma=False,
    )
```

```python
import functools

import jax
import jax.numpy as jnp
from jax import lax
from jax.experimental import pallas as pl
from jax.experimental.pallas import tpu as pltpu
from jax.sharding import PartitionSpec as P

F32 = jnp.float32
BF16 = jnp.bfloat16
VMEM_LIMIT = 24 * 1024 * 1024
ACC_ROWS = 64 + 64 + 8 + 8 + 64 + 8
LANES = 896


def partner(index, step, count):
    if count & (count - 1) == 0:
        return index ^ step
    return lax.rem(index + step, count)


def route(step, count):
    if count & (count - 1) == 0:
        return [(i, i ^ step) for i in range(count)]
    return [(i, (i + step) % count) for i in range(count)]


def source(index, step, count):
    if count & (count - 1) == 0:
        return index ^ step
    return lax.rem(index + (count - step), count)


def in_hbm(arrays):
    return [pltpu.with_memory_space_constraint(a, pltpu.HBM) for a in arrays]


def halves(x):
    high = x.astype(BF16)
    return high, (x - high.astype(F32)).astype(BF16)


def dot(left, right, left_dim=1, right_dim=0):
    return lax.dot_general(
        left, right, (((left_dim,), (right_dim,)), ((), ())), preferred_element_type=F32
    )


def set_scalars(log_ref, heat_ref, out_ref):
    precision = jnp.exp(jnp.full((8, 128), log_ref[0], F32))
    heat = jnp.full((8, 128), heat_ref[0], F32)
    row = lax.broadcasted_iota(jnp.int32, (8, 128), 0)
    factor = -0.5 * precision / heat
    out_ref[...] = jnp.where(row == 0, precision, jnp.where(row == 1, 1.0 / heat, factor))


def scalars(ref):
    return ref[0:1, 0:1], ref[1:2, 0:1], ref[2:3, 0:1]


def prepare(refs, book_scr, books_scr, weight_scr, backward=True):
    weight_ref, bias_ref, book_ref, scalar_ref = refs
    dim, codes = book_ref.shape
    precision, _, _ = scalars(scalar_ref)
    book = book_ref[...]
    high, low = halves(book)
    norm = -0.5 * precision * jnp.sum(book * book, axis=0, keepdims=True)
    n0 = norm.astype(BF16).astype(F32)
    n1 = (norm - n0).astype(BF16).astype(F32)
    n2 = norm - n0 - n1
    row = lax.broadcasted_iota(jnp.int32, (16, codes), 0)
    extra = jnp.where(
        row < 3,
        1.0,
        jnp.where(row == 3, n0, jnp.where(row == 4, n1, jnp.where(row == 5, n2, 0.0))),
    ).astype(BF16)
    book_scr[0:dim] = high
    book_scr[dim : 2 * dim] = low
    book_scr[2 * dim : 3 * dim] = high
    book_scr[3 * dim : 3 * dim + 16] = extra
    if backward:
        books_scr[0:dim] = high
        books_scr[dim : 2 * dim] = low
        books_scr[2 * dim : 2 * dim + 16] = jnp.ones((16, codes), BF16)
    high, low = halves(weight_ref[...])
    weight_scr[0:dim] = high
    weight_scr[dim : 2 * dim] = low
    weight_scr[2 * dim : 3 * dim] = high


def latents(refs, shared, feat):
    weight_ref, bias_ref, book_ref, scalar_ref = refs
    weight_scr = shared[2]
    dim = book_ref.shape[0]
    precision, _, _ = scalars(scalar_ref)
    eye = lax.broadcasted_iota(jnp.int32, (dim, dim), 0) == lax.broadcasted_iota(
        jnp.int32, (dim, dim), 1
    )
    bias = jnp.sum(jnp.where(eye, bias_ref[...], 0.0), axis=1, keepdims=True)
    fh, fl = halves(feat)
    both = weight_scr[0 : 2 * dim]
    z2 = dot(both, fh, 1, 1) + dot(both, fl, 1, 1)
    z = z2[0:dim] + z2[dim : 2 * dim] + bias
    square = -0.5 * precision * jnp.sum(z * z, axis=0, keepdims=True)
    return fh, fl, z, square


def logit_rows(zh, zl, square):
    rows = zh.shape[1]
    s0 = square.astype(BF16).astype(F32)
    s1 = (square - s0).astype(BF16).astype(F32)
    s2 = square - s0 - s1
    row = lax.broadcasted_iota(jnp.int32, (16, rows), 0)
    extra = jnp.where(
        row == 0,
        s0,
        jnp.where(row == 1, s1, jnp.where(row == 2, s2, jnp.where(row < 6, 1.0, 0.0))),
    ).astype(BF16)
    return jnp.concatenate([zh, zh, zl, extra], axis=0)


def cot_rows(ch, cl):
    return jnp.concatenate([ch, ch, cl, jnp.zeros((16, ch.shape[1]), BF16)], axis=0)


def over_rows(rows, body, carry):
    step = next(s for s in (32, 16, 8) if rows % s == 0)

    def at(i, carry):
        return body(pl.ds(pl.multiple_of(i * step, step), step), carry)

    return lax.fori_loop(0, rows // step, at, carry, unroll=True)


def folded(x):
    return jnp.sum(x.reshape(x.shape[0] // 8, 8, x.shape[1]), axis=0)


def probabilities(logits):
    top = jnp.max(logits, axis=1, keepdims=True)
    e = jnp.exp(logits - top)
    return e * (1.0 / jnp.sum(e, axis=1, keepdims=True))


def forward_products(refs, shared, feat, l_scr):
    precision, _, _ = scalars(refs[3])
    _, _, z, square = latents(refs, shared, feat)
    zh, zl = halves(precision * z)
    l_scr[0 : feat.shape[0]] = dot(logit_rows(zh, zl, square), shared[0][...], 0, 0)


def forward_rows(refs, l_scr, noise_ref, code_ref, usage):
    _, cold, _ = scalars(refs[3])

    def body(at, usage):
        logits = l_scr[at]
        code_ref[at] = probabilities((logits + noise_ref[at]) * cold)
        return usage + folded(probabilities(logits))

    return over_rows(code_ref.shape[0], body, usage)


def products(refs, shared, scr, feat, cot, forward):
    l_scr, g_scr = scr[0:2]
    rows = feat.shape[0]
    precision, _, factor = scalars(refs[3])
    fh, fl, z, square = latents(refs, shared, feat)
    zh, zl = halves(precision * z)
    ch, cl = halves(factor * cot)
    if forward:
        left = jnp.concatenate([logit_rows(zh, zl, square), cot_rows(ch, cl)], axis=1)
        p = dot(left, shared[0][...], 0, 0)
        l_scr[0:rows] = p[0:rows]
        g_scr[0:rows] = p[rows : 2 * rows]
    else:
        g_scr[0:rows] = dot(cot_rows(ch, cl), shared[0][...], 0, 0)
    return fh, fl, z, square, zh, zl, ch, cl


def both_rows(refs, scr, noise_ref, code_ref, usage):
    l_scr, g_scr, wh_scr, wl_scr, gh_scr, gl_scr = scr
    _, cold, _ = scalars(refs[3])

    def body(at, usage):
        logits = l_scr[at]
        s = (logits + noise_ref[at]) * cold
        e = jnp.exp(s - jnp.max(s, axis=1, keepdims=True))
        gw = g_scr[at]
        scale = 1.0 / jnp.sum(e, axis=1, keepdims=True)
        inner = jnp.sum(e * gw, axis=1, keepdims=True) * scale
        w = e * scale
        code_ref[at] = w
        gd = w * (gw - inner)
        wh_scr[at], wl_scr[at] = halves(w)
        gh_scr[at], gl_scr[at] = halves(gd)
        return usage + folded(probabilities(logits))

    return over_rows(code_ref.shape[0], body, usage)


def backward_rows(scr, code_ref):
    _, g_scr, wh_scr, wl_scr, gh_scr, gl_scr = scr

    def body(at, carry):
        w = code_ref[at]
        gw = g_scr[at]
        gd = w * (gw - jnp.sum(w * gw, axis=1, keepdims=True))
        wh_scr[at], wl_scr[at] = halves(w)
        gh_scr[at], gl_scr[at] = halves(gd)
        return carry

    over_rows(code_ref.shape[0], body, 0)


def gradients(refs, shared, scr, state, acc_ref):
    _, books_scr, weight_scr = shared
    wh_scr, wl_scr, gh_scr, gl_scr = scr[2:6]
    fh, fl, z, square, zh, zl, ch, cl = state
    rows, feats = fh.shape
    dim, codes = refs[2].shape
    wh, wl = wh_scr[0:rows], wl_scr[0:rows]
    gh, gl = gh_scr[0:rows], gl_scr[0:rows]
    p = dot(jnp.concatenate([ch, cl], axis=0), wh)
    acc_ref[0:64] += p[0:dim] + p[dim : 2 * dim] + dot(ch, wl)
    left = jnp.concatenate([zh, zl, jnp.ones((16, rows), BF16)], axis=0)
    p = dot(left, gh) + dot(left, gl)
    acc_ref[64:128] += p[0:dim] + p[dim : 2 * dim]
    acc_ref[128:136] += p[2 * dim : 2 * dim + 8]
    p = dot(books_scr[...], gh, 1, 1) + dot(books_scr[...], gl, 1, 1)
    row_d = p[2 * dim : 2 * dim + 1]
    gz = 2.0 * (row_d * z - (p[0:dim] + p[dim : 2 * dim]))
    zh, zl = halves(gz)
    p = dot(jnp.concatenate([zh, zl], axis=0), fh)
    acc_ref[144:208, 0:feats] += p[0:dim] + p[dim : 2 * dim] + dot(zh, fl)
    acc_ref[144:208, feats : feats + 128] += jnp.broadcast_to(
        jnp.sum(gz, axis=1, keepdims=True), (dim, 128)
    )
    total = jnp.sum(square * row_d, axis=1, keepdims=True)
    acc_ref[208:216] += jnp.broadcast_to(total, (8, codes))
    return dot(jnp.concatenate([zh, zh, zl], axis=0), weight_scr[...], 0, 0)


def shared_scratch(dim, codes, feats):
    return [
        pltpu.VMEM((3 * dim + 16, codes), BF16),
        pltpu.VMEM((2 * dim + 16, codes), BF16),
        pltpu.VMEM((3 * dim, feats), BF16),
    ]


def tile_scratch(rows, codes):
    return [pltpu.VMEM((rows, codes), F32)] * 2 + [pltpu.VMEM((rows, codes), BF16)] * 4


def settings(limit=VMEM_LIMIT):
    return pltpu.CompilerParams(vmem_limit_bytes=limit)


def cost(rows, feats, dim, codes, tenths):
    return pl.CostEstimate(
        flops=rows * 24 * tenths * (5 * dim * codes + 3 * dim * feats) // 10,
        bytes_accessed=4 * rows * (2 * feats + 2 * codes + dim),
        transcendentals=2 * rows * codes,
    )


SMEM = pl.BlockSpec(memory_space=pltpu.SMEM)
VMEM = pl.BlockSpec(memory_space=pltpu.VMEM)
HBM = pl.BlockSpec(memory_space=pltpu.HBM)


def fixed(shape):
    return pl.BlockSpec(shape, lambda *_: (0,) * len(shape))


class Lane:
    def __init__(self, runs):
        self.runs = list(runs)
        self.bounds = [0]
        for _, _, slots in self.runs:
            self.bounds.append(self.bounds[-1] + slots)

    def total(self):
        return self.bounds[-1]

    def index(self, i, order_ref, count):
        share = order_ref.shape[1] // count
        step, slot = 0, 0
        for (whose, first, _), start in zip(self.runs, self.bounds):
            here = first + i - start
            step = whose if start == 0 else jnp.where(i >= start, whose, step)
            slot = here if start == 0 else jnp.where(i >= start, here, slot)
        there = partner(lax.axis_index("space"), step, count)
        return order_ref[0, there * share + slot]

    def image(self, shape, count):
        return pl.BlockSpec(
            (None, *shape), lambda i, order_ref: (self.index(i, order_ref, count), 0, 0)
        )

    def blocks(self, shape):
        return [
            pl.BlockSpec(
                shape,
                lambda i, _, start=start, last=slots - 1: (jnp.clip(i - start, 0, last), 0),
            )
            for (_, _, slots), start in zip(self.runs, self.bounds)
        ]

    def each(self, step, body):
        for i, (low, high) in enumerate(zip(self.bounds, self.bounds[1:])):
            pl.when((step >= low) & (step < high))(functools.partial(body, i))


def split(runs, ways):
    whole = Lane(runs)
    lanes, current = [], []
    for run in whole.runs:
        current.append(run)
        if Lane(current).total() * ways == whole.total():
            lanes.append(Lane(current))
            current = []
    return lanes if len(lanes) == ways and not current else [whole]


def take(refs, *sizes):
    groups, at = [], 0
    for size in sizes:
        groups.append(refs[at : at + size])
        at += size
    return groups


def by_lane(refs, lanes):
    return take(refs, *[len(lane.runs) for lane in lanes])


def keep_codes(step, lanes, sends, code_scrs):
    for lane, refs, code_scr in zip(lanes, by_lane(sends, lanes), code_scrs):
        if len(lane.runs) > 1:

            def keep(i, refs=refs, code_scr=code_scr):
                refs[i][...] = code_scr[...]

            lane.each(step, keep)


def code_targets(lanes, sends, code_scrs):
    return [
        refs[0] if len(lane.runs) == 1 else code_scr
        for lane, refs, code_scr in zip(lanes, by_lane(sends, lanes), code_scrs)
    ]


class Gradients:
    def __init__(self, out_ref, scr, sems):
        self.out_ref, self.scr, self.sems = out_ref, scr, sems

    def copy(self, lane, slot, image):
        return pltpu.make_async_copy(
            self.scr.at[lane, slot], self.out_ref.at[image], self.sems.at[lane, slot]
        )

    def ready(self, step, lanes):
        @pl.when(step >= 2)
        def _():
            for lane in range(lanes):
                self.copy(lane, lax.rem(step, 2), 0).wait()

    def store(self, step, values, images):
        slot = lax.rem(step, 2)
        for lane, (value, image) in enumerate(zip(values, images)):
            self.scr[lane, slot] = value
            self.copy(lane, slot, image).start()

    def end(self, step, lanes, steps):
        @pl.when(step == steps - 1)
        def _():
            for lane in range(lanes):
                for slot in range(min(2, steps)):
                    self.copy(lane, slot, 0).wait()


def gradient_scratch(lanes, strip, width):
    return [pltpu.VMEM((lanes, 2, strip, width), F32), pltpu.SemaphoreType.DMA((lanes, 2))]


def places_of(orders, shapes, groups, steps, count):
    me = lax.axis_index("space")
    strips = []
    at = 0
    for k, step in enumerate(steps):
        there = partner(me, step, count)
        row = 0
        for size in range(2):
            strip = shapes[size][1]
            for j in range(groups[size]):
                image = orders[size][0, there * groups[size] + j]
                strips.append((k, row, size, image, at, strip))
                row += strip
                at += strip
    return strips


def small_forward_kernel(count, steps, groups, *refs):
    sources, wide_in, (log_ref, heat_ref), sends, (usage_ref, scalar_ref), wide_out, held, rest = (
        take(refs, 9, 1, 2, len(steps), 2, 1, 9, len(refs))
    )
    (sems, feat_scr), shared, (l_scr, noise_scr) = take(rest, 2, 3, 2)
    copies = [
        pltpu.make_async_copy(there, here, sems.at[i])
        for i, (there, here) in enumerate(zip([*sources, *wide_in], [*held, *wide_out]))
    ]
    for copy in copies:
        copy.start()
    params, orders, feats, noises = (*held[0:3], scalar_ref), held[3:5], held[5:7], held[7:9]
    set_scalars(log_ref, heat_ref, scalar_ref)
    for copy in copies[0:7]:
        copy.wait()
    prepare(params, *shared, backward=False)
    strips = places_of(orders, [f.shape for f in feats], groups, steps, count)
    for _, _, size, image, at, strip in strips:
        feat_scr[at : at + strip] = feats[size][image]
    forward_products(params, shared, feat_scr[...], l_scr)
    for copy in copies[7:9]:
        copy.wait()
    usage = jnp.zeros(usage_ref.shape, F32)
    part = sends[0].shape[0]
    if all(noise.shape[1] % 8 == 0 for noise in noises):
        for k, row, size, image, at, strip in strips:
            rows = pl.ds(at, strip)
            target = sends[k].at[pl.ds(row, strip)]
            usage = forward_rows(params, l_scr.at[rows], noises[size].at[image], target, usage)
    else:
        for _, _, size, image, at, strip in strips:
            noise_scr[at : at + strip] = noises[size][image]
        for k, send in enumerate(sends):
            rows = pl.ds(k * part, part)
            usage = forward_rows(params, l_scr.at[rows], noise_scr.at[rows], send, usage)
    usage_ref[...] = usage
    copies[9].wait()


def small_forward(count, steps, orders, feats, noises, params):
    dim, codes = params[2].shape
    width = feats[0].shape[2]
    groups = tuple(f.shape[0] // count for f in feats)
    part = sum(g * f.shape[1] for g, f in zip(groups, feats))
    rows = part * len(steps)
    arrays = [*params[0:3], *orders[0:2], *feats, *noises]
    return pl.pallas_call(
        functools.partial(small_forward_kernel, count, steps, groups),
        out_shape=[jax.ShapeDtypeStruct((part, codes), F32)] * len(steps)
        + [
            jax.ShapeDtypeStruct((8, codes), F32),
            jax.ShapeDtypeStruct((8, 128), F32),
            jax.ShapeDtypeStruct(orders[2].shape, jnp.int32),
        ],
        in_specs=[HBM] * 10 + [SMEM] * 2,
        out_specs=[VMEM] * (len(steps) + 3),
        scratch_shapes=[
            (pltpu.SMEM if 3 <= i < 5 else pltpu.VMEM)(a.shape, a.dtype)
            for i, a in enumerate(arrays)
        ]
        + [pltpu.SemaphoreType.DMA((10,)), pltpu.VMEM((rows, width), F32)]
        + shared_scratch(dim, codes, width)
        + [pltpu.VMEM((rows, codes), F32)] * 2,
        compiler_params=settings(),
        cost_estimate=cost(rows, width, dim, codes, 4),
        name="small_forward",
    )(*in_hbm([*arrays, orders[2]]), *params[3:5])


def small_backward_kernel(count, steps, devices, groups, *refs):
    orders, feats, cots, parts, params, (acc_in, *usages), grads, shards, rest = take(
        refs, 2, 2, 2, count, 4, 3, 2, devices, len(refs)
    )
    acc_ref, sum_scr, feat_scr, cot_scr, code_scr = rest[0:5]
    scr = rest[5:]
    strips = places_of(orders, [f.shape for f in feats], groups, steps, count)
    for _, _, size, image, at, strip in strips:
        feat_scr[at : at + strip] = feats[size][image]
        cot_scr[at : at + strip] = cots[size][image]
    part = parts[0].shape[0]
    for step in range(count):
        code_scr[step * part : (step + 1) * part] = parts[step][...]
    shared, tile_scr = take(scr, 3, 6)
    prepare(params, *shared)
    acc_ref[...] = acc_in[...]
    state = products(params, shared, tile_scr, feat_scr[...], cot_scr[...].T, False)
    backward_rows(tile_scr, code_scr)
    feat_scr[...] = gradients(params, shared, tile_scr, state, acc_ref)
    acc_ref[136:144] += usages[0][...] + usages[1][...]
    lay_out(params, acc_ref, sum_scr, shards)
    for _, _, size, image, at, strip in strips:
        grads[size][image] = feat_scr[at : at + strip]


def small_backward(count, steps, devices, orders, feats, cots, parts, params, acc, usages):
    dim, codes = params[2].shape
    width = feats[0].shape[2]
    groups = tuple(f.shape[0] // count for f in feats)
    rows = parts[0].shape[0] * count
    return pl.pallas_call(
        functools.partial(small_backward_kernel, count, steps, devices, groups),
        out_shape=[pltpu.HBM(f.shape, F32) for f in feats]
        + [jax.ShapeDtypeStruct((64 // devices, LANES), F32)] * devices,
        in_specs=[SMEM] * 2 + [VMEM] * (11 + count),
        out_specs=[VMEM] * (2 + devices),
        scratch_shapes=[
            pltpu.VMEM(acc.shape, F32),
            pltpu.VMEM((64, LANES), F32),
            pltpu.VMEM((rows, width), F32),
            pltpu.VMEM((rows, dim), F32),
            pltpu.VMEM((rows, codes), F32),
        ]
        + shared_scratch(dim, codes, width)
        + tile_scratch(rows, codes),
        compiler_params=settings(),
        cost_estimate=cost(rows, width, dim, codes, 6),
        name="small_backward",
    )(
        *orders,
        *in_hbm([*feats, *cots]),
        *parts,
        *in_hbm(params[0:3]),
        params[3],
        acc,
        *usages,
    )


def wide_forward_kernel(lanes, joined, *refs):
    n = len(lanes)
    arrays = len(joined) if joined else sum(len(lane.runs) for lane in lanes)
    _, feats, noises, params, usage_in, sends, rest = take(
        refs, 1, n, n, 4, 1, arrays, len(refs)
    )
    (usage_ref,), code_scrs, shared, l_scrs = take(rest, 1, n, 3, n)
    step = pl.program_id(0)

    @pl.when(step == 0)
    def _():
        prepare(params, *shared, backward=False)
        usage_ref[...] = usage_in[0][...]

    if joined:
        strip = code_scrs[0].shape[0]
        targets = [
            send.at[pl.ds(i * strip, strip)] for send, k in zip(sends, joined) for i in range(k)
        ]
    else:
        targets = code_targets(lanes, sends, code_scrs)
    for feat_ref, l_scr in zip(feats, l_scrs):
        forward_products(params, shared, feat_ref[...], l_scr)
    usage = usage_ref[...]
    for l_scr, noise_ref, target in zip(l_scrs, noises, targets):
        usage = forward_rows(params, l_scr, noise_ref, target, usage)
    usage_ref[...] = usage
    if not joined:
        keep_codes(step, lanes, sends, code_scrs)


def wide_forward(count, lanes, joined, order, feat, noise, params, usage, tenths):
    dim, codes = params[2].shape
    images, strip, width = feat.shape
    n, steps = len(lanes), lanes[0].total()
    if joined:
        blocks = [fixed((k * strip, codes)) for k in joined]
        sizes = joined
    else:
        blocks = [block for lane in lanes for block in lane.blocks((strip, codes))]
        sizes = [run[2] for lane in lanes for run in lane.runs]
    return pl.pallas_call(
        functools.partial(wide_forward_kernel, lanes, joined),
        grid_spec=pltpu.PrefetchScalarGridSpec(
            num_scalar_prefetch=1,
            grid=(steps,),
            in_specs=[lane.image((strip, width), count) for lane in lanes]
            + [lane.image((strip, codes), count) for lane in lanes]
            + [fixed(p.shape) for p in params]
            + [fixed(usage.shape)],
            out_specs=blocks + [fixed(usage.shape)],
            scratch_shapes=[pltpu.VMEM((strip, codes), F32)] * n
            + shared_scratch(dim, codes, width)
            + [pltpu.VMEM((strip, codes), F32)] * n,
        ),
        out_shape=[jax.ShapeDtypeStruct((strip * slots, codes), F32) for slots in sizes]
        + [jax.ShapeDtypeStruct(usage.shape, F32)],
        input_output_aliases={5 + 2 * n: len(sizes)},
        compiler_params=settings(),
        cost_estimate=cost(n * steps * strip, width, dim, codes, tenths),
        name="wide_forward",
    )(order, *in_hbm([feat] * n + [noise] * n + [*params[0:3]]), params[3], usage)


def wide_both_kernel(lanes, count, *refs):
    n = len(lanes)
    arrays = sum(len(lane.runs) for lane in lanes)
    order, feats, noises, cots, params, sends, rest = take(
        refs, 1, n, n, n, 4, arrays, len(refs)
    )
    (grad_out, acc_ref), code_scrs, (grad_scr, sems), shared, rest = take(
        rest, 2, n, 2, 3, 6 * n
    )
    scrs = take(rest, *[6] * n)
    grads = Gradients(grad_out, grad_scr, sems)
    step, steps = pl.program_id(0), lanes[0].total()

    @pl.when(step == 0)
    def _():
        prepare(params, *shared)
        acc_ref[...] = jnp.zeros(acc_ref.shape, F32)

    grads.ready(step, n)
    targets = code_targets(lanes, sends, code_scrs)
    states = [
        products(params, shared, scr, feat_ref[...], cot_ref[...], True)
        for scr, feat_ref, cot_ref in zip(scrs, feats, cots)
    ]
    usage = acc_ref[136:144]
    for scr, noise_ref, target in zip(scrs, noises, targets):
        usage = both_rows(params, scr, noise_ref, target, usage)
    acc_ref[136:144] = usage
    values = [
        gradients(params, shared, scr, state, acc_ref) for scr, state in zip(scrs, states)
    ]
    grads.store(step, values, [lane.index(step, order[0], count) for lane in lanes])
    keep_codes(step, lanes, sends, code_scrs)
    grads.end(step, n, steps)


def wide_both(count, lanes, order, feat, noise, cot, params):
    dim, codes = params[2].shape
    images, strip, width = feat.shape
    n, steps = len(lanes), lanes[0].total()
    acc_shape = (ACC_ROWS, codes)
    sizes = [run[2] for lane in lanes for run in lane.runs]
    return pl.pallas_call(
        functools.partial(wide_both_kernel, lanes, count),
        grid_spec=pltpu.PrefetchScalarGridSpec(
            num_scalar_prefetch=1,
            grid=(steps,),
            in_specs=[lane.image((strip, width), count) for lane in lanes]
            + [lane.image((strip, codes), count) for lane in lanes]
            + [lane.image((dim, strip), count) for lane in lanes]
            + [fixed(p.shape) for p in params],
            out_specs=[block for lane in lanes for block in lane.blocks((strip, codes))]
            + [HBM, fixed(acc_shape)],
            scratch_shapes=[pltpu.VMEM((strip, codes), F32)] * n
            + gradient_scratch(n, strip, width)
            + shared_scratch(dim, codes, width)
            + tile_scratch(strip, codes) * n,
        ),
        out_shape=[jax.ShapeDtypeStruct((strip * slots, codes), F32) for slots in sizes]
        + [pltpu.HBM(feat.shape, F32), jax.ShapeDtypeStruct(acc_shape, F32)],
        compiler_params=settings(),
        cost_estimate=cost(n * steps * strip, width, dim, codes, 10),
        name="wide_both",
    )(order, *in_hbm([feat] * n + [noise] * n + [cot] * n + [*params[0:3]]), params[3])


def wide_backward_kernel(lanes, count, *refs):
    n = len(lanes)
    arrays = sum(len(lane.runs) for lane in lanes)
    order, feats, cots, parts, params, (acc_in, _), rest = take(
        refs, 1, n, n, arrays, 4, 2, len(refs)
    )
    (grad_out, acc_ref), code_scrs, (grad_scr, sems), shared, rest = take(
        rest, 2, n, 2, 3, 6 * n
    )
    scrs = take(rest, *[6] * n)
    grads = Gradients(grad_out, grad_scr, sems)
    step, steps = pl.program_id(0), lanes[0].total()

    @pl.when(step == 0)
    def _():
        prepare(params, *shared)
        acc_ref[...] = acc_in[...]

    grads.ready(step, n)
    for lane, refs_of, code_scr in zip(lanes, by_lane(parts, lanes), code_scrs):
        if len(lane.runs) > 1:

            def fetch(i, refs_of=refs_of, code_scr=code_scr):
                code_scr[...] = refs_of[i][...]

            lane.each(step, fetch)
    states = [
        products(params, shared, scr, feat_ref[...], cot_ref[...], False)
        for scr, feat_ref, cot_ref in zip(scrs, feats, cots)
    ]
    for scr, code_ref in zip(scrs, code_targets(lanes, parts, code_scrs)):
        backward_rows(scr, code_ref)
    values = [
        gradients(params, shared, scr, state, acc_ref) for scr, state in zip(scrs, states)
    ]
    grads.store(step, values, [lane.index(step, order[0], count) for lane in lanes])
    grads.end(step, n, steps)


def wide_backward(count, lanes, parts, order, feat, cot, params, acc, grad):
    dim, codes = params[2].shape
    images, strip, width = feat.shape
    n, steps = len(lanes), lanes[0].total()
    return pl.pallas_call(
        functools.partial(wide_backward_kernel, lanes, count),
        grid_spec=pltpu.PrefetchScalarGridSpec(
            num_scalar_prefetch=1,
            grid=(steps,),
            in_specs=[lane.image((strip, width), count) for lane in lanes]
            + [lane.image((dim, strip), count) for lane in lanes]
            + [block for lane in lanes for block in lane.blocks((strip, codes))]
            + [fixed(p.shape) for p in params]
            + [fixed(acc.shape), HBM],
            out_specs=[HBM, fixed(acc.shape)],
            scratch_shapes=[pltpu.VMEM((strip, codes), F32)] * n
            + gradient_scratch(n, strip, width)
            + shared_scratch(dim, codes, width)
            + tile_scratch(strip, codes) * n,
        ),
        out_shape=[pltpu.HBM(feat.shape, F32), jax.ShapeDtypeStruct(acc.shape, F32)],
        input_output_aliases={5 + 2 * n + len(parts): 1, 6 + 2 * n + len(parts): 0},
        compiler_params=settings(),
        cost_estimate=cost(n * steps * strip, width, dim, codes, 6),
        name="wide_backward",
    )(
        order,
        *in_hbm([feat] * n + [cot] * n),
        *parts,
        *in_hbm(params[0:3]),
        params[3],
        acc,
        *in_hbm([grad]),
    )


def shard_at(index, parts):
    height = 64 // parts
    return pl.ds(pl.multiple_of(index * height, height), height)


def lay_out(params, acc_ref, sum_scr, shards):
    weight_ref, bias_ref, book_ref, scalar_ref = params
    codes = book_ref.shape[1]
    width = weight_ref.shape[1]
    devices = len(shards)
    me = lax.rem(lax.axis_index("dp"), devices)
    precision, _, factor = scalars(scalar_ref)
    book = book_ref[...]
    column = acc_ref[128:129]
    moment = acc_ref[64:128] * (1.0 / precision)
    book_sum = acc_ref[0:64] * (1.0 / factor) + 2.0 * (column * book - moment)
    slope = jnp.sum(
        jnp.sum(book * book, axis=0, keepdims=True) * column, axis=1, keepdims=True
    ) - 2.0 * jnp.sum(jnp.sum(book * moment, axis=0, keepdims=True), axis=1, keepdims=True)
    slope = slope + acc_ref[208:209, 0:1] / (-0.5 * precision)
    usage = jnp.sum(acc_ref[136:144], axis=0, keepdims=True)
    dim = book_ref.shape[0]
    eye = lax.broadcasted_iota(jnp.int32, (dim, dim), 0) == lax.broadcasted_iota(
        jnp.int32, (dim, dim), 1
    )
    bias = acc_ref[144:208, width : width + dim]
    bias = jnp.sum(jnp.where(eye, bias, 0.0), axis=0, keepdims=True)
    rest = codes + width
    sum_scr[:, 0:codes] = book_sum
    sum_scr[:, codes:rest] = acc_ref[144:208, 0:width]
    sum_scr[:, rest : rest + 128] = jnp.broadcast_to(slope, (64, 128))
    rows = codes // 128
    for i in range(rows):
        sum_scr[i : i + 1, rest : rest + 128] = usage[:, i * 128 : (i + 1) * 128]
    sum_scr[rows : rows + 1, rest : rest + dim] = bias
    for i in range(devices):
        shards[i][...] = sum_scr[shard_at(partner(me, i, devices), devices)]


def own_kernel(n, count, *refs):
    order, feats, noises, cots, params, (acc_in, _), rest = take(
        refs, 1, n, n, n, 4, 2, len(refs)
    )
    (code_ref, grad_out, acc_ref), (grad_scr, sems), shared, rest = take(rest, 3, 2, 3, 6 * n)
    scrs = take(rest, *[6] * n)
    grads = Gradients(grad_out, grad_scr, sems)
    step = pl.program_id(0)

    @pl.when(step == 0)
    def _():
        prepare(params, *shared)
        acc_ref[...] = acc_in[...]

    grads.ready(step, n)
    states = [
        products(params, shared, scr, feat_ref[...], cot_ref[...], True)
        for scr, feat_ref, cot_ref in zip(scrs, feats, cots)
    ]
    usage = acc_ref[136:144]
    for i, (scr, noise_ref) in enumerate(zip(scrs, noises)):
        usage = both_rows(params, scr, noise_ref, code_ref.at[i], usage)
    acc_ref[136:144] = usage
    values = [
        gradients(params, shared, scr, state, acc_ref) for scr, state in zip(scrs, states)
    ]
    grads.store(step, values, [own_image(step, i, n, order[0], count) for i in range(n)])
    grads.end(step, n, pl.num_programs(0))


def own_image(step, lane, n, order_ref, count):
    share = order_ref.shape[1] // count
    return order_ref[0, lax.axis_index("space") * share + step * n + lane]


def run_own(count, order, feat, noise, cot, params, acc, grad):
    dim, codes = params[2].shape
    images, strip, width = feat.shape
    share = images // count
    n = 2 if share % 2 == 0 else 1

    def image(lane, shape):
        return pl.BlockSpec(
            (None, *shape), lambda i, order_ref: (own_image(i, lane, n, order_ref, count), 0, 0)
        )

    return pl.pallas_call(
        functools.partial(own_kernel, n, count),
        grid_spec=pltpu.PrefetchScalarGridSpec(
            num_scalar_prefetch=1,
            grid=(share // n,),
            in_specs=[image(lane, (strip, width)) for lane in range(n)]
            + [image(lane, (strip, codes)) for lane in range(n)]
            + [image(lane, (dim, strip)) for lane in range(n)]
            + [fixed(p.shape) for p in params]
            + [fixed(acc.shape), HBM],
            out_specs=[
                pl.BlockSpec(
                    (n, strip, codes),
                    lambda i, _: (i, lax.axis_index("space"), 0),
                ),
                HBM,
                fixed(acc.shape),
            ],
            scratch_shapes=gradient_scratch(n, strip, width)
            + shared_scratch(dim, codes, width)
            + tile_scratch(strip, codes) * n,
        ),
        out_shape=[
            pltpu.HBM((share, strip * count, codes), F32),
            pltpu.HBM(feat.shape, F32),
            jax.ShapeDtypeStruct(acc.shape, F32),
        ],
        input_output_aliases={5 + 3 * n: 2, 6 + 3 * n: 1},
        compiler_params=settings(),
        cost_estimate=cost(share * strip, width, dim, codes, 10),
        name="own_images",
    )(
        order,
        *in_hbm([feat] * n + [noise] * n + [cot] * n + [*params[0:3]]),
        params[3],
        acc,
        *in_hbm([grad]),
    )


def place_kernel(count, runs, *refs):
    parts = refs[0 : len(runs)]
    out_ref, sem = refs[len(runs) + 1 : len(runs) + 3]
    me = lax.axis_index("space")
    copies = []
    for part, (step, first, slots) in zip(parts, runs):
        strip = part.shape[0] // slots
        row = pl.multiple_of(source(me, step, count) * strip, strip)
        for j in range(slots):
            copies.append(
                pltpu.make_async_copy(
                    part.at[pl.ds(j * strip, strip)],
                    out_ref.at[first + j, pl.ds(row, strip)],
                    sem.at[len(copies)],
                )
            )
    for copy in copies:
        copy.start()
    for copy in copies:
        copy.wait()


def place_wide(count, runs, parts, whole):
    return pl.pallas_call(
        functools.partial(place_kernel, count, runs),
        out_shape=pltpu.HBM(whole.shape, F32),
        in_specs=[VMEM] * len(runs) + [HBM],
        out_specs=HBM,
        scratch_shapes=[pltpu.SemaphoreType.DMA((sum(r[2] for r in runs),))],
        input_output_aliases={len(runs): 0},
        compiler_params=settings(VMEM_LIMIT // 2),
        cost_estimate=pl.CostEstimate(
            flops=0, bytes_accessed=2 * sum(p.size * 4 for p in parts), transcendentals=0
        ),
        name="place_wide",
    )(*[pltpu.with_memory_space_constraint(p, pltpu.VMEM) for p in parts], *in_hbm([whole]))


def join_kernel(count, steps, *refs):
    parts = refs[0:count]
    outs = refs[count:]
    me = lax.axis_index("space")
    for part, step in zip(parts, steps):
        here = source(me, step, count)
        base = 0
        for out in outs:
            for j in range(out.shape[0]):
                strip = out.shape[2]
                out[j, here] = part[base : base + strip]
                base += strip


def join_small(count, steps, parts, shapes):
    codes = parts[0].shape[1]
    return pl.pallas_call(
        functools.partial(join_kernel, count, steps),
        out_shape=[
            jax.ShapeDtypeStruct((images // count, count, strip, codes), F32)
            for images, strip, _ in shapes
        ],
        compiler_params=settings(VMEM_LIMIT // 2),
        name="join_small",
    )(*parts)


def tree(values):
    while len(values) > 1:
        values = [
            values[i] + values[i + 1] if i + 1 < len(values) else values[i]
            for i in range(0, len(values), 2)
        ]
    return values[0]


def sum_kernel(*refs):
    refs[-1][...] = tree([ref[...] for ref in refs[:-1]])


def add_all(parts):
    return pl.pallas_call(
        sum_kernel,
        out_shape=jax.ShapeDtypeStruct(parts[0].shape, F32),
        compiler_params=settings(VMEM_LIMIT // 2),
        name="add_parts",
    )(*parts)


def final_kernel(devices, pixels, *refs):
    shards = refs[0:devices]
    weight_ref, bias_ref, book_ref, log_ref, usage_ref = refs[devices : devices + 5]
    weight_out, bias_out, book_out, log_out, usage_out = refs[devices + 5 : devices + 10]
    sum_scr = refs[devices + 10]
    me = lax.rem(lax.axis_index("dp"), devices)
    for i in range(devices):
        sum_scr[shard_at(source(me, i, devices), devices)] = shards[i][...]
    dim, codes = book_ref.shape
    width = weight_ref.shape[1]
    scale = 0.5 * lax.rsqrt(jnp.full((8, 128), pixels, F32))[0:1, 0:1]
    book_out[...] = 0.5 * book_ref[...] + scale * sum_scr[:, 0:codes]
    rest = codes + width
    weight_out[...] = 0.5 * weight_ref[...] + scale * sum_scr[:, codes:rest]
    rows = codes // 128
    bias_out[...] = 0.5 * bias_ref[...] + scale * sum_scr[rows : rows + 1, rest : rest + dim]
    usage = jnp.concatenate(
        [sum_scr[i : i + 1, rest : rest + 128] for i in range(rows)], axis=1
    )
    usage_out[...] = 0.5 * usage_ref[...] + 0.5 * (codes / pixels) * usage
    log_out[...] = 0.5 * log_ref[...] + scale * sum_scr[rows + 1 : rows + 2, rest : rest + 1]


def finish(devices, pixels, shards, weight, bias, book, log, usage):
    outs = (weight.T, bias.reshape(1, -1), book.T, log.reshape(1, 1), usage.reshape(1, -1))
    outs = pl.pallas_call(
        functools.partial(final_kernel, devices, pixels),
        out_shape=[jax.ShapeDtypeStruct(out.shape, F32) for out in outs],
        scratch_shapes=[pltpu.VMEM((64, LANES), F32)],
        compiler_params=settings(VMEM_LIMIT // 2),
        name="new_averages",
    )(*shards, *outs)
    return outs[0].T, outs[1].reshape(-1), outs[2].T, outs[3].reshape(-1), outs[4].reshape(-1)


def exchange(value, bit, size, pairs):
    while bit < size:
        value = value + pairs(value, bit)
        bit = 2 * bit
    return value


def per_device(
    feat_small,
    feat_mid,
    feat_wide,
    noise_small,
    noise_mid,
    noise_wide,
    cot_small,
    cot_mid,
    cot_wide,
    order_small,
    order_mid,
    order_wide,
    weight,
    bias,
    book,
    log,
    heat,
    weight_mean,
    bias_mean,
    book_mean,
    log_mean,
    usage_mean,
):
    count = lax.axis_size("space")
    devices = lax.axis_size("dp")
    params = (weight.T, bias.reshape(1, -1), book.T, log, heat)
    feats = (feat_small, feat_mid, feat_wide)
    pixels = sum(f.shape[0] * f.shape[1] for f in feats) * count * devices
    share = feat_wide.shape[0] // count
    cot_wide = jnp.swapaxes(cot_wide, 1, 2)

    def send(values):
        return [lax.ppermute(v, "space", route(i, count)) for i, v in zip(turns, values)]

    def follow(codes, before, parts):
        here, codes[-1] = lax.optimization_barrier(([before[i] for i in parts], codes[-1]))
        for i, part in zip(parts, here):
            before[i] = part
        return send(codes)

    last = count - 1
    turns = list(range(1, count))
    orders = (order_small, order_mid, order_wide)
    noises = (noise_small, noise_mid)
    *small, usage, scalar, order_wide = small_forward(
        count, turns, orders, feats[0:2], noises, params
    )
    arrived = [send(small)]
    own_params = params
    params = (*params[0:3], scalar)
    near = min(4, devices)
    early = [(step, 0, 1) for step in turns]
    direct = [(step, 1, share - 1) for step in turns[:-1]]
    late = [(last, 1, share - 2), (last, share - 1, 1)]
    *early_codes, usage = wide_forward(
        count, split(early, 3), [], order_wide, feat_wide, noise_wide, params, usage, 4
    )
    ahead = [count - 2, *range(count - 2)]
    arrived.append(follow(list(early_codes), arrived[0], ahead))
    *codes, grad, acc = wide_both(
        count, split(direct, 2), order_wide, feat_wide, noise_wide, cot_wide, params
    )
    late_lanes = [Lane([(last, slot, 1)]) for slot in range(1, share)]
    late_codes, end_codes, usage = wide_forward(
        count, late_lanes, [share - 2, 1], order_wide, feat_wide, noise_wide, params, usage, 1
    )
    arrived.append(follow([*codes, late_codes], arrived[1], [0]))
    arrived[1][-1], leaving = lax.optimization_barrier((arrived[1][-1], end_codes))
    arrived[2].append(lax.ppermute(leaving, "space", route(last, count)))
    arrived[1], acc = lax.optimization_barrier((arrived[1], acc))
    whole, grad, acc = run_own(
        count, order_wide, feat_wide, noise_wide, cot_wide, params, acc, grad
    )
    whole = place_wide(count, early, arrived[1], whole)
    acc, own_params = lax.optimization_barrier((acc, own_params))
    own, own_usage, _, _ = small_forward(
        count, range(1), orders, feats[0:2], noises, own_params
    )
    small = [own, *small]
    codes_small, codes_mid = join_small(
        count, [0, *turns], [own] + arrived[0], [f.shape for f in feats[0:2]]
    )
    whole, codes_small, codes_mid, acc = lax.optimization_barrier(
        (whole, codes_small, codes_mid, acc)
    )
    grad, acc = wide_backward(
        count,
        split(early + late, 2),
        [*early_codes, late_codes, end_codes],
        order_wide,
        feat_wide,
        cot_wide,
        params,
        acc,
        grad,
    )
    grad_small, grad_mid, *shards = small_backward(
        count,
        [0, *turns],
        near,
        orders[0:2],
        feats[0:2],
        (cot_small, cot_mid),
        small,
        params,
        acc,
        (usage, own_usage),
    )
    group = [
        [(i, i - i % near + partner(i % near, step, near)) for i in range(devices)]
        for step in range(near)
    ]
    parts = [lax.ppermute(shards[i], "dp", group[i]) for i in range(1, near)]
    mine = add_all([shards[0]] + parts)

    def along(value, offset):
        return lax.ppermute(value, "dp", [(i, i ^ offset) for i in range(devices)])

    def across(value, offset):
        turn = near if devices > near else 0
        pairs = [
            (i * count + j, (i ^ turn) * count + (j ^ offset))
            for i in range(devices)
            for j in range(count)
        ]
        return lax.ppermute(value, ("dp", "space"), pairs)

    mine = exchange(mine, near, devices, along)
    arrived[2][:-2], mine = lax.optimization_barrier((arrived[2][:-2], mine))
    mine = exchange(mine, 1, count, across)
    shards = [mine] + [lax.ppermute(mine, "dp", group[i]) for i in range(1, near)]
    updated = finish(
        near, pixels, shards, weight_mean, bias_mean, book_mean, log_mean, usage_mean
    )
    *before, final = zip(direct + late, arrived[2])
    for run, part in before:
        whole = place_wide(count, [run], [part], whole)
    whole, updated = lax.optimization_barrier((whole, updated))
    whole = place_wide(count, [final[0]], [final[1]], whole)
    codes = whole.shape[2]
    return (
        codes_small.reshape(codes_small.shape[0], -1, codes),
        codes_mid.reshape(codes_mid.shape[0], -1, codes),
        whole,
        grad_small,
        grad_mid,
        grad,
        *updated,
    )


def solution(mesh):
    strips = P("dp", "space", None)
    placed = (strips,) * 9 + (P("dp", None),) * 3 + (P(),) * 10
    return jax.shard_map(
        per_device,
        mesh=mesh,
        in_specs=placed,
        out_specs=(P(("dp", "space"), None, None),) * 3 + (strips,) * 3 + (P(),) * 5,
        check_vma=False,
    )
```

```python
import functools

import jax
import jax.numpy as jnp
from jax import lax
from jax.experimental import pallas as pl
from jax.experimental.pallas import tpu as pltpu
from jax.sharding import PartitionSpec as P

F32 = jnp.float32
BF16 = jnp.bfloat16
VMEM_LIMIT = 24 * 1024 * 1024
ACC_ROWS = 64 + 64 + 8 + 8 + 64 + 8
LANES = 896


def partner(index, step, count):
    if count & (count - 1) == 0:
        return index ^ step
    return lax.rem(index + step, count)


def route(step, count):
    if count & (count - 1) == 0:
        return [(i, i ^ step) for i in range(count)]
    return [(i, (i + step) % count) for i in range(count)]


def source(index, step, count):
    if count & (count - 1) == 0:
        return index ^ step
    return lax.rem(index + (count - step), count)


def in_hbm(arrays):
    return [pltpu.with_memory_space_constraint(a, pltpu.HBM) for a in arrays]


def halves(x):
    high = x.astype(BF16)
    return high, (x - high.astype(F32)).astype(BF16)


def dot(left, right, left_dim=1, right_dim=0):
    return lax.dot_general(
        left, right, (((left_dim,), (right_dim,)), ((), ())), preferred_element_type=F32
    )


def set_scalars(log_ref, heat_ref, out_ref):
    precision = jnp.exp(jnp.full((8, 128), log_ref[0], F32))
    heat = jnp.full((8, 128), heat_ref[0], F32)
    row = lax.broadcasted_iota(jnp.int32, (8, 128), 0)
    factor = -0.5 * precision / heat
    out_ref[...] = jnp.where(row == 0, precision, jnp.where(row == 1, 1.0 / heat, factor))


def scalars(ref):
    return ref[0:1, 0:1], ref[1:2, 0:1], ref[2:3, 0:1]


def prepare(refs, book_scr, books_scr, weight_scr, backward=True):
    weight_ref, bias_ref, book_ref, scalar_ref = refs
    dim, codes = book_ref.shape
    precision, _, _ = scalars(scalar_ref)
    book = book_ref[...]
    high, low = halves(book)
    norm = -0.5 * precision * jnp.sum(book * book, axis=0, keepdims=True)
    n0 = norm.astype(BF16).astype(F32)
    n1 = (norm - n0).astype(BF16).astype(F32)
    n2 = norm - n0 - n1
    row = lax.broadcasted_iota(jnp.int32, (16, codes), 0)
    extra = jnp.where(
        row < 3,
        1.0,
        jnp.where(row == 3, n0, jnp.where(row == 4, n1, jnp.where(row == 5, n2, 0.0))),
    ).astype(BF16)
    book_scr[0:dim] = high
    book_scr[dim : 2 * dim] = low
    book_scr[2 * dim : 3 * dim] = high
    book_scr[3 * dim : 3 * dim + 16] = extra
    if backward:
        books_scr[0:dim] = high
        books_scr[dim : 2 * dim] = low
        books_scr[2 * dim : 2 * dim + 16] = jnp.ones((16, codes), BF16)
    high, low = halves(weight_ref[...])
    weight_scr[0:dim] = high
    weight_scr[dim : 2 * dim] = low
    weight_scr[2 * dim : 3 * dim] = high


def latents(refs, shared, feat):
    weight_ref, bias_ref, book_ref, scalar_ref = refs
    weight_scr = shared[2]
    dim = book_ref.shape[0]
    precision, _, _ = scalars(scalar_ref)
    eye = lax.broadcasted_iota(jnp.int32, (dim, dim), 0) == lax.broadcasted_iota(
        jnp.int32, (dim, dim), 1
    )
    bias = jnp.sum(jnp.where(eye, bias_ref[...], 0.0), axis=1, keepdims=True)
    fh, fl = halves(feat)
    both = weight_scr[0 : 2 * dim]
    z2 = dot(both, fh, 1, 1) + dot(both, fl, 1, 1)
    z = z2[0:dim] + z2[dim : 2 * dim] + bias
    square = -0.5 * precision * jnp.sum(z * z, axis=0, keepdims=True)
    return fh, fl, z, square


def logit_rows(zh, zl, square):
    rows = zh.shape[1]
    s0 = square.astype(BF16).astype(F32)
    s1 = (square - s0).astype(BF16).astype(F32)
    s2 = square - s0 - s1
    row = lax.broadcasted_iota(jnp.int32, (16, rows), 0)
    extra = jnp.where(
        row == 0,
        s0,
        jnp.where(row == 1, s1, jnp.where(row == 2, s2, jnp.where(row < 6, 1.0, 0.0))),
    ).astype(BF16)
    return jnp.concatenate([zh, zh, zl, extra], axis=0)


def cot_rows(ch, cl):
    return jnp.concatenate([ch, ch, cl, jnp.zeros((16, ch.shape[1]), BF16)], axis=0)


def over_rows(rows, body, carry):
    step = next(s for s in (32, 16, 8) if rows % s == 0)

    def at(i, carry):
        return body(pl.ds(pl.multiple_of(i * step, step), step), carry)

    return lax.fori_loop(0, rows // step, at, carry, unroll=True)


def folded(x):
    return jnp.sum(x.reshape(x.shape[0] // 8, 8, x.shape[1]), axis=0)


def probabilities(logits):
    top = jnp.max(logits, axis=1, keepdims=True)
    e = jnp.exp(logits - top)
    return e * (1.0 / jnp.sum(e, axis=1, keepdims=True))


def forward_products(refs, shared, feat, l_scr):
    precision, _, _ = scalars(refs[3])
    _, _, z, square = latents(refs, shared, feat)
    zh, zl = halves(precision * z)
    l_scr[0 : feat.shape[0]] = dot(logit_rows(zh, zl, square), shared[0][...], 0, 0)


def forward_rows(refs, l_scr, noise_ref, code_ref, usage):
    _, cold, _ = scalars(refs[3])

    def body(at, usage):
        logits = l_scr[at]
        code_ref[at] = probabilities((logits + noise_ref[at]) * cold)
        return None if usage is None else usage + folded(probabilities(logits))

    return over_rows(code_ref.shape[0], body, usage)


def products(refs, shared, scr, feat, cot, forward):
    l_scr, g_scr = scr[0:2]
    rows = feat.shape[0]
    precision, _, factor = scalars(refs[3])
    fh, fl, z, square = latents(refs, shared, feat)
    zh, zl = halves(precision * z)
    ch, cl = halves(factor * cot)
    if forward:
        left = jnp.concatenate([logit_rows(zh, zl, square), cot_rows(ch, cl)], axis=1)
        p = dot(left, shared[0][...], 0, 0)
        l_scr[0:rows] = p[0:rows]
        g_scr[0:rows] = p[rows : 2 * rows]
    else:
        g_scr[0:rows] = dot(cot_rows(ch, cl), shared[0][...], 0, 0)
    return fh, fl, z, square, zh, zl, ch, cl


def both_rows(refs, scr, noise_ref, code_ref, usage):
    l_scr, g_scr, wh_scr, wl_scr, gh_scr, gl_scr = scr
    _, cold, _ = scalars(refs[3])

    def body(at, usage):
        logits = l_scr[at]
        s = (logits + noise_ref[at]) * cold
        e = jnp.exp(s - jnp.max(s, axis=1, keepdims=True))
        gw = g_scr[at]
        scale = 1.0 / jnp.sum(e, axis=1, keepdims=True)
        inner = jnp.sum(e * gw, axis=1, keepdims=True) * scale
        w = e * scale
        code_ref[at] = w
        gd = w * (gw - inner)
        wh_scr[at], wl_scr[at] = halves(w)
        gh_scr[at], gl_scr[at] = halves(gd)
        return usage + folded(probabilities(logits))

    return over_rows(code_ref.shape[0], body, usage)


def backward_rows(scr, code_ref):
    _, g_scr, wh_scr, wl_scr, gh_scr, gl_scr = scr

    def body(at, carry):
        w = code_ref[at]
        gw = g_scr[at]
        gd = w * (gw - jnp.sum(w * gw, axis=1, keepdims=True))
        wh_scr[at], wl_scr[at] = halves(w)
        gh_scr[at], gl_scr[at] = halves(gd)
        return carry

    over_rows(code_ref.shape[0], body, 0)


def gradients(refs, shared, scr, state, acc_ref):
    _, books_scr, weight_scr = shared
    wh_scr, wl_scr, gh_scr, gl_scr = scr[2:6]
    fh, fl, z, square, zh, zl, ch, cl = state
    rows, feats = fh.shape
    dim, codes = refs[2].shape
    wh, wl = wh_scr[0:rows], wl_scr[0:rows]
    gh, gl = gh_scr[0:rows], gl_scr[0:rows]
    p = dot(jnp.concatenate([ch, cl], axis=0), wh)
    acc_ref[0:64] += p[0:dim] + p[dim : 2 * dim] + dot(ch, wl)
    left = jnp.concatenate([zh, zl, jnp.ones((16, rows), BF16)], axis=0)
    p = dot(left, gh) + dot(left, gl)
    acc_ref[64:128] += p[0:dim] + p[dim : 2 * dim]
    acc_ref[128:136] += p[2 * dim : 2 * dim + 8]
    p = dot(books_scr[...], gh, 1, 1) + dot(books_scr[...], gl, 1, 1)
    row_d = p[2 * dim : 2 * dim + 1]
    gz = 2.0 * (row_d * z - (p[0:dim] + p[dim : 2 * dim]))
    zh, zl = halves(gz)
    p = dot(jnp.concatenate([zh, zl], axis=0), fh)
    acc_ref[144:208, 0:feats] += p[0:dim] + p[dim : 2 * dim] + dot(zh, fl)
    acc_ref[144:208, feats : feats + 128] += jnp.broadcast_to(
        jnp.sum(gz, axis=1, keepdims=True), (dim, 128)
    )
    total = jnp.sum(square * row_d, axis=1, keepdims=True)
    acc_ref[208:216] += jnp.broadcast_to(total, (8, codes))
    return dot(jnp.concatenate([zh, zh, zl], axis=0), weight_scr[...], 0, 0)


def shared_scratch(dim, codes, feats):
    return [
        pltpu.VMEM((3 * dim + 16, codes), BF16),
        pltpu.VMEM((2 * dim + 16, codes), BF16),
        pltpu.VMEM((3 * dim, feats), BF16),
    ]


def tile_scratch(rows, codes):
    return [pltpu.VMEM((rows, codes), F32)] * 2 + [pltpu.VMEM((rows, codes), BF16)] * 4


def settings(limit=VMEM_LIMIT):
    return pltpu.CompilerParams(vmem_limit_bytes=limit)


def cost(rows, feats, dim, codes, tenths):
    return pl.CostEstimate(
        flops=rows * 24 * tenths * (5 * dim * codes + 3 * dim * feats) // 10,
        bytes_accessed=4 * rows * (2 * feats + 2 * codes + dim),
        transcendentals=2 * rows * codes,
    )


SMEM = pl.BlockSpec(memory_space=pltpu.SMEM)
VMEM = pl.BlockSpec(memory_space=pltpu.VMEM)
HBM = pl.BlockSpec(memory_space=pltpu.HBM)


def fixed(shape):
    return pl.BlockSpec(shape, lambda *_: (0,) * len(shape))


class Lane:
    def __init__(self, runs):
        self.runs = list(runs)
        self.bounds = [0]
        for _, _, slots in self.runs:
            self.bounds.append(self.bounds[-1] + slots)

    def total(self):
        return self.bounds[-1]

    def index(self, i, order_ref, count):
        share = order_ref.shape[1] // count
        step, slot = 0, 0
        for (whose, first, _), start in zip(self.runs, self.bounds):
            here = first + i - start
            step = whose if start == 0 else jnp.where(i >= start, whose, step)
            slot = here if start == 0 else jnp.where(i >= start, here, slot)
        there = partner(lax.axis_index("space"), step, count)
        return order_ref[0, there * share + slot]

    def image(self, shape, count):
        return pl.BlockSpec(
            (None, *shape), lambda i, order_ref: (self.index(i, order_ref, count), 0, 0)
        )

    def blocks(self, shape):
        return [
            pl.BlockSpec(
                shape,
                lambda i, _, start=start, last=slots - 1: (jnp.clip(i - start, 0, last), 0),
            )
            for (_, _, slots), start in zip(self.runs, self.bounds)
        ]

    def each(self, step, body):
        for i, (low, high) in enumerate(zip(self.bounds, self.bounds[1:])):
            pl.when((step >= low) & (step < high))(functools.partial(body, i))


def split(runs, ways):
    whole = Lane(runs)
    lanes, current = [], []
    for run in whole.runs:
        current.append(run)
        if Lane(current).total() * ways == whole.total():
            lanes.append(Lane(current))
            current = []
    return lanes if len(lanes) == ways and not current else [whole]


def take(refs, *sizes):
    groups, at = [], 0
    for size in sizes:
        groups.append(refs[at : at + size])
        at += size
    return groups


def by_lane(refs, lanes):
    return take(refs, *[len(lane.runs) for lane in lanes])


def keep_codes(step, lanes, sends, code_scrs):
    for lane, refs, code_scr in zip(lanes, by_lane(sends, lanes), code_scrs):
        if len(lane.runs) > 1:

            def keep(i, refs=refs, code_scr=code_scr):
                refs[i][...] = code_scr[...]

            lane.each(step, keep)


def code_targets(lanes, sends, code_scrs):
    return [
        refs[0] if len(lane.runs) == 1 else code_scr
        for lane, refs, code_scr in zip(lanes, by_lane(sends, lanes), code_scrs)
    ]


class Gradients:
    def __init__(self, out_ref, scr, sems):
        self.out_ref, self.scr, self.sems = out_ref, scr, sems

    def copy(self, lane, slot, image):
        return pltpu.make_async_copy(
            self.scr.at[lane, slot], self.out_ref.at[image], self.sems.at[lane, slot]
        )

    def ready(self, step, lanes):
        @pl.when(step >= 2)
        def _():
            for lane in range(lanes):
                self.copy(lane, lax.rem(step, 2), 0).wait()

    def store(self, step, values, images):
        slot = lax.rem(step, 2)
        for lane, (value, image) in enumerate(zip(values, images)):
            self.scr[lane, slot] = value
            self.copy(lane, slot, image).start()

    def end(self, step, lanes, steps):
        @pl.when(step == steps - 1)
        def _():
            for lane in range(lanes):
                for slot in range(min(2, steps)):
                    self.copy(lane, slot, 0).wait()


def gradient_scratch(lanes, strip, width):
    return [pltpu.VMEM((lanes, 2, strip, width), F32), pltpu.SemaphoreType.DMA((lanes, 2))]


def places_of(orders, shapes, groups, steps, count):
    me = lax.axis_index("space")
    strips = []
    at = 0
    for k, step in enumerate(steps):
        there = partner(me, step, count)
        row = 0
        for size in range(2):
            strip = shapes[size][1]
            for j in range(groups[size]):
                image = orders[size][0, there * groups[size] + j]
                strips.append((k, row, size, image, at, strip))
                row += strip
                at += strip
    return strips


def small_forward_kernel(count, steps, groups, counted, *refs):
    sources, wide_in, (log_ref, heat_ref), sends, (usage_ref, scalar_ref), wide_out, held, rest = (
        take(refs, 9, 1, 2, len(steps), 2, 1, 9, len(refs))
    )
    (sems, feat_scr), shared, (l_scr, noise_scr) = take(rest, 2, 3, 2)
    copies = [
        pltpu.make_async_copy(there, here, sems.at[i])
        for i, (there, here) in enumerate(zip([*sources, *wide_in], [*held, *wide_out]))
    ]
    for copy in copies:
        copy.start()
    params, orders, feats, noises = (*held[0:3], scalar_ref), held[3:5], held[5:7], held[7:9]
    set_scalars(log_ref, heat_ref, scalar_ref)
    for copy in copies[0:7]:
        copy.wait()
    prepare(params, *shared, backward=False)
    strips = places_of(orders, [f.shape for f in feats], groups, steps, count)
    for _, _, size, image, at, strip in strips:
        feat_scr[at : at + strip] = feats[size][image]
    forward_products(params, shared, feat_scr[...], l_scr)
    for copy in copies[7:9]:
        copy.wait()
    usage = jnp.zeros(usage_ref.shape, F32) if counted else None
    part = sends[0].shape[0]
    if all(noise.shape[1] % 8 == 0 for noise in noises):
        for k, row, size, image, at, strip in strips:
            rows = pl.ds(at, strip)
            target = sends[k].at[pl.ds(row, strip)]
            usage = forward_rows(params, l_scr.at[rows], noises[size].at[image], target, usage)
    else:
        for _, _, size, image, at, strip in strips:
            noise_scr[at : at + strip] = noises[size][image]
        for k, send in enumerate(sends):
            rows = pl.ds(k * part, part)
            usage = forward_rows(params, l_scr.at[rows], noise_scr.at[rows], send, usage)
    usage_ref[...] = usage if counted else jnp.zeros(usage_ref.shape, F32)
    copies[9].wait()


def small_forward(count, steps, counted, orders, feats, noises, params):
    dim, codes = params[2].shape
    width = feats[0].shape[2]
    groups = tuple(f.shape[0] // count for f in feats)
    part = sum(g * f.shape[1] for g, f in zip(groups, feats))
    rows = part * len(steps)
    arrays = [*params[0:3], *orders[0:2], *feats, *noises]
    return pl.pallas_call(
        functools.partial(small_forward_kernel, count, steps, groups, counted),
        out_shape=[jax.ShapeDtypeStruct((part, codes), F32)] * len(steps)
        + [
            jax.ShapeDtypeStruct((8, codes), F32),
            jax.ShapeDtypeStruct((8, 128), F32),
            jax.ShapeDtypeStruct(orders[2].shape, jnp.int32),
        ],
        in_specs=[HBM] * 10 + [SMEM] * 2,
        out_specs=[VMEM] * (len(steps) + 3),
        scratch_shapes=[
            (pltpu.SMEM if 3 <= i < 5 else pltpu.VMEM)(a.shape, a.dtype)
            for i, a in enumerate(arrays)
        ]
        + [pltpu.SemaphoreType.DMA((10,)), pltpu.VMEM((rows, width), F32)]
        + shared_scratch(dim, codes, width)
        + [pltpu.VMEM((rows, codes), F32)] * 2,
        compiler_params=settings(),
        cost_estimate=cost(rows, width, dim, codes, 4),
        name="small_forward",
    )(*in_hbm([*arrays, orders[2]]), *params[3:5])


def small_backward_kernel(count, steps, devices, groups, *refs):
    orders, feats, cots, parts, params, (acc_in, *usages), grads, shards, rest = take(
        refs, 2, 2, 2, count, 4, 3, 2, devices, len(refs)
    )
    acc_ref, sum_scr, feat_scr, cot_scr, code_scr = rest[0:5]
    scr = rest[5:]
    strips = places_of(orders, [f.shape for f in feats], groups, steps, count)
    for _, _, size, image, at, strip in strips:
        feat_scr[at : at + strip] = feats[size][image]
        cot_scr[at : at + strip] = cots[size][image]
    part = parts[0].shape[0]
    for step in range(count):
        code_scr[step * part : (step + 1) * part] = parts[step][...]
    shared, tile_scr = take(scr, 3, 6)
    prepare(params, *shared)
    acc_ref[...] = acc_in[...]
    state = products(params, shared, tile_scr, feat_scr[...], cot_scr[...].T, False)
    backward_rows(tile_scr, code_scr)
    feat_scr[...] = gradients(params, shared, tile_scr, state, acc_ref)
    acc_ref[136:144] += usages[0][...] + usages[1][...]
    lay_out(params, acc_ref, sum_scr, shards)
    for _, _, size, image, at, strip in strips:
        grads[size][image] = feat_scr[at : at + strip]


def small_backward(count, steps, devices, orders, feats, cots, parts, params, acc, usages):
    dim, codes = params[2].shape
    width = feats[0].shape[2]
    groups = tuple(f.shape[0] // count for f in feats)
    rows = parts[0].shape[0] * count
    return pl.pallas_call(
        functools.partial(small_backward_kernel, count, steps, devices, groups),
        out_shape=[pltpu.HBM(f.shape, F32) for f in feats]
        + [jax.ShapeDtypeStruct((64 // devices, LANES), F32)] * devices,
        in_specs=[SMEM] * 2 + [VMEM] * (11 + count),
        out_specs=[VMEM] * (2 + devices),
        scratch_shapes=[
            pltpu.VMEM(acc.shape, F32),
            pltpu.VMEM((64, LANES), F32),
            pltpu.VMEM((rows, width), F32),
            pltpu.VMEM((rows, dim), F32),
            pltpu.VMEM((rows, codes), F32),
        ]
        + shared_scratch(dim, codes, width)
        + tile_scratch(rows, codes),
        compiler_params=settings(),
        cost_estimate=cost(rows, width, dim, codes, 6),
        name="small_backward",
    )(
        *orders,
        *in_hbm([*feats, *cots]),
        *parts,
        *in_hbm(params[0:3]),
        params[3],
        acc,
        *usages,
    )


def wide_forward_kernel(lanes, joined, *refs):
    n = len(lanes)
    arrays = len(joined) if joined else sum(len(lane.runs) for lane in lanes)
    _, feats, noises, params, usage_in, sends, rest = take(
        refs, 1, n, n, 4, 1, arrays, len(refs)
    )
    (usage_ref,), code_scrs, shared, l_scrs = take(rest, 1, n, 3, n)
    step = pl.program_id(0)

    @pl.when(step == 0)
    def _():
        prepare(params, *shared, backward=False)
        usage_ref[...] = usage_in[0][...]

    if joined:
        strip = code_scrs[0].shape[0]
        targets = [
            send.at[pl.ds(i * strip, strip)] for send, k in zip(sends, joined) for i in range(k)
        ]
    else:
        targets = code_targets(lanes, sends, code_scrs)
    for feat_ref, l_scr in zip(feats, l_scrs):
        forward_products(params, shared, feat_ref[...], l_scr)
    usage = usage_ref[...]
    for l_scr, noise_ref, target in zip(l_scrs, noises, targets):
        usage = forward_rows(params, l_scr, noise_ref, target, usage)
    usage_ref[...] = usage
    if not joined:
        keep_codes(step, lanes, sends, code_scrs)


def wide_forward(count, lanes, joined, order, feat, noise, params, usage, tenths):
    dim, codes = params[2].shape
    images, strip, width = feat.shape
    n, steps = len(lanes), lanes[0].total()
    if joined:
        blocks = [fixed((k * strip, codes)) for k in joined]
        sizes = joined
    else:
        blocks = [block for lane in lanes for block in lane.blocks((strip, codes))]
        sizes = [run[2] for lane in lanes for run in lane.runs]
    return pl.pallas_call(
        functools.partial(wide_forward_kernel, lanes, joined),
        grid_spec=pltpu.PrefetchScalarGridSpec(
            num_scalar_prefetch=1,
            grid=(steps,),
            in_specs=[lane.image((strip, width), count) for lane in lanes]
            + [lane.image((strip, codes), count) for lane in lanes]
            + [fixed(p.shape) for p in params]
            + [fixed(usage.shape)],
            out_specs=blocks + [fixed(usage.shape)],
            scratch_shapes=[pltpu.VMEM((strip, codes), F32)] * n
            + shared_scratch(dim, codes, width)
            + [pltpu.VMEM((strip, codes), F32)] * n,
        ),
        out_shape=[jax.ShapeDtypeStruct((strip * slots, codes), F32) for slots in sizes]
        + [jax.ShapeDtypeStruct(usage.shape, F32)],
        input_output_aliases={5 + 2 * n: len(sizes)},
        compiler_params=settings(),
        cost_estimate=cost(n * steps * strip, width, dim, codes, tenths),
        name="wide_forward",
    )(order, *in_hbm([feat] * n + [noise] * n + [*params[0:3]]), params[3], usage)


def wide_both_kernel(lanes, count, *refs):
    n = len(lanes)
    arrays = sum(len(lane.runs) for lane in lanes)
    order, feats, noises, cots, params, sends, rest = take(
        refs, 1, n, n, n, 4, arrays, len(refs)
    )
    (grad_out, acc_ref), code_scrs, (grad_scr, sems), shared, rest = take(
        rest, 2, n, 2, 3, 6 * n
    )
    scrs = take(rest, *[6] * n)
    grads = Gradients(grad_out, grad_scr, sems)
    step, steps = pl.program_id(0), lanes[0].total()

    @pl.when(step == 0)
    def _():
        prepare(params, *shared)
        acc_ref[...] = jnp.zeros(acc_ref.shape, F32)

    grads.ready(step, n)
    targets = code_targets(lanes, sends, code_scrs)
    states = [
        products(params, shared, scr, feat_ref[...], cot_ref[...], True)
        for scr, feat_ref, cot_ref in zip(scrs, feats, cots)
    ]
    usage = acc_ref[136:144]
    for scr, noise_ref, target in zip(scrs, noises, targets):
        usage = both_rows(params, scr, noise_ref, target, usage)
    acc_ref[136:144] = usage
    values = [
        gradients(params, shared, scr, state, acc_ref) for scr, state in zip(scrs, states)
    ]
    grads.store(step, values, [lane.index(step, order[0], count) for lane in lanes])
    keep_codes(step, lanes, sends, code_scrs)
    grads.end(step, n, steps)


def wide_both(count, lanes, order, feat, noise, cot, params):
    dim, codes = params[2].shape
    images, strip, width = feat.shape
    n, steps = len(lanes), lanes[0].total()
    acc_shape = (ACC_ROWS, codes)
    sizes = [run[2] for lane in lanes for run in lane.runs]
    return pl.pallas_call(
        functools.partial(wide_both_kernel, lanes, count),
        grid_spec=pltpu.PrefetchScalarGridSpec(
            num_scalar_prefetch=1,
            grid=(steps,),
            in_specs=[lane.image((strip, width), count) for lane in lanes]
            + [lane.image((strip, codes), count) for lane in lanes]
            + [lane.image((dim, strip), count) for lane in lanes]
            + [fixed(p.shape) for p in params],
            out_specs=[block for lane in lanes for block in lane.blocks((strip, codes))]
            + [HBM, fixed(acc_shape)],
            scratch_shapes=[pltpu.VMEM((strip, codes), F32)] * n
            + gradient_scratch(n, strip, width)
            + shared_scratch(dim, codes, width)
            + tile_scratch(strip, codes) * n,
        ),
        out_shape=[jax.ShapeDtypeStruct((strip * slots, codes), F32) for slots in sizes]
        + [pltpu.HBM(feat.shape, F32), jax.ShapeDtypeStruct(acc_shape, F32)],
        compiler_params=settings(),
        cost_estimate=cost(n * steps * strip, width, dim, codes, 10),
        name="wide_both",
    )(order, *in_hbm([feat] * n + [noise] * n + [cot] * n + [*params[0:3]]), params[3])


def wide_backward_kernel(lanes, count, *refs):
    n = len(lanes)
    arrays = sum(len(lane.runs) for lane in lanes)
    order, feats, cots, parts, params, (acc_in, _), rest = take(
        refs, 1, n, n, arrays, 4, 2, len(refs)
    )
    (grad_out, acc_ref), code_scrs, (grad_scr, sems), shared, rest = take(
        rest, 2, n, 2, 3, 6 * n
    )
    scrs = take(rest, *[6] * n)
    grads = Gradients(grad_out, grad_scr, sems)
    step, steps = pl.program_id(0), lanes[0].total()

    @pl.when(step == 0)
    def _():
        prepare(params, *shared)
        acc_ref[...] = acc_in[...]

    grads.ready(step, n)
    for lane, refs_of, code_scr in zip(lanes, by_lane(parts, lanes), code_scrs):
        if len(lane.runs) > 1:

            def fetch(i, refs_of=refs_of, code_scr=code_scr):
                code_scr[...] = refs_of[i][...]

            lane.each(step, fetch)
    states = [
        products(params, shared, scr, feat_ref[...], cot_ref[...], False)
        for scr, feat_ref, cot_ref in zip(scrs, feats, cots)
    ]
    for scr, code_ref in zip(scrs, code_targets(lanes, parts, code_scrs)):
        backward_rows(scr, code_ref)
    values = [
        gradients(params, shared, scr, state, acc_ref) for scr, state in zip(scrs, states)
    ]
    grads.store(step, values, [lane.index(step, order[0], count) for lane in lanes])
    grads.end(step, n, steps)


def wide_backward(count, lanes, parts, order, feat, cot, params, acc, grad):
    dim, codes = params[2].shape
    images, strip, width = feat.shape
    n, steps = len(lanes), lanes[0].total()
    return pl.pallas_call(
        functools.partial(wide_backward_kernel, lanes, count),
        grid_spec=pltpu.PrefetchScalarGridSpec(
            num_scalar_prefetch=1,
            grid=(steps,),
            in_specs=[lane.image((strip, width), count) for lane in lanes]
            + [lane.image((dim, strip), count) for lane in lanes]
            + [block for lane in lanes for block in lane.blocks((strip, codes))]
            + [fixed(p.shape) for p in params]
            + [fixed(acc.shape), HBM],
            out_specs=[HBM, fixed(acc.shape)],
            scratch_shapes=[pltpu.VMEM((strip, codes), F32)] * n
            + gradient_scratch(n, strip, width)
            + shared_scratch(dim, codes, width)
            + tile_scratch(strip, codes) * n,
        ),
        out_shape=[pltpu.HBM(feat.shape, F32), jax.ShapeDtypeStruct(acc.shape, F32)],
        input_output_aliases={5 + 2 * n + len(parts): 1, 6 + 2 * n + len(parts): 0},
        compiler_params=settings(),
        cost_estimate=cost(n * steps * strip, width, dim, codes, 6),
        name="wide_backward",
    )(
        order,
        *in_hbm([feat] * n + [cot] * n),
        *parts,
        *in_hbm(params[0:3]),
        params[3],
        acc,
        *in_hbm([grad]),
    )


def shard_at(index, parts):
    height = 64 // parts
    return pl.ds(pl.multiple_of(index * height, height), height)


def lay_out(params, acc_ref, sum_scr, shards):
    weight_ref, bias_ref, book_ref, scalar_ref = params
    codes = book_ref.shape[1]
    width = weight_ref.shape[1]
    devices = len(shards)
    me = lax.rem(lax.axis_index("dp"), devices)
    precision, _, factor = scalars(scalar_ref)
    book = book_ref[...]
    column = acc_ref[128:129]
    moment = acc_ref[64:128] * (1.0 / precision)
    book_sum = acc_ref[0:64] * (1.0 / factor) + 2.0 * (column * book - moment)
    slope = jnp.sum(
        jnp.sum(book * book, axis=0, keepdims=True) * column, axis=1, keepdims=True
    ) - 2.0 * jnp.sum(jnp.sum(book * moment, axis=0, keepdims=True), axis=1, keepdims=True)
    slope = slope + acc_ref[208:209, 0:1] / (-0.5 * precision)
    usage = jnp.sum(acc_ref[136:144], axis=0, keepdims=True)
    dim = book_ref.shape[0]
    eye = lax.broadcasted_iota(jnp.int32, (dim, dim), 0) == lax.broadcasted_iota(
        jnp.int32, (dim, dim), 1
    )
    bias = acc_ref[144:208, width : width + dim]
    bias = jnp.sum(jnp.where(eye, bias, 0.0), axis=0, keepdims=True)
    rest = codes + width
    sum_scr[:, 0:codes] = book_sum
    sum_scr[:, codes:rest] = acc_ref[144:208, 0:width]
    sum_scr[:, rest : rest + 128] = jnp.broadcast_to(slope, (64, 128))
    rows = codes // 128
    for i in range(rows):
        sum_scr[i : i + 1, rest : rest + 128] = usage[:, i * 128 : (i + 1) * 128]
    sum_scr[rows : rows + 1, rest : rest + dim] = bias
    for i in range(devices):
        shards[i][...] = sum_scr[shard_at(partner(me, i, devices), devices)]


def own_kernel(n, count, *refs):
    order, feats, noises, cots, params, (acc_in, _), rest = take(
        refs, 1, n, n, n, 4, 2, len(refs)
    )
    (code_ref, grad_out, acc_ref), (grad_scr, sems), shared, rest = take(rest, 3, 2, 3, 6 * n)
    scrs = take(rest, *[6] * n)
    grads = Gradients(grad_out, grad_scr, sems)
    step = pl.program_id(0)

    @pl.when(step == 0)
    def _():
        prepare(params, *shared)
        acc_ref[...] = acc_in[...]

    grads.ready(step, n)
    states = [
        products(params, shared, scr, feat_ref[...], cot_ref[...], True)
        for scr, feat_ref, cot_ref in zip(scrs, feats, cots)
    ]
    usage = acc_ref[136:144]
    for i, (scr, noise_ref) in enumerate(zip(scrs, noises)):
        usage = both_rows(params, scr, noise_ref, code_ref.at[i], usage)
    acc_ref[136:144] = usage
    values = [
        gradients(params, shared, scr, state, acc_ref) for scr, state in zip(scrs, states)
    ]
    grads.store(step, values, [own_image(step, i, n, order[0], count) for i in range(n)])
    grads.end(step, n, pl.num_programs(0))


def own_image(step, lane, n, order_ref, count):
    share = order_ref.shape[1] // count
    return order_ref[0, lax.axis_index("space") * share + step * n + lane]


def run_own(count, order, feat, noise, cot, params, acc, grad):
    dim, codes = params[2].shape
    images, strip, width = feat.shape
    share = images // count
    n = 2 if share % 2 == 0 else 1

    def image(lane, shape):
        return pl.BlockSpec(
            (None, *shape), lambda i, order_ref: (own_image(i, lane, n, order_ref, count), 0, 0)
        )

    return pl.pallas_call(
        functools.partial(own_kernel, n, count),
        grid_spec=pltpu.PrefetchScalarGridSpec(
            num_scalar_prefetch=1,
            grid=(share // n,),
            in_specs=[image(lane, (strip, width)) for lane in range(n)]
            + [image(lane, (strip, codes)) for lane in range(n)]
            + [image(lane, (dim, strip)) for lane in range(n)]
            + [fixed(p.shape) for p in params]
            + [fixed(acc.shape), HBM],
            out_specs=[
                pl.BlockSpec(
                    (n, strip, codes),
                    lambda i, _: (i, lax.axis_index("space"), 0),
                ),
                HBM,
                fixed(acc.shape),
            ],
            scratch_shapes=gradient_scratch(n, strip, width)
            + shared_scratch(dim, codes, width)
            + tile_scratch(strip, codes) * n,
        ),
        out_shape=[
            pltpu.HBM((share, strip * count, codes), F32),
            pltpu.HBM(feat.shape, F32),
            jax.ShapeDtypeStruct(acc.shape, F32),
        ],
        input_output_aliases={5 + 3 * n: 2, 6 + 3 * n: 1},
        compiler_params=settings(),
        cost_estimate=cost(share * strip, width, dim, codes, 10),
        name="own_images",
    )(
        order,
        *in_hbm([feat] * n + [noise] * n + [cot] * n + [*params[0:3]]),
        params[3],
        acc,
        *in_hbm([grad]),
    )


def place_kernel(count, runs, *refs):
    parts = refs[0 : len(runs)]
    out_ref, sem = refs[len(runs) + 1 : len(runs) + 3]
    me = lax.axis_index("space")
    copies = []
    for part, (step, first, slots) in zip(parts, runs):
        strip = part.shape[0] // slots
        row = pl.multiple_of(source(me, step, count) * strip, strip)
        for j in range(slots):
            copies.append(
                pltpu.make_async_copy(
                    part.at[pl.ds(j * strip, strip)],
                    out_ref.at[first + j, pl.ds(row, strip)],
                    sem.at[len(copies)],
                )
            )
    for copy in copies:
        copy.start()
    for copy in copies:
        copy.wait()


def place_wide(count, runs, parts, whole):
    return pl.pallas_call(
        functools.partial(place_kernel, count, runs),
        out_shape=pltpu.HBM(whole.shape, F32),
        in_specs=[VMEM] * len(runs) + [HBM],
        out_specs=HBM,
        scratch_shapes=[pltpu.SemaphoreType.DMA((sum(r[2] for r in runs),))],
        input_output_aliases={len(runs): 0},
        compiler_params=settings(VMEM_LIMIT // 2),
        cost_estimate=pl.CostEstimate(
            flops=0, bytes_accessed=2 * sum(p.size * 4 for p in parts), transcendentals=0
        ),
        name="place_wide",
    )(*[pltpu.with_memory_space_constraint(p, pltpu.VMEM) for p in parts], *in_hbm([whole]))


def join_kernel(count, steps, *refs):
    parts = refs[0:count]
    outs = refs[count:]
    me = lax.axis_index("space")
    for part, step in zip(parts, steps):
        here = source(me, step, count)
        base = 0
        for out in outs:
            for j in range(out.shape[0]):
                strip = out.shape[2]
                out[j, here] = part[base : base + strip]
                base += strip


def join_small(count, steps, parts, shapes):
    codes = parts[0].shape[1]
    return pl.pallas_call(
        functools.partial(join_kernel, count, steps),
        out_shape=[
            jax.ShapeDtypeStruct((images // count, count, strip, codes), F32)
            for images, strip, _ in shapes
        ],
        compiler_params=settings(VMEM_LIMIT // 2),
        name="join_small",
    )(*parts)


def tree(values):
    while len(values) > 1:
        values = [
            values[i] + values[i + 1] if i + 1 < len(values) else values[i]
            for i in range(0, len(values), 2)
        ]
    return values[0]


def sum_kernel(*refs):
    refs[-1][...] = tree([ref[...] for ref in refs[:-1]])


def add_all(parts):
    return pl.pallas_call(
        sum_kernel,
        out_shape=jax.ShapeDtypeStruct(parts[0].shape, F32),
        compiler_params=settings(VMEM_LIMIT // 2),
        name="add_parts",
    )(*parts)


def final_kernel(devices, pixels, *refs):
    shards = refs[0:devices]
    weight_ref, bias_ref, book_ref, log_ref, usage_ref = refs[devices : devices + 5]
    weight_out, bias_out, book_out, log_out, usage_out = refs[devices + 5 : devices + 10]
    sum_scr = refs[devices + 10]
    me = lax.rem(lax.axis_index("dp"), devices)
    for i in range(devices):
        sum_scr[shard_at(source(me, i, devices), devices)] = shards[i][...]
    dim, codes = book_ref.shape
    width = weight_ref.shape[1]
    scale = 0.5 * lax.rsqrt(jnp.full((8, 128), pixels, F32))[0:1, 0:1]
    book_out[...] = 0.5 * book_ref[...] + scale * sum_scr[:, 0:codes]
    rest = codes + width
    weight_out[...] = 0.5 * weight_ref[...] + scale * sum_scr[:, codes:rest]
    rows = codes // 128
    bias_out[...] = 0.5 * bias_ref[...] + scale * sum_scr[rows : rows + 1, rest : rest + dim]
    usage = jnp.concatenate(
        [sum_scr[i : i + 1, rest : rest + 128] for i in range(rows)], axis=1
    )
    usage_out[...] = 0.5 * usage_ref[...] + 0.5 * (codes / pixels) * usage
    log_out[...] = 0.5 * log_ref[...] + scale * sum_scr[rows + 1 : rows + 2, rest : rest + 1]


def finish(devices, pixels, shards, weight, bias, book, log, usage):
    outs = (weight.T, bias.reshape(1, -1), book.T, log.reshape(1, 1), usage.reshape(1, -1))
    outs = pl.pallas_call(
        functools.partial(final_kernel, devices, pixels),
        out_shape=[jax.ShapeDtypeStruct(out.shape, F32) for out in outs],
        scratch_shapes=[pltpu.VMEM((64, LANES), F32)],
        compiler_params=settings(VMEM_LIMIT // 2),
        name="new_averages",
    )(*shards, *outs)
    return outs[0].T, outs[1].reshape(-1), outs[2].T, outs[3].reshape(-1), outs[4].reshape(-1)


def exchange(value, bit, size, pairs):
    while bit < size:
        value = value + pairs(value, bit)
        bit = 2 * bit
    return value


def per_device(
    feat_small,
    feat_mid,
    feat_wide,
    noise_small,
    noise_mid,
    noise_wide,
    cot_small,
    cot_mid,
    cot_wide,
    order_small,
    order_mid,
    order_wide,
    weight,
    bias,
    book,
    log,
    heat,
    weight_mean,
    bias_mean,
    book_mean,
    log_mean,
    usage_mean,
):
    count = lax.axis_size("space")
    devices = lax.axis_size("dp")
    params = (weight.T, bias.reshape(1, -1), book.T, log, heat)
    feats = (feat_small, feat_mid, feat_wide)
    pixels = sum(f.shape[0] * f.shape[1] for f in feats) * count * devices
    share = feat_wide.shape[0] // count
    cot_wide = jnp.swapaxes(cot_wide, 1, 2)

    def send(values):
        return [lax.ppermute(v, "space", route(i, count)) for i, v in zip(turns, values)]

    def follow(codes, before, parts):
        here, codes[-1] = lax.optimization_barrier(([before[i] for i in parts], codes[-1]))
        for i, part in zip(parts, here):
            before[i] = part
        return send(codes)

    last = count - 1
    turns = list(range(1, count))
    orders = (order_small, order_mid, order_wide)
    noises = (noise_small, noise_mid)
    *small, usage, scalar, order_wide = small_forward(
        count, turns, False, orders, feats[0:2], noises, params
    )
    arrived = [send(small)]
    own_params = params
    params = (*params[0:3], scalar)
    near = min(4, devices)
    early = [(step, 0, 1) for step in turns]
    direct = [(step, 1, share - 1) for step in turns[:-1]]
    late = [(last, 1, share - 2), (last, share - 1, 1)]
    *early_codes, usage = wide_forward(
        count, split(early, 3), [], order_wide, feat_wide, noise_wide, params, usage, 4
    )
    ahead = [count - 2, *range(count - 2)]
    arrived.append(follow(list(early_codes), arrived[0], ahead))
    *codes, grad, acc = wide_both(
        count, split(direct, 2), order_wide, feat_wide, noise_wide, cot_wide, params
    )
    late_lanes = [Lane([(last, slot, 1)]) for slot in range(1, share)]
    late_codes, end_codes, usage = wide_forward(
        count, late_lanes, [share - 2, 1], order_wide, feat_wide, noise_wide, params, usage, 1
    )
    arrived.append(follow([*codes, late_codes], arrived[1], [0]))
    arrived[1][-1], leaving = lax.optimization_barrier((arrived[1][-1], end_codes))
    arrived[2].append(lax.ppermute(leaving, "space", route(last, count)))
    arrived[1], acc = lax.optimization_barrier((arrived[1], acc))
    whole, grad, acc = run_own(
        count, order_wide, feat_wide, noise_wide, cot_wide, params, acc, grad
    )
    whole = place_wide(count, early, arrived[1], whole)
    acc, own_params = lax.optimization_barrier((acc, own_params))
    own, *_, own_usage, _, _ = small_forward(
        count, [0, *turns], True, orders, feats[0:2], noises, own_params
    )
    small = [own, *small]
    codes_small, codes_mid = join_small(
        count, [0, *turns], [own] + arrived[0], [f.shape for f in feats[0:2]]
    )
    whole, codes_small, codes_mid, acc = lax.optimization_barrier(
        (whole, codes_small, codes_mid, acc)
    )
    grad, acc = wide_backward(
        count,
        split(early + late, 2),
        [*early_codes, late_codes, end_codes],
        order_wide,
        feat_wide,
        cot_wide,
        params,
        acc,
        grad,
    )
    grad_small, grad_mid, *shards = small_backward(
        count,
        [0, *turns],
        near,
        orders[0:2],
        feats[0:2],
        (cot_small, cot_mid),
        small,
        params,
        acc,
        (usage, own_usage),
    )
    group = [
        [(i, i - i % near + partner(i % near, step, near)) for i in range(devices)]
        for step in range(near)
    ]
    parts = [lax.ppermute(shards[i], "dp", group[i]) for i in range(1, near)]
    mine = add_all([shards[0]] + parts)

    def along(value, offset):
        return lax.ppermute(value, "dp", [(i, i ^ offset) for i in range(devices)])

    def across(value, offset):
        turn = near if devices > near else 0
        pairs = [
            (i * count + j, (i ^ turn) * count + (j ^ offset))
            for i in range(devices)
            for j in range(count)
        ]
        return lax.ppermute(value, ("dp", "space"), pairs)

    mine = exchange(mine, near, devices, along)
    arrived[2][:-2], mine = lax.optimization_barrier((arrived[2][:-2], mine))
    mine = exchange(mine, 1, count, across)
    shards = [mine] + [lax.ppermute(mine, "dp", group[i]) for i in range(1, near)]
    updated = finish(
        near, pixels, shards, weight_mean, bias_mean, book_mean, log_mean, usage_mean
    )
    *before, final = zip(direct + late, arrived[2])
    for run, part in before:
        whole = place_wide(count, [run], [part], whole)
    whole, updated = lax.optimization_barrier((whole, updated))
    whole = place_wide(count, [final[0]], [final[1]], whole)
    codes = whole.shape[2]
    return (
        codes_small.reshape(codes_small.shape[0], -1, codes),
        codes_mid.reshape(codes_mid.shape[0], -1, codes),
        whole,
        grad_small,
        grad_mid,
        grad,
        *updated,
    )


def solution(mesh):
    strips = P("dp", "space", None)
    placed = (strips,) * 9 + (P("dp", None),) * 3 + (P(),) * 10
    return jax.shard_map(
        per_device,
        mesh=mesh,
        in_specs=placed,
        out_specs=(P(("dp", "space"), None, None),) * 3 + (strips,) * 3 + (P(),) * 5,
        check_vma=False,
    )
```

```python
import functools

import jax
import jax.numpy as jnp
from jax import lax
from jax.experimental import pallas as pl
from jax.experimental.pallas import tpu as pltpu
from jax.sharding import PartitionSpec as P

F32 = jnp.float32
BF16 = jnp.bfloat16
VMEM_LIMIT = 24 * 1024 * 1024
ACC_ROWS = 64 + 64 + 8 + 8 + 64 + 8
LANES = 896


def partner(index, step, count):
    if count & (count - 1) == 0:
        return index ^ step
    return lax.rem(index + step, count)


def route(step, count):
    if count & (count - 1) == 0:
        return [(i, i ^ step) for i in range(count)]
    return [(i, (i + step) % count) for i in range(count)]


def source(index, step, count):
    if count & (count - 1) == 0:
        return index ^ step
    return lax.rem(index + (count - step), count)


def in_hbm(arrays):
    return [pltpu.with_memory_space_constraint(a, pltpu.HBM) for a in arrays]


def halves(x):
    high = x.astype(BF16)
    return high, (x - high.astype(F32)).astype(BF16)


def dot(left, right, left_dim=1, right_dim=0):
    return lax.dot_general(
        left, right, (((left_dim,), (right_dim,)), ((), ())), preferred_element_type=F32
    )


def set_scalars(log_ref, heat_ref, out_ref):
    precision = jnp.exp(jnp.full((8, 128), log_ref[0], F32))
    heat = jnp.full((8, 128), heat_ref[0], F32)
    row = lax.broadcasted_iota(jnp.int32, (8, 128), 0)
    factor = -0.5 * precision / heat
    out_ref[...] = jnp.where(row == 0, precision, jnp.where(row == 1, 1.0 / heat, factor))


def scalars(ref):
    return ref[0:1, 0:1], ref[1:2, 0:1], ref[2:3, 0:1]


def prepare(refs, book_scr, books_scr, weight_scr, backward=True):
    weight_ref, bias_ref, book_ref, scalar_ref = refs
    dim, codes = book_ref.shape
    precision, _, _ = scalars(scalar_ref)
    book = book_ref[...]
    high, low = halves(book)
    norm = -0.5 * precision * jnp.sum(book * book, axis=0, keepdims=True)
    n0 = norm.astype(BF16).astype(F32)
    n1 = (norm - n0).astype(BF16).astype(F32)
    n2 = norm - n0 - n1
    row = lax.broadcasted_iota(jnp.int32, (16, codes), 0)
    extra = jnp.where(
        row < 3,
        1.0,
        jnp.where(row == 3, n0, jnp.where(row == 4, n1, jnp.where(row == 5, n2, 0.0))),
    ).astype(BF16)
    book_scr[0:dim] = high
    book_scr[dim : 2 * dim] = low
    book_scr[2 * dim : 3 * dim] = high
    book_scr[3 * dim : 3 * dim + 16] = extra
    if backward:
        books_scr[0:dim] = high
        books_scr[dim : 2 * dim] = low
        books_scr[2 * dim : 2 * dim + 16] = jnp.ones((16, codes), BF16)
    high, low = halves(weight_ref[...])
    weight_scr[0:dim] = high
    weight_scr[dim : 2 * dim] = low
    weight_scr[2 * dim : 3 * dim] = high


def latents(refs, shared, feat):
    weight_ref, bias_ref, book_ref, scalar_ref = refs
    weight_scr = shared[2]
    dim = book_ref.shape[0]
    precision, _, _ = scalars(scalar_ref)
    eye = lax.broadcasted_iota(jnp.int32, (dim, dim), 0) == lax.broadcasted_iota(
        jnp.int32, (dim, dim), 1
    )
    bias = jnp.sum(jnp.where(eye, bias_ref[...], 0.0), axis=1, keepdims=True)
    fh, fl = halves(feat)
    both = weight_scr[0 : 2 * dim]
    z2 = dot(both, fh, 1, 1) + dot(both, fl, 1, 1)
    z = z2[0:dim] + z2[dim : 2 * dim] + bias
    square = -0.5 * precision * jnp.sum(z * z, axis=0, keepdims=True)
    return fh, fl, z, square


def logit_rows(zh, zl, square):
    rows = zh.shape[1]
    s0 = square.astype(BF16).astype(F32)
    s1 = (square - s0).astype(BF16).astype(F32)
    s2 = square - s0 - s1
    row = lax.broadcasted_iota(jnp.int32, (16, rows), 0)
    extra = jnp.where(
        row == 0,
        s0,
        jnp.where(row == 1, s1, jnp.where(row == 2, s2, jnp.where(row < 6, 1.0, 0.0))),
    ).astype(BF16)
    return jnp.concatenate([zh, zh, zl, extra], axis=0)


def cot_rows(ch, cl):
    return jnp.concatenate([ch, ch, cl, jnp.zeros((16, ch.shape[1]), BF16)], axis=0)


def over_rows(rows, body, carry):
    step = next(s for s in (32, 16, 8) if rows % s == 0)

    def at(i, carry):
        return body(pl.ds(pl.multiple_of(i * step, step), step), carry)

    return lax.fori_loop(0, rows // step, at, carry, unroll=True)


def folded(x):
    return jnp.sum(x.reshape(x.shape[0] // 8, 8, x.shape[1]), axis=0)


def probabilities(logits):
    top = jnp.max(logits, axis=1, keepdims=True)
    e = jnp.exp(logits - top)
    return e * (1.0 / jnp.sum(e, axis=1, keepdims=True))


def forward_products(refs, shared, feat, l_scr):
    precision, _, _ = scalars(refs[3])
    _, _, z, square = latents(refs, shared, feat)
    zh, zl = halves(precision * z)
    l_scr[0 : feat.shape[0]] = dot(logit_rows(zh, zl, square), shared[0][...], 0, 0)


def forward_rows(refs, l_scr, noise_ref, code_ref, usage):
    _, cold, _ = scalars(refs[3])

    def body(at, usage):
        logits = l_scr[at]
        code_ref[at] = probabilities((logits + noise_ref[at]) * cold)
        return usage + folded(probabilities(logits))

    return over_rows(code_ref.shape[0], body, usage)


def products(refs, shared, scr, feat, cot, forward):
    l_scr, g_scr = scr[0:2]
    rows = feat.shape[0]
    precision, _, factor = scalars(refs[3])
    fh, fl, z, square = latents(refs, shared, feat)
    zh, zl = halves(precision * z)
    ch, cl = halves(factor * cot)
    if forward:
        left = jnp.concatenate([logit_rows(zh, zl, square), cot_rows(ch, cl)], axis=1)
        p = dot(left, shared[0][...], 0, 0)
        l_scr[0:rows] = p[0:rows]
        g_scr[0:rows] = p[rows : 2 * rows]
    else:
        g_scr[0:rows] = dot(cot_rows(ch, cl), shared[0][...], 0, 0)
    return fh, fl, z, square, zh, zl, ch, cl


def both_rows(refs, scr, noise_ref, code_ref, usage):
    l_scr, g_scr, wh_scr, wl_scr, gh_scr, gl_scr = scr
    _, cold, _ = scalars(refs[3])

    def body(at, usage):
        logits = l_scr[at]
        s = (logits + noise_ref[at]) * cold
        e = jnp.exp(s - jnp.max(s, axis=1, keepdims=True))
        gw = g_scr[at]
        scale = 1.0 / jnp.sum(e, axis=1, keepdims=True)
        inner = jnp.sum(e * gw, axis=1, keepdims=True) * scale
        w = e * scale
        code_ref[at] = w
        gd = w * (gw - inner)
        wh_scr[at], wl_scr[at] = halves(w)
        gh_scr[at], gl_scr[at] = halves(gd)
        return usage + folded(probabilities(logits))

    return over_rows(code_ref.shape[0], body, usage)


def backward_rows(scr, code_ref):
    _, g_scr, wh_scr, wl_scr, gh_scr, gl_scr = scr

    def body(at, carry):
        w = code_ref[at]
        gw = g_scr[at]
        gd = w * (gw - jnp.sum(w * gw, axis=1, keepdims=True))
        wh_scr[at], wl_scr[at] = halves(w)
        gh_scr[at], gl_scr[at] = halves(gd)
        return carry

    over_rows(code_ref.shape[0], body, 0)


def gradients(refs, shared, scr, state, acc_ref):
    _, books_scr, weight_scr = shared
    wh_scr, wl_scr, gh_scr, gl_scr = scr[2:6]
    fh, fl, z, square, zh, zl, ch, cl = state
    rows, feats = fh.shape
    dim, codes = refs[2].shape
    wh, wl = wh_scr[0:rows], wl_scr[0:rows]
    gh, gl = gh_scr[0:rows], gl_scr[0:rows]
    p = dot(jnp.concatenate([ch, cl], axis=0), wh)
    acc_ref[0:64] += p[0:dim] + p[dim : 2 * dim] + dot(ch, wl)
    left = jnp.concatenate([zh, zl, jnp.ones((16, rows), BF16)], axis=0)
    p = dot(left, gh) + dot(left, gl)
    acc_ref[64:128] += p[0:dim] + p[dim : 2 * dim]
    acc_ref[128:136] += p[2 * dim : 2 * dim + 8]
    p = dot(books_scr[...], gh, 1, 1) + dot(books_scr[...], gl, 1, 1)
    row_d = p[2 * dim : 2 * dim + 1]
    gz = 2.0 * (row_d * z - (p[0:dim] + p[dim : 2 * dim]))
    zh, zl = halves(gz)
    p = dot(jnp.concatenate([zh, zl], axis=0), fh)
    acc_ref[144:208, 0:feats] += p[0:dim] + p[dim : 2 * dim] + dot(zh, fl)
    acc_ref[144:208, feats : feats + 128] += jnp.broadcast_to(
        jnp.sum(gz, axis=1, keepdims=True), (dim, 128)
    )
    total = jnp.sum(square * row_d, axis=1, keepdims=True)
    acc_ref[208:216] += jnp.broadcast_to(total, (8, codes))
    return dot(jnp.concatenate([zh, zh, zl], axis=0), weight_scr[...], 0, 0)


def shared_scratch(dim, codes, feats):
    return [
        pltpu.VMEM((3 * dim + 16, codes), BF16),
        pltpu.VMEM((2 * dim + 16, codes), BF16),
        pltpu.VMEM((3 * dim, feats), BF16),
    ]


def tile_scratch(rows, codes):
    return [pltpu.VMEM((rows, codes), F32)] * 2 + [pltpu.VMEM((rows, codes), BF16)] * 4


def settings(limit=VMEM_LIMIT):
    return pltpu.CompilerParams(vmem_limit_bytes=limit)


def cost(rows, feats, dim, codes, tenths):
    return pl.CostEstimate(
        flops=rows * 24 * tenths * (5 * dim * codes + 3 * dim * feats) // 10,
        bytes_accessed=4 * rows * (2 * feats + 2 * codes + dim),
        transcendentals=2 * rows * codes,
    )


SMEM = pl.BlockSpec(memory_space=pltpu.SMEM)
VMEM = pl.BlockSpec(memory_space=pltpu.VMEM)
HBM = pl.BlockSpec(memory_space=pltpu.HBM)


def fixed(shape):
    return pl.BlockSpec(shape, lambda *_: (0,) * len(shape))


class Lane:
    def __init__(self, runs):
        self.runs = list(runs)
        self.bounds = [0]
        for _, _, slots in self.runs:
            self.bounds.append(self.bounds[-1] + slots)

    def total(self):
        return self.bounds[-1]

    def index(self, i, order_ref, count):
        share = order_ref.shape[1] // count
        step, slot = 0, 0
        for (whose, first, _), start in zip(self.runs, self.bounds):
            here = first + i - start
            step = whose if start == 0 else jnp.where(i >= start, whose, step)
            slot = here if start == 0 else jnp.where(i >= start, here, slot)
        there = partner(lax.axis_index("space"), step, count)
        return order_ref[0, there * share + slot]

    def image(self, shape, count):
        return pl.BlockSpec(
            (None, *shape), lambda i, order_ref: (self.index(i, order_ref, count), 0, 0)
        )

    def blocks(self, shape):
        return [
            pl.BlockSpec(
                shape,
                lambda i, _, start=start, last=slots - 1: (jnp.clip(i - start, 0, last), 0),
            )
            for (_, _, slots), start in zip(self.runs, self.bounds)
        ]

    def each(self, step, body):
        for i, (low, high) in enumerate(zip(self.bounds, self.bounds[1:])):
            pl.when((step >= low) & (step < high))(functools.partial(body, i))


def split(runs, ways):
    whole = Lane(runs)
    lanes, current = [], []
    for run in whole.runs:
        current.append(run)
        if Lane(current).total() * ways == whole.total():
            lanes.append(Lane(current))
            current = []
    return lanes if len(lanes) == ways and not current else [whole]


def take(refs, *sizes):
    groups, at = [], 0
    for size in sizes:
        groups.append(refs[at : at + size])
        at += size
    return groups


def by_lane(refs, lanes):
    return take(refs, *[len(lane.runs) for lane in lanes])


def keep_codes(step, lanes, sends, code_scrs):
    for lane, refs, code_scr in zip(lanes, by_lane(sends, lanes), code_scrs):
        if len(lane.runs) > 1:

            def keep(i, refs=refs, code_scr=code_scr):
                refs[i][...] = code_scr[...]

            lane.each(step, keep)


def code_targets(lanes, sends, code_scrs):
    return [
        refs[0] if len(lane.runs) == 1 else code_scr
        for lane, refs, code_scr in zip(lanes, by_lane(sends, lanes), code_scrs)
    ]


class Gradients:
    def __init__(self, out_ref, scr, sems):
        self.out_ref, self.scr, self.sems = out_ref, scr, sems

    def copy(self, lane, slot, image):
        return pltpu.make_async_copy(
            self.scr.at[lane, slot], self.out_ref.at[image], self.sems.at[lane, slot]
        )

    def ready(self, step, lanes):
        @pl.when(step >= 2)
        def _():
            for lane in range(lanes):
                self.copy(lane, lax.rem(step, 2), 0).wait()

    def store(self, step, values, images):
        slot = lax.rem(step, 2)
        for lane, (value, image) in enumerate(zip(values, images)):
            self.scr[lane, slot] = value
            self.copy(lane, slot, image).start()

    def end(self, step, lanes, steps):
        @pl.when(step == steps - 1)
        def _():
            for lane in range(lanes):
                for slot in range(min(2, steps)):
                    self.copy(lane, slot, 0).wait()


def gradient_scratch(lanes, strip, width):
    return [pltpu.VMEM((lanes, 2, strip, width), F32), pltpu.SemaphoreType.DMA((lanes, 2))]


def places_of(orders, shapes, groups, steps, count):
    me = lax.axis_index("space")
    strips = []
    at = 0
    for k, step in enumerate(steps):
        there = partner(me, step, count)
        row = 0
        for size in range(2):
            strip = shapes[size][1]
            for j in range(groups[size]):
                image = orders[size][0, there * groups[size] + j]
                strips.append((k, row, size, image, at, strip))
                row += strip
                at += strip
    return strips


def small_forward_kernel(count, steps, groups, *refs):
    sources, wide_in, (log_ref, heat_ref), sends, (usage_ref, scalar_ref), wide_out, held, rest = (
        take(refs, 9, 1, 2, len(steps), 2, 1, 9, len(refs))
    )
    (sems, feat_scr), shared, (l_scr, noise_scr) = take(rest, 2, 3, 2)
    copies = [
        pltpu.make_async_copy(there, here, sems.at[i])
        for i, (there, here) in enumerate(zip([*sources, *wide_in], [*held, *wide_out]))
    ]
    for copy in copies:
        copy.start()
    params, orders, feats, noises = (*held[0:3], scalar_ref), held[3:5], held[5:7], held[7:9]
    set_scalars(log_ref, heat_ref, scalar_ref)
    for copy in copies[0:7]:
        copy.wait()
    prepare(params, *shared, backward=False)
    strips = places_of(orders, [f.shape for f in feats], groups, steps, count)
    for _, _, size, image, at, strip in strips:
        feat_scr[at : at + strip] = feats[size][image]
    forward_products(params, shared, feat_scr[...], l_scr)
    for copy in copies[7:9]:
        copy.wait()
    usage = jnp.zeros(usage_ref.shape, F32)
    part = sends[0].shape[0]
    if all(noise.shape[1] % 8 == 0 for noise in noises):
        for k, row, size, image, at, strip in strips:
            rows = pl.ds(at, strip)
            target = sends[k].at[pl.ds(row, strip)]
            usage = forward_rows(params, l_scr.at[rows], noises[size].at[image], target, usage)
    else:
        for _, _, size, image, at, strip in strips:
            noise_scr[at : at + strip] = noises[size][image]
        for k, send in enumerate(sends):
            rows = pl.ds(k * part, part)
            usage = forward_rows(params, l_scr.at[rows], noise_scr.at[rows], send, usage)
    usage_ref[...] = usage
    copies[9].wait()


def small_forward(count, steps, orders, feats, noises, params):
    dim, codes = params[2].shape
    width = feats[0].shape[2]
    groups = tuple(f.shape[0] // count for f in feats)
    part = sum(g * f.shape[1] for g, f in zip(groups, feats))
    rows = part * len(steps)
    arrays = [*params[0:3], *orders[0:2], *feats, *noises]
    return pl.pallas_call(
        functools.partial(small_forward_kernel, count, steps, groups),
        out_shape=[jax.ShapeDtypeStruct((part, codes), F32)] * len(steps)
        + [
            jax.ShapeDtypeStruct((8, codes), F32),
            jax.ShapeDtypeStruct((8, 128), F32),
            jax.ShapeDtypeStruct(orders[2].shape, jnp.int32),
        ],
        in_specs=[HBM] * 10 + [SMEM] * 2,
        out_specs=[VMEM] * (len(steps) + 3),
        scratch_shapes=[
            (pltpu.SMEM if 3 <= i < 5 else pltpu.VMEM)(a.shape, a.dtype)
            for i, a in enumerate(arrays)
        ]
        + [pltpu.SemaphoreType.DMA((10,)), pltpu.VMEM((rows, width), F32)]
        + shared_scratch(dim, codes, width)
        + [pltpu.VMEM((rows, codes), F32)] * 2,
        compiler_params=settings(),
        cost_estimate=cost(rows, width, dim, codes, 4),
        name="small_forward",
    )(*in_hbm([*arrays, orders[2]]), *params[3:5])


def small_backward_kernel(count, steps, devices, groups, *refs):
    orders, feats, cots, parts, params, (acc_in, *usages), grads, shards, rest = take(
        refs, 2, 2, 2, count, 4, 3, 2, devices, len(refs)
    )
    acc_ref, sum_scr, feat_scr, cot_scr, code_scr = rest[0:5]
    scr = rest[5:]
    strips = places_of(orders, [f.shape for f in feats], groups, steps, count)
    for _, _, size, image, at, strip in strips:
        feat_scr[at : at + strip] = feats[size][image]
        cot_scr[at : at + strip] = cots[size][image]
    part = parts[0].shape[0]
    for step in range(count):
        code_scr[step * part : (step + 1) * part] = parts[step][...]
    shared, tile_scr = take(scr, 3, 6)
    prepare(params, *shared)
    acc_ref[...] = acc_in[...]
    state = products(params, shared, tile_scr, feat_scr[...], cot_scr[...].T, False)
    backward_rows(tile_scr, code_scr)
    feat_scr[...] = gradients(params, shared, tile_scr, state, acc_ref)
    acc_ref[136:144] += usages[0][...] + usages[1][...]
    lay_out(params, acc_ref, sum_scr, shards)
    for _, _, size, image, at, strip in strips:
        grads[size][image] = feat_scr[at : at + strip]


def small_backward(count, steps, devices, orders, feats, cots, parts, params, acc, usages):
    dim, codes = params[2].shape
    width = feats[0].shape[2]
    groups = tuple(f.shape[0] // count for f in feats)
    rows = parts[0].shape[0] * count
    return pl.pallas_call(
        functools.partial(small_backward_kernel, count, steps, devices, groups),
        out_shape=[pltpu.HBM(f.shape, F32) for f in feats]
        + [jax.ShapeDtypeStruct((64 // devices, LANES), F32)] * devices,
        in_specs=[SMEM] * 2 + [VMEM] * (11 + count),
        out_specs=[VMEM] * (2 + devices),
        scratch_shapes=[
            pltpu.VMEM(acc.shape, F32),
            pltpu.VMEM((64, LANES), F32),
            pltpu.VMEM((rows, width), F32),
            pltpu.VMEM((rows, dim), F32),
            pltpu.VMEM((rows, codes), F32),
        ]
        + shared_scratch(dim, codes, width)
        + tile_scratch(rows, codes),
        compiler_params=settings(),
        cost_estimate=cost(rows, width, dim, codes, 6),
        name="small_backward",
    )(
        *orders,
        *in_hbm([*feats, *cots]),
        *parts,
        *in_hbm(params[0:3]),
        params[3],
        acc,
        *usages,
    )


def wide_forward_kernel(lanes, joined, *refs):
    n = len(lanes)
    arrays = len(joined) if joined else sum(len(lane.runs) for lane in lanes)
    _, feats, noises, params, usage_in, sends, rest = take(
        refs, 1, n, n, 4, 1, arrays, len(refs)
    )
    (usage_ref,), code_scrs, shared, l_scrs = take(rest, 1, n, 3, n)
    step = pl.program_id(0)

    @pl.when(step == 0)
    def _():
        prepare(params, *shared, backward=False)
        usage_ref[...] = usage_in[0][...]

    if joined:
        strip = code_scrs[0].shape[0]
        targets = [
            send.at[pl.ds(i * strip, strip)] for send, k in zip(sends, joined) for i in range(k)
        ]
    else:
        targets = code_targets(lanes, sends, code_scrs)
    for feat_ref, l_scr in zip(feats, l_scrs):
        forward_products(params, shared, feat_ref[...], l_scr)
    usage = usage_ref[...]
    for l_scr, noise_ref, target in zip(l_scrs, noises, targets):
        usage = forward_rows(params, l_scr, noise_ref, target, usage)
    usage_ref[...] = usage
    if not joined:
        keep_codes(step, lanes, sends, code_scrs)


def wide_forward(count, lanes, joined, order, feat, noise, params, usage, tenths):
    dim, codes = params[2].shape
    images, strip, width = feat.shape
    n, steps = len(lanes), lanes[0].total()
    if joined:
        blocks = [fixed((k * strip, codes)) for k in joined]
        sizes = joined
    else:
        blocks = [block for lane in lanes for block in lane.blocks((strip, codes))]
        sizes = [run[2] for lane in lanes for run in lane.runs]
    return pl.pallas_call(
        functools.partial(wide_forward_kernel, lanes, joined),
        grid_spec=pltpu.PrefetchScalarGridSpec(
            num_scalar_prefetch=1,
            grid=(steps,),
            in_specs=[lane.image((strip, width), count) for lane in lanes]
            + [lane.image((strip, codes), count) for lane in lanes]
            + [fixed(p.shape) for p in params]
            + [fixed(usage.shape)],
            out_specs=blocks + [fixed(usage.shape)],
            scratch_shapes=[pltpu.VMEM((strip, codes), F32)] * n
            + shared_scratch(dim, codes, width)
            + [pltpu.VMEM((strip, codes), F32)] * n,
        ),
        out_shape=[jax.ShapeDtypeStruct((strip * slots, codes), F32) for slots in sizes]
        + [jax.ShapeDtypeStruct(usage.shape, F32)],
        input_output_aliases={5 + 2 * n: len(sizes)},
        compiler_params=settings(),
        cost_estimate=cost(n * steps * strip, width, dim, codes, tenths),
        name="wide_forward",
    )(order, *in_hbm([feat] * n + [noise] * n + [*params[0:3]]), params[3], usage)


def wide_both_kernel(lanes, count, *refs):
    n = len(lanes)
    arrays = sum(len(lane.runs) for lane in lanes)
    order, feats, noises, cots, params, sends, rest = take(
        refs, 1, n, n, n, 4, arrays, len(refs)
    )
    (grad_out, acc_ref), code_scrs, (grad_scr, sems), shared, rest = take(
        rest, 2, n, 2, 3, 6 * n
    )
    scrs = take(rest, *[6] * n)
    grads = Gradients(grad_out, grad_scr, sems)
    step, steps = pl.program_id(0), lanes[0].total()

    @pl.when(step == 0)
    def _():
        prepare(params, *shared)
        acc_ref[...] = jnp.zeros(acc_ref.shape, F32)

    grads.ready(step, n)
    targets = code_targets(lanes, sends, code_scrs)
    states = [
        products(params, shared, scr, feat_ref[...], cot_ref[...], True)
        for scr, feat_ref, cot_ref in zip(scrs, feats, cots)
    ]
    usage = acc_ref[136:144]
    for scr, noise_ref, target in zip(scrs, noises, targets):
        usage = both_rows(params, scr, noise_ref, target, usage)
    acc_ref[136:144] = usage
    values = [
        gradients(params, shared, scr, state, acc_ref) for scr, state in zip(scrs, states)
    ]
    grads.store(step, values, [lane.index(step, order[0], count) for lane in lanes])
    keep_codes(step, lanes, sends, code_scrs)
    grads.end(step, n, steps)


def wide_both(count, lanes, order, feat, noise, cot, params):
    dim, codes = params[2].shape
    images, strip, width = feat.shape
    n, steps = len(lanes), lanes[0].total()
    acc_shape = (ACC_ROWS, codes)
    sizes = [run[2] for lane in lanes for run in lane.runs]
    return pl.pallas_call(
        functools.partial(wide_both_kernel, lanes, count),
        grid_spec=pltpu.PrefetchScalarGridSpec(
            num_scalar_prefetch=1,
            grid=(steps,),
            in_specs=[lane.image((strip, width), count) for lane in lanes]
            + [lane.image((strip, codes), count) for lane in lanes]
            + [lane.image((dim, strip), count) for lane in lanes]
            + [fixed(p.shape) for p in params],
            out_specs=[block for lane in lanes for block in lane.blocks((strip, codes))]
            + [HBM, fixed(acc_shape)],
            scratch_shapes=[pltpu.VMEM((strip, codes), F32)] * n
            + gradient_scratch(n, strip, width)
            + shared_scratch(dim, codes, width)
            + tile_scratch(strip, codes) * n,
        ),
        out_shape=[jax.ShapeDtypeStruct((strip * slots, codes), F32) for slots in sizes]
        + [pltpu.HBM(feat.shape, F32), jax.ShapeDtypeStruct(acc_shape, F32)],
        compiler_params=settings(),
        cost_estimate=cost(n * steps * strip, width, dim, codes, 10),
        name="wide_both",
    )(order, *in_hbm([feat] * n + [noise] * n + [cot] * n + [*params[0:3]]), params[3])


def wide_backward_kernel(lanes, count, *refs):
    n = len(lanes)
    arrays = sum(len(lane.runs) for lane in lanes)
    order, feats, cots, parts, params, (acc_in, _), rest = take(
        refs, 1, n, n, arrays, 4, 2, len(refs)
    )
    (grad_out, acc_ref), code_scrs, (grad_scr, sems), shared, rest = take(
        rest, 2, n, 2, 3, 6 * n
    )
    scrs = take(rest, *[6] * n)
    grads = Gradients(grad_out, grad_scr, sems)
    step, steps = pl.program_id(0), lanes[0].total()

    @pl.when(step == 0)
    def _():
        prepare(params, *shared)
        acc_ref[...] = acc_in[...]

    grads.ready(step, n)
    for lane, refs_of, code_scr in zip(lanes, by_lane(parts, lanes), code_scrs):
        if len(lane.runs) > 1:

            def fetch(i, refs_of=refs_of, code_scr=code_scr):
                code_scr[...] = refs_of[i][...]

            lane.each(step, fetch)
    states = [
        products(params, shared, scr, feat_ref[...], cot_ref[...], False)
        for scr, feat_ref, cot_ref in zip(scrs, feats, cots)
    ]
    for scr, code_ref in zip(scrs, code_targets(lanes, parts, code_scrs)):
        backward_rows(scr, code_ref)
    values = [
        gradients(params, shared, scr, state, acc_ref) for scr, state in zip(scrs, states)
    ]
    grads.store(step, values, [lane.index(step, order[0], count) for lane in lanes])
    grads.end(step, n, steps)


def wide_backward(count, lanes, parts, order, feat, cot, params, acc, grad):
    dim, codes = params[2].shape
    images, strip, width = feat.shape
    n, steps = len(lanes), lanes[0].total()
    return pl.pallas_call(
        functools.partial(wide_backward_kernel, lanes, count),
        grid_spec=pltpu.PrefetchScalarGridSpec(
            num_scalar_prefetch=1,
            grid=(steps,),
            in_specs=[lane.image((strip, width), count) for lane in lanes]
            + [lane.image((dim, strip), count) for lane in lanes]
            + [block for lane in lanes for block in lane.blocks((strip, codes))]
            + [fixed(p.shape) for p in params]
            + [fixed(acc.shape), HBM],
            out_specs=[HBM, fixed(acc.shape)],
            scratch_shapes=[pltpu.VMEM((strip, codes), F32)] * n
            + gradient_scratch(n, strip, width)
            + shared_scratch(dim, codes, width)
            + tile_scratch(strip, codes) * n,
        ),
        out_shape=[pltpu.HBM(feat.shape, F32), jax.ShapeDtypeStruct(acc.shape, F32)],
        input_output_aliases={5 + 2 * n + len(parts): 1, 6 + 2 * n + len(parts): 0},
        compiler_params=settings(),
        cost_estimate=cost(n * steps * strip, width, dim, codes, 6),
        name="wide_backward",
    )(
        order,
        *in_hbm([feat] * n + [cot] * n),
        *parts,
        *in_hbm(params[0:3]),
        params[3],
        acc,
        *in_hbm([grad]),
    )


def shard_at(index, parts):
    height = 64 // parts
    return pl.ds(pl.multiple_of(index * height, height), height)


def lay_out(params, acc_ref, sum_scr, shards):
    weight_ref, bias_ref, book_ref, scalar_ref = params
    codes = book_ref.shape[1]
    width = weight_ref.shape[1]
    devices = len(shards)
    me = lax.rem(lax.axis_index("dp"), devices)
    precision, _, factor = scalars(scalar_ref)
    book = book_ref[...]
    column = acc_ref[128:129]
    moment = acc_ref[64:128] * (1.0 / precision)
    book_sum = acc_ref[0:64] * (1.0 / factor) + 2.0 * (column * book - moment)
    slope = jnp.sum(
        jnp.sum(book * book, axis=0, keepdims=True) * column, axis=1, keepdims=True
    ) - 2.0 * jnp.sum(jnp.sum(book * moment, axis=0, keepdims=True), axis=1, keepdims=True)
    slope = slope + acc_ref[208:209, 0:1] / (-0.5 * precision)
    usage = jnp.sum(acc_ref[136:144], axis=0, keepdims=True)
    dim = book_ref.shape[0]
    eye = lax.broadcasted_iota(jnp.int32, (dim, dim), 0) == lax.broadcasted_iota(
        jnp.int32, (dim, dim), 1
    )
    bias = acc_ref[144:208, width : width + dim]
    bias = jnp.sum(jnp.where(eye, bias, 0.0), axis=0, keepdims=True)
    rest = codes + width
    sum_scr[:, 0:codes] = book_sum
    sum_scr[:, codes:rest] = acc_ref[144:208, 0:width]
    sum_scr[:, rest : rest + 128] = jnp.broadcast_to(slope, (64, 128))
    rows = codes // 128
    for i in range(rows):
        sum_scr[i : i + 1, rest : rest + 128] = usage[:, i * 128 : (i + 1) * 128]
    sum_scr[rows : rows + 1, rest : rest + dim] = bias
    for i in range(devices):
        shards[i][...] = sum_scr[shard_at(partner(me, i, devices), devices)]


def own_kernel(n, count, *refs):
    order, feats, noises, cots, params, (acc_in, _), rest = take(
        refs, 1, n, n, n, 4, 2, len(refs)
    )
    (code_ref, grad_out, acc_ref), (grad_scr, sems), shared, rest = take(rest, 3, 2, 3, 6 * n)
    scrs = take(rest, *[6] * n)
    grads = Gradients(grad_out, grad_scr, sems)
    step = pl.program_id(0)

    @pl.when(step == 0)
    def _():
        prepare(params, *shared)
        acc_ref[...] = acc_in[...]

    grads.ready(step, n)
    states = [
        products(params, shared, scr, feat_ref[...], cot_ref[...], True)
        for scr, feat_ref, cot_ref in zip(scrs, feats, cots)
    ]
    usage = acc_ref[136:144]
    for i, (scr, noise_ref) in enumerate(zip(scrs, noises)):
        usage = both_rows(params, scr, noise_ref, code_ref.at[i], usage)
    acc_ref[136:144] = usage
    values = [
        gradients(params, shared, scr, state, acc_ref) for scr, state in zip(scrs, states)
    ]
    grads.store(step, values, [own_image(step, i, n, order[0], count) for i in range(n)])
    grads.end(step, n, pl.num_programs(0))


def own_image(step, lane, n, order_ref, count):
    share = order_ref.shape[1] // count
    return order_ref[0, lax.axis_index("space") * share + step * n + lane]


def run_own(count, order, feat, noise, cot, params, acc, grad):
    dim, codes = params[2].shape
    images, strip, width = feat.shape
    share = images // count
    n = 2 if share % 2 == 0 else 1

    def image(lane, shape):
        return pl.BlockSpec(
            (None, *shape), lambda i, order_ref: (own_image(i, lane, n, order_ref, count), 0, 0)
        )

    return pl.pallas_call(
        functools.partial(own_kernel, n, count),
        grid_spec=pltpu.PrefetchScalarGridSpec(
            num_scalar_prefetch=1,
            grid=(share // n,),
            in_specs=[image(lane, (strip, width)) for lane in range(n)]
            + [image(lane, (strip, codes)) for lane in range(n)]
            + [image(lane, (dim, strip)) for lane in range(n)]
            + [fixed(p.shape) for p in params]
            + [fixed(acc.shape), HBM],
            out_specs=[
                pl.BlockSpec(
                    (n, strip, codes),
                    lambda i, _: (i, lax.axis_index("space"), 0),
                ),
                HBM,
                fixed(acc.shape),
            ],
            scratch_shapes=gradient_scratch(n, strip, width)
            + shared_scratch(dim, codes, width)
            + tile_scratch(strip, codes) * n,
        ),
        out_shape=[
            pltpu.HBM((share, strip * count, codes), F32),
            pltpu.HBM(feat.shape, F32),
            jax.ShapeDtypeStruct(acc.shape, F32),
        ],
        input_output_aliases={5 + 3 * n: 2, 6 + 3 * n: 1},
        compiler_params=settings(),
        cost_estimate=cost(share * strip, width, dim, codes, 10),
        name="own_images",
    )(
        order,
        *in_hbm([feat] * n + [noise] * n + [cot] * n + [*params[0:3]]),
        params[3],
        acc,
        *in_hbm([grad]),
    )


def place_kernel(count, runs, *refs):
    parts = refs[0 : len(runs)]
    out_ref, sem = refs[len(runs) + 1 : len(runs) + 3]
    me = lax.axis_index("space")
    copies = []
    for part, (step, first, slots) in zip(parts, runs):
        strip = part.shape[0] // slots
        row = pl.multiple_of(source(me, step, count) * strip, strip)
        rows = strip // 4
        for j in range(4 * slots):
            copies.append(
                pltpu.make_async_copy(
                    part.at[pl.ds(j * rows, rows)],
                    out_ref.at[first + j // 4, pl.ds(row + j % 4 * rows, rows)],
                    sem.at[len(copies)],
                )
            )
    for copy in copies:
        copy.start()
    for copy in copies:
        copy.wait()


def place_wide(count, runs, parts, whole):
    return pl.pallas_call(
        functools.partial(place_kernel, count, runs),
        out_shape=pltpu.HBM(whole.shape, F32),
        in_specs=[VMEM] * len(runs) + [HBM],
        out_specs=HBM,
        scratch_shapes=[pltpu.SemaphoreType.DMA((4 * sum(r[2] for r in runs),))],
        input_output_aliases={len(runs): 0},
        compiler_params=settings(VMEM_LIMIT // 2),
        cost_estimate=pl.CostEstimate(
            flops=0, bytes_accessed=2 * sum(p.size * 4 for p in parts), transcendentals=0
        ),
        name="place_wide",
    )(*[pltpu.with_memory_space_constraint(p, pltpu.VMEM) for p in parts], *in_hbm([whole]))


def join_kernel(count, steps, *refs):
    parts = refs[0:count]
    outs = refs[count:]
    me = lax.axis_index("space")
    for part, step in zip(parts, steps):
        here = source(me, step, count)
        base = 0
        for out in outs:
            for j in range(out.shape[0]):
                strip = out.shape[2]
                out[j, here] = part[base : base + strip]
                base += strip


def join_small(count, steps, parts, shapes):
    codes = parts[0].shape[1]
    return pl.pallas_call(
        functools.partial(join_kernel, count, steps),
        out_shape=[
            jax.ShapeDtypeStruct((images // count, count, strip, codes), F32)
            for images, strip, _ in shapes
        ],
        compiler_params=settings(VMEM_LIMIT // 2),
        name="join_small",
    )(*parts)


def tree(values):
    while len(values) > 1:
        values = [
            values[i] + values[i + 1] if i + 1 < len(values) else values[i]
            for i in range(0, len(values), 2)
        ]
    return values[0]


def sum_kernel(*refs):
    refs[-1][...] = tree([ref[...] for ref in refs[:-1]])


def add_all(parts):
    return pl.pallas_call(
        sum_kernel,
        out_shape=jax.ShapeDtypeStruct(parts[0].shape, F32),
        compiler_params=settings(VMEM_LIMIT // 2),
        name="add_parts",
    )(*parts)


def final_kernel(devices, pixels, *refs):
    shards = refs[0:devices]
    weight_ref, bias_ref, book_ref, log_ref, usage_ref = refs[devices : devices + 5]
    weight_out, bias_out, book_out, log_out, usage_out = refs[devices + 5 : devices + 10]
    sum_scr = refs[devices + 10]
    me = lax.rem(lax.axis_index("dp"), devices)
    for i in range(devices):
        sum_scr[shard_at(source(me, i, devices), devices)] = shards[i][...]
    dim, codes = book_ref.shape
    width = weight_ref.shape[1]
    scale = 0.5 * lax.rsqrt(jnp.full((8, 128), pixels, F32))[0:1, 0:1]
    book_out[...] = 0.5 * book_ref[...] + scale * sum_scr[:, 0:codes]
    rest = codes + width
    weight_out[...] = 0.5 * weight_ref[...] + scale * sum_scr[:, codes:rest]
    rows = codes // 128
    bias_out[...] = 0.5 * bias_ref[...] + scale * sum_scr[rows : rows + 1, rest : rest + dim]
    usage = jnp.concatenate(
        [sum_scr[i : i + 1, rest : rest + 128] for i in range(rows)], axis=1
    )
    usage_out[...] = 0.5 * usage_ref[...] + 0.5 * (codes / pixels) * usage
    log_out[...] = 0.5 * log_ref[...] + scale * sum_scr[rows + 1 : rows + 2, rest : rest + 1]


def finish(devices, pixels, shards, weight, bias, book, log, usage):
    outs = (weight.T, bias.reshape(1, -1), book.T, log.reshape(1, 1), usage.reshape(1, -1))
    outs = pl.pallas_call(
        functools.partial(final_kernel, devices, pixels),
        out_shape=[jax.ShapeDtypeStruct(out.shape, F32) for out in outs],
        scratch_shapes=[pltpu.VMEM((64, LANES), F32)],
        compiler_params=settings(VMEM_LIMIT // 2),
        name="new_averages",
    )(*shards, *outs)
    return outs[0].T, outs[1].reshape(-1), outs[2].T, outs[3].reshape(-1), outs[4].reshape(-1)


def exchange(value, bit, size, pairs):
    while bit < size:
        value = value + pairs(value, bit)
        bit = 2 * bit
    return value


def per_device(
    feat_small,
    feat_mid,
    feat_wide,
    noise_small,
    noise_mid,
    noise_wide,
    cot_small,
    cot_mid,
    cot_wide,
    order_small,
    order_mid,
    order_wide,
    weight,
    bias,
    book,
    log,
    heat,
    weight_mean,
    bias_mean,
    book_mean,
    log_mean,
    usage_mean,
):
    count = lax.axis_size("space")
    devices = lax.axis_size("dp")
    params = (weight.T, bias.reshape(1, -1), book.T, log, heat)
    feats = (feat_small, feat_mid, feat_wide)
    pixels = sum(f.shape[0] * f.shape[1] for f in feats) * count * devices
    share = feat_wide.shape[0] // count
    cot_wide = jnp.swapaxes(cot_wide, 1, 2)

    def send(values):
        return [lax.ppermute(v, "space", route(i, count)) for i, v in zip(turns, values)]

    def follow(codes, before, parts):
        here, codes[-1] = lax.optimization_barrier(([before[i] for i in parts], codes[-1]))
        for i, part in zip(parts, here):
            before[i] = part
        return send(codes)

    last = count - 1
    turns = list(range(1, count))
    orders = (order_small, order_mid, order_wide)
    noises = (noise_small, noise_mid)
    *small, usage, scalar, order_wide = small_forward(
        count, turns, orders, feats[0:2], noises, params
    )
    arrived = [send(small)]
    own_params = params
    params = (*params[0:3], scalar)
    near = min(4, devices)
    early = [(step, 0, 1) for step in turns]
    direct = [(step, 1, share - 1) for step in turns[:-1]]
    late = [(last, 1, share - 2), (last, share - 1, 1)]
    *early_codes, usage = wide_forward(
        count, split(early, 3), [], order_wide, feat_wide, noise_wide, params, usage, 4
    )
    ahead = [count - 2, *range(count - 2)]
    arrived.append(follow(list(early_codes), arrived[0], ahead))
    *codes, grad, acc = wide_both(
        count, split(direct, 2), order_wide, feat_wide, noise_wide, cot_wide, params
    )
    late_lanes = [Lane([(last, slot, 1)]) for slot in range(1, share)]
    late_codes, end_codes, usage = wide_forward(
        count, late_lanes, [share - 2, 1], order_wide, feat_wide, noise_wide, params, usage, 1
    )
    arrived.append(follow([*codes, late_codes], arrived[1], [0]))
    arrived[1][-1], leaving = lax.optimization_barrier((arrived[1][-1], end_codes))
    arrived[2].append(lax.ppermute(leaving, "space", route(last, count)))
    arrived[1], acc = lax.optimization_barrier((arrived[1], acc))
    whole, grad, acc = run_own(
        count, order_wide, feat_wide, noise_wide, cot_wide, params, acc, grad
    )
    whole = place_wide(count, early, arrived[1], whole)
    acc, own_params = lax.optimization_barrier((acc, own_params))
    own, own_usage, _, _ = small_forward(
        count, range(1), orders, feats[0:2], noises, own_params
    )
    small = [own, *small]
    codes_small, codes_mid = join_small(
        count, [0, *turns], [own] + arrived[0], [f.shape for f in feats[0:2]]
    )
    whole, codes_small, codes_mid, acc = lax.optimization_barrier(
        (whole, codes_small, codes_mid, acc)
    )
    grad, acc = wide_backward(
        count,
        split(early + late, 2),
        [*early_codes, late_codes, end_codes],
        order_wide,
        feat_wide,
        cot_wide,
        params,
        acc,
        grad,
    )
    grad_small, grad_mid, *shards = small_backward(
        count,
        [0, *turns],
        near,
        orders[0:2],
        feats[0:2],
        (cot_small, cot_mid),
        small,
        params,
        acc,
        (usage, own_usage),
    )
    group = [
        [(i, i - i % near + partner(i % near, step, near)) for i in range(devices)]
        for step in range(near)
    ]
    parts = [lax.ppermute(shards[i], "dp", group[i]) for i in range(1, near)]
    mine = add_all([shards[0]] + parts)

    def along(value, offset):
        return lax.ppermute(value, "dp", [(i, i ^ offset) for i in range(devices)])

    def across(value, offset):
        turn = near if devices > near else 0
        pairs = [
            (i * count + j, (i ^ turn) * count + (j ^ offset))
            for i in range(devices)
            for j in range(count)
        ]
        return lax.ppermute(value, ("dp", "space"), pairs)

    mine = exchange(mine, near, devices, along)
    arrived[2][:-2], mine = lax.optimization_barrier((arrived[2][:-2], mine))
    mine = exchange(mine, 1, count, across)
    shards = [mine] + [lax.ppermute(mine, "dp", group[i]) for i in range(1, near)]
    updated = finish(
        near, pixels, shards, weight_mean, bias_mean, book_mean, log_mean, usage_mean
    )
    *before, final = zip(direct + late, arrived[2])
    for run, part in before:
        whole = place_wide(count, [run], [part], whole)
    whole, updated = lax.optimization_barrier((whole, updated))
    whole = place_wide(count, [final[0]], [final[1]], whole)
    codes = whole.shape[2]
    return (
        codes_small.reshape(codes_small.shape[0], -1, codes),
        codes_mid.reshape(codes_mid.shape[0], -1, codes),
        whole,
        grad_small,
        grad_mid,
        grad,
        *updated,
    )


def solution(mesh):
    strips = P("dp", "space", None)
    placed = (strips,) * 9 + (P("dp", None),) * 3 + (P(),) * 10
    return jax.shard_map(
        per_device,
        mesh=mesh,
        in_specs=placed,
        out_specs=(P(("dp", "space"), None, None),) * 3 + (strips,) * 3 + (P(),) * 5,
        check_vma=False,
    )
```
